32 devices in a mesh: section: 2 (over core), dp: 16 (over z, y, x).
Axes of the slice: x: 2, y: 2, z: 4, core: 2. Of those that a mesh axis runs over, the one named last changes fastest.
Arguments:
- patches: bfloat16 [12288, 768], P('dp'), may hold values from -6 to 6
- segment_ids: int32 [32, 384], P('dp'), may hold values from 0 to 11, never falling along the last dimension, each value on 1 to 64 neighbouring positions
- patch_order: int32 [384, 128], P('dp'), may hold values from 0 to 127, each once within a row
- encoder_gain1: float32 [768], replicated, may hold values from 0.5 to 1.5
- encoder_bias1: float32 [768], replicated, may hold values from -1.75 to 1.75
- encoder_qkv: bfloat16 [768, 2304], replicated, may hold values from -0.21875 to 0.21875
- encoder_out: bfloat16 [768, 768], replicated, may hold values from -1.25 to 1.25
- encoder_out_bias: float32 [768], replicated, may hold values from -1.75 to 1.75
- encoder_gain2: float32 [768], replicated, may hold values from 0.5 to 1.5
- encoder_bias2: float32 [768], replicated, may hold values from -1.75 to 1.75
- encoder_up: bfloat16 [768, 3072], replicated, may hold values from -0.21875 to 0.21875
- encoder_up_bias: float32 [3072], replicated, may hold values from -1.75 to 1.75
- encoder_down: bfloat16 [3072, 768], replicated, may hold values from -0.109375 to 0.109375
- encoder_down_bias: float32 [768], replicated, may hold values from -1.75 to 1.75
- embed_weight: bfloat16 [768, 512], replicated, may hold values from -0.21875 to 0.21875
- embed_bias: float32 [512], replicated, may hold values from -1.75 to 1.75
- mask_token: float32 [512], replicated, may hold values from -6 to 6
- decoder_gain1: float32 [512], replicated, may hold values from 0.5 to 1.5
- decoder_bias1: float32 [512], replicated, may hold values from -1.75 to 1.75
- decoder_qkv: bfloat16 [512, 1536], replicated, may hold values from -0.25 to 0.25
- decoder_out: bfloat16 [512, 512], replicated, may hold values from -3 to 3
- decoder_out_bias: float32 [512], replicated, may hold values from -1.75 to 1.75
- decoder_gain2: float32 [512], replicated, may hold values from 0.5 to 1.5
- decoder_bias2: float32 [512], replicated, may hold values from -1.75 to 1.75
- decoder_up: bfloat16 [512, 2048], replicated, may hold values from -0.25 to 0.25
- decoder_up_bias: float32 [2048], replicated, may hold values from -1.75 to 1.75
- decoder_down: bfloat16 [2048, 512], replicated, may hold values from -0.125 to 0.125
- decoder_down_bias: float32 [512], replicated, may hold values from -1.75 to 1.75
- cotangent: bfloat16 [384, 128, 512], P('dp'), may hold values from -6 to 6
Outputs:
- decoded: bfloat16 [384, 128, 512], P('dp', 'section')
- patches_grad: bfloat16 [12288, 768], P('dp', 'section')
- grad_encoder_gain1: float32 [768], P('dp')
- grad_encoder_bias1: float32 [768], P('dp')
- grad_encoder_qkv: float32 [768, 2304], P('dp')
- grad_encoder_out: float32 [768, 768], P('dp')
- grad_encoder_out_bias: float32 [768], P('dp')
- grad_encoder_gain2: float32 [768], P('dp')
- grad_encoder_bias2: float32 [768], P('dp')
- grad_encoder_up: float32 [768, 3072], P('dp')
- grad_encoder_up_bias: float32 [3072], P('dp')
- grad_encoder_down: float32 [3072, 768], P('dp')
- grad_encoder_down_bias: float32 [768], P('dp')
- grad_embed_weight: float32 [768, 512], P('dp')
- grad_embed_bias: float32 [512], P('dp')
- grad_mask_token: float32 [512], P('dp')
- grad_decoder_gain1: float32 [512], P('dp')
- grad_decoder_bias1: float32 [512], P('dp')
- grad_decoder_qkv: float32 [512, 1536], P('dp')
- grad_decoder_out: float32 [512, 512], P('dp')
- grad_decoder_out_bias: float32 [512], P('dp')
- grad_decoder_gain2: float32 [512], P('dp')
- grad_decoder_bias2: float32 [512], P('dp')
- grad_decoder_up: float32 [512, 2048], P('dp')
- grad_decoder_up_bias: float32 [2048], P('dp')
- grad_decoder_down: float32 [2048, 512], P('dp')
- grad_decoder_down_bias: float32 [512], P('dp')
The draws below stay inside these ranges and needn't reach their ends.
Inputs may be any that keep to these rules, and one draw needn't show every extreme that they name: `segment_ids`: in each micro-batch the sample numbers never fall, each of the 12 samples has 1 to 64 rows, and some sample has exactly 64. `patch_order`: each row holds every patch number once.
All inputs are finite; a program needn't handle non-finite values.
Results may differ from the reference program's by a relative error of at most 0.02.
Values may be sent and summed in bfloat16 or wider, within the bound.
A program may use at most 384 MiB of HBM per device.

```python
import math
import jax
import jax.numpy as jnp
import numpy as np
from jax import lax

D_ENC = 768
H_ENC = 12
FF_ENC = 3072
DECODER_WIDTH = 512
H_DEC = 16
FF_DEC = 2048
PATCHES = 128
VISIBLE = 32
SAMP_MB = 12
ROWS_MB = 384
NUM_MB = 32
SAMPLES = 384
ROWS = 12288


def with_spikes(array, own_key, source, target, parts, factor):
    owner, partner = [(jnp.arange(array.shape[axis_at]) // (array.shape[axis_at] // parts)).reshape([-1 if axis == axis_at else 1 for axis in range(array.ndim)]) for axis_at in (source, target)]
    chosen = jax.random.permutation(own_key, parts)[partner]
    strong = (owner == chosen) | (owner == (partner + parts // 2) % parts)
    return jnp.where(strong, factor * array, array)


def block_levels(key, extent, pieces, smallest, largest):
    loudness, own = 1.0, jax.random.fold_in(key, 6)
    for axis_at, shards_of in pieces:
        heights = jnp.exp(jax.random.uniform(jax.random.fold_in(own, axis_at), (shards_of,), jnp.float32, smallest / len(pieces), largest / len(pieces)))
        loudness = loudness * jnp.repeat(heights, extent[axis_at] // shards_of).reshape([-1 if axis == axis_at else 1 for axis in range(len(extent))])
    return loudness


def split_up(count, total, limit, lean):
    weights = [(1 << 20) // math.isqrt(grade ** lean) + 1 for grade in range(2, count + 1)]
    spare, holding = total - limit - (count - 1), [1] * (count - 1)
    while spare > 0:
        movable = [i for i in range(count - 1) if holding[i] < limit]
        whole, remaining = sum([weights[i] for i in movable]), spare
        for i in movable:
            more = min(limit - holding[i], max(1, remaining * weights[i] // whole), spare)
            holding[i] = holding[i] + more
            spare = spare - more
    return np.array([limit] + holding)


def uneven(key, count, total, bound, lean):
    if count == 2:
        one = jax.random.randint(key, (), max(1, total - bound), min(bound, total - 1) + 1)
        return jnp.stack([one, total - one])
    sizes = jnp.asarray(split_up(count, total, bound, lean), jnp.int32)
    couples = (count - 1) // 2
    source_of, sink = sizes[1:1 + 2 * couples:2], sizes[2:2 + 2 * couples:2]
    room = jnp.minimum(source_of - 1, bound - sink)
    shifted = jax.random.randint(jax.random.fold_in(key, 1), (couples,), 0, 1 << 20) % (room + 1)
    sizes = sizes.at[1:1 + 2 * couples:2].set(source_of - shifted).at[2:2 + 2 * couples:2].set(sink + shifted)
    return sizes[jax.random.permutation(jax.random.fold_in(key, 2), count)]


def noise(key, shape, scale, bound, shards=(), held_as=jnp.bfloat16):
    values = scale * jax.random.normal(key, shape, jnp.float32)
    if shards:
        values = values * block_levels(key, shape, shards, -0.22, 0.18)
    return jnp.clip(values, -bound, bound).astype(held_as)


def bell_draw_with(own_key, shape, scale, reach, split, heavy, kind=jnp.bfloat16):
    result = scale * jax.random.normal(own_key, shape, jnp.float32)
    if split:
        result = result * block_levels(own_key, shape, split, -0.22, 0.18)
    return jnp.clip(with_spikes(result, jax.random.fold_in(own_key, 3), *heavy), -reach, reach).astype(kind)


def setup_inputs(seed: int = 0) -> dict:
    seeds = jax.random.split(jax.random.key(seed), 30)
    patches = bell_draw_with(seeds[0], (ROWS, D_ENC), 1.0, 6.0, ((0, 16),), (0, 1, 16, 2.0))
    segment_ids = jax.vmap(lambda own: jnp.searchsorted(jnp.cumsum(uneven(own, SAMP_MB, ROWS_MB, 2 * VISIBLE, 2)), jnp.arange(ROWS_MB), side="right"))(jax.random.split(seeds[1], NUM_MB)).reshape((NUM_MB, ROWS_MB)).astype(jnp.int32)
    patch_order = jax.vmap(lambda own: jax.random.permutation(own, PATCHES))(jax.random.split(seeds[2], SAMPLES)).reshape((SAMPLES, PATCHES)).astype(jnp.int32)
    encoder_gain1 = jnp.clip(1.0 + 0.1 * jax.random.normal(seeds[3], (D_ENC,), jnp.float32), 0.5, 1.5)
    encoder_bias1 = noise(seeds[4], (D_ENC,), 0.3, 1.75, (), jnp.float32)
    encoder_qkv = noise(seeds[5], (D_ENC, 3 * D_ENC), D_ENC ** -0.5, 0.21875)
    encoder_out = noise(seeds[6], (D_ENC, D_ENC), (D_ENC // VISIBLE) ** -0.5, 1.25)
    encoder_out_bias = noise(seeds[7], (D_ENC,), 0.3, 1.75, (), jnp.float32)
    encoder_gain2 = jnp.clip(1.0 + 0.1 * jax.random.normal(seeds[8], (D_ENC,), jnp.float32), 0.5, 1.5)
    encoder_bias2 = noise(seeds[9], (D_ENC,), 0.3, 1.75, (), jnp.float32)
    encoder_up = noise(seeds[10], (D_ENC, FF_ENC), D_ENC ** -0.5, 0.21875)
    encoder_up_bias = noise(seeds[11], (FF_ENC,), 0.3, 1.75, (), jnp.float32)
    encoder_down = noise(seeds[12], (FF_ENC, D_ENC), FF_ENC ** -0.5, 0.109375)
    encoder_down_bias = noise(seeds[13], (D_ENC,), 0.3, 1.75, (), jnp.float32)
    embed_weight = noise(seeds[14], (D_ENC, DECODER_WIDTH), D_ENC ** -0.5, 0.21875)
    embed_bias = noise(seeds[15], (DECODER_WIDTH,), 0.3, 1.75, (), jnp.float32)
    mask_token = noise(seeds[16], (DECODER_WIDTH,), 1.0, 6.0, (), jnp.float32)
    decoder_gain1 = jnp.clip(1.0 + 0.1 * jax.random.normal(seeds[17], (DECODER_WIDTH,), jnp.float32), 0.5, 1.5)
    decoder_bias1 = noise(seeds[18], (DECODER_WIDTH,), 0.3, 1.75, (), jnp.float32)
    decoder_qkv = noise(seeds[19], (DECODER_WIDTH, 3 * DECODER_WIDTH), DECODER_WIDTH ** -0.5, 0.25)
    decoder_out = noise(seeds[20], (DECODER_WIDTH, DECODER_WIDTH), (DECODER_WIDTH // PATCHES) ** -0.5, 3.0)
    decoder_out_bias = noise(seeds[21], (DECODER_WIDTH,), 0.3, 1.75, (), jnp.float32)
    decoder_gain2 = jnp.clip(1.0 + 0.1 * jax.random.normal(seeds[22], (DECODER_WIDTH,), jnp.float32), 0.5, 1.5)
    decoder_bias2 = noise(seeds[23], (DECODER_WIDTH,), 0.3, 1.75, (), jnp.float32)
    decoder_up = noise(seeds[24], (DECODER_WIDTH, FF_DEC), DECODER_WIDTH ** -0.5, 0.25)
    decoder_up_bias = noise(seeds[25], (FF_DEC,), 0.3, 1.75, (), jnp.float32)
    decoder_down = noise(seeds[26], (FF_DEC, DECODER_WIDTH), FF_DEC ** -0.5, 0.125)
    decoder_down_bias = noise(seeds[27], (DECODER_WIDTH,), 0.3, 1.75, (), jnp.float32)
    cotangent = bell_draw_with(seeds[28], (SAMPLES, PATCHES, DECODER_WIDTH), 1.0, 6.0, ((0, 16),), (0, 2, 16, 2.0))
    return dict(patches=patches, segment_ids=segment_ids, patch_order=patch_order, encoder_gain1=encoder_gain1, encoder_bias1=encoder_bias1, encoder_qkv=encoder_qkv, encoder_out=encoder_out, encoder_out_bias=encoder_out_bias, encoder_gain2=encoder_gain2, encoder_bias2=encoder_bias2, encoder_up=encoder_up, encoder_up_bias=encoder_up_bias, encoder_down=encoder_down, encoder_down_bias=encoder_down_bias, embed_weight=embed_weight, embed_bias=embed_bias, mask_token=mask_token, decoder_gain1=decoder_gain1, decoder_bias1=decoder_bias1, decoder_qkv=decoder_qkv, decoder_out=decoder_out, decoder_out_bias=decoder_out_bias, decoder_gain2=decoder_gain2, decoder_bias2=decoder_bias2, decoder_up=decoder_up, decoder_up_bias=decoder_up_bias, decoder_down=decoder_down, decoder_down_bias=decoder_down_bias, cotangent=cotangent)


HIGH_PRECISION = lax.Precision.HIGHEST
EPSILON = 1e-06
MASKED = -1e+30

@jax.custom_vjp
def low(v):
    return lax.optimization_barrier(v.astype(jnp.bfloat16)).astype(jnp.float32)

@jax.custom_vjp
def low_back(v):
    return v

def low_keep(v):
    return (low(v), None)

def low_pass(kept, grad):
    return (grad,)

def back_keep(v):
    return (v, None)

def back_low(kept, grad):
    return (low(grad),)
low.defvjp(low_keep, low_pass)
low_back.defvjp(back_keep, back_low)

def layer_norm(inputs, gain_vec, bias_vec):
    center = inputs - lax.optimization_barrier(jnp.mean(inputs, axis=-1, keepdims=True))
    spread = lax.optimization_barrier(jnp.mean(center * center, axis=-1, keepdims=True))
    return center * lax.rsqrt(spread + EPSILON) * gain_vec + bias_vec

def matmul(left_side, right_side):
    return jnp.einsum('...k,kn->...n', left_side, right_side, precision=HIGH_PRECISION)

def positions(count, features):
    place_col = jnp.arange(count, dtype=jnp.float32)[:, None]
    column = jnp.arange(features)
    rate_row = jnp.exp(-math.log(10000.0) * (2 * (column // 2)).astype(jnp.float32) / features)
    angles = place_col * rate_row[None, :]
    return jnp.where(column % 2 == 0, jnp.sin(angles), jnp.cos(angles))

def mixing(normed, w_qkv, w_out, b_out, allowed, head_count):
    batch_size, seq_len, features = normed.shape
    head_size = features // head_count
    joined = matmul(normed, w_qkv).reshape(batch_size, seq_len, 3, head_count, head_size)
    queries = low_back(low(joined[:, :, 0]))
    key_rows = low_back(low(joined[:, :, 1]))
    value_rows = low_back(low(joined[:, :, 2]))
    scores = low_back(jnp.einsum('bqhd,bkhd->bhqk', queries, key_rows, precision=HIGH_PRECISION) * head_size ** (-0.5))
    scores = jnp.where(allowed[:, None], scores, MASKED)
    attn_probs = low(jax.nn.softmax(scores, axis=-1))
    mixed = jnp.einsum('bhqk,bkhd->bqhd', attn_probs, value_rows, precision=HIGH_PRECISION).reshape(batch_size, seq_len, features)
    mixed = low_back(low(mixed))
    return low_back(matmul(mixed, w_out)) + b_out

def block(inputs, params, allowed, head_count):
    gain_a, bias_a, w_qkv, w_out, b_out, gain_b, bias_b, w_up, b_up, w_down, b_down = params
    normed = low(layer_norm(inputs, gain_a, bias_a))
    middle = inputs + mixing(normed, w_qkv, w_out, b_out, allowed, head_count)
    normed_b = low(layer_norm(middle, gain_b, bias_b))
    before = low_back(matmul(normed_b, w_up) + b_up)
    active = low(jax.nn.gelu(before))
    return middle + (low_back(matmul(active, w_down)) + b_down)

def slot_index(segments, order_rows):
    row_count = segments.shape[0]
    earlier = lax.optimization_barrier(jnp.sum((segments[None, :] < segments[:, None]).astype(jnp.int32), axis=1))
    rank_row = jnp.arange(row_count, dtype=jnp.int32) - earlier
    patch_num = order_rows[segments, rank_row]
    return segments * PATCHES + patch_num

def micro_step(rows_m, segments, order_rows, enc_params, embed_params, dec_params):
    allowed = (segments[:, None] == segments[None, :])[None]
    encoded = block(rows_m[None], enc_params, allowed, H_ENC)[0]
    boundary = low_back(low(encoded))
    embed_w, embed_b, mask_tok = embed_params
    patch_embedding = low_back(matmul(boundary, embed_w)) + embed_b
    slots = slot_index(segments, order_rows)
    one_hot_matrix = (jnp.arange(SAMP_MB * PATCHES, dtype=jnp.int32)[:, None] == slots[None, :]).astype(jnp.float32)
    filled = lax.optimization_barrier(jnp.sum(one_hot_matrix, axis=1))
    placed = jnp.dot(one_hot_matrix, patch_embedding, precision=HIGH_PRECISION) + (1.0 - filled)[:, None] * mask_tok
    tokens = placed.reshape(SAMP_MB, PATCHES, DECODER_WIDTH) + positions(PATCHES, DECODER_WIDTH)
    all_allowed = jnp.ones((SAMP_MB, PATCHES, PATCHES), dtype=bool)
    return block(tokens, dec_params, all_allowed, H_DEC)

def forward(rows_all, enc_params, embed_params, dec_params, segments, orders):

    def one_step(carried, inputs_m):
        rows_m, segments_m, order_m = inputs_m
        return (carried, micro_step(rows_m, segments_m, order_m, enc_params, embed_params, dec_params))
    _, outputs = lax.scan(jax.checkpoint(one_step), jnp.zeros((), jnp.float32), (rows_all.reshape(NUM_MB, ROWS_MB, D_ENC), segments, orders.reshape(NUM_MB, SAMP_MB, PATCHES)))
    return outputs.reshape(SAMPLES, PATCHES, DECODER_WIDTH)

def reference(patches, segment_ids, patch_order, encoder_gain1, encoder_bias1, encoder_qkv, encoder_out, encoder_out_bias, encoder_gain2, encoder_bias2, encoder_up, encoder_up_bias, encoder_down, encoder_down_bias, embed_weight, embed_bias, mask_token, decoder_gain1, decoder_bias1, decoder_qkv, decoder_out, decoder_out_bias, decoder_gain2, decoder_bias2, decoder_up, decoder_up_bias, decoder_down, decoder_down_bias, cotangent):
    widen = lambda leaf_value: leaf_value.astype(jnp.float32)
    enc_params = jax.tree.map(widen, (encoder_gain1, encoder_bias1, encoder_qkv, encoder_out, encoder_out_bias, encoder_gain2, encoder_bias2, encoder_up, encoder_up_bias, encoder_down, encoder_down_bias))
    embed_params = jax.tree.map(widen, (embed_weight, embed_bias, mask_token))
    dec_params = jax.tree.map(widen, (decoder_gain1, decoder_bias1, decoder_qkv, decoder_out, decoder_out_bias, decoder_gain2, decoder_bias2, decoder_up, decoder_up_bias, decoder_down, decoder_down_bias))

    def run_forward(rows_all, enc_set, embed_set, dec_set):
        return forward(rows_all, enc_set, embed_set, dec_set, segment_ids, patch_order)
    outputs, pullback = jax.vjp(run_forward, patches.astype(jnp.float32), enc_params, embed_params, dec_params)
    grad_rows, grad_enc, grad_embed, grad_dec = pullback(cotangent.astype(jnp.float32))
    return (outputs.astype(jnp.bfloat16), grad_rows.astype(jnp.bfloat16), grad_enc[0], grad_enc[1], grad_enc[2], grad_enc[3], grad_enc[4], grad_enc[5], grad_enc[6], grad_enc[7], grad_enc[8], grad_enc[9], grad_enc[10], grad_embed[0], grad_embed[1], grad_embed[2], grad_dec[0], grad_dec[1], grad_dec[2], grad_dec[3], grad_dec[4], grad_dec[5], grad_dec[6], grad_dec[7], grad_dec[8], grad_dec[9], grad_dec[10])
```

```python
import math

import jax
import jax.numpy as jnp
from jax import lax
from jax.sharding import PartitionSpec as P

H_ENC = 12
DECODER_WIDTH = 512
H_DEC = 16
PATCHES = 128
SAMP_MB = 12


HIGH_PRECISION = lax.Precision.HIGHEST
EPSILON = 1e-06
MASKED = -1e30


def swapped(block, axis, apart):
    count = lax.axis_size(axis)
    route = []
    for low in range(count):
        high = low | 1 << apart
        if high != low and high < count:
            route += [(low, high), (high, low)]
    return lax.ppermute(block, axis, route)


def layer_norm(inputs, gain_vec, bias_vec):
    center = inputs - jnp.mean(inputs, axis=-1, keepdims=True)
    spread = jnp.mean(center * center, axis=-1, keepdims=True)
    return center * lax.rsqrt(spread + EPSILON) * gain_vec + bias_vec


def positions(count, features):
    place_col = jnp.arange(count, dtype=jnp.float32)[:, None]
    column = jnp.arange(features)
    rate_row = jnp.exp(-math.log(10000.0) * (2 * (column // 2)).astype(jnp.float32) / features)
    angles = place_col * rate_row[None, :]
    return jnp.where(column % 2 == 0, jnp.sin(angles), jnp.cos(angles))


def project(left_side, right_side):
    return lax.dot_general(
        left_side,
        right_side,
        (((left_side.ndim - 1,), (0,)), ((), ())),
        preferred_element_type=jnp.float32,
    )


def project_back(grads, right_side):
    return lax.dot_general(
        grads, right_side, (((grads.ndim - 1,), (1,)), ((), ())), preferred_element_type=jnp.float32
    )


def weight_grad(left_side, grads):
    flat_left = left_side.reshape(-1, left_side.shape[-1])
    flat_grads = grads.reshape(-1, grads.shape[-1])
    return lax.dot_general(
        flat_left, flat_grads, (((0,), (0,)), ((), ())), preferred_element_type=jnp.float32
    )


def column_sum(grads):
    return jnp.sum(grads.reshape(-1, grads.shape[-1]).astype(jnp.float32), axis=0)


def attn_scores(query_rows, key_rows, allowed):
    scaling = query_rows.shape[-1] ** (-0.5)
    scores = (
        jnp.einsum("bqhd,bkhd->bhqk", query_rows, key_rows, preferred_element_type=jnp.float32)
        * scaling
    )
    if allowed is not None:
        scores = jnp.where(allowed[:, None], scores, MASKED)
    return scores


def attend(normed, w_qkv, allowed, head_count):
    batch_size, seq_len, features = normed.shape
    head_size = features // head_count
    joined = (
        project(normed, w_qkv)
        .astype(jnp.bfloat16)
        .reshape(batch_size, seq_len, 3, head_count, head_size)
    )
    query_rows = joined[:, :, 0]
    key_rows = joined[:, :, 1]
    value_rows = joined[:, :, 2]
    scores = attn_scores(query_rows, key_rows, allowed)
    row_max = jnp.max(scores, axis=-1, keepdims=True)
    exponent = jnp.exp(scores - row_max)
    row_sum = jnp.sum(exponent, axis=-1, keepdims=True)
    attn_probs = (exponent / row_sum).astype(jnp.bfloat16)
    mixed = jnp.einsum(
        "bhqk,bkhd->bqhd", attn_probs, value_rows, preferred_element_type=jnp.float32
    )
    mixed = mixed.astype(jnp.bfloat16).reshape(batch_size, seq_len, features)
    log_total = row_max + jnp.log(row_sum)
    return (mixed, (query_rows, key_rows, value_rows, log_total))


def attend_back(grad_mixed, kept, allowed):
    query_rows, key_rows, value_rows, log_total = kept
    batch_size, seq_len, head_count, head_size = query_rows.shape
    scaling = head_size ** (-0.5)
    grad_heads = grad_mixed.reshape(batch_size, seq_len, head_count, head_size)
    scores = attn_scores(query_rows, key_rows, allowed)
    probs_full = jnp.exp(scores - log_total)
    attn_probs = probs_full.astype(jnp.bfloat16)
    grad_value = jnp.einsum(
        "bhqk,bqhd->bkhd", attn_probs, grad_heads, preferred_element_type=jnp.float32
    ).astype(jnp.bfloat16)
    grad_probs = jnp.einsum(
        "bqhd,bkhd->bhqk", grad_heads, value_rows, preferred_element_type=jnp.float32
    )
    inner = jnp.sum(probs_full * grad_probs, axis=-1, keepdims=True)
    grad_scores = (probs_full * (grad_probs - inner)).astype(jnp.bfloat16)
    grad_query = (
        jnp.einsum("bhqk,bkhd->bqhd", grad_scores, key_rows, preferred_element_type=jnp.float32)
        * scaling
    ).astype(jnp.bfloat16)
    grad_key = (
        jnp.einsum("bhqk,bqhd->bkhd", grad_scores, query_rows, preferred_element_type=jnp.float32)
        * scaling
    ).astype(jnp.bfloat16)
    stacked = jnp.stack([grad_query, grad_key, grad_value], axis=2)
    return stacked.reshape(batch_size, seq_len, 3 * head_count * head_size)


def block_forward(inputs, params, allowed, head_count):
    gain_a, bias_a, w_qkv, w_out, b_out, gain_b, bias_b, w_up, b_up, w_down, b_down = params
    normed = layer_norm(inputs, gain_a, bias_a).astype(jnp.bfloat16)
    mixed, kept = attend(normed, w_qkv, allowed, head_count)
    middle = inputs + (project(mixed, w_out) + b_out)
    normed_b = layer_norm(middle, gain_b, bias_b).astype(jnp.bfloat16)
    before = project(normed_b, w_up) + b_up
    active = jax.nn.gelu(before).astype(jnp.bfloat16)
    output = middle + (project(active, w_down) + b_down)
    return (output, (inputs, normed, mixed, kept, middle, normed_b, before, active))


def block_backward(grad_out, params, saved, allowed):
    gain_a, bias_a, w_qkv, w_out, b_out, gain_b, bias_b, w_up, b_up, w_down, b_down = params
    inputs, normed, mixed, kept, middle, normed_b, before, active = saved
    grad_branch = grad_out.astype(jnp.bfloat16)
    grad_down = weight_grad(active, grad_branch)
    grad_bdown = column_sum(grad_out)
    _, gelu_pull = jax.vjp(jax.nn.gelu, before)
    grad_before = gelu_pull(project_back(grad_branch, w_down))[0].astype(jnp.bfloat16)
    grad_up = weight_grad(normed_b, grad_before)
    grad_bup = column_sum(grad_before)
    _, norm_pull = jax.vjp(layer_norm, middle, gain_b, bias_b)
    grad_middle, grad_gain_b, grad_bias_b = norm_pull(project_back(grad_before, w_up))
    grad_middle = grad_middle + grad_out
    grad_attn = grad_middle.astype(jnp.bfloat16)
    grad_wout = weight_grad(mixed, grad_attn)
    grad_bout = column_sum(grad_middle)
    grad_mixed = project_back(grad_attn, w_out).astype(jnp.bfloat16)
    grad_joined = attend_back(grad_mixed, kept, allowed)
    grad_qkv = weight_grad(normed, grad_joined)
    _, first_pull = jax.vjp(layer_norm, inputs, gain_a, bias_a)
    grad_inputs, grad_gain_a, grad_bias_a = first_pull(project_back(grad_joined, w_qkv))
    grad_inputs = grad_inputs + grad_middle
    return (
        grad_inputs,
        (
            grad_gain_a,
            grad_bias_a,
            grad_qkv,
            grad_wout,
            grad_bout,
            grad_gain_b,
            grad_bias_b,
            grad_up,
            grad_bup,
            grad_down,
            grad_bdown,
        ),
    )


def encoder_mask(segment_ids):
    microbatch_count = segment_ids.shape[0]
    labels = segment_ids + jnp.arange(microbatch_count, dtype=jnp.int32)[:, None] * SAMP_MB
    labels = labels.reshape(1, -1)
    return labels[:, :, None] == labels[:, None, :]


def slot_table(segment_ids, patch_order):
    microbatch_count, microbatch_rows = segment_ids.shape
    earlier = jnp.sum((segment_ids[:, None, :] < segment_ids[:, :, None]).astype(jnp.int32), axis=2)
    rank_row = jnp.arange(microbatch_rows, dtype=jnp.int32)[None, :] - earlier
    sample_num = segment_ids + jnp.arange(microbatch_count, dtype=jnp.int32)[:, None] * SAMP_MB
    patch_num = jnp.take(patch_order.reshape(-1), sample_num * PATCHES + rank_row)
    return segment_ids * PATCHES + patch_num


def encode(patches, enc_params, allowed):
    encoded, saved = block_forward(patches.astype(jnp.float32)[None], enc_params, allowed, H_ENC)
    return (encoded[0].astype(jnp.bfloat16), saved)


def encode_back(grad_boundary, enc_params, saved, allowed):
    grad_rows, enc_grads = block_backward(
        grad_boundary.astype(jnp.float32)[None], enc_params, saved, allowed
    )
    return (grad_rows[0].astype(jnp.bfloat16), enc_grads)


def decode_all(boundary, segment_ids, patch_order, embed_params, dec_params, cotangent):
    microbatch_count, microbatch_rows = segment_ids.shape
    embed_weight, embed_bias, mask_token = embed_params
    patch_embedding = project(boundary, embed_weight) + embed_bias
    slots = slot_table(segment_ids, patch_order)
    one_hot_matrix = (
        jnp.arange(SAMP_MB * PATCHES, dtype=jnp.int32)[None, :, None] == slots[:, None, :]
    ).astype(jnp.float32)
    filled = jnp.sum(one_hot_matrix, axis=2)
    placed = jnp.einsum(
        "vxn,vnp->vxp",
        one_hot_matrix,
        patch_embedding.reshape(microbatch_count, microbatch_rows, DECODER_WIDTH),
        precision=HIGH_PRECISION,
    )
    placed = placed + (1.0 - filled)[:, :, None] * mask_token
    tokens = placed.reshape(microbatch_count * SAMP_MB, PATCHES, DECODER_WIDTH) + positions(
        PATCHES, DECODER_WIDTH
    )
    output, saved = block_forward(tokens, dec_params, None, H_DEC)
    grad_tokens, dec_grads = block_backward(cotangent.astype(jnp.float32), dec_params, saved, None)
    grad_placed_tokens = grad_tokens.reshape(microbatch_count, SAMP_MB * PATCHES, DECODER_WIDTH)
    grad_patch_embedding = jnp.einsum(
        "thb,thl->tbl", one_hot_matrix, grad_placed_tokens, precision=HIGH_PRECISION
    ).reshape(-1, DECODER_WIDTH)
    grad_mask = jnp.sum((1.0 - filled)[:, :, None] * grad_placed_tokens, axis=(0, 1))
    grad_bias = jnp.sum(grad_patch_embedding, axis=0)
    low_embedded = grad_patch_embedding.astype(jnp.bfloat16)
    grad_weight = weight_grad(boundary, low_embedded)
    grad_boundary = project_back(low_embedded, embed_weight).astype(jnp.bfloat16)
    return (
        output.astype(jnp.bfloat16),
        grad_boundary,
        (grad_weight, grad_bias, grad_mask),
        dec_grads,
    )


def pack(grads_all, groups):
    flat = [g.reshape(groups, -1).astype(jnp.bfloat16) for g in grads_all]
    return jnp.concatenate(flat, axis=1)


def unpack(row, grads_all, groups):
    out, at = [], 0
    for g in grads_all:
        size = g.size // groups
        out.append(row[at : at + size].reshape((g.shape[0] // groups,) + g.shape[1:]))
        at += size
    return tuple(out)


def reduce_every(grads_all, section_index):
    groups = lax.axis_size("dp")
    packed = pack(grads_all, groups)
    half = packed.shape[1] // 2
    keep = lax.dynamic_slice_in_dim(packed, section_index * half, half, 1)
    give = lax.dynamic_slice_in_dim(packed, (1 - section_index) * half, half, 1)
    got = swapped(give, "section", 0)
    chip = (keep.astype(jnp.float32) + got.astype(jnp.float32)).astype(jnp.bfloat16)
    mine = lax.psum_scatter(chip, "dp", scatter_dimension=0, tiled=True)[0]
    other = swapped(mine, "section", 0)
    first = section_index == 0
    row = jnp.concatenate([jnp.where(first, mine, other), jnp.where(first, other, mine)])
    return unpack(row.astype(jnp.float32), grads_all, groups)


def shards(
    patches,
    segment_ids,
    patch_order,
    encoder_gain1,
    encoder_bias1,
    encoder_qkv,
    encoder_out,
    encoder_out_bias,
    encoder_gain2,
    encoder_bias2,
    encoder_up,
    encoder_up_bias,
    encoder_down,
    encoder_down_bias,
    embed_weight,
    embed_bias,
    mask_token,
    decoder_gain1,
    decoder_bias1,
    decoder_qkv,
    decoder_out,
    decoder_out_bias,
    decoder_gain2,
    decoder_bias2,
    decoder_up,
    decoder_up_bias,
    decoder_down,
    decoder_down_bias,
    cotangent,
):
    enc_params = (
        encoder_gain1,
        encoder_bias1,
        encoder_qkv,
        encoder_out,
        encoder_out_bias,
        encoder_gain2,
        encoder_bias2,
        encoder_up,
        encoder_up_bias,
        encoder_down,
        encoder_down_bias,
    )
    embed_params = (embed_weight, embed_bias, mask_token)
    dec_params = (
        decoder_gain1,
        decoder_bias1,
        decoder_qkv,
        decoder_out,
        decoder_out_bias,
        decoder_gain2,
        decoder_bias2,
        decoder_up,
        decoder_up_bias,
        decoder_down,
        decoder_down_bias,
    )
    section_index = lax.axis_index("section")
    first_section = section_index == 0

    def own(x):
        half = x.shape[0] // 2
        return lax.dynamic_slice_in_dim(x, section_index * half, half, 0)

    patches, segment_ids, patch_order, cotangent = map(
        own, (patches, segment_ids, patch_order, cotangent)
    )
    allowed = encoder_mask(segment_ids)
    encoded, saved = encode(patches, enc_params, allowed)
    decoded, grad_boundary, embed_grads, dec_grads = decode_all(
        encoded, segment_ids, patch_order, embed_params, dec_params, cotangent
    )
    grad_rows, enc_grads = encode_back(grad_boundary, enc_params, saved, allowed)
    patch_half = decoded.shape[1] // 2
    feature_half = grad_rows.shape[1] // 2

    def halves(x, half):
        keep = lax.dynamic_slice_in_dim(x, section_index * half, half, 1)
        give = lax.dynamic_slice_in_dim(x, (1 - section_index) * half, half, 1)
        return keep, give

    keep_decoded, give_decoded = halves(decoded, patch_half)
    keep_grad, give_grad = halves(grad_rows, feature_half)
    got_decoded, got_grad = swapped((give_decoded, give_grad), "section", 0)

    def joined(mine, other):
        return jnp.concatenate(
            [jnp.where(first_section, mine, other), jnp.where(first_section, other, mine)]
        )

    decoded = joined(keep_decoded, got_decoded)
    grad_rows = joined(keep_grad, got_grad)
    totals = reduce_every(enc_grads + embed_grads + dec_grads, section_index)
    return (
        decoded,
        grad_rows,
        totals[0],
        totals[1],
        totals[2],
        totals[3],
        totals[4],
        totals[5],
        totals[6],
        totals[7],
        totals[8],
        totals[9],
        totals[10],
        totals[11],
        totals[12],
        totals[13],
        totals[14],
        totals[15],
        totals[16],
        totals[17],
        totals[18],
        totals[19],
        totals[20],
        totals[21],
        totals[22],
        totals[23],
        totals[24],
    )


def solution(mesh):
    in_specs = (
        P("dp", None),
        P("dp", None),
        P("dp", None),
        P(),
        P(),
        P(),
        P(),
        P(),
        P(),
        P(),
        P(),
        P(),
        P(),
        P(),
        P(),
        P(),
        P(),
        P(),
        P(),
        P(),
        P(),
        P(),
        P(),
        P(),
        P(),
        P(),
        P(),
        P(),
        P("dp", None, None),
    )
    out_specs = (
        P("dp", "section", None),
        P("dp", "section"),
        P("dp"),
        P("dp"),
        P("dp", None),
        P("dp", None),
        P("dp"),
        P("dp"),
        P("dp"),
        P("dp", None),
        P("dp"),
        P("dp", None),
        P("dp"),
        P("dp", None),
        P("dp"),
        P("dp"),
        P("dp"),
        P("dp"),
        P("dp", None),
        P("dp", None),
        P("dp"),
        P("dp"),
        P("dp"),
        P("dp", None),
        P("dp"),
        P("dp", None),
        P("dp"),
    )
    return jax.shard_map(shards, mesh=mesh, in_specs=in_specs, out_specs=out_specs, check_vma=False)
```

```python
import functools
import math

import jax
import jax.numpy as jnp
from jax import lax
from jax.experimental import pallas as pl
from jax.experimental.pallas import tpu as pltpu
from jax.sharding import PartitionSpec as P

H_ENC = 12
DECODER_WIDTH = 512
H_DEC = 16
PATCHES = 128
SAMP_MB = 12


HIGH_PRECISION = lax.Precision.HIGHEST
EPSILON = 1e-06
MASKED = -1e30


def swapped(block, axis, apart):
    count = lax.axis_size(axis)
    route = []
    for low in range(count):
        high = low | 1 << apart
        if high != low and high < count:
            route += [(low, high), (high, low)]
    return lax.ppermute(block, axis, route)


def layer_norm(inputs, gain_vec, bias_vec):
    center = inputs - jnp.mean(inputs, axis=-1, keepdims=True)
    spread = jnp.mean(center * center, axis=-1, keepdims=True)
    return center * lax.rsqrt(spread + EPSILON) * gain_vec + bias_vec


def positions(count, features):
    place_col = jnp.arange(count, dtype=jnp.float32)[:, None]
    column = jnp.arange(features)
    rate_row = jnp.exp(-math.log(10000.0) * (2 * (column // 2)).astype(jnp.float32) / features)
    angles = place_col * rate_row[None, :]
    return jnp.where(column % 2 == 0, jnp.sin(angles), jnp.cos(angles))


def project(left_side, right_side):
    return lax.dot_general(
        left_side,
        right_side,
        (((left_side.ndim - 1,), (0,)), ((), ())),
        preferred_element_type=jnp.float32,
    )


def project_back(grads, right_side):
    return lax.dot_general(
        grads, right_side, (((grads.ndim - 1,), (1,)), ((), ())), preferred_element_type=jnp.float32
    )


def weight_grad(left_side, grads):
    flat_left = left_side.reshape(-1, left_side.shape[-1])
    flat_grads = grads.reshape(-1, grads.shape[-1])
    return lax.dot_general(
        flat_left, flat_grads, (((0,), (0,)), ((), ())), preferred_element_type=jnp.float32
    )


def column_sum(grads):
    return jnp.sum(grads.reshape(-1, grads.shape[-1]).astype(jnp.float32), axis=0)


def attn_scores(query_rows, key_rows, allowed):
    scaling = query_rows.shape[-1] ** (-0.5)
    scores = (
        jnp.einsum("bqhd,bkhd->bhqk", query_rows, key_rows, preferred_element_type=jnp.float32)
        * scaling
    )
    if allowed is not None:
        scores = jnp.where(allowed[:, None], scores, MASKED)
    return scores


def attend(normed, w_qkv, allowed, head_count):
    batch_size, seq_len, features = normed.shape
    head_size = features // head_count
    joined = (
        project(normed, w_qkv)
        .astype(jnp.bfloat16)
        .reshape(batch_size, seq_len, 3, head_count, head_size)
    )
    query_rows = joined[:, :, 0]
    key_rows = joined[:, :, 1]
    value_rows = joined[:, :, 2]
    scores = attn_scores(query_rows, key_rows, allowed)
    row_max = jnp.max(scores, axis=-1, keepdims=True)
    exponent = jnp.exp(scores - row_max)
    row_sum = jnp.sum(exponent, axis=-1, keepdims=True)
    attn_probs = (exponent / row_sum).astype(jnp.bfloat16)
    mixed = jnp.einsum(
        "bhqk,bkhd->bqhd", attn_probs, value_rows, preferred_element_type=jnp.float32
    )
    mixed = mixed.astype(jnp.bfloat16).reshape(batch_size, seq_len, features)
    log_total = row_max + jnp.log(row_sum)
    return (mixed, (query_rows, key_rows, value_rows, log_total))


def attend_back(grad_mixed, kept, allowed):
    query_rows, key_rows, value_rows, log_total = kept
    batch_size, seq_len, head_count, head_size = query_rows.shape
    scaling = head_size ** (-0.5)
    grad_heads = grad_mixed.reshape(batch_size, seq_len, head_count, head_size)
    scores = attn_scores(query_rows, key_rows, allowed)
    probs_full = jnp.exp(scores - log_total)
    attn_probs = probs_full.astype(jnp.bfloat16)
    grad_value = jnp.einsum(
        "bhqk,bqhd->bkhd", attn_probs, grad_heads, preferred_element_type=jnp.float32
    ).astype(jnp.bfloat16)
    grad_probs = jnp.einsum(
        "bqhd,bkhd->bhqk", grad_heads, value_rows, preferred_element_type=jnp.float32
    )
    inner = jnp.sum(probs_full * grad_probs, axis=-1, keepdims=True)
    grad_scores = (probs_full * (grad_probs - inner)).astype(jnp.bfloat16)
    grad_query = (
        jnp.einsum("bhqk,bkhd->bqhd", grad_scores, key_rows, preferred_element_type=jnp.float32)
        * scaling
    ).astype(jnp.bfloat16)
    grad_key = (
        jnp.einsum("bhqk,bqhd->bkhd", grad_scores, query_rows, preferred_element_type=jnp.float32)
        * scaling
    ).astype(jnp.bfloat16)
    stacked = jnp.stack([grad_query, grad_key, grad_value], axis=2)
    return stacked.reshape(batch_size, seq_len, 3 * head_count * head_size)


def block_forward(inputs, params, allowed, head_count):
    gain_a, bias_a, w_qkv, w_out, b_out, gain_b, bias_b, w_up, b_up, w_down, b_down = params
    normed = layer_norm(inputs, gain_a, bias_a).astype(jnp.bfloat16)
    mixed, kept = attend(normed, w_qkv, allowed, head_count)
    middle = inputs + (project(mixed, w_out) + b_out)
    normed_b = layer_norm(middle, gain_b, bias_b).astype(jnp.bfloat16)
    before = project(normed_b, w_up) + b_up
    active = jax.nn.gelu(before).astype(jnp.bfloat16)
    output = middle + (project(active, w_down) + b_down)
    return (output, (inputs, normed, mixed, kept, middle, normed_b, before, active))


def block_backward(grad_out, params, saved, allowed):
    gain_a, bias_a, w_qkv, w_out, b_out, gain_b, bias_b, w_up, b_up, w_down, b_down = params
    inputs, normed, mixed, kept, middle, normed_b, before, active = saved
    grad_branch = grad_out.astype(jnp.bfloat16)
    grad_down = weight_grad(active, grad_branch)
    grad_bdown = column_sum(grad_out)
    _, gelu_pull = jax.vjp(jax.nn.gelu, before)
    grad_before = gelu_pull(project_back(grad_branch, w_down))[0].astype(jnp.bfloat16)
    grad_up = weight_grad(normed_b, grad_before)
    grad_bup = column_sum(grad_before)
    _, norm_pull = jax.vjp(layer_norm, middle, gain_b, bias_b)
    grad_middle, grad_gain_b, grad_bias_b = norm_pull(project_back(grad_before, w_up))
    grad_middle = grad_middle + grad_out
    grad_attn = grad_middle.astype(jnp.bfloat16)
    grad_wout = weight_grad(mixed, grad_attn)
    grad_bout = column_sum(grad_middle)
    grad_mixed = project_back(grad_attn, w_out).astype(jnp.bfloat16)
    grad_joined = attend_back(grad_mixed, kept, allowed)
    grad_qkv = weight_grad(normed, grad_joined)
    _, first_pull = jax.vjp(layer_norm, inputs, gain_a, bias_a)
    grad_inputs, grad_gain_a, grad_bias_a = first_pull(project_back(grad_joined, w_qkv))
    grad_inputs = grad_inputs + grad_middle
    return (
        grad_inputs,
        (
            grad_gain_a,
            grad_bias_a,
            grad_qkv,
            grad_wout,
            grad_bout,
            grad_gain_b,
            grad_bias_b,
            grad_up,
            grad_bup,
            grad_down,
            grad_bdown,
        ),
    )


def encoder_mask(segment_ids):
    microbatch_count = segment_ids.shape[0]
    labels = segment_ids + jnp.arange(microbatch_count, dtype=jnp.int32)[:, None] * SAMP_MB
    labels = labels.reshape(1, -1)
    return labels[:, :, None] == labels[:, None, :]


def slot_table(segment_ids, patch_order):
    microbatch_count, microbatch_rows = segment_ids.shape
    earlier = jnp.sum((segment_ids[:, None, :] < segment_ids[:, :, None]).astype(jnp.int32), axis=2)
    rank_row = jnp.arange(microbatch_rows, dtype=jnp.int32)[None, :] - earlier
    sample_num = segment_ids + jnp.arange(microbatch_count, dtype=jnp.int32)[:, None] * SAMP_MB
    patch_num = jnp.take(patch_order.reshape(-1), sample_num * PATCHES + rank_row)
    return segment_ids * PATCHES + patch_num


def encode(patches, enc_params, allowed):
    encoded, saved = block_forward(patches.astype(jnp.float32)[None], enc_params, allowed, H_ENC)
    return (encoded[0].astype(jnp.bfloat16), saved)


def encode_back(grad_boundary, enc_params, saved, allowed):
    grad_rows, enc_grads = block_backward(
        grad_boundary.astype(jnp.float32)[None], enc_params, saved, allowed
    )
    return (grad_rows[0].astype(jnp.bfloat16), enc_grads)


def decode_all(boundary, segment_ids, patch_order, embed_params, dec_params, cotangent):
    microbatch_count, microbatch_rows = segment_ids.shape
    embed_weight, embed_bias, mask_token = embed_params
    patch_embedding = project(boundary, embed_weight) + embed_bias
    slots = slot_table(segment_ids, patch_order)
    one_hot_matrix = (
        jnp.arange(SAMP_MB * PATCHES, dtype=jnp.int32)[None, :, None] == slots[:, None, :]
    ).astype(jnp.float32)
    filled = jnp.sum(one_hot_matrix, axis=2)
    placed = jnp.einsum(
        "vxn,vnp->vxp",
        one_hot_matrix,
        patch_embedding.reshape(microbatch_count, microbatch_rows, DECODER_WIDTH),
        precision=HIGH_PRECISION,
    )
    placed = placed + (1.0 - filled)[:, :, None] * mask_token
    tokens = placed.reshape(microbatch_count * SAMP_MB, PATCHES, DECODER_WIDTH) + positions(
        PATCHES, DECODER_WIDTH
    )
    output, saved = block_forward(tokens, dec_params, None, H_DEC)
    grad_tokens, dec_grads = block_backward(cotangent.astype(jnp.float32), dec_params, saved, None)
    grad_placed_tokens = grad_tokens.reshape(microbatch_count, SAMP_MB * PATCHES, DECODER_WIDTH)
    grad_patch_embedding = jnp.einsum(
        "thb,thl->tbl", one_hot_matrix, grad_placed_tokens, precision=HIGH_PRECISION
    ).reshape(-1, DECODER_WIDTH)
    grad_mask = jnp.sum((1.0 - filled)[:, :, None] * grad_placed_tokens, axis=(0, 1))
    grad_bias = jnp.sum(grad_patch_embedding, axis=0)
    low_embedded = grad_patch_embedding.astype(jnp.bfloat16)
    grad_weight = weight_grad(boundary, low_embedded)
    grad_boundary = project_back(low_embedded, embed_weight).astype(jnp.bfloat16)
    return (
        output.astype(jnp.bfloat16),
        grad_boundary,
        (grad_weight, grad_bias, grad_mask),
        dec_grads,
    )


MESH = pl.DeviceIdType.MESH


class Chunk:
    def __init__(self, array, offset, width, x_first):
        self.array, self.offset, self.width, self.x_first = array, offset, width, x_first


def plan_chunks(shapes, widths):
    chunks = []
    for j, (shape, width) in enumerate(zip(shapes, widths)):
        half = shape[1] // 2
        for offset in range(0, half, width):
            chunks.append(Chunk(j, offset, width, len(chunks) % 2 == 0))
    return chunks


def reduce_kernel(chunks, n_arrays, *refs):
    ins, outs = refs[:n_arrays], refs[n_arrays : 2 * n_arrays]
    n = len(chunks)
    scratch = refs[2 * n_arrays :]
    own, recv0, recv1, recv2, recv3, fin, recv4 = (scratch[i * n : (i + 1) * n] for i in range(7))
    local_sem, send_sem, recv_sem = scratch[7 * n :]
    s = lax.axis_index("section")
    d = lax.axis_index("dp")
    z, y, x = d // 4, (d // 2) % 2, d % 2
    x_peer, y_peer = d + 1 - 2 * x, d + 2 - 4 * y
    z_peers = [lax.rem(z + k, 4) for k in (1, 2, 3)]

    barrier = pltpu.get_barrier_semaphore()
    pl.semaphore_signal(barrier, inc=1, device_id={"section": 1 - s}, device_id_type=MESH)
    for peer in [x_peer, y_peer] + [d + 4 * (p - z) for p in z_peers]:
        pl.semaphore_signal(barrier, inc=1, device_id={"dp": peer}, device_id_type=MESH)
    pl.semaphore_wait(barrier, 6)

    def remote(src, dst, c, slot, peer):
        return pltpu.make_async_remote_copy(
            src_ref=src,
            dst_ref=dst,
            send_sem=send_sem.at[c, slot],
            recv_sem=recv_sem.at[c, slot],
            device_id=peer,
            device_id_type=MESH,
        )

    def columns(c, side):
        chunk = chunks[c]
        half = ins[chunk.array].shape[-1] // 2
        return pl.ds(pl.multiple_of(side * half + chunk.offset, 128), chunk.width)

    copies = [dict() for _ in range(n)]

    def stage0(c):
        src = ins[chunks[c].array]
        away = remote(src.at[:, :, :, :, columns(c, 1 - s)], recv0[c], c, 0, {"section": 1 - s})
        away.start()
        here = pltpu.make_async_copy(src.at[:, :, :, :, columns(c, s)], own[c], local_sem.at[c])
        here.start()
        copies[c].update(here=here, p0=away)

    def stage1(c):
        copies[c]["here"].wait()
        copies[c]["p0"].wait_recv()

        def add(t, carry):
            at = (t // 4, (t // 2) % 2, t % 2)
            own[c][at] = own[c][at] + recv0[c][at]
            return carry

        lax.fori_loop(0, 16, add, 0)
        if chunks[c].x_first:
            p1 = remote(own[c].at[:, :, 1 - x], recv1[c], c, 1, {"dp": x_peer})
        else:
            p1 = remote(own[c].at[:, 1 - y], recv1[c], c, 1, {"dp": y_peer})
        p1.start()
        copies[c]["p1"] = p1

    def stage2(c):
        copies[c]["p1"].wait_recv()
        x_first = chunks[c].x_first

        def add(t, carry):
            at = (t // 2, t % 2, x) if x_first else (t // 2, y, t % 2)
            own[c][at] = own[c][at] + recv1[c][t // 2, t % 2]
            return carry

        lax.fori_loop(0, 8, add, 0)
        if x_first:
            p2 = remote(own[c].at[:, 1 - y, x], recv2[c], c, 2, {"dp": y_peer})
        else:
            p2 = remote(own[c].at[:, y, 1 - x], recv2[c], c, 2, {"dp": x_peer})
        p2.start()
        copies[c]["p2"] = p2

    def stage3(c):
        copies[c]["p2"].wait_recv()

        def add(t, carry):
            own[c][t, y, x] = own[c][t, y, x] + recv2[c][t]
            return carry

        lax.fori_loop(0, 4, add, 0)
        for k, peer in enumerate(z_peers):
            p3 = remote(own[c].at[peer, y, x], recv3[c].at[k], c, 3 + k, {"dp": d + 4 * (peer - z)})
            p3.start()
            copies[c]["p3", k] = p3

    def stage4(c):
        for k in range(3):
            copies[c]["p3", k].wait_recv()
        total = own[c][z, y, x].astype(jnp.float32)
        for k in range(3):
            total = total + recv3[c][k].astype(jnp.float32)
        fin[c][...] = total.astype(jnp.bfloat16)
        p4 = remote(fin[c], recv4[c], c, 6, {"section": 1 - s})
        p4.start()
        copies[c]["p4"] = p4

    def stage5(c):
        copies[c]["p4"].wait_recv()
        out = outs[chunks[c].array]
        out[:, columns(c, s)] = fin[c][...].astype(jnp.float32)
        out[:, columns(c, 1 - s)] = recv4[c][...].astype(jnp.float32)

    pairs = [list(range(i, min(i + 2, n))) for i in range(0, n, 2)]
    stages = (stage1, stage2, stage3, stage4, stage5)
    ahead = 2
    for pair in pairs[:ahead]:
        for c in pair:
            stage0(c)
    for step in range(len(pairs) + len(stages) - 1):
        if step + ahead < len(pairs):
            for c in pairs[step + ahead]:
                stage0(c)
        for k, stage in enumerate(stages):
            if 0 <= step - k < len(pairs):
                for c in pairs[step - k]:
                    stage(c)
    for c in range(n):
        for copy in [copies[c][name] for name in ("p0", "p1", "p2", "p4")] + [
            copies[c]["p3", k] for k in range(3)
        ]:
            copy.wait_send()


def reduce_arrays(arrays, widths, collective_id):
    shapes = [a.shape for a in arrays]
    chunks = plan_chunks(shapes, widths)
    blocks = [(shapes[c.array][0] // 16, c.width) for c in chunks]
    bf16 = jnp.bfloat16

    def buffers(*lead):
        return [pltpu.VMEM(lead + block, bf16) for block in blocks]

    n = len(chunks)
    return pl.pallas_call(
        functools.partial(reduce_kernel, chunks, len(arrays)),
        out_shape=[jax.ShapeDtypeStruct((r // 16, w), jnp.float32) for r, w in shapes],
        in_specs=[pl.BlockSpec(memory_space=pl.ANY)] * len(arrays),
        out_specs=[pl.BlockSpec(memory_space=pltpu.VMEM)] * len(arrays),
        scratch_shapes=buffers(4, 2, 2)
        + buffers(4, 2, 2)
        + buffers(4, 2)
        + buffers(4)
        + buffers(3)
        + buffers()
        + buffers()
        + [
            pltpu.SemaphoreType.DMA((n,)),
            pltpu.SemaphoreType.DMA((n, 7)),
            pltpu.SemaphoreType.DMA((n, 7)),
        ],
        compiler_params=pltpu.CompilerParams(
            collective_id=collective_id, has_side_effects=True, vmem_limit_bytes=56 * 2**20
        ),
        name="reduce_gradients",
    )(*[a.reshape(4, 2, 2, a.shape[0] // 16, a.shape[1]) for a in arrays])


def reduce_plain(arrays, section_index):
    first = section_index == 0
    results = []
    for a in arrays:
        half = a.shape[1] // 2
        keep = lax.dynamic_slice_in_dim(a, section_index * half, half, 1)
        give = lax.dynamic_slice_in_dim(a, (1 - section_index) * half, half, 1)
        got = swapped(give, "section", 0)
        chip = (keep.astype(jnp.float32) + got.astype(jnp.float32)).astype(jnp.bfloat16)
        mine = lax.psum_scatter(chip, "dp", scatter_dimension=0, tiled=True)
        other = swapped(mine, "section", 0)
        whole = jnp.concatenate(
            [jnp.where(first, mine, other), jnp.where(first, other, mine)], axis=1
        )
        results.append(whole.astype(jnp.float32))
    return results


SMALL_ROWS, SMALL_COLUMNS = 16, 256


def reduce_every(grads_all, section_index):
    groups = lax.axis_size("dp")
    big = [g for g in grads_all if g.ndim == 2]
    small = [g for g in grads_all if g.ndim == 1]
    flat = jnp.concatenate([g.reshape(groups, -1) for g in small], axis=1)
    room = SMALL_ROWS * SMALL_COLUMNS
    flat = jnp.pad(flat, ((0, 0), (0, room - flat.shape[1])))
    packed = flat.reshape(groups * SMALL_ROWS, SMALL_COLUMNS).astype(jnp.bfloat16)
    arrays = [g.astype(jnp.bfloat16) for g in big] + [packed]
    if groups == 16:
        widths = [CHUNK_WIDTHS[a.shape] for a in arrays]
        results = reduce_arrays(arrays, widths, 1)
    else:
        results = reduce_plain(arrays, section_index)
    row = results[-1].reshape(-1)
    results = list(results[:-1])
    totals, at = [], 0
    for g in grads_all:
        if g.ndim == 2:
            totals.append(results.pop(0))
        else:
            size = g.shape[0] // groups
            totals.append(row[at : at + size])
            at += size
    return totals


CHUNK_WIDTHS = {
    (768, 2304): 384,
    (768, 768): 384,
    (768, 3072): 384,
    (3072, 768): 128,
    (768, 512): 256,
    (512, 1536): 384,
    (512, 512): 256,
    (512, 2048): 512,
    (2048, 512): 128,
    (256, 256): 128,
}


def shards(
    patches,
    segment_ids,
    patch_order,
    encoder_gain1,
    encoder_bias1,
    encoder_qkv,
    encoder_out,
    encoder_out_bias,
    encoder_gain2,
    encoder_bias2,
    encoder_up,
    encoder_up_bias,
    encoder_down,
    encoder_down_bias,
    embed_weight,
    embed_bias,
    mask_token,
    decoder_gain1,
    decoder_bias1,
    decoder_qkv,
    decoder_out,
    decoder_out_bias,
    decoder_gain2,
    decoder_bias2,
    decoder_up,
    decoder_up_bias,
    decoder_down,
    decoder_down_bias,
    cotangent,
):
    enc_params = (
        encoder_gain1,
        encoder_bias1,
        encoder_qkv,
        encoder_out,
        encoder_out_bias,
        encoder_gain2,
        encoder_bias2,
        encoder_up,
        encoder_up_bias,
        encoder_down,
        encoder_down_bias,
    )
    embed_params = (embed_weight, embed_bias, mask_token)
    dec_params = (
        decoder_gain1,
        decoder_bias1,
        decoder_qkv,
        decoder_out,
        decoder_out_bias,
        decoder_gain2,
        decoder_bias2,
        decoder_up,
        decoder_up_bias,
        decoder_down,
        decoder_down_bias,
    )
    section_index = lax.axis_index("section")
    first_section = section_index == 0

    def own(x):
        half = x.shape[0] // 2
        return lax.dynamic_slice_in_dim(x, section_index * half, half, 0)

    patches, segment_ids, patch_order, cotangent = map(
        own, (patches, segment_ids, patch_order, cotangent)
    )
    allowed = encoder_mask(segment_ids)
    encoded, saved = encode(patches, enc_params, allowed)
    decoded, grad_boundary, embed_grads, dec_grads = decode_all(
        encoded, segment_ids, patch_order, embed_params, dec_params, cotangent
    )
    grad_rows, enc_grads = encode_back(grad_boundary, enc_params, saved, allowed)
    patch_half = decoded.shape[1] // 2
    feature_half = grad_rows.shape[1] // 2

    def halves(x, half):
        keep = lax.dynamic_slice_in_dim(x, section_index * half, half, 1)
        give = lax.dynamic_slice_in_dim(x, (1 - section_index) * half, half, 1)
        return keep, give

    keep_decoded, give_decoded = halves(decoded, patch_half)
    keep_grad, give_grad = halves(grad_rows, feature_half)
    got_decoded, got_grad = swapped((give_decoded, give_grad), "section", 0)

    def joined(mine, other):
        return jnp.concatenate(
            [jnp.where(first_section, mine, other), jnp.where(first_section, other, mine)]
        )

    decoded = joined(keep_decoded, got_decoded)
    grad_rows = joined(keep_grad, got_grad)
    totals = reduce_every(enc_grads + embed_grads + dec_grads, section_index)
    return (
        decoded,
        grad_rows,
        totals[0],
        totals[1],
        totals[2],
        totals[3],
        totals[4],
        totals[5],
        totals[6],
        totals[7],
        totals[8],
        totals[9],
        totals[10],
        totals[11],
        totals[12],
        totals[13],
        totals[14],
        totals[15],
        totals[16],
        totals[17],
        totals[18],
        totals[19],
        totals[20],
        totals[21],
        totals[22],
        totals[23],
        totals[24],
    )


def solution(mesh):
    in_specs = (
        P("dp", None),
        P("dp", None),
        P("dp", None),
        P(),
        P(),
        P(),
        P(),
        P(),
        P(),
        P(),
        P(),
        P(),
        P(),
        P(),
        P(),
        P(),
        P(),
        P(),
        P(),
        P(),
        P(),
        P(),
        P(),
        P(),
        P(),
        P(),
        P(),
        P(),
        P("dp", None, None),
    )
    out_specs = (
        P("dp", "section", None),
        P("dp", "section"),
        P("dp"),
        P("dp"),
        P("dp", None),
        P("dp", None),
        P("dp"),
        P("dp"),
        P("dp"),
        P("dp", None),
        P("dp"),
        P("dp", None),
        P("dp"),
        P("dp", None),
        P("dp"),
        P("dp"),
        P("dp"),
        P("dp"),
        P("dp", None),
        P("dp", None),
        P("dp"),
        P("dp"),
        P("dp"),
        P("dp", None),
        P("dp"),
        P("dp", None),
        P("dp"),
    )
    return jax.shard_map(shards, mesh=mesh, in_specs=in_specs, out_specs=out_specs, check_vma=False)
```

```python
import functools
import math

import jax
import jax.numpy as jnp
from jax import lax
from jax.experimental import pallas as pl
from jax.experimental.pallas import tpu as pltpu
from jax.sharding import PartitionSpec as P

H_ENC = 12
DECODER_WIDTH = 512
H_DEC = 16
PATCHES = 128
SAMP_MB = 12


EPSILON = 1e-06
MASKED = -1e30


def swapped(block, axis, apart):
    count = lax.axis_size(axis)
    route = []
    for low in range(count):
        high = low | 1 << apart
        if high != low and high < count:
            route += [(low, high), (high, low)]
    return lax.ppermute(block, axis, route)


def positions(count, features):
    place_col = jnp.arange(count, dtype=jnp.float32)[:, None]
    column = jnp.arange(features)
    rate_row = jnp.exp(-math.log(10000.0) * (2 * (column // 2)).astype(jnp.float32) / features)
    angles = place_col * rate_row[None, :]
    return jnp.where(column % 2 == 0, jnp.sin(angles), jnp.cos(angles))


def weight_grad(left_side, grads):
    return lax.dot_general(
        left_side, grads, (((0,), (0,)), ((), ())), preferred_element_type=jnp.float32
    ).astype(jnp.bfloat16)


BF16 = jnp.bfloat16
F32 = jnp.float32


def mm(left, right):
    return lax.dot_general(left, right, (((1,), (0,)), ((), ())), preferred_element_type=F32)


def mm_nt(left, right):
    return lax.dot_general(left, right, (((1,), (1,)), ((), ())), preferred_element_type=F32)


def mm_tn(left, right):
    return lax.dot_general(left, right, (((0,), (0,)), ((), ())), preferred_element_type=F32)


def normalise(x):
    center = x - jnp.mean(x, axis=-1, keepdims=True)
    scale = lax.rsqrt(jnp.mean(center * center, axis=-1, keepdims=True) + EPSILON)
    return center * scale, scale


def normalise_back(grad, n, scale, gain):
    gn = grad * gain
    mean_gn = jnp.mean(gn, axis=-1, keepdims=True)
    mean_gnn = jnp.mean(gn * n, axis=-1, keepdims=True)
    return (gn - mean_gn - n * mean_gnn) * scale


def rows_sum(x):
    return jnp.sum(x, axis=0, keepdims=True)


def gelu_both(f):
    c0, c1 = math.sqrt(2.0 / math.pi), 0.044715
    square = f * f
    t = jnp.tanh(c0 * f * (1.0 + c1 * square))
    half = 0.5 * (1.0 + t)
    slope = half + (0.5 * c0) * f * (1.0 - t * t) * (1.0 + 3.0 * c1 * square)
    return f * half, slope


def lane_masks(head_size):
    lane = lax.broadcasted_iota(jnp.int32, (1, 128), 1)
    return [
        jnp.where((lane >= h * head_size) & (lane < (h + 1) * head_size), 1.0, 0.0).astype(BF16)
        for h in range(128 // head_size)
    ]


def stacked(x, masks):
    return jnp.concatenate([x * m for m in masks], axis=0)


def stacked_ones(x, masks, value):
    return jnp.concatenate(
        [jnp.broadcast_to(m * jnp.asarray(value, BF16), x.shape) for m in masks], axis=0
    )


def attention_forward(qkv_ref, o_ref, e_ref, rl_ref, rows, tokens, features, head_size, allowed):
    masks = lane_masks(head_size)
    per_group = len(masks)
    factor = head_size ** (-0.5) * math.log2(math.e)
    for g in range(features // 128):
        q, k, v = (qkv_ref[rows, j * features + g * 128 : j * features + (g + 1) * 128] for j in range(3))
        scores = mm_nt(q, stacked(k, masks))
        parts = []
        for h in range(per_group):
            part = scores[:, h * tokens : (h + 1) * tokens]
            if allowed is not None:
                part = jnp.where(allowed, part, MASKED)
            top = jnp.max(part, axis=-1, keepdims=True)
            parts.append(jnp.exp2((part - top) * factor).astype(BF16))
        e = jnp.concatenate(parts, axis=1)
        width = per_group * tokens
        e_ref[rows, g * width : (g + 1) * width] = e
        both = mm(e, jnp.concatenate([stacked(v, masks), stacked_ones(v, masks, 1.0)], axis=1))
        rl = 1.0 / both[:, 128:]
        rl_ref[rows, g * 128 : (g + 1) * 128] = rl
        o_ref[rows, g * 128 : (g + 1) * 128] = (both[:, :128] * rl).astype(BF16)


def attention_backward(
    qkv_ref, go_ref, o_ref, e_ref, rl_ref, gqkv_ref, rows, tokens, features, head_size
):
    masks = lane_masks(head_size)
    per_group = len(masks)
    scaling = head_size ** (-0.5)
    for g in range(features // 128):
        at = slice(g * 128, (g + 1) * 128)
        q, k, v = (qkv_ref[rows, j * features + g * 128 : j * features + (g + 1) * 128] for j in range(3))
        width = per_group * tokens
        e = e_ref[rows, g * width : (g + 1) * width]
        go = go_ref[rows, at].astype(F32) * rl_ref[rows, at]
        go_low = go.astype(BF16)
        inner = (go * o_ref[rows, at].astype(F32)).astype(BF16)
        left = jnp.concatenate([go_low, inner], axis=1)
        right = jnp.concatenate([stacked(v, masks), stacked_ones(v, masks, -1.0)], axis=1)
        gs = (e.astype(F32) * mm_nt(left, right)).astype(BF16)
        gq = mm(gs, stacked(k, masks)) * scaling
        gqkv_ref[rows, at] = gq.astype(BF16)

        def diagonal(wide):
            return jnp.concatenate(
                [
                    wide[h * head_size : (h + 1) * head_size, h * tokens : (h + 1) * tokens]
                    for h in range(per_group)
                ],
                axis=0,
            )

        gk = jnp.transpose(diagonal(mm_tn(q, gs)) * scaling)
        gqkv_ref[rows, features + g * 128 : features + (g + 1) * 128] = gk.astype(BF16)
        gv = jnp.transpose(diagonal(mm_tn(go_low, e)))
        gqkv_ref[rows, 2 * features + g * 128 : 2 * features + (g + 1) * 128] = gv.astype(BF16)


def feed_forward(c_ref, up_ref, bup_ref, u_ref, slope_ref, tile):
    def step(t, carry):
        at = pl.ds(pl.multiple_of(t * tile, tile), tile)
        f = mm(c_ref[...], up_ref[:, at]) + bup_ref[:, at]
        u, slope = gelu_both(f)
        u_ref[:, at] = u.astype(BF16)
        slope_ref[:, at] = slope.astype(BF16)
        return carry

    lax.fori_loop(0, up_ref.shape[1] // tile, step, 0)


def feed_forward_back(gm_ref, down_ref, slope_ref, gf_ref, gbup_ref, tile):
    def step(t, carry):
        at = pl.ds(pl.multiple_of(t * tile, tile), tile)
        gu = mm_nt(gm_ref[...], down_ref[at, :])
        gf = (gu * slope_ref[:, at].astype(F32)).astype(BF16)
        gf_ref[:, at] = gf
        gbup_ref[:, at] += rows_sum(gf.astype(F32))
        return carry

    lax.fori_loop(0, down_ref.shape[0] // tile, step, 0)


def encoder_forward_kernel(
    x_ref, seg_col_ref, seg_row_ref,
    gain1, bias1, w_qkv, w_out, b_out, gain2, bias2, w_up, b_up, w_down, b_down,
    y_ref, a_ref, qkv_ref, e_ref, rl_ref, o_ref, n2_ref, s2_ref, c_ref, u_ref, slope_ref,
    h_ref,
):
    rows = slice(None)
    tokens, features = x_ref.shape
    n1, _ = normalise(x_ref[...].astype(F32))
    a_ref[...] = (n1 * gain1[...] + bias1[...]).astype(BF16)
    qkv_ref[...] = mm(a_ref[...], w_qkv[...]).astype(BF16)
    allowed = seg_col_ref[...] == seg_row_ref[...]
    attention_forward(
        qkv_ref, o_ref, e_ref, rl_ref, rows, tokens, features, features // H_ENC, allowed
    )
    h_ref[...] = x_ref[...].astype(F32) + (mm(o_ref[...], w_out[...]) + b_out[...])
    n2, s2 = normalise(h_ref[...])
    n2_ref[...] = n2
    s2_ref[...] = s2
    c_ref[...] = (n2 * gain2[...] + bias2[...]).astype(BF16)
    feed_forward(c_ref, w_up, b_up, u_ref, slope_ref, 512)
    y_ref[...] = (h_ref[...] + (mm(u_ref[...], w_down[...]) + b_down[...])).astype(BF16)


def encoder_backward_kernel(
    x_ref, gy_ref, qkv_ref, e_ref, rl_ref, o_ref, n2_ref, s2_ref, slope_ref,
    gain1, w_qkv, w_out, gain2, w_up, w_down,
    gx_ref, gf_ref, ga_ref, gqkv_ref, small_ref, gbup_ref,
    gh_ref, go_ref,
):
    tokens, features = x_ref.shape
    gbup_ref[...] = jnp.zeros_like(gbup_ref)
    feed_forward_back(gy_ref, w_down, slope_ref, gf_ref, gbup_ref, 512)
    gc = mm_nt(gf_ref[...], w_up[...])
    g = gy_ref[...].astype(F32)
    n2 = n2_ref[...]
    gh = g + normalise_back(gc, n2, s2_ref[...], gain2[...])
    gh_ref[...] = gh
    ga_ref[...] = gh.astype(BF16)
    small_ref[2:3, :] = rows_sum(gh)
    small_ref[3:4, :] = rows_sum(gc * n2)
    small_ref[4:5, :] = rows_sum(gc)
    small_ref[5:6, :] = rows_sum(g)
    go_ref[...] = mm_nt(ga_ref[...], w_out[...]).astype(BF16)
    attention_backward(
        qkv_ref, go_ref, o_ref, e_ref, rl_ref, gqkv_ref, slice(None), tokens, features,
        features // H_ENC,
    )
    gn = mm_nt(gqkv_ref[...], w_qkv[...])
    n1, s1 = normalise(x_ref[...].astype(F32))
    small_ref[0:1, :] = rows_sum(gn * n1)
    small_ref[1:2, :] = rows_sum(gn)
    gx_ref[...] = (gh_ref[...] + normalise_back(gn, n1, s1, gain1[...])).astype(BF16)


def split_low(x):
    high = x.astype(BF16)
    return high, (x - high.astype(F32)).astype(BF16)


def decoder_kernel(
    y_ref, slot_col_ref, slot_row_ref, pos_ref, g_ref,
    w_embed, b_embed, mask_token,
    gain1, bias1, w_qkv, w_out, b_out, gain2, bias2, w_up, b_up, w_down, b_down,
    out_ref, a_ref, o_ref, c_ref, u_ref, gf_ref, ga_ref, gqkv_ref, geb_ref, gy_ref, small_ref, gbup_ref,
    eh_ref, el_ref, z_ref, s1_ref, qkv_ref, e_ref, rl_ref, h_ref, s2_ref, slope_ref, go_ref, ge_ref,
):
    step = pl.program_id(0)
    packed = y_ref.shape[0]
    rows, features = z_ref.shape
    samples = rows // PATCHES
    head_size = features // H_DEC

    @pl.when(step == 0)
    def _():
        high, low = split_low(mm(y_ref[...], w_embed[...]) + b_embed[...])
        eh_ref[...] = high
        el_ref[...] = low
        small_ref[...] = jnp.zeros_like(small_ref)
        gbup_ref[...] = jnp.zeros_like(gbup_ref)
        ge_ref[...] = jnp.zeros_like(ge_ref)

    slot_col = slot_col_ref[...]
    column = lax.broadcasted_iota(jnp.int32, (rows, packed), 1)
    one_hot = jnp.where(slot_col == column, 1.0, 0.0).astype(BF16)
    empty = jnp.where(slot_col < 0, 1.0, 0.0)
    z = mm(one_hot, eh_ref[...]) + mm(one_hot, el_ref[...]) + empty * mask_token[...]
    z = z + jnp.concatenate([pos_ref[...]] * samples, axis=0)
    n1, s1 = normalise(z)
    z_ref[...] = z
    s1_ref[...] = s1
    a_ref[...] = (n1 * gain1[...] + bias1[...]).astype(BF16)
    qkv_ref[...] = mm(a_ref[...], w_qkv[...]).astype(BF16)

    def forward(b, carry):
        at = pl.ds(pl.multiple_of(b * PATCHES, PATCHES), PATCHES)
        attention_forward(qkv_ref, o_ref, e_ref, rl_ref, at, PATCHES, features, head_size, None)
        return carry

    lax.fori_loop(0, samples, forward, 0)
    h_ref[...] = z_ref[...] + (mm(o_ref[...], w_out[...]) + b_out[...])
    n2, s2 = normalise(h_ref[...])
    s2_ref[...] = s2
    c_ref[...] = (n2 * gain2[...] + bias2[...]).astype(BF16)
    feed_forward(c_ref, w_up, b_up, u_ref, slope_ref, 512)
    out_ref[...] = (h_ref[...] + (mm(u_ref[...], w_down[...]) + b_down[...])).astype(BF16)

    feed_forward_back(g_ref, w_down, slope_ref, gf_ref, gbup_ref, 512)
    gc = mm_nt(gf_ref[...], w_up[...])
    g = g_ref[...].astype(F32)
    h = h_ref[...]
    n2 = (h - jnp.mean(h, axis=-1, keepdims=True)) * s2_ref[...]
    gh = g + normalise_back(gc, n2, s2_ref[...], gain2[...])
    small_ref[2:3, :] += rows_sum(gh)
    small_ref[3:4, :] += rows_sum(gc * n2)
    small_ref[4:5, :] += rows_sum(gc)
    small_ref[5:6, :] += rows_sum(g)
    h_ref[...] = gh
    ga_ref[...] = gh.astype(BF16)
    go_ref[...] = mm_nt(ga_ref[...], w_out[...]).astype(BF16)

    def backward(b, carry):
        at = pl.ds(pl.multiple_of(b * PATCHES, PATCHES), PATCHES)
        attention_backward(
            qkv_ref, go_ref, o_ref, e_ref, rl_ref, gqkv_ref, at, PATCHES, features, head_size
        )
        return carry

    lax.fori_loop(0, samples, backward, 0)
    gn = mm_nt(gqkv_ref[...], w_qkv[...])
    z = z_ref[...]
    n1 = (z - jnp.mean(z, axis=-1, keepdims=True)) * s1_ref[...]
    gz = h_ref[...] + normalise_back(gn, n1, s1_ref[...], gain1[...])
    small_ref[0:1, :] += rows_sum(gn * n1)
    small_ref[1:2, :] += rows_sum(gn)
    small_ref[6:7, :] += rows_sum(gz * empty)
    row = lax.broadcasted_iota(jnp.int32, (packed, rows), 0)
    place = jnp.where(slot_row_ref[0] == row, 1.0, 0.0).astype(BF16)
    high, low = split_low(gz)
    ge_ref[...] += mm(place, high) + mm(place, low)

    @pl.when(step == pl.num_programs(0) - 1)
    def _():
        ge = ge_ref[...]
        small_ref[7:8, :] = rows_sum(ge)
        geb_ref[...] = ge.astype(BF16)
        gy_ref[...] = mm_nt(geb_ref[...], w_embed[...]).astype(BF16)


def as_rows(params):
    return [p.reshape(1, -1) if p.ndim == 1 else p for p in params]


def in_vmem(count):
    return [pl.BlockSpec(memory_space=pltpu.VMEM)] * count


def shape(rows, columns, dtype=BF16):
    return jax.ShapeDtypeStruct((rows, columns), dtype)


KERNEL_VMEM = 60 * 2**20


def encoder_forward(x, segments, params):
    rows, d = x.shape
    ff = params[7].shape[1]
    outs = [
        shape(rows, d),
        shape(rows, d),
        shape(rows, 3 * d),
        shape(rows, H_ENC * rows),
        shape(rows, d, F32),
        shape(rows, d),
        shape(rows, d, F32),
        shape(rows, 1, F32),
        shape(rows, d),
        shape(rows, ff),
        shape(rows, ff),
    ]
    args = [x, segments.reshape(rows, 1), segments.reshape(1, rows)] + as_rows(params)
    return pl.pallas_call(
        encoder_forward_kernel,
        out_shape=outs,
        in_specs=in_vmem(len(args)),
        out_specs=in_vmem(len(outs)),
        scratch_shapes=[pltpu.VMEM((rows, d), F32)],
        compiler_params=pltpu.CompilerParams(vmem_limit_bytes=KERNEL_VMEM),
        name="encoder_forward",
    )(*args)


def encoder_backward(x, gy, saved, params):
    gain1, _, w_qkv, w_out, _, gain2, _, w_up, _, w_down, _ = as_rows(params)
    rows, d = x.shape
    ff = w_up.shape[1]
    outs = [
        shape(rows, d),
        shape(rows, ff),
        shape(rows, d),
        shape(rows, 3 * d),
        shape(8, d, F32),
        shape(1, ff, F32),
    ]
    args = [x, gy, *saved, gain1, w_qkv, w_out, gain2, w_up, w_down]
    return pl.pallas_call(
        encoder_backward_kernel,
        out_shape=outs,
        in_specs=in_vmem(len(args)),
        out_specs=in_vmem(len(outs)),
        scratch_shapes=[pltpu.VMEM((rows, d), F32), pltpu.VMEM((rows, d), BF16)],
        compiler_params=pltpu.CompilerParams(vmem_limit_bytes=KERNEL_VMEM),
        name="encoder_backward",
    )(*args)


def decoder_both(y, slots, g, embed_params, params):
    w_embed, b_embed, mask_token = as_rows(embed_params)
    packed, d_enc = y.shape
    total, d = g.shape
    samples = 4
    rows = samples * PATCHES
    steps = total // rows
    ff = params[7].shape[1]
    pos = positions(PATCHES, d)
    args = [y, slots.reshape(total, 1), slots.reshape(steps, 1, rows), pos, g]
    args += [w_embed, b_embed, mask_token] + as_rows(params)

    def whole(x):
        return pl.BlockSpec(x.shape, lambda i: (0,) * len(x.shape), pipeline_mode=pl.Buffered(1))

    def part(columns):
        return pl.BlockSpec((rows, columns), lambda i: (i, 0))

    in_specs = [
        whole(y),
        part(1),
        pl.BlockSpec((1, 1, rows), lambda i: (i, 0, 0)),
        whole(pos),
        part(d),
    ] + [whole(x) for x in args[5:]]
    wide = [d, d, d, d, ff, ff, d, 3 * d]
    outs = [shape(total, w) for w in wide]
    out_specs = [part(w) for w in wide]
    last = [shape(packed, d), shape(packed, d_enc), shape(8, d, F32), shape(1, ff, F32)]
    outs += last
    out_specs += [pl.BlockSpec(x.shape, lambda i: (0, 0)) for x in last]
    scratch = [
        (packed, d, BF16),
        (packed, d, BF16),
        (rows, d, F32),
        (rows, 1, F32),
        (rows, 3 * d, BF16),
        (rows, H_DEC * PATCHES, BF16),
        (rows, d, F32),
        (rows, d, F32),
        (rows, 1, F32),
        (rows, ff, BF16),
        (rows, d, BF16),
        (packed, d, F32),
    ]
    return pl.pallas_call(
        decoder_kernel,
        out_shape=outs,
        grid=(steps,),
        in_specs=in_specs,
        out_specs=out_specs,
        scratch_shapes=[pltpu.VMEM((r, w), t) for r, w, t in scratch],
        compiler_params=pltpu.CompilerParams(
            vmem_limit_bytes=KERNEL_VMEM, dimension_semantics=("arbitrary",)
        ),
        name="decoder_both",
    )(*args)


def slot_rows(segments, patch_order):
    sample = jnp.arange(SAMP_MB, dtype=jnp.int32)[:, None]
    start = jnp.sum((segments[None, :] < sample).astype(jnp.int32), axis=1)
    count = jnp.sum((segments[None, :] == sample).astype(jnp.int32), axis=1)
    patch = jnp.arange(PATCHES, dtype=jnp.int32)
    hit = patch_order[:, None, :] == patch[None, :, None]
    rank = jnp.sum(jnp.where(hit, patch[None, None, :], 0), axis=2)
    return jnp.where(rank < count[:, None], start[:, None] + rank, -1)


MESH = pl.DeviceIdType.MESH


class Chunk:
    def __init__(self, array, offset, width, x_first):
        self.array, self.offset, self.width, self.x_first = array, offset, width, x_first


def plan_chunks(shapes, widths):
    chunks = []
    for j, (shape, width) in enumerate(zip(shapes, widths)):
        half = shape[1] // 2
        for offset in range(0, half, width):
            chunks.append(Chunk(j, offset, width, len(chunks) % 2 == 0))
    return chunks


def reduce_kernel(chunks, n_arrays, *refs):
    ins, outs = refs[:n_arrays], refs[n_arrays : 2 * n_arrays]
    n = len(chunks)
    scratch = refs[2 * n_arrays :]
    own, recv0, recv1, recv2, recv3, fin, recv4 = (scratch[i * n : (i + 1) * n] for i in range(7))
    local_sem, send_sem, recv_sem = scratch[7 * n :]
    s = lax.axis_index("section")
    d = lax.axis_index("dp")
    z, y, x = d // 4, (d // 2) % 2, d % 2
    x_peer, y_peer = d + 1 - 2 * x, d + 2 - 4 * y
    z_peers = [lax.rem(z + k, 4) for k in (1, 2, 3)]

    barrier = pltpu.get_barrier_semaphore()
    pl.semaphore_signal(barrier, inc=1, device_id={"section": 1 - s}, device_id_type=MESH)
    for peer in [x_peer, y_peer] + [d + 4 * (p - z) for p in z_peers]:
        pl.semaphore_signal(barrier, inc=1, device_id={"dp": peer}, device_id_type=MESH)
    pl.semaphore_wait(barrier, 6)

    def remote(src, dst, c, slot, peer):
        return pltpu.make_async_remote_copy(
            src_ref=src,
            dst_ref=dst,
            send_sem=send_sem.at[c, slot],
            recv_sem=recv_sem.at[c, slot],
            device_id=peer,
            device_id_type=MESH,
        )

    def columns(c, side):
        chunk = chunks[c]
        half = ins[chunk.array].shape[-1] // 2
        return pl.ds(pl.multiple_of(side * half + chunk.offset, 128), chunk.width)

    copies = [dict() for _ in range(n)]

    def stage0(c):
        src = ins[chunks[c].array]
        away = remote(src.at[:, :, :, :, columns(c, 1 - s)], recv0[c], c, 0, {"section": 1 - s})
        away.start()
        here = pltpu.make_async_copy(src.at[:, :, :, :, columns(c, s)], own[c], local_sem.at[c])
        here.start()
        copies[c].update(here=here, p0=away)

    def stage1(c):
        copies[c]["here"].wait()
        copies[c]["p0"].wait_recv()

        def add(t, carry):
            at = (t // 4, (t // 2) % 2, t % 2)
            own[c][at] = own[c][at] + recv0[c][at]
            return carry

        lax.fori_loop(0, 16, add, 0)
        if chunks[c].x_first:
            p1 = remote(own[c].at[:, :, 1 - x], recv1[c], c, 1, {"dp": x_peer})
        else:
            p1 = remote(own[c].at[:, 1 - y], recv1[c], c, 1, {"dp": y_peer})
        p1.start()
        copies[c]["p1"] = p1

    def stage2(c):
        copies[c]["p1"].wait_recv()
        x_first = chunks[c].x_first

        def add(t, carry):
            at = (t // 2, t % 2, x) if x_first else (t // 2, y, t % 2)
            own[c][at] = own[c][at] + recv1[c][t // 2, t % 2]
            return carry

        lax.fori_loop(0, 8, add, 0)
        if x_first:
            p2 = remote(own[c].at[:, 1 - y, x], recv2[c], c, 2, {"dp": y_peer})
        else:
            p2 = remote(own[c].at[:, y, 1 - x], recv2[c], c, 2, {"dp": x_peer})
        p2.start()
        copies[c]["p2"] = p2

    def stage3(c):
        copies[c]["p2"].wait_recv()

        def add(t, carry):
            own[c][t, y, x] = own[c][t, y, x] + recv2[c][t]
            return carry

        lax.fori_loop(0, 4, add, 0)
        for k, peer in enumerate(z_peers):
            p3 = remote(own[c].at[peer, y, x], recv3[c].at[k], c, 3 + k, {"dp": d + 4 * (peer - z)})
            p3.start()
            copies[c]["p3", k] = p3

    def stage4(c):
        for k in range(3):
            copies[c]["p3", k].wait_recv()
        total = own[c][z, y, x].astype(jnp.float32)
        for k in range(3):
            total = total + recv3[c][k].astype(jnp.float32)
        fin[c][...] = total.astype(jnp.bfloat16)
        p4 = remote(fin[c], recv4[c], c, 6, {"section": 1 - s})
        p4.start()
        copies[c]["p4"] = p4

    def stage5(c):
        copies[c]["p4"].wait_recv()
        out = outs[chunks[c].array]
        out[:, columns(c, s)] = fin[c][...].astype(jnp.float32)
        out[:, columns(c, 1 - s)] = recv4[c][...].astype(jnp.float32)

    pairs = [list(range(i, min(i + 2, n))) for i in range(0, n, 2)]
    stages = (stage1, stage2, stage3, stage4, stage5)
    ahead = 2
    for pair in pairs[:ahead]:
        for c in pair:
            stage0(c)
    for step in range(len(pairs) + len(stages) - 1):
        if step + ahead < len(pairs):
            for c in pairs[step + ahead]:
                stage0(c)
        for k, stage in enumerate(stages):
            if 0 <= step - k < len(pairs):
                for c in pairs[step - k]:
                    stage(c)
    for c in range(n):
        for copy in [copies[c][name] for name in ("p0", "p1", "p2", "p4")] + [
            copies[c]["p3", k] for k in range(3)
        ]:
            copy.wait_send()


def reduce_arrays(arrays, widths, collective_id):
    shapes = [a.shape for a in arrays]
    chunks = plan_chunks(shapes, widths)
    blocks = [(shapes[c.array][0] // 16, c.width) for c in chunks]
    bf16 = jnp.bfloat16

    def buffers(*lead):
        return [pltpu.VMEM(lead + block, bf16) for block in blocks]

    n = len(chunks)
    return pl.pallas_call(
        functools.partial(reduce_kernel, chunks, len(arrays)),
        out_shape=[jax.ShapeDtypeStruct((r // 16, w), jnp.float32) for r, w in shapes],
        in_specs=[pl.BlockSpec(memory_space=pl.ANY)] * len(arrays),
        out_specs=[pl.BlockSpec(memory_space=pltpu.VMEM)] * len(arrays),
        scratch_shapes=buffers(4, 2, 2)
        + buffers(4, 2, 2)
        + buffers(4, 2)
        + buffers(4)
        + buffers(3)
        + buffers()
        + buffers()
        + [
            pltpu.SemaphoreType.DMA((n,)),
            pltpu.SemaphoreType.DMA((n, 7)),
            pltpu.SemaphoreType.DMA((n, 7)),
        ],
        compiler_params=pltpu.CompilerParams(
            collective_id=collective_id, has_side_effects=True, vmem_limit_bytes=56 * 2**20
        ),
        name="reduce_gradients",
    )(*[a.reshape(4, 2, 2, a.shape[0] // 16, a.shape[1]) for a in arrays])


def reduce_plain(arrays, section_index):
    first = section_index == 0
    results = []
    for a in arrays:
        half = a.shape[1] // 2
        keep = lax.dynamic_slice_in_dim(a, section_index * half, half, 1)
        give = lax.dynamic_slice_in_dim(a, (1 - section_index) * half, half, 1)
        got = swapped(give, "section", 0)
        chip = (keep.astype(jnp.float32) + got.astype(jnp.float32)).astype(jnp.bfloat16)
        mine = lax.psum_scatter(chip, "dp", scatter_dimension=0, tiled=True)
        other = swapped(mine, "section", 0)
        whole = jnp.concatenate(
            [jnp.where(first, mine, other), jnp.where(first, other, mine)], axis=1
        )
        results.append(whole.astype(jnp.float32))
    return results


SMALL_ROWS, SMALL_COLUMNS = 16, 256


def reduce_every(grads_all, section_index):
    groups = lax.axis_size("dp")
    big = [g for g in grads_all if g.ndim == 2]
    small = [g for g in grads_all if g.ndim == 1]
    flat = jnp.concatenate([g.reshape(groups, -1) for g in small], axis=1)
    room = SMALL_ROWS * SMALL_COLUMNS
    flat = jnp.pad(flat, ((0, 0), (0, room - flat.shape[1])))
    packed = flat.reshape(groups * SMALL_ROWS, SMALL_COLUMNS).astype(jnp.bfloat16)
    arrays = [g.astype(jnp.bfloat16) for g in big] + [packed]
    if groups == 16:
        widths = [CHUNK_WIDTHS[a.shape] for a in arrays]
        results = reduce_arrays(arrays, widths, 1)
    else:
        results = reduce_plain(arrays, section_index)
    row = results[-1].reshape(-1)
    results = list(results[:-1])
    totals, at = [], 0
    for g in grads_all:
        if g.ndim == 2:
            totals.append(results.pop(0))
        else:
            size = g.shape[0] // groups
            totals.append(row[at : at + size])
            at += size
    return totals


CHUNK_WIDTHS = {
    (768, 2304): 384,
    (768, 768): 384,
    (768, 3072): 384,
    (3072, 768): 128,
    (768, 512): 256,
    (512, 1536): 384,
    (512, 512): 256,
    (512, 2048): 512,
    (2048, 512): 128,
    (256, 256): 128,
}


def shards(
    patches,
    segment_ids,
    patch_order,
    encoder_gain1,
    encoder_bias1,
    encoder_qkv,
    encoder_out,
    encoder_out_bias,
    encoder_gain2,
    encoder_bias2,
    encoder_up,
    encoder_up_bias,
    encoder_down,
    encoder_down_bias,
    embed_weight,
    embed_bias,
    mask_token,
    decoder_gain1,
    decoder_bias1,
    decoder_qkv,
    decoder_out,
    decoder_out_bias,
    decoder_gain2,
    decoder_bias2,
    decoder_up,
    decoder_up_bias,
    decoder_down,
    decoder_down_bias,
    cotangent,
):
    enc_params = (
        encoder_gain1,
        encoder_bias1,
        encoder_qkv,
        encoder_out,
        encoder_out_bias,
        encoder_gain2,
        encoder_bias2,
        encoder_up,
        encoder_up_bias,
        encoder_down,
        encoder_down_bias,
    )
    embed_params = (embed_weight, embed_bias, mask_token)
    dec_params = (
        decoder_gain1,
        decoder_bias1,
        decoder_qkv,
        decoder_out,
        decoder_out_bias,
        decoder_gain2,
        decoder_bias2,
        decoder_up,
        decoder_up_bias,
        decoder_down,
        decoder_down_bias,
    )
    section_index = lax.axis_index("section")
    first_section = section_index == 0

    def own(x):
        half = x.shape[0] // 2
        return lax.dynamic_slice_in_dim(x, section_index * half, half, 0)

    patches, segment_ids, patch_order, cotangent = map(
        own, (patches, segment_ids, patch_order, cotangent)
    )
    segments = segment_ids[0]
    slots = slot_rows(segments, patch_order)
    y, a1, qkv, e, rl, o1, n2, s2, c1, u1, slope = encoder_forward(patches, segments, enc_params)
    g = cotangent.reshape(-1, DECODER_WIDTH)
    decoded, a2, o2, c2, u2, gf2, ga2, gqkv2, geb, gy, small2, gbup2 = decoder_both(
        y, slots, g, embed_params, dec_params
    )
    grad_rows, gf1, ga1, gqkv1, small1, gbup1 = encoder_backward(
        patches, gy, (qkv, e, rl, o1, n2, s2, slope), enc_params
    )
    decoded = decoded.reshape(cotangent.shape)
    enc_grads = (
        small1[0], small1[1], weight_grad(a1, gqkv1), weight_grad(o1, ga1), small1[2], small1[3],
        small1[4], weight_grad(c1, gf1), gbup1[0], weight_grad(u1, gy), small1[5],
    )
    embed_grads = (weight_grad(y, geb), small2[7], small2[6])
    dec_grads = (
        small2[0], small2[1], weight_grad(a2, gqkv2), weight_grad(o2, ga2), small2[2], small2[3],
        small2[4], weight_grad(c2, gf2), gbup2[0], weight_grad(u2, g), small2[5],
    )
    patch_half = decoded.shape[1] // 2
    feature_half = grad_rows.shape[1] // 2

    def halves(x, half):
        keep = lax.dynamic_slice_in_dim(x, section_index * half, half, 1)
        give = lax.dynamic_slice_in_dim(x, (1 - section_index) * half, half, 1)
        return keep, give

    keep_decoded, give_decoded = halves(decoded, patch_half)
    keep_grad, give_grad = halves(grad_rows, feature_half)
    got_decoded, got_grad = swapped((give_decoded, give_grad), "section", 0)

    def joined(mine, other):
        return jnp.concatenate(
            [jnp.where(first_section, mine, other), jnp.where(first_section, other, mine)]
        )

    decoded = joined(keep_decoded, got_decoded)
    grad_rows = joined(keep_grad, got_grad)
    totals = reduce_every(enc_grads + embed_grads + dec_grads, section_index)
    return (
        decoded,
        grad_rows,
        totals[0],
        totals[1],
        totals[2],
        totals[3],
        totals[4],
        totals[5],
        totals[6],
        totals[7],
        totals[8],
        totals[9],
        totals[10],
        totals[11],
        totals[12],
        totals[13],
        totals[14],
        totals[15],
        totals[16],
        totals[17],
        totals[18],
        totals[19],
        totals[20],
        totals[21],
        totals[22],
        totals[23],
        totals[24],
    )


def solution(mesh):
    in_specs = (
        P("dp", None),
        P("dp", None),
        P("dp", None),
        P(),
        P(),
        P(),
        P(),
        P(),
        P(),
        P(),
        P(),
        P(),
        P(),
        P(),
        P(),
        P(),
        P(),
        P(),
        P(),
        P(),
        P(),
        P(),
        P(),
        P(),
        P(),
        P(),
        P(),
        P(),
        P("dp", None, None),
    )
    out_specs = (
        P("dp", "section", None),
        P("dp", "section"),
        P("dp"),
        P("dp"),
        P("dp", None),
        P("dp", None),
        P("dp"),
        P("dp"),
        P("dp"),
        P("dp", None),
        P("dp"),
        P("dp", None),
        P("dp"),
        P("dp", None),
        P("dp"),
        P("dp"),
        P("dp"),
        P("dp"),
        P("dp", None),
        P("dp", None),
        P("dp"),
        P("dp"),
        P("dp"),
        P("dp", None),
        P("dp"),
        P("dp", None),
        P("dp"),
    )
    return jax.shard_map(shards, mesh=mesh, in_specs=in_specs, out_specs=out_specs, check_vma=False)
```

```python
import functools
import math

import jax
import jax.numpy as jnp
import numpy as np
from jax import lax
from jax.experimental import pallas as pl
from jax.experimental.pallas import tpu as pltpu
from jax.sharding import PartitionSpec as P

H_ENC = 12
DECODER_WIDTH = 512
H_DEC = 16
PATCHES = 128
SAMP_MB = 12


EPSILON = 1e-06
MASKED = -1e30


def swapped(block, axis, apart):
    count = lax.axis_size(axis)
    route = []
    for low in range(count):
        high = low | 1 << apart
        if high != low and high < count:
            route += [(low, high), (high, low)]
    return lax.ppermute(block, axis, route)


def positions(count, features):
    column = np.arange(features)
    rate = np.exp(-math.log(10000.0) * (2 * (column // 2)) / features)
    angles = np.arange(count)[:, None] * rate[None, :]
    return np.where(column % 2 == 0, np.sin(angles), np.cos(angles)).astype(np.float32)


def weight_grad(left_side, grads):
    return lax.dot_general(
        left_side, grads, (((0,), (0,)), ((), ())), preferred_element_type=jnp.float32
    ).astype(jnp.bfloat16)


BF16 = jnp.bfloat16
F32 = jnp.float32


def mm(left, right):
    return lax.dot_general(left, right, (((1,), (0,)), ((), ())), preferred_element_type=F32)


def mm_nt(left, right):
    return lax.dot_general(left, right, (((1,), (1,)), ((), ())), preferred_element_type=F32)


def mm_tn(left, right):
    return lax.dot_general(left, right, (((0,), (0,)), ((), ())), preferred_element_type=F32)


def normalise(x):
    center = x - jnp.mean(x, axis=-1, keepdims=True)
    scale = lax.rsqrt(jnp.mean(center * center, axis=-1, keepdims=True) + EPSILON)
    return center * scale, scale


def normalise_back(grad, n, scale, gain):
    gn = grad * gain
    mean_gn = jnp.mean(gn, axis=-1, keepdims=True)
    mean_gnn = jnp.mean(gn * n, axis=-1, keepdims=True)
    return (gn - mean_gn - n * mean_gnn) * scale


def rows_sum(x):
    return jnp.sum(x, axis=0, keepdims=True)


def gelu_both(f):
    c0, c1 = math.sqrt(2.0 / math.pi), 0.044715
    square = f * f
    t = jnp.tanh(c0 * f * (1.0 + c1 * square))
    half = 0.5 * (1.0 + t)
    slope = half + (0.5 * c0) * f * (1.0 - t * t) * (1.0 + 3.0 * c1 * square)
    return f * half, slope


def lane_masks(head_size):
    lane = lax.broadcasted_iota(jnp.int32, (1, 128), 1)
    return [
        jnp.where((lane >= h * head_size) & (lane < (h + 1) * head_size), 1.0, 0.0).astype(BF16)
        for h in range(128 // head_size)
    ]


def stacked(x, masks):
    return jnp.concatenate([x * m for m in masks], axis=0)


def stacked_ones(x, masks, value):
    return jnp.concatenate(
        [jnp.broadcast_to(m * jnp.asarray(value, BF16), x.shape) for m in masks], axis=0
    )


def attention_forward(qkv_ref, o_ref, e_ref, rl_ref, rows, tokens, features, head_size, allowed):
    masks = lane_masks(head_size)
    per_group = len(masks)
    factor = head_size ** (-0.5) * math.log2(math.e)
    for g in range(features // 128):
        q, k, v = (qkv_ref[rows, j * features + g * 128 : j * features + (g + 1) * 128] for j in range(3))
        scores = mm_nt(q, stacked(k, masks))
        parts = []
        for h in range(per_group):
            part = scores[:, h * tokens : (h + 1) * tokens]
            if allowed is not None:
                part = jnp.where(allowed, part, MASKED)
            top = jnp.max(part, axis=-1, keepdims=True)
            parts.append(jnp.exp2((part - top) * factor).astype(BF16))
        e = jnp.concatenate(parts, axis=1)
        width = per_group * tokens
        e_ref[rows, g * width : (g + 1) * width] = e
        both = mm(e, jnp.concatenate([stacked(v, masks), stacked_ones(v, masks, 1.0)], axis=1))
        rl = 1.0 / both[:, 128:]
        rl_ref[rows, g * 128 : (g + 1) * 128] = rl
        o_ref[rows, g * 128 : (g + 1) * 128] = (both[:, :128] * rl).astype(BF16)


def attention_backward_group(q, k, v, e, go, o, rl, head_size):
    masks = lane_masks(head_size)
    per_group, tokens = len(masks), q.shape[0]
    scaling = head_size ** (-0.5)
    go = go.astype(F32) * rl
    go_low = go.astype(BF16)
    inner = (go * o.astype(F32)).astype(BF16)
    left = jnp.concatenate([go_low, inner], axis=1)
    right = jnp.concatenate([stacked(v, masks), stacked_ones(v, masks, -1.0)], axis=1)
    gs = (e.astype(F32) * mm_nt(left, right)).astype(BF16)

    def diagonal(wide):
        return jnp.concatenate(
            [
                wide[h * head_size : (h + 1) * head_size, h * tokens : (h + 1) * tokens]
                for h in range(per_group)
            ],
            axis=0,
        )

    gq = mm(gs, stacked(k, masks)) * scaling
    gk = jnp.transpose(diagonal(mm_tn(q, gs)) * scaling)
    gv = jnp.transpose(diagonal(mm_tn(go_low, e)))
    return gq.astype(BF16), gk.astype(BF16), gv.astype(BF16)


def attention_backward(
    qkv_ref, go_ref, o_ref, e_ref, rl_ref, gqkv_ref, rows, tokens, features, head_size
):
    width = 128 // head_size * tokens
    for g in range(features // 128):
        at = slice(g * 128, (g + 1) * 128)
        spots = [slice(j * features + g * 128, j * features + (g + 1) * 128) for j in range(3)]
        q, k, v = (qkv_ref[rows, spot] for spot in spots)
        e = e_ref[rows, g * width : (g + 1) * width]
        grads = attention_backward_group(
            q, k, v, e, go_ref[rows, at], o_ref[rows, at], rl_ref[rows, at], head_size
        )
        for spot, grad in zip(spots, grads):
            gqkv_ref[rows, spot] = grad


def feed_forward(c_ref, up_ref, bup_ref, u_ref, slope_ref, tile):
    def step(t, carry):
        at = pl.ds(pl.multiple_of(t * tile, tile), tile)
        f = mm(c_ref[...], up_ref[:, at]) + bup_ref[at].reshape(1, tile)
        u, slope = gelu_both(f)
        u_ref[:, at] = u.astype(BF16)
        slope_ref[:, at] = slope.astype(BF16)
        return carry

    lax.fori_loop(0, up_ref.shape[1] // tile, step, 0)


def feed_forward_back(gm_ref, down_ref, slope_ref, gf_ref, gbup_ref, tile):
    def step(t, carry):
        at = pl.ds(pl.multiple_of(t * tile, tile), tile)
        gu = mm_nt(gm_ref[...], down_ref[at, :])
        gf = (gu * slope_ref[:, at].astype(F32)).astype(BF16)
        gf_ref[:, at] = gf
        gbup_ref[:, at] += rows_sum(gf.astype(F32))
        return carry

    lax.fori_loop(0, down_ref.shape[0] // tile, step, 0)


def row(ref):
    return ref[...].reshape(1, -1)


def segment_mask(seg_ref, section):
    seg = seg_ref[pl.ds(section, 1), :].astype(F32)
    rows = seg.shape[1]
    column = jnp.transpose(jnp.broadcast_to(seg, (128, rows)))
    return jnp.concatenate([column] * (rows // 128), axis=1) == seg


def encoder_forward_kernel(
    x_ref, seg_ref,
    gain1, bias1, w_qkv, w_out, b_out, gain2, bias2, w_up, b_up, w_down, b_down,
    y_ref, a_ref, qkv_ref, e_ref, rl_ref, o_ref, n2_ref, s2_ref, c_ref, u_ref, slope_ref,
    h_ref, qkv_v, out_v, up_v, down_v, sem,
):
    tokens, features = a_ref.shape
    pairs = ((w_qkv, qkv_v), (w_out, out_v), (w_up, up_v), (w_down, down_v))
    loads = [pltpu.make_async_copy(w, v, sem.at[i]) for i, (w, v) in enumerate(pairs)]
    for load in loads:
        load.start()
    section = lax.axis_index("section")
    x = x_ref[pl.ds(pl.multiple_of(section * tokens, tokens), tokens), :].astype(F32)
    n1, _ = normalise(x)
    a_ref[...] = (n1 * row(gain1) + row(bias1)).astype(BF16)
    loads[0].wait()
    qkv_ref[...] = mm(a_ref[...], qkv_v[...]).astype(BF16)
    allowed = segment_mask(seg_ref, section)
    attention_forward(
        qkv_ref, o_ref, e_ref, rl_ref, slice(None), tokens, features, features // H_ENC, allowed
    )
    loads[1].wait()
    h_ref[...] = x + (mm(o_ref[...], out_v[...]) + row(b_out))
    n2, s2 = normalise(h_ref[...])
    n2_ref[...] = n2
    s2_ref[...] = s2
    c_ref[...] = (n2 * row(gain2) + row(bias2)).astype(BF16)
    loads[2].wait()
    feed_forward(c_ref, up_v, b_up, u_ref, slope_ref, 512)
    loads[3].wait()
    y_ref[...] = (h_ref[...] + (mm(u_ref[...], down_v[...]) + row(b_down))).astype(BF16)


def encoder_backward_kernel(
    x_ref, gy_ref, qkv_ref, e_ref, rl_ref, o_ref, n2_ref, s2_ref, slope_ref,
    gain1, w_qkv, w_out, gain2, w_up, w_down,
    gx_ref, gf_ref, ga_ref, gqkv_ref, small_ref, gbup_ref,
    gh_ref, go_ref,
):
    tokens, features = gy_ref.shape
    section = lax.axis_index("section")
    x = x_ref[pl.ds(pl.multiple_of(section * tokens, tokens), tokens), :].astype(F32)
    gbup_ref[...] = jnp.zeros_like(gbup_ref)
    feed_forward_back(gy_ref, w_down, slope_ref, gf_ref, gbup_ref, 512)
    gc = mm_nt(gf_ref[...], w_up[...])
    g = gy_ref[...].astype(F32)
    n2 = n2_ref[...]
    gh = g + normalise_back(gc, n2, s2_ref[...], row(gain2))
    gh_ref[...] = gh
    ga_ref[...] = gh.astype(BF16)
    small_ref[2:3, :] = rows_sum(gh)
    small_ref[3:4, :] = rows_sum(gc * n2)
    small_ref[4:5, :] = rows_sum(gc)
    small_ref[5:6, :] = rows_sum(g)
    go_ref[...] = mm_nt(ga_ref[...], w_out[...]).astype(BF16)
    attention_backward(
        qkv_ref, go_ref, o_ref, e_ref, rl_ref, gqkv_ref, slice(None), tokens, features,
        features // H_ENC,
    )
    gn = mm_nt(gqkv_ref[...], w_qkv[...])
    n1, s1 = normalise(x)
    small_ref[0:1, :] = rows_sum(gn * n1)
    small_ref[1:2, :] = rows_sum(gn)
    gx_ref[...] = (gh_ref[...] + normalise_back(gn, n1, s1, row(gain1))).astype(BF16)


def split_low(x):
    high = x.astype(BF16)
    return high, (x - high.astype(F32)).astype(BF16)


def decoder_kernel(
    y_ref, slot_col_ref, slot_row_ref, pos_ref, g_hbm,
    w_embed, b_embed, mask_token,
    gain1, bias1, w_qkv, w_out, b_out, gain2, bias2, w_up, b_up, w_down, b_down,
    out_ref, at_ref, ot_ref, ct_ref, gt_ref, u_ref, gf_ref, ga_ref, gqkv_ref, geb_ref, gy_ref, small_ref, gbup_ref,
    eh_ref, el_ref, z_ref, s1_ref, qkv_ref, e_ref, rl_ref, h_ref, s2_ref, slope_ref, go_ref, ge_ref, o_ref, c_ref,
    g2_ref, g_sem,
):
    step = pl.program_id(0)
    packed = y_ref.shape[0]
    rows, features = z_ref.shape
    samples = rows // PATCHES
    head_size = features // H_DEC
    steps = g_hbm.shape[0] // (2 * rows)
    section = lax.axis_index("section")

    def fetch(i):
        at = pl.ds(pl.multiple_of((section * steps + i) * rows, rows), rows)
        slot = lax.rem(i, 2)
        return pltpu.make_async_copy(g_hbm.at[at, :], g2_ref.at[slot], g_sem.at[slot])

    @pl.when(step == 0)
    def _():
        fetch(0).start()
        high, low = split_low(mm(y_ref[...], w_embed[...]) + row(b_embed))
        eh_ref[...] = high
        el_ref[...] = low
        small_ref[...] = jnp.zeros_like(small_ref)
        gbup_ref[...] = jnp.zeros_like(gbup_ref)
        ge_ref[...] = jnp.zeros_like(ge_ref)

    @pl.when(step + 1 < steps)
    def _():
        fetch(step + 1).start()

    slot_col = slot_col_ref[...]
    column = lax.broadcasted_iota(jnp.int32, (rows, packed), 1)
    one_hot = jnp.where(slot_col == column, 1.0, 0.0).astype(BF16)
    empty = jnp.where(slot_col < 0, 1.0, 0.0)
    z = mm(one_hot, eh_ref[...]) + mm(one_hot, el_ref[...]) + empty * row(mask_token)
    z = z + jnp.concatenate([pos_ref[...]] * samples, axis=0)
    n1, s1 = normalise(z)
    z_ref[...] = z
    s1_ref[...] = s1
    a = (n1 * row(gain1) + row(bias1)).astype(BF16)
    at_ref[...] = jnp.transpose(a)
    qkv_ref[...] = mm(a, w_qkv[...]).astype(BF16)

    def forward(b, carry):
        at = pl.ds(pl.multiple_of(b * PATCHES, PATCHES), PATCHES)
        attention_forward(qkv_ref, o_ref, e_ref, rl_ref, at, PATCHES, features, head_size, None)
        return carry

    lax.fori_loop(0, samples, forward, 0)
    ot_ref[...] = jnp.transpose(o_ref[...])
    h_ref[...] = z_ref[...] + (mm(o_ref[...], w_out[...]) + row(b_out))
    n2, s2 = normalise(h_ref[...])
    s2_ref[...] = s2
    c_ref[...] = (n2 * row(gain2) + row(bias2)).astype(BF16)
    ct_ref[...] = jnp.transpose(c_ref[...])
    feed_forward(c_ref, w_up, b_up, u_ref, slope_ref, 512)
    out_ref[...] = (h_ref[...] + (mm(u_ref[...], w_down[...]) + row(b_down))).astype(BF16)

    fetch(step).wait()
    g_ref = g2_ref.at[lax.rem(step, 2)]
    gt_ref[...] = jnp.transpose(g_ref[...])
    feed_forward_back(g_ref, w_down, slope_ref, gf_ref, gbup_ref, 512)
    gc = mm_nt(gf_ref[...], w_up[...])
    g = g_ref[...].astype(F32)
    h = h_ref[...]
    n2 = (h - jnp.mean(h, axis=-1, keepdims=True)) * s2_ref[...]
    gh = g + normalise_back(gc, n2, s2_ref[...], row(gain2))
    small_ref[2:3, :] += rows_sum(gh)
    small_ref[3:4, :] += rows_sum(gc * n2)
    small_ref[4:5, :] += rows_sum(gc)
    small_ref[5:6, :] += rows_sum(g)
    h_ref[...] = gh
    ga_ref[...] = gh.astype(BF16)
    go_ref[...] = mm_nt(ga_ref[...], w_out[...]).astype(BF16)

    def backward(b, carry):
        at = pl.ds(pl.multiple_of(b * PATCHES, PATCHES), PATCHES)
        attention_backward(
            qkv_ref, go_ref, o_ref, e_ref, rl_ref, gqkv_ref, at, PATCHES, features, head_size
        )
        return carry

    lax.fori_loop(0, samples, backward, 0)
    gn = mm_nt(gqkv_ref[...], w_qkv[...])
    z = z_ref[...]
    n1 = (z - jnp.mean(z, axis=-1, keepdims=True)) * s1_ref[...]
    gz = h_ref[...] + normalise_back(gn, n1, s1_ref[...], row(gain1))
    small_ref[0:1, :] += rows_sum(gn * n1)
    small_ref[1:2, :] += rows_sum(gn)
    small_ref[6:7, :] += rows_sum(gz * empty)
    packed_row = lax.broadcasted_iota(jnp.int32, (packed, rows), 0)
    place = jnp.where(slot_row_ref[0] == packed_row, 1.0, 0.0).astype(BF16)
    high, low = split_low(gz)
    ge_ref[...] += mm(place, high) + mm(place, low)

    @pl.when(step == pl.num_programs(0) - 1)
    def _():
        ge = ge_ref[...]
        small_ref[7:8, :] = rows_sum(ge)
        geb_ref[...] = ge.astype(BF16)
        gy_ref[...] = mm_nt(geb_ref[...], w_embed[...]).astype(BF16)


def in_vmem(count):
    return [pl.BlockSpec(memory_space=pltpu.VMEM)] * count


def in_hbm():
    return pl.BlockSpec(memory_space=pl.ANY)


def shape(rows, columns, dtype=BF16):
    return jax.ShapeDtypeStruct((rows, columns), dtype)


KERNEL_VMEM = 60 * 2**20


def encoder_forward(x, segments, params):
    rows, d = x.shape[0] // 2, x.shape[1]
    ff = params[7].shape[1]
    outs = [
        shape(rows, d),
        shape(rows, d),
        shape(rows, 3 * d),
        shape(rows, H_ENC * rows),
        shape(rows, d, F32),
        shape(rows, d),
        shape(rows, d, F32),
        shape(rows, 1, F32),
        shape(rows, d),
        shape(rows, ff),
        shape(rows, ff),
    ]
    args = [x, segments, *params]
    return pl.pallas_call(
        encoder_forward_kernel,
        out_shape=outs,
        in_specs=[in_hbm() if a.dtype == BF16 and a is not x else in_vmem(1)[0] for a in args],
        out_specs=in_vmem(len(outs)),
        scratch_shapes=[pltpu.VMEM((rows, d), F32)]
        + [pltpu.VMEM(w.shape, BF16) for w in args if w.dtype == BF16 and w is not x]
        + [pltpu.SemaphoreType.DMA((4,))],
        compiler_params=pltpu.CompilerParams(vmem_limit_bytes=KERNEL_VMEM),
        name="encoder_forward",
    )(*args)


def encoder_backward(x, gy, saved, params):
    gain1, _, w_qkv, w_out, _, gain2, _, w_up, _, w_down, _ = params
    rows, d = gy.shape
    ff = w_up.shape[1]
    outs = [
        shape(rows, d),
        shape(rows, ff),
        shape(rows, d),
        shape(rows, 3 * d),
        shape(8, d, F32),
        shape(1, ff, F32),
    ]
    args = [x, gy, *saved, gain1, w_qkv, w_out, gain2, w_up, w_down]
    return pl.pallas_call(
        encoder_backward_kernel,
        out_shape=outs,
        in_specs=in_vmem(len(args)),
        out_specs=in_vmem(len(outs)),
        scratch_shapes=[pltpu.VMEM((rows, d), F32), pltpu.VMEM((rows, d), BF16)],
        compiler_params=pltpu.CompilerParams(vmem_limit_bytes=KERNEL_VMEM),
        name="encoder_backward",
    )(*args)


def decoder_both(y, slots, g, embed_params, params):
    packed, d_enc = y.shape
    total, d = g.shape[0] // 2, g.shape[1]
    samples = 6
    rows = samples * PATCHES
    steps = total // rows
    ff = params[7].shape[1]
    pos = positions(PATCHES, d)
    args = [y, slots.reshape(total, 1), slots.reshape(steps, 1, rows), pos, g]
    args += [*embed_params, *params]

    def whole(x):
        return pl.BlockSpec(x.shape, lambda i: (0,) * len(x.shape), pipeline_mode=pl.Buffered(1))

    def part(columns):
        return pl.BlockSpec((rows, columns), lambda i: (i, 0))

    in_specs = [
        whole(y),
        part(1),
        pl.BlockSpec((1, 1, rows), lambda i: (i, 0, 0)),
        whole(pos),
        pl.BlockSpec(memory_space=pl.ANY),
    ] + [whole(x) for x in args[5:]]
    turned = pl.BlockSpec((d, rows), lambda i: (0, i))
    wide = [ff, ff, d, 3 * d]
    outs = [shape(total, d)] + [shape(d, total)] * 4 + [shape(total, w) for w in wide]
    out_specs = [part(d)] + [turned] * 4 + [part(w) for w in wide]
    last = [shape(packed, d), shape(packed, d_enc), shape(8, d, F32), shape(1, ff, F32)]
    outs += last
    out_specs += [pl.BlockSpec(x.shape, lambda i: (0, 0)) for x in last]
    scratch = [
        (packed, d, BF16),
        (packed, d, BF16),
        (rows, d, F32),
        (rows, 1, F32),
        (rows, 3 * d, BF16),
        (rows, H_DEC * PATCHES, BF16),
        (rows, d, F32),
        (rows, d, F32),
        (rows, 1, F32),
        (rows, ff, BF16),
        (rows, d, BF16),
        (packed, d, F32),
        (rows, d, BF16),
        (rows, d, BF16),
    ]
    return pl.pallas_call(
        decoder_kernel,
        out_shape=outs,
        grid=(steps,),
        in_specs=in_specs,
        out_specs=out_specs,
        scratch_shapes=[pltpu.VMEM((r, w), t) for r, w, t in scratch]
        + [pltpu.VMEM((2, rows, d), BF16), pltpu.SemaphoreType.DMA((2,))],
        compiler_params=pltpu.CompilerParams(
            vmem_limit_bytes=KERNEL_VMEM, dimension_semantics=("arbitrary",)
        ),
        name="decoder_both",
    )(*args)


def slot_rows(segments, patch_order):
    sample = jnp.arange(SAMP_MB, dtype=jnp.int32)[:, None]
    start = jnp.sum((segments[None, :] < sample).astype(jnp.int32), axis=1)
    count = jnp.sum((segments[None, :] == sample).astype(jnp.int32), axis=1)
    patch = jnp.arange(PATCHES, dtype=jnp.int32)
    hit = patch_order[:, None, :] == patch[None, :, None]
    rank = jnp.sum(jnp.where(hit, patch[None, None, :], 0), axis=2)
    return jnp.where(rank < count[:, None], start[:, None] + rank, -1)


MESH = pl.DeviceIdType.MESH
BIG = ("enc_qkv", "enc_out", "enc_up", "enc_down", "embed", "dec_qkv", "dec_out", "dec_up", "dec_down")
ROW_BUP, ROW_DEC_BUP, ROW_DEC, SMALL_ROWS = 6, 10, 16, 24


class Chunk:
    def __init__(self, name, half, offset, rows, width, first_row=None):
        self.name, self.half, self.offset, self.rows, self.width = name, half, offset, rows, width
        self.first_row, self.turned, self.x_first = first_row, name == "dec_down", True

    def place(self, side):
        if self.turned:
            return (pl.ds(pl.multiple_of(side * self.half + self.offset, 128), self.rows), slice(None))
        columns = pl.ds(pl.multiple_of(side * self.half + self.offset, 128), self.width)
        if self.first_row is None:
            return (slice(None), columns)
        return (pl.ds(self.first_row, self.rows), columns)

    @property
    def bytes(self):
        return 32 * self.rows * self.width


def make_chunks():
    chunks = [Chunk("dec_qkv", 768, o, 32, 256) for o in (0, 256, 512)]
    chunks += [Chunk("dec_up", 1024, o, 32, 256) for o in (0, 256, 512, 768)]
    chunks += [Chunk("dec_out", 256, 0, 32, 256)]
    chunks += [Chunk("dec_down", 256, o, 128, 128) for o in (0, 128)]
    chunks += [Chunk("embed", 256, 0, 48, 256)]
    chunks += [Chunk("enc_down", 384, 0, 48, 384, 48 * q) for q in range(4)]
    chunks += [Chunk("enc_up", 1536, o, 48, 384) for o in (0, 384, 768, 1152)]
    chunks += [Chunk("enc_out", 384, 0, 48, 384)]
    chunks += [Chunk("enc_qkv", 1152, o, 48, 384) for o in (0, 384, 768)]
    load = [0, 0]
    for chunk in chunks:
        chunk.x_first = load[0] <= load[1]
        load[0 if chunk.x_first else 1] += chunk.bytes
    return chunks


def tasks_in_order(chunks):
    tasks = []

    def gives(name, cost):
        tasks.extend(("give", c, cost) for c, k in enumerate(chunks) if k.name == name)

    for name in ("dec_qkv", "dec_up", "dec_out"):
        gives(name, 1.1)
    tasks.append(("pair", [c for c, k in enumerate(chunks) if k.turned], 5.0))
    gives("embed", 0.8)
    tasks.extend(("ffn", t, 2.3) for t in range(4))
    tasks += [("ln2", 0, 1.2), ("ut", 0, 1.0)]
    gives("enc_down", 0.6)
    tasks.append(("ct", 0, 0.6))
    gives("enc_up", 0.6)
    tasks.append(("go", 0, 1.1))
    tasks.extend(("att", g, 2.0) for g in range(6))
    tasks.append(("ot", 0, 0.6))
    gives("enc_out", 0.6)
    tasks.append(("at", 0, 0.6))
    gives("enc_qkv", 0.6)
    tasks.extend(("gn", j, 1.1) for j in range(3))
    tasks.append(("last", 0, 1.5))
    return tasks


def make_plan(chunks):
    tasks = tasks_in_order(chunks)
    lhs = ["dec_qkv", "dec_up", "dec_out", "dec_down"]
    free = dict(core=0.0, x=0.0, y=0.0, z=0.0)
    rate = dict(core=500e3, x=82e3, y=82e3, z=82e3)
    pending, plan, now, owned = [], [], 2.0, {}

    def send(link, size, latency):
        begin = max(now, free[link])
        free[link] = begin + size / rate[link]
        return free[link] + latency

    def blocked(task):
        if task[0] == "give" and chunks[task[1]].name in lhs[2:]:
            name = lhs[lhs.index(chunks[task[1]].name) - 2]
        elif task[0] == "pair":
            name = lhs[1]
        else:
            return False
        return any(k.name == name and c not in owned for c, k in enumerate(chunks))

    while tasks or pending:
        pending.sort()
        if pending and (pending[0][0] <= now or not tasks or blocked(tasks[0])):
            arrive, stage, c = pending.pop(0)
            now = max(now, arrive)
            plan.append((stage, c))
            if c == "small":
                now += 0.1
                if stage < 4:
                    pending.append((now + 2.0, stage + 1, c))
                continue
            k = chunks[c]
            first, second = ("x", "y") if k.x_first else ("y", "x")
            if stage == 1:
                owned[c] = True
                now += 0.3 if k.turned else 0.8 if k.name.startswith("enc") else 1.3
                pending.append((send(first, k.bytes, 1.5), 2, c))
            elif stage == 2:
                now += 0.2
                pending.append((send(second, k.bytes / 2, 1.5), 3, c))
            elif stage == 3:
                now += 0.15
                pending.append((send("z", k.bytes / 2, 2.0), 4, c))
            elif stage == 4:
                now += 0.15
                pending.append((send("core", k.bytes / 16, 1.0), 5, c))
            continue
        name, arg, cost = tasks.pop(0)
        plan.append((name, arg))
        now += cost
        if name == "give":
            pending.append((send("core", chunks[arg].bytes, 1.0), 1, arg))
        elif name == "pair":
            for c in arg:
                pending.append((send("core", chunks[c].bytes, 1.0), 1, c))
        elif name == "last":
            pending.append((now + 2.0, 1, "small"))
    return plan


class Ring:
    def __init__(self, sources, slots, semaphores):
        self.copies = [
            pltpu.make_async_copy(source, slots[i % len(slots)], semaphores())
            for i, source in enumerate(sources)
        ]
        self.slots, self.at = slots, 0

    def begin(self, count=None):
        for copy in self.copies[: len(self.slots)][:count]:
            copy.start()

    def take(self):
        self.copies[self.at].wait()
        return self.slots[self.at % len(self.slots)]

    def done(self):
        ahead = self.at + len(self.slots)
        if ahead < len(self.copies):
            self.copies[ahead].start()
        self.at += 1


SAVED = ("qkv", "e", "rl", "o", "n2", "s2", "slope")
DEC_ACTS = ("at", "ot", "ct", "gt", "u", "gf", "ga", "gqkv")
FINISH_IN = (
    ("x", "gy", "geb", "y", "a", "c", "u", "decoded", "w_qkv", "w_out", "w_up", "w_down")
    + SAVED
    + tuple(k + "2" for k in DEC_ACTS)
    + ("small2", "gbup2", "gain1", "gain2")
)
FINISH_VMEM_IN = ("small2", "gbup2", "gain1", "gain2")
LOADS = 96


def finish_kernel(chunks, plan, names, *refs):
    r = dict(zip(names, refs))
    n = len(chunks)
    s = lax.axis_index("section")
    d = lax.axis_index("dp")
    z, y, x = d // 4, (d // 2) % 2, d % 2
    sibling = {"section": 1 - s}
    x_peer, y_peer = {"dp": d + 1 - 2 * x}, {"dp": d + 2 - 4 * y}
    z_at = [lax.rem(z + k, 4) for k in (1, 2, 3)]
    z_peers = [{"dp": d + 4 * (p - z)} for p in z_at]

    barrier = pltpu.get_barrier_semaphore()
    for peer in [sibling, x_peer, y_peer] + z_peers:
        pl.semaphore_signal(barrier, inc=1, device_id=peer, device_id_type=MESH)

    counter = iter(range(LOADS))

    def semaphore():
        return r["load_sem"].at[next(counter)]

    def remote(src, dst, send, recv, peer):
        return pltpu.make_async_remote_copy(
            src_ref=src, dst_ref=dst, send_sem=send, recv_sem=recv, device_id=peer, device_id_type=MESH
        )

    rhs_of = dict(dec_qkv="gqkv2", dec_up="gf2", dec_out="ga2")
    lhs_of = dict(dec_qkv="at2", dec_up="ct2", dec_out="ot2", dec_down="gt2")

    def side_columns(k, side):
        return pl.ds(pl.multiple_of(side * k.half + k.offset, 128), k.width)

    tiles, last_use = [], {}
    for i, (name, arg) in enumerate(plan):
        if name == "pair":
            tiles += [r["u2"].at[:, t * 256 : (t + 1) * 256] for t in range(8)]
            last_use["dec_down"] = i
        elif name in ("give", 1) and arg != "small" and chunks[arg].name in rhs_of:
            k = chunks[arg]
            side = 1 - s if name == "give" else s
            tiles.append(r[rhs_of[k.name]].at[:, side_columns(k, side)])
            last_use[k.name] = i
    rhs = Ring(tiles, [r["rhs"].at[i] for i in range(3)], semaphore)
    lhs_names = ["dec_qkv", "dec_up", "dec_out", "dec_down"]
    lhs = Ring([r[lhs_of[k]] for k in lhs_names], [r["lhs"].at[i] for i in range(2)], semaphore)
    lhs.begin(1)
    rhs.begin()
    lhs.copies[1].start()
    d_enc = r["gy"].shape[1]
    tokens = r["gy"].shape[0]
    blocks = []
    for t in range(4):
        at = pl.ds(t * d_enc, d_enc)
        blocks += [r["w_down"].at[at, :], r["w_up"].at[:, at]]
    blocks.append(r["w_out"])
    blocks += [r["w_qkv"].at[:, pl.ds(j * d_enc, d_enc)] for j in range(3)]
    weights = Ring(blocks, [r["w"].at[i] for i in range(4)], semaphore)
    e_width = 2 * tokens
    e_ring = Ring(
        [r["e"].at[:, pl.ds(g * e_width, e_width)] for g in range(6)],
        [r["e_v"].at[i] for i in range(2)],
        semaphore,
    )
    mine = pl.ds(pl.multiple_of(s * tokens, tokens), tokens)
    loads = {}
    for name in ("y", "geb", "gy", "slope", "n2", "s2", "u", "c", "qkv", "o", "rl", "x"):
        source = r[name].at[mine, :] if name == "x" else r[name]
        loads[name] = pltpu.make_async_copy(source, r[name + "_v"], semaphore())
    load_a = pltpu.make_async_copy(r["a"], r["c_v"], semaphore())
    for name in ("y", "geb", "gy", "slope"):
        loads[name].start()
    weights.begin()
    for name in ("n2", "s2", "u", "c", "qkv", "o", "rl", "x"):
        loads[name].start()
    e_ring.begin()

    half = r["decoded"].shape[1] // 2
    give_half = r["decoded"].at[:, pl.ds(pl.multiple_of((1 - s) * half, half), half), :]
    decoded_away = remote(
        give_half, r["decoded_got"], r["swap_sem"].at[0], r["swap_sem"].at[1], sibling
    )
    gx_columns = d_enc // 2
    gx_half = r["gx"].at[:, pl.ds(pl.multiple_of((1 - s) * gx_columns, 128), gx_columns)]
    gx_away = remote(gx_half, r["gx_got"], r["swap_sem"].at[2], r["swap_sem"].at[3], sibling)

    small, small_got = r["small"], r["small_got"]
    small[...] = jnp.zeros_like(small)
    small[ROW_DEC : ROW_DEC + 8, : r["small2"].shape[1]] = r["small2"][...]
    quarter = r["gbup2"].shape[1] // 4
    for i in range(4):
        small[ROW_DEC_BUP + i : ROW_DEC_BUP + i + 1, :quarter] = r["gbup2"][
            :, i * quarter : (i + 1) * quarter
        ]

    pl.semaphore_wait(barrier, 6)
    decoded_away.start()

    copies = {}

    def chunk_copy(c, slot, src, dst, peer):
        copy = remote(src, dst, r["send_sem"].at[c, slot], r["recv_sem"].at[c, slot], peer)
        copy.start()
        copies[c, slot] = copy

    sent = set()

    def sent_by(c, slot):
        if (c, slot) not in sent:
            sent.add((c, slot))
            copies[c, slot].wait_send()

    staged = {}

    def staging(c):
        k = chunks[c]
        buffers = r["stage", k.rows, k.width]
        turn = staged.setdefault((k.rows, k.width), [])
        if len(turn) >= len(buffers):
            sent_by(turn[-len(buffers)], 0)
        turn.append(c)
        return buffers[(len(turn) - 1) % len(buffers)]

    def shard(i):
        return (i // 4, (i // 2) % 2, i % 2)

    def product(k, side):
        columns = side_columns(k, side)
        if k.name in rhs_of:
            return mm(lhs.slots[lhs_names.index(k.name) % 2][...], rhs.take()[...])
        if k.name == "embed":
            return mm_tn(r["y_v"][...], r["geb_v"][:, columns])
        if k.name == "enc_down":
            left = jnp.concatenate(
                [
                    r["ut_v"][i * 192 + k.first_row : i * 192 + k.first_row + k.rows, :]
                    for i in range(16)
                ],
                axis=0,
            )
            return mm(left, r["gy_v"][:, columns])
        if k.name == "enc_up":
            return mm(r["ct_v"][...], r["slope_v"][:, columns])
        if k.name == "enc_out":
            return mm(r["ot_v"][...], r["ga_v"][:, columns])
        return mm(r["at_v"][...], r["qkv_v"][:, columns])

    def after_product(i, k):
        if k.name in rhs_of:
            rhs.done()
            if last_use[k.name] == i:
                lhs.done()

    waited = set()

    def wait_lhs(k):
        if k.name in lhs_of and k.name not in waited:
            waited.add(k.name)
            lhs.copies[lhs_names.index(k.name)].wait()

    def give(i, c):
        k = chunks[c]
        if k.name == "embed":
            loads["y"].wait()
            loads["geb"].wait()
        wait_lhs(k)
        buffer = staging(c)
        value = product(k, 1 - s).astype(BF16)
        for j in range(16):
            buffer[shard(j)] = value[j * k.rows : (j + 1) * k.rows]
        after_product(i, k)
        chunk_copy(c, 0, buffer, r["acc", c], sibling)

    def pair(i, both):
        wait_lhs(chunks[both[0]])
        left = lhs.slots[lhs_names.index("dec_down") % 2]
        side_rows = chunks[both[0]].half
        buffers = [staging(c) for c in both]
        for t in range(8):
            tile = rhs.take()
            for side, targets in ((1 - s, buffers), (s, [r["acc", c] for c in both])):
                at = pl.ds(pl.multiple_of(side * side_rows, side_rows), side_rows)
                value = mm(left[at, :], tile[...]).astype(BF16)
                for c, target in zip(both, targets):
                    k = chunks[c]
                    for j in range(2):
                        target[shard(2 * t + j)] = value[
                            k.offset : k.offset + k.rows, j * k.width : (j + 1) * k.width
                        ]
            rhs.done()
        lhs.done()
        for c, buffer in zip(both, buffers):
            chunk_copy(c, 0, buffer, r["got", c], sibling)

    def stage1(i, c):
        k, acc = chunks[c], r["acc", c]
        copies[c, 0].wait_recv()
        if k.turned:

            def add(j, carry):
                at = (j // 4, (j // 2) % 2, j % 2)
                acc[at] = acc[at] + r["got", c][at]
                return carry

            lax.fori_loop(0, 16, add, 0)
        else:
            value = product(k, s)
            for j in range(16):
                part = value[j * k.rows : (j + 1) * k.rows]
                acc[shard(j)] = (part + acc[shard(j)].astype(F32)).astype(BF16)
            after_product(i, k)
        if k.x_first:
            chunk_copy(c, 1, acc.at[:, :, 1 - x], r["recv1", c], x_peer)
        else:
            chunk_copy(c, 1, acc.at[:, 1 - y], r["recv1", c], y_peer)

    def stage2(i, c):
        k, acc, got = chunks[c], r["acc", c], r["recv1", c]
        copies[c, 1].wait_recv()

        def add(j, carry):
            at = (j // 2, j % 2, x) if k.x_first else (j // 2, y, j % 2)
            acc[at] = acc[at] + got[j // 2, j % 2]
            return carry

        lax.fori_loop(0, 8, add, 0)
        if k.x_first:
            chunk_copy(c, 2, acc.at[:, 1 - y, x], r["recv2", c], y_peer)
        else:
            chunk_copy(c, 2, acc.at[:, y, 1 - x], r["recv2", c], x_peer)

    def stage3(i, c):
        acc, got = r["acc", c], r["recv2", c]
        copies[c, 2].wait_recv()

        def add(j, carry):
            acc[j, y, x] = acc[j, y, x] + got[j]
            return carry

        lax.fori_loop(0, 4, add, 0)
        for j in range(3):
            chunk_copy(c, 3 + j, acc.at[z_at[j], y, x], r["recv3", c].at[j], z_peers[j])

    def stage4(i, c):
        k = chunks[c]
        total = r["acc", c][z, y, x].astype(F32)
        for j in range(3):
            copies[c, 3 + j].wait_recv()
            total = total + r["recv3", c][j].astype(F32)
        out = r["out_" + k.name]
        out[k.place(s)] = total.astype(BF16)
        here = out.at[k.place(s)]
        chunk_copy(c, 6, here, here, sibling)

    def stage5(i, c):
        copies[c, 6].wait_recv()

    def small_copy(slot, peer):
        copy = remote(
            small if slot < 3 else r["small_sum"],
            small_got.at[slot],
            r["small_sem"].at[0, slot],
            r["small_sem"].at[1, slot],
            peer,
        )
        copy.start()
        copies["small", slot] = copy

    def small_stage(stage):
        if stage < 4:
            copies["small", stage - 1].wait()
            total = small[...] + small_got[stage - 1]
            if stage < 3:
                small[...] = total
                small_copy(stage, x_peer if stage == 1 else y_peer)
            else:
                r["small_sum"][...] = total
                for j in range(3):
                    small_copy(3 + j, z_peers[j])
        else:
            total = r["small_sum"][...]
            for j in range(3):
                copies["small", 3 + j].wait()
                total = total + small_got[3 + j]
            r["out_small"][...] = total

    def ffn(i, t):
        if t == 0:
            loads["gy"].wait()
            loads["slope"].wait()
        at = slice(t * d_enc, (t + 1) * d_enc)
        gu = mm_nt(r["gy_v"][...], weights.take()[...])
        weights.done()
        gf = (gu * r["slope_v"][:, at].astype(F32)).astype(BF16)
        r["slope_v"][:, at] = gf
        small[ROW_BUP + t : ROW_BUP + t + 1, :] = rows_sum(gf.astype(F32))
        gc = mm_nt(gf, weights.take()[...])
        weights.done()
        r["sum_v"][...] = gc if t == 0 else r["sum_v"][...] + gc

    def ln2(i, _):
        loads["n2"].wait()
        loads["s2"].wait()
        g, gc, n2 = r["gy_v"][...].astype(F32), r["sum_v"][...], r["n2_v"][...]
        gh = g + normalise_back(gc, n2, r["s2_v"][...], row(r["gain2"]))
        small[2:3, :] = rows_sum(gh)
        small[3:4, :] = rows_sum(gc * n2)
        small[4:5, :] = rows_sum(gc)
        small[5:6, :] = rows_sum(g)
        r["n2_v"][...] = gh
        r["ga_v"][...] = gh.astype(BF16)

    def ut(i, _):
        loads["u"].wait()
        for t in range(8):
            at = slice(t * 384, (t + 1) * 384)
            r["ut_v"][at, :] = jnp.transpose(r["u_v"][:, at])

    def ct(i, _):
        loads["c"].wait()
        r["ct_v"][...] = jnp.transpose(r["c_v"][...])
        load_a.start()

    def go(i, _):
        r["go_v"][...] = mm_nt(r["ga_v"][...], weights.take()[...]).astype(BF16)
        weights.done()

    def att(i, g):
        if g == 0:
            for name in ("qkv", "o", "rl"):
                loads[name].wait()
        at = slice(g * 128, (g + 1) * 128)
        q, k, v = (r["qkv_v"][:, j * d_enc + g * 128 : j * d_enc + (g + 1) * 128] for j in range(3))
        grads = attention_backward_group(
            q, k, v, e_ring.take()[...], r["go_v"][:, at], r["o_v"][:, at], r["rl_v"][:, at],
            d_enc // H_ENC,
        )
        e_ring.done()
        for j in range(3):
            r["qkv_v"][:, j * d_enc + g * 128 : j * d_enc + (g + 1) * 128] = grads[j]

    def ot(i, _):
        r["ot_v"][...] = jnp.transpose(r["o_v"][...])

    def at_task(i, _):
        load_a.wait()
        r["at_v"][...] = jnp.transpose(r["c_v"][...])

    def gn(i, j):
        part = mm_nt(r["qkv_v"][:, j * d_enc : (j + 1) * d_enc], weights.take()[...])
        weights.done()
        r["sum_v"][...] = part if j == 0 else r["sum_v"][...] + part

    def last(i, _):
        loads["x"].wait()
        n1, s1 = normalise(r["x_v"][...].astype(F32))
        total = r["sum_v"][...]
        small[0:1, :] = rows_sum(total * n1)
        small[1:2, :] = rows_sum(total)
        small_copy(0, sibling)
        gx = r["n2_v"][...] + normalise_back(total, n1, s1, row(r["gain1"]))
        r["gx"][...] = gx.astype(BF16)
        gx_away.start()

    run = dict(
        give=give, pair=pair, ffn=ffn, ln2=ln2, ut=ut, ct=ct, go=go, att=att, ot=ot, at=at_task,
        gn=gn, last=last,
    )
    run.update({1: stage1, 2: stage2, 3: stage3, 4: stage4, 5: stage5})
    for i, (name, arg) in enumerate(plan):
        if arg == "small":
            small_stage(name)
        else:
            run[name](i, arg)

    for c in range(n):
        for slot in range(7):
            sent_by(c, slot)
    for copy in (decoded_away, gx_away):
        copy.wait()


def finish_buffers(chunks, rows, d, ff, dec_total, dec):
    buffers = {}
    for c, k in enumerate(chunks):
        block = (k.rows, k.width)
        buffers["acc", c] = ((4, 2, 2) + block, BF16)
        if k.turned:
            buffers["got", c] = ((4, 2, 2) + block, BF16)
        buffers["recv1", c] = ((4, 2) + block, BF16)
        buffers["recv2", c] = ((4,) + block, BF16)
        buffers["recv3", c] = ((3,) + block, BF16)
    for name, width, dtype in [
        ("y_v", d, BF16), ("geb_v", dec, BF16), ("gy_v", d, BF16), ("slope_v", ff, BF16),
        ("n2_v", d, F32), ("s2_v", 1, F32), ("u_v", ff, BF16), ("c_v", d, BF16),
        ("qkv_v", 3 * d, BF16), ("o_v", d, BF16), ("rl_v", d, F32), ("x_v", d, BF16),
        ("ga_v", d, BF16), ("go_v", d, BF16), ("sum_v", d, F32),
    ]:
        buffers[name] = ((rows, width), dtype)
    for name, height in [("ut_v", ff), ("ct_v", d), ("at_v", d), ("ot_v", d)]:
        buffers[name] = ((height, rows), BF16)
    buffers["e_v"] = ((2, rows, 2 * rows), BF16)
    buffers["w"] = ((4, d, d), BF16)
    buffers["lhs"] = ((2, dec, dec_total), BF16)
    buffers["rhs"] = ((3, dec_total, 256), BF16)
    buffers["small"] = ((SMALL_ROWS, d), F32)
    buffers["small_sum"] = ((SMALL_ROWS, d), F32)
    buffers["small_got"] = ((6, SMALL_ROWS, d), F32)
    return buffers


def finish(acts):
    enc, dec = acts["enc"], acts["dec"]
    gain1, _, w_qkv, w_out, _, gain2, _, w_up, _, w_down, _ = enc["params"]
    given = dict(zip(SAVED, acts["saved"]))
    given.update({k: acts[k] for k in ("x", "y", "gy", "geb", "small2", "gbup2")})
    given.update({k: enc[k] for k in "acu"})
    given.update({k + "2": dec[k] for k in DEC_ACTS})
    given.update(w_qkv=w_qkv, w_out=w_out, w_up=w_up, w_down=w_down, gain1=gain1, gain2=gain2)
    given["decoded"] = acts["decoded"].reshape(SAMP_MB, PATCHES, -1)
    rows, d = acts["gy"].shape
    ff = w_up.shape[1]
    dec_d, dec_total = dec["at"].shape
    dec_ff = dec["u"].shape[1]
    chunks = make_chunks()
    plan = make_plan(chunks)

    grads = dict(
        enc_qkv=(d, 3 * d), enc_out=(d, d), enc_up=(d, ff), enc_down=(ff, d), embed=(d, dec_d),
        dec_qkv=(dec_d, 3 * dec_d), dec_out=(dec_d, dec_d), dec_up=(dec_d, dec_ff),
        dec_down=(dec_ff, dec_d),
    )
    outs = {}
    for name in BIG:
        r, w = grads[name]
        outs["out_" + name] = shape(w, r // 16) if name == "dec_down" else shape(r // 16, w)
    outs["out_small"] = shape(SMALL_ROWS, d, F32)
    outs["decoded_got"] = jax.ShapeDtypeStruct((SAMP_MB, PATCHES // 2, dec_d), BF16)
    outs["gx"] = shape(rows, d)
    outs["gx_got"] = shape(rows, d // 2)
    buffers = finish_buffers(chunks, rows, d, ff, dec_total, dec_d)
    stages = {(k.rows, k.width): 2 for k in chunks}
    for block, count in stages.items():
        for i in range(count):
            buffers["stage", *block, i] = ((4, 2, 2) + block, BF16)
    n = len(chunks)
    semaphores = dict(
        load_sem=(LOADS,), send_sem=(n, 7), recv_sem=(n, 7), small_sem=(2, 6), swap_sem=(4,)
    )
    names = list(FINISH_IN) + list(outs) + list(buffers) + list(semaphores)

    def kernel(*refs):
        r = dict(zip(names, refs))
        for block, count in stages.items():
            r["stage", *block] = [r["stage", *block, i] for i in range(count)]
        finish_kernel(chunks, plan, list(r), *r.values())

    any_space, vmem = pl.BlockSpec(memory_space=pl.ANY), pl.BlockSpec(memory_space=pltpu.VMEM)
    results = pl.pallas_call(
        kernel,
        out_shape=list(outs.values()),
        in_specs=[vmem if k in FINISH_VMEM_IN else any_space for k in FINISH_IN],
        out_specs=[vmem] * len(outs),
        scratch_shapes=[pltpu.VMEM(*b) for b in buffers.values()]
        + [pltpu.SemaphoreType.DMA(v) for v in semaphores.values()],
        compiler_params=pltpu.CompilerParams(
            collective_id=1, has_side_effects=True, vmem_limit_bytes=FINISH_VMEM
        ),
        name="finish",
    )(*[given[k] for k in FINISH_IN])
    results = dict(zip(outs, results))
    results["decoded_own"] = given["decoded"]
    results["gx_own"] = results.pop("gx")
    return write_outputs(results, grads)


FINISH_VMEM = 62 * 2**20


def write_kernel(names, *refs):
    r = dict(zip(names, refs))
    s = lax.axis_index("section")
    half = r["decoded"].shape[1]
    samples, rows, columns = r["decoded_own"].shape[0], r["gx_own"].shape[0], r["gx"].shape[1]
    for side, part in (
        (s, r["decoded_own"][:, pl.ds(pl.multiple_of(s * half, half), half), :]),
        (1 - s, r["decoded_got"][...]),
    ):
        r["decoded"][pl.ds(side * samples, samples)] = part
    own = r["gx_own"][:, pl.ds(pl.multiple_of(s * columns, 128), columns)]
    for side, part in ((s, own), (1 - s, r["gx_got"][...])):
        r["gx"][pl.ds(pl.multiple_of(side * rows, rows), rows), :] = part
    for name in BIG:
        value = r["out_" + name][...].astype(F32)
        r[name][...] = jnp.transpose(value) if name == "dec_down" else value
    d = lax.axis_index("dp")
    small = r["out_small"]

    def piece(name, line, lanes, position):
        size = r[name].shape[0]
        value = small[pl.ds(line, 1), :lanes]
        value = pltpu.roll(value, lax.rem(lanes - position * size, lanes), 1)
        r[name][...] = value[:, :size].reshape(size)

    wide, narrow = small.shape[1], r["dec_gain1"].shape[0] * 16
    for i, name in enumerate(SMALL_NAMES):
        piece("enc_" + name, i, wide, d)
        piece("dec_" + name, ROW_DEC + i, narrow, d)
    piece("mask", ROW_DEC + 6, narrow, d)
    piece("embed_bias", ROW_DEC + 7, narrow, d)
    piece("enc_bup", ROW_BUP + d // 4, wide, d % 4)
    piece("dec_bup", ROW_DEC_BUP + d // 4, narrow, d % 4)


SMALL_NAMES = ("gain1", "bias1", "bout", "gain2", "bias2", "bdown")
BLOCK_ORDER = (
    "gain1", "bias1", "qkv", "out", "bout", "gain2", "bias2", "up", "bup", "down", "bdown",
)


def write_outputs(results, grads):
    d, ff = grads["enc_up"]
    dec_d, dec_ff = grads["dec_up"]
    order = ["decoded", "gx"] + ["enc_" + k for k in BLOCK_ORDER]
    order += ["embed", "embed_bias", "mask"] + ["dec_" + k for k in BLOCK_ORDER]
    samples, half, width = results["decoded_got"].shape
    rows, columns = results["gx_got"].shape
    shapes = dict(
        decoded=jax.ShapeDtypeStruct((2 * samples, half, width), BF16),
        gx=jax.ShapeDtypeStruct((2 * rows, columns), BF16),
    )
    for name in order[2:]:
        if name in grads:
            dims = (grads[name][0] // 16, grads[name][1])
        elif name == "enc_bup":
            dims = (ff // 16,)
        elif name == "dec_bup":
            dims = (dec_ff // 16,)
        else:
            dims = ((d if name.startswith("enc") else dec_d) // 16,)
        shapes[name] = jax.ShapeDtypeStruct(dims, F32)
    out_shape = [shapes[k] for k in order]
    names = list(results) + order
    return tuple(
        pl.pallas_call(
            functools.partial(write_kernel, names),
            out_shape=out_shape,
            in_specs=in_vmem(len(results)),
            out_specs=in_vmem(len(order)),
            compiler_params=pltpu.CompilerParams(vmem_limit_bytes=KERNEL_VMEM),
            name="write_outputs",
        )(*results.values())
    )


def reduce_plain(arrays, section_index):
    first = section_index == 0
    results = []
    for a in arrays:
        half = a.shape[1] // 2
        keep = lax.dynamic_slice_in_dim(a, section_index * half, half, 1)
        give = lax.dynamic_slice_in_dim(a, (1 - section_index) * half, half, 1)
        got = swapped(give, "section", 0)
        chip = (keep.astype(jnp.float32) + got.astype(jnp.float32)).astype(jnp.bfloat16)
        mine = lax.psum_scatter(chip, "dp", scatter_dimension=0, tiled=True)
        other = swapped(mine, "section", 0)
        whole = jnp.concatenate(
            [jnp.where(first, mine, other), jnp.where(first, other, mine)], axis=1
        )
        results.append(whole.astype(jnp.float32))
    return results


def finish_plain(acts, section_index):
    x, gy, seg_saved, enc, dec = acts["x"], acts["gy"], acts["saved"], acts["enc"], acts["dec"]
    gx, gf1, ga1, gqkv1, small1, gbup1 = encoder_backward(x, gy, seg_saved, enc["params"])
    small2, gbup2 = acts["small2"], acts["gbup2"]
    grads = (
        small1[0], small1[1], weight_grad(enc["a"], gqkv1), weight_grad(enc["o"], ga1), small1[2],
        small1[3], small1[4], weight_grad(enc["c"], gf1), gbup1[0], weight_grad(enc["u"], gy),
        small1[5],
        weight_grad(acts["y"], acts["geb"]), small2[7], small2[6],
        small2[0], small2[1], mm(dec["at"], dec["gqkv"]).astype(BF16),
        mm(dec["ot"], dec["ga"]).astype(BF16), small2[2], small2[3], small2[4],
        mm(dec["ct"], dec["gf"]).astype(BF16), gbup2[0],
        jnp.transpose(mm(dec["gt"], dec["u"])).astype(BF16), small2[5],
    )
    groups = lax.axis_size("dp")
    big = reduce_plain([g for g in grads if g.ndim == 2], section_index)
    flat = jnp.concatenate([g.reshape(groups, -1) for g in grads if g.ndim == 1], axis=1)
    line = lax.psum_scatter(flat, ("dp"), scatter_dimension=0, tiled=True)
    line = lax.psum(line, "section")[0]
    totals, at = [], 0
    for g in grads:
        if g.ndim == 2:
            totals.append(big.pop(0))
        else:
            size = g.shape[0] // groups
            totals.append(line[at : at + size])
            at += size
    decoded = acts["decoded"].reshape(SAMP_MB, PATCHES, -1)
    first = section_index == 0

    def halves(whole):
        half = whole.shape[1] // 2
        keep = lax.dynamic_slice_in_dim(whole, section_index * half, half, 1)
        give = lax.dynamic_slice_in_dim(whole, (1 - section_index) * half, half, 1)
        got = swapped(give, "section", 0)
        return jnp.concatenate([jnp.where(first, keep, got), jnp.where(first, got, keep)])

    return (halves(decoded), halves(gx), *totals)


def shards(
    patches,
    segment_ids,
    patch_order,
    encoder_gain1,
    encoder_bias1,
    encoder_qkv,
    encoder_out,
    encoder_out_bias,
    encoder_gain2,
    encoder_bias2,
    encoder_up,
    encoder_up_bias,
    encoder_down,
    encoder_down_bias,
    embed_weight,
    embed_bias,
    mask_token,
    decoder_gain1,
    decoder_bias1,
    decoder_qkv,
    decoder_out,
    decoder_out_bias,
    decoder_gain2,
    decoder_bias2,
    decoder_up,
    decoder_up_bias,
    decoder_down,
    decoder_down_bias,
    cotangent,
):
    enc_params = (
        encoder_gain1,
        encoder_bias1,
        encoder_qkv,
        encoder_out,
        encoder_out_bias,
        encoder_gain2,
        encoder_bias2,
        encoder_up,
        encoder_up_bias,
        encoder_down,
        encoder_down_bias,
    )
    embed_params = (embed_weight, embed_bias, mask_token)
    dec_params = (
        decoder_gain1,
        decoder_bias1,
        decoder_qkv,
        decoder_out,
        decoder_out_bias,
        decoder_gain2,
        decoder_bias2,
        decoder_up,
        decoder_up_bias,
        decoder_down,
        decoder_down_bias,
    )
    section_index = lax.axis_index("section")
    segments = lax.dynamic_index_in_dim(segment_ids, section_index, 0, keepdims=False)
    orders = lax.dynamic_slice_in_dim(patch_order, section_index * SAMP_MB, SAMP_MB, 0)
    slots = slot_rows(segments, orders)
    y, a1, qkv, e, rl, o1, n2, s2, c1, u1, slope = encoder_forward(patches, segment_ids, enc_params)
    g = cotangent.reshape(-1, DECODER_WIDTH)
    decoded, at2, ot2, ct2, gt2, u2, gf2, ga2, gqkv2, geb, gy, small2, gbup2 = decoder_both(
        y, slots, g, embed_params, dec_params
    )
    acts = dict(
        x=patches,
        y=y,
        gy=gy,
        geb=geb,
        decoded=decoded,
        small2=small2,
        gbup2=gbup2,
        saved=(qkv, e, rl, o1, n2, s2, slope),
        enc=dict(a=a1, o=o1, c=c1, u=u1, params=enc_params),
        dec=dict(at=at2, ot=ot2, ct=ct2, gt=gt2, u=u2, gf=gf2, ga=ga2, gqkv=gqkv2),
    )
    if lax.axis_size("dp") == 16:
        return finish(acts)
    return finish_plain(acts, section_index)


def solution(mesh):
    in_specs = (
        P("dp", None),
        P("dp", None),
        P("dp", None),
        P(),
        P(),
        P(),
        P(),
        P(),
        P(),
        P(),
        P(),
        P(),
        P(),
        P(),
        P(),
        P(),
        P(),
        P(),
        P(),
        P(),
        P(),
        P(),
        P(),
        P(),
        P(),
        P(),
        P(),
        P(),
        P("dp", None, None),
    )
    out_specs = (
        P("dp", "section", None),
        P("dp", "section"),
        P("dp"),
        P("dp"),
        P("dp", None),
        P("dp", None),
        P("dp"),
        P("dp"),
        P("dp"),
        P("dp", None),
        P("dp"),
        P("dp", None),
        P("dp"),
        P("dp", None),
        P("dp"),
        P("dp"),
        P("dp"),
        P("dp"),
        P("dp", None),
        P("dp", None),
        P("dp"),
        P("dp"),
        P("dp"),
        P("dp", None),
        P("dp"),
        P("dp", None),
        P("dp"),
    )
    return jax.shard_map(shards, mesh=mesh, in_specs=in_specs, out_specs=out_specs, check_vma=False)
```

```python
import functools
import math

import jax
import jax.numpy as jnp
import numpy as np
from jax import lax
from jax.experimental import pallas as pl
from jax.experimental.pallas import tpu as pltpu
from jax.sharding import PartitionSpec as P

H_ENC = 12
DECODER_WIDTH = 512
H_DEC = 16
PATCHES = 128
SAMP_MB = 12


EPSILON = 1e-06
MASKED = -1e30


def swapped(block, axis, apart):
    count = lax.axis_size(axis)
    route = []
    for low in range(count):
        high = low | 1 << apart
        if high != low and high < count:
            route += [(low, high), (high, low)]
    return lax.ppermute(block, axis, route)


def positions(count, features):
    column = np.arange(features)
    rate = np.exp(-math.log(10000.0) * (2 * (column // 2)) / features)
    angles = np.arange(count)[:, None] * rate[None, :]
    return np.where(column % 2 == 0, np.sin(angles), np.cos(angles)).astype(np.float32)


def weight_grad(left_side, grads):
    return lax.dot_general(
        left_side, grads, (((0,), (0,)), ((), ())), preferred_element_type=jnp.float32
    ).astype(jnp.bfloat16)


BF16 = jnp.bfloat16
F32 = jnp.float32


def mm(left, right):
    return lax.dot_general(left, right, (((1,), (0,)), ((), ())), preferred_element_type=F32)


def mm_nt(left, right):
    return lax.dot_general(left, right, (((1,), (1,)), ((), ())), preferred_element_type=F32)


def mm_tn(left, right):
    return lax.dot_general(left, right, (((0,), (0,)), ((), ())), preferred_element_type=F32)


def normalise(x):
    center = x - jnp.mean(x, axis=-1, keepdims=True)
    scale = lax.rsqrt(jnp.mean(center * center, axis=-1, keepdims=True) + EPSILON)
    return center * scale, scale


def normalise_back(grad, n, scale, gain):
    gn = grad * gain
    mean_gn = jnp.mean(gn, axis=-1, keepdims=True)
    mean_gnn = jnp.mean(gn * n, axis=-1, keepdims=True)
    return (gn - mean_gn - n * mean_gnn) * scale


def rows_sum(x):
    return jnp.sum(x, axis=0, keepdims=True)


def gelu_both(f):
    c0, c1 = math.sqrt(2.0 / math.pi), 0.044715
    square = f * f
    t = jnp.tanh(c0 * f * (1.0 + c1 * square))
    half = 0.5 * (1.0 + t)
    slope = half + (0.5 * c0) * f * (1.0 - t * t) * (1.0 + 3.0 * c1 * square)
    return f * half, slope


def lane_masks(head_size):
    lane = lax.broadcasted_iota(jnp.int32, (1, 128), 1)
    return [
        jnp.where((lane >= h * head_size) & (lane < (h + 1) * head_size), 1.0, 0.0).astype(BF16)
        for h in range(128 // head_size)
    ]


def stacked(x, masks):
    return jnp.concatenate([x * m for m in masks], axis=0)


def stacked_ones(x, masks, value):
    return jnp.concatenate(
        [jnp.broadcast_to(m * jnp.asarray(value, BF16), x.shape) for m in masks], axis=0
    )


def attention_forward(qkv_ref, o_ref, e_ref, rl_ref, rows, tokens, features, head_size, allowed):
    masks = lane_masks(head_size)
    per_group = len(masks)
    factor = head_size ** (-0.5) * math.log2(math.e)
    for g in range(features // 128):
        q, k, v = (qkv_ref[rows, j * features + g * 128 : j * features + (g + 1) * 128] for j in range(3))
        scores = mm_nt(q, stacked(k, masks))
        parts = []
        for h in range(per_group):
            part = scores[:, h * tokens : (h + 1) * tokens]
            if allowed is not None:
                part = jnp.where(allowed, part, MASKED)
            top = jnp.max(part, axis=-1, keepdims=True)
            parts.append(jnp.exp2((part - top) * factor).astype(BF16))
        e = jnp.concatenate(parts, axis=1)
        width = per_group * tokens
        e_ref[rows, g * width : (g + 1) * width] = e
        both = mm(e, jnp.concatenate([stacked(v, masks), stacked_ones(v, masks, 1.0)], axis=1))
        rl = 1.0 / both[:, 128:]
        rl_ref[rows, g * 128 : (g + 1) * 128] = rl
        o_ref[rows, g * 128 : (g + 1) * 128] = (both[:, :128] * rl).astype(BF16)


def attention_backward_group(q, k, v, e, go, o, rl, head_size):
    masks = lane_masks(head_size)
    per_group, tokens = len(masks), q.shape[0]
    scaling = head_size ** (-0.5)
    go = go.astype(F32) * rl
    go_low = go.astype(BF16)
    inner = (go * o.astype(F32)).astype(BF16)
    left = jnp.concatenate([go_low, inner], axis=1)
    right = jnp.concatenate([stacked(v, masks), stacked_ones(v, masks, -1.0)], axis=1)
    gs = (e.astype(F32) * mm_nt(left, right)).astype(BF16)

    def diagonal(wide):
        return jnp.concatenate(
            [
                wide[h * head_size : (h + 1) * head_size, h * tokens : (h + 1) * tokens]
                for h in range(per_group)
            ],
            axis=0,
        )

    gq = mm(gs, stacked(k, masks)) * scaling
    gk = jnp.transpose(diagonal(mm_tn(q, gs)) * scaling)
    gv = jnp.transpose(diagonal(mm_tn(go_low, e)))
    return gq.astype(BF16), gk.astype(BF16), gv.astype(BF16)


def attention_backward(
    qkv_ref, go_ref, o_ref, e_ref, rl_ref, gqkv_ref, rows, tokens, features, head_size
):
    width = 128 // head_size * tokens
    for g in range(features // 128):
        at = slice(g * 128, (g + 1) * 128)
        spots = [slice(j * features + g * 128, j * features + (g + 1) * 128) for j in range(3)]
        q, k, v = (qkv_ref[rows, spot] for spot in spots)
        e = e_ref[rows, g * width : (g + 1) * width]
        grads = attention_backward_group(
            q, k, v, e, go_ref[rows, at], o_ref[rows, at], rl_ref[rows, at], head_size
        )
        for spot, grad in zip(spots, grads):
            gqkv_ref[rows, spot] = grad


def feed_forward(c_ref, up_ref, bup_ref, u_ref, slope_ref, tile):
    def step(t, carry):
        at = pl.ds(pl.multiple_of(t * tile, tile), tile)
        f = mm(c_ref[...], up_ref[:, at]) + bup_ref[at].reshape(1, tile)
        u, slope = gelu_both(f)
        u_ref[:, at] = u.astype(BF16)
        slope_ref[:, at] = slope.astype(BF16)
        return carry

    lax.fori_loop(0, up_ref.shape[1] // tile, step, 0, unroll=True)


def feed_forward_back(gm_ref, down_ref, slope_ref, gf_ref, gbup_ref, tile):
    def step(t, carry):
        at = pl.ds(pl.multiple_of(t * tile, tile), tile)
        gu = mm_nt(gm_ref[...], down_ref[at, :])
        gf = (gu * slope_ref[:, at].astype(F32)).astype(BF16)
        gf_ref[:, at] = gf
        gbup_ref[:, at] += rows_sum(gf.astype(F32))
        return carry

    lax.fori_loop(0, down_ref.shape[0] // tile, step, 0, unroll=True)


def row(ref):
    return ref[...].reshape(1, -1)


def segment_mask(seg_ref, section):
    seg = seg_ref[pl.ds(section, 1), :].astype(F32)
    rows = seg.shape[1]
    column = jnp.transpose(jnp.broadcast_to(seg, (128, rows)))
    return jnp.concatenate([column] * (rows // 128), axis=1) == seg


def encoder_forward_kernel(
    x_ref, seg_ref,
    gain1, bias1, w_qkv, w_out, b_out, gain2, bias2, w_up, b_up, w_down, b_down,
    y_ref, a_ref, qkv_ref, e_ref, rl_ref, o_ref, n2_ref, s2_ref, c_ref, u_ref, slope_ref,
    h_ref, qkv_v, out_v, up_v, down_v, sem,
):
    tokens, features = a_ref.shape
    pairs = ((w_qkv, qkv_v), (w_out, out_v), (w_up, up_v), (w_down, down_v))
    loads = [pltpu.make_async_copy(w, v, sem.at[i]) for i, (w, v) in enumerate(pairs)]
    for load in loads:
        load.start()
    section = lax.axis_index("section")
    x = x_ref[pl.ds(pl.multiple_of(section * tokens, tokens), tokens), :].astype(F32)
    n1, _ = normalise(x)
    a_ref[...] = (n1 * row(gain1) + row(bias1)).astype(BF16)
    loads[0].wait()
    qkv_ref[...] = mm(a_ref[...], qkv_v[...]).astype(BF16)
    allowed = segment_mask(seg_ref, section)
    attention_forward(
        qkv_ref, o_ref, e_ref, rl_ref, slice(None), tokens, features, features // H_ENC, allowed
    )
    loads[1].wait()
    h_ref[...] = x + (mm(o_ref[...], out_v[...]) + row(b_out))
    n2, s2 = normalise(h_ref[...])
    n2_ref[...] = n2
    s2_ref[...] = s2
    c_ref[...] = (n2 * row(gain2) + row(bias2)).astype(BF16)
    loads[2].wait()
    feed_forward(c_ref, up_v, b_up, u_ref, slope_ref, 512)
    loads[3].wait()
    y_ref[...] = (h_ref[...] + (mm(u_ref[...], down_v[...]) + row(b_down))).astype(BF16)


def encoder_backward_kernel(
    x_ref, gy_ref, qkv_ref, e_ref, rl_ref, o_ref, n2_ref, s2_ref, slope_ref,
    gain1, w_qkv, w_out, gain2, w_up, w_down,
    gx_ref, gf_ref, ga_ref, gqkv_ref, small_ref, gbup_ref,
    gh_ref, go_ref,
):
    tokens, features = gy_ref.shape
    section = lax.axis_index("section")
    x = x_ref[pl.ds(pl.multiple_of(section * tokens, tokens), tokens), :].astype(F32)
    gbup_ref[...] = jnp.zeros_like(gbup_ref)
    feed_forward_back(gy_ref, w_down, slope_ref, gf_ref, gbup_ref, 512)
    gc = mm_nt(gf_ref[...], w_up[...])
    g = gy_ref[...].astype(F32)
    n2 = n2_ref[...]
    gh = g + normalise_back(gc, n2, s2_ref[...], row(gain2))
    gh_ref[...] = gh
    ga_ref[...] = gh.astype(BF16)
    small_ref[2:3, :] = rows_sum(gh)
    small_ref[3:4, :] = rows_sum(gc * n2)
    small_ref[4:5, :] = rows_sum(gc)
    small_ref[5:6, :] = rows_sum(g)
    go_ref[...] = mm_nt(ga_ref[...], w_out[...]).astype(BF16)
    attention_backward(
        qkv_ref, go_ref, o_ref, e_ref, rl_ref, gqkv_ref, slice(None), tokens, features,
        features // H_ENC,
    )
    gn = mm_nt(gqkv_ref[...], w_qkv[...])
    n1, s1 = normalise(x)
    small_ref[0:1, :] = rows_sum(gn * n1)
    small_ref[1:2, :] = rows_sum(gn)
    gx_ref[...] = (gh_ref[...] + normalise_back(gn, n1, s1, row(gain1))).astype(BF16)


def split_low(x):
    high = x.astype(BF16)
    return high, (x - high.astype(F32)).astype(BF16)


def decoder_kernel(
    y_ref, slot_col_ref, slot_row_ref, pos_ref, g_hbm,
    w_embed, b_embed, mask_token,
    gain1, bias1, w_qkv, w_out, b_out, gain2, bias2, w_up, b_up, w_down, b_down,
    out_ref, at_ref, ot_ref, ct_ref, gt_ref, u_ref, gf_ref, ga_ref, gqkv_ref, geb_ref, gy_ref, small_ref, gbup_ref,
    e2_ref, z_ref, s1_ref, qkv_ref, e_ref, rl_ref, h_ref, s2_ref, slope_ref, go_ref, ge_ref, o_ref, c_ref,
    g2_ref, g_sem,
):
    step = pl.program_id(0)
    packed = y_ref.shape[0]
    rows, features = z_ref.shape
    samples = rows // PATCHES
    head_size = features // H_DEC
    steps = g_hbm.shape[0] // (2 * rows)
    section = lax.axis_index("section")

    def fetch(i):
        at = pl.ds(pl.multiple_of((section * steps + i) * rows, rows), rows)
        slot = lax.rem(i, 2)
        return pltpu.make_async_copy(g_hbm.at[at, :], g2_ref.at[slot], g_sem.at[slot])

    @pl.when(step == 0)
    def _():
        fetch(0).start()
        high, low = split_low(mm(y_ref[...], w_embed[...]) + row(b_embed))
        e2_ref[:packed, :] = high
        e2_ref[packed:, :] = low
        small_ref[...] = jnp.zeros_like(small_ref)
        gbup_ref[...] = jnp.zeros_like(gbup_ref)
        ge_ref[...] = jnp.zeros_like(ge_ref)

    @pl.when(step + 1 < steps)
    def _():
        fetch(step + 1).start()

    slot_col = slot_col_ref[...]
    column = lax.broadcasted_iota(jnp.int32, (rows, packed), 1)
    one_hot = jnp.where(slot_col == column, 1.0, 0.0).astype(BF16)
    empty = jnp.where(slot_col < 0, 1.0, 0.0)
    twice = jnp.concatenate([one_hot, one_hot], axis=1)
    z = mm(twice, e2_ref[...]) + empty * row(mask_token)
    z = z + jnp.concatenate([pos_ref[...]] * samples, axis=0)
    n1, s1 = normalise(z)
    z_ref[...] = z
    s1_ref[...] = s1
    a = (n1 * row(gain1) + row(bias1)).astype(BF16)
    at_ref[...] = jnp.transpose(a)
    qkv_ref[...] = mm(a, w_qkv[...]).astype(BF16)

    def forward(b, carry):
        at = pl.ds(pl.multiple_of(b * PATCHES, PATCHES), PATCHES)
        attention_forward(qkv_ref, o_ref, e_ref, rl_ref, at, PATCHES, features, head_size, None)
        return carry

    lax.fori_loop(0, samples, forward, 0, unroll=2)
    ot_ref[...] = jnp.transpose(o_ref[...])
    h_ref[...] = z_ref[...] + (mm(o_ref[...], w_out[...]) + row(b_out))
    n2, s2 = normalise(h_ref[...])
    s2_ref[...] = s2
    c_ref[...] = (n2 * row(gain2) + row(bias2)).astype(BF16)
    ct_ref[...] = jnp.transpose(c_ref[...])
    feed_forward(c_ref, w_up, b_up, u_ref, slope_ref, 512)
    out_ref[...] = (h_ref[...] + (mm(u_ref[...], w_down[...]) + row(b_down))).astype(BF16)

    fetch(step).wait()
    g_ref = g2_ref.at[lax.rem(step, 2)]
    gt_ref[...] = jnp.transpose(g_ref[...])
    feed_forward_back(g_ref, w_down, slope_ref, gf_ref, gbup_ref, 512)
    gc = mm_nt(gf_ref[...], w_up[...])
    g = g_ref[...].astype(F32)
    h = h_ref[...]
    n2 = (h - jnp.mean(h, axis=-1, keepdims=True)) * s2_ref[...]
    gh = g + normalise_back(gc, n2, s2_ref[...], row(gain2))
    small_ref[2:3, :] += rows_sum(gh)
    small_ref[3:4, :] += rows_sum(gc * n2)
    small_ref[4:5, :] += rows_sum(gc)
    small_ref[5:6, :] += rows_sum(g)
    h_ref[...] = gh
    ga_ref[...] = gh.astype(BF16)
    go_ref[...] = mm_nt(ga_ref[...], w_out[...]).astype(BF16)

    def backward(b, carry):
        at = pl.ds(pl.multiple_of(b * PATCHES, PATCHES), PATCHES)
        attention_backward(
            qkv_ref, go_ref, o_ref, e_ref, rl_ref, gqkv_ref, at, PATCHES, features, head_size
        )
        return carry

    lax.fori_loop(0, samples, backward, 0, unroll=2)
    gn = mm_nt(gqkv_ref[...], w_qkv[...])
    z = z_ref[...]
    n1 = (z - jnp.mean(z, axis=-1, keepdims=True)) * s1_ref[...]
    gz = h_ref[...] + normalise_back(gn, n1, s1_ref[...], row(gain1))
    small_ref[0:1, :] += rows_sum(gn * n1)
    small_ref[1:2, :] += rows_sum(gn)
    small_ref[6:7, :] += rows_sum(gz * empty)
    packed_row = lax.broadcasted_iota(jnp.int32, (packed, rows), 0)
    place = jnp.where(slot_row_ref[0] == packed_row, 1.0, 0.0).astype(BF16)
    ge_ref[...] += mm(place, gz.astype(BF16))

    @pl.when(step == pl.num_programs(0) - 1)
    def _():
        ge = ge_ref[...]
        small_ref[7:8, :] = rows_sum(ge)
        geb_ref[...] = ge.astype(BF16)
        gy_ref[...] = mm_nt(geb_ref[...], w_embed[...]).astype(BF16)


def in_vmem(count):
    return [pl.BlockSpec(memory_space=pltpu.VMEM)] * count


def in_hbm():
    return pl.BlockSpec(memory_space=pl.ANY)


def shape(rows, columns, dtype=BF16):
    return jax.ShapeDtypeStruct((rows, columns), dtype)


KERNEL_VMEM = 60 * 2**20


def encoder_forward(x, segments, params):
    rows, d = x.shape[0] // 2, x.shape[1]
    ff = params[7].shape[1]
    outs = [
        shape(rows, d),
        shape(rows, d),
        shape(rows, 3 * d),
        shape(rows, H_ENC * rows),
        shape(rows, d, F32),
        shape(rows, d),
        shape(rows, d, F32),
        shape(rows, 1, F32),
        shape(rows, d),
        shape(rows, ff),
        shape(rows, ff),
    ]
    args = [x, segments, *params]
    return pl.pallas_call(
        encoder_forward_kernel,
        out_shape=outs,
        in_specs=[in_hbm() if a.dtype == BF16 and a is not x else in_vmem(1)[0] for a in args],
        out_specs=in_vmem(len(outs)),
        scratch_shapes=[pltpu.VMEM((rows, d), F32)]
        + [pltpu.VMEM(w.shape, BF16) for w in args if w.dtype == BF16 and w is not x]
        + [pltpu.SemaphoreType.DMA((4,))],
        compiler_params=pltpu.CompilerParams(vmem_limit_bytes=KERNEL_VMEM),
        name="encoder_forward",
    )(*args)


def encoder_backward(x, gy, saved, params):
    gain1, _, w_qkv, w_out, _, gain2, _, w_up, _, w_down, _ = params
    rows, d = gy.shape
    ff = w_up.shape[1]
    outs = [
        shape(rows, d),
        shape(rows, ff),
        shape(rows, d),
        shape(rows, 3 * d),
        shape(8, d, F32),
        shape(1, ff, F32),
    ]
    args = [x, gy, *saved, gain1, w_qkv, w_out, gain2, w_up, w_down]
    return pl.pallas_call(
        encoder_backward_kernel,
        out_shape=outs,
        in_specs=in_vmem(len(args)),
        out_specs=in_vmem(len(outs)),
        scratch_shapes=[pltpu.VMEM((rows, d), F32), pltpu.VMEM((rows, d), BF16)],
        compiler_params=pltpu.CompilerParams(vmem_limit_bytes=KERNEL_VMEM),
        name="encoder_backward",
    )(*args)


def decoder_both(y, slots, g, embed_params, params):
    packed, d_enc = y.shape
    total, d = g.shape[0] // 2, g.shape[1]
    samples = 6
    rows = samples * PATCHES
    steps = total // rows
    ff = params[7].shape[1]
    pos = positions(PATCHES, d)
    args = [y, slots.reshape(total, 1), slots.reshape(steps, 1, rows), pos, g]
    args += [*embed_params, *params]

    def whole(x):
        return pl.BlockSpec(x.shape, lambda i: (0,) * len(x.shape), pipeline_mode=pl.Buffered(1))

    def part(columns):
        return pl.BlockSpec((rows, columns), lambda i: (i, 0))

    in_specs = [
        whole(y),
        part(1),
        pl.BlockSpec((1, 1, rows), lambda i: (i, 0, 0)),
        whole(pos),
        pl.BlockSpec(memory_space=pl.ANY),
    ] + [whole(x) for x in args[5:]]
    turned = pl.BlockSpec((d, rows), lambda i: (0, i))
    wide = [ff, ff, d, 3 * d]
    outs = [shape(total, d)] + [shape(d, total)] * 4 + [shape(total, w) for w in wide]
    out_specs = [part(d)] + [turned] * 4 + [part(w) for w in wide]
    last = [shape(packed, d), shape(packed, d_enc), shape(8, d, F32), shape(1, ff, F32)]
    outs += last
    out_specs += [pl.BlockSpec(x.shape, lambda i: (0, 0)) for x in last]
    scratch = [
        (2 * packed, d, BF16),
        (rows, d, F32),
        (rows, 1, F32),
        (rows, 3 * d, BF16),
        (rows, H_DEC * PATCHES, BF16),
        (rows, d, F32),
        (rows, d, F32),
        (rows, 1, F32),
        (rows, ff, BF16),
        (rows, d, BF16),
        (packed, d, F32),
        (rows, d, BF16),
        (rows, d, BF16),
    ]
    return pl.pallas_call(
        decoder_kernel,
        out_shape=outs,
        grid=(steps,),
        in_specs=in_specs,
        out_specs=out_specs,
        scratch_shapes=[pltpu.VMEM((r, w), t) for r, w, t in scratch]
        + [pltpu.VMEM((2, rows, d), BF16), pltpu.SemaphoreType.DMA((2,))],
        compiler_params=pltpu.CompilerParams(
            vmem_limit_bytes=KERNEL_VMEM, dimension_semantics=("arbitrary",)
        ),
        name="decoder_both",
    )(*args)


def slot_rows(segments, patch_order):
    sample = jnp.arange(SAMP_MB, dtype=jnp.int32)[:, None]
    start = jnp.sum((segments[None, :] < sample).astype(jnp.int32), axis=1)
    count = jnp.sum((segments[None, :] == sample).astype(jnp.int32), axis=1)
    patch = jnp.arange(PATCHES, dtype=jnp.int32)
    hit = patch_order[:, None, :] == patch[None, :, None]
    rank = jnp.sum(jnp.where(hit, patch[None, None, :], 0), axis=2)
    return jnp.where(rank < count[:, None], start[:, None] + rank, -1)


MESH = pl.DeviceIdType.MESH
ENC_QKV, ENC_OUT, ENC_UP, ENC_DOWN, EMBED, DEC_QKV, DEC_OUT, DEC_UP, DEC_DOWN = range(9)
GIVE, PAIR, FFN, LN2, UT, CT, GO, ATT, OT, AT, GN, LAST = range(10, 22)
SMALL = -1
ROW_BUP, ROW_DEC_BUP, ROW_DEC, SMALL_ROWS = 6, 10, 16, 24
Z, Y, X, CORE = range(4)
ORDERS = ((X, Y, Z), (Y, X, Z), (X, Z, Y), (Y, Z, X))


class Chunk:
    def __init__(self, name, half, offset, rows, width, first_row=None):
        self.name, self.half, self.offset, self.rows, self.width = name, half, offset, rows, width
        self.first_row, self.turned, self.order = first_row, name == DEC_DOWN, None
        self.decoder = name in (DEC_QKV, DEC_UP, DEC_OUT)

    def columns(self, side):
        return pl.ds(pl.multiple_of(side * self.half + self.offset, 128), self.width)

    def place(self, side):
        if self.turned:
            return (pl.ds(pl.multiple_of(side * self.half + self.offset, 128), self.rows), slice(None))
        if self.first_row is None:
            return (slice(None), self.columns(side))
        return (pl.ds(self.first_row, self.rows), self.columns(side))

    @property
    def bytes(self):
        return 32 * self.rows * self.width

    def loads(self, order):
        first, second, third = order
        if second == Z:
            return (self.bytes, self.bytes, self.bytes / 8)
        return (self.bytes, self.bytes / 2, self.bytes / 2)


def make_chunks():
    chunks = [Chunk(DEC_QKV, 768, o, 32, 256) for o in (0, 256, 512)]
    chunks += [Chunk(DEC_OUT, 256, 0, 32, 256)]
    chunks += [Chunk(ENC_DOWN, 384, 0, 48, 384, 48 * q) for q in range(4)]
    chunks += [Chunk(ENC_UP, 1536, o, 48, 384) for o in (0, 384, 768, 1152)]
    chunks += [Chunk(ENC_OUT, 384, 0, 48, 384)]
    chunks += [Chunk(ENC_QKV, 1152, o, 48, 384) for o in (0, 384, 768)]
    chunks += [Chunk(DEC_UP, 1024, o, 32, 256) for o in (0, 256, 512, 768)]
    chunks += [Chunk(DEC_DOWN, 256, o, 128, 128) for o in (0, 128)]
    chunks += [Chunk(EMBED, 256, 0, 48, 256)]
    load = [0.0, 0.0, 0.0]
    for chunk in chunks:

        def after(order):
            new = list(load)
            for axis, size in zip(order, chunk.loads(order)):
                new[axis] += size
            return new

        chunk.order = min(ORDERS, key=lambda order: (max(after(order)), sum(after(order))))
        load = after(chunk.order)
    return chunks


def tasks_in_order(chunks):
    def gives(name, cost):
        return [(GIVE, c, cost) for c, k in enumerate(chunks) if k.name == name]

    tasks = gives(DEC_QKV, 1.3) + gives(DEC_OUT, 1.3)
    tasks += [(FFN, t, 2.8) for t in range(4)] + [(UT, 0, 1.0)]
    tasks += gives(ENC_DOWN, 0.8) + [(CT, 0, 0.6)] + gives(ENC_UP, 0.8)
    tasks += [(LN2, 0, 1.5), (GO, 0, 1.3)]
    tasks += [(ATT, g, 2.5) for g in range(6)]
    tasks += [(OT, 0, 0.6)] + gives(ENC_OUT, 0.8) + [(AT, 0, 0.6)] + gives(ENC_QKV, 0.8)
    tasks += [(GN, j, 1.3) for j in range(3)] + [(LAST, 0, 2.0)]
    tasks += gives(DEC_UP, 1.3)
    tasks.append((PAIR, [c for c, k in enumerate(chunks) if k.turned], 6.0))
    tasks += gives(EMBED, 1.0)
    return tasks


def decoder_arrays(chunks):
    names = []
    for k in chunks:
        if (k.decoder or k.turned) and k.name not in names:
            names.append(k.name)
    return names


def make_plan(chunks):
    tasks = tasks_in_order(chunks)
    lhs = decoder_arrays(chunks)
    free = [0.0] * 4
    rate = [82e3, 82e3, 82e3, 500e3]
    pending, plan, now, owned = [], [], 2.0, set()

    def send(link, size, latency):
        begin = max(now, free[link])
        free[link] = begin + size / rate[link]
        return free[link] + latency

    def blocked(task):
        if task[0] not in (GIVE, PAIR):
            return False
        name = chunks[task[1] if task[0] == GIVE else task[1][0]].name
        if name not in lhs[2:]:
            return False
        name = lhs[lhs.index(name) - 2]
        return any(k.name == name and c not in owned for c, k in enumerate(chunks))

    while tasks or pending:
        pending.sort()
        if pending and (pending[0][0] <= now or not tasks or blocked(tasks[0])):
            arrive, stage, c = pending.pop(0)
            now = max(now, arrive)
            plan.append((stage, c))
            if c == SMALL:
                now += 0.1
                if stage < 4:
                    pending.append((now + 2.0, stage + 1, c))
                continue
            k = chunks[c]
            if stage == 1:
                owned.add(c)
                now += 0.3 if k.turned else 1.5 if k.decoder else 1.0
            else:
                now += 0.2
            if stage < 4:
                axis = k.order[stage - 1]
                latency = 2.0 if axis == Z else 1.5
                pending.append((send(axis, k.loads(k.order)[stage - 1], latency), stage + 1, c))
            elif stage == 4:
                pending.append((send(CORE, k.bytes / 16, 1.0), 5, c))
            continue
        name, arg, cost = tasks.pop(0)
        plan.append((name, arg))
        now += cost
        if name in (GIVE, PAIR):
            for c in arg if name == PAIR else [arg]:
                pending.append((send(CORE, chunks[c].bytes, 1.0), 1, c))
        elif name == LAST:
            pending.append((now + 2.0, 1, SMALL))
    return plan


class Ring:
    def __init__(self, sources, slots, semaphores):
        self.copies = [
            pltpu.make_async_copy(source, slots[i % len(slots)], semaphores())
            for i, source in enumerate(sources)
        ]
        self.slots, self.at = slots, 0

    def begin(self):
        for copy in self.copies[: len(self.slots)]:
            copy.start()

    def take(self):
        self.copies[self.at].wait()
        return self.slots[self.at % len(self.slots)]

    def done(self):
        ahead = self.at + len(self.slots)
        if ahead < len(self.copies):
            self.copies[ahead].start()
        self.at += 1


class Names:
    def __init__(self, names, refs):
        self.__dict__.update(zip(names, refs))


LOADS = 96


def finish_kernel(chunks, plan, r):
    n = len(chunks)
    s = lax.axis_index("section")
    d = lax.axis_index("dp")
    here = (d // 4, (d // 2) % 2, d % 2)
    z, y, x = here
    sibling = {"section": 1 - s}
    z_at = [lax.rem(z + k, 4) for k in (1, 2, 3)]
    peers = {
        X: [(1 - x, {"dp": d + 1 - 2 * x})],
        Y: [(1 - y, {"dp": d + 2 - 4 * y})],
        Z: [(p, {"dp": d + 4 * (p - z)}) for p in z_at],
    }
    every = [sibling] + [peer for axis in (X, Y, Z) for _, peer in peers[axis]]

    barrier = pltpu.get_barrier_semaphore()
    for peer in every:
        pl.semaphore_signal(barrier, inc=1, device_id=peer, device_id_type=MESH)

    counter = iter(range(LOADS))

    def semaphore():
        return r.load_sem.at[next(counter)]

    def remote(src, dst, send, recv, peer):
        return pltpu.make_async_remote_copy(
            src_ref=src, dst_ref=dst, send_sem=send, recv_sem=recv, device_id=peer, device_id_type=MESH
        )

    rhs_of = {DEC_QKV: r.gqkv2, DEC_UP: r.gf2, DEC_OUT: r.ga2}
    lhs_of = {DEC_QKV: r.at2, DEC_UP: r.ct2, DEC_OUT: r.ot2, DEC_DOWN: r.gt2}
    tiles, last_use = [], {}
    for i, (name, arg) in enumerate(plan):
        if name == PAIR:
            tiles += [r.u2.at[:, t * 256 : (t + 1) * 256] for t in range(8)]
            last_use[DEC_DOWN] = i
        elif name in (GIVE, 1) and arg != SMALL and chunks[arg].decoder:
            k = chunks[arg]
            tiles.append(rhs_of[k.name].at[:, k.columns(1 - s if name == GIVE else s)])
            last_use[k.name] = i
    lhs_names = decoder_arrays(chunks)
    assert sorted(lhs_names, key=last_use.get) == lhs_names
    rhs = Ring(tiles, [r.rhs.at[i] for i in range(3)], semaphore)
    lhs = Ring([lhs_of[k] for k in lhs_names], [r.lhs.at[i] for i in range(2)], semaphore)
    lhs.copies[0].start()
    rhs.begin()
    lhs.copies[1].start()
    tokens, d_enc = r.gy.shape
    blocks = []
    for t in range(4):
        at = pl.ds(t * d_enc, d_enc)
        blocks += [r.w_down.at[at, :], r.w_up.at[:, at]]
    blocks.append(r.w_out)
    blocks += [r.w_qkv.at[:, pl.ds(j * d_enc, d_enc)] for j in range(3)]
    weights = Ring(blocks, [r.w.at[i] for i in range(4)], semaphore)
    e_width = 2 * tokens
    e_ring = Ring(
        [r.e.at[:, pl.ds(g * e_width, e_width)] for g in range(6)],
        [r.e_v.at[i] for i in range(2)],
        semaphore,
    )

    def load(source, target):
        return pltpu.make_async_copy(source, target, semaphore())

    mine = pl.ds(pl.multiple_of(s * tokens, tokens), tokens)
    load_gy, load_slope, load_u = load(r.gy, r.gy_v), load(r.slope, r.slope_v), load(r.u, r.u_v)
    load_c, load_a, load_n2 = load(r.c, r.c_v), load(r.a, r.c_v), load(r.n2, r.n2_v)
    load_s2, load_qkv, load_o = load(r.s2, r.s2_v), load(r.qkv, r.qkv_v), load(r.o, r.o_v)
    load_rl, load_x = load(r.rl, r.rl_v), load(r.x.at[mine, :], r.x_v)
    load_y, load_geb = load(r.y, r.y_v), load(r.geb, r.geb_v)
    load_gy.start()
    load_slope.start()
    weights.begin()
    for copy in (load_u, load_c, load_n2, load_s2, load_qkv, load_o, load_rl):
        copy.start()
    e_ring.begin()
    for copy in (load_x, load_y, load_geb):
        copy.start()

    half = r.decoded.shape[1] // 2
    give_half = r.decoded.at[:, pl.ds(pl.multiple_of((1 - s) * half, half), half), :]
    decoded_away = remote(give_half, r.decoded_got, r.swap_sem.at[0], r.swap_sem.at[1], sibling)
    gx_columns = d_enc // 2
    gx_half = r.gx.at[:, pl.ds(pl.multiple_of((1 - s) * gx_columns, 128), gx_columns)]
    gx_away = remote(gx_half, r.gx_got, r.swap_sem.at[2], r.swap_sem.at[3], sibling)

    small = r.small
    small[...] = jnp.zeros_like(small)
    small[ROW_DEC : ROW_DEC + 8, : r.small2.shape[1]] = r.small2[...]
    quarter = r.gbup2.shape[1] // 4
    for i in range(4):
        piece = r.gbup2[:, i * quarter : (i + 1) * quarter]
        small[ROW_DEC_BUP + i : ROW_DEC_BUP + i + 1, :quarter] = piece

    pl.semaphore_wait(barrier, len(every))

    copies = {}
    first_slot = (0, 1, 2, 5, 8)

    def chunk_copy(c, slot, src, dst, peer):
        copy = remote(src, dst, r.send_sem.at[c, slot], r.recv_sem.at[c, slot], peer)
        copy.start()
        copies[c, slot] = copy

    sent = set()

    def sent_by(c, slot):
        if (c, slot) not in sent:
            sent.add((c, slot))
            copies[c, slot].wait_send()

    staged = {}

    def staging(c):
        k = chunks[c]
        buffers = r.stage[k.rows, k.width]
        turn = staged.setdefault((k.rows, k.width), [])
        if len(turn) >= len(buffers):
            sent_by(turn[-len(buffers)], 0)
        turn.append(c)
        return buffers[(len(turn) - 1) % len(buffers)]

    def shard(i):
        return (i // 4, (i // 2) % 2, i % 2)

    def product(k, side):
        columns = k.columns(side)
        if k.decoder:
            return mm(lhs.slots[lhs_names.index(k.name) % 2][...], rhs.take()[...])
        if k.name == EMBED:
            return mm_tn(r.y_v[...], r.geb_v[:, columns])
        if k.name == ENC_DOWN:
            at = [i * 192 + k.first_row for i in range(16)]
            left = jnp.concatenate([r.ut_v[i : i + k.rows, :] for i in at], axis=0)
            return mm(left, r.gy_v[:, columns])
        if k.name == ENC_UP:
            return mm(r.ct_v[...], r.slope_v[:, columns])
        if k.name == ENC_OUT:
            return mm(r.ot_v[...], r.ga_v[:, columns])
        return mm(r.at_v[...], r.qkv_v[:, columns])

    def after_product(i, k):
        if k.decoder:
            rhs.done()
            if last_use[k.name] == i:
                lhs.done()

    waited = set()

    def wait_lhs(k):
        if k.name in lhs_names and k.name not in waited:
            waited.add(k.name)
            lhs.copies[lhs_names.index(k.name)].wait()

    def give(i, c):
        k = chunks[c]
        if k.name == EMBED:
            load_y.wait()
            load_geb.wait()
        wait_lhs(k)
        buffer = staging(c)
        value = product(k, 1 - s).astype(BF16)
        for j in range(16):
            buffer[shard(j)] = value[j * k.rows : (j + 1) * k.rows]
        after_product(i, k)
        chunk_copy(c, 0, buffer, r.acc[c], sibling)

    def pair(i, both):
        wait_lhs(chunks[both[0]])
        left = lhs.slots[lhs_names.index(DEC_DOWN) % 2]
        side_rows = chunks[both[0]].half
        buffers = [staging(c) for c in both]
        for t in range(8):
            tile = rhs.take()
            for side, targets in ((1 - s, buffers), (s, [r.acc[c] for c in both])):
                at = pl.ds(pl.multiple_of(side * side_rows, side_rows), side_rows)
                value = mm(left[at, :], tile[...]).astype(BF16)
                for c, target in zip(both, targets):
                    k = chunks[c]
                    rows = slice(k.offset, k.offset + k.rows)
                    for j in range(2):
                        target[shard(2 * t + j)] = value[rows, j * k.width : (j + 1) * k.width]
            rhs.done()
        lhs.done()
        for c, buffer in zip(both, buffers):
            chunk_copy(c, 0, buffer, r.got[c], sibling)

    def spots(k, stage):
        fixed = {axis: here[axis] for axis in k.order[: stage - 1]}
        return [fixed.get(axis, slice(None)) for axis in (Z, Y, X)]

    def send_stage(c, stage):
        k = chunks[c]
        axis = k.order[stage - 1]
        for j, (coordinate, peer) in enumerate(peers[axis]):
            at = spots(k, stage)
            at[axis] = coordinate
            src = r.acc[c].at[tuple(at)]
            chunk_copy(c, first_slot[stage] + j, src, r.recv[stage - 1][c].at[j], peer)

    def got_stage(c, stage):
        k = chunks[c]
        count = len(peers[k.order[stage - 1]])
        for j in range(count):
            copies[c, first_slot[stage] + j].wait_recv()
        return count

    def add_stage(c, stage):
        k, acc, got = chunks[c], r.acc[c], r.recv[stage - 1][c]
        count = got_stage(c, stage)
        left = [axis for axis in (Z, Y, X) if axis not in k.order[:stage]]
        sizes = [(4, 2, 2)[axis] for axis in left]
        for j in range(math.prod(sizes)):
            place, rest = {}, j
            for axis, size in reversed(list(zip(left, sizes))):
                place[axis] = rest % size
                rest //= size
            at = tuple(place.get(axis, here[axis]) for axis in (Z, Y, X))
            index = tuple(place[axis] for axis in left)
            if count == 1:
                acc[at] = acc[at] + got[(0,) + index]
            else:
                total = acc[at].astype(F32)
                for m in range(count):
                    total = total + got[(m,) + index].astype(F32)
                acc[at] = total.astype(BF16)

    def stage1(i, c):
        k, acc = chunks[c], r.acc[c]
        copies[c, 0].wait_recv()
        if k.turned:
            for j in range(16):
                acc[shard(j)] = acc[shard(j)] + r.got[c][shard(j)]
        else:
            value = product(k, s)
            for j in range(16):
                part = value[j * k.rows : (j + 1) * k.rows]
                acc[shard(j)] = (part + acc[shard(j)].astype(F32)).astype(BF16)
            after_product(i, k)
        send_stage(c, 1)

    def stage2(i, c):
        add_stage(c, 1)
        send_stage(c, 2)

    def stage3(i, c):
        add_stage(c, 2)
        send_stage(c, 3)

    def stage4(i, c):
        k = chunks[c]
        total = r.acc[c][here].astype(F32)
        for j in range(got_stage(c, 3)):
            total = total + r.recv[2][c][j].astype(F32)
        out = r.out[k.name]
        out[k.place(s)] = total.astype(BF16)
        final = out.at[k.place(s)]
        chunk_copy(c, 8, final, final, sibling)

    def stage5(i, c):
        copies[c, 8].wait_recv()

    small_copies = []

    def small_copy(source, peer):
        slot = len(small_copies)
        copy = remote(
            source, r.small_got.at[slot], r.small_sem.at[0, slot], r.small_sem.at[1, slot], peer
        )
        copy.start()
        small_copies.append(copy)

    def small_stage(stage):
        if stage < 4:
            small_copies[stage - 1].wait()
            total = small[...] + r.small_got[stage - 1]
            if stage < 3:
                small[...] = total
                small_copy(small, peers[X if stage == 1 else Y][0][1])
            else:
                r.small_sum[...] = total
                for _, peer in peers[Z]:
                    small_copy(r.small_sum, peer)
        else:
            total = r.small_sum[...]
            for j in range(3):
                small_copies[3 + j].wait()
                total = total + r.small_got[3 + j]
            r.out_small[...] = total

    def ffn(i, t):
        if t == 0:
            load_gy.wait()
            load_slope.wait()
        at = slice(t * d_enc, (t + 1) * d_enc)
        gu = mm_nt(r.gy_v[...], weights.take()[...])
        weights.done()
        gf = (gu * r.slope_v[:, at].astype(F32)).astype(BF16)
        r.slope_v[:, at] = gf
        small[ROW_BUP + t : ROW_BUP + t + 1, :] = rows_sum(gf.astype(F32))
        gc = mm_nt(gf, weights.take()[...])
        weights.done()
        r.sum_v[...] = gc if t == 0 else r.sum_v[...] + gc

    def ln2(i, _):
        load_n2.wait()
        load_s2.wait()
        g, gc, n2 = r.gy_v[...].astype(F32), r.sum_v[...], r.n2_v[...]
        gh = g + normalise_back(gc, n2, r.s2_v[...], row(r.gain2))
        small[2:3, :] = rows_sum(gh)
        small[3:4, :] = rows_sum(gc * n2)
        small[4:5, :] = rows_sum(gc)
        small[5:6, :] = rows_sum(g)
        r.n2_v[...] = gh
        r.ga_v[...] = gh.astype(BF16)

    def ut(i, _):
        load_u.wait()
        for t in range(8):
            at = slice(t * 384, (t + 1) * 384)
            r.ut_v[at, :] = jnp.transpose(r.u_v[:, at])

    def ct(i, _):
        load_c.wait()
        r.ct_v[...] = jnp.transpose(r.c_v[...])
        load_a.start()

    def go(i, _):
        r.go_v[...] = mm_nt(r.ga_v[...], weights.take()[...]).astype(BF16)
        weights.done()

    def att(i, g):
        if g == 0:
            for copy in (load_qkv, load_o, load_rl):
                copy.wait()
        at = slice(g * 128, (g + 1) * 128)
        parts = [slice(j * d_enc + g * 128, j * d_enc + (g + 1) * 128) for j in range(3)]
        q, k, v = (r.qkv_v[:, part] for part in parts)
        grads = attention_backward_group(
            q, k, v, e_ring.take()[...], r.go_v[:, at], r.o_v[:, at], r.rl_v[:, at],
            d_enc // H_ENC,
        )
        e_ring.done()
        for part, grad in zip(parts, grads):
            r.qkv_v[:, part] = grad

    def ot(i, _):
        r.ot_v[...] = jnp.transpose(r.o_v[...])

    def at_task(i, _):
        load_a.wait()
        r.at_v[...] = jnp.transpose(r.c_v[...])

    def gn(i, j):
        part = mm_nt(r.qkv_v[:, j * d_enc : (j + 1) * d_enc], weights.take()[...])
        weights.done()
        r.sum_v[...] = part if j == 0 else r.sum_v[...] + part

    def last(i, _):
        load_x.wait()
        n1, s1 = normalise(r.x_v[...].astype(F32))
        total = r.sum_v[...]
        small[0:1, :] = rows_sum(total * n1)
        small[1:2, :] = rows_sum(total)
        small_copy(small, sibling)
        gx = r.n2_v[...] + normalise_back(total, n1, s1, row(r.gain1))
        r.gx[...] = gx.astype(BF16)
        gx_away.start()
        decoded_away.start()

    run = {
        GIVE: give, PAIR: pair, FFN: ffn, LN2: ln2, UT: ut, CT: ct, GO: go, ATT: att, OT: ot,
        AT: at_task, GN: gn, LAST: last, 1: stage1, 2: stage2, 3: stage3, 4: stage4, 5: stage5,
    }
    for i, (name, arg) in enumerate(plan):
        if arg == SMALL:
            small_stage(name)
        else:
            run[name](i, arg)

    for c, slot in copies:
        sent_by(c, slot)
    gx_away.wait()
    decoded_away.wait()


def finish_buffers(chunks, rows, d, ff, dec_total, dec):
    def of(dtype, *dims):
        return (dims, dtype)

    return dict(
        y_v=of(BF16, rows, d),
        geb_v=of(BF16, rows, dec),
        gy_v=of(BF16, rows, d),
        slope_v=of(BF16, rows, ff),
        n2_v=of(F32, rows, d),
        s2_v=of(F32, rows, 1),
        u_v=of(BF16, rows, ff),
        c_v=of(BF16, rows, d),
        qkv_v=of(BF16, rows, 3 * d),
        o_v=of(BF16, rows, d),
        rl_v=of(F32, rows, d),
        x_v=of(BF16, rows, d),
        ga_v=of(BF16, rows, d),
        go_v=of(BF16, rows, d),
        sum_v=of(F32, rows, d),
        ut_v=of(BF16, ff, rows),
        ct_v=of(BF16, d, rows),
        at_v=of(BF16, d, rows),
        ot_v=of(BF16, d, rows),
        e_v=of(BF16, 2, rows, 2 * rows),
        w=of(BF16, 4, d, d),
        lhs=of(BF16, 2, dec, dec_total),
        rhs=of(BF16, 3, dec_total, 256),
        small=of(F32, SMALL_ROWS, d),
        small_sum=of(F32, SMALL_ROWS, d),
        small_got=of(F32, 6, SMALL_ROWS, d),
    )


def finish(acts):
    enc, dec = acts["enc"], acts["dec"]
    gain1, _, w_qkv, w_out, _, gain2, _, w_up, _, w_down, _ = enc["params"]
    qkv, e, rl, o, n2, s2, slope = acts["saved"]
    given = dict(
        x=acts["x"], y=acts["y"], gy=acts["gy"], geb=acts["geb"], qkv=qkv, e=e, rl=rl, o=o, n2=n2,
        s2=s2, slope=slope, a=enc["a"], c=enc["c"], u=enc["u"], at2=dec["at"], ot2=dec["ot"],
        ct2=dec["ct"], gt2=dec["gt"], u2=dec["u"], gf2=dec["gf"], ga2=dec["ga"],
        gqkv2=dec["gqkv"], w_qkv=w_qkv, w_out=w_out, w_up=w_up, w_down=w_down,
        decoded=acts["decoded"].reshape(SAMP_MB, PATCHES, -1),
    )
    n_hbm = len(given)
    given.update(small2=acts["small2"], gbup2=acts["gbup2"], gain1=gain1, gain2=gain2)
    rows, d = acts["gy"].shape
    ff = w_up.shape[1]
    dec_d, dec_total = dec["at"].shape
    dec_ff = dec["u"].shape[1]
    chunks = make_chunks()
    n = len(chunks)
    plan = make_plan(chunks)

    dims = {
        ENC_QKV: (d, 3 * d), ENC_OUT: (d, d), ENC_UP: (d, ff), ENC_DOWN: (ff, d),
        EMBED: (d, dec_d), DEC_QKV: (dec_d, 3 * dec_d), DEC_OUT: (dec_d, dec_d),
        DEC_UP: (dec_d, dec_ff), DEC_DOWN: (dec_ff, dec_d),
    }
    big = [
        shape(dims[k][1], dims[k][0] // 16) if k == DEC_DOWN else shape(dims[k][0] // 16, dims[k][1])
        for k in range(9)
    ]
    outs = dict(
        out_small=shape(SMALL_ROWS, d, F32),
        decoded_got=jax.ShapeDtypeStruct((SAMP_MB, PATCHES // 2, dec_d), BF16),
        gx=shape(rows, d),
        gx_got=shape(rows, d // 2),
    )
    single = finish_buffers(chunks, rows, d, ff, dec_total, dec_d)
    left = (4, 2, 2)
    lists = [[], [], [], [], []]
    for k in chunks:
        block = (k.rows, k.width)
        lists[0].append((left + block, BF16))
        if k.turned:
            lists[1].append((left + block, BF16))
        for stage in range(3):
            rest = [left[axis] for axis in (Z, Y, X) if axis not in k.order[: stage + 1]]
            count = 3 if k.order[stage] == Z else 1
            lists[2 + stage].append(((count, *rest, *block), BF16))
    blocks = sorted({(k.rows, k.width) for k in chunks})
    lists.append([(left + block, BF16) for block in blocks for _ in range(2)])
    semaphores = dict(
        load_sem=(LOADS,), send_sem=(n, 9), recv_sem=(n, 9), small_sem=(2, 6), swap_sem=(4,)
    )

    def kernel(*refs):
        refs = list(refs)

        def take(count):
            taken = refs[:count]
            del refs[:count]
            return taken

        names = list(given) + list(outs)
        r = Names(names, take(len(names)))
        r.out = take(9)
        r.__dict__.update(zip(single, take(len(single))))
        r.acc = take(n)
        r.got = dict(zip([c for c, k in enumerate(chunks) if k.turned], take(len(lists[1]))))
        r.recv = [take(n) for _ in range(3)]
        r.stage = {block: take(2) for block in blocks}
        r.__dict__.update(zip(semaphores, take(len(semaphores))))
        finish_kernel(chunks, plan, r)

    flat = list(single.values()) + [b for group in lists for b in group]
    results = pl.pallas_call(
        kernel,
        out_shape=list(outs.values()) + big,
        in_specs=[in_hbm()] * n_hbm + in_vmem(len(given) - n_hbm),
        out_specs=in_vmem(len(outs) + 9),
        scratch_shapes=[pltpu.VMEM(*b) for b in flat]
        + [pltpu.SemaphoreType.DMA(v) for v in semaphores.values()],
        compiler_params=pltpu.CompilerParams(
            collective_id=1, has_side_effects=True, vmem_limit_bytes=FINISH_VMEM
        ),
        name="finish",
    )(*given.values())
    return write_outputs(results, given["decoded"], dims)


FINISH_VMEM = 62 * 2**20


def write_kernel(small, decoded_got, gx_own, gx_got, *refs):
    big, decoded_own = refs[:9], refs[9]
    decoded, gx, *totals = refs[10:]
    s = lax.axis_index("section")
    half = decoded.shape[1]
    samples, rows, columns = decoded_own.shape[0], gx_own.shape[0], gx.shape[1]
    own = decoded_own[:, pl.ds(pl.multiple_of(s * half, half), half), :]
    for side, part in ((s, own), (1 - s, decoded_got[...])):
        decoded[pl.ds(side * samples, samples)] = part
    own = gx_own[:, pl.ds(pl.multiple_of(s * columns, 128), columns)]
    for side, part in ((s, own), (1 - s, gx_got[...])):
        gx[pl.ds(pl.multiple_of(side * rows, rows), rows), :] = part
    d = lax.axis_index("dp")
    wide, narrow = small.shape[1], big[DEC_OUT].shape[1]

    def piece(out, line, lanes, position):
        size = out.shape[0]
        value = small[pl.ds(line, 1), :lanes]
        value = pltpu.roll(value, lax.rem(lanes - position * size, lanes), 1)
        out[...] = value[:, :size].reshape(size)

    def matrix(out, name):
        value = big[name][...].astype(F32)
        out[...] = jnp.transpose(value) if name == DEC_DOWN else value

    def block(outs, first_row, bup_row, lanes, names):
        for i, out in zip((0, 1, None, None, 2, 3, 4, None, None, None, 5), outs):
            if i is not None:
                piece(out, first_row + i, lanes, d)
        piece(outs[8], bup_row + d // 4, lanes, d % 4)
        for at, name in zip((2, 3, 7, 9), names):
            matrix(outs[at], name)

    block(totals[:11], 0, ROW_BUP, wide, (ENC_QKV, ENC_OUT, ENC_UP, ENC_DOWN))
    matrix(totals[11], EMBED)
    piece(totals[12], ROW_DEC + 7, narrow, d)
    piece(totals[13], ROW_DEC + 6, narrow, d)
    block(totals[14:], ROW_DEC, ROW_DEC_BUP, narrow, (DEC_QKV, DEC_OUT, DEC_UP, DEC_DOWN))


def write_outputs(results, decoded_own, dims):
    def vector(size):
        return jax.ShapeDtypeStruct((size // 16,), F32)

    def matrix(name):
        return shape(dims[name][0] // 16, dims[name][1], F32)

    def block(qkv, out, up, down):
        d, ff = dims[up]
        return [
            vector(d), vector(d), matrix(qkv), matrix(out), vector(d), vector(d), vector(d),
            matrix(up), vector(ff), matrix(down), vector(d),
        ]

    samples, half, width = results[1].shape
    rows, columns = results[3].shape
    out_shape = [
        jax.ShapeDtypeStruct((2 * samples, half, width), BF16),
        shape(2 * rows, columns),
        *block(ENC_QKV, ENC_OUT, ENC_UP, ENC_DOWN),
        matrix(EMBED),
        vector(width),
        vector(width),
        *block(DEC_QKV, DEC_OUT, DEC_UP, DEC_DOWN),
    ]
    return tuple(
        pl.pallas_call(
            write_kernel,
            out_shape=out_shape,
            in_specs=in_vmem(len(results) + 1),
            out_specs=in_vmem(len(out_shape)),
            compiler_params=pltpu.CompilerParams(vmem_limit_bytes=KERNEL_VMEM),
            name="write_outputs",
        )(*results, decoded_own)
    )


def reduce_plain(arrays, section_index):
    first = section_index == 0
    results = []
    for a in arrays:
        half = a.shape[1] // 2
        keep = lax.dynamic_slice_in_dim(a, section_index * half, half, 1)
        give = lax.dynamic_slice_in_dim(a, (1 - section_index) * half, half, 1)
        got = swapped(give, "section", 0)
        chip = (keep.astype(jnp.float32) + got.astype(jnp.float32)).astype(jnp.bfloat16)
        mine = lax.psum_scatter(chip, "dp", scatter_dimension=0, tiled=True)
        other = swapped(mine, "section", 0)
        whole = jnp.concatenate(
            [jnp.where(first, mine, other), jnp.where(first, other, mine)], axis=1
        )
        results.append(whole.astype(jnp.float32))
    return results


def finish_plain(acts, section_index):
    x, gy, seg_saved, enc, dec = acts["x"], acts["gy"], acts["saved"], acts["enc"], acts["dec"]
    gx, gf1, ga1, gqkv1, small1, gbup1 = encoder_backward(x, gy, seg_saved, enc["params"])
    small2, gbup2 = acts["small2"], acts["gbup2"]
    grads = (
        small1[0], small1[1], weight_grad(enc["a"], gqkv1), weight_grad(enc["o"], ga1), small1[2],
        small1[3], small1[4], weight_grad(enc["c"], gf1), gbup1[0], weight_grad(enc["u"], gy),
        small1[5],
        weight_grad(acts["y"], acts["geb"]), small2[7], small2[6],
        small2[0], small2[1], mm(dec["at"], dec["gqkv"]).astype(BF16),
        mm(dec["ot"], dec["ga"]).astype(BF16), small2[2], small2[3], small2[4],
        mm(dec["ct"], dec["gf"]).astype(BF16), gbup2[0],
        jnp.transpose(mm(dec["gt"], dec["u"])).astype(BF16), small2[5],
    )
    groups = lax.axis_size("dp")
    big = reduce_plain([g for g in grads if g.ndim == 2], section_index)
    flat = jnp.concatenate([g.reshape(groups, -1) for g in grads if g.ndim == 1], axis=1)
    line = lax.psum_scatter(flat, ("dp"), scatter_dimension=0, tiled=True)
    line = lax.psum(line, "section")[0]
    totals, at = [], 0
    for g in grads:
        if g.ndim == 2:
            totals.append(big.pop(0))
        else:
            size = g.shape[0] // groups
            totals.append(line[at : at + size])
            at += size
    decoded = acts["decoded"].reshape(SAMP_MB, PATCHES, -1)
    first = section_index == 0

    def halves(whole):
        half = whole.shape[1] // 2
        keep = lax.dynamic_slice_in_dim(whole, section_index * half, half, 1)
        give = lax.dynamic_slice_in_dim(whole, (1 - section_index) * half, half, 1)
        got = swapped(give, "section", 0)
        return jnp.concatenate([jnp.where(first, keep, got), jnp.where(first, got, keep)])

    return (halves(decoded), halves(gx), *totals)


def shards(
    patches,
    segment_ids,
    patch_order,
    encoder_gain1,
    encoder_bias1,
    encoder_qkv,
    encoder_out,
    encoder_out_bias,
    encoder_gain2,
    encoder_bias2,
    encoder_up,
    encoder_up_bias,
    encoder_down,
    encoder_down_bias,
    embed_weight,
    embed_bias,
    mask_token,
    decoder_gain1,
    decoder_bias1,
    decoder_qkv,
    decoder_out,
    decoder_out_bias,
    decoder_gain2,
    decoder_bias2,
    decoder_up,
    decoder_up_bias,
    decoder_down,
    decoder_down_bias,
    cotangent,
):
    enc_params = (
        encoder_gain1,
        encoder_bias1,
        encoder_qkv,
        encoder_out,
        encoder_out_bias,
        encoder_gain2,
        encoder_bias2,
        encoder_up,
        encoder_up_bias,
        encoder_down,
        encoder_down_bias,
    )
    embed_params = (embed_weight, embed_bias, mask_token)
    dec_params = (
        decoder_gain1,
        decoder_bias1,
        decoder_qkv,
        decoder_out,
        decoder_out_bias,
        decoder_gain2,
        decoder_bias2,
        decoder_up,
        decoder_up_bias,
        decoder_down,
        decoder_down_bias,
    )
    section_index = lax.axis_index("section")
    segments = lax.dynamic_index_in_dim(segment_ids, section_index, 0, keepdims=False)
    orders = lax.dynamic_slice_in_dim(patch_order, section_index * SAMP_MB, SAMP_MB, 0)
    slots = slot_rows(segments, orders)
    y, a1, qkv, e, rl, o1, n2, s2, c1, u1, slope = encoder_forward(patches, segment_ids, enc_params)
    g = cotangent.reshape(-1, DECODER_WIDTH)
    decoded, at2, ot2, ct2, gt2, u2, gf2, ga2, gqkv2, geb, gy, small2, gbup2 = decoder_both(
        y, slots, g, embed_params, dec_params
    )
    acts = dict(
        x=patches,
        y=y,
        gy=gy,
        geb=geb,
        decoded=decoded,
        small2=small2,
        gbup2=gbup2,
        saved=(qkv, e, rl, o1, n2, s2, slope),
        enc=dict(a=a1, o=o1, c=c1, u=u1, params=enc_params),
        dec=dict(at=at2, ot=ot2, ct=ct2, gt=gt2, u=u2, gf=gf2, ga=ga2, gqkv=gqkv2),
    )
    if lax.axis_size("dp") == 16:
        return finish(acts)
    return finish_plain(acts, section_index)


def solution(mesh):
    in_specs = (
        P("dp", None),
        P("dp", None),
        P("dp", None),
        P(),
        P(),
        P(),
        P(),
        P(),
        P(),
        P(),
        P(),
        P(),
        P(),
        P(),
        P(),
        P(),
        P(),
        P(),
        P(),
        P(),
        P(),
        P(),
        P(),
        P(),
        P(),
        P(),
        P(),
        P(),
        P("dp", None, None),
    )
    out_specs = (
        P("dp", "section", None),
        P("dp", "section"),
        P("dp"),
        P("dp"),
        P("dp", None),
        P("dp", None),
        P("dp"),
        P("dp"),
        P("dp"),
        P("dp", None),
        P("dp"),
        P("dp", None),
        P("dp"),
        P("dp", None),
        P("dp"),
        P("dp"),
        P("dp"),
        P("dp"),
        P("dp", None),
        P("dp", None),
        P("dp"),
        P("dp"),
        P("dp"),
        P("dp", None),
        P("dp"),
        P("dp", None),
        P("dp"),
    )
    return jax.shard_map(shards, mesh=mesh, in_specs=in_specs, out_specs=out_specs, check_vma=False)
```

```python
import functools
import math

import jax
import jax.numpy as jnp
import numpy as np
from jax import lax
from jax.experimental import pallas as pl
from jax.experimental.pallas import tpu as pltpu
from jax.sharding import PartitionSpec as P

H_ENC = 12
DECODER_WIDTH = 512
H_DEC = 16
PATCHES = 128
SAMP_MB = 12


EPSILON = 1e-06
MASKED = -1e30


def swapped(block, axis, apart):
    count = lax.axis_size(axis)
    route = []
    for low in range(count):
        high = low | 1 << apart
        if high != low and high < count:
            route += [(low, high), (high, low)]
    return lax.ppermute(block, axis, route)


def positions(count, features):
    column = np.arange(features)
    rate = np.exp(-math.log(10000.0) * (2 * (column // 2)) / features)
    angles = np.arange(count)[:, None] * rate[None, :]
    return np.where(column % 2 == 0, np.sin(angles), np.cos(angles)).astype(np.float32)


def weight_grad(left_side, grads):
    return lax.dot_general(
        left_side, grads, (((0,), (0,)), ((), ())), preferred_element_type=jnp.float32
    ).astype(jnp.bfloat16)


BF16 = jnp.bfloat16
F32 = jnp.float32


def mm(left, right):
    return lax.dot_general(left, right, (((1,), (0,)), ((), ())), preferred_element_type=F32)


def mm_nt(left, right):
    return lax.dot_general(left, right, (((1,), (1,)), ((), ())), preferred_element_type=F32)


def mm_tn(left, right):
    return lax.dot_general(left, right, (((0,), (0,)), ((), ())), preferred_element_type=F32)


def normalise(x):
    center = x - jnp.mean(x, axis=-1, keepdims=True)
    scale = lax.rsqrt(jnp.mean(center * center, axis=-1, keepdims=True) + EPSILON)
    return center * scale, scale


def normalise_back(grad, n, scale, gain):
    gn = grad * gain
    mean_gn = jnp.mean(gn, axis=-1, keepdims=True)
    mean_gnn = jnp.mean(gn * n, axis=-1, keepdims=True)
    return (gn - mean_gn - n * mean_gnn) * scale


def rows_sum(x):
    return jnp.sum(x, axis=0, keepdims=True)


def gelu_both(f):
    c0, c1 = math.sqrt(2.0 / math.pi), 0.044715
    square = f * f
    half = 0.5 + 0.5 * jnp.tanh(f * (c0 + (c0 * c1) * square))
    u = f * half
    return u, half + u * (1.0 - half) * (2.0 * c0 + (6.0 * c0 * c1) * square)


def lane_masks(head_size):
    lane = lax.broadcasted_iota(jnp.int32, (1, 128), 1)
    return [
        jnp.where((lane >= h * head_size) & (lane < (h + 1) * head_size), 1.0, 0.0).astype(BF16)
        for h in range(128 // head_size)
    ]


def stacked(x, masks):
    return jnp.concatenate([x * m for m in masks], axis=0)


def stacked_ones(x, masks, value):
    return jnp.concatenate(
        [jnp.broadcast_to(m * jnp.asarray(value, BF16), x.shape) for m in masks], axis=0
    )


def attention_forward(qkv_ref, o_ref, e_ref, rl_ref, rows, tokens, features, head_size, allowed):
    masks = lane_masks(head_size)
    per_group = len(masks)
    factor = head_size ** (-0.5) * math.log2(math.e)
    for g in range(features // 128):
        q, k, v = (qkv_ref[rows, j * features + g * 128 : j * features + (g + 1) * 128] for j in range(3))
        scores = mm_nt(q, stacked(k, masks))
        parts = []
        for h in range(per_group):
            part = scores[:, h * tokens : (h + 1) * tokens]
            if allowed is not None:
                part = jnp.where(allowed, part, MASKED)
            top = jnp.max(part, axis=-1, keepdims=True)
            parts.append(jnp.exp2((part - top) * factor).astype(BF16))
        e = jnp.concatenate(parts, axis=1)
        width = per_group * tokens
        e_ref[rows, g * width : (g + 1) * width] = e
        both = mm(e, jnp.concatenate([stacked(v, masks), stacked_ones(v, masks, 1.0)], axis=1))
        rl = 1.0 / both[:, 128:]
        rl_ref[rows, g * 128 : (g + 1) * 128] = rl
        o_ref[rows, g * 128 : (g + 1) * 128] = (both[:, :128] * rl).astype(BF16)


def attention_backward_group(q, k, v, e, go, o, rl, head_size):
    masks = lane_masks(head_size)
    per_group, tokens = len(masks), q.shape[0]
    scaling = head_size ** (-0.5)
    go = go.astype(F32) * rl
    go_low = go.astype(BF16)
    inner = (go * o.astype(F32)).astype(BF16)
    left = jnp.concatenate([go_low, inner], axis=1)
    right = jnp.concatenate([stacked(v, masks), stacked_ones(v, masks, -1.0)], axis=1)
    gs = (e.astype(F32) * mm_nt(left, right)).astype(BF16)

    def diagonal(wide):
        return jnp.concatenate(
            [
                wide[h * head_size : (h + 1) * head_size, h * tokens : (h + 1) * tokens]
                for h in range(per_group)
            ],
            axis=0,
        )

    gq = mm(gs, stacked(k, masks)) * scaling
    gk = jnp.transpose(diagonal(mm_tn(q, gs)) * scaling)
    gv = jnp.transpose(diagonal(mm_tn(go_low, e)))
    return gq.astype(BF16), gk.astype(BF16), gv.astype(BF16)


def attention_backward(
    qkv_ref, go_ref, o_ref, e_ref, rl_ref, gqkv_ref, rows, tokens, features, head_size
):
    width = 128 // head_size * tokens
    for g in range(features // 128):
        at = slice(g * 128, (g + 1) * 128)
        spots = [slice(j * features + g * 128, j * features + (g + 1) * 128) for j in range(3)]
        q, k, v = (qkv_ref[rows, spot] for spot in spots)
        e = e_ref[rows, g * width : (g + 1) * width]
        grads = attention_backward_group(
            q, k, v, e, go_ref[rows, at], o_ref[rows, at], rl_ref[rows, at], head_size
        )
        for spot, grad in zip(spots, grads):
            gqkv_ref[rows, spot] = grad


def feed_forward(c_ref, up_ref, bup_ref, u_ref, slope_ref, tile, ut_ref=None):
    for t in range(up_ref.shape[1] // tile):
        at = slice(t * tile, (t + 1) * tile)
        f = mm(c_ref[...], up_ref[:, at]) + bup_ref[at].reshape(1, tile)
        u, slope = gelu_both(f)
        u = u.astype(BF16)
        u_ref[:, at] = u
        slope_ref[:, at] = slope.astype(BF16)
        if ut_ref is not None:
            ut_ref[at, :] = jnp.transpose(u)


def feed_forward_back(gm_ref, down_ref, slope_ref, gf_ref, gbup_ref, tile):
    for t in range(down_ref.shape[0] // tile):
        at = slice(t * tile, (t + 1) * tile)
        gu = mm_nt(gm_ref[...], down_ref[at, :])
        gf = (gu * slope_ref[:, at].astype(F32)).astype(BF16)
        gf_ref[:, at] = gf
        gbup_ref[:, at] += rows_sum(gf.astype(F32))


def row(ref):
    return ref[...].reshape(1, -1)


def segment_mask(seg_ref, section):
    seg = seg_ref[pl.ds(section, 1), :].astype(F32)
    rows = seg.shape[1]
    column = jnp.transpose(jnp.broadcast_to(seg, (128, rows)))
    return jnp.concatenate([column] * (rows // 128), axis=1) == seg


class Writer:
    def __init__(self, semaphores):
        self.semaphores, self.copies = semaphores, []

    def start(self, source, target):
        copy = pltpu.make_async_copy(source, target, self.semaphores.at[len(self.copies)])
        copy.start()
        self.copies.append(copy)

    def wait(self):
        for copy in self.copies:
            copy.wait()


def encoder_forward_kernel(
    x_ref, seg_ref,
    gain1, bias1, w_qkv, w_out, b_out, gain2, bias2, w_up, b_up, w_down, b_down,
    *refs,
):
    outs, scratch = refs[:12], refs[12:24]
    y_ref, at_ref, qkv_ref, e_ref, rl_ref, o_ref, ot_ref, n2_ref, s2_ref, ct_ref, ut_ref, slope_ref = scratch
    h_ref, c_ref, u_ref, qkv_v, out_v, up_v, down_v, sem, out_sem = refs[24:]
    target = {id(v): o for v, o in zip(scratch, outs)}
    writer = Writer(out_sem)

    def write(*done):
        for v in done:
            writer.start(v, target[id(v)])

    tokens, features = y_ref.shape
    pairs = ((w_qkv, qkv_v), (w_out, out_v), (w_up, up_v), (w_down, down_v))
    loads = [pltpu.make_async_copy(w, v, sem.at[i]) for i, (w, v) in enumerate(pairs)]
    for load in loads:
        load.start()
    section = lax.axis_index("section")
    x = x_ref[pl.ds(pl.multiple_of(section * tokens, tokens), tokens), :].astype(F32)
    n1, _ = normalise(x)
    a = (n1 * row(gain1) + row(bias1)).astype(BF16)
    at_ref[...] = jnp.transpose(a)
    allowed = segment_mask(seg_ref, section)
    loads[0].wait()
    qkv_ref[...] = mm(a, qkv_v[...]).astype(BF16)
    write(at_ref, qkv_ref)
    attention_forward(
        qkv_ref, o_ref, e_ref, rl_ref, slice(None), tokens, features, features // H_ENC, allowed
    )
    ot_ref[...] = jnp.transpose(o_ref[...])
    write(e_ref, rl_ref, o_ref, ot_ref)
    loads[1].wait()
    h_ref[...] = x + (mm(o_ref[...], out_v[...]) + row(b_out))
    n2, s2 = normalise(h_ref[...])
    n2_ref[...] = n2
    s2_ref[...] = s2
    c_ref[...] = (n2 * row(gain2) + row(bias2)).astype(BF16)
    ct_ref[...] = jnp.transpose(c_ref[...])
    write(n2_ref, s2_ref, ct_ref)
    loads[2].wait()
    feed_forward(c_ref, up_v, b_up, u_ref, slope_ref, 512, ut_ref)
    write(ut_ref, slope_ref)
    loads[3].wait()
    y_ref[...] = (h_ref[...] + (mm(u_ref[...], down_v[...]) + row(b_down))).astype(BF16)
    write(y_ref)
    writer.wait()


def encoder_backward_kernel(
    x_ref, gy_ref, qkv_ref, e_ref, rl_ref, o_ref, n2_ref, s2_ref, slope_ref,
    gain1, w_qkv, w_out, gain2, w_up, w_down,
    gx_ref, gf_ref, ga_ref, gqkv_ref, small_ref, gbup_ref,
    gh_ref, go_ref,
):
    tokens, features = gy_ref.shape
    section = lax.axis_index("section")
    x = x_ref[pl.ds(pl.multiple_of(section * tokens, tokens), tokens), :].astype(F32)
    gbup_ref[...] = jnp.zeros_like(gbup_ref)
    feed_forward_back(gy_ref, w_down, slope_ref, gf_ref, gbup_ref, 512)
    gc = mm_nt(gf_ref[...], w_up[...])
    g = gy_ref[...].astype(F32)
    n2 = n2_ref[...]
    gh = g + normalise_back(gc, n2, s2_ref[...], row(gain2))
    gh_ref[...] = gh
    ga_ref[...] = gh.astype(BF16)
    small_ref[2:3, :] = rows_sum(gh)
    small_ref[3:4, :] = rows_sum(gc * n2)
    small_ref[4:5, :] = rows_sum(gc)
    small_ref[5:6, :] = rows_sum(g)
    go_ref[...] = mm_nt(ga_ref[...], w_out[...]).astype(BF16)
    attention_backward(
        qkv_ref, go_ref, o_ref, e_ref, rl_ref, gqkv_ref, slice(None), tokens, features,
        features // H_ENC,
    )
    gn = mm_nt(gqkv_ref[...], w_qkv[...])
    n1, s1 = normalise(x)
    small_ref[0:1, :] = rows_sum(gn * n1)
    small_ref[1:2, :] = rows_sum(gn)
    gx_ref[...] = (gh_ref[...] + normalise_back(gn, n1, s1, row(gain1))).astype(BF16)


def split_low(x):
    high = x.astype(BF16)
    return high, (x - high.astype(F32)).astype(BF16)


def slot_rows(order, seg, sample):
    start = jnp.sum(jnp.where(seg < sample, 1.0, 0.0), axis=1, keepdims=True)
    count = jnp.sum(jnp.where(seg == sample, 1.0, 0.0), axis=1, keepdims=True)
    wide = jnp.broadcast_to(order, (PATCHES, PATCHES))
    lane = lax.broadcasted_iota(jnp.int32, (PATCHES, PATCHES), 1).astype(F32)
    line = lax.broadcasted_iota(jnp.int32, (PATCHES, PATCHES), 0).astype(F32)
    across = jnp.sum(jnp.where(jnp.transpose(wide) == lane, line, 0.0), axis=0, keepdims=True)
    down = jnp.sum(jnp.where(wide == line, lane, 0.0), axis=1, keepdims=True)
    return [jnp.where(rank < count, start + rank, -1.0) for rank in (across, down)]


def decoder_kernel(
    y_ref, seg_ref, order_ref, pos_ref, g_hbm,
    w_embed_hbm, b_embed, mask_token,
    gain1, bias1, w_qkv_hbm, w_out_hbm, b_out, gain2, bias2, w_up_hbm, b_up, w_down_hbm, b_down,
    *refs,
):
    hbm, (geb_ref, gy_ref, small_ref, gbup_ref) = refs[:9], refs[9:13]
    buffers = refs[13:22]
    out_ref, at_ref, ot_ref, ct_ref, gt_ref, u_ref, slope_ref, ga_ref, qkv_ref = buffers
    (
        e2_ref, z_ref, s1_ref, e_ref, rl_ref, h_ref, s2_ref, go_ref, ge_ref, o_ref, c_ref,
        g2_ref, w_embed, w_qkv, w_out, w_up, w_down, g_sem, w_sem, out_sem,
    ) = refs[22:]
    step = pl.program_id(0)
    packed = y_ref.shape[0]
    rows, features = z_ref.shape
    samples = rows // PATCHES
    head_size = features // H_DEC
    steps = g_hbm.shape[0] // (2 * rows)
    section = lax.axis_index("section")
    mine = pl.ds(pl.multiple_of(step * rows, rows), rows)

    def fetch(i):
        at = pl.ds(pl.multiple_of((section * steps + i) * rows, rows), rows)
        slot = lax.rem(i, 2)
        return pltpu.make_async_copy(g_hbm.at[at, :], g2_ref.at[slot], g_sem.at[slot])

    weights = [
        pltpu.make_async_copy(source, target, w_sem.at[i])
        for i, (source, target) in enumerate(
            (
                (w_embed_hbm, w_embed),
                (w_qkv_hbm, w_qkv),
                (w_out_hbm, w_out),
                (w_up_hbm, w_up),
                (w_down_hbm, w_down),
            )
        )
    ]

    def write_copy(i):
        target = hbm[i].at[:, mine] if 1 <= i <= 4 else hbm[i].at[mine, :]
        return pltpu.make_async_copy(buffers[i], target, out_sem.at[i])

    def free(*which):
        @pl.when(step > 0)
        def _():
            for i in which:
                write_copy(i).wait()

    def write(*which):
        for i in which:
            write_copy(i).start()

    def loaded(i):
        @pl.when(step == 0)
        def _():
            weights[i].wait()

    @pl.when(step == 0)
    def _():
        for weight in weights:
            weight.start()
        fetch(0).start()
        small_ref[...] = jnp.zeros_like(small_ref)
        gbup_ref[...] = jnp.zeros_like(gbup_ref)
        ge_ref[...] = jnp.zeros_like(ge_ref)
        weights[0].wait()
        high, low = split_low(mm(y_ref[...], w_embed[...]) + row(b_embed))
        e2_ref[:packed, :] = high
        e2_ref[packed:, :] = low

    @pl.when(step + 1 < steps)
    def _():
        fetch(step + 1).start()

    seg = seg_ref[pl.ds(section, 1), :].astype(F32)
    hots, places, empties = [], [], []
    for j in range(samples):
        sample = step * samples + j
        order = order_ref[pl.ds(section * SAMP_MB + sample, 1), :].astype(F32)
        across, down = slot_rows(order, seg, sample.astype(F32))
        column = lax.broadcasted_iota(jnp.int32, (PATCHES, packed), 1).astype(F32)
        line = lax.broadcasted_iota(jnp.int32, (packed, PATCHES), 0).astype(F32)
        hots.append(jnp.where(column == down, 1.0, 0.0).astype(BF16))
        places.append(jnp.where(line == across, 1.0, 0.0).astype(BF16))
        empties.append(jnp.where(down < 0.0, 1.0, 0.0))
    one_hot = jnp.concatenate(hots, axis=0)
    empty = jnp.concatenate(empties, axis=0)
    twice = jnp.concatenate([one_hot, one_hot], axis=1)
    z = mm(twice, e2_ref[...]) + empty * row(mask_token)
    z = z + jnp.concatenate([pos_ref[...]] * samples, axis=0)
    n1, s1 = normalise(z)
    z_ref[...] = z
    s1_ref[...] = s1
    a = (n1 * row(gain1) + row(bias1)).astype(BF16)
    free(1, 8)
    at_ref[...] = jnp.transpose(a)
    write(1)
    loaded(1)
    qkv_ref[...] = mm(a, w_qkv[...]).astype(BF16)

    def forward(b, carry):
        at = pl.ds(pl.multiple_of(b * PATCHES, PATCHES), PATCHES)
        attention_forward(qkv_ref, o_ref, e_ref, rl_ref, at, PATCHES, features, head_size, None)
        return carry

    lax.fori_loop(0, samples, forward, 0, unroll=2)
    free(2, 3, 5, 6)
    loaded(2)
    ot_ref[...] = jnp.transpose(o_ref[...])
    h_ref[...] = z_ref[...] + (mm(o_ref[...], w_out[...]) + row(b_out))
    n2, s2 = normalise(h_ref[...])
    s2_ref[...] = s2
    c_ref[...] = (n2 * row(gain2) + row(bias2)).astype(BF16)
    ct_ref[...] = jnp.transpose(c_ref[...])
    write(2, 3)
    loaded(3)
    feed_forward(c_ref, w_up, b_up, u_ref, slope_ref, 512)
    write(5)
    free(0, 4, 7)
    loaded(4)
    out_ref[...] = (h_ref[...] + (mm(u_ref[...], w_down[...]) + row(b_down))).astype(BF16)
    write(0)

    fetch(step).wait()
    g_ref = g2_ref.at[lax.rem(step, 2)]
    gt_ref[...] = jnp.transpose(g_ref[...])
    feed_forward_back(g_ref, w_down, slope_ref, slope_ref, gbup_ref, 512)
    write(4, 6)
    gc = mm_nt(slope_ref[...], w_up[...])
    g = g_ref[...].astype(F32)
    h = h_ref[...]
    n2 = (h - jnp.mean(h, axis=-1, keepdims=True)) * s2_ref[...]
    gh = g + normalise_back(gc, n2, s2_ref[...], row(gain2))
    small_ref[2:3, :] += rows_sum(gh)
    small_ref[3:4, :] += rows_sum(gc * n2)
    small_ref[4:5, :] += rows_sum(gc)
    small_ref[5:6, :] += rows_sum(g)
    h_ref[...] = gh
    ga_ref[...] = gh.astype(BF16)
    write(7)
    go_ref[...] = mm_nt(ga_ref[...], w_out[...]).astype(BF16)

    def backward(b, carry):
        at = pl.ds(pl.multiple_of(b * PATCHES, PATCHES), PATCHES)
        attention_backward(
            qkv_ref, go_ref, o_ref, e_ref, rl_ref, qkv_ref, at, PATCHES, features, head_size
        )
        return carry

    lax.fori_loop(0, samples, backward, 0, unroll=2)
    write(8)
    gn = mm_nt(qkv_ref[...], w_qkv[...])
    z = z_ref[...]
    n1 = (z - jnp.mean(z, axis=-1, keepdims=True)) * s1_ref[...]
    gz = h_ref[...] + normalise_back(gn, n1, s1_ref[...], row(gain1))
    small_ref[0:1, :] += rows_sum(gn * n1)
    small_ref[1:2, :] += rows_sum(gn)
    small_ref[6:7, :] += rows_sum(gz * empty)
    ge_ref[...] += mm(jnp.concatenate(places, axis=1), gz.astype(BF16))

    @pl.when(step == steps - 1)
    def _():
        ge = ge_ref[...]
        small_ref[7:8, :] = rows_sum(ge)
        geb_ref[...] = ge.astype(BF16)
        gy_ref[...] = mm_nt(geb_ref[...], w_embed[...]).astype(BF16)
        for i in range(9):
            write_copy(i).wait()


def in_vmem(count):
    return [pl.BlockSpec(memory_space=pltpu.VMEM)] * count


def in_hbm():
    return pl.BlockSpec(memory_space=pl.ANY)


def shape(rows, columns, dtype=BF16):
    return jax.ShapeDtypeStruct((rows, columns), dtype)


KERNEL_VMEM = 60 * 2**20


def encoder_forward(x, segments, params):
    rows, d = x.shape[0] // 2, x.shape[1]
    ff = params[7].shape[1]
    outs = [
        (rows, d, BF16),
        (d, rows, BF16),
        (rows, 3 * d, BF16),
        (rows, H_ENC * rows, BF16),
        (rows, d, F32),
        (rows, d, BF16),
        (d, rows, BF16),
        (rows, d, F32),
        (rows, 1, F32),
        (d, rows, BF16),
        (ff, rows, BF16),
        (rows, ff, BF16),
    ]
    more = [(rows, d, F32), (rows, d, BF16), (rows, ff, BF16)]
    args = [x, segments, *params]
    matrices = [w for w in params if w.dtype == BF16]
    return pl.pallas_call(
        encoder_forward_kernel,
        out_shape=[shape(*o) for o in outs],
        in_specs=in_vmem(2) + [in_hbm() if w.dtype == BF16 else in_vmem(1)[0] for w in params],
        out_specs=[in_hbm()] * len(outs),
        scratch_shapes=[pltpu.VMEM((r, w), t) for r, w, t in outs + more]
        + [pltpu.VMEM(w.shape, BF16) for w in matrices]
        + [pltpu.SemaphoreType.DMA((len(matrices),)), pltpu.SemaphoreType.DMA((len(outs),))],
        compiler_params=pltpu.CompilerParams(vmem_limit_bytes=KERNEL_VMEM),
        name="encoder_forward",
    )(*args)


def encoder_backward(x, gy, saved, params):
    gain1, _, w_qkv, w_out, _, gain2, _, w_up, _, w_down, _ = params
    rows, d = gy.shape
    ff = w_up.shape[1]
    outs = [
        shape(rows, d),
        shape(rows, ff),
        shape(rows, d),
        shape(rows, 3 * d),
        shape(8, d, F32),
        shape(1, ff, F32),
    ]
    args = [x, gy, *saved, gain1, w_qkv, w_out, gain2, w_up, w_down]
    return pl.pallas_call(
        encoder_backward_kernel,
        out_shape=outs,
        in_specs=in_vmem(len(args)),
        out_specs=in_vmem(len(outs)),
        scratch_shapes=[pltpu.VMEM((rows, d), F32), pltpu.VMEM((rows, d), BF16)],
        compiler_params=pltpu.CompilerParams(vmem_limit_bytes=KERNEL_VMEM),
        name="encoder_backward",
    )(*args)


def decoder_both(y, segments, orders, g, embed_params, params):
    packed, d_enc = y.shape
    total, d = g.shape[0] // 2, g.shape[1]
    samples = 6
    rows = samples * PATCHES
    steps = total // rows
    ff = params[7].shape[1]
    args = [y, segments, orders, positions(PATCHES, d), g, *embed_params, *params]

    def whole(x):
        return pl.BlockSpec(x.shape, lambda i: (0,) * len(x.shape), pipeline_mode=pl.Buffered(1))

    in_specs = [whole(x) for x in args[:4]] + [in_hbm()]
    in_specs += [in_hbm() if x.dtype == BF16 else whole(x) for x in args[5:]]
    wide = [ff, ff, d, 3 * d]
    outs = [shape(total, d)] + [shape(d, total)] * 4 + [shape(total, w) for w in wide]
    buffers = [(rows, d, BF16)] + [(d, rows, BF16)] * 4 + [(rows, w, BF16) for w in wide]
    last = [shape(packed, d), shape(packed, d_enc), shape(8, d, F32), shape(1, ff, F32)]
    out_specs = [in_hbm()] * len(outs) + [pl.BlockSpec(x.shape, lambda i: (0, 0)) for x in last]
    scratch = [
        (2 * packed, d, BF16),
        (rows, d, F32),
        (rows, 1, F32),
        (rows, H_DEC * PATCHES, BF16),
        (rows, d, F32),
        (rows, d, F32),
        (rows, 1, F32),
        (rows, d, BF16),
        (packed, d, F32),
        (rows, d, BF16),
        (rows, d, BF16),
    ]
    matrices = [x for x in args[5:] if x.dtype == BF16]
    return pl.pallas_call(
        decoder_kernel,
        out_shape=outs + last,
        grid=(steps,),
        in_specs=in_specs,
        out_specs=out_specs,
        scratch_shapes=[pltpu.VMEM((r, w), t) for r, w, t in buffers + scratch]
        + [pltpu.VMEM((2, rows, d), BF16)]
        + [pltpu.VMEM(x.shape, BF16) for x in matrices]
        + [pltpu.SemaphoreType.DMA((k,)) for k in (2, len(matrices), len(outs))],
        compiler_params=pltpu.CompilerParams(
            vmem_limit_bytes=KERNEL_VMEM, dimension_semantics=("arbitrary",)
        ),
        name="decoder_both",
    )(*args)


MESH = pl.DeviceIdType.MESH
ENC_QKV, ENC_OUT, ENC_UP, ENC_DOWN, EMBED, DEC_QKV, DEC_OUT, DEC_UP, DEC_DOWN = range(9)
GIVE, PAIR, FFN, LN2, GO, ATT, GN, LAST = range(10, 18)
SMALL = -1
ROW_BUP, ROW_DEC_BUP, ROW_DEC, SMALL_ROWS = 6, 10, 16, 24
Z, Y, X, CORE = range(4)
ORDERS = ((X, Y, Z), (Y, X, Z), (X, Z, Y), (Y, Z, X))


class Chunk:
    def __init__(self, name, half, offset, rows, width, first_row=None):
        self.name, self.half, self.offset, self.rows, self.width = name, half, offset, rows, width
        self.first_row, self.turned, self.order = first_row, name == DEC_DOWN, None
        self.decoder = name in (DEC_QKV, DEC_UP, DEC_OUT)

    def columns(self, side):
        return pl.ds(pl.multiple_of(side * self.half + self.offset, 128), self.width)

    def place(self, side):
        if self.turned:
            return (pl.ds(pl.multiple_of(side * self.half + self.offset, 128), self.rows), slice(None))
        if self.first_row is None:
            return (slice(None), self.columns(side))
        return (pl.ds(self.first_row, self.rows), self.columns(side))

    @property
    def bytes(self):
        return 32 * self.rows * self.width

    def loads(self, order):
        first, second, third = order
        if second == Z:
            return (self.bytes, self.bytes, self.bytes / 8)
        return (self.bytes, self.bytes / 2, self.bytes / 2)


def make_chunks():
    chunks = [Chunk(DEC_OUT, 256, 0, 32, 256)]
    chunks += [Chunk(DEC_QKV, 768, o, 32, 256) for o in (0, 256, 512)]
    chunks += [Chunk(ENC_DOWN, 384, 0, 48, 384, 48 * q) for q in range(4)]
    chunks += [Chunk(ENC_UP, 1536, o, 48, 384) for o in (0, 384, 768, 1152)]
    chunks += [Chunk(ENC_OUT, 384, 0, 48, 384)]
    chunks += [Chunk(ENC_QKV, 1152, o, 48, 384) for o in (0, 384, 768)]
    chunks += [Chunk(DEC_UP, 1024, o, 32, 256) for o in (0, 256, 512, 768)]
    chunks += [Chunk(DEC_DOWN, 256, o, 128, 128) for o in (0, 128)]
    chunks += [Chunk(EMBED, 256, 0, 48, 256)]
    load = [0.0, 0.0, 0.0]
    for chunk in chunks:

        def after(order):
            new = list(load)
            for axis, size in zip(order, chunk.loads(order)):
                new[axis] += size
            return new

        chunk.order = min(ORDERS, key=lambda order: (max(after(order)), sum(after(order))))
        load = after(chunk.order)
    return chunks


TOGETHER = {ENC_UP: 2, ENC_QKV: 3, DEC_QKV: 3, DEC_UP: 2, DEC_DOWN: 2}


def make_groups(chunks):
    groups = []
    for c, k in enumerate(chunks):
        if groups and chunks[groups[-1][0]].name == k.name and len(groups[-1]) < TOGETHER.get(k.name, 1):
            groups[-1].append(c)
        else:
            groups.append([c])
    return groups


def product_cost(k, count):
    return count * (1.1 if k.decoder else 3.0 if k.turned else 0.7)


def tasks_in_order(chunks, groups):
    def gives(name):
        found = [(g, chunks[m[0]], len(m)) for g, m in enumerate(groups)]
        kind = PAIR if name == DEC_DOWN else GIVE
        return [(kind, g, product_cost(k, size)) for g, k, size in found if k.name == name]

    tasks = gives(DEC_OUT) + gives(DEC_QKV)
    tasks += [(FFN, t, 2.5) for t in range(4)]
    tasks += gives(ENC_DOWN) + gives(ENC_UP)
    tasks += [(LN2, 0, 1.5), (GO, 0, 1.2)]
    tasks += [(ATT, g, 2.2) for g in range(6)]
    tasks += gives(ENC_OUT) + gives(ENC_QKV)
    tasks += [(GN, j, 1.2) for j in range(3)] + [(LAST, 0, 2.0)]
    return tasks + gives(DEC_UP) + gives(DEC_DOWN) + gives(EMBED)


def decoder_arrays(chunks):
    names = []
    for k in chunks:
        if (k.decoder or k.turned) and k.name not in names:
            names.append(k.name)
    return names


def make_plan(chunks, groups):
    tasks = tasks_in_order(chunks, groups)
    lhs = decoder_arrays(chunks)
    free = [0.0] * 4
    rate = [88e3, 88e3, 88e3, 500e3]
    pending, plan, now, owned = [], [], 2.0, set()

    def send(link, size, latency):
        begin = max(now, free[link])
        free[link] = begin + size / rate[link]
        return free[link] + latency

    def blocked(task):
        if task[0] not in (GIVE, PAIR):
            return False
        name = chunks[groups[task[1]][0]].name
        if name not in lhs[2:]:
            return False
        name = lhs[lhs.index(name) - 2]
        return any(chunks[m[0]].name == name and g not in owned for g, m in enumerate(groups))

    while tasks or pending:
        pending.sort()
        if pending and (pending[0][0] <= now or not tasks or blocked(tasks[0])):
            arrive, stage, c = pending.pop(0)
            now = max(now, arrive)
            plan.append((stage, c))
            if c == SMALL:
                now += 0.1
                if stage < 4:
                    pending.append((now + 2.0, stage + 1, c))
                continue
            members = groups[c] if stage == 1 else [c]
            k = chunks[members[0]]
            if stage == 1:
                owned.add(c)
                now += 0.6 if k.turned else product_cost(k, len(members)) + 0.2 * len(members)
            else:
                now += 0.25
            for c in members:
                k = chunks[c]
                if stage < 4:
                    axis = k.order[stage - 1]
                    latency = 2.0 if axis == Z else 1.5
                    arrive = send(axis, k.loads(k.order)[stage - 1], latency)
                    pending.append((arrive, stage + 1, c))
                elif stage == 4:
                    pending.append((send(CORE, k.bytes / 16, 1.0), 5, c))
            continue
        name, arg, cost = tasks.pop(0)
        plan.append((name, arg))
        now += cost
        if name in (GIVE, PAIR):
            arrive = [send(CORE, chunks[c].bytes, 1.0) for c in groups[arg]]
            pending.append((max(arrive), 1, arg))
        elif name == LAST:
            pending.append((now + 2.0, 1, SMALL))
    return plan


class Ring:
    def __init__(self, sources, slots, semaphores, depth):
        self.copies = [
            pltpu.make_async_copy(source, slot, semaphores())
            for source, slot in zip(sources, slots)
        ]
        self.slots, self.depth, self.at = slots, depth, 0

    def begin(self):
        for copy in self.copies[: self.depth]:
            copy.start()

    def take(self):
        self.copies[self.at].wait()
        return self.slots[self.at]

    def done(self):
        ahead = self.at + self.depth
        if ahead < len(self.copies):
            self.copies[ahead].start()
        self.at += 1


class Names:
    def __init__(self, names, refs):
        self.__dict__.update(zip(names, refs))


LOADS = 96


def finish_kernel(chunks, groups, plan, r):
    n = len(chunks)
    s = lax.axis_index("section")
    d = lax.axis_index("dp")
    here = (d // 4, (d // 2) % 2, d % 2)
    z, y, x = here
    sibling = {"section": 1 - s}
    z_at = [lax.rem(z + k, 4) for k in (1, 2, 3)]
    peers = {
        X: [(1 - x, {"dp": d + 1 - 2 * x})],
        Y: [(1 - y, {"dp": d + 2 - 4 * y})],
        Z: [(p, {"dp": d + 4 * (p - z)}) for p in z_at],
    }
    every = [sibling] + [peer for axis in (X, Y, Z) for _, peer in peers[axis]]

    barrier = pltpu.get_barrier_semaphore()
    for peer in every:
        pl.semaphore_signal(barrier, inc=1, device_id=peer, device_id_type=MESH)

    counter = iter(range(LOADS))

    def semaphore():
        return r.load_sem.at[next(counter)]

    def remote(src, dst, send, recv, peer):
        return pltpu.make_async_remote_copy(
            src_ref=src, dst_ref=dst, send_sem=send, recv_sem=recv, device_id=peer, device_id_type=MESH
        )

    rhs_of = {DEC_QKV: r.gqkv2, DEC_UP: r.gf2, DEC_OUT: r.ga2}
    lhs_of = {DEC_QKV: r.at2, DEC_UP: r.ct2, DEC_OUT: r.ot2, DEC_DOWN: r.gt2}
    tiles, widths, last_use = [], [], {}

    def wide_columns(g, side):
        k, width = chunks[groups[g][0]], sum(chunks[c].width for c in groups[g])
        return pl.ds(pl.multiple_of(side * k.half + k.offset, 128), width)

    for i, (name, arg) in enumerate(plan):
        if name == PAIR:
            tiles += [r.u2.at[:, t * 512 : (t + 1) * 512] for t in range(4)]
            last_use[DEC_DOWN] = i
        elif name in (GIVE, 1) and arg != SMALL and chunks[groups[arg][0]].decoder:
            k = chunks[groups[arg][0]]
            tiles.append(rhs_of[k.name].at[:, wide_columns(arg, 1 - s if name == GIVE else s)])
            last_use[k.name] = i
    lhs_names = decoder_arrays(chunks)
    assert sorted(lhs_names, key=last_use.get) == lhs_names
    rhs_slots = [r.rhs.at[i % 2, :, : tile.shape[1]] for i, tile in enumerate(tiles)]
    rhs = Ring(tiles, rhs_slots, semaphore, 2)
    lhs = Ring([lhs_of[k] for k in lhs_names], [r.lhs.at[i % 2] for i in range(4)], semaphore, 2)
    lhs.copies[0].start()
    rhs.begin()
    lhs.copies[1].start()
    tokens, d_enc = r.gy.shape
    blocks = []
    for t in range(4):
        at = pl.ds(t * d_enc, d_enc)
        blocks += [r.w_down.at[at, :], r.w_up.at[:, at]]
    blocks.append(r.w_out)
    blocks += [r.w_qkv.at[:, pl.ds(j * d_enc, d_enc)] for j in range(3)]
    weights = Ring(blocks, [r.w.at[i % 4] for i in range(12)], semaphore, 4)
    e_width = 2 * tokens
    e_ring = Ring(
        [r.e.at[:, pl.ds(g * e_width, e_width)] for g in range(6)],
        [r.e_v.at[g % 2] for g in range(6)],
        semaphore,
        2,
    )

    def load(source, target):
        return pltpu.make_async_copy(source, target, semaphore())

    mine = pl.ds(pl.multiple_of(s * tokens, tokens), tokens)
    load_gy, load_slope, load_ut = load(r.gy, r.gy_v), load(r.slope, r.slope_v), load(r.ut, r.ut_v)
    load_ct, load_at, load_ot = load(r.ct, r.ct_v), load(r.at, r.at_v), load(r.ot, r.ot_v)
    load_n2, load_s2, load_qkv = load(r.n2, r.n2_v), load(r.s2, r.s2_v), load(r.qkv, r.qkv_v)
    load_o, load_rl, load_x = load(r.o, r.o_v), load(r.rl, r.rl_v), load(r.x.at[mine, :], r.x_v)
    load_y, load_geb = load(r.y, r.y_v), load(r.geb, r.geb_v)
    begun = [
        (load_gy, load_slope, weights),
        (load_ut, load_ct, load_n2, load_s2),
        (load_qkv, load_o, load_rl, e_ring),
        (load_ot, load_at, load_x, load_y, load_geb),
    ]

    def begin_some():
        for copy in begun.pop(0) if begun else ():
            copy.begin() if isinstance(copy, Ring) else copy.start()

    half = r.decoded.shape[1] // 2
    give_half = r.decoded.at[:, pl.ds(pl.multiple_of((1 - s) * half, half), half), :]
    decoded_away = remote(give_half, r.decoded_got, r.swap_sem.at[0], r.swap_sem.at[1], sibling)
    gx_columns = d_enc // 2
    gx_half = r.gx.at[:, pl.ds(pl.multiple_of((1 - s) * gx_columns, 128), gx_columns)]
    gx_away = remote(gx_half, r.gx_got, r.swap_sem.at[2], r.swap_sem.at[3], sibling)

    small = r.small
    small[...] = jnp.zeros_like(small)
    small[ROW_DEC : ROW_DEC + 8, : r.small2.shape[1]] = r.small2[...]
    quarter = r.gbup2.shape[1] // 4
    for i in range(4):
        piece = r.gbup2[:, i * quarter : (i + 1) * quarter]
        small[ROW_DEC_BUP + i : ROW_DEC_BUP + i + 1, :quarter] = piece

    pl.semaphore_wait(barrier, len(every))

    copies = {}
    first_slot = (0, 1, 2, 5, 8)

    def chunk_copy(c, slot, src, dst, peer):
        copy = remote(src, dst, r.send_sem.at[c, slot], r.recv_sem.at[c, slot], peer)
        copy.start()
        copies[c, slot] = copy

    sent = set()

    def sent_by(c, slot):
        if (c, slot) not in sent:
            sent.add((c, slot))
            copies[c, slot].wait_send()

    staged = {}

    def staging(c):
        k = chunks[c]
        buffers = r.stage[k.rows, k.width]
        turn = staged.setdefault((k.rows, k.width), [])
        if len(turn) >= len(buffers):
            sent_by(turn[-len(buffers)], 0)
        turn.append(c)
        return buffers[(len(turn) - 1) % len(buffers)]

    def shard(i):
        return (i // 4, (i // 2) % 2, i % 2)

    waited = set()

    def arrived(copy):
        if id(copy) not in waited:
            waited.add(id(copy))
            copy.wait()

    def product(g, side):
        k, columns = chunks[groups[g][0]], wide_columns(g, side)
        if k.decoder:
            return mm(lhs.slots[lhs_names.index(k.name)][...], rhs.take()[...])
        if k.name == EMBED:
            arrived(load_y)
            arrived(load_geb)
            return mm_tn(r.y_v[...], r.geb_v[:, columns])
        if k.name == ENC_DOWN:
            arrived(load_ut)
            at = [i * 192 + k.first_row for i in range(16)]
            left = jnp.concatenate([r.ut_v[i : i + k.rows, :] for i in at], axis=0)
            return mm(left, r.gy_v[:, columns])
        if k.name == ENC_UP:
            arrived(load_ct)
            return mm(r.ct_v[...], r.slope_v[:, columns])
        if k.name == ENC_OUT:
            arrived(load_ot)
            return mm(r.ot_v[...], r.ga_v[:, columns])
        arrived(load_at)
        return mm(r.at_v[...], r.qkv_v[:, columns])

    def after_product(i, g):
        k = chunks[groups[g][0]]
        if k.decoder:
            rhs.done()
            if last_use[k.name] == i:
                lhs.done()

    def wait_lhs(k):
        if k.name in lhs_names:
            arrived(lhs.copies[lhs_names.index(k.name)])

    def give(i, g):
        members = groups[g]
        wait_lhs(chunks[members[0]])
        buffers = [staging(c) for c in members]
        value = product(g, 1 - s).astype(BF16)
        for m, (c, buffer) in enumerate(zip(members, buffers)):
            k = chunks[c]
            part = value[:, m * k.width : (m + 1) * k.width]
            for j in range(16):
                buffer[shard(j)] = part[j * k.rows : (j + 1) * k.rows]
            chunk_copy(c, 0, buffer, r.acc[c], sibling)
        after_product(i, g)
        begin_some()

    def pair(i, g):
        both = groups[g]
        wait_lhs(chunks[both[0]])
        left = lhs.slots[lhs_names.index(DEC_DOWN)]
        side_rows = chunks[both[0]].half
        buffers = [staging(c) for c in both]
        for t in range(4):
            tile = rhs.take()
            for side, targets in ((1 - s, buffers), (s, [r.acc[c] for c in both])):
                at = pl.ds(pl.multiple_of(side * side_rows, side_rows), side_rows)
                value = mm(left[at, :], tile[...]).astype(BF16)
                for c, target in zip(both, targets):
                    k = chunks[c]
                    rows = slice(k.offset, k.offset + k.rows)
                    for j in range(4):
                        target[shard(4 * t + j)] = value[rows, j * k.width : (j + 1) * k.width]
            rhs.done()
        lhs.done()
        for c, buffer in zip(both, buffers):
            chunk_copy(c, 0, buffer, r.got[c], sibling)

    def spots(k, stage):
        fixed = {axis: here[axis] for axis in k.order[: stage - 1]}
        return [fixed.get(axis, slice(None)) for axis in (Z, Y, X)]

    def send_stage(c, stage):
        k = chunks[c]
        axis = k.order[stage - 1]
        for j, (coordinate, peer) in enumerate(peers[axis]):
            at = spots(k, stage)
            at[axis] = coordinate
            src = r.acc[c].at[tuple(at)]
            chunk_copy(c, first_slot[stage] + j, src, r.recv[stage - 1][c].at[j], peer)

    def got_stage(c, stage):
        k = chunks[c]
        count = len(peers[k.order[stage - 1]])
        for j in range(count):
            copies[c, first_slot[stage] + j].wait_recv()
        return count

    def add_stage(c, stage):
        k, acc, got = chunks[c], r.acc[c], r.recv[stage - 1][c]
        count = got_stage(c, stage)
        left = [axis for axis in (Z, Y, X) if axis not in k.order[:stage]]
        sizes = [(4, 2, 2)[axis] for axis in left]
        for j in range(math.prod(sizes)):
            place, rest = {}, j
            for axis, size in reversed(list(zip(left, sizes))):
                place[axis] = rest % size
                rest //= size
            at = tuple(place.get(axis, here[axis]) for axis in (Z, Y, X))
            index = tuple(place[axis] for axis in left)
            if count == 1:
                acc[at] = acc[at] + got[(0,) + index]
            else:
                total = acc[at].astype(F32)
                for m in range(count):
                    total = total + got[(m,) + index].astype(F32)
                acc[at] = total.astype(BF16)

    def stage1(i, g):
        members = groups[g]
        for c in members:
            copies[c, 0].wait_recv()
        if chunks[members[0]].turned:
            for c in members:
                acc = r.acc[c]
                for j in range(16):
                    acc[shard(j)] = acc[shard(j)] + r.got[c][shard(j)]
                send_stage(c, 1)
            return
        value = product(g, s)
        for m, c in enumerate(members):
            k, acc = chunks[c], r.acc[c]
            wide = value[:, m * k.width : (m + 1) * k.width]
            for j in range(16):
                part = wide[j * k.rows : (j + 1) * k.rows]
                acc[shard(j)] = (part + acc[shard(j)].astype(F32)).astype(BF16)
            send_stage(c, 1)
        after_product(i, g)

    def stage2(i, c):
        add_stage(c, 1)
        send_stage(c, 2)

    def stage3(i, c):
        add_stage(c, 2)
        send_stage(c, 3)

    def stage4(i, c):
        k = chunks[c]
        total = r.acc[c][here].astype(F32)
        for j in range(got_stage(c, 3)):
            total = total + r.recv[2][c][j].astype(F32)
        out = r.out[k.name]
        out[k.place(s)] = total.astype(BF16)
        final = out.at[k.place(s)]
        chunk_copy(c, 8, final, final, sibling)

    def stage5(i, c):
        copies[c, 8].wait_recv()

    small_copies = []

    def small_copy(source, peer):
        slot = len(small_copies)
        copy = remote(
            source, r.small_got.at[slot], r.small_sem.at[0, slot], r.small_sem.at[1, slot], peer
        )
        copy.start()
        small_copies.append(copy)

    def small_stage(stage):
        if stage < 4:
            small_copies[stage - 1].wait()
            total = small[...] + r.small_got[stage - 1]
            if stage < 3:
                small[...] = total
                small_copy(small, peers[X if stage == 1 else Y][0][1])
            else:
                r.small_sum[...] = total
                for _, peer in peers[Z]:
                    small_copy(r.small_sum, peer)
        else:
            total = r.small_sum[...]
            for j in range(3):
                small_copies[3 + j].wait()
                total = total + r.small_got[3 + j]
            r.out_small[...] = total

    def ffn(i, t):
        if t == 0:
            load_gy.wait()
            load_slope.wait()
            begin_some()
        at = slice(t * d_enc, (t + 1) * d_enc)
        gu = mm_nt(r.gy_v[...], weights.take()[...])
        weights.done()
        gf = (gu * r.slope_v[:, at].astype(F32)).astype(BF16)
        r.slope_v[:, at] = gf
        small[ROW_BUP + t : ROW_BUP + t + 1, :] = rows_sum(gf.astype(F32))
        gc = mm_nt(gf, weights.take()[...])
        weights.done()
        r.sum_v[...] = gc if t == 0 else r.sum_v[...] + gc

    def ln2(i, _):
        load_n2.wait()
        load_s2.wait()
        g, gc, n2 = r.gy_v[...].astype(F32), r.sum_v[...], r.n2_v[...]
        gh = g + normalise_back(gc, n2, r.s2_v[...], row(r.gain2))
        begin_some()
        small[2:3, :] = rows_sum(gh)
        small[3:4, :] = rows_sum(gc * n2)
        small[4:5, :] = rows_sum(gc)
        small[5:6, :] = rows_sum(g)
        r.n2_v[...] = gh
        r.ga_v[...] = gh.astype(BF16)

    def go(i, _):
        r.go_v[...] = mm_nt(r.ga_v[...], weights.take()[...]).astype(BF16)
        weights.done()

    def att(i, g):
        if g == 0:
            for copy in (load_qkv, load_o, load_rl):
                copy.wait()
        at = slice(g * 128, (g + 1) * 128)
        parts = [slice(j * d_enc + g * 128, j * d_enc + (g + 1) * 128) for j in range(3)]
        q, k, v = (r.qkv_v[:, part] for part in parts)
        grads = attention_backward_group(
            q, k, v, e_ring.take()[...], r.go_v[:, at], r.o_v[:, at], r.rl_v[:, at],
            d_enc // H_ENC,
        )
        e_ring.done()
        for part, grad in zip(parts, grads):
            r.qkv_v[:, part] = grad

    def gn(i, j):
        part = mm_nt(r.qkv_v[:, j * d_enc : (j + 1) * d_enc], weights.take()[...])
        weights.done()
        r.sum_v[...] = part if j == 0 else r.sum_v[...] + part

    def last(i, _):
        load_x.wait()
        n1, s1 = normalise(r.x_v[...].astype(F32))
        total = r.sum_v[...]
        small[0:1, :] = rows_sum(total * n1)
        small[1:2, :] = rows_sum(total)
        small_copy(small, sibling)
        gx = r.n2_v[...] + normalise_back(total, n1, s1, row(r.gain1))
        r.gx[...] = gx.astype(BF16)
        gx_away.start()
        decoded_away.start()

    run = {
        GIVE: give, PAIR: pair, FFN: ffn, LN2: ln2, GO: go, ATT: att, GN: gn, LAST: last,
        1: stage1, 2: stage2, 3: stage3, 4: stage4, 5: stage5,
    }
    for i, (name, arg) in enumerate(plan):
        if arg == SMALL:
            small_stage(name)
        else:
            run[name](i, arg)

    for c, slot in copies:
        sent_by(c, slot)
    gx_away.wait()
    decoded_away.wait()


def finish_buffers(chunks, rows, d, ff, dec_total, dec):
    def of(dtype, *dims):
        return (dims, dtype)

    return dict(
        y_v=of(BF16, rows, d),
        geb_v=of(BF16, rows, dec),
        gy_v=of(BF16, rows, d),
        slope_v=of(BF16, rows, ff),
        n2_v=of(F32, rows, d),
        s2_v=of(F32, rows, 1),
        qkv_v=of(BF16, rows, 3 * d),
        o_v=of(BF16, rows, d),
        rl_v=of(F32, rows, d),
        x_v=of(BF16, rows, d),
        ga_v=of(BF16, rows, d),
        go_v=of(BF16, rows, d),
        sum_v=of(F32, rows, d),
        ut_v=of(BF16, ff, rows),
        ct_v=of(BF16, d, rows),
        at_v=of(BF16, d, rows),
        ot_v=of(BF16, d, rows),
        e_v=of(BF16, 2, rows, 2 * rows),
        w=of(BF16, 4, d, d),
        lhs=of(BF16, 2, dec, dec_total),
        rhs=of(BF16, 2, dec_total, 768),
        small=of(F32, SMALL_ROWS, d),
        small_sum=of(F32, SMALL_ROWS, d),
        small_got=of(F32, 6, SMALL_ROWS, d),
    )


def finish(acts):
    enc, dec = acts["enc"], acts["dec"]
    gain1, _, w_qkv, w_out, _, gain2, _, w_up, _, w_down, _ = enc["params"]
    qkv, e, rl, o, n2, s2, slope = acts["saved"]
    given = dict(
        x=acts["x"], y=acts["y"], gy=acts["gy"], geb=acts["geb"], qkv=qkv, e=e, rl=rl, o=o, n2=n2,
        s2=s2, slope=slope, at=enc["at"], ot=enc["ot"], ct=enc["ct"], ut=enc["ut"], at2=dec["at"], ot2=dec["ot"],
        ct2=dec["ct"], gt2=dec["gt"], u2=dec["u"], gf2=dec["gf"], ga2=dec["ga"],
        gqkv2=dec["gqkv"], w_qkv=w_qkv, w_out=w_out, w_up=w_up, w_down=w_down,
        decoded=acts["decoded"].reshape(SAMP_MB, PATCHES, -1),
    )
    n_hbm = len(given)
    given.update(small2=acts["small2"], gbup2=acts["gbup2"], gain1=gain1, gain2=gain2)
    rows, d = acts["gy"].shape
    ff = w_up.shape[1]
    dec_d, dec_total = dec["at"].shape
    dec_ff = dec["u"].shape[1]
    chunks = make_chunks()
    n = len(chunks)
    groups = make_groups(chunks)
    plan = make_plan(chunks, groups)

    dims = {
        ENC_QKV: (d, 3 * d), ENC_OUT: (d, d), ENC_UP: (d, ff), ENC_DOWN: (ff, d),
        EMBED: (d, dec_d), DEC_QKV: (dec_d, 3 * dec_d), DEC_OUT: (dec_d, dec_d),
        DEC_UP: (dec_d, dec_ff), DEC_DOWN: (dec_ff, dec_d),
    }
    big = [
        shape(dims[k][1], dims[k][0] // 16) if k == DEC_DOWN else shape(dims[k][0] // 16, dims[k][1])
        for k in range(9)
    ]
    outs = dict(
        out_small=shape(SMALL_ROWS, d, F32),
        decoded_got=jax.ShapeDtypeStruct((SAMP_MB, PATCHES // 2, dec_d), BF16),
        gx=shape(rows, d),
        gx_got=shape(rows, d // 2),
    )
    single = finish_buffers(chunks, rows, d, ff, dec_total, dec_d)
    left = (4, 2, 2)
    lists = [[], [], [], [], []]
    for k in chunks:
        block = (k.rows, k.width)
        lists[0].append((left + block, BF16))
        if k.turned:
            lists[1].append((left + block, BF16))
        for stage in range(3):
            rest = [left[axis] for axis in (Z, Y, X) if axis not in k.order[: stage + 1]]
            count = 3 if k.order[stage] == Z else 1
            lists[2 + stage].append(((count, *rest, *block), BF16))
    blocks = sorted({(k.rows, k.width) for k in chunks})
    slots = [3 if block in ((32, 256), (48, 384)) else 2 if block[0] == 128 else 1 for block in blocks]
    lists.append([(left + block, BF16) for block, m in zip(blocks, slots) for _ in range(m)])
    semaphores = dict(
        load_sem=(LOADS,), send_sem=(n, 9), recv_sem=(n, 9), small_sem=(2, 6), swap_sem=(4,)
    )

    def kernel(*refs):
        refs = list(refs)

        def take(count):
            taken = refs[:count]
            del refs[:count]
            return taken

        names = list(given) + list(outs)
        r = Names(names, take(len(names)))
        r.out = take(9)
        r.__dict__.update(zip(single, take(len(single))))
        r.acc = take(n)
        r.got = dict(zip([c for c, k in enumerate(chunks) if k.turned], take(len(lists[1]))))
        r.recv = [take(n) for _ in range(3)]
        r.stage = {block: take(m) for block, m in zip(blocks, slots)}
        r.__dict__.update(zip(semaphores, take(len(semaphores))))
        finish_kernel(chunks, groups, plan, r)

    flat = list(single.values()) + [b for group in lists for b in group]
    results = pl.pallas_call(
        kernel,
        out_shape=list(outs.values()) + big,
        in_specs=[in_hbm()] * n_hbm + in_vmem(len(given) - n_hbm),
        out_specs=in_vmem(len(outs) + 9),
        scratch_shapes=[pltpu.VMEM(*b) for b in flat]
        + [pltpu.SemaphoreType.DMA(v) for v in semaphores.values()],
        compiler_params=pltpu.CompilerParams(
            collective_id=1, has_side_effects=True, vmem_limit_bytes=FINISH_VMEM
        ),
        name="finish",
    )(*given.values())
    return write_outputs(results, given["decoded"], dims)


FINISH_VMEM = 62 * 2**20


def write_kernel(small, decoded_got, gx_own, gx_got, *refs):
    big, decoded_own = refs[:9], refs[9]
    decoded, gx, *totals = refs[10:]
    s = lax.axis_index("section")
    half = decoded.shape[1]
    samples, rows, columns = decoded_own.shape[0], gx_own.shape[0], gx.shape[1]
    own = decoded_own[:, pl.ds(pl.multiple_of(s * half, half), half), :]
    for side, part in ((s, own), (1 - s, decoded_got[...])):
        decoded[pl.ds(side * samples, samples)] = part
    own = gx_own[:, pl.ds(pl.multiple_of(s * columns, 128), columns)]
    for side, part in ((s, own), (1 - s, gx_got[...])):
        gx[pl.ds(pl.multiple_of(side * rows, rows), rows), :] = part
    d = lax.axis_index("dp")
    wide, narrow = small.shape[1], big[DEC_OUT].shape[1]

    def piece(out, line, lanes, position):
        size = out.shape[0]
        value = small[pl.ds(line, 1), :lanes]
        value = pltpu.roll(value, lax.rem(lanes - position * size, lanes), 1)
        out[...] = value[:, :size].reshape(size)

    def matrix(out, name):
        value = big[name][...].astype(F32)
        out[...] = jnp.transpose(value) if name == DEC_DOWN else value

    def block(outs, first_row, bup_row, lanes, names):
        for i, out in zip((0, 1, None, None, 2, 3, 4, None, None, None, 5), outs):
            if i is not None:
                piece(out, first_row + i, lanes, d)
        piece(outs[8], bup_row + d // 4, lanes, d % 4)
        for at, name in zip((2, 3, 7, 9), names):
            matrix(outs[at], name)

    block(totals[:11], 0, ROW_BUP, wide, (ENC_QKV, ENC_OUT, ENC_UP, ENC_DOWN))
    matrix(totals[11], EMBED)
    piece(totals[12], ROW_DEC + 7, narrow, d)
    piece(totals[13], ROW_DEC + 6, narrow, d)
    block(totals[14:], ROW_DEC, ROW_DEC_BUP, narrow, (DEC_QKV, DEC_OUT, DEC_UP, DEC_DOWN))


def write_outputs(results, decoded_own, dims):
    def vector(size):
        return jax.ShapeDtypeStruct((size // 16,), F32)

    def matrix(name):
        return shape(dims[name][0] // 16, dims[name][1], F32)

    def block(qkv, out, up, down):
        d, ff = dims[up]
        return [
            vector(d), vector(d), matrix(qkv), matrix(out), vector(d), vector(d), vector(d),
            matrix(up), vector(ff), matrix(down), vector(d),
        ]

    samples, half, width = results[1].shape
    rows, columns = results[3].shape
    out_shape = [
        jax.ShapeDtypeStruct((2 * samples, half, width), BF16),
        shape(2 * rows, columns),
        *block(ENC_QKV, ENC_OUT, ENC_UP, ENC_DOWN),
        matrix(EMBED),
        vector(width),
        vector(width),
        *block(DEC_QKV, DEC_OUT, DEC_UP, DEC_DOWN),
    ]
    return tuple(
        pl.pallas_call(
            write_kernel,
            out_shape=out_shape,
            in_specs=in_vmem(len(results) + 1),
            out_specs=in_vmem(len(out_shape)),
            compiler_params=pltpu.CompilerParams(vmem_limit_bytes=KERNEL_VMEM),
            name="write_outputs",
        )(*results, decoded_own)
    )


def reduce_plain(arrays, section_index):
    first = section_index == 0
    results = []
    for a in arrays:
        half = a.shape[1] // 2
        keep = lax.dynamic_slice_in_dim(a, section_index * half, half, 1)
        give = lax.dynamic_slice_in_dim(a, (1 - section_index) * half, half, 1)
        got = swapped(give, "section", 0)
        chip = (keep.astype(jnp.float32) + got.astype(jnp.float32)).astype(jnp.bfloat16)
        mine = lax.psum_scatter(chip, "dp", scatter_dimension=0, tiled=True)
        other = swapped(mine, "section", 0)
        whole = jnp.concatenate(
            [jnp.where(first, mine, other), jnp.where(first, other, mine)], axis=1
        )
        results.append(whole.astype(jnp.float32))
    return results


def finish_plain(acts, section_index):
    x, gy, seg_saved, enc, dec = acts["x"], acts["gy"], acts["saved"], acts["enc"], acts["dec"]
    gx, gf1, ga1, gqkv1, small1, gbup1 = encoder_backward(x, gy, seg_saved, enc["params"])
    small2, gbup2 = acts["small2"], acts["gbup2"]
    grads = (
        small1[0], small1[1], mm(enc["at"], gqkv1).astype(BF16), mm(enc["ot"], ga1).astype(BF16), small1[2],
        small1[3], small1[4], mm(enc["ct"], gf1).astype(BF16), gbup1[0], mm(enc["ut"], gy).astype(BF16),
        small1[5],
        weight_grad(acts["y"], acts["geb"]), small2[7], small2[6],
        small2[0], small2[1], mm(dec["at"], dec["gqkv"]).astype(BF16),
        mm(dec["ot"], dec["ga"]).astype(BF16), small2[2], small2[3], small2[4],
        mm(dec["ct"], dec["gf"]).astype(BF16), gbup2[0],
        jnp.transpose(mm(dec["gt"], dec["u"])).astype(BF16), small2[5],
    )
    groups = lax.axis_size("dp")
    big = reduce_plain([g for g in grads if g.ndim == 2], section_index)
    flat = jnp.concatenate([g.reshape(groups, -1) for g in grads if g.ndim == 1], axis=1)
    line = lax.psum_scatter(flat, ("dp"), scatter_dimension=0, tiled=True)
    line = lax.psum(line, "section")[0]
    totals, at = [], 0
    for g in grads:
        if g.ndim == 2:
            totals.append(big.pop(0))
        else:
            size = g.shape[0] // groups
            totals.append(line[at : at + size])
            at += size
    decoded = acts["decoded"].reshape(SAMP_MB, PATCHES, -1)
    first = section_index == 0

    def halves(whole):
        half = whole.shape[1] // 2
        keep = lax.dynamic_slice_in_dim(whole, section_index * half, half, 1)
        give = lax.dynamic_slice_in_dim(whole, (1 - section_index) * half, half, 1)
        got = swapped(give, "section", 0)
        return jnp.concatenate([jnp.where(first, keep, got), jnp.where(first, got, keep)])

    return (halves(decoded), halves(gx), *totals)


def shards(
    patches,
    segment_ids,
    patch_order,
    encoder_gain1,
    encoder_bias1,
    encoder_qkv,
    encoder_out,
    encoder_out_bias,
    encoder_gain2,
    encoder_bias2,
    encoder_up,
    encoder_up_bias,
    encoder_down,
    encoder_down_bias,
    embed_weight,
    embed_bias,
    mask_token,
    decoder_gain1,
    decoder_bias1,
    decoder_qkv,
    decoder_out,
    decoder_out_bias,
    decoder_gain2,
    decoder_bias2,
    decoder_up,
    decoder_up_bias,
    decoder_down,
    decoder_down_bias,
    cotangent,
):
    enc_params = (
        encoder_gain1,
        encoder_bias1,
        encoder_qkv,
        encoder_out,
        encoder_out_bias,
        encoder_gain2,
        encoder_bias2,
        encoder_up,
        encoder_up_bias,
        encoder_down,
        encoder_down_bias,
    )
    embed_params = (embed_weight, embed_bias, mask_token)
    dec_params = (
        decoder_gain1,
        decoder_bias1,
        decoder_qkv,
        decoder_out,
        decoder_out_bias,
        decoder_gain2,
        decoder_bias2,
        decoder_up,
        decoder_up_bias,
        decoder_down,
        decoder_down_bias,
    )
    section_index = lax.axis_index("section")
    y, at1, qkv, e, rl, o1, ot1, n2, s2, ct1, ut1, slope = encoder_forward(
        patches, segment_ids, enc_params
    )
    g = cotangent.reshape(-1, DECODER_WIDTH)
    decoded, at2, ot2, ct2, gt2, u2, gf2, ga2, gqkv2, geb, gy, small2, gbup2 = decoder_both(
        y, segment_ids, patch_order, g, embed_params, dec_params
    )
    acts = dict(
        x=patches,
        y=y,
        gy=gy,
        geb=geb,
        decoded=decoded,
        small2=small2,
        gbup2=gbup2,
        saved=(qkv, e, rl, o1, n2, s2, slope),
        enc=dict(at=at1, ot=ot1, ct=ct1, ut=ut1, params=enc_params),
        dec=dict(at=at2, ot=ot2, ct=ct2, gt=gt2, u=u2, gf=gf2, ga=ga2, gqkv=gqkv2),
    )
    if lax.axis_size("dp") == 16:
        return finish(acts)
    return finish_plain(acts, section_index)


def solution(mesh):
    in_specs = (
        P("dp", None),
        P("dp", None),
        P("dp", None),
        P(),
        P(),
        P(),
        P(),
        P(),
        P(),
        P(),
        P(),
        P(),
        P(),
        P(),
        P(),
        P(),
        P(),
        P(),
        P(),
        P(),
        P(),
        P(),
        P(),
        P(),
        P(),
        P(),
        P(),
        P(),
        P("dp", None, None),
    )
    out_specs = (
        P("dp", "section", None),
        P("dp", "section"),
        P("dp"),
        P("dp"),
        P("dp", None),
        P("dp", None),
        P("dp"),
        P("dp"),
        P("dp"),
        P("dp", None),
        P("dp"),
        P("dp", None),
        P("dp"),
        P("dp", None),
        P("dp"),
        P("dp"),
        P("dp"),
        P("dp"),
        P("dp", None),
        P("dp", None),
        P("dp"),
        P("dp"),
        P("dp"),
        P("dp", None),
        P("dp"),
        P("dp", None),
        P("dp"),
    )
    return jax.shard_map(shards, mesh=mesh, in_specs=in_specs, out_specs=out_specs, check_vma=False)
```

```python
import functools
import math

import jax
import jax.numpy as jnp
import numpy as np
from jax import lax
from jax.experimental import pallas as pl
from jax.experimental.pallas import tpu as pltpu
from jax.sharding import PartitionSpec as P

H_ENC = 12
DECODER_WIDTH = 512
H_DEC = 16
PATCHES = 128
SAMP_MB = 12


EPSILON = 1e-06
MASKED = -1e30


def swapped(block, axis, apart):
    count = lax.axis_size(axis)
    route = []
    for low in range(count):
        high = low | 1 << apart
        if high != low and high < count:
            route += [(low, high), (high, low)]
    return lax.ppermute(block, axis, route)


def positions(count, features):
    column = np.arange(features)
    rate = np.exp(-math.log(10000.0) * (2 * (column // 2)) / features)
    angles = np.arange(count)[:, None] * rate[None, :]
    return np.where(column % 2 == 0, np.sin(angles), np.cos(angles)).astype(np.float32)


def weight_grad(left_side, grads):
    return lax.dot_general(
        left_side, grads, (((0,), (0,)), ((), ())), preferred_element_type=jnp.float32
    ).astype(jnp.bfloat16)


BF16 = jnp.bfloat16
F32 = jnp.float32


def mm(left, right):
    return lax.dot_general(left, right, (((1,), (0,)), ((), ())), preferred_element_type=F32)


def mm_nt(left, right):
    return lax.dot_general(left, right, (((1,), (1,)), ((), ())), preferred_element_type=F32)


def mm_tn(left, right):
    return lax.dot_general(left, right, (((0,), (0,)), ((), ())), preferred_element_type=F32)


def normalise(x):
    center = x - jnp.mean(x, axis=-1, keepdims=True)
    scale = lax.rsqrt(jnp.mean(center * center, axis=-1, keepdims=True) + EPSILON)
    return center * scale, scale


def normalise_back(grad, n, scale, gain):
    gn = grad * gain
    mean_gn = jnp.mean(gn, axis=-1, keepdims=True)
    mean_gnn = jnp.mean(gn * n, axis=-1, keepdims=True)
    return (gn - mean_gn - n * mean_gnn) * scale


def rows_sum(x):
    return jnp.sum(x, axis=0, keepdims=True)


def gelu_both(f):
    c0, c1 = math.sqrt(2.0 / math.pi), 0.044715
    square = f * f
    half = 0.5 + 0.5 * jnp.tanh(f * (c0 + (c0 * c1) * square))
    u = f * half
    return u, half + u * (1.0 - half) * (2.0 * c0 + (6.0 * c0 * c1) * square)


def lane_masks(head_size):
    lane = lax.broadcasted_iota(jnp.int32, (1, 128), 1)
    return [
        jnp.where((lane >= h * head_size) & (lane < (h + 1) * head_size), 1.0, 0.0).astype(BF16)
        for h in range(128 // head_size)
    ]


def stacked(x, masks):
    return jnp.concatenate([x * m for m in masks], axis=0)


def stacked_ones(x, masks, value):
    return jnp.concatenate(
        [jnp.broadcast_to(m * jnp.asarray(value, BF16), x.shape) for m in masks], axis=0
    )


def attention_forward(qkv_ref, o_ref, e_ref, rl_ref, rows, tokens, features, head_size, allowed):
    masks = lane_masks(head_size)
    per_group = len(masks)
    factor = head_size ** (-0.5) * math.log2(math.e)
    for g in range(features // 128):
        q, k, v = (qkv_ref[rows, j * features + g * 128 : j * features + (g + 1) * 128] for j in range(3))
        scores = mm_nt(q, stacked(k, masks))
        parts = []
        for h in range(per_group):
            part = scores[:, h * tokens : (h + 1) * tokens]
            if allowed is not None:
                part = jnp.where(allowed, part, MASKED)
            top = jnp.max(part, axis=-1, keepdims=True)
            parts.append(jnp.exp2((part - top) * factor).astype(BF16))
        e = jnp.concatenate(parts, axis=1)
        width = per_group * tokens
        e_ref[rows, g * width : (g + 1) * width] = e
        both = mm(e, jnp.concatenate([stacked(v, masks), stacked_ones(v, masks, 1.0)], axis=1))
        rl = 1.0 / both[:, 128:]
        rl_ref[rows, g * 128 : (g + 1) * 128] = rl
        o_ref[rows, g * 128 : (g + 1) * 128] = (both[:, :128] * rl).astype(BF16)


def attention_backward_group(q, k, v, e, go, o, rl, head_size):
    masks = lane_masks(head_size)
    per_group, tokens = len(masks), q.shape[0]
    scaling = head_size ** (-0.5)
    go = go.astype(F32) * rl
    go_low = go.astype(BF16)
    inner = (go * o.astype(F32)).astype(BF16)
    left = jnp.concatenate([go_low, inner], axis=1)
    right = jnp.concatenate([stacked(v, masks), stacked_ones(v, masks, -1.0)], axis=1)
    gs = (e.astype(F32) * mm_nt(left, right)).astype(BF16)

    def diagonal(wide):
        return jnp.concatenate(
            [
                wide[h * head_size : (h + 1) * head_size, h * tokens : (h + 1) * tokens]
                for h in range(per_group)
            ],
            axis=0,
        )

    gq = mm(gs, stacked(k, masks)) * scaling
    gk = jnp.transpose(diagonal(mm_tn(q, gs)) * scaling)
    gv = jnp.transpose(diagonal(mm_tn(go_low, e)))
    return gq.astype(BF16), gk.astype(BF16), gv.astype(BF16)


def attention_backward(
    qkv_ref, go_ref, o_ref, e_ref, rl_ref, gqkv_ref, rows, tokens, features, head_size
):
    width = 128 // head_size * tokens
    for g in range(features // 128):
        at = slice(g * 128, (g + 1) * 128)
        spots = [slice(j * features + g * 128, j * features + (g + 1) * 128) for j in range(3)]
        q, k, v = (qkv_ref[rows, spot] for spot in spots)
        e = e_ref[rows, g * width : (g + 1) * width]
        grads = attention_backward_group(
            q, k, v, e, go_ref[rows, at], o_ref[rows, at], rl_ref[rows, at], head_size
        )
        for spot, grad in zip(spots, grads):
            gqkv_ref[rows, spot] = grad


def feed_forward(c_ref, up_ref, bup_ref, u_ref, slope_ref, tile, ut_ref=None):
    for t in range(up_ref.shape[1] // tile):
        at = slice(t * tile, (t + 1) * tile)
        f = mm(c_ref[...], up_ref[:, at]) + bup_ref[at].reshape(1, tile)
        u, slope = gelu_both(f)
        u = u.astype(BF16)
        u_ref[:, at] = u
        slope_ref[:, at] = slope.astype(BF16)
        if ut_ref is not None:
            ut_ref[at, :] = jnp.transpose(u)


def feed_forward_back(gm_ref, down_ref, slope_ref, gf_ref, gbup_ref, tile):
    for t in range(down_ref.shape[0] // tile):
        at = slice(t * tile, (t + 1) * tile)
        gu = mm_nt(gm_ref[...], down_ref[at, :])
        gf = (gu * slope_ref[:, at].astype(F32)).astype(BF16)
        gf_ref[:, at] = gf
        gbup_ref[:, at] += rows_sum(gf.astype(F32))


def row(ref):
    return ref[...].reshape(1, -1)


def segment_mask(seg_ref, section):
    seg = seg_ref[pl.ds(section, 1), :].astype(F32)
    rows = seg.shape[1]
    column = jnp.transpose(jnp.broadcast_to(seg, (128, rows)))
    return jnp.concatenate([column] * (rows // 128), axis=1) == seg


class Writer:
    def __init__(self, semaphores):
        self.semaphores, self.copies = semaphores, []

    def start(self, source, target):
        copy = pltpu.make_async_copy(source, target, self.semaphores.at[len(self.copies)])
        copy.start()
        self.copies.append(copy)

    def wait(self):
        for copy in self.copies:
            copy.wait()


def encoder_forward_kernel(
    x_ref, seg_ref,
    gain1, bias1, w_qkv, w_out, b_out, gain2, bias2, w_up, b_up, w_down, b_down,
    *refs,
):
    outs, scratch = refs[:12], refs[12:24]
    y_ref, at_ref, qkv_ref, e_ref, rl_ref, o_ref, ot_ref, n2_ref, s2_ref, ct_ref, ut_ref, slope_ref = scratch
    h_ref, c_ref, u_ref, qkv_v, out_v, up_v, down_v, sem, out_sem = refs[24:]
    target = {id(v): o for v, o in zip(scratch, outs)}
    writer = Writer(out_sem)

    def write(*done):
        for v in done:
            writer.start(v, target[id(v)])

    tokens, features = y_ref.shape
    pairs = ((w_qkv, qkv_v), (w_out, out_v), (w_up, up_v), (w_down, down_v))
    loads = [pltpu.make_async_copy(w, v, sem.at[i]) for i, (w, v) in enumerate(pairs)]
    for load in loads:
        load.start()
    section = lax.axis_index("section")
    x = x_ref[pl.ds(pl.multiple_of(section * tokens, tokens), tokens), :].astype(F32)
    n1, _ = normalise(x)
    a = (n1 * row(gain1) + row(bias1)).astype(BF16)
    at_ref[...] = jnp.transpose(a)
    allowed = segment_mask(seg_ref, section)
    loads[0].wait()
    qkv_ref[...] = mm(a, qkv_v[...]).astype(BF16)
    write(at_ref, qkv_ref)
    attention_forward(
        qkv_ref, o_ref, e_ref, rl_ref, slice(None), tokens, features, features // H_ENC, allowed
    )
    ot_ref[...] = jnp.transpose(o_ref[...])
    write(e_ref, rl_ref, o_ref, ot_ref)
    loads[1].wait()
    h_ref[...] = x + (mm(o_ref[...], out_v[...]) + row(b_out))
    n2, s2 = normalise(h_ref[...])
    n2_ref[...] = n2
    s2_ref[...] = s2
    c_ref[...] = (n2 * row(gain2) + row(bias2)).astype(BF16)
    ct_ref[...] = jnp.transpose(c_ref[...])
    write(n2_ref, s2_ref, ct_ref)
    loads[2].wait()
    feed_forward(c_ref, up_v, b_up, u_ref, slope_ref, 512, ut_ref)
    write(ut_ref, slope_ref)
    loads[3].wait()
    y_ref[...] = (h_ref[...] + (mm(u_ref[...], down_v[...]) + row(b_down))).astype(BF16)
    write(y_ref)
    writer.wait()


def encoder_backward_kernel(
    x_ref, gy_ref, qkv_ref, e_ref, rl_ref, o_ref, n2_ref, s2_ref, slope_ref,
    gain1, w_qkv, w_out, gain2, w_up, w_down,
    gx_ref, gf_ref, ga_ref, gqkv_ref, small_ref, gbup_ref,
    gh_ref, go_ref,
):
    tokens, features = gy_ref.shape
    section = lax.axis_index("section")
    x = x_ref[pl.ds(pl.multiple_of(section * tokens, tokens), tokens), :].astype(F32)
    gbup_ref[...] = jnp.zeros_like(gbup_ref)
    feed_forward_back(gy_ref, w_down, slope_ref, gf_ref, gbup_ref, 512)
    gc = mm_nt(gf_ref[...], w_up[...])
    g = gy_ref[...].astype(F32)
    n2 = n2_ref[...]
    gh = g + normalise_back(gc, n2, s2_ref[...], row(gain2))
    gh_ref[...] = gh
    ga_ref[...] = gh.astype(BF16)
    small_ref[2:3, :] = rows_sum(gh)
    small_ref[3:4, :] = rows_sum(gc * n2)
    small_ref[4:5, :] = rows_sum(gc)
    small_ref[5:6, :] = rows_sum(g)
    go_ref[...] = mm_nt(ga_ref[...], w_out[...]).astype(BF16)
    attention_backward(
        qkv_ref, go_ref, o_ref, e_ref, rl_ref, gqkv_ref, slice(None), tokens, features,
        features // H_ENC,
    )
    gn = mm_nt(gqkv_ref[...], w_qkv[...])
    n1, s1 = normalise(x)
    small_ref[0:1, :] = rows_sum(gn * n1)
    small_ref[1:2, :] = rows_sum(gn)
    gx_ref[...] = (gh_ref[...] + normalise_back(gn, n1, s1, row(gain1))).astype(BF16)


def split_low(x):
    high = x.astype(BF16)
    return high, (x - high.astype(F32)).astype(BF16)


def slot_rows(order, seg, sample):
    start = jnp.sum(jnp.where(seg < sample, 1.0, 0.0), axis=1, keepdims=True)
    count = jnp.sum(jnp.where(seg == sample, 1.0, 0.0), axis=1, keepdims=True)
    wide = jnp.broadcast_to(order, (PATCHES, PATCHES))
    lane = lax.broadcasted_iota(jnp.int32, (PATCHES, PATCHES), 1).astype(F32)
    line = lax.broadcasted_iota(jnp.int32, (PATCHES, PATCHES), 0).astype(F32)
    across = jnp.sum(jnp.where(jnp.transpose(wide) == lane, line, 0.0), axis=0, keepdims=True)
    down = jnp.sum(jnp.where(wide == line, lane, 0.0), axis=1, keepdims=True)
    return [jnp.where(rank < count, start + rank, -1.0) for rank in (across, down)]


def decoder_kernel(
    y_ref, seg_ref, order_ref, pos_ref, g_hbm,
    w_embed_hbm, b_embed, mask_token,
    gain1, bias1, w_qkv_hbm, w_out_hbm, b_out, gain2, bias2, w_up_hbm, b_up, w_down_hbm, b_down,
    *refs,
):
    hbm, (geb_ref, gy_ref, small_ref, gbup_ref) = refs[:9], refs[9:13]
    buffers = refs[13:22]
    out_ref, at_ref, ot_ref, ct_ref, gt_ref, u_ref, gf_ref, ga_ref, gqkv_ref = buffers
    (
        e2_ref, z_ref, s1_ref, e_ref, rl_ref, h_ref, s2_ref, go_ref, ge_ref, o_ref, c_ref, qkv_ref,
        slope_ref, g_all, w_embed, w_qkv, w_out, w_up, w_down, w_sem, out_sem,
    ) = refs[22:]
    packed = y_ref.shape[0]
    rows, features = z_ref.shape
    samples = rows // PATCHES
    head_size = features // H_DEC
    total = g_all.shape[0]
    section = lax.axis_index("section")
    mine = pl.ds(pl.multiple_of(section * total, total), total)
    pairs = (
        (w_embed_hbm, w_embed), (w_qkv_hbm, w_qkv), (w_out_hbm, w_out), (w_up_hbm, w_up),
        (w_down_hbm, w_down), (g_hbm.at[mine, :], g_all),
    )
    loads = [pltpu.make_async_copy(a, b, w_sem.at[i]) for i, (a, b) in enumerate(pairs)]
    for load in loads:
        load.start()
    writing = {}

    def write(step, *which):
        at = slice(step * rows, (step + 1) * rows)
        for i in which:
            target = hbm[i].at[:, at] if 1 <= i <= 4 else hbm[i].at[at, :]
            writing[i] = pltpu.make_async_copy(buffers[i], target, out_sem.at[i])
            writing[i].start()

    def free(*which):
        for i in which:
            if i in writing:
                writing.pop(i).wait()

    small_ref[...] = jnp.zeros_like(small_ref)
    gbup_ref[...] = jnp.zeros_like(gbup_ref)
    seg = seg_ref[pl.ds(section, 1), :].astype(F32)
    loads[0].wait()
    high, low = split_low(mm(y_ref[...], w_embed[...]) + row(b_embed))
    e2_ref[:packed, :] = high
    e2_ref[packed:, :] = low

    def one_step(step):
        first = step == 0
        hots, places, empties = [], [], []
        for j in range(samples):
            sample = step * samples + j
            order = order_ref[pl.ds(section * SAMP_MB + sample, 1), :].astype(F32)
            across, down = slot_rows(order, seg, float(sample))
            column = lax.broadcasted_iota(jnp.int32, (PATCHES, packed), 1).astype(F32)
            line = lax.broadcasted_iota(jnp.int32, (packed, PATCHES), 0).astype(F32)
            hots.append(jnp.where(column == down, 1.0, 0.0).astype(BF16))
            places.append(jnp.where(line == across, 1.0, 0.0).astype(BF16))
            empties.append(jnp.where(down < 0.0, 1.0, 0.0))
        one_hot = jnp.concatenate(hots, axis=0)
        empty = jnp.concatenate(empties, axis=0)
        twice = jnp.concatenate([one_hot, one_hot], axis=1)
        z = mm(twice, e2_ref[...]) + empty * row(mask_token)
        z = z + jnp.concatenate([pos_ref[...]] * samples, axis=0)
        n1, s1 = normalise(z)
        z_ref[...] = z
        s1_ref[...] = s1
        a = (n1 * row(gain1) + row(bias1)).astype(BF16)
        free(1)
        at_ref[...] = jnp.transpose(a)
        write(step, 1)
        if first:
            loads[1].wait()
        qkv_ref[...] = mm(a, w_qkv[...]).astype(BF16)

        def forward(b, carry):
            at = pl.ds(pl.multiple_of(b * PATCHES, PATCHES), PATCHES)
            attention_forward(qkv_ref, o_ref, e_ref, rl_ref, at, PATCHES, features, head_size, None)
            return carry

        lax.fori_loop(0, samples, forward, 0, unroll=2)
        free(2, 3, 5)
        if first:
            loads[2].wait()
            loads[3].wait()
        ot_ref[...] = jnp.transpose(o_ref[...])
        h_ref[...] = z_ref[...] + (mm(o_ref[...], w_out[...]) + row(b_out))
        n2, s2 = normalise(h_ref[...])
        s2_ref[...] = s2
        c_ref[...] = (n2 * row(gain2) + row(bias2)).astype(BF16)
        ct_ref[...] = jnp.transpose(c_ref[...])
        feed_forward(c_ref, w_up, b_up, u_ref, slope_ref, 512)
        write(step, 2, 3, 5)
        free(0, 4, 6, 7)
        if first:
            loads[4].wait()
            loads[5].wait()
        out_ref[...] = (h_ref[...] + (mm(u_ref[...], w_down[...]) + row(b_down))).astype(BF16)

        g_ref = g_all.at[step * rows : (step + 1) * rows, :]
        gt_ref[...] = jnp.transpose(g_ref[...])
        feed_forward_back(g_ref, w_down, slope_ref, gf_ref, gbup_ref, 512)
        write(step, 0, 4, 6)
        gc = mm_nt(gf_ref[...], w_up[...])
        g = g_ref[...].astype(F32)
        h = h_ref[...]
        n2 = (h - jnp.mean(h, axis=-1, keepdims=True)) * s2_ref[...]
        gh = g + normalise_back(gc, n2, s2_ref[...], row(gain2))
        small_ref[2:3, :] += rows_sum(gh)
        small_ref[3:4, :] += rows_sum(gc * n2)
        small_ref[4:5, :] += rows_sum(gc)
        small_ref[5:6, :] += rows_sum(g)
        h_ref[...] = gh
        ga_ref[...] = gh.astype(BF16)
        go_ref[...] = mm_nt(ga_ref[...], w_out[...]).astype(BF16)
        write(step, 7)
        free(8)

        def backward(b, carry):
            at = pl.ds(pl.multiple_of(b * PATCHES, PATCHES), PATCHES)
            attention_backward(
                qkv_ref, go_ref, o_ref, e_ref, rl_ref, gqkv_ref, at, PATCHES, features, head_size
            )
            return carry

        lax.fori_loop(0, samples, backward, 0, unroll=2)
        write(step, 8)
        gn = mm_nt(gqkv_ref[...], w_qkv[...])
        z = z_ref[...]
        n1 = (z - jnp.mean(z, axis=-1, keepdims=True)) * s1_ref[...]
        gz = h_ref[...] + normalise_back(gn, n1, s1_ref[...], row(gain1))
        small_ref[0:1, :] += rows_sum(gn * n1)
        small_ref[1:2, :] += rows_sum(gn)
        small_ref[6:7, :] += rows_sum(gz * empty)
        part = mm(jnp.concatenate(places, axis=1), gz.astype(BF16))
        ge_ref[...] = part if first else ge_ref[...] + part

    for step in range(total // rows):
        one_step(step)
    ge = ge_ref[...]
    small_ref[7:8, :] = rows_sum(ge)
    geb_ref[...] = ge.astype(BF16)
    gy_ref[...] = mm_nt(geb_ref[...], w_embed[...]).astype(BF16)
    free(*range(9))


def in_vmem(count):
    return [pl.BlockSpec(memory_space=pltpu.VMEM)] * count


def in_hbm():
    return pl.BlockSpec(memory_space=pl.ANY)


def shape(rows, columns, dtype=BF16):
    return jax.ShapeDtypeStruct((rows, columns), dtype)


KERNEL_VMEM = 60 * 2**20


def encoder_forward(x, segments, params):
    rows, d = x.shape[0] // 2, x.shape[1]
    ff = params[7].shape[1]
    outs = [
        (rows, d, BF16),
        (d, rows, BF16),
        (rows, 3 * d, BF16),
        (rows, H_ENC * rows, BF16),
        (rows, d, F32),
        (rows, d, BF16),
        (d, rows, BF16),
        (rows, d, F32),
        (rows, 1, F32),
        (d, rows, BF16),
        (ff, rows, BF16),
        (rows, ff, BF16),
    ]
    more = [(rows, d, F32), (rows, d, BF16), (rows, ff, BF16)]
    args = [x, segments, *params]
    matrices = [w for w in params if w.dtype == BF16]
    return pl.pallas_call(
        encoder_forward_kernel,
        out_shape=[shape(*o) for o in outs],
        in_specs=in_vmem(2) + [in_hbm() if w.dtype == BF16 else in_vmem(1)[0] for w in params],
        out_specs=[in_hbm()] * len(outs),
        scratch_shapes=[pltpu.VMEM((r, w), t) for r, w, t in outs + more]
        + [pltpu.VMEM(w.shape, BF16) for w in matrices]
        + [pltpu.SemaphoreType.DMA((len(matrices),)), pltpu.SemaphoreType.DMA((len(outs),))],
        compiler_params=pltpu.CompilerParams(vmem_limit_bytes=KERNEL_VMEM),
        name="encoder_forward",
    )(*args)


def encoder_backward(x, gy, saved, params):
    gain1, _, w_qkv, w_out, _, gain2, _, w_up, _, w_down, _ = params
    rows, d = gy.shape
    ff = w_up.shape[1]
    outs = [
        shape(rows, d),
        shape(rows, ff),
        shape(rows, d),
        shape(rows, 3 * d),
        shape(8, d, F32),
        shape(1, ff, F32),
    ]
    args = [x, gy, *saved, gain1, w_qkv, w_out, gain2, w_up, w_down]
    return pl.pallas_call(
        encoder_backward_kernel,
        out_shape=outs,
        in_specs=in_vmem(len(args)),
        out_specs=in_vmem(len(outs)),
        scratch_shapes=[pltpu.VMEM((rows, d), F32), pltpu.VMEM((rows, d), BF16)],
        compiler_params=pltpu.CompilerParams(vmem_limit_bytes=KERNEL_VMEM),
        name="encoder_backward",
    )(*args)


def decoder_both(y, segments, orders, g, embed_params, params):
    packed, d_enc = y.shape
    total, d = g.shape[0] // 2, g.shape[1]
    rows = 6 * PATCHES
    ff = params[7].shape[1]
    args = [y, segments, orders, positions(PATCHES, d), g, *embed_params, *params]
    in_specs = in_vmem(4) + [in_hbm()]
    in_specs += [in_hbm() if x.dtype == BF16 else in_vmem(1)[0] for x in args[5:]]
    wide = [ff, ff, d, 3 * d]
    outs = [shape(total, d)] + [shape(d, total)] * 4 + [shape(total, w) for w in wide]
    buffers = [(rows, d, BF16)] + [(d, rows, BF16)] * 4 + [(rows, w, BF16) for w in wide]
    last = [shape(packed, d), shape(packed, d_enc), shape(8, d, F32), shape(1, ff, F32)]
    scratch = [
        (2 * packed, d, BF16),
        (rows, d, F32),
        (rows, 1, F32),
        (rows, H_DEC * PATCHES, BF16),
        (rows, d, F32),
        (rows, d, F32),
        (rows, 1, F32),
        (rows, d, BF16),
        (packed, d, F32),
        (rows, d, BF16),
        (rows, d, BF16),
        (rows, 3 * d, BF16),
        (rows, ff, BF16),
        (total, d, BF16),
    ]
    matrices = [x for x in args[5:] if x.dtype == BF16]
    return pl.pallas_call(
        decoder_kernel,
        out_shape=outs + last,
        in_specs=in_specs,
        out_specs=[in_hbm()] * len(outs) + in_vmem(len(last)),
        scratch_shapes=[pltpu.VMEM((r, w), t) for r, w, t in buffers + scratch]
        + [pltpu.VMEM(x.shape, BF16) for x in matrices]
        + [pltpu.SemaphoreType.DMA((k,)) for k in (len(matrices) + 1, len(outs))],
        compiler_params=pltpu.CompilerParams(vmem_limit_bytes=KERNEL_VMEM),
        name="decoder_both",
    )(*args)


MESH = pl.DeviceIdType.MESH
ENC_QKV, ENC_OUT, ENC_UP, ENC_DOWN, EMBED, DEC_QKV, DEC_OUT, DEC_UP, DEC_DOWN = range(9)
GIVE, PAIR, FFN, LN2, GO, ATT, GN, LAST = range(10, 18)
SMALL = -1
ROW_BUP, ROW_DEC_BUP, ROW_DEC, SMALL_ROWS = 6, 10, 16, 24
Z, Y, X, CORE = range(4)
ORDERS = ((X, Y, Z), (Y, X, Z), (X, Z, Y), (Y, Z, X))


class Chunk:
    def __init__(self, name, half, offset, rows, width, first_row=None):
        self.name, self.half, self.offset, self.rows, self.width = name, half, offset, rows, width
        self.first_row, self.turned, self.order = first_row, name == DEC_DOWN, None
        self.decoder = name in (DEC_QKV, DEC_UP, DEC_OUT)

    def columns(self, side):
        return pl.ds(pl.multiple_of(side * self.half + self.offset, 128), self.width)

    def place(self, side):
        if self.turned:
            return (pl.ds(pl.multiple_of(side * self.half + self.offset, 128), self.rows), slice(None))
        if self.first_row is None:
            return (slice(None), self.columns(side))
        return (pl.ds(self.first_row, self.rows), self.columns(side))

    @property
    def bytes(self):
        return 32 * self.rows * self.width

    def loads(self, order):
        first, second, third = order
        if second == Z:
            return (self.bytes, self.bytes, self.bytes / 8)
        return (self.bytes, self.bytes / 2, self.bytes / 2)


def make_chunks():
    chunks = [Chunk(DEC_OUT, 256, 0, 32, 256)]
    chunks += [Chunk(DEC_QKV, 768, o, 32, 256) for o in (0, 256, 512)]
    chunks += [Chunk(ENC_DOWN, 384, 0, 48, 384, 48 * q) for q in range(4)]
    chunks += [Chunk(ENC_UP, 1536, o, 48, 384) for o in (0, 384, 768, 1152)]
    chunks += [Chunk(ENC_OUT, 384, 0, 48, 384)]
    chunks += [Chunk(ENC_QKV, 1152, o, 48, 384) for o in (0, 384, 768)]
    chunks += [Chunk(EMBED, 256, 0, 48, 256)]
    chunks += [Chunk(DEC_DOWN, 256, o, 128, 128) for o in (0, 128)]
    chunks += [Chunk(DEC_UP, 1024, o, 32, 256) for o in (0, 256, 512, 768)]
    for c, chunk in enumerate(chunks):
        chunk.order = ORDERS[c % 2]

    def busiest():
        load = [0.0, 0.0, 0.0]
        for chunk in chunks:
            for axis, size in zip(chunk.order, chunk.loads(chunk.order)):
                load[axis] += size
        return sorted(load, reverse=True)

    best, better = busiest(), True
    while better:
        better = False
        for chunk in chunks:
            for order in ORDERS:
                before, chunk.order = chunk.order, order
                if busiest() < best:
                    best, better = busiest(), True
                else:
                    chunk.order = before
    return chunks


TOGETHER = {ENC_UP: 2, ENC_QKV: 3, DEC_QKV: 3, DEC_UP: 2, DEC_DOWN: 2}


def make_groups(chunks):
    groups = []
    for c, k in enumerate(chunks):
        if groups and chunks[groups[-1][0]].name == k.name and len(groups[-1]) < TOGETHER.get(k.name, 1):
            groups[-1].append(c)
        else:
            groups.append([c])
    return groups


def product_cost(k, count):
    return count * (1.1 if k.decoder else 3.0 if k.turned else 0.7)


def tasks_in_order(chunks, groups):
    def gives(name):
        found = [(g, chunks[m[0]], len(m)) for g, m in enumerate(groups)]
        kind = PAIR if name == DEC_DOWN else GIVE
        return [(kind, g, product_cost(k, size)) for g, k, size in found if k.name == name]

    tasks = gives(DEC_OUT) + gives(DEC_QKV)
    tasks += [(FFN, t, 2.5) for t in range(4)]
    tasks += gives(ENC_DOWN) + gives(ENC_UP)
    tasks += [(LN2, 0, 1.5), (GO, 0, 1.2)]
    tasks += [(ATT, g, 2.2) for g in range(6)]
    tasks += gives(ENC_OUT) + gives(ENC_QKV)
    tasks += [(GN, j, 1.2) for j in range(3)] + [(LAST, 0, 2.0)]
    return tasks + gives(EMBED) + gives(DEC_DOWN) + gives(DEC_UP)


def decoder_arrays(chunks):
    names = []
    for k in chunks:
        if (k.decoder or k.turned) and k.name not in names:
            names.append(k.name)
    return names


def make_plan(chunks, groups):
    tasks = tasks_in_order(chunks, groups)
    lhs = decoder_arrays(chunks)
    free = [0.0] * 4
    rate = [82e3, 82e3, 82e3, 500e3]
    pending, plan, now, owned = [], [], 2.0, set()

    def send(link, size, latency):
        begin = max(now, free[link])
        free[link] = begin + size / rate[link]
        return free[link] + latency

    def blocked(task):
        if task[0] not in (GIVE, PAIR):
            return False
        name = chunks[groups[task[1]][0]].name
        if name not in lhs[2:]:
            return False
        name = lhs[lhs.index(name) - 2]
        return any(chunks[m[0]].name == name and g not in owned for g, m in enumerate(groups))

    while tasks or pending:
        pending.sort()
        if pending and (pending[0][0] <= now or not tasks or blocked(tasks[0])):
            arrive, stage, c = pending.pop(0)
            now = max(now, arrive)
            plan.append((stage, c))
            if c == SMALL:
                now += 0.1
                if stage < 4:
                    pending.append((now + 2.0, stage + 1, c))
                continue
            members = groups[c] if stage == 1 else [c]
            k = chunks[members[0]]
            if stage == 1:
                owned.add(c)
                now += 0.6 if k.turned else product_cost(k, len(members)) + 0.2 * len(members)
            else:
                now += 0.25
            for c in members:
                k = chunks[c]
                if stage < 4:
                    axis = k.order[stage - 1]
                    latency = 2.0 if axis == Z else 1.5
                    arrive = send(axis, k.loads(k.order)[stage - 1], latency)
                    pending.append((arrive, stage + 1, c))
                elif stage == 4:
                    pending.append((send(CORE, k.bytes / 16, 1.0), 5, c))
            continue
        name, arg, cost = tasks.pop(0)
        plan.append((name, arg))
        now += cost
        if name in (GIVE, PAIR):
            arrive = [send(CORE, chunks[c].bytes, 1.0) for c in groups[arg]]
            pending.append((max(arrive), 1, arg))
        elif name == LAST:
            pending.append((now + 2.0, 1, SMALL))
    return plan


class Ring:
    def __init__(self, sources, slots, semaphores, depth):
        self.copies = [
            pltpu.make_async_copy(source, slot, semaphores())
            for source, slot in zip(sources, slots)
        ]
        self.slots, self.depth, self.at = slots, depth, 0

    def begin(self):
        for copy in self.copies[: self.depth]:
            copy.start()

    def take(self):
        self.copies[self.at].wait()
        return self.slots[self.at]

    def done(self):
        ahead = self.at + self.depth
        if ahead < len(self.copies):
            self.copies[ahead].start()
        self.at += 1


class Names:
    def __init__(self, names, refs):
        self.__dict__.update(zip(names, refs))


LOADS = 96


def finish_kernel(chunks, groups, plan, r):
    n = len(chunks)
    s = lax.axis_index("section")
    d = lax.axis_index("dp")
    here = (d // 4, (d // 2) % 2, d % 2)
    z, y, x = here
    sibling = {"section": 1 - s}
    z_at = [lax.rem(z + k, 4) for k in (1, 2, 3)]
    peers = {
        X: [(1 - x, {"dp": d + 1 - 2 * x})],
        Y: [(1 - y, {"dp": d + 2 - 4 * y})],
        Z: [(p, {"dp": d + 4 * (p - z)}) for p in z_at],
    }
    every = [sibling] + [peer for axis in (X, Y, Z) for _, peer in peers[axis]]

    barrier = pltpu.get_barrier_semaphore()
    for peer in every:
        pl.semaphore_signal(barrier, inc=1, device_id=peer, device_id_type=MESH)

    counter = iter(range(LOADS))

    def semaphore():
        return r.load_sem.at[next(counter)]

    def remote(src, dst, send, recv, peer):
        return pltpu.make_async_remote_copy(
            src_ref=src, dst_ref=dst, send_sem=send, recv_sem=recv, device_id=peer, device_id_type=MESH
        )

    rhs_of = {DEC_QKV: r.gqkv2, DEC_UP: r.gf2, DEC_OUT: r.ga2}
    lhs_of = {DEC_QKV: r.at2, DEC_UP: r.ct2, DEC_OUT: r.ot2, DEC_DOWN: r.gt2}
    tiles, widths, last_use = [], [], {}

    def wide_columns(g, side):
        k, width = chunks[groups[g][0]], sum(chunks[c].width for c in groups[g])
        return pl.ds(pl.multiple_of(side * k.half + k.offset, 128), width)

    for i, (name, arg) in enumerate(plan):
        if name == PAIR:
            tiles += [r.u2.at[:, t * 512 : (t + 1) * 512] for t in range(4)]
            last_use[DEC_DOWN] = i
        elif name in (GIVE, 1) and arg != SMALL and chunks[groups[arg][0]].decoder:
            k = chunks[groups[arg][0]]
            tiles.append(rhs_of[k.name].at[:, wide_columns(arg, 1 - s if name == GIVE else s)])
            last_use[k.name] = i
    lhs_names = decoder_arrays(chunks)
    assert sorted(lhs_names, key=last_use.get) == lhs_names
    rhs_slots = [r.rhs.at[i % 2, :, : tile.shape[1]] for i, tile in enumerate(tiles)]
    rhs = Ring(tiles, rhs_slots, semaphore, 2)
    lhs = Ring([lhs_of[k] for k in lhs_names], [r.lhs.at[i % 2] for i in range(4)], semaphore, 2)
    lhs.copies[0].start()
    rhs.begin()
    lhs.copies[1].start()
    tokens, d_enc = r.gy.shape
    blocks = []
    for t in range(4):
        at = pl.ds(t * d_enc, d_enc)
        blocks += [r.w_down.at[at, :], r.w_up.at[:, at]]
    blocks.append(r.w_out)
    blocks += [r.w_qkv.at[:, pl.ds(j * d_enc, d_enc)] for j in range(3)]
    weights = Ring(blocks, [r.w.at[i % 4] for i in range(12)], semaphore, 4)
    e_width = 2 * tokens
    e_ring = Ring(
        [r.e.at[:, pl.ds(g * e_width, e_width)] for g in range(6)],
        [r.e_v.at[g % 2] for g in range(6)],
        semaphore,
        2,
    )

    def load(source, target):
        return pltpu.make_async_copy(source, target, semaphore())

    mine = pl.ds(pl.multiple_of(s * tokens, tokens), tokens)
    load_gy, load_slope, load_ut = load(r.gy, r.gy_v), load(r.slope, r.slope_v), load(r.ut, r.ut_v)
    load_ct, load_at, load_ot = load(r.ct, r.ct_v), load(r.at, r.at_v), load(r.ot, r.ot_v)
    load_n2, load_s2, load_qkv = load(r.n2, r.n2_v), load(r.s2, r.s2_v), load(r.qkv, r.qkv_v)
    load_o, load_rl, load_x = load(r.o, r.o_v), load(r.rl, r.rl_v), load(r.x.at[mine, :], r.x_v)
    load_y, load_geb = load(r.y, r.y_v), load(r.geb, r.geb_v)
    begun = [
        (load_gy, load_slope, weights),
        (load_ut, load_ct, load_n2, load_s2),
        (load_qkv, load_o, load_rl, e_ring),
        (load_ot, load_at, load_x, load_y, load_geb),
    ]

    def begin_some():
        for copy in begun.pop(0) if begun else ():
            copy.begin() if isinstance(copy, Ring) else copy.start()

    half = r.decoded.shape[1] // 2
    give_half = r.decoded.at[:, pl.ds(pl.multiple_of((1 - s) * half, half), half), :]
    decoded_away = remote(give_half, r.decoded_got, r.swap_sem.at[0], r.swap_sem.at[1], sibling)
    gx_columns = d_enc // 2
    gx_half = r.gx.at[:, pl.ds(pl.multiple_of((1 - s) * gx_columns, 128), gx_columns)]
    gx_away = remote(gx_half, r.gx_got, r.swap_sem.at[2], r.swap_sem.at[3], sibling)

    small = r.small
    small[...] = jnp.zeros_like(small)
    small[ROW_DEC : ROW_DEC + 8, : r.small2.shape[1]] = r.small2[...]
    quarter = r.gbup2.shape[1] // 4
    for i in range(4):
        piece = r.gbup2[:, i * quarter : (i + 1) * quarter]
        small[ROW_DEC_BUP + i : ROW_DEC_BUP + i + 1, :quarter] = piece

    pl.semaphore_wait(barrier, len(every))

    copies = {}
    first_slot = (0, 1, 2, 5, 8)

    def chunk_copy(c, slot, src, dst, peer):
        copy = remote(src, dst, r.send_sem.at[c, slot], r.recv_sem.at[c, slot], peer)
        copy.start()
        copies[c, slot] = copy

    sent = set()

    def sent_by(c, slot):
        if (c, slot) not in sent:
            sent.add((c, slot))
            copies[c, slot].wait_send()

    staged = {}

    def staging(c):
        k = chunks[c]
        buffers = r.stage[k.rows, k.width]
        turn = staged.setdefault((k.rows, k.width), [])
        if len(turn) >= len(buffers):
            sent_by(turn[-len(buffers)], 0)
        turn.append(c)
        return buffers[(len(turn) - 1) % len(buffers)]

    def shard(i):
        return (i // 4, (i // 2) % 2, i % 2)

    waited = set()

    def arrived(copy):
        if id(copy) not in waited:
            waited.add(id(copy))
            copy.wait()

    def product(g, side):
        k, columns = chunks[groups[g][0]], wide_columns(g, side)
        if k.decoder:
            return mm(lhs.slots[lhs_names.index(k.name)][...], rhs.take()[...])
        if k.name == EMBED:
            arrived(load_y)
            arrived(load_geb)
            return mm_tn(r.y_v[...], r.geb_v[:, columns])
        if k.name == ENC_DOWN:
            arrived(load_ut)
            at = [i * 192 + k.first_row for i in range(16)]
            left = jnp.concatenate([r.ut_v[i : i + k.rows, :] for i in at], axis=0)
            return mm(left, r.gy_v[:, columns])
        if k.name == ENC_UP:
            arrived(load_ct)
            return mm(r.ct_v[...], r.slope_v[:, columns])
        if k.name == ENC_OUT:
            arrived(load_ot)
            return mm(r.ot_v[...], r.ga_v[:, columns])
        arrived(load_at)
        return mm(r.at_v[...], r.qkv_v[:, columns])

    def after_product(i, g):
        k = chunks[groups[g][0]]
        if k.decoder:
            rhs.done()
            if last_use[k.name] == i:
                lhs.done()

    def wait_lhs(k):
        if k.name in lhs_names:
            arrived(lhs.copies[lhs_names.index(k.name)])

    def give(i, g):
        members = groups[g]
        wait_lhs(chunks[members[0]])
        buffers = [staging(c) for c in members]
        value = product(g, 1 - s).astype(BF16)
        for m, (c, buffer) in enumerate(zip(members, buffers)):
            k = chunks[c]
            part = value[:, m * k.width : (m + 1) * k.width]
            for j in range(16):
                buffer[shard(j)] = part[j * k.rows : (j + 1) * k.rows]
            chunk_copy(c, 0, buffer, r.acc[c], sibling)
        after_product(i, g)
        begin_some()

    def pair(i, g):
        both = groups[g]
        wait_lhs(chunks[both[0]])
        left = lhs.slots[lhs_names.index(DEC_DOWN)]
        side_rows = chunks[both[0]].half
        buffers = [staging(c) for c in both]
        for t in range(4):
            tile = rhs.take()
            for side, targets in ((1 - s, buffers), (s, [r.acc[c] for c in both])):
                at = pl.ds(pl.multiple_of(side * side_rows, side_rows), side_rows)
                value = mm(left[at, :], tile[...]).astype(BF16)
                for c, target in zip(both, targets):
                    k = chunks[c]
                    rows = slice(k.offset, k.offset + k.rows)
                    for j in range(4):
                        target[shard(4 * t + j)] = value[rows, j * k.width : (j + 1) * k.width]
            rhs.done()
        lhs.done()
        for c, buffer in zip(both, buffers):
            chunk_copy(c, 0, buffer, r.got[c], sibling)

    def spots(k, stage):
        fixed = {axis: here[axis] for axis in k.order[: stage - 1]}
        return [fixed.get(axis, slice(None)) for axis in (Z, Y, X)]

    def send_stage(c, stage):
        k = chunks[c]
        axis = k.order[stage - 1]
        for j, (coordinate, peer) in enumerate(peers[axis]):
            at = spots(k, stage)
            at[axis] = coordinate
            src = r.acc[c].at[tuple(at)]
            chunk_copy(c, first_slot[stage] + j, src, r.recv[stage - 1][c].at[j], peer)

    def got_stage(c, stage):
        k = chunks[c]
        count = len(peers[k.order[stage - 1]])
        for j in range(count):
            copies[c, first_slot[stage] + j].wait_recv()
        return count

    def add_stage(c, stage):
        k, acc, got = chunks[c], r.acc[c], r.recv[stage - 1][c]
        count = got_stage(c, stage)
        left = [axis for axis in (Z, Y, X) if axis not in k.order[:stage]]
        sizes = [(4, 2, 2)[axis] for axis in left]
        for j in range(math.prod(sizes)):
            place, rest = {}, j
            for axis, size in reversed(list(zip(left, sizes))):
                place[axis] = rest % size
                rest //= size
            at = tuple(place.get(axis, here[axis]) for axis in (Z, Y, X))
            index = tuple(place[axis] for axis in left)
            if count == 1:
                acc[at] = acc[at] + got[(0,) + index]
            else:
                total = acc[at].astype(F32)
                for m in range(count):
                    total = total + got[(m,) + index].astype(F32)
                acc[at] = total.astype(BF16)

    def stage1(i, g):
        members = groups[g]
        for c in members:
            copies[c, 0].wait_recv()
        if chunks[members[0]].turned:
            for c in members:
                acc = r.acc[c]
                for j in range(16):
                    acc[shard(j)] = acc[shard(j)] + r.got[c][shard(j)]
                send_stage(c, 1)
            return
        value = product(g, s)
        for m, c in enumerate(members):
            k, acc = chunks[c], r.acc[c]
            wide = value[:, m * k.width : (m + 1) * k.width]
            for j in range(16):
                part = wide[j * k.rows : (j + 1) * k.rows]
                acc[shard(j)] = (part + acc[shard(j)].astype(F32)).astype(BF16)
            send_stage(c, 1)
        after_product(i, g)

    def stage2(i, c):
        add_stage(c, 1)
        send_stage(c, 2)

    def stage3(i, c):
        add_stage(c, 2)
        send_stage(c, 3)

    def stage4(i, c):
        k = chunks[c]
        total = r.acc[c][here].astype(F32)
        for j in range(got_stage(c, 3)):
            total = total + r.recv[2][c][j].astype(F32)
        out = r.out[k.name]
        out[k.place(s)] = total.astype(BF16)
        final = out.at[k.place(s)]
        chunk_copy(c, 8, final, final, sibling)

    def stage5(i, c):
        copies[c, 8].wait_recv()

    small_copies = []

    def small_copy(source, peer):
        slot = len(small_copies)
        copy = remote(
            source, r.small_got.at[slot], r.small_sem.at[0, slot], r.small_sem.at[1, slot], peer
        )
        copy.start()
        small_copies.append(copy)

    def small_stage(stage):
        if stage < 4:
            small_copies[stage - 1].wait()
            total = small[...] + r.small_got[stage - 1]
            if stage < 3:
                small[...] = total
                small_copy(small, peers[X if stage == 1 else Y][0][1])
            else:
                r.small_sum[...] = total
                for _, peer in peers[Z]:
                    small_copy(r.small_sum, peer)
        else:
            total = r.small_sum[...]
            for j in range(3):
                small_copies[3 + j].wait()
                total = total + r.small_got[3 + j]
            r.out_small[...] = total

    def ffn(i, t):
        if t == 0:
            load_gy.wait()
            load_slope.wait()
            begin_some()
        at = slice(t * d_enc, (t + 1) * d_enc)
        gu = mm_nt(r.gy_v[...], weights.take()[...])
        weights.done()
        gf = (gu * r.slope_v[:, at].astype(F32)).astype(BF16)
        r.slope_v[:, at] = gf
        small[ROW_BUP + t : ROW_BUP + t + 1, :] = rows_sum(gf.astype(F32))
        gc = mm_nt(gf, weights.take()[...])
        weights.done()
        r.sum_v[...] = gc if t == 0 else r.sum_v[...] + gc

    def ln2(i, _):
        load_n2.wait()
        load_s2.wait()
        g, gc, n2 = r.gy_v[...].astype(F32), r.sum_v[...], r.n2_v[...]
        gh = g + normalise_back(gc, n2, r.s2_v[...], row(r.gain2))
        begin_some()
        small[2:3, :] = rows_sum(gh)
        small[3:4, :] = rows_sum(gc * n2)
        small[4:5, :] = rows_sum(gc)
        small[5:6, :] = rows_sum(g)
        r.n2_v[...] = gh
        r.ga_v[...] = gh.astype(BF16)

    def go(i, _):
        r.go_v[...] = mm_nt(r.ga_v[...], weights.take()[...]).astype(BF16)
        weights.done()

    def att(i, g):
        if g == 0:
            for copy in (load_qkv, load_o, load_rl):
                copy.wait()
        at = slice(g * 128, (g + 1) * 128)
        parts = [slice(j * d_enc + g * 128, j * d_enc + (g + 1) * 128) for j in range(3)]
        q, k, v = (r.qkv_v[:, part] for part in parts)
        grads = attention_backward_group(
            q, k, v, e_ring.take()[...], r.go_v[:, at], r.o_v[:, at], r.rl_v[:, at],
            d_enc // H_ENC,
        )
        e_ring.done()
        for part, grad in zip(parts, grads):
            r.qkv_v[:, part] = grad

    def gn(i, j):
        part = mm_nt(r.qkv_v[:, j * d_enc : (j + 1) * d_enc], weights.take()[...])
        weights.done()
        r.sum_v[...] = part if j == 0 else r.sum_v[...] + part

    def last(i, _):
        load_x.wait()
        n1, s1 = normalise(r.x_v[...].astype(F32))
        total = r.sum_v[...]
        small[0:1, :] = rows_sum(total * n1)
        small[1:2, :] = rows_sum(total)
        small_copy(small, sibling)
        gx = r.n2_v[...] + normalise_back(total, n1, s1, row(r.gain1))
        r.gx[...] = gx.astype(BF16)
        gx_away.start()
        decoded_away.start()

    run = {
        GIVE: give, PAIR: pair, FFN: ffn, LN2: ln2, GO: go, ATT: att, GN: gn, LAST: last,
        1: stage1, 2: stage2, 3: stage3, 4: stage4, 5: stage5,
    }
    for i, (name, arg) in enumerate(plan):
        if arg == SMALL:
            small_stage(name)
        else:
            run[name](i, arg)

    for c, slot in copies:
        sent_by(c, slot)
    gx_away.wait()
    decoded_away.wait()


def finish_buffers(chunks, rows, d, ff, dec_total, dec):
    def of(dtype, *dims):
        return (dims, dtype)

    return dict(
        y_v=of(BF16, rows, d),
        geb_v=of(BF16, rows, dec),
        gy_v=of(BF16, rows, d),
        slope_v=of(BF16, rows, ff),
        n2_v=of(F32, rows, d),
        s2_v=of(F32, rows, 1),
        qkv_v=of(BF16, rows, 3 * d),
        o_v=of(BF16, rows, d),
        rl_v=of(F32, rows, d),
        x_v=of(BF16, rows, d),
        ga_v=of(BF16, rows, d),
        go_v=of(BF16, rows, d),
        sum_v=of(F32, rows, d),
        ut_v=of(BF16, ff, rows),
        ct_v=of(BF16, d, rows),
        at_v=of(BF16, d, rows),
        ot_v=of(BF16, d, rows),
        e_v=of(BF16, 2, rows, 2 * rows),
        w=of(BF16, 4, d, d),
        lhs=of(BF16, 2, dec, dec_total),
        rhs=of(BF16, 2, dec_total, 768),
        small=of(F32, SMALL_ROWS, d),
        small_sum=of(F32, SMALL_ROWS, d),
        small_got=of(F32, 6, SMALL_ROWS, d),
    )


def finish(acts):
    enc, dec = acts["enc"], acts["dec"]
    gain1, _, w_qkv, w_out, _, gain2, _, w_up, _, w_down, _ = enc["params"]
    qkv, e, rl, o, n2, s2, slope = acts["saved"]
    given = dict(
        x=acts["x"], y=acts["y"], gy=acts["gy"], geb=acts["geb"], qkv=qkv, e=e, rl=rl, o=o, n2=n2,
        s2=s2, slope=slope, at=enc["at"], ot=enc["ot"], ct=enc["ct"], ut=enc["ut"], at2=dec["at"], ot2=dec["ot"],
        ct2=dec["ct"], gt2=dec["gt"], u2=dec["u"], gf2=dec["gf"], ga2=dec["ga"],
        gqkv2=dec["gqkv"], w_qkv=w_qkv, w_out=w_out, w_up=w_up, w_down=w_down,
        decoded=acts["decoded"].reshape(SAMP_MB, PATCHES, -1),
    )
    n_hbm = len(given)
    given.update(small2=acts["small2"], gbup2=acts["gbup2"], gain1=gain1, gain2=gain2)
    rows, d = acts["gy"].shape
    ff = w_up.shape[1]
    dec_d, dec_total = dec["at"].shape
    dec_ff = dec["u"].shape[1]
    chunks = make_chunks()
    n = len(chunks)
    groups = make_groups(chunks)
    plan = make_plan(chunks, groups)

    dims = {
        ENC_QKV: (d, 3 * d), ENC_OUT: (d, d), ENC_UP: (d, ff), ENC_DOWN: (ff, d),
        EMBED: (d, dec_d), DEC_QKV: (dec_d, 3 * dec_d), DEC_OUT: (dec_d, dec_d),
        DEC_UP: (dec_d, dec_ff), DEC_DOWN: (dec_ff, dec_d),
    }
    big = [
        shape(dims[k][1], dims[k][0] // 16) if k == DEC_DOWN else shape(dims[k][0] // 16, dims[k][1])
        for k in range(9)
    ]
    outs = dict(
        out_small=shape(SMALL_ROWS, d, F32),
        decoded_got=jax.ShapeDtypeStruct((SAMP_MB, PATCHES // 2, dec_d), BF16),
        gx=shape(rows, d),
        gx_got=shape(rows, d // 2),
    )
    single = finish_buffers(chunks, rows, d, ff, dec_total, dec_d)
    left = (4, 2, 2)
    lists = [[], [], [], [], []]
    for k in chunks:
        block = (k.rows, k.width)
        lists[0].append((left + block, BF16))
        if k.turned:
            lists[1].append((left + block, BF16))
        for stage in range(3):
            rest = [left[axis] for axis in (Z, Y, X) if axis not in k.order[: stage + 1]]
            count = 3 if k.order[stage] == Z else 1
            lists[2 + stage].append(((count, *rest, *block), BF16))
    blocks = sorted({(k.rows, k.width) for k in chunks})
    slots = [3 if block in ((32, 256), (48, 384)) else 2 if block[0] == 128 else 1 for block in blocks]
    lists.append([(left + block, BF16) for block, m in zip(blocks, slots) for _ in range(m)])
    semaphores = dict(
        load_sem=(LOADS,), send_sem=(n, 9), recv_sem=(n, 9), small_sem=(2, 6), swap_sem=(4,)
    )

    def kernel(*refs):
        refs = list(refs)

        def take(count):
            taken = refs[:count]
            del refs[:count]
            return taken

        names = list(given) + list(outs)
        r = Names(names, take(len(names)))
        r.out = take(9)
        r.__dict__.update(zip(single, take(len(single))))
        r.acc = take(n)
        r.got = dict(zip([c for c, k in enumerate(chunks) if k.turned], take(len(lists[1]))))
        r.recv = [take(n) for _ in range(3)]
        r.stage = {block: take(m) for block, m in zip(blocks, slots)}
        r.__dict__.update(zip(semaphores, take(len(semaphores))))
        finish_kernel(chunks, groups, plan, r)

    flat = list(single.values()) + [b for group in lists for b in group]
    results = pl.pallas_call(
        kernel,
        out_shape=list(outs.values()) + big,
        in_specs=[in_hbm()] * n_hbm + in_vmem(len(given) - n_hbm),
        out_specs=in_vmem(len(outs) + 9),
        scratch_shapes=[pltpu.VMEM(*b) for b in flat]
        + [pltpu.SemaphoreType.DMA(v) for v in semaphores.values()],
        compiler_params=pltpu.CompilerParams(
            collective_id=1, has_side_effects=True, vmem_limit_bytes=FINISH_VMEM
        ),
        name="finish",
    )(*given.values())
    return write_outputs(results, given["decoded"], dims)


FINISH_VMEM = 62 * 2**20


def write_kernel(small, decoded_got, gx_own, gx_got, *refs):
    big, decoded_own = refs[:9], refs[9]
    decoded, gx, *totals = refs[10:]
    s = lax.axis_index("section")
    half = decoded.shape[1]
    samples, rows, columns = decoded_own.shape[0], gx_own.shape[0], gx.shape[1]
    own = decoded_own[:, pl.ds(pl.multiple_of(s * half, half), half), :]
    for side, part in ((s, own), (1 - s, decoded_got[...])):
        decoded[pl.ds(side * samples, samples)] = part
    own = gx_own[:, pl.ds(pl.multiple_of(s * columns, 128), columns)]
    for side, part in ((s, own), (1 - s, gx_got[...])):
        gx[pl.ds(pl.multiple_of(side * rows, rows), rows), :] = part
    d = lax.axis_index("dp")
    wide, narrow = small.shape[1], big[DEC_OUT].shape[1]

    def piece(out, line, lanes, position):
        size = out.shape[0]
        value = small[pl.ds(line, 1), :lanes]
        value = pltpu.roll(value, lax.rem(lanes - position * size, lanes), 1)
        out[...] = value[:, :size].reshape(size)

    def matrix(out, name):
        value = big[name][...].astype(F32)
        out[...] = jnp.transpose(value) if name == DEC_DOWN else value

    def block(outs, first_row, bup_row, lanes, names):
        for i, out in zip((0, 1, None, None, 2, 3, 4, None, None, None, 5), outs):
            if i is not None:
                piece(out, first_row + i, lanes, d)
        piece(outs[8], bup_row + d // 4, lanes, d % 4)
        for at, name in zip((2, 3, 7, 9), names):
            matrix(outs[at], name)

    block(totals[:11], 0, ROW_BUP, wide, (ENC_QKV, ENC_OUT, ENC_UP, ENC_DOWN))
    matrix(totals[11], EMBED)
    piece(totals[12], ROW_DEC + 7, narrow, d)
    piece(totals[13], ROW_DEC + 6, narrow, d)
    block(totals[14:], ROW_DEC, ROW_DEC_BUP, narrow, (DEC_QKV, DEC_OUT, DEC_UP, DEC_DOWN))


def write_outputs(results, decoded_own, dims):
    def vector(size):
        return jax.ShapeDtypeStruct((size // 16,), F32)

    def matrix(name):
        return shape(dims[name][0] // 16, dims[name][1], F32)

    def block(qkv, out, up, down):
        d, ff = dims[up]
        return [
            vector(d), vector(d), matrix(qkv), matrix(out), vector(d), vector(d), vector(d),
            matrix(up), vector(ff), matrix(down), vector(d),
        ]

    samples, half, width = results[1].shape
    rows, columns = results[3].shape
    out_shape = [
        jax.ShapeDtypeStruct((2 * samples, half, width), BF16),
        shape(2 * rows, columns),
        *block(ENC_QKV, ENC_OUT, ENC_UP, ENC_DOWN),
        matrix(EMBED),
        vector(width),
        vector(width),
        *block(DEC_QKV, DEC_OUT, DEC_UP, DEC_DOWN),
    ]
    return tuple(
        pl.pallas_call(
            write_kernel,
            out_shape=out_shape,
            in_specs=in_vmem(len(results) + 1),
            out_specs=in_vmem(len(out_shape)),
            compiler_params=pltpu.CompilerParams(vmem_limit_bytes=KERNEL_VMEM),
            name="write_outputs",
        )(*results, decoded_own)
    )


def reduce_plain(arrays, section_index):
    first = section_index == 0
    results = []
    for a in arrays:
        half = a.shape[1] // 2
        keep = lax.dynamic_slice_in_dim(a, section_index * half, half, 1)
        give = lax.dynamic_slice_in_dim(a, (1 - section_index) * half, half, 1)
        got = swapped(give, "section", 0)
        chip = (keep.astype(jnp.float32) + got.astype(jnp.float32)).astype(jnp.bfloat16)
        mine = lax.psum_scatter(chip, "dp", scatter_dimension=0, tiled=True)
        other = swapped(mine, "section", 0)
        whole = jnp.concatenate(
            [jnp.where(first, mine, other), jnp.where(first, other, mine)], axis=1
        )
        results.append(whole.astype(jnp.float32))
    return results


def finish_plain(acts, section_index):
    x, gy, seg_saved, enc, dec = acts["x"], acts["gy"], acts["saved"], acts["enc"], acts["dec"]
    gx, gf1, ga1, gqkv1, small1, gbup1 = encoder_backward(x, gy, seg_saved, enc["params"])
    small2, gbup2 = acts["small2"], acts["gbup2"]
    grads = (
        small1[0], small1[1], mm(enc["at"], gqkv1).astype(BF16), mm(enc["ot"], ga1).astype(BF16), small1[2],
        small1[3], small1[4], mm(enc["ct"], gf1).astype(BF16), gbup1[0], mm(enc["ut"], gy).astype(BF16),
        small1[5],
        weight_grad(acts["y"], acts["geb"]), small2[7], small2[6],
        small2[0], small2[1], mm(dec["at"], dec["gqkv"]).astype(BF16),
        mm(dec["ot"], dec["ga"]).astype(BF16), small2[2], small2[3], small2[4],
        mm(dec["ct"], dec["gf"]).astype(BF16), gbup2[0],
        jnp.transpose(mm(dec["gt"], dec["u"])).astype(BF16), small2[5],
    )
    groups = lax.axis_size("dp")
    big = reduce_plain([g for g in grads if g.ndim == 2], section_index)
    flat = jnp.concatenate([g.reshape(groups, -1) for g in grads if g.ndim == 1], axis=1)
    line = lax.psum_scatter(flat, ("dp"), scatter_dimension=0, tiled=True)
    line = lax.psum(line, "section")[0]
    totals, at = [], 0
    for g in grads:
        if g.ndim == 2:
            totals.append(big.pop(0))
        else:
            size = g.shape[0] // groups
            totals.append(line[at : at + size])
            at += size
    decoded = acts["decoded"].reshape(SAMP_MB, PATCHES, -1)
    first = section_index == 0

    def halves(whole):
        half = whole.shape[1] // 2
        keep = lax.dynamic_slice_in_dim(whole, section_index * half, half, 1)
        give = lax.dynamic_slice_in_dim(whole, (1 - section_index) * half, half, 1)
        got = swapped(give, "section", 0)
        return jnp.concatenate([jnp.where(first, keep, got), jnp.where(first, got, keep)])

    return (halves(decoded), halves(gx), *totals)


def shards(
    patches,
    segment_ids,
    patch_order,
    encoder_gain1,
    encoder_bias1,
    encoder_qkv,
    encoder_out,
    encoder_out_bias,
    encoder_gain2,
    encoder_bias2,
    encoder_up,
    encoder_up_bias,
    encoder_down,
    encoder_down_bias,
    embed_weight,
    embed_bias,
    mask_token,
    decoder_gain1,
    decoder_bias1,
    decoder_qkv,
    decoder_out,
    decoder_out_bias,
    decoder_gain2,
    decoder_bias2,
    decoder_up,
    decoder_up_bias,
    decoder_down,
    decoder_down_bias,
    cotangent,
):
    enc_params = (
        encoder_gain1,
        encoder_bias1,
        encoder_qkv,
        encoder_out,
        encoder_out_bias,
        encoder_gain2,
        encoder_bias2,
        encoder_up,
        encoder_up_bias,
        encoder_down,
        encoder_down_bias,
    )
    embed_params = (embed_weight, embed_bias, mask_token)
    dec_params = (
        decoder_gain1,
        decoder_bias1,
        decoder_qkv,
        decoder_out,
        decoder_out_bias,
        decoder_gain2,
        decoder_bias2,
        decoder_up,
        decoder_up_bias,
        decoder_down,
        decoder_down_bias,
    )
    section_index = lax.axis_index("section")
    y, at1, qkv, e, rl, o1, ot1, n2, s2, ct1, ut1, slope = encoder_forward(
        patches, segment_ids, enc_params
    )
    g = cotangent.reshape(-1, DECODER_WIDTH)
    decoded, at2, ot2, ct2, gt2, u2, gf2, ga2, gqkv2, geb, gy, small2, gbup2 = decoder_both(
        y, segment_ids, patch_order, g, embed_params, dec_params
    )
    acts = dict(
        x=patches,
        y=y,
        gy=gy,
        geb=geb,
        decoded=decoded,
        small2=small2,
        gbup2=gbup2,
        saved=(qkv, e, rl, o1, n2, s2, slope),
        enc=dict(at=at1, ot=ot1, ct=ct1, ut=ut1, params=enc_params),
        dec=dict(at=at2, ot=ot2, ct=ct2, gt=gt2, u=u2, gf=gf2, ga=ga2, gqkv=gqkv2),
    )
    if lax.axis_size("dp") == 16:
        return finish(acts)
    return finish_plain(acts, section_index)


def solution(mesh):
    in_specs = (
        P("dp", None),
        P("dp", None),
        P("dp", None),
        P(),
        P(),
        P(),
        P(),
        P(),
        P(),
        P(),
        P(),
        P(),
        P(),
        P(),
        P(),
        P(),
        P(),
        P(),
        P(),
        P(),
        P(),
        P(),
        P(),
        P(),
        P(),
        P(),
        P(),
        P(),
        P("dp", None, None),
    )
    out_specs = (
        P("dp", "section", None),
        P("dp", "section"),
        P("dp"),
        P("dp"),
        P("dp", None),
        P("dp", None),
        P("dp"),
        P("dp"),
        P("dp"),
        P("dp", None),
        P("dp"),
        P("dp", None),
        P("dp"),
        P("dp", None),
        P("dp"),
        P("dp"),
        P("dp"),
        P("dp"),
        P("dp", None),
        P("dp", None),
        P("dp"),
        P("dp"),
        P("dp"),
        P("dp", None),
        P("dp"),
        P("dp", None),
        P("dp"),
    )
    return jax.shard_map(shards, mesh=mesh, in_specs=in_specs, out_specs=out_specs, check_vma=False)
```

```python
import functools
import math

import jax
import jax.numpy as jnp
import numpy as np
from jax import lax
from jax.experimental import pallas as pl
from jax.experimental.pallas import tpu as pltpu
from jax.sharding import PartitionSpec as P

H_ENC = 12
DECODER_WIDTH = 512
H_DEC = 16
PATCHES = 128
SAMP_MB = 12


EPSILON = 1e-06
MASKED = -1e30


def swapped(block, axis, apart):
    count = lax.axis_size(axis)
    route = []
    for low in range(count):
        high = low | 1 << apart
        if high != low and high < count:
            route += [(low, high), (high, low)]
    return lax.ppermute(block, axis, route)


def positions(count, features):
    column = np.arange(features)
    rate = np.exp(-math.log(10000.0) * (2 * (column // 2)) / features)
    angles = np.arange(count)[:, None] * rate[None, :]
    return np.where(column % 2 == 0, np.sin(angles), np.cos(angles)).astype(np.float32)


def weight_grad(left_side, grads):
    return lax.dot_general(
        left_side, grads, (((0,), (0,)), ((), ())), preferred_element_type=jnp.float32
    ).astype(jnp.bfloat16)


BF16 = jnp.bfloat16
F32 = jnp.float32


def mm(left, right):
    return lax.dot_general(left, right, (((1,), (0,)), ((), ())), preferred_element_type=F32)


def mm_nt(left, right):
    return lax.dot_general(left, right, (((1,), (1,)), ((), ())), preferred_element_type=F32)


def mm_tn(left, right):
    return lax.dot_general(left, right, (((0,), (0,)), ((), ())), preferred_element_type=F32)


def normalise(x):
    center = x - jnp.mean(x, axis=-1, keepdims=True)
    scale = lax.rsqrt(jnp.mean(center * center, axis=-1, keepdims=True) + EPSILON)
    return center * scale, scale


def normalise_back(grad, n, scale, gain):
    gn = grad * gain
    mean_gn = jnp.mean(gn, axis=-1, keepdims=True)
    mean_gnn = jnp.mean(gn * n, axis=-1, keepdims=True)
    return (gn - mean_gn - n * mean_gnn) * scale


def rows_sum(x):
    return jnp.sum(x, axis=0, keepdims=True)


def gelu_both(f):
    c0, c1 = math.sqrt(2.0 / math.pi), 0.044715
    square = f * f
    half = 0.5 + 0.5 * jnp.tanh(f * (c0 + (c0 * c1) * square))
    u = f * half
    return u, half + u * (1.0 - half) * (2.0 * c0 + (6.0 * c0 * c1) * square)


def lane_masks(head_size):
    lane = lax.broadcasted_iota(jnp.int32, (1, 128), 1)
    return [
        jnp.where((lane >= h * head_size) & (lane < (h + 1) * head_size), 1.0, 0.0).astype(BF16)
        for h in range(128 // head_size)
    ]


def stacked(x, masks):
    return jnp.concatenate([x * m for m in masks], axis=0)


def stacked_ones(x, masks, value):
    return jnp.concatenate(
        [jnp.broadcast_to(m * jnp.asarray(value, BF16), x.shape) for m in masks], axis=0
    )


def attention_forward(qkv_ref, o_ref, e_ref, rl_ref, rows, tokens, features, head_size, allowed):
    masks = lane_masks(head_size)
    per_group = len(masks)
    factor = head_size ** (-0.5) * math.log2(math.e)
    for g in range(features // 128):
        q, k, v = (qkv_ref[rows, j * features + g * 128 : j * features + (g + 1) * 128] for j in range(3))
        scores = mm_nt(q, stacked(k, masks))
        parts = []
        for h in range(per_group):
            part = scores[:, h * tokens : (h + 1) * tokens]
            if allowed is not None:
                part = jnp.where(allowed, part, MASKED)
            top = jnp.max(part, axis=-1, keepdims=True)
            parts.append(jnp.exp2((part - top) * factor).astype(BF16))
        e = jnp.concatenate(parts, axis=1)
        width = per_group * tokens
        e_ref[rows, g * width : (g + 1) * width] = e
        both = mm(e, jnp.concatenate([stacked(v, masks), stacked_ones(v, masks, 1.0)], axis=1))
        rl = 1.0 / both[:, 128:]
        rl_ref[rows, g * 128 : (g + 1) * 128] = rl
        o_ref[rows, g * 128 : (g + 1) * 128] = (both[:, :128] * rl).astype(BF16)


def attention_backward_group(q, k, v, e, go, o, rl, head_size):
    masks = lane_masks(head_size)
    per_group, tokens = len(masks), q.shape[0]
    scaling = head_size ** (-0.5)
    go = go.astype(F32) * rl
    go_low = go.astype(BF16)
    inner = (go * o.astype(F32)).astype(BF16)
    left = jnp.concatenate([go_low, inner], axis=1)
    right = jnp.concatenate([stacked(v, masks), stacked_ones(v, masks, -1.0)], axis=1)
    gs = (e.astype(F32) * mm_nt(left, right)).astype(BF16)

    def diagonal(wide):
        return jnp.concatenate(
            [
                wide[h * head_size : (h + 1) * head_size, h * tokens : (h + 1) * tokens]
                for h in range(per_group)
            ],
            axis=0,
        )

    gq = mm(gs, stacked(k, masks)) * scaling
    gk = jnp.transpose(diagonal(mm_tn(q, gs)) * scaling)
    gv = jnp.transpose(diagonal(mm_tn(go_low, e)))
    return gq.astype(BF16), gk.astype(BF16), gv.astype(BF16)


def attention_backward(
    qkv_ref, go_ref, o_ref, e_ref, rl_ref, gqkv_ref, rows, tokens, features, head_size
):
    width = 128 // head_size * tokens
    for g in range(features // 128):
        at = slice(g * 128, (g + 1) * 128)
        spots = [slice(j * features + g * 128, j * features + (g + 1) * 128) for j in range(3)]
        q, k, v = (qkv_ref[rows, spot] for spot in spots)
        e = e_ref[rows, g * width : (g + 1) * width]
        grads = attention_backward_group(
            q, k, v, e, go_ref[rows, at], o_ref[rows, at], rl_ref[rows, at], head_size
        )
        for spot, grad in zip(spots, grads):
            gqkv_ref[rows, spot] = grad


def feed_forward(c_ref, up_ref, bup_ref, u_ref, slope_ref, tile, ut_ref=None):
    for t in range(up_ref.shape[1] // tile):
        at = slice(t * tile, (t + 1) * tile)
        f = mm(c_ref[...], up_ref[:, at]) + bup_ref[at].reshape(1, tile)
        u, slope = gelu_both(f)
        u = u.astype(BF16)
        u_ref[:, at] = u
        slope_ref[:, at] = slope.astype(BF16)
        if ut_ref is not None:
            ut_ref[at, :] = jnp.transpose(u)


def feed_forward_back(gm_ref, down_ref, slope_ref, gf_ref, gbup_ref, tile):
    for t in range(down_ref.shape[0] // tile):
        at = slice(t * tile, (t + 1) * tile)
        gu = mm_nt(gm_ref[...], down_ref[at, :])
        gf = (gu * slope_ref[:, at].astype(F32)).astype(BF16)
        gf_ref[:, at] = gf
        gbup_ref[:, at] += rows_sum(gf.astype(F32))


def row(ref):
    return ref[...].reshape(1, -1)


def segment_mask(seg_ref, section):
    seg = seg_ref[pl.ds(section, 1), :].astype(F32)
    rows = seg.shape[1]
    column = jnp.transpose(jnp.broadcast_to(seg, (128, rows)))
    return jnp.concatenate([column] * (rows // 128), axis=1) == seg


class Writer:
    def __init__(self, semaphores):
        self.semaphores, self.copies = semaphores, []

    def start(self, source, target):
        copy = pltpu.make_async_copy(source, target, self.semaphores.at[len(self.copies)])
        copy.start()
        self.copies.append(copy)

    def wait(self):
        for copy in self.copies:
            copy.wait()


def encoder_forward_kernel(
    x_ref, seg_ref,
    gain1, bias1, w_qkv, w_out, b_out, gain2, bias2, w_up, b_up, w_down, b_down,
    *refs,
):
    outs, scratch = refs[:12], refs[12:24]
    y_ref, at_ref, qkv_ref, e_ref, rl_ref, o_ref, ot_ref, n2_ref, s2_ref, ct_ref, ut_ref, slope_ref = scratch
    h_ref, c_ref, u_ref, qkv_v, out_v, up_v, down_v, sem, out_sem = refs[24:]
    target = {id(v): o for v, o in zip(scratch, outs)}
    writer = Writer(out_sem)

    def write(*done):
        for v in done:
            writer.start(v, target[id(v)])

    tokens, features = y_ref.shape
    pairs = ((w_qkv, qkv_v), (w_out, out_v), (w_up, up_v), (w_down, down_v))
    loads = [pltpu.make_async_copy(w, v, sem.at[i]) for i, (w, v) in enumerate(pairs)]
    for load in loads:
        load.start()
    section = lax.axis_index("section")
    x = x_ref[pl.ds(pl.multiple_of(section * tokens, tokens), tokens), :].astype(F32)
    n1, _ = normalise(x)
    a = (n1 * row(gain1) + row(bias1)).astype(BF16)
    at_ref[...] = jnp.transpose(a)
    allowed = segment_mask(seg_ref, section)
    loads[0].wait()
    qkv_ref[...] = mm(a, qkv_v[...]).astype(BF16)
    write(at_ref, qkv_ref)
    attention_forward(
        qkv_ref, o_ref, e_ref, rl_ref, slice(None), tokens, features, features // H_ENC, allowed
    )
    ot_ref[...] = jnp.transpose(o_ref[...])
    write(e_ref, rl_ref, o_ref, ot_ref)
    loads[1].wait()
    h_ref[...] = x + (mm(o_ref[...], out_v[...]) + row(b_out))
    n2, s2 = normalise(h_ref[...])
    n2_ref[...] = n2
    s2_ref[...] = s2
    c_ref[...] = (n2 * row(gain2) + row(bias2)).astype(BF16)
    ct_ref[...] = jnp.transpose(c_ref[...])
    write(n2_ref, s2_ref, ct_ref)
    loads[2].wait()
    feed_forward(c_ref, up_v, b_up, u_ref, slope_ref, 512, ut_ref)
    write(ut_ref, slope_ref)
    loads[3].wait()
    y_ref[...] = (h_ref[...] + (mm(u_ref[...], down_v[...]) + row(b_down))).astype(BF16)
    write(y_ref)
    writer.wait()


def encoder_backward_kernel(
    x_ref, gy_ref, qkv_ref, e_ref, rl_ref, o_ref, n2_ref, s2_ref, slope_ref,
    gain1, w_qkv, w_out, gain2, w_up, w_down,
    gx_ref, gf_ref, ga_ref, gqkv_ref, small_ref, gbup_ref,
    gh_ref, go_ref,
):
    tokens, features = gy_ref.shape
    section = lax.axis_index("section")
    x = x_ref[pl.ds(pl.multiple_of(section * tokens, tokens), tokens), :].astype(F32)
    gbup_ref[...] = jnp.zeros_like(gbup_ref)
    feed_forward_back(gy_ref, w_down, slope_ref, gf_ref, gbup_ref, 512)
    gc = mm_nt(gf_ref[...], w_up[...])
    g = gy_ref[...].astype(F32)
    n2 = n2_ref[...]
    gh = g + normalise_back(gc, n2, s2_ref[...], row(gain2))
    gh_ref[...] = gh
    ga_ref[...] = gh.astype(BF16)
    small_ref[2:3, :] = rows_sum(gh)
    small_ref[3:4, :] = rows_sum(gc * n2)
    small_ref[4:5, :] = rows_sum(gc)
    small_ref[5:6, :] = rows_sum(g)
    go_ref[...] = mm_nt(ga_ref[...], w_out[...]).astype(BF16)
    attention_backward(
        qkv_ref, go_ref, o_ref, e_ref, rl_ref, gqkv_ref, slice(None), tokens, features,
        features // H_ENC,
    )
    gn = mm_nt(gqkv_ref[...], w_qkv[...])
    n1, s1 = normalise(x)
    small_ref[0:1, :] = rows_sum(gn * n1)
    small_ref[1:2, :] = rows_sum(gn)
    gx_ref[...] = (gh_ref[...] + normalise_back(gn, n1, s1, row(gain1))).astype(BF16)


def split_low(x):
    high = x.astype(BF16)
    return high, (x - high.astype(F32)).astype(BF16)


def place_slots(order_ref, seg, section, hot_ref, place_ref, empty_ref):
    packed = seg.shape[1]
    sample = lax.broadcasted_iota(jnp.int32, (16, packed), 0).astype(F32)
    starts = jnp.sum(jnp.where(seg < sample, 1.0, 0.0), axis=1, keepdims=True)
    counts = jnp.sum(jnp.where(seg == sample, 1.0, 0.0), axis=1, keepdims=True)
    line = lax.broadcasted_iota(jnp.int32, (PATCHES, PATCHES), 0).astype(F32)
    line_low = line.astype(BF16)
    lane_low = lax.broadcasted_iota(jnp.int32, (8, PATCHES), 1).astype(F32).astype(BF16)
    column = lax.broadcasted_iota(jnp.int32, (PATCHES, packed), 1).astype(F32)
    packed_line = lax.broadcasted_iota(jnp.int32, (packed, PATCHES), 0).astype(F32)
    for j in range(SAMP_MB):
        at = slice(j * PATCHES, (j + 1) * PATCHES)
        order = order_ref[pl.ds(section * SAMP_MB + j, 1), :].astype(F32)
        hit = jnp.where(order == line, 1.0, 0.0).astype(BF16)
        start, count = starts[j : j + 1, :], counts[j : j + 1, :]
        down, across = mm(hit, line_low), mm_nt(lane_low, hit)[:1, :]
        down = jnp.where(down < count, start + down, -1.0)
        across = jnp.where(across < count, start + across, -1.0)
        wide = jnp.concatenate([down] * (packed // PATCHES), axis=1)
        hot_ref[at, :] = jnp.where(column == wide, 1.0, 0.0).astype(BF16)
        place_ref[:, at] = jnp.where(packed_line == across, 1.0, 0.0).astype(BF16)
        empty_ref[at, :] = jnp.where(down < 0.0, 1.0, 0.0)


def decoder_kernel(
    y_ref, seg_ref, order_ref, pos_ref, g_hbm,
    w_embed_hbm, b_embed, mask_token,
    gain1, bias1, w_qkv_hbm, w_out_hbm, b_out, gain2, bias2, w_up_hbm, b_up, w_down_hbm, b_down,
    *refs,
):
    hbm, (geb_ref, gy_ref, small_ref, gbup_ref) = refs[:9], refs[9:13]
    buffers = refs[13:22]
    out_ref, at_ref, ot_ref, ct_ref, gt_ref, u_ref, gf_ref, ga_ref, gqkv_ref = buffers
    (
        e2_ref, z_ref, s1_ref, e_ref, rl_ref, h_ref, s2_ref, go_ref, ge_ref, o_ref, c_ref, qkv_ref,
        slope_ref, g_all, hot_ref, place_ref, empty_ref, w_embed, w_qkv, w_out, w_up, w_down,
        w_sem, out_sem,
    ) = refs[22:]
    packed = y_ref.shape[0]
    rows, features = z_ref.shape
    samples = rows // PATCHES
    head_size = features // H_DEC
    total = g_all.shape[0]
    section = lax.axis_index("section")
    mine = pl.ds(pl.multiple_of(section * total, total), total)
    pairs = (
        (w_embed_hbm, w_embed), (w_qkv_hbm, w_qkv), (w_out_hbm, w_out), (w_up_hbm, w_up),
        (w_down_hbm, w_down), (g_hbm.at[mine, :], g_all),
    )
    loads = [pltpu.make_async_copy(a, b, w_sem.at[i]) for i, (a, b) in enumerate(pairs)]
    for load in loads:
        load.start()

    def write(at, *which):
        copies = []
        for i in which:
            target = hbm[i].at[:, at] if 1 <= i <= 4 else hbm[i].at[at, :]
            copies.append(pltpu.make_async_copy(buffers[i], target, out_sem.at[i]))
            copies[-1].start()
        return copies

    small_ref[...] = jnp.zeros_like(small_ref)
    gbup_ref[...] = jnp.zeros_like(gbup_ref)
    ge_ref[...] = jnp.zeros_like(ge_ref)
    seg = seg_ref[pl.ds(section, 1), :].astype(F32)
    place_slots(order_ref, seg, section, hot_ref, place_ref, empty_ref)
    loads[0].wait()
    high, low = split_low(mm(y_ref[...], w_embed[...]) + row(b_embed))
    e2_ref[:packed, :] = high
    e2_ref[packed:, :] = low
    for load in loads[1:]:
        load.wait()

    def one_step(step, carry):
        here = pl.ds(pl.multiple_of(step * rows, rows), rows)
        one_hot = hot_ref[here, :]
        empty = jnp.concatenate([empty_ref[here, :]] * (features // 128), axis=1)
        twice = jnp.concatenate([one_hot, one_hot], axis=1)
        z = mm(twice, e2_ref[...]) + empty * row(mask_token)
        z = z + jnp.concatenate([pos_ref[...]] * samples, axis=0)
        n1, s1 = normalise(z)
        z_ref[...] = z
        s1_ref[...] = s1
        a = (n1 * row(gain1) + row(bias1)).astype(BF16)
        at_ref[...] = jnp.transpose(a)
        writing = write(here, 1)
        qkv_ref[...] = mm(a, w_qkv[...]).astype(BF16)

        def forward(b, carry):
            at = pl.ds(pl.multiple_of(b * PATCHES, PATCHES), PATCHES)
            attention_forward(qkv_ref, o_ref, e_ref, rl_ref, at, PATCHES, features, head_size, None)
            return carry

        lax.fori_loop(0, samples, forward, 0, unroll=2)
        ot_ref[...] = jnp.transpose(o_ref[...])
        h_ref[...] = z_ref[...] + (mm(o_ref[...], w_out[...]) + row(b_out))
        n2, s2 = normalise(h_ref[...])
        s2_ref[...] = s2
        c_ref[...] = (n2 * row(gain2) + row(bias2)).astype(BF16)
        ct_ref[...] = jnp.transpose(c_ref[...])
        feed_forward(c_ref, w_up, b_up, u_ref, slope_ref, 512)
        writing += write(here, 2, 3, 5)
        out_ref[...] = (h_ref[...] + (mm(u_ref[...], w_down[...]) + row(b_down))).astype(BF16)

        g_ref = g_all.at[here, :]
        gt_ref[...] = jnp.transpose(g_ref[...])
        feed_forward_back(g_ref, w_down, slope_ref, gf_ref, gbup_ref, 512)
        writing += write(here, 0, 4, 6)
        gc = mm_nt(gf_ref[...], w_up[...])
        g = g_ref[...].astype(F32)
        h = h_ref[...]
        n2 = (h - jnp.mean(h, axis=-1, keepdims=True)) * s2_ref[...]
        gh = g + normalise_back(gc, n2, s2_ref[...], row(gain2))
        small_ref[2:3, :] += rows_sum(gh)
        small_ref[3:4, :] += rows_sum(gc * n2)
        small_ref[4:5, :] += rows_sum(gc)
        small_ref[5:6, :] += rows_sum(g)
        h_ref[...] = gh
        ga_ref[...] = gh.astype(BF16)
        go_ref[...] = mm_nt(ga_ref[...], w_out[...]).astype(BF16)
        writing += write(here, 7)

        def backward(b, carry):
            at = pl.ds(pl.multiple_of(b * PATCHES, PATCHES), PATCHES)
            attention_backward(
                qkv_ref, go_ref, o_ref, e_ref, rl_ref, gqkv_ref, at, PATCHES, features, head_size
            )
            return carry

        lax.fori_loop(0, samples, backward, 0, unroll=2)
        writing += write(here, 8)
        gn = mm_nt(gqkv_ref[...], w_qkv[...])
        z = z_ref[...]
        n1 = (z - jnp.mean(z, axis=-1, keepdims=True)) * s1_ref[...]
        gz = h_ref[...] + normalise_back(gn, n1, s1_ref[...], row(gain1))
        small_ref[0:1, :] += rows_sum(gn * n1)
        small_ref[1:2, :] += rows_sum(gn)
        small_ref[6:7, :] += rows_sum(gz * empty)
        ge_ref[...] += mm(place_ref[:, here], gz.astype(BF16))
        for copy in writing:
            copy.wait()
        return carry

    lax.fori_loop(0, total // rows, one_step, 0)
    ge = ge_ref[...]
    small_ref[7:8, :] = rows_sum(ge)
    geb_ref[...] = ge.astype(BF16)
    gy_ref[...] = mm_nt(geb_ref[...], w_embed[...]).astype(BF16)


def in_vmem(count):
    return [pl.BlockSpec(memory_space=pltpu.VMEM)] * count


def in_hbm():
    return pl.BlockSpec(memory_space=pl.ANY)


def shape(rows, columns, dtype=BF16):
    return jax.ShapeDtypeStruct((rows, columns), dtype)


KERNEL_VMEM = 60 * 2**20


def encoder_forward(x, segments, params):
    rows, d = x.shape[0] // 2, x.shape[1]
    ff = params[7].shape[1]
    outs = [
        (rows, d, BF16),
        (d, rows, BF16),
        (rows, 3 * d, BF16),
        (rows, H_ENC * rows, BF16),
        (rows, d, F32),
        (rows, d, BF16),
        (d, rows, BF16),
        (rows, d, F32),
        (rows, 1, F32),
        (d, rows, BF16),
        (ff, rows, BF16),
        (rows, ff, BF16),
    ]
    more = [(rows, d, F32), (rows, d, BF16), (rows, ff, BF16)]
    args = [x, segments, *params]
    matrices = [w for w in params if w.dtype == BF16]
    return pl.pallas_call(
        encoder_forward_kernel,
        out_shape=[shape(*o) for o in outs],
        in_specs=in_vmem(2) + [in_hbm() if w.dtype == BF16 else in_vmem(1)[0] for w in params],
        out_specs=[in_hbm()] * len(outs),
        scratch_shapes=[pltpu.VMEM((r, w), t) for r, w, t in outs + more]
        + [pltpu.VMEM(w.shape, BF16) for w in matrices]
        + [pltpu.SemaphoreType.DMA((len(matrices),)), pltpu.SemaphoreType.DMA((len(outs),))],
        compiler_params=pltpu.CompilerParams(vmem_limit_bytes=KERNEL_VMEM),
        name="encoder_forward",
    )(*args)


def encoder_backward(x, gy, saved, params):
    gain1, _, w_qkv, w_out, _, gain2, _, w_up, _, w_down, _ = params
    rows, d = gy.shape
    ff = w_up.shape[1]
    outs = [
        shape(rows, d),
        shape(rows, ff),
        shape(rows, d),
        shape(rows, 3 * d),
        shape(8, d, F32),
        shape(1, ff, F32),
    ]
    args = [x, gy, *saved, gain1, w_qkv, w_out, gain2, w_up, w_down]
    return pl.pallas_call(
        encoder_backward_kernel,
        out_shape=outs,
        in_specs=in_vmem(len(args)),
        out_specs=in_vmem(len(outs)),
        scratch_shapes=[pltpu.VMEM((rows, d), F32), pltpu.VMEM((rows, d), BF16)],
        compiler_params=pltpu.CompilerParams(vmem_limit_bytes=KERNEL_VMEM),
        name="encoder_backward",
    )(*args)


def decoder_both(y, segments, orders, g, embed_params, params):
    packed, d_enc = y.shape
    total, d = g.shape[0] // 2, g.shape[1]
    rows = 6 * PATCHES
    ff = params[7].shape[1]
    args = [y, segments, orders, positions(PATCHES, d), g, *embed_params, *params]
    in_specs = in_vmem(4) + [in_hbm()]
    in_specs += [in_hbm() if x.dtype == BF16 else in_vmem(1)[0] for x in args[5:]]
    wide = [ff, ff, d, 3 * d]
    outs = [shape(total, d)] + [shape(d, total)] * 4 + [shape(total, w) for w in wide]
    buffers = [(rows, d, BF16)] + [(d, rows, BF16)] * 4 + [(rows, w, BF16) for w in wide]
    last = [shape(packed, d), shape(packed, d_enc), shape(8, d, F32), shape(1, ff, F32)]
    scratch = [
        (2 * packed, d, BF16),
        (rows, d, F32),
        (rows, 1, F32),
        (rows, H_DEC * PATCHES, BF16),
        (rows, d, F32),
        (rows, d, F32),
        (rows, 1, F32),
        (rows, d, BF16),
        (packed, d, F32),
        (rows, d, BF16),
        (rows, d, BF16),
        (rows, 3 * d, BF16),
        (rows, ff, BF16),
        (total, d, BF16),
        (total, packed, BF16),
        (packed, total, BF16),
        (total, 128, F32),
    ]
    matrices = [x for x in args[5:] if x.dtype == BF16]
    return pl.pallas_call(
        decoder_kernel,
        out_shape=outs + last,
        in_specs=in_specs,
        out_specs=[in_hbm()] * len(outs) + in_vmem(len(last)),
        scratch_shapes=[pltpu.VMEM((r, w), t) for r, w, t in buffers + scratch]
        + [pltpu.VMEM(x.shape, BF16) for x in matrices]
        + [pltpu.SemaphoreType.DMA((k,)) for k in (len(matrices) + 1, len(outs))],
        compiler_params=pltpu.CompilerParams(vmem_limit_bytes=KERNEL_VMEM),
        name="decoder_both",
    )(*args)


MESH = pl.DeviceIdType.MESH
ENC_QKV, ENC_OUT, ENC_UP, ENC_DOWN, EMBED, DEC_QKV, DEC_OUT, DEC_UP, DEC_DOWN = range(9)
GIVE, PAIR, FFN, LN2, GO, ATT, GN, LAST = range(10, 18)
SMALL = -1
ROW_BUP, ROW_DEC_BUP, ROW_DEC, SMALL_ROWS = 6, 10, 16, 24
Z, Y, X, CORE = range(4)
ORDERS = ((X, Y, Z), (Y, X, Z), (X, Z, Y), (Y, Z, X))


class Chunk:
    def __init__(self, name, half, offset, rows, width, first_row=None):
        self.name, self.half, self.offset, self.rows, self.width = name, half, offset, rows, width
        self.first_row, self.turned, self.order = first_row, name == DEC_DOWN, None
        self.decoder = name in (DEC_QKV, DEC_UP, DEC_OUT)

    def columns(self, side):
        return pl.ds(pl.multiple_of(side * self.half + self.offset, 128), self.width)

    def place(self, side):
        if self.turned:
            return (pl.ds(pl.multiple_of(side * self.half + self.offset, 128), self.rows), slice(None))
        if self.first_row is None:
            return (slice(None), self.columns(side))
        return (pl.ds(self.first_row, self.rows), self.columns(side))

    @property
    def bytes(self):
        return 32 * self.rows * self.width

    def loads(self, order):
        first, second, third = order
        if second == Z:
            return (self.bytes, self.bytes, self.bytes / 8)
        return (self.bytes, self.bytes / 2, self.bytes / 2)


def make_chunks():
    chunks = [Chunk(DEC_OUT, 256, 0, 32, 256), Chunk(DEC_QKV, 768, 0, 32, 768)]
    for q in range(2):
        chunks.append(Chunk(ENC_DOWN, 384, 0, 96, 384, 96 * q))
        chunks.append(Chunk(ENC_UP, 1536, 768 * q, 48, 768))
    chunks += [Chunk(ENC_OUT, 384, 0, 48, 384)]
    chunks += [Chunk(ENC_QKV, 1152, 0, 48, 768), Chunk(ENC_QKV, 1152, 768, 48, 384)]
    chunks += [Chunk(EMBED, 256, 0, 48, 256), Chunk(DEC_DOWN, 256, 0, 256, 128)]
    chunks += [Chunk(DEC_UP, 1024, o, 32, 512) for o in (0, 512)]
    for c, chunk in enumerate(chunks):
        chunk.order = ORDERS[c % 2]

    def busiest():
        load = [0.0, 0.0, 0.0]
        for chunk in chunks:
            for axis, size in zip(chunk.order, chunk.loads(chunk.order)):
                load[axis] += size
        return sorted(load, reverse=True)

    best, better = busiest(), True
    while better:
        better = False
        for chunk in chunks:
            for order in ORDERS:
                before, chunk.order = chunk.order, order
                if busiest() < best:
                    best, better = busiest(), True
                else:
                    chunk.order = before
    return chunks


def make_groups(chunks):
    return [[c] for c in range(len(chunks))]


def product_cost(k, count):
    if k.turned:
        return 6.0
    return k.rows * k.width * (1.1 / 8192 if k.decoder else 0.7 / 18432)


def tasks_in_order(chunks, groups):
    def gives(name):
        found = [(g, chunks[m[0]], len(m)) for g, m in enumerate(groups)]
        kind = PAIR if name == DEC_DOWN else GIVE
        return [(kind, g, product_cost(k, size)) for g, k, size in found if k.name == name]

    tasks = gives(DEC_OUT) + gives(DEC_QKV)
    tasks += [(FFN, t, 2.5) for t in range(4)]
    for pair in zip(gives(ENC_DOWN), gives(ENC_UP)):
        tasks += pair
    tasks += [(LN2, 0, 1.5), (GO, 0, 1.2)]
    tasks += [(ATT, g, 2.2) for g in range(6)]
    tasks += gives(ENC_OUT) + gives(ENC_QKV)
    tasks += [(GN, j, 1.2) for j in range(3)] + [(LAST, 0, 2.0)]
    return tasks + gives(EMBED) + gives(DEC_DOWN) + gives(DEC_UP)


def decoder_arrays(chunks):
    names = []
    for k in chunks:
        if (k.decoder or k.turned) and k.name not in names:
            names.append(k.name)
    return names


def make_plan(chunks, groups):
    tasks = tasks_in_order(chunks, groups)
    lhs = decoder_arrays(chunks)
    free = [0.0] * 4
    rate = [82e3, 82e3, 82e3, 500e3]
    pending, plan, now, owned = [], [], 2.0, set()

    def send(link, size, latency):
        begin = max(now, free[link])
        free[link] = begin + size / rate[link]
        return free[link] + latency

    def blocked(task):
        if task[0] not in (GIVE, PAIR):
            return False
        name = chunks[groups[task[1]][0]].name
        if name not in lhs[2:]:
            return False
        name = lhs[lhs.index(name) - 2]
        return any(chunks[m[0]].name == name and g not in owned for g, m in enumerate(groups))

    while tasks or pending:
        pending.sort()
        if pending and (pending[0][0] <= now or not tasks or blocked(tasks[0])):
            arrive, stage, c = pending.pop(0)
            now = max(now, arrive)
            plan.append((stage, c))
            if c == SMALL:
                now += 0.1
                if stage < 4:
                    pending.append((now + 2.0, stage + 1, c))
                continue
            members = groups[c] if stage == 1 else [c]
            k = chunks[members[0]]
            if stage == 1:
                owned.add(c)
                now += 0.6 if k.turned else product_cost(k, len(members)) + 0.2 * len(members)
            else:
                now += 0.25
            for c in members:
                k = chunks[c]
                if stage < 4:
                    axis = k.order[stage - 1]
                    latency = 2.0 if axis == Z else 1.5
                    arrive = send(axis, k.loads(k.order)[stage - 1], latency)
                    pending.append((arrive, stage + 1, c))
                elif stage == 4:
                    pending.append((send(CORE, k.bytes / 16, 1.0), 5, c))
            continue
        name, arg, cost = tasks.pop(0)
        plan.append((name, arg))
        now += cost
        if name in (GIVE, PAIR):
            arrive = [send(CORE, chunks[c].bytes, 1.0) for c in groups[arg]]
            pending.append((max(arrive), 1, arg))
        elif name == LAST:
            pending.append((now + 2.0, 1, SMALL))
    return plan


class Ring:
    def __init__(self, sources, slots, semaphores, depth):
        self.copies = [
            pltpu.make_async_copy(source, slot, semaphores())
            for source, slot in zip(sources, slots)
        ]
        self.slots, self.depth, self.at = slots, depth, 0

    def begin(self):
        for copy in self.copies[: self.depth]:
            copy.start()

    def take(self):
        self.copies[self.at].wait()
        return self.slots[self.at]

    def done(self):
        ahead = self.at + self.depth
        if ahead < len(self.copies):
            self.copies[ahead].start()
        self.at += 1


class Names:
    def __init__(self, names, refs):
        self.__dict__.update(zip(names, refs))


LOADS = 96


def finish_kernel(chunks, groups, plan, r):
    n = len(chunks)
    s = lax.axis_index("section")
    d = lax.axis_index("dp")
    here = (d // 4, (d // 2) % 2, d % 2)
    z, y, x = here
    sibling = {"section": 1 - s}
    z_at = [lax.rem(z + k, 4) for k in (1, 2, 3)]
    peers = {
        X: [(1 - x, {"dp": d + 1 - 2 * x})],
        Y: [(1 - y, {"dp": d + 2 - 4 * y})],
        Z: [(p, {"dp": d + 4 * (p - z)}) for p in z_at],
    }
    every = [sibling] + [peer for axis in (X, Y, Z) for _, peer in peers[axis]]

    barrier = pltpu.get_barrier_semaphore()
    for peer in every:
        pl.semaphore_signal(barrier, inc=1, device_id=peer, device_id_type=MESH)

    counter = iter(range(LOADS))

    def semaphore():
        return r.load_sem.at[next(counter)]

    def remote(src, dst, send, recv, peer):
        return pltpu.make_async_remote_copy(
            src_ref=src, dst_ref=dst, send_sem=send, recv_sem=recv, device_id=peer, device_id_type=MESH
        )

    rhs_of = {DEC_QKV: r.gqkv2, DEC_UP: r.gf2, DEC_OUT: r.ga2}
    lhs_of = {DEC_QKV: r.at2, DEC_UP: r.ct2, DEC_OUT: r.ot2, DEC_DOWN: r.gt2}
    tiles, widths, last_use = [], [], {}

    def wide_columns(g, side):
        k, width = chunks[groups[g][0]], sum(chunks[c].width for c in groups[g])
        return pl.ds(pl.multiple_of(side * k.half + k.offset, 128), width)

    for i, (name, arg) in enumerate(plan):
        if name == PAIR:
            tiles += [r.u2.at[:, t * 512 : (t + 1) * 512] for t in range(4)]
            last_use[DEC_DOWN] = i
        elif name in (GIVE, 1) and arg != SMALL and chunks[groups[arg][0]].decoder:
            k = chunks[groups[arg][0]]
            tiles.append(rhs_of[k.name].at[:, wide_columns(arg, 1 - s if name == GIVE else s)])
            last_use[k.name] = i
    lhs_names = decoder_arrays(chunks)
    assert sorted(lhs_names, key=last_use.get) == lhs_names
    rhs_slots = [r.rhs.at[i % 2, :, : tile.shape[1]] for i, tile in enumerate(tiles)]
    rhs = Ring(tiles, rhs_slots, semaphore, 2)
    lhs = Ring([lhs_of[k] for k in lhs_names], [r.lhs.at[i % 2] for i in range(4)], semaphore, 2)
    lhs.copies[0].start()
    rhs.begin()
    lhs.copies[1].start()
    tokens, d_enc = r.gy.shape
    blocks = []
    for t in range(4):
        at = pl.ds(t * d_enc, d_enc)
        blocks += [r.w_down.at[at, :], r.w_up.at[:, at]]
    blocks.append(r.w_out)
    blocks += [r.w_qkv.at[:, pl.ds(j * d_enc, d_enc)] for j in range(3)]
    weights = Ring(blocks, [r.w.at[i % 4] for i in range(12)], semaphore, 4)
    e_width = 2 * tokens
    e_ring = Ring(
        [r.e.at[:, pl.ds(g * e_width, e_width)] for g in range(6)],
        [r.e_v.at[g % 2] for g in range(6)],
        semaphore,
        2,
    )

    def load(source, target):
        return pltpu.make_async_copy(source, target, semaphore())

    mine = pl.ds(pl.multiple_of(s * tokens, tokens), tokens)
    load_gy, load_slope, load_ut = load(r.gy, r.gy_v), load(r.slope, r.slope_v), load(r.ut, r.ut_v)
    load_ct, load_at, load_ot = load(r.ct, r.ct_v), load(r.at, r.at_v), load(r.ot, r.ot_v)
    load_n2, load_s2, load_qkv = load(r.n2, r.n2_v), load(r.s2, r.s2_v), load(r.qkv, r.qkv_v)
    load_o, load_rl, load_x = load(r.o, r.o_v), load(r.rl, r.rl_v), load(r.x.at[mine, :], r.x_v)
    load_y, load_geb = load(r.y, r.y_v), load(r.geb, r.geb_v)
    begun = [
        (load_gy, load_slope, weights),
        (load_ut, load_ct, load_n2, load_s2),
        (load_qkv, load_o, load_rl, e_ring),
        (load_ot, load_at, load_x, load_y, load_geb),
    ]

    def begin_some():
        for copy in begun.pop(0) if begun else ():
            copy.begin() if isinstance(copy, Ring) else copy.start()

    half = r.decoded.shape[1] // 2
    give_half = r.decoded.at[:, pl.ds(pl.multiple_of((1 - s) * half, half), half), :]
    decoded_away = remote(give_half, r.decoded_got, r.swap_sem.at[0], r.swap_sem.at[1], sibling)
    gx_columns = d_enc // 2
    gx_half = r.gx.at[:, pl.ds(pl.multiple_of((1 - s) * gx_columns, 128), gx_columns)]
    gx_away = remote(gx_half, r.gx_got, r.swap_sem.at[2], r.swap_sem.at[3], sibling)

    small = r.small
    small[...] = jnp.zeros_like(small)
    small[ROW_DEC : ROW_DEC + 8, : r.small2.shape[1]] = r.small2[...]
    quarter = r.gbup2.shape[1] // 4
    for i in range(4):
        piece = r.gbup2[:, i * quarter : (i + 1) * quarter]
        small[ROW_DEC_BUP + i : ROW_DEC_BUP + i + 1, :quarter] = piece

    pl.semaphore_wait(barrier, len(every))

    copies = {}
    first_slot = (0, 1, 2, 5, 8)

    def chunk_copy(c, slot, src, dst, peer):
        copy = remote(src, dst, r.send_sem.at[c, slot], r.recv_sem.at[c, slot], peer)
        copy.start()
        copies[c, slot] = copy

    sent = set()

    def sent_by(c, slot):
        if (c, slot) not in sent:
            sent.add((c, slot))
            copies[c, slot].wait_send()

    staged = {}

    def staging(c):
        k = chunks[c]
        buffers = r.stage[k.rows, k.width]
        turn = staged.setdefault((k.rows, k.width), [])
        if len(turn) >= len(buffers):
            sent_by(turn[-len(buffers)], 0)
        turn.append(c)
        return buffers[(len(turn) - 1) % len(buffers)]

    def shard(i):
        return (i // 4, (i // 2) % 2, i % 2)

    waited = set()

    def arrived(copy):
        if id(copy) not in waited:
            waited.add(id(copy))
            copy.wait()

    def product(g, side):
        k, columns = chunks[groups[g][0]], wide_columns(g, side)
        if k.decoder:
            return mm(lhs.slots[lhs_names.index(k.name)][...], rhs.take()[...])
        if k.name == EMBED:
            arrived(load_y)
            arrived(load_geb)
            return mm_tn(r.y_v[...], r.geb_v[:, columns])
        if k.name == ENC_DOWN:
            arrived(load_ut)
            at = [i * 192 + k.first_row for i in range(16)]
            left = jnp.concatenate([r.ut_v[i : i + k.rows, :] for i in at], axis=0)
            return mm(left, r.gy_v[:, columns])
        if k.name == ENC_UP:
            arrived(load_ct)
            return mm(r.ct_v[...], r.slope_v[:, columns])
        if k.name == ENC_OUT:
            arrived(load_ot)
            return mm(r.ot_v[...], r.ga_v[:, columns])
        arrived(load_at)
        return mm(r.at_v[...], r.qkv_v[:, columns])

    def after_product(i, g):
        k = chunks[groups[g][0]]
        if k.decoder:
            rhs.done()
            if last_use[k.name] == i:
                lhs.done()

    def wait_lhs(k):
        if k.name in lhs_names:
            arrived(lhs.copies[lhs_names.index(k.name)])

    def give(i, g):
        members = groups[g]
        wait_lhs(chunks[members[0]])
        buffers = [staging(c) for c in members]
        value = product(g, 1 - s).astype(BF16)
        for m, (c, buffer) in enumerate(zip(members, buffers)):
            k = chunks[c]
            part = value[:, m * k.width : (m + 1) * k.width]
            for j in range(16):
                buffer[shard(j)] = part[j * k.rows : (j + 1) * k.rows]
            chunk_copy(c, 0, buffer, r.acc[c], sibling)
        after_product(i, g)
        begin_some()

    def pair(i, g):
        both = groups[g]
        wait_lhs(chunks[both[0]])
        left = lhs.slots[lhs_names.index(DEC_DOWN)]
        side_rows = chunks[both[0]].half
        buffers = [staging(c) for c in both]
        for t in range(4):
            tile = rhs.take()
            for side, targets in ((1 - s, buffers), (s, [r.acc[c] for c in both])):
                at = pl.ds(pl.multiple_of(side * side_rows, side_rows), side_rows)
                value = mm(left[at, :], tile[...]).astype(BF16)
                for c, target in zip(both, targets):
                    k = chunks[c]
                    rows = slice(k.offset, k.offset + k.rows)
                    for j in range(4):
                        target[shard(4 * t + j)] = value[rows, j * k.width : (j + 1) * k.width]
            rhs.done()
        lhs.done()
        for c, buffer in zip(both, buffers):
            chunk_copy(c, 0, buffer, r.got[c], sibling)

    def spots(k, stage):
        fixed = {axis: here[axis] for axis in k.order[: stage - 1]}
        return [fixed.get(axis, slice(None)) for axis in (Z, Y, X)]

    def send_stage(c, stage):
        k = chunks[c]
        axis = k.order[stage - 1]
        for j, (coordinate, peer) in enumerate(peers[axis]):
            at = spots(k, stage)
            at[axis] = coordinate
            src = r.acc[c].at[tuple(at)]
            chunk_copy(c, first_slot[stage] + j, src, r.recv[stage - 1][c].at[j], peer)

    def got_stage(c, stage):
        k = chunks[c]
        count = len(peers[k.order[stage - 1]])
        for j in range(count):
            copies[c, first_slot[stage] + j].wait_recv()
        return count

    def add_stage(c, stage):
        k, acc, got = chunks[c], r.acc[c], r.recv[stage - 1][c]
        count = got_stage(c, stage)
        left = [axis for axis in (Z, Y, X) if axis not in k.order[:stage]]
        sizes = [(4, 2, 2)[axis] for axis in left]
        for j in range(math.prod(sizes)):
            place, rest = {}, j
            for axis, size in reversed(list(zip(left, sizes))):
                place[axis] = rest % size
                rest //= size
            at = tuple(place.get(axis, here[axis]) for axis in (Z, Y, X))
            index = tuple(place[axis] for axis in left)
            if count == 1:
                acc[at] = acc[at] + got[(0,) + index]
            else:
                total = acc[at].astype(F32)
                for m in range(count):
                    total = total + got[(m,) + index].astype(F32)
                acc[at] = total.astype(BF16)

    def stage1(i, g):
        members = groups[g]
        for c in members:
            copies[c, 0].wait_recv()
        if chunks[members[0]].turned:
            for c in members:
                acc = r.acc[c]
                for j in range(16):
                    acc[shard(j)] = acc[shard(j)] + r.got[c][shard(j)]
                send_stage(c, 1)
            return
        value = product(g, s)
        for m, c in enumerate(members):
            k, acc = chunks[c], r.acc[c]
            wide = value[:, m * k.width : (m + 1) * k.width]
            for j in range(16):
                part = wide[j * k.rows : (j + 1) * k.rows]
                acc[shard(j)] = (part + acc[shard(j)].astype(F32)).astype(BF16)
            send_stage(c, 1)
        after_product(i, g)

    def stage2(i, c):
        add_stage(c, 1)
        send_stage(c, 2)

    def stage3(i, c):
        add_stage(c, 2)
        send_stage(c, 3)

    def stage4(i, c):
        k = chunks[c]
        total = r.acc[c][here].astype(F32)
        for j in range(got_stage(c, 3)):
            total = total + r.recv[2][c][j].astype(F32)
        out = r.out[k.name]
        out[k.place(s)] = total.astype(BF16)
        final = out.at[k.place(s)]
        chunk_copy(c, 8, final, final, sibling)

    def stage5(i, c):
        copies[c, 8].wait_recv()

    small_copies = []

    def small_copy(source, peer):
        slot = len(small_copies)
        copy = remote(
            source, r.small_got.at[slot], r.small_sem.at[0, slot], r.small_sem.at[1, slot], peer
        )
        copy.start()
        small_copies.append(copy)

    def small_stage(stage):
        if stage < 4:
            small_copies[stage - 1].wait()
            total = small[...] + r.small_got[stage - 1]
            if stage < 3:
                small[...] = total
                small_copy(small, peers[X if stage == 1 else Y][0][1])
            else:
                r.small_sum[...] = total
                for _, peer in peers[Z]:
                    small_copy(r.small_sum, peer)
        else:
            total = r.small_sum[...]
            for j in range(3):
                small_copies[3 + j].wait()
                total = total + r.small_got[3 + j]
            r.out_small[...] = total

    def ffn(i, t):
        if t == 0:
            load_gy.wait()
            load_slope.wait()
            begin_some()
        at = slice(t * d_enc, (t + 1) * d_enc)
        gu = mm_nt(r.gy_v[...], weights.take()[...])
        weights.done()
        gf = (gu * r.slope_v[:, at].astype(F32)).astype(BF16)
        r.slope_v[:, at] = gf
        small[ROW_BUP + t : ROW_BUP + t + 1, :] = rows_sum(gf.astype(F32))
        gc = mm_nt(gf, weights.take()[...])
        weights.done()
        r.sum_v[...] = gc if t == 0 else r.sum_v[...] + gc

    def ln2(i, _):
        load_n2.wait()
        load_s2.wait()
        g, gc, n2 = r.gy_v[...].astype(F32), r.sum_v[...], r.n2_v[...]
        gh = g + normalise_back(gc, n2, r.s2_v[...], row(r.gain2))
        begin_some()
        small[2:3, :] = rows_sum(gh)
        small[3:4, :] = rows_sum(gc * n2)
        small[4:5, :] = rows_sum(gc)
        small[5:6, :] = rows_sum(g)
        r.n2_v[...] = gh
        r.ga_v[...] = gh.astype(BF16)

    def go(i, _):
        r.go_v[...] = mm_nt(r.ga_v[...], weights.take()[...]).astype(BF16)
        weights.done()

    def att(i, g):
        if g == 0:
            for copy in (load_qkv, load_o, load_rl):
                copy.wait()
        at = slice(g * 128, (g + 1) * 128)
        parts = [slice(j * d_enc + g * 128, j * d_enc + (g + 1) * 128) for j in range(3)]
        q, k, v = (r.qkv_v[:, part] for part in parts)
        grads = attention_backward_group(
            q, k, v, e_ring.take()[...], r.go_v[:, at], r.o_v[:, at], r.rl_v[:, at],
            d_enc // H_ENC,
        )
        e_ring.done()
        for part, grad in zip(parts, grads):
            r.qkv_v[:, part] = grad

    def gn(i, j):
        part = mm_nt(r.qkv_v[:, j * d_enc : (j + 1) * d_enc], weights.take()[...])
        weights.done()
        r.sum_v[...] = part if j == 0 else r.sum_v[...] + part

    def last(i, _):
        load_x.wait()
        n1, s1 = normalise(r.x_v[...].astype(F32))
        total = r.sum_v[...]
        small[0:1, :] = rows_sum(total * n1)
        small[1:2, :] = rows_sum(total)
        small_copy(small, sibling)
        gx = r.n2_v[...] + normalise_back(total, n1, s1, row(r.gain1))
        r.gx[...] = gx.astype(BF16)
        gx_away.start()
        decoded_away.start()

    run = {
        GIVE: give, PAIR: pair, FFN: ffn, LN2: ln2, GO: go, ATT: att, GN: gn, LAST: last,
        1: stage1, 2: stage2, 3: stage3, 4: stage4, 5: stage5,
    }
    for i, (name, arg) in enumerate(plan):
        if arg == SMALL:
            small_stage(name)
        else:
            run[name](i, arg)

    for c, slot in copies:
        sent_by(c, slot)
    gx_away.wait()
    decoded_away.wait()


def finish_buffers(chunks, rows, d, ff, dec_total, dec):
    def of(dtype, *dims):
        return (dims, dtype)

    return dict(
        y_v=of(BF16, rows, d),
        geb_v=of(BF16, rows, dec),
        gy_v=of(BF16, rows, d),
        slope_v=of(BF16, rows, ff),
        n2_v=of(F32, rows, d),
        s2_v=of(F32, rows, 1),
        qkv_v=of(BF16, rows, 3 * d),
        o_v=of(BF16, rows, d),
        rl_v=of(F32, rows, d),
        x_v=of(BF16, rows, d),
        ga_v=of(BF16, rows, d),
        go_v=of(BF16, rows, d),
        sum_v=of(F32, rows, d),
        ut_v=of(BF16, ff, rows),
        ct_v=of(BF16, d, rows),
        at_v=of(BF16, d, rows),
        ot_v=of(BF16, d, rows),
        e_v=of(BF16, 2, rows, 2 * rows),
        w=of(BF16, 4, d, d),
        lhs=of(BF16, 2, dec, dec_total),
        rhs=of(BF16, 2, dec_total, 768),
        small=of(F32, SMALL_ROWS, d),
        small_sum=of(F32, SMALL_ROWS, d),
        small_got=of(F32, 6, SMALL_ROWS, d),
    )


def finish(acts):
    enc, dec = acts["enc"], acts["dec"]
    gain1, _, w_qkv, w_out, _, gain2, _, w_up, _, w_down, _ = enc["params"]
    qkv, e, rl, o, n2, s2, slope = acts["saved"]
    given = dict(
        x=acts["x"], y=acts["y"], gy=acts["gy"], geb=acts["geb"], qkv=qkv, e=e, rl=rl, o=o, n2=n2,
        s2=s2, slope=slope, at=enc["at"], ot=enc["ot"], ct=enc["ct"], ut=enc["ut"], at2=dec["at"], ot2=dec["ot"],
        ct2=dec["ct"], gt2=dec["gt"], u2=dec["u"], gf2=dec["gf"], ga2=dec["ga"],
        gqkv2=dec["gqkv"], w_qkv=w_qkv, w_out=w_out, w_up=w_up, w_down=w_down,
        decoded=acts["decoded"].reshape(SAMP_MB, PATCHES, -1),
    )
    n_hbm = len(given)
    given.update(small2=acts["small2"], gbup2=acts["gbup2"], gain1=gain1, gain2=gain2)
    rows, d = acts["gy"].shape
    ff = w_up.shape[1]
    dec_d, dec_total = dec["at"].shape
    dec_ff = dec["u"].shape[1]
    chunks = make_chunks()
    n = len(chunks)
    groups = make_groups(chunks)
    plan = make_plan(chunks, groups)

    dims = {
        ENC_QKV: (d, 3 * d), ENC_OUT: (d, d), ENC_UP: (d, ff), ENC_DOWN: (ff, d),
        EMBED: (d, dec_d), DEC_QKV: (dec_d, 3 * dec_d), DEC_OUT: (dec_d, dec_d),
        DEC_UP: (dec_d, dec_ff), DEC_DOWN: (dec_ff, dec_d),
    }
    big = [
        shape(dims[k][1], dims[k][0] // 16) if k == DEC_DOWN else shape(dims[k][0] // 16, dims[k][1])
        for k in range(9)
    ]
    outs = dict(
        out_small=shape(SMALL_ROWS, d, F32),
        decoded_got=jax.ShapeDtypeStruct((SAMP_MB, PATCHES // 2, dec_d), BF16),
        gx=shape(rows, d),
        gx_got=shape(rows, d // 2),
    )
    single = finish_buffers(chunks, rows, d, ff, dec_total, dec_d)
    left = (4, 2, 2)
    lists = [[], [], [], [], []]
    for k in chunks:
        block = (k.rows, k.width)
        lists[0].append((left + block, BF16))
        if k.turned:
            lists[1].append((left + block, BF16))
        for stage in range(3):
            rest = [left[axis] for axis in (Z, Y, X) if axis not in k.order[: stage + 1]]
            count = 3 if k.order[stage] == Z else 1
            lists[2 + stage].append(((count, *rest, *block), BF16))
    blocks = sorted({(k.rows, k.width) for k in chunks})
    slots = [1] * len(blocks)
    lists.append([(left + block, BF16) for block, m in zip(blocks, slots) for _ in range(m)])
    semaphores = dict(
        load_sem=(LOADS,), send_sem=(n, 9), recv_sem=(n, 9), small_sem=(2, 6), swap_sem=(4,)
    )

    def kernel(*refs):
        refs = list(refs)

        def take(count):
            taken = refs[:count]
            del refs[:count]
            return taken

        names = list(given) + list(outs)
        r = Names(names, take(len(names)))
        r.out = take(9)
        r.__dict__.update(zip(single, take(len(single))))
        r.acc = take(n)
        r.got = dict(zip([c for c, k in enumerate(chunks) if k.turned], take(len(lists[1]))))
        r.recv = [take(n) for _ in range(3)]
        r.stage = {block: take(m) for block, m in zip(blocks, slots)}
        r.__dict__.update(zip(semaphores, take(len(semaphores))))
        finish_kernel(chunks, groups, plan, r)

    flat = list(single.values()) + [b for group in lists for b in group]
    results = pl.pallas_call(
        kernel,
        out_shape=list(outs.values()) + big,
        in_specs=[in_hbm()] * n_hbm + in_vmem(len(given) - n_hbm),
        out_specs=in_vmem(len(outs) + 9),
        scratch_shapes=[pltpu.VMEM(*b) for b in flat]
        + [pltpu.SemaphoreType.DMA(v) for v in semaphores.values()],
        compiler_params=pltpu.CompilerParams(
            collective_id=1, has_side_effects=True, vmem_limit_bytes=FINISH_VMEM
        ),
        name="finish",
    )(*given.values())
    return write_outputs(results, given["decoded"], dims)


FINISH_VMEM = 62 * 2**20


def write_kernel(small, decoded_got, gx_own, gx_got, *refs):
    big, decoded_own = refs[:9], refs[9]
    decoded, gx, *totals = refs[10:]
    s = lax.axis_index("section")
    half = decoded.shape[1]
    samples, rows, columns = decoded_own.shape[0], gx_own.shape[0], gx.shape[1]
    own = decoded_own[:, pl.ds(pl.multiple_of(s * half, half), half), :]
    for side, part in ((s, own), (1 - s, decoded_got[...])):
        decoded[pl.ds(side * samples, samples)] = part
    own = gx_own[:, pl.ds(pl.multiple_of(s * columns, 128), columns)]
    for side, part in ((s, own), (1 - s, gx_got[...])):
        gx[pl.ds(pl.multiple_of(side * rows, rows), rows), :] = part
    d = lax.axis_index("dp")
    wide, narrow = small.shape[1], big[DEC_OUT].shape[1]

    def piece(out, line, lanes, position):
        size = out.shape[0]
        value = small[pl.ds(line, 1), :lanes]
        value = pltpu.roll(value, lax.rem(lanes - position * size, lanes), 1)
        out[...] = value[:, :size].reshape(size)

    def matrix(out, name):
        value = big[name][...].astype(F32)
        out[...] = jnp.transpose(value) if name == DEC_DOWN else value

    def block(outs, first_row, bup_row, lanes, names):
        for i, out in zip((0, 1, None, None, 2, 3, 4, None, None, None, 5), outs):
            if i is not None:
                piece(out, first_row + i, lanes, d)
        piece(outs[8], bup_row + d // 4, lanes, d % 4)
        for at, name in zip((2, 3, 7, 9), names):
            matrix(outs[at], name)

    block(totals[:11], 0, ROW_BUP, wide, (ENC_QKV, ENC_OUT, ENC_UP, ENC_DOWN))
    matrix(totals[11], EMBED)
    piece(totals[12], ROW_DEC + 7, narrow, d)
    piece(totals[13], ROW_DEC + 6, narrow, d)
    block(totals[14:], ROW_DEC, ROW_DEC_BUP, narrow, (DEC_QKV, DEC_OUT, DEC_UP, DEC_DOWN))


def write_outputs(results, decoded_own, dims):
    def vector(size):
        return jax.ShapeDtypeStruct((size // 16,), F32)

    def matrix(name):
        return shape(dims[name][0] // 16, dims[name][1], F32)

    def block(qkv, out, up, down):
        d, ff = dims[up]
        return [
            vector(d), vector(d), matrix(qkv), matrix(out), vector(d), vector(d), vector(d),
            matrix(up), vector(ff), matrix(down), vector(d),
        ]

    samples, half, width = results[1].shape
    rows, columns = results[3].shape
    out_shape = [
        jax.ShapeDtypeStruct((2 * samples, half, width), BF16),
        shape(2 * rows, columns),
        *block(ENC_QKV, ENC_OUT, ENC_UP, ENC_DOWN),
        matrix(EMBED),
        vector(width),
        vector(width),
        *block(DEC_QKV, DEC_OUT, DEC_UP, DEC_DOWN),
    ]
    return tuple(
        pl.pallas_call(
            write_kernel,
            out_shape=out_shape,
            in_specs=in_vmem(len(results) + 1),
            out_specs=in_vmem(len(out_shape)),
            compiler_params=pltpu.CompilerParams(vmem_limit_bytes=KERNEL_VMEM),
            name="write_outputs",
        )(*results, decoded_own)
    )


def reduce_plain(arrays, section_index):
    first = section_index == 0
    results = []
    for a in arrays:
        half = a.shape[1] // 2
        keep = lax.dynamic_slice_in_dim(a, section_index * half, half, 1)
        give = lax.dynamic_slice_in_dim(a, (1 - section_index) * half, half, 1)
        got = swapped(give, "section", 0)
        chip = (keep.astype(jnp.float32) + got.astype(jnp.float32)).astype(jnp.bfloat16)
        mine = lax.psum_scatter(chip, "dp", scatter_dimension=0, tiled=True)
        other = swapped(mine, "section", 0)
        whole = jnp.concatenate(
            [jnp.where(first, mine, other), jnp.where(first, other, mine)], axis=1
        )
        results.append(whole.astype(jnp.float32))
    return results


def finish_plain(acts, section_index):
    x, gy, seg_saved, enc, dec = acts["x"], acts["gy"], acts["saved"], acts["enc"], acts["dec"]
    gx, gf1, ga1, gqkv1, small1, gbup1 = encoder_backward(x, gy, seg_saved, enc["params"])
    small2, gbup2 = acts["small2"], acts["gbup2"]
    grads = (
        small1[0], small1[1], mm(enc["at"], gqkv1).astype(BF16), mm(enc["ot"], ga1).astype(BF16), small1[2],
        small1[3], small1[4], mm(enc["ct"], gf1).astype(BF16), gbup1[0], mm(enc["ut"], gy).astype(BF16),
        small1[5],
        weight_grad(acts["y"], acts["geb"]), small2[7], small2[6],
        small2[0], small2[1], mm(dec["at"], dec["gqkv"]).astype(BF16),
        mm(dec["ot"], dec["ga"]).astype(BF16), small2[2], small2[3], small2[4],
        mm(dec["ct"], dec["gf"]).astype(BF16), gbup2[0],
        jnp.transpose(mm(dec["gt"], dec["u"])).astype(BF16), small2[5],
    )
    groups = lax.axis_size("dp")
    big = reduce_plain([g for g in grads if g.ndim == 2], section_index)
    flat = jnp.concatenate([g.reshape(groups, -1) for g in grads if g.ndim == 1], axis=1)
    line = lax.psum_scatter(flat, ("dp"), scatter_dimension=0, tiled=True)
    line = lax.psum(line, "section")[0]
    totals, at = [], 0
    for g in grads:
        if g.ndim == 2:
            totals.append(big.pop(0))
        else:
            size = g.shape[0] // groups
            totals.append(line[at : at + size])
            at += size
    decoded = acts["decoded"].reshape(SAMP_MB, PATCHES, -1)
    first = section_index == 0

    def halves(whole):
        half = whole.shape[1] // 2
        keep = lax.dynamic_slice_in_dim(whole, section_index * half, half, 1)
        give = lax.dynamic_slice_in_dim(whole, (1 - section_index) * half, half, 1)
        got = swapped(give, "section", 0)
        return jnp.concatenate([jnp.where(first, keep, got), jnp.where(first, got, keep)])

    return (halves(decoded), halves(gx), *totals)


def shards(
    patches,
    segment_ids,
    patch_order,
    encoder_gain1,
    encoder_bias1,
    encoder_qkv,
    encoder_out,
    encoder_out_bias,
    encoder_gain2,
    encoder_bias2,
    encoder_up,
    encoder_up_bias,
    encoder_down,
    encoder_down_bias,
    embed_weight,
    embed_bias,
    mask_token,
    decoder_gain1,
    decoder_bias1,
    decoder_qkv,
    decoder_out,
    decoder_out_bias,
    decoder_gain2,
    decoder_bias2,
    decoder_up,
    decoder_up_bias,
    decoder_down,
    decoder_down_bias,
    cotangent,
):
    enc_params = (
        encoder_gain1,
        encoder_bias1,
        encoder_qkv,
        encoder_out,
        encoder_out_bias,
        encoder_gain2,
        encoder_bias2,
        encoder_up,
        encoder_up_bias,
        encoder_down,
        encoder_down_bias,
    )
    embed_params = (embed_weight, embed_bias, mask_token)
    dec_params = (
        decoder_gain1,
        decoder_bias1,
        decoder_qkv,
        decoder_out,
        decoder_out_bias,
        decoder_gain2,
        decoder_bias2,
        decoder_up,
        decoder_up_bias,
        decoder_down,
        decoder_down_bias,
    )
    section_index = lax.axis_index("section")
    y, at1, qkv, e, rl, o1, ot1, n2, s2, ct1, ut1, slope = encoder_forward(
        patches, segment_ids, enc_params
    )
    g = cotangent.reshape(-1, DECODER_WIDTH)
    decoded, at2, ot2, ct2, gt2, u2, gf2, ga2, gqkv2, geb, gy, small2, gbup2 = decoder_both(
        y, segment_ids, patch_order, g, embed_params, dec_params
    )
    acts = dict(
        x=patches,
        y=y,
        gy=gy,
        geb=geb,
        decoded=decoded,
        small2=small2,
        gbup2=gbup2,
        saved=(qkv, e, rl, o1, n2, s2, slope),
        enc=dict(at=at1, ot=ot1, ct=ct1, ut=ut1, params=enc_params),
        dec=dict(at=at2, ot=ot2, ct=ct2, gt=gt2, u=u2, gf=gf2, ga=ga2, gqkv=gqkv2),
    )
    if lax.axis_size("dp") == 16:
        return finish(acts)
    return finish_plain(acts, section_index)


def solution(mesh):
    in_specs = (
        P("dp", None),
        P("dp", None),
        P("dp", None),
        P(),
        P(),
        P(),
        P(),
        P(),
        P(),
        P(),
        P(),
        P(),
        P(),
        P(),
        P(),
        P(),
        P(),
        P(),
        P(),
        P(),
        P(),
        P(),
        P(),
        P(),
        P(),
        P(),
        P(),
        P(),
        P("dp", None, None),
    )
    out_specs = (
        P("dp", "section", None),
        P("dp", "section"),
        P("dp"),
        P("dp"),
        P("dp", None),
        P("dp", None),
        P("dp"),
        P("dp"),
        P("dp"),
        P("dp", None),
        P("dp"),
        P("dp", None),
        P("dp"),
        P("dp", None),
        P("dp"),
        P("dp"),
        P("dp"),
        P("dp"),
        P("dp", None),
        P("dp", None),
        P("dp"),
        P("dp"),
        P("dp"),
        P("dp", None),
        P("dp"),
        P("dp", None),
        P("dp"),
    )
    return jax.shard_map(shards, mesh=mesh, in_specs=in_specs, out_specs=out_specs, check_vma=False)
```

```python
import functools
import math

import jax
import jax.numpy as jnp
import numpy as np
from jax import lax
from jax.experimental import pallas as pl
from jax.experimental.pallas import tpu as pltpu
from jax.sharding import PartitionSpec as P

H_ENC = 12
DECODER_WIDTH = 512
H_DEC = 16
PATCHES = 128
SAMP_MB = 12


EPSILON = 1e-06
MASKED = -1e30


def swapped(block, axis, apart):
    count = lax.axis_size(axis)
    route = []
    for low in range(count):
        high = low | 1 << apart
        if high != low and high < count:
            route += [(low, high), (high, low)]
    return lax.ppermute(block, axis, route)


def positions(count, features):
    column = np.arange(features)
    rate = np.exp(-math.log(10000.0) * (2 * (column // 2)) / features)
    angles = np.arange(count)[:, None] * rate[None, :]
    return np.where(column % 2 == 0, np.sin(angles), np.cos(angles)).astype(np.float32)


def weight_grad(left_side, grads):
    return lax.dot_general(
        left_side, grads, (((0,), (0,)), ((), ())), preferred_element_type=jnp.float32
    ).astype(jnp.bfloat16)


BF16 = jnp.bfloat16
F32 = jnp.float32


def mm(left, right):
    return lax.dot_general(left, right, (((1,), (0,)), ((), ())), preferred_element_type=F32)


def mm_nt(left, right):
    return lax.dot_general(left, right, (((1,), (1,)), ((), ())), preferred_element_type=F32)


def mm_tn(left, right):
    return lax.dot_general(left, right, (((0,), (0,)), ((), ())), preferred_element_type=F32)


def normalise(x):
    center = x - jnp.mean(x, axis=-1, keepdims=True)
    scale = lax.rsqrt(jnp.mean(center * center, axis=-1, keepdims=True) + EPSILON)
    return center * scale, scale


def normalise_back(grad, n, scale, gain):
    gn = grad * gain
    mean_gn = jnp.mean(gn, axis=-1, keepdims=True)
    mean_gnn = jnp.mean(gn * n, axis=-1, keepdims=True)
    return (gn - mean_gn - n * mean_gnn) * scale


def rows_sum(x):
    return jnp.sum(x, axis=0, keepdims=True)


def gelu_both(f):
    c0, c1 = math.sqrt(2.0 / math.pi), 0.044715
    square = f * f
    half = 0.5 + 0.5 * jnp.tanh(f * (c0 + (c0 * c1) * square))
    u = f * half
    return u, half + u * (1.0 - half) * (2.0 * c0 + (6.0 * c0 * c1) * square)


def lane_masks(head_size):
    lane = lax.broadcasted_iota(jnp.int32, (1, 128), 1)
    return [
        jnp.where((lane >= h * head_size) & (lane < (h + 1) * head_size), 1.0, 0.0).astype(BF16)
        for h in range(128 // head_size)
    ]


def stacked(x, masks):
    return jnp.concatenate([x * m for m in masks], axis=0)


def stacked_ones(x, masks, value):
    return jnp.concatenate(
        [jnp.broadcast_to(m * jnp.asarray(value, BF16), x.shape) for m in masks], axis=0
    )


def attention_forward(qkv_ref, o_ref, e_ref, rl_ref, rows, tokens, features, head_size, allowed):
    masks = lane_masks(head_size)
    per_group = len(masks)
    factor = head_size ** (-0.5) * math.log2(math.e)
    for g in range(features // 128):
        q, k, v = (qkv_ref[rows, j * features + g * 128 : j * features + (g + 1) * 128] for j in range(3))
        scores = mm_nt(q, stacked(k, masks))
        parts = []
        for h in range(per_group):
            part = scores[:, h * tokens : (h + 1) * tokens]
            if allowed is not None:
                part = jnp.where(allowed, part, MASKED)
            top = jnp.max(part, axis=-1, keepdims=True)
            parts.append(jnp.exp2((part - top) * factor).astype(BF16))
        e = jnp.concatenate(parts, axis=1)
        width = per_group * tokens
        e_ref[rows, g * width : (g + 1) * width] = e
        both = mm(e, jnp.concatenate([stacked(v, masks), stacked_ones(v, masks, 1.0)], axis=1))
        rl = 1.0 / both[:, 128:]
        rl_ref[rows, g * 128 : (g + 1) * 128] = rl
        o_ref[rows, g * 128 : (g + 1) * 128] = (both[:, :128] * rl).astype(BF16)


def attention_backward_group(q, k, v, e, go, o, rl, head_size):
    masks = lane_masks(head_size)
    per_group, tokens = len(masks), q.shape[0]
    scaling = head_size ** (-0.5)
    go = go.astype(F32) * rl
    go_low = go.astype(BF16)
    inner = (go * o.astype(F32)).astype(BF16)
    left = jnp.concatenate([go_low, inner], axis=1)
    right = jnp.concatenate([stacked(v, masks), stacked_ones(v, masks, -1.0)], axis=1)
    gs = (e.astype(F32) * mm_nt(left, right)).astype(BF16)

    def diagonal(wide):
        return jnp.concatenate(
            [
                wide[h * head_size : (h + 1) * head_size, h * tokens : (h + 1) * tokens]
                for h in range(per_group)
            ],
            axis=0,
        )

    gq = mm(gs, stacked(k, masks)) * scaling
    gk = jnp.transpose(diagonal(mm_tn(q, gs)) * scaling)
    gv = jnp.transpose(diagonal(mm_tn(go_low, e)))
    return gq.astype(BF16), gk.astype(BF16), gv.astype(BF16)


def attention_backward(
    qkv_ref, go_ref, o_ref, e_ref, rl_ref, gqkv_ref, rows, tokens, features, head_size
):
    width = 128 // head_size * tokens
    for g in range(features // 128):
        at = slice(g * 128, (g + 1) * 128)
        spots = [slice(j * features + g * 128, j * features + (g + 1) * 128) for j in range(3)]
        q, k, v = (qkv_ref[rows, spot] for spot in spots)
        e = e_ref[rows, g * width : (g + 1) * width]
        grads = attention_backward_group(
            q, k, v, e, go_ref[rows, at], o_ref[rows, at], rl_ref[rows, at], head_size
        )
        for spot, grad in zip(spots, grads):
            gqkv_ref[rows, spot] = grad


def feed_forward(c_ref, up_ref, bup_ref, u_ref, slope_ref, tile, ut_ref=None):
    for t in range(up_ref.shape[1] // tile):
        at = slice(t * tile, (t + 1) * tile)
        f = mm(c_ref[...], up_ref[:, at]) + bup_ref[at].reshape(1, tile)
        u, slope = gelu_both(f)
        u = u.astype(BF16)
        u_ref[:, at] = u
        slope_ref[:, at] = slope.astype(BF16)
        if ut_ref is not None:
            ut_ref[at, :] = jnp.transpose(u)


def feed_forward_back(gm_ref, down_ref, slope_ref, gf_ref, gbup_ref, tile):
    for t in range(down_ref.shape[0] // tile):
        at = slice(t * tile, (t + 1) * tile)
        gu = mm_nt(gm_ref[...], down_ref[at, :])
        gf = (gu * slope_ref[:, at].astype(F32)).astype(BF16)
        gf_ref[:, at] = gf
        gbup_ref[:, at] += rows_sum(gf.astype(F32))


def row(ref):
    return ref[...].reshape(1, -1)


def segment_mask(seg_ref, section):
    seg = seg_ref[pl.ds(section, 1), :].astype(F32)
    rows = seg.shape[1]
    column = jnp.transpose(jnp.broadcast_to(seg, (128, rows)))
    return jnp.concatenate([column] * (rows // 128), axis=1) == seg


class Writer:
    def __init__(self, semaphores):
        self.semaphores, self.copies = semaphores, []

    def start(self, source, target):
        copy = pltpu.make_async_copy(source, target, self.semaphores.at[len(self.copies)])
        copy.start()
        self.copies.append(copy)

    def wait(self):
        for copy in self.copies:
            copy.wait()


def encoder_forward_kernel(
    x_ref, seg_ref,
    gain1, bias1, w_qkv, w_out, b_out, gain2, bias2, w_up, b_up, w_down, b_down,
    *refs,
):
    outs, scratch = refs[:12], refs[12:24]
    y_ref, at_ref, qkv_ref, e_ref, rl_ref, o_ref, ot_ref, n2_ref, s2_ref, ct_ref, ut_ref, slope_ref = scratch
    h_ref, c_ref, u_ref, qkv_v, out_v, up_v, down_v, sem, out_sem = refs[24:]
    target = {id(v): o for v, o in zip(scratch, outs)}
    writer = Writer(out_sem)

    def write(*done):
        for v in done:
            writer.start(v, target[id(v)])

    tokens, features = y_ref.shape
    pairs = ((w_qkv, qkv_v), (w_out, out_v), (w_up, up_v), (w_down, down_v))
    loads = [pltpu.make_async_copy(w, v, sem.at[i]) for i, (w, v) in enumerate(pairs)]
    for load in loads:
        load.start()
    section = lax.axis_index("section")
    x = x_ref[pl.ds(pl.multiple_of(section * tokens, tokens), tokens), :].astype(F32)
    n1, _ = normalise(x)
    a = (n1 * row(gain1) + row(bias1)).astype(BF16)
    at_ref[...] = jnp.transpose(a)
    allowed = segment_mask(seg_ref, section)
    loads[0].wait()
    qkv_ref[...] = mm(a, qkv_v[...]).astype(BF16)
    write(at_ref, qkv_ref)
    attention_forward(
        qkv_ref, o_ref, e_ref, rl_ref, slice(None), tokens, features, features // H_ENC, allowed
    )
    ot_ref[...] = jnp.transpose(o_ref[...])
    write(e_ref, rl_ref, o_ref, ot_ref)
    loads[1].wait()
    h_ref[...] = x + (mm(o_ref[...], out_v[...]) + row(b_out))
    n2, s2 = normalise(h_ref[...])
    n2_ref[...] = n2
    s2_ref[...] = s2
    c_ref[...] = (n2 * row(gain2) + row(bias2)).astype(BF16)
    ct_ref[...] = jnp.transpose(c_ref[...])
    write(n2_ref, s2_ref, ct_ref)
    loads[2].wait()
    feed_forward(c_ref, up_v, b_up, u_ref, slope_ref, 512, ut_ref)
    write(ut_ref, slope_ref)
    loads[3].wait()
    y_ref[...] = (h_ref[...] + (mm(u_ref[...], down_v[...]) + row(b_down))).astype(BF16)
    write(y_ref)
    writer.wait()


def encoder_backward_kernel(
    x_ref, gy_ref, qkv_ref, e_ref, rl_ref, o_ref, n2_ref, s2_ref, slope_ref,
    gain1, w_qkv, w_out, gain2, w_up, w_down,
    gx_ref, gf_ref, ga_ref, gqkv_ref, small_ref, gbup_ref,
    gh_ref, go_ref,
):
    tokens, features = gy_ref.shape
    section = lax.axis_index("section")
    x = x_ref[pl.ds(pl.multiple_of(section * tokens, tokens), tokens), :].astype(F32)
    gbup_ref[...] = jnp.zeros_like(gbup_ref)
    feed_forward_back(gy_ref, w_down, slope_ref, gf_ref, gbup_ref, 512)
    gc = mm_nt(gf_ref[...], w_up[...])
    g = gy_ref[...].astype(F32)
    n2 = n2_ref[...]
    gh = g + normalise_back(gc, n2, s2_ref[...], row(gain2))
    gh_ref[...] = gh
    ga_ref[...] = gh.astype(BF16)
    small_ref[2:3, :] = rows_sum(gh)
    small_ref[3:4, :] = rows_sum(gc * n2)
    small_ref[4:5, :] = rows_sum(gc)
    small_ref[5:6, :] = rows_sum(g)
    go_ref[...] = mm_nt(ga_ref[...], w_out[...]).astype(BF16)
    attention_backward(
        qkv_ref, go_ref, o_ref, e_ref, rl_ref, gqkv_ref, slice(None), tokens, features,
        features // H_ENC,
    )
    gn = mm_nt(gqkv_ref[...], w_qkv[...])
    n1, s1 = normalise(x)
    small_ref[0:1, :] = rows_sum(gn * n1)
    small_ref[1:2, :] = rows_sum(gn)
    gx_ref[...] = (gh_ref[...] + normalise_back(gn, n1, s1, row(gain1))).astype(BF16)


def split_low(x):
    high = x.astype(BF16)
    return high, (x - high.astype(F32)).astype(BF16)


def place_slots(order_ref, seg, section, hot_ref, place_ref, empty_ref):
    packed = seg.shape[1]
    sample = lax.broadcasted_iota(jnp.int32, (16, packed), 0).astype(F32)
    starts = jnp.sum(jnp.where(seg < sample, 1.0, 0.0), axis=1, keepdims=True)
    counts = jnp.sum(jnp.where(seg == sample, 1.0, 0.0), axis=1, keepdims=True)
    line = lax.broadcasted_iota(jnp.int32, (PATCHES, PATCHES), 0).astype(F32)
    line_low = line.astype(BF16)
    lane_low = lax.broadcasted_iota(jnp.int32, (8, PATCHES), 1).astype(F32).astype(BF16)
    column = lax.broadcasted_iota(jnp.int32, (PATCHES, packed), 1).astype(F32)
    packed_line = lax.broadcasted_iota(jnp.int32, (packed, PATCHES), 0).astype(F32)
    for j in range(SAMP_MB):
        at = slice(j * PATCHES, (j + 1) * PATCHES)
        order = order_ref[pl.ds(section * SAMP_MB + j, 1), :].astype(F32)
        hit = jnp.where(order == line, 1.0, 0.0).astype(BF16)
        start, count = starts[j : j + 1, :], counts[j : j + 1, :]
        down, across = mm(hit, line_low), mm_nt(lane_low, hit)[:1, :]
        down = jnp.where(down < count, start + down, -1.0)
        across = jnp.where(across < count, start + across, -1.0)
        wide = jnp.concatenate([down] * (packed // PATCHES), axis=1)
        hot_ref[at, :] = jnp.where(column == wide, 1.0, 0.0).astype(BF16)
        place_ref[:, at] = jnp.where(packed_line == across, 1.0, 0.0).astype(BF16)
        empty_ref[at, :] = jnp.where(down < 0.0, 1.0, 0.0)


def decoder_kernel(
    y_ref, seg_ref, order_ref, pos_ref, g_hbm,
    w_embed_hbm, b_embed, mask_token,
    gain1, bias1, w_qkv_hbm, w_out_hbm, b_out, gain2, bias2, w_up_hbm, b_up, w_down_hbm, b_down,
    *refs,
):
    hbm, (geb_ref, gy_ref, small_ref, gbup_ref) = refs[:9], refs[9:13]
    buffers = refs[13:22]
    out_ref, at_ref, ot_ref, ct_ref, gt_ref, u_ref, gf_ref, ga_ref, gqkv_ref = buffers
    (
        e2_ref, z_ref, s1_ref, e_ref, rl_ref, h_ref, s2_ref, go_ref, ge_ref, o_ref, c_ref, qkv_ref,
        slope_ref, g_all, hot_ref, place_ref, empty_ref, w_embed, w_qkv, w_out, w_up, w_down,
        w_sem, out_sem,
    ) = refs[22:]
    packed = y_ref.shape[0]
    rows, features = z_ref.shape
    samples = rows // PATCHES
    head_size = features // H_DEC
    total = g_all.shape[0]
    section = lax.axis_index("section")
    mine = pl.ds(pl.multiple_of(section * total, total), total)
    pairs = (
        (w_embed_hbm, w_embed), (w_qkv_hbm, w_qkv), (w_out_hbm, w_out), (w_up_hbm, w_up),
        (w_down_hbm, w_down), (g_hbm.at[mine, :], g_all),
    )
    loads = [pltpu.make_async_copy(a, b, w_sem.at[i]) for i, (a, b) in enumerate(pairs)]
    for load in loads:
        load.start()

    def write(at, *which):
        copies = []
        for i in which:
            target = hbm[i].at[:, at] if 1 <= i <= 4 else hbm[i].at[at, :]
            copies.append(pltpu.make_async_copy(buffers[i], target, out_sem.at[i]))
            copies[-1].start()
        return copies

    small_ref[...] = jnp.zeros_like(small_ref)
    gbup_ref[...] = jnp.zeros_like(gbup_ref)
    ge_ref[...] = jnp.zeros_like(ge_ref)
    seg = seg_ref[pl.ds(section, 1), :].astype(F32)
    place_slots(order_ref, seg, section, hot_ref, place_ref, empty_ref)
    loads[0].wait()
    high, low = split_low(mm(y_ref[...], w_embed[...]) + row(b_embed))
    e2_ref[:packed, :] = high
    e2_ref[packed:, :] = low
    for load in loads[1:]:
        load.wait()

    def one_step(step, carry):
        here = pl.ds(pl.multiple_of(step * rows, rows), rows)
        one_hot = hot_ref[here, :]
        empty = jnp.concatenate([empty_ref[here, :]] * (features // 128), axis=1)
        twice = jnp.concatenate([one_hot, one_hot], axis=1)
        z = mm(twice, e2_ref[...]) + empty * row(mask_token)
        z = z + jnp.concatenate([pos_ref[...]] * samples, axis=0)
        n1, s1 = normalise(z)
        z_ref[...] = z
        s1_ref[...] = s1
        a = (n1 * row(gain1) + row(bias1)).astype(BF16)
        at_ref[...] = jnp.transpose(a)
        writing = write(here, 1)
        qkv_ref[...] = mm(a, w_qkv[...]).astype(BF16)

        def forward(b, carry):
            at = pl.ds(pl.multiple_of(b * PATCHES, PATCHES), PATCHES)
            attention_forward(qkv_ref, o_ref, e_ref, rl_ref, at, PATCHES, features, head_size, None)
            return carry

        lax.fori_loop(0, samples, forward, 0, unroll=3)
        ot_ref[...] = jnp.transpose(o_ref[...])
        h_ref[...] = z_ref[...] + (mm(o_ref[...], w_out[...]) + row(b_out))
        n2, s2 = normalise(h_ref[...])
        s2_ref[...] = s2
        c_ref[...] = (n2 * row(gain2) + row(bias2)).astype(BF16)
        ct_ref[...] = jnp.transpose(c_ref[...])
        feed_forward(c_ref, w_up, b_up, u_ref, slope_ref, 512)
        writing += write(here, 2, 3, 5)
        out_ref[...] = (h_ref[...] + (mm(u_ref[...], w_down[...]) + row(b_down))).astype(BF16)

        g_ref = g_all.at[here, :]
        gt_ref[...] = jnp.transpose(g_ref[...])
        feed_forward_back(g_ref, w_down, slope_ref, gf_ref, gbup_ref, 512)
        writing += write(here, 0, 4, 6)
        gc = mm_nt(gf_ref[...], w_up[...])
        g = g_ref[...].astype(F32)
        h = h_ref[...]
        n2 = (h - jnp.mean(h, axis=-1, keepdims=True)) * s2_ref[...]
        gh = g + normalise_back(gc, n2, s2_ref[...], row(gain2))
        small_ref[2:3, :] += rows_sum(gh)
        small_ref[3:4, :] += rows_sum(gc * n2)
        small_ref[4:5, :] += rows_sum(gc)
        small_ref[5:6, :] += rows_sum(g)
        h_ref[...] = gh
        ga_ref[...] = gh.astype(BF16)
        go_ref[...] = mm_nt(ga_ref[...], w_out[...]).astype(BF16)
        writing += write(here, 7)

        def backward(b, carry):
            at = pl.ds(pl.multiple_of(b * PATCHES, PATCHES), PATCHES)
            attention_backward(
                qkv_ref, go_ref, o_ref, e_ref, rl_ref, gqkv_ref, at, PATCHES, features, head_size
            )
            return carry

        lax.fori_loop(0, samples, backward, 0, unroll=3)
        writing += write(here, 8)
        gn = mm_nt(gqkv_ref[...], w_qkv[...])
        z = z_ref[...]
        n1 = (z - jnp.mean(z, axis=-1, keepdims=True)) * s1_ref[...]
        gz = h_ref[...] + normalise_back(gn, n1, s1_ref[...], row(gain1))
        small_ref[0:1, :] += rows_sum(gn * n1)
        small_ref[1:2, :] += rows_sum(gn)
        small_ref[6:7, :] += rows_sum(gz * empty)
        ge_ref[...] += mm(place_ref[:, here], gz.astype(BF16))
        for copy in writing:
            copy.wait()
        return carry

    lax.fori_loop(0, total // rows, one_step, 0)
    ge = ge_ref[...]
    small_ref[7:8, :] = rows_sum(ge)
    geb_ref[...] = ge.astype(BF16)
    gy_ref[...] = mm_nt(geb_ref[...], w_embed[...]).astype(BF16)


def in_vmem(count):
    return [pl.BlockSpec(memory_space=pltpu.VMEM)] * count


def in_hbm():
    return pl.BlockSpec(memory_space=pl.ANY)


def shape(rows, columns, dtype=BF16):
    return jax.ShapeDtypeStruct((rows, columns), dtype)


KERNEL_VMEM = 60 * 2**20


def encoder_forward(x, segments, params):
    rows, d = x.shape[0] // 2, x.shape[1]
    ff = params[7].shape[1]
    outs = [
        (rows, d, BF16),
        (d, rows, BF16),
        (rows, 3 * d, BF16),
        (rows, H_ENC * rows, BF16),
        (rows, d, F32),
        (rows, d, BF16),
        (d, rows, BF16),
        (rows, d, F32),
        (rows, 1, F32),
        (d, rows, BF16),
        (ff, rows, BF16),
        (rows, ff, BF16),
    ]
    more = [(rows, d, F32), (rows, d, BF16), (rows, ff, BF16)]
    args = [x, segments, *params]
    matrices = [w for w in params if w.dtype == BF16]
    return pl.pallas_call(
        encoder_forward_kernel,
        out_shape=[shape(*o) for o in outs],
        in_specs=in_vmem(2) + [in_hbm() if w.dtype == BF16 else in_vmem(1)[0] for w in params],
        out_specs=[in_hbm()] * len(outs),
        scratch_shapes=[pltpu.VMEM((r, w), t) for r, w, t in outs + more]
        + [pltpu.VMEM(w.shape, BF16) for w in matrices]
        + [pltpu.SemaphoreType.DMA((len(matrices),)), pltpu.SemaphoreType.DMA((len(outs),))],
        compiler_params=pltpu.CompilerParams(vmem_limit_bytes=KERNEL_VMEM),
        name="encoder_forward",
    )(*args)


def encoder_backward(x, gy, saved, params):
    gain1, _, w_qkv, w_out, _, gain2, _, w_up, _, w_down, _ = params
    rows, d = gy.shape
    ff = w_up.shape[1]
    outs = [
        shape(rows, d),
        shape(rows, ff),
        shape(rows, d),
        shape(rows, 3 * d),
        shape(8, d, F32),
        shape(1, ff, F32),
    ]
    args = [x, gy, *saved, gain1, w_qkv, w_out, gain2, w_up, w_down]
    return pl.pallas_call(
        encoder_backward_kernel,
        out_shape=outs,
        in_specs=in_vmem(len(args)),
        out_specs=in_vmem(len(outs)),
        scratch_shapes=[pltpu.VMEM((rows, d), F32), pltpu.VMEM((rows, d), BF16)],
        compiler_params=pltpu.CompilerParams(vmem_limit_bytes=KERNEL_VMEM),
        name="encoder_backward",
    )(*args)


def decoder_both(y, segments, orders, g, embed_params, params):
    packed, d_enc = y.shape
    total, d = g.shape[0] // 2, g.shape[1]
    rows = 6 * PATCHES
    ff = params[7].shape[1]
    args = [y, segments, orders, positions(PATCHES, d), g, *embed_params, *params]
    in_specs = in_vmem(4) + [in_hbm()]
    in_specs += [in_hbm() if x.dtype == BF16 else in_vmem(1)[0] for x in args[5:]]
    wide = [ff, ff, d, 3 * d]
    outs = [shape(total, d)] + [shape(d, total)] * 4 + [shape(total, w) for w in wide]
    buffers = [(rows, d, BF16)] + [(d, rows, BF16)] * 4 + [(rows, w, BF16) for w in wide]
    last = [shape(packed, d), shape(packed, d_enc), shape(8, d, F32), shape(1, ff, F32)]
    scratch = [
        (2 * packed, d, BF16),
        (rows, d, F32),
        (rows, 1, F32),
        (rows, H_DEC * PATCHES, BF16),
        (rows, d, F32),
        (rows, d, F32),
        (rows, 1, F32),
        (rows, d, BF16),
        (packed, d, F32),
        (rows, d, BF16),
        (rows, d, BF16),
        (rows, 3 * d, BF16),
        (rows, ff, BF16),
        (total, d, BF16),
        (total, packed, BF16),
        (packed, total, BF16),
        (total, 128, F32),
    ]
    matrices = [x for x in args[5:] if x.dtype == BF16]
    return pl.pallas_call(
        decoder_kernel,
        out_shape=outs + last,
        in_specs=in_specs,
        out_specs=[in_hbm()] * len(outs) + in_vmem(len(last)),
        scratch_shapes=[pltpu.VMEM((r, w), t) for r, w, t in buffers + scratch]
        + [pltpu.VMEM(x.shape, BF16) for x in matrices]
        + [pltpu.SemaphoreType.DMA((k,)) for k in (len(matrices) + 1, len(outs))],
        compiler_params=pltpu.CompilerParams(vmem_limit_bytes=KERNEL_VMEM),
        name="decoder_both",
    )(*args)


MESH = pl.DeviceIdType.MESH
ENC_QKV, ENC_OUT, ENC_UP, ENC_DOWN, EMBED, DEC_QKV, DEC_OUT, DEC_UP, DEC_DOWN = range(9)
GIVE, PAIR, FFN, LN2, GO, ATT, GN, LAST = range(10, 18)
SMALL = -1
ROW_BUP, ROW_DEC_BUP, ROW_DEC, SMALL_ROWS = 6, 10, 16, 24
Z, Y, X, CORE = range(4)
ORDERS = ((X, Y, Z), (Y, X, Z), (X, Z, Y), (Y, Z, X), (Z, X, Y), (Z, Y, X))


class Chunk:
    def __init__(self, name, half, offset, rows, width, first_row=None):
        self.name, self.half, self.offset, self.rows, self.width = name, half, offset, rows, width
        self.first_row, self.turned, self.order = first_row, name == DEC_DOWN, None
        self.decoder = name in (DEC_QKV, DEC_UP, DEC_OUT)

    def columns(self, side):
        return pl.ds(pl.multiple_of(side * self.half + self.offset, 128), self.width)

    def place(self, side):
        if self.turned:
            return (pl.ds(pl.multiple_of(side * self.half + self.offset, 128), self.rows), slice(None))
        if self.first_row is None:
            return (slice(None), self.columns(side))
        return (pl.ds(self.first_row, self.rows), self.columns(side))

    @property
    def bytes(self):
        return 32 * self.rows * self.width

    def loads(self, order):
        if order[0] == Z:
            return (2 * self.bytes, self.bytes / 4, self.bytes / 8)
        if order[1] == Z:
            return (self.bytes, self.bytes, self.bytes / 8)
        return (self.bytes, self.bytes / 2, self.bytes / 2)


LINK_ORDERS = (0, 1, 2, 4, 3, 0, 3, 0, 3, 3, 0, 0, 0, 0, 1)


def make_chunks():
    chunks = [Chunk(ENC_DOWN, 384, 0, 48, 384, 48 * q) for q in range(4)]
    chunks += [Chunk(ENC_UP, 1536, 768 * q, 48, 768) for q in range(2)]
    chunks += [Chunk(ENC_OUT, 384, 0, 48, 384)]
    chunks += [Chunk(ENC_QKV, 1152, 0, 48, 768), Chunk(ENC_QKV, 1152, 768, 48, 384)]
    chunks += [Chunk(EMBED, 256, 0, 48, 256)]
    chunks += [Chunk(DEC_QKV, 768, 0, 32, 768), Chunk(DEC_DOWN, 256, 0, 256, 128)]
    chunks += [Chunk(DEC_UP, 1024, o, 32, 512) for o in (0, 512)]
    chunks += [Chunk(DEC_OUT, 256, 0, 32, 256)]
    for chunk, order in zip(chunks, LINK_ORDERS):
        chunk.order = ORDERS[order]
    return chunks


def make_groups(chunks):
    return [[c] for c in range(len(chunks))]


def product_cost(k, count):
    if k.turned:
        return 5.0
    return k.rows * k.width * (0.9 / 8192 if k.decoder else 0.6 / 18432)


def tasks_in_order(chunks, groups):
    def gives(name):
        found = [(g, chunks[m[0]], len(m)) for g, m in enumerate(groups)]
        kind = PAIR if name == DEC_DOWN else GIVE
        return [(kind, g, product_cost(k, size)) for g, k, size in found if k.name == name]

    tasks = gives(ENC_DOWN)
    tasks += [(FFN, t, 1.7) for t in range(4)] + gives(ENC_UP)
    tasks += [(LN2, 0, 1.0), (GO, 0, 0.9)]
    tasks += [(ATT, g, 1.5) for g in range(6)]
    tasks += gives(ENC_OUT) + gives(ENC_QKV) + gives(EMBED)
    tasks += gives(DEC_QKV) + gives(DEC_DOWN)
    tasks += [(GN, j, 0.9) for j in range(3)] + [(LAST, 0, 1.5)]
    return tasks + gives(DEC_UP) + gives(DEC_OUT)


def decoder_arrays(chunks):
    names = []
    for k in chunks:
        if (k.decoder or k.turned) and k.name not in names:
            names.append(k.name)
    return names


def make_plan(chunks, groups):
    tasks = tasks_in_order(chunks, groups)
    lhs = decoder_arrays(chunks)
    free = [0.0] * 4
    rate = [80e3, 80e3, 80e3, 500e3]
    pending, plan, now, owned = [], [], 2.0, set()

    def send(link, size, latency):
        begin = max(now, free[link])
        free[link] = begin + size / rate[link]
        return free[link] + latency

    def blocked(task):
        if task[0] not in (GIVE, PAIR):
            return False
        name = chunks[groups[task[1]][0]].name
        if name not in lhs[2:]:
            return False
        name = lhs[lhs.index(name) - 2]
        return any(chunks[m[0]].name == name and g not in owned for g, m in enumerate(groups))

    while tasks or pending:
        pending.sort()
        if pending and (pending[0][0] <= now or not tasks or blocked(tasks[0])):
            arrive, stage, c = pending.pop(0)
            now = max(now, arrive)
            plan.append((stage, c))
            if c == SMALL:
                now += 0.1
                if stage < 4:
                    pending.append((now + 2.0, stage + 1, c))
                continue
            members = groups[c] if stage == 1 else [c]
            k = chunks[members[0]]
            if stage == 1:
                owned.add(c)
                now += 0.6 if k.turned else product_cost(k, len(members)) + 0.2 * len(members)
            else:
                now += 0.25
            for c in members:
                k = chunks[c]
                if stage < 4:
                    axis = k.order[stage - 1]
                    latency = 2.0 if axis == Z else 1.5
                    arrive = send(axis, k.loads(k.order)[stage - 1], latency)
                    pending.append((arrive, stage + 1, c))
                elif stage == 4:
                    pending.append((send(CORE, k.bytes / 16, 1.0), 5, c))
            continue
        name, arg, cost = tasks.pop(0)
        plan.append((name, arg))
        now += cost
        if name in (GIVE, PAIR):
            arrive = [send(CORE, chunks[c].bytes, 1.0) for c in groups[arg]]
            pending.append((max(arrive), 1, arg))
        elif name == LAST:
            pending.append((now + 2.0, 1, SMALL))
    return plan


class Ring:
    def __init__(self, sources, slots, semaphores, depth):
        self.copies = [
            pltpu.make_async_copy(source, slot, semaphores())
            for source, slot in zip(sources, slots)
        ]
        self.slots, self.depth, self.at = slots, depth, 0

    def begin(self):
        for copy in self.copies[: self.depth]:
            copy.start()

    def take(self):
        self.copies[self.at].wait()
        return self.slots[self.at]

    def done(self):
        ahead = self.at + self.depth
        if ahead < len(self.copies):
            self.copies[ahead].start()
        self.at += 1


class Names:
    def __init__(self, names, refs):
        self.__dict__.update(zip(names, refs))


LOADS = 96


def finish_kernel(chunks, groups, plan, r):
    n = len(chunks)
    s = lax.axis_index("section")
    d = lax.axis_index("dp")
    here = (d // 4, (d // 2) % 2, d % 2)
    z, y, x = here
    sibling = {"section": 1 - s}
    z_at = [lax.rem(z + k, 4) for k in (1, 2, 3)]
    peers = {
        X: [(1 - x, {"dp": d + 1 - 2 * x})],
        Y: [(1 - y, {"dp": d + 2 - 4 * y})],
        Z: [(p, {"dp": d + 4 * (p - z)}) for p in z_at],
    }
    every = [sibling] + [peer for axis in (X, Y, Z) for _, peer in peers[axis]]

    barrier = pltpu.get_barrier_semaphore()
    for peer in every:
        pl.semaphore_signal(barrier, inc=1, device_id=peer, device_id_type=MESH)

    counter = iter(range(LOADS))

    def semaphore():
        return r.load_sem.at[next(counter)]

    def remote(src, dst, send, recv, peer):
        return pltpu.make_async_remote_copy(
            src_ref=src, dst_ref=dst, send_sem=send, recv_sem=recv, device_id=peer, device_id_type=MESH
        )

    rhs_of = {DEC_QKV: r.gqkv2, DEC_UP: r.gf2, DEC_OUT: r.ga2}
    lhs_of = {DEC_QKV: r.at2, DEC_UP: r.ct2, DEC_OUT: r.ot2, DEC_DOWN: r.gt2}
    tiles, widths, last_use = [], [], {}

    def wide_columns(g, side):
        k, width = chunks[groups[g][0]], sum(chunks[c].width for c in groups[g])
        return pl.ds(pl.multiple_of(side * k.half + k.offset, 128), width)

    for i, (name, arg) in enumerate(plan):
        if name == PAIR:
            tiles += [r.u2.at[:, t * 512 : (t + 1) * 512] for t in range(4)]
            last_use[DEC_DOWN] = i
        elif name in (GIVE, 1) and arg != SMALL and chunks[groups[arg][0]].decoder:
            k = chunks[groups[arg][0]]
            tiles.append(rhs_of[k.name].at[:, wide_columns(arg, 1 - s if name == GIVE else s)])
            last_use[k.name] = i
    lhs_names = decoder_arrays(chunks)
    assert sorted(lhs_names, key=last_use.get) == lhs_names
    rhs_slots = [r.rhs.at[i % 2, :, : tile.shape[1]] for i, tile in enumerate(tiles)]
    rhs = Ring(tiles, rhs_slots, semaphore, 2)
    lhs = Ring([lhs_of[k] for k in lhs_names], [r.lhs.at[i % 2] for i in range(4)], semaphore, 2)
    tokens, d_enc = r.gy.shape
    blocks = []
    for t in range(4):
        at = pl.ds(t * d_enc, d_enc)
        blocks += [r.w_down.at[at, :], r.w_up.at[:, at]]
    blocks.append(r.w_out)
    blocks += [r.w_qkv.at[:, pl.ds(j * d_enc, d_enc)] for j in range(3)]
    weights = Ring(blocks, [r.w.at[i % 4] for i in range(12)], semaphore, 4)
    e_width = 2 * tokens
    e_ring = Ring(
        [r.e.at[:, pl.ds(g * e_width, e_width)] for g in range(6)],
        [r.e_v.at[g % 2] for g in range(6)],
        semaphore,
        2,
    )

    def load(source, target):
        return pltpu.make_async_copy(source, target, semaphore())

    mine = pl.ds(pl.multiple_of(s * tokens, tokens), tokens)
    load_gy, load_slope, load_ut = load(r.gy, r.gy_v), load(r.slope, r.slope_v), load(r.ut, r.ut_v)
    load_ct, load_at, load_ot = load(r.ct, r.ct_v), load(r.at, r.at_v), load(r.ot, r.ot_v)
    load_n2, load_s2, load_qkv = load(r.n2, r.n2_v), load(r.s2, r.s2_v), load(r.qkv, r.qkv_v)
    load_o, load_rl, load_x = load(r.o, r.o_v), load(r.rl, r.rl_v), load(r.x.at[mine, :], r.x_v)
    load_y, load_geb = load(r.y, r.y_v), load(r.geb, r.geb_v)
    load_gy.start()
    load_ut.start()
    load_slope.start()
    weights.begin()
    begun = [
        (load_ct, load_n2, load_s2),
        (load_qkv, load_o, load_rl, e_ring),
        (load_ot, load_at, load_y, load_geb),
        (load_x, lhs, rhs),
    ]

    def begin_some():
        for copy in begun.pop(0) if begun else ():
            copy.begin() if isinstance(copy, Ring) else copy.start()

    half = r.decoded.shape[1] // 2
    give_half = r.decoded.at[:, pl.ds(pl.multiple_of((1 - s) * half, half), half), :]
    decoded_away = remote(give_half, r.decoded_got, r.swap_sem.at[0], r.swap_sem.at[1], sibling)
    gx_columns = d_enc // 2
    gx_half = r.gx.at[:, pl.ds(pl.multiple_of((1 - s) * gx_columns, 128), gx_columns)]
    gx_away = remote(gx_half, r.gx_got, r.swap_sem.at[2], r.swap_sem.at[3], sibling)

    small = r.small
    small[...] = jnp.zeros_like(small)
    small[ROW_DEC : ROW_DEC + 8, : r.small2.shape[1]] = r.small2[...]
    quarter = r.gbup2.shape[1] // 4
    for i in range(4):
        piece = r.gbup2[:, i * quarter : (i + 1) * quarter]
        small[ROW_DEC_BUP + i : ROW_DEC_BUP + i + 1, :quarter] = piece

    pl.semaphore_wait(barrier, len(every))

    copies = {}
    first_slot = (0, 1, 4, 7, 10)

    def chunk_copy(c, slot, src, dst, peer):
        copy = remote(src, dst, r.send_sem.at[c, slot], r.recv_sem.at[c, slot], peer)
        copy.start()
        copies[c, slot] = copy

    sent = set()

    def sent_by(c, slot):
        if (c, slot) not in sent:
            sent.add((c, slot))
            copies[c, slot].wait_send()

    staged = {}

    def staging(c):
        k = chunks[c]
        buffers = r.stage[k.rows, k.width]
        turn = staged.setdefault((k.rows, k.width), [])
        if len(turn) >= len(buffers):
            sent_by(turn[-len(buffers)], 0)
        turn.append(c)
        return buffers[(len(turn) - 1) % len(buffers)]

    def shard(i):
        return (i // 4, (i // 2) % 2, i % 2)

    waited = set()

    def arrived(copy):
        if id(copy) not in waited:
            waited.add(id(copy))
            copy.wait()

    def product(g, side):
        k, columns = chunks[groups[g][0]], wide_columns(g, side)
        if k.decoder:
            return mm(lhs.slots[lhs_names.index(k.name)][...], rhs.take()[...])
        if k.name == EMBED:
            arrived(load_y)
            arrived(load_geb)
            return mm_tn(r.y_v[...], r.geb_v[:, columns])
        if k.name == ENC_DOWN:
            arrived(load_ut)
            arrived(load_gy)
            at = [i * 192 + k.first_row for i in range(16)]
            left = jnp.concatenate([r.ut_v[i : i + k.rows, :] for i in at], axis=0)
            return mm(left, r.gy_v[:, columns])
        if k.name == ENC_UP:
            arrived(load_ct)
            return mm(r.ct_v[...], r.slope_v[:, columns])
        if k.name == ENC_OUT:
            arrived(load_ot)
            return mm(r.ot_v[...], r.ga_v[:, columns])
        arrived(load_at)
        return mm(r.at_v[...], r.qkv_v[:, columns])

    def after_product(i, g):
        k = chunks[groups[g][0]]
        if k.decoder:
            rhs.done()
            if last_use[k.name] == i:
                lhs.done()

    def wait_lhs(k):
        if k.name in lhs_names:
            arrived(lhs.copies[lhs_names.index(k.name)])

    def give(i, g):
        members = groups[g]
        wait_lhs(chunks[members[0]])
        buffers = [staging(c) for c in members]
        value = product(g, 1 - s).astype(BF16)
        for m, (c, buffer) in enumerate(zip(members, buffers)):
            k = chunks[c]
            part = value[:, m * k.width : (m + 1) * k.width]
            for j in range(16):
                buffer[shard(j)] = part[j * k.rows : (j + 1) * k.rows]
            chunk_copy(c, 0, buffer, r.acc[c], sibling)
        after_product(i, g)
        begin_some()

    def pair(i, g):
        both = groups[g]
        wait_lhs(chunks[both[0]])
        left = lhs.slots[lhs_names.index(DEC_DOWN)]
        side_rows = chunks[both[0]].half
        buffers = [staging(c) for c in both]
        for t in range(4):
            tile = rhs.take()
            for side, targets in ((1 - s, buffers), (s, [r.acc[c] for c in both])):
                at = pl.ds(pl.multiple_of(side * side_rows, side_rows), side_rows)
                value = mm(left[at, :], tile[...]).astype(BF16)
                for c, target in zip(both, targets):
                    k = chunks[c]
                    rows = slice(k.offset, k.offset + k.rows)
                    for j in range(4):
                        target[shard(4 * t + j)] = value[rows, j * k.width : (j + 1) * k.width]
            rhs.done()
        lhs.done()
        for c, buffer in zip(both, buffers):
            chunk_copy(c, 0, buffer, r.got[c], sibling)

    def spots(k, stage):
        fixed = {axis: here[axis] for axis in k.order[: stage - 1]}
        return [fixed.get(axis, slice(None)) for axis in (Z, Y, X)]

    def send_stage(c, stage):
        k = chunks[c]
        axis = k.order[stage - 1]
        for j, (coordinate, peer) in enumerate(peers[axis]):
            at = spots(k, stage)
            at[axis] = coordinate
            src = r.acc[c].at[tuple(at)]
            chunk_copy(c, first_slot[stage] + j, src, r.recv[stage - 1][c].at[j], peer)

    def got_stage(c, stage):
        k = chunks[c]
        count = len(peers[k.order[stage - 1]])
        for j in range(count):
            copies[c, first_slot[stage] + j].wait_recv()
        return count

    def add_stage(c, stage):
        k, acc, got = chunks[c], r.acc[c], r.recv[stage - 1][c]
        count = got_stage(c, stage)
        left = [axis for axis in (Z, Y, X) if axis not in k.order[:stage]]
        sizes = [(4, 2, 2)[axis] for axis in left]
        for j in range(math.prod(sizes)):
            place, rest = {}, j
            for axis, size in reversed(list(zip(left, sizes))):
                place[axis] = rest % size
                rest //= size
            at = tuple(place.get(axis, here[axis]) for axis in (Z, Y, X))
            index = tuple(place[axis] for axis in left)
            if count == 1:
                acc[at] = acc[at] + got[(0,) + index]
            else:
                total = acc[at].astype(F32)
                for m in range(count):
                    total = total + got[(m,) + index].astype(F32)
                acc[at] = total.astype(BF16)

    def stage1(i, g):
        members = groups[g]
        for c in members:
            copies[c, 0].wait_recv()
        if chunks[members[0]].turned:
            for c in members:
                acc = r.acc[c]
                for j in range(16):
                    acc[shard(j)] = acc[shard(j)] + r.got[c][shard(j)]
                send_stage(c, 1)
            return
        value = product(g, s)
        for m, c in enumerate(members):
            k, acc = chunks[c], r.acc[c]
            wide = value[:, m * k.width : (m + 1) * k.width]
            for j in range(16):
                part = wide[j * k.rows : (j + 1) * k.rows]
                acc[shard(j)] = (part + acc[shard(j)].astype(F32)).astype(BF16)
            send_stage(c, 1)
        after_product(i, g)

    def stage2(i, c):
        add_stage(c, 1)
        send_stage(c, 2)

    def stage3(i, c):
        add_stage(c, 2)
        send_stage(c, 3)

    def stage4(i, c):
        k = chunks[c]
        total = r.acc[c][here].astype(F32)
        for j in range(got_stage(c, 3)):
            total = total + r.recv[2][c][j].astype(F32)
        out = r.out[k.name]
        out[k.place(s)] = total.astype(BF16)
        final = out.at[k.place(s)]
        chunk_copy(c, 10, final, final, sibling)

    def stage5(i, c):
        copies[c, 10].wait_recv()

    small_copies = []

    def small_copy(source, peer):
        slot = len(small_copies)
        copy = remote(
            source, r.small_got.at[slot], r.small_sem.at[0, slot], r.small_sem.at[1, slot], peer
        )
        copy.start()
        small_copies.append(copy)

    def small_stage(stage):
        if stage < 4:
            small_copies[stage - 1].wait()
            total = small[...] + r.small_got[stage - 1]
            if stage < 3:
                small[...] = total
                small_copy(small, peers[X if stage == 1 else Y][0][1])
            else:
                r.small_sum[...] = total
                for _, peer in peers[Z]:
                    small_copy(r.small_sum, peer)
        else:
            total = r.small_sum[...]
            for j in range(3):
                small_copies[3 + j].wait()
                total = total + r.small_got[3 + j]
            r.out_small[...] = total

    def ffn(i, t):
        if t == 0:
            arrived(load_gy)
            load_slope.wait()
        at = slice(t * d_enc, (t + 1) * d_enc)
        gu = mm_nt(r.gy_v[...], weights.take()[...])
        weights.done()
        gf = (gu * r.slope_v[:, at].astype(F32)).astype(BF16)
        r.slope_v[:, at] = gf
        small[ROW_BUP + t : ROW_BUP + t + 1, :] = rows_sum(gf.astype(F32))
        gc = mm_nt(gf, weights.take()[...])
        weights.done()
        r.sum_v[...] = gc if t == 0 else r.sum_v[...] + gc

    def ln2(i, _):
        load_n2.wait()
        load_s2.wait()
        g, gc, n2 = r.gy_v[...].astype(F32), r.sum_v[...], r.n2_v[...]
        gh = g + normalise_back(gc, n2, r.s2_v[...], row(r.gain2))
        small[2:3, :] = rows_sum(gh)
        small[3:4, :] = rows_sum(gc * n2)
        small[4:5, :] = rows_sum(gc)
        small[5:6, :] = rows_sum(g)
        r.n2_v[...] = gh
        r.ga_v[...] = gh.astype(BF16)

    def go(i, _):
        r.go_v[...] = mm_nt(r.ga_v[...], weights.take()[...]).astype(BF16)
        weights.done()

    def att(i, g):
        if g == 0:
            for copy in (load_qkv, load_o, load_rl):
                copy.wait()
        at = slice(g * 128, (g + 1) * 128)
        parts = [slice(j * d_enc + g * 128, j * d_enc + (g + 1) * 128) for j in range(3)]
        q, k, v = (r.qkv_v[:, part] for part in parts)
        grads = attention_backward_group(
            q, k, v, e_ring.take()[...], r.go_v[:, at], r.o_v[:, at], r.rl_v[:, at],
            d_enc // H_ENC,
        )
        e_ring.done()
        for part, grad in zip(parts, grads):
            r.qkv_v[:, part] = grad

    def gn(i, j):
        part = mm_nt(r.qkv_v[:, j * d_enc : (j + 1) * d_enc], weights.take()[...])
        weights.done()
        r.sum_v[...] = part if j == 0 else r.sum_v[...] + part

    def last(i, _):
        load_x.wait()
        n1, s1 = normalise(r.x_v[...].astype(F32))
        total = r.sum_v[...]
        small[0:1, :] = rows_sum(total * n1)
        small[1:2, :] = rows_sum(total)
        small_copy(small, sibling)
        gx = r.n2_v[...] + normalise_back(total, n1, s1, row(r.gain1))
        r.gx[...] = gx.astype(BF16)
        gx_away.start()
        decoded_away.start()

    run = {
        GIVE: give, PAIR: pair, FFN: ffn, LN2: ln2, GO: go, ATT: att, GN: gn, LAST: last,
        1: stage1, 2: stage2, 3: stage3, 4: stage4, 5: stage5,
    }
    for i, (name, arg) in enumerate(plan):
        if arg == SMALL:
            small_stage(name)
        else:
            run[name](i, arg)

    for c, slot in copies:
        sent_by(c, slot)
    gx_away.wait()
    decoded_away.wait()


def finish_buffers(chunks, rows, d, ff, dec_total, dec):
    def of(dtype, *dims):
        return (dims, dtype)

    return dict(
        y_v=of(BF16, rows, d),
        geb_v=of(BF16, rows, dec),
        gy_v=of(BF16, rows, d),
        slope_v=of(BF16, rows, ff),
        n2_v=of(F32, rows, d),
        s2_v=of(F32, rows, 1),
        qkv_v=of(BF16, rows, 3 * d),
        o_v=of(BF16, rows, d),
        rl_v=of(F32, rows, d),
        x_v=of(BF16, rows, d),
        ga_v=of(BF16, rows, d),
        go_v=of(BF16, rows, d),
        sum_v=of(F32, rows, d),
        ut_v=of(BF16, ff, rows),
        ct_v=of(BF16, d, rows),
        at_v=of(BF16, d, rows),
        ot_v=of(BF16, d, rows),
        e_v=of(BF16, 2, rows, 2 * rows),
        w=of(BF16, 4, d, d),
        lhs=of(BF16, 2, dec, dec_total),
        rhs=of(BF16, 2, dec_total, 768),
        small=of(F32, SMALL_ROWS, d),
        small_sum=of(F32, SMALL_ROWS, d),
        small_got=of(F32, 6, SMALL_ROWS, d),
    )


def finish(acts):
    enc, dec = acts["enc"], acts["dec"]
    gain1, _, w_qkv, w_out, _, gain2, _, w_up, _, w_down, _ = enc["params"]
    qkv, e, rl, o, n2, s2, slope = acts["saved"]
    given = dict(
        x=acts["x"], y=acts["y"], gy=acts["gy"], geb=acts["geb"], qkv=qkv, e=e, rl=rl, o=o, n2=n2,
        s2=s2, slope=slope, at=enc["at"], ot=enc["ot"], ct=enc["ct"], ut=enc["ut"], at2=dec["at"], ot2=dec["ot"],
        ct2=dec["ct"], gt2=dec["gt"], u2=dec["u"], gf2=dec["gf"], ga2=dec["ga"],
        gqkv2=dec["gqkv"], w_qkv=w_qkv, w_out=w_out, w_up=w_up, w_down=w_down,
        decoded=acts["decoded"].reshape(SAMP_MB, PATCHES, -1),
    )
    n_hbm = len(given)
    given.update(small2=acts["small2"], gbup2=acts["gbup2"], gain1=gain1, gain2=gain2)
    rows, d = acts["gy"].shape
    ff = w_up.shape[1]
    dec_d, dec_total = dec["at"].shape
    dec_ff = dec["u"].shape[1]
    chunks = make_chunks()
    n = len(chunks)
    groups = make_groups(chunks)
    plan = make_plan(chunks, groups)

    dims = {
        ENC_QKV: (d, 3 * d), ENC_OUT: (d, d), ENC_UP: (d, ff), ENC_DOWN: (ff, d),
        EMBED: (d, dec_d), DEC_QKV: (dec_d, 3 * dec_d), DEC_OUT: (dec_d, dec_d),
        DEC_UP: (dec_d, dec_ff), DEC_DOWN: (dec_ff, dec_d),
    }
    big = [
        shape(dims[k][1], dims[k][0] // 16) if k == DEC_DOWN else shape(dims[k][0] // 16, dims[k][1])
        for k in range(9)
    ]
    outs = dict(
        out_small=shape(SMALL_ROWS, d, F32),
        decoded_got=jax.ShapeDtypeStruct((SAMP_MB, PATCHES // 2, dec_d), BF16),
        gx=shape(rows, d),
        gx_got=shape(rows, d // 2),
    )
    single = finish_buffers(chunks, rows, d, ff, dec_total, dec_d)
    left = (4, 2, 2)
    lists = [[], [], [], [], []]
    for k in chunks:
        block = (k.rows, k.width)
        lists[0].append((left + block, BF16))
        if k.turned:
            lists[1].append((left + block, BF16))
        for stage in range(3):
            rest = [left[axis] for axis in (Z, Y, X) if axis not in k.order[: stage + 1]]
            count = 3 if k.order[stage] == Z else 1
            lists[2 + stage].append(((count, *rest, *block), BF16))
    blocks = sorted({(k.rows, k.width) for k in chunks})
    slots = [2 if block == (48, 384) else 1 for block in blocks]
    lists.append([(left + block, BF16) for block, m in zip(blocks, slots) for _ in range(m)])
    semaphores = dict(
        load_sem=(LOADS,), send_sem=(n, 11), recv_sem=(n, 11), small_sem=(2, 6), swap_sem=(4,)
    )

    def kernel(*refs):
        refs = list(refs)

        def take(count):
            taken = refs[:count]
            del refs[:count]
            return taken

        names = list(given) + list(outs)
        r = Names(names, take(len(names)))
        r.out = take(9)
        r.__dict__.update(zip(single, take(len(single))))
        r.acc = take(n)
        r.got = dict(zip([c for c, k in enumerate(chunks) if k.turned], take(len(lists[1]))))
        r.recv = [take(n) for _ in range(3)]
        r.stage = {block: take(m) for block, m in zip(blocks, slots)}
        r.__dict__.update(zip(semaphores, take(len(semaphores))))
        finish_kernel(chunks, groups, plan, r)

    flat = list(single.values()) + [b for group in lists for b in group]
    results = pl.pallas_call(
        kernel,
        out_shape=list(outs.values()) + big,
        in_specs=[in_hbm()] * n_hbm + in_vmem(len(given) - n_hbm),
        out_specs=in_vmem(len(outs) + 9),
        scratch_shapes=[pltpu.VMEM(*b) for b in flat]
        + [pltpu.SemaphoreType.DMA(v) for v in semaphores.values()],
        compiler_params=pltpu.CompilerParams(
            collective_id=1, has_side_effects=True, vmem_limit_bytes=FINISH_VMEM
        ),
        name="finish",
    )(*given.values())
    return write_outputs(results, given["decoded"], dims)


FINISH_VMEM = 62 * 2**20


def write_kernel(small, decoded_got, gx_own, gx_got, *refs):
    big, decoded_own = refs[:9], refs[9]
    decoded, gx, *totals = refs[10:]
    s = lax.axis_index("section")
    half = decoded.shape[1]
    samples, rows, columns = decoded_own.shape[0], gx_own.shape[0], gx.shape[1]
    own = decoded_own[:, pl.ds(pl.multiple_of(s * half, half), half), :]
    for side, part in ((s, own), (1 - s, decoded_got[...])):
        decoded[pl.ds(side * samples, samples)] = part
    own = gx_own[:, pl.ds(pl.multiple_of(s * columns, 128), columns)]
    for side, part in ((s, own), (1 - s, gx_got[...])):
        gx[pl.ds(pl.multiple_of(side * rows, rows), rows), :] = part
    d = lax.axis_index("dp")
    wide, narrow = small.shape[1], big[DEC_OUT].shape[1]

    def piece(out, line, lanes, position):
        size = out.shape[0]
        value = small[pl.ds(line, 1), :lanes]
        value = pltpu.roll(value, lax.rem(lanes - position * size, lanes), 1)
        out[...] = value[:, :size].reshape(size)

    def matrix(out, name):
        value = big[name][...].astype(F32)
        out[...] = jnp.transpose(value) if name == DEC_DOWN else value

    def block(outs, first_row, bup_row, lanes, names):
        for i, out in zip((0, 1, None, None, 2, 3, 4, None, None, None, 5), outs):
            if i is not None:
                piece(out, first_row + i, lanes, d)
        piece(outs[8], bup_row + d // 4, lanes, d % 4)
        for at, name in zip((2, 3, 7, 9), names):
            matrix(outs[at], name)

    block(totals[:11], 0, ROW_BUP, wide, (ENC_QKV, ENC_OUT, ENC_UP, ENC_DOWN))
    matrix(totals[11], EMBED)
    piece(totals[12], ROW_DEC + 7, narrow, d)
    piece(totals[13], ROW_DEC + 6, narrow, d)
    block(totals[14:], ROW_DEC, ROW_DEC_BUP, narrow, (DEC_QKV, DEC_OUT, DEC_UP, DEC_DOWN))


def write_outputs(results, decoded_own, dims):
    def vector(size):
        return jax.ShapeDtypeStruct((size // 16,), F32)

    def matrix(name):
        return shape(dims[name][0] // 16, dims[name][1], F32)

    def block(qkv, out, up, down):
        d, ff = dims[up]
        return [
            vector(d), vector(d), matrix(qkv), matrix(out), vector(d), vector(d), vector(d),
            matrix(up), vector(ff), matrix(down), vector(d),
        ]

    samples, half, width = results[1].shape
    rows, columns = results[3].shape
    out_shape = [
        jax.ShapeDtypeStruct((2 * samples, half, width), BF16),
        shape(2 * rows, columns),
        *block(ENC_QKV, ENC_OUT, ENC_UP, ENC_DOWN),
        matrix(EMBED),
        vector(width),
        vector(width),
        *block(DEC_QKV, DEC_OUT, DEC_UP, DEC_DOWN),
    ]
    return tuple(
        pl.pallas_call(
            write_kernel,
            out_shape=out_shape,
            in_specs=in_vmem(len(results) + 1),
            out_specs=in_vmem(len(out_shape)),
            compiler_params=pltpu.CompilerParams(vmem_limit_bytes=KERNEL_VMEM),
            name="write_outputs",
        )(*results, decoded_own)
    )


def reduce_plain(arrays, section_index):
    first = section_index == 0
    results = []
    for a in arrays:
        half = a.shape[1] // 2
        keep = lax.dynamic_slice_in_dim(a, section_index * half, half, 1)
        give = lax.dynamic_slice_in_dim(a, (1 - section_index) * half, half, 1)
        got = swapped(give, "section", 0)
        chip = (keep.astype(jnp.float32) + got.astype(jnp.float32)).astype(jnp.bfloat16)
        mine = lax.psum_scatter(chip, "dp", scatter_dimension=0, tiled=True)
        other = swapped(mine, "section", 0)
        whole = jnp.concatenate(
            [jnp.where(first, mine, other), jnp.where(first, other, mine)], axis=1
        )
        results.append(whole.astype(jnp.float32))
    return results


def finish_plain(acts, section_index):
    x, gy, seg_saved, enc, dec = acts["x"], acts["gy"], acts["saved"], acts["enc"], acts["dec"]
    gx, gf1, ga1, gqkv1, small1, gbup1 = encoder_backward(x, gy, seg_saved, enc["params"])
    small2, gbup2 = acts["small2"], acts["gbup2"]
    grads = (
        small1[0], small1[1], mm(enc["at"], gqkv1).astype(BF16), mm(enc["ot"], ga1).astype(BF16), small1[2],
        small1[3], small1[4], mm(enc["ct"], gf1).astype(BF16), gbup1[0], mm(enc["ut"], gy).astype(BF16),
        small1[5],
        weight_grad(acts["y"], acts["geb"]), small2[7], small2[6],
        small2[0], small2[1], mm(dec["at"], dec["gqkv"]).astype(BF16),
        mm(dec["ot"], dec["ga"]).astype(BF16), small2[2], small2[3], small2[4],
        mm(dec["ct"], dec["gf"]).astype(BF16), gbup2[0],
        jnp.transpose(mm(dec["gt"], dec["u"])).astype(BF16), small2[5],
    )
    groups = lax.axis_size("dp")
    big = reduce_plain([g for g in grads if g.ndim == 2], section_index)
    flat = jnp.concatenate([g.reshape(groups, -1) for g in grads if g.ndim == 1], axis=1)
    line = lax.psum_scatter(flat, ("dp"), scatter_dimension=0, tiled=True)
    line = lax.psum(line, "section")[0]
    totals, at = [], 0
    for g in grads:
        if g.ndim == 2:
            totals.append(big.pop(0))
        else:
            size = g.shape[0] // groups
            totals.append(line[at : at + size])
            at += size
    decoded = acts["decoded"].reshape(SAMP_MB, PATCHES, -1)
    first = section_index == 0

    def halves(whole):
        half = whole.shape[1] // 2
        keep = lax.dynamic_slice_in_dim(whole, section_index * half, half, 1)
        give = lax.dynamic_slice_in_dim(whole, (1 - section_index) * half, half, 1)
        got = swapped(give, "section", 0)
        return jnp.concatenate([jnp.where(first, keep, got), jnp.where(first, got, keep)])

    return (halves(decoded), halves(gx), *totals)


def shards(
    patches,
    segment_ids,
    patch_order,
    encoder_gain1,
    encoder_bias1,
    encoder_qkv,
    encoder_out,
    encoder_out_bias,
    encoder_gain2,
    encoder_bias2,
    encoder_up,
    encoder_up_bias,
    encoder_down,
    encoder_down_bias,
    embed_weight,
    embed_bias,
    mask_token,
    decoder_gain1,
    decoder_bias1,
    decoder_qkv,
    decoder_out,
    decoder_out_bias,
    decoder_gain2,
    decoder_bias2,
    decoder_up,
    decoder_up_bias,
    decoder_down,
    decoder_down_bias,
    cotangent,
):
    enc_params = (
        encoder_gain1,
        encoder_bias1,
        encoder_qkv,
        encoder_out,
        encoder_out_bias,
        encoder_gain2,
        encoder_bias2,
        encoder_up,
        encoder_up_bias,
        encoder_down,
        encoder_down_bias,
    )
    embed_params = (embed_weight, embed_bias, mask_token)
    dec_params = (
        decoder_gain1,
        decoder_bias1,
        decoder_qkv,
        decoder_out,
        decoder_out_bias,
        decoder_gain2,
        decoder_bias2,
        decoder_up,
        decoder_up_bias,
        decoder_down,
        decoder_down_bias,
    )
    section_index = lax.axis_index("section")
    y, at1, qkv, e, rl, o1, ot1, n2, s2, ct1, ut1, slope = encoder_forward(
        patches, segment_ids, enc_params
    )
    g = cotangent.reshape(-1, DECODER_WIDTH)
    decoded, at2, ot2, ct2, gt2, u2, gf2, ga2, gqkv2, geb, gy, small2, gbup2 = decoder_both(
        y, segment_ids, patch_order, g, embed_params, dec_params
    )
    acts = dict(
        x=patches,
        y=y,
        gy=gy,
        geb=geb,
        decoded=decoded,
        small2=small2,
        gbup2=gbup2,
        saved=(qkv, e, rl, o1, n2, s2, slope),
        enc=dict(at=at1, ot=ot1, ct=ct1, ut=ut1, params=enc_params),
        dec=dict(at=at2, ot=ot2, ct=ct2, gt=gt2, u=u2, gf=gf2, ga=ga2, gqkv=gqkv2),
    )
    if lax.axis_size("dp") == 16:
        return finish(acts)
    return finish_plain(acts, section_index)


def solution(mesh):
    in_specs = (
        P("dp", None),
        P("dp", None),
        P("dp", None),
        P(),
        P(),
        P(),
        P(),
        P(),
        P(),
        P(),
        P(),
        P(),
        P(),
        P(),
        P(),
        P(),
        P(),
        P(),
        P(),
        P(),
        P(),
        P(),
        P(),
        P(),
        P(),
        P(),
        P(),
        P(),
        P("dp", None, None),
    )
    out_specs = (
        P("dp", "section", None),
        P("dp", "section"),
        P("dp"),
        P("dp"),
        P("dp", None),
        P("dp", None),
        P("dp"),
        P("dp"),
        P("dp"),
        P("dp", None),
        P("dp"),
        P("dp", None),
        P("dp"),
        P("dp", None),
        P("dp"),
        P("dp"),
        P("dp"),
        P("dp"),
        P("dp", None),
        P("dp", None),
        P("dp"),
        P("dp"),
        P("dp"),
        P("dp", None),
        P("dp"),
        P("dp", None),
        P("dp"),
    )
    return jax.shard_map(shards, mesh=mesh, in_specs=in_specs, out_specs=out_specs, check_vma=False)
```

```python
import functools
import math

import jax
import jax.numpy as jnp
import numpy as np
from jax import lax
from jax.experimental import pallas as pl
from jax.experimental.pallas import tpu as pltpu
from jax.sharding import PartitionSpec as P

H_ENC = 12
DECODER_WIDTH = 512
H_DEC = 16
PATCHES = 128
SAMP_MB = 12


EPSILON = 1e-06
MASKED = -1e30


def swapped(block, axis, apart):
    count = lax.axis_size(axis)
    route = []
    for low in range(count):
        high = low | 1 << apart
        if high != low and high < count:
            route += [(low, high), (high, low)]
    return lax.ppermute(block, axis, route)


def positions(count, features):
    column = np.arange(features)
    rate = np.exp(-math.log(10000.0) * (2 * (column // 2)) / features)
    angles = np.arange(count)[:, None] * rate[None, :]
    return np.where(column % 2 == 0, np.sin(angles), np.cos(angles)).astype(np.float32)


def weight_grad(left_side, grads):
    return lax.dot_general(
        left_side, grads, (((0,), (0,)), ((), ())), preferred_element_type=jnp.float32
    ).astype(jnp.bfloat16)


BF16 = jnp.bfloat16
F32 = jnp.float32


def mm(left, right):
    return lax.dot_general(left, right, (((1,), (0,)), ((), ())), preferred_element_type=F32)


def mm_nt(left, right):
    return lax.dot_general(left, right, (((1,), (1,)), ((), ())), preferred_element_type=F32)


def mm_tn(left, right):
    return lax.dot_general(left, right, (((0,), (0,)), ((), ())), preferred_element_type=F32)


def normalise(x):
    center = x - jnp.mean(x, axis=-1, keepdims=True)
    scale = lax.rsqrt(jnp.mean(center * center, axis=-1, keepdims=True) + EPSILON)
    return center * scale, scale


def normalise_back(grad, n, scale, gain):
    gn = grad * gain
    mean_gn = jnp.mean(gn, axis=-1, keepdims=True)
    mean_gnn = jnp.mean(gn * n, axis=-1, keepdims=True)
    return (gn - mean_gn - n * mean_gnn) * scale


def rows_sum(x):
    return jnp.sum(x, axis=0, keepdims=True)


def gelu_both(f):
    c0, c1 = math.sqrt(2.0 / math.pi), 0.044715
    square = f * f
    half = 0.5 + 0.5 * jnp.tanh(f * (c0 + (c0 * c1) * square))
    u = f * half
    return u, half + u * (1.0 - half) * (2.0 * c0 + (6.0 * c0 * c1) * square)


def lanes(start, size):
    return slice(start, start + size) if isinstance(start, int) else pl.ds(pl.multiple_of(start, 128), size)


def lane_masks(head_size):
    lane = lax.broadcasted_iota(jnp.int32, (1, 128), 1)
    return [
        jnp.where((lane >= h * head_size) & (lane < (h + 1) * head_size), 1.0, 0.0).astype(BF16)
        for h in range(128 // head_size)
    ]


def stacked(x, masks):
    return jnp.concatenate([x * m for m in masks], axis=0)


def stacked_ones(x, masks, value):
    return jnp.concatenate(
        [jnp.broadcast_to(m * jnp.asarray(value, BF16), x.shape) for m in masks], axis=0
    )


def attention_forward(
    qkv_ref, o_ref, e_ref, rl_ref, rows, tokens, features, head_size, mask_ref, g
):
    masks = lane_masks(head_size)
    per_group = len(masks)
    factor = head_size ** (-0.5) * math.log2(math.e)
    q, k, v = (qkv_ref[rows, lanes(j * features + g * 128, 128)] for j in range(3))
    scores = mm_nt(q, stacked(k, masks))
    parts = []
    for h in range(per_group):
        part = scores[:, h * tokens : (h + 1) * tokens]
        if mask_ref is not None:
            part = jnp.where(mask_ref[...] > 0.0, part, MASKED)
        top = jnp.max(part, axis=-1, keepdims=True)
        parts.append(jnp.exp2((part - top) * factor).astype(BF16))
    e = jnp.concatenate(parts, axis=1)
    width = per_group * tokens
    e_ref[rows, lanes(g * width, width)] = e
    both = mm(e, jnp.concatenate([stacked(v, masks), stacked_ones(v, masks, 1.0)], axis=1))
    rl = 1.0 / both[:, 128:]
    rl_ref[rows, lanes(g * 128, 128)] = rl
    o_ref[rows, lanes(g * 128, 128)] = (both[:, :128] * rl).astype(BF16)


def attention_backward_group(q, k, v, e, go, o, rl, head_size):
    masks = lane_masks(head_size)
    per_group, tokens = len(masks), q.shape[0]
    scaling = head_size ** (-0.5)
    go = go.astype(F32) * rl
    go_low = go.astype(BF16)
    inner = (go * o.astype(F32)).astype(BF16)
    left = jnp.concatenate([go_low, inner], axis=1)
    right = jnp.concatenate([stacked(v, masks), stacked_ones(v, masks, -1.0)], axis=1)
    gs = (e.astype(F32) * mm_nt(left, right)).astype(BF16)

    def diagonal(wide):
        return jnp.concatenate(
            [
                wide[h * head_size : (h + 1) * head_size, h * tokens : (h + 1) * tokens]
                for h in range(per_group)
            ],
            axis=0,
        )

    gq = mm(gs, stacked(k, masks)) * scaling
    gk = jnp.transpose(diagonal(mm_tn(q, gs)) * scaling)
    gv = jnp.transpose(diagonal(mm_tn(go_low, e)))
    return gq.astype(BF16), gk.astype(BF16), gv.astype(BF16)


def attention_backward(
    qkv_ref, go_ref, o_ref, e_ref, rl_ref, gqkv_ref, rows, tokens, features, head_size, g
):
    width = 128 // head_size * tokens
    at = lanes(g * 128, 128)
    spots = [lanes(j * features + g * 128, 128) for j in range(3)]
    q, k, v = (qkv_ref[rows, spot] for spot in spots)
    e = e_ref[rows, lanes(g * width, width)]
    grads = attention_backward_group(
        q, k, v, e, go_ref[rows, at], o_ref[rows, at], rl_ref[rows, at], head_size
    )
    for spot, grad in zip(spots, grads):
        gqkv_ref[rows, spot] = grad


def tiles(extent, size, body):
    def step(t, carry):
        body(pl.ds(pl.multiple_of(t * size, size), size))
        return carry

    lax.fori_loop(0, extent // size, step, 0)


def feed_forward(c_ref, up_ref, bup_ref, u_ref, slope_ref, tile, ut_ref=None):
    def body(at):
        f = mm(c_ref[...], up_ref[:, at]) + bup_ref[at].reshape(1, tile)
        u, slope = gelu_both(f)
        u = u.astype(BF16)
        u_ref[:, at] = u
        slope_ref[:, at] = slope.astype(BF16)
        if ut_ref is not None:
            ut_ref[at, :] = jnp.transpose(u)

    tiles(up_ref.shape[1], tile, body)


def feed_forward_back(gm_ref, down_ref, slope_ref, gf_ref, gbup_ref, tile):
    def body(at):
        gu = mm_nt(gm_ref[...], down_ref[at, :])
        gf = (gu * slope_ref[:, at].astype(F32)).astype(BF16)
        gf_ref[:, at] = gf
        gbup_ref[:, at] += rows_sum(gf.astype(F32))

    tiles(down_ref.shape[0], tile, body)


def project(left_ref, right_ref, out_ref, tile, bias_ref=None, more_ref=None):
    def body(at):
        value = mm(left_ref[...], right_ref[:, at])
        if bias_ref is not None:
            value = value + bias_ref[at].reshape(1, tile)
        if more_ref is not None:
            value = more_ref[:, at].astype(F32) + value
        out_ref[:, at] = value.astype(out_ref.dtype)

    tiles(right_ref.shape[1], tile, body)


def project_back(left_ref, right_ref, out_ref, tile):
    def body(at):
        out_ref[:, at] = mm_nt(left_ref[...], right_ref[at, :]).astype(out_ref.dtype)

    tiles(right_ref.shape[0], tile, body)


def row(ref):
    return ref[...].reshape(1, -1)


def segment_mask(seg_ref, section):
    seg = seg_ref[pl.ds(section, 1), :].astype(F32)
    rows = seg.shape[1]
    column = jnp.transpose(jnp.broadcast_to(seg, (128, rows)))
    return jnp.concatenate([column] * (rows // 128), axis=1) == seg


class Writer:
    def __init__(self, semaphores):
        self.semaphores, self.copies = semaphores, []

    def start(self, source, target):
        copy = pltpu.make_async_copy(source, target, self.semaphores.at[len(self.copies)])
        copy.start()
        self.copies.append(copy)

    def wait(self):
        for copy in self.copies:
            copy.wait()


def encoder_forward_kernel(
    x_ref, seg_ref,
    gain1, bias1, w_qkv, w_out, b_out, gain2, bias2, w_up, b_up, w_down, b_down,
    *refs,
):
    outs, scratch = refs[:12], refs[12:24]
    y_ref, at_ref, qkv_ref, e_ref, rl_ref, o_ref, ot_ref, n2_ref, s2_ref, ct_ref, ut_ref, slope_ref = scratch
    h_ref, c_ref, u_ref, mask_ref, qkv_v, out_v, up_v, down_v, sem, out_sem = refs[24:]
    target = {id(v): o for v, o in zip(scratch, outs)}
    writer = Writer(out_sem)

    def write(*done):
        for v in done:
            writer.start(v, target[id(v)])

    tokens, features = y_ref.shape
    pairs = ((w_qkv, qkv_v), (w_out, out_v), (w_up, up_v), (w_down, down_v))
    loads = [pltpu.make_async_copy(w, v, sem.at[i]) for i, (w, v) in enumerate(pairs)]
    for load in loads:
        load.start()
    section = lax.axis_index("section")

    def first_norm(at):
        x = x_ref[pl.ds(pl.multiple_of(section * tokens + at.start, 128), 128), :].astype(F32)
        h_ref[at, :] = x
        n1, _ = normalise(x)
        a = (n1 * row(gain1) + row(bias1)).astype(BF16)
        c_ref[at, :] = a
        at_ref[:, at] = jnp.transpose(a)

    tiles(tokens, 128, first_norm)
    mask_ref[...] = jnp.where(segment_mask(seg_ref, section), 1.0, 0.0)
    loads[0].wait()
    project(c_ref, qkv_v, qkv_ref, 256)
    write(at_ref, qkv_ref)

    def group(g, carry):
        attention_forward(
            qkv_ref, o_ref, e_ref, rl_ref, slice(None), tokens, features, features // H_ENC,
            mask_ref, g,
        )
        ot_ref[lanes(g * 128, 128), :] = jnp.transpose(o_ref[:, lanes(g * 128, 128)])
        return carry

    lax.fori_loop(0, features // 128, group, 0)
    write(e_ref, rl_ref, o_ref, ot_ref)
    loads[1].wait()
    project(o_ref, out_v, h_ref, 256, b_out, h_ref)

    def second_norm(at):
        n2, s2 = normalise(h_ref[at, :])
        n2_ref[at, :] = n2
        s2_ref[at, :] = s2
        c = (n2 * row(gain2) + row(bias2)).astype(BF16)
        c_ref[at, :] = c
        ct_ref[:, at] = jnp.transpose(c)

    tiles(tokens, 128, second_norm)
    write(n2_ref, s2_ref, ct_ref)
    loads[2].wait()
    feed_forward(c_ref, up_v, b_up, u_ref, slope_ref, 256, ut_ref)
    write(ut_ref, slope_ref)
    loads[3].wait()
    project(u_ref, down_v, y_ref, 256, b_down, h_ref)
    write(y_ref)
    writer.wait()


def encoder_backward_kernel(
    x_ref, gy_ref, qkv_ref, e_ref, rl_ref, o_ref, n2_ref, s2_ref, slope_ref,
    gain1, w_qkv, w_out, gain2, w_up, w_down,
    gx_ref, gf_ref, ga_ref, gqkv_ref, small_ref, gbup_ref,
    gh_ref, go_ref,
):
    tokens, features = gy_ref.shape
    section = lax.axis_index("section")
    x = x_ref[pl.ds(pl.multiple_of(section * tokens, tokens), tokens), :].astype(F32)
    gbup_ref[...] = jnp.zeros_like(gbup_ref)
    feed_forward_back(gy_ref, w_down, slope_ref, gf_ref, gbup_ref, 512)
    gc = mm_nt(gf_ref[...], w_up[...])
    g = gy_ref[...].astype(F32)
    n2 = n2_ref[...]
    gh = g + normalise_back(gc, n2, s2_ref[...], row(gain2))
    gh_ref[...] = gh
    ga_ref[...] = gh.astype(BF16)
    small_ref[2:3, :] = rows_sum(gh)
    small_ref[3:4, :] = rows_sum(gc * n2)
    small_ref[4:5, :] = rows_sum(gc)
    small_ref[5:6, :] = rows_sum(g)
    go_ref[...] = mm_nt(ga_ref[...], w_out[...]).astype(BF16)
    for g in range(features // 128):
        attention_backward(
            qkv_ref, go_ref, o_ref, e_ref, rl_ref, gqkv_ref, slice(None), tokens, features,
            features // H_ENC, g,
        )
    gn = mm_nt(gqkv_ref[...], w_qkv[...])
    n1, s1 = normalise(x)
    small_ref[0:1, :] = rows_sum(gn * n1)
    small_ref[1:2, :] = rows_sum(gn)
    gx_ref[...] = (gh_ref[...] + normalise_back(gn, n1, s1, row(gain1))).astype(BF16)


def split_low(x):
    high = x.astype(BF16)
    return high, (x - high.astype(F32)).astype(BF16)


def place_slots(order_ref, seg, section, hot_ref, place_ref, empty_ref):
    packed = seg.shape[1]
    line = lax.broadcasted_iota(jnp.int32, (PATCHES, PATCHES), 0).astype(F32)
    line_low = line.astype(BF16)
    lane_low = lax.broadcasted_iota(jnp.int32, (8, PATCHES), 1).astype(F32).astype(BF16)
    column = lax.broadcasted_iota(jnp.int32, (PATCHES, packed), 1).astype(F32)
    packed_line = lax.broadcasted_iota(jnp.int32, (packed, PATCHES), 0).astype(F32)

    def one_sample(j, carry):
        at = pl.ds(pl.multiple_of(j * PATCHES, PATCHES), PATCHES)
        order = order_ref[pl.ds(section * SAMP_MB + j, 1), :].astype(F32)
        hit = jnp.where(order == line, 1.0, 0.0).astype(BF16)
        mine = lax.convert_element_type(j, F32)
        start = jnp.sum(jnp.where(seg < mine, 1.0, 0.0), axis=1, keepdims=True)
        count = jnp.sum(jnp.where(seg == mine, 1.0, 0.0), axis=1, keepdims=True)
        down, across = mm(hit, line_low), mm_nt(lane_low, hit)[:1, :]
        down = jnp.where(down < count, start + down, -1.0)
        across = jnp.where(across < count, start + across, -1.0)
        wide = jnp.concatenate([down] * (packed // PATCHES), axis=1)
        hot_ref[at, :] = jnp.where(column == wide, 1.0, 0.0).astype(BF16)
        place_ref[:, at] = jnp.where(packed_line == across, 1.0, 0.0).astype(BF16)
        empty_ref[at, :] = jnp.where(down < 0.0, 1.0, 0.0)
        return carry

    lax.fori_loop(0, SAMP_MB, one_sample, 0, unroll=2)


def decoder_kernel(
    y_ref, seg_ref, order_ref, pos_ref, g_hbm,
    w_embed_hbm, b_embed, mask_token,
    gain1, bias1, w_qkv_hbm, w_out_hbm, b_out, gain2, bias2, w_up_hbm, b_up, w_down_hbm, b_down,
    *refs,
):
    hbm, (geb_ref, gy_ref, small_ref, gbup_ref) = refs[:9], refs[9:13]
    buffers = refs[13:22]
    out_ref, at_ref, ot_ref, ct_ref, gt_ref, u_ref, gf_ref, ga_ref, gqkv_ref = buffers
    (
        e2_ref, z_ref, s1_ref, e_ref, rl_ref, h_ref, s2_ref, go_ref, ge_ref, o_ref, c_ref, qkv_ref,
        slope_ref, sum_ref, g_all, hot_ref, place_ref, empty_ref, w_embed, w_qkv, w_out, w_up, w_down,
        w_sem, out_sem,
    ) = refs[22:]
    packed = y_ref.shape[0]
    rows, features = z_ref.shape
    samples = rows // PATCHES
    head_size = features // H_DEC
    total = g_all.shape[0]
    section = lax.axis_index("section")
    mine = pl.ds(pl.multiple_of(section * total, total), total)
    pairs = (
        (w_embed_hbm, w_embed), (w_qkv_hbm, w_qkv), (w_out_hbm, w_out), (w_up_hbm, w_up),
        (w_down_hbm, w_down), (g_hbm.at[mine, :], g_all),
    )
    loads = [pltpu.make_async_copy(a, b, w_sem.at[i]) for i, (a, b) in enumerate(pairs)]
    for load in loads:
        load.start()

    def write(at, *which):
        copies = []
        for i in which:
            target = hbm[i].at[:, at] if 1 <= i <= 4 else hbm[i].at[at, :]
            copies.append(pltpu.make_async_copy(buffers[i], target, out_sem.at[i]))
            copies[-1].start()
        return copies

    small_ref[...] = jnp.zeros_like(small_ref)
    gbup_ref[...] = jnp.zeros_like(gbup_ref)
    ge_ref[...] = jnp.zeros_like(ge_ref)
    seg = seg_ref[pl.ds(section, 1), :].astype(F32)
    place_slots(order_ref, seg, section, hot_ref, place_ref, empty_ref)
    loads[0].wait()
    high, low = split_low(mm(y_ref[...], w_embed[...]) + row(b_embed))
    e2_ref[:packed, :] = high
    e2_ref[packed:, :] = low
    for load in loads[1:]:
        load.wait()

    def one_step(step, carry):
        here = pl.ds(pl.multiple_of(step * rows, rows), rows)

        def first_norm(at):
            there = pl.ds(pl.multiple_of(step * rows + at.start, 128), 128)
            one_hot = hot_ref[there, :]
            empty = jnp.concatenate([empty_ref[there, :]] * (features // 128), axis=1)
            twice = jnp.concatenate([one_hot, one_hot], axis=1)
            z = mm(twice, e2_ref[...]) + empty * row(mask_token) + pos_ref[...]
            n1, s1 = normalise(z)
            z_ref[at, :] = z
            s1_ref[at, :] = s1
            a = (n1 * row(gain1) + row(bias1)).astype(BF16)
            c_ref[at, :] = a
            at_ref[:, at] = jnp.transpose(a)

        tiles(rows, PATCHES, first_norm)
        writing = write(here, 1)
        project(c_ref, w_qkv, qkv_ref, 256)

        def forward(b, carry):
            at = pl.ds(pl.multiple_of(b * PATCHES, PATCHES), PATCHES)
            for g in range(features // 128):
                attention_forward(
                    qkv_ref, o_ref, e_ref, rl_ref, at, PATCHES, features, head_size, None, g
                )
            ot_ref[:, at] = jnp.transpose(o_ref[at, :])
            return carry

        lax.fori_loop(0, samples, forward, 0, unroll=2)
        project(o_ref, w_out, h_ref, 256, b_out, z_ref)

        def second_norm(at):
            n2, s2 = normalise(h_ref[at, :])
            s2_ref[at, :] = s2
            c = (n2 * row(gain2) + row(bias2)).astype(BF16)
            c_ref[at, :] = c
            ct_ref[:, at] = jnp.transpose(c)

        tiles(rows, PATCHES, second_norm)
        feed_forward(c_ref, w_up, b_up, u_ref, slope_ref, 256)
        writing += write(here, 2, 3, 5)
        project(u_ref, w_down, out_ref, 256, b_down, h_ref)

        def turn(at):
            gt_ref[:, at] = jnp.transpose(
                g_all[pl.ds(pl.multiple_of(step * rows + at.start, 128), 128), :]
            )

        tiles(rows, PATCHES, turn)
        g_ref = g_all.at[here, :]
        feed_forward_back(g_ref, w_down, slope_ref, gf_ref, gbup_ref, 256)
        writing += write(here, 0, 4, 6)
        project_back(gf_ref, w_up, sum_ref, 256)

        def second_back(at):
            there = pl.ds(pl.multiple_of(step * rows + at.start, 128), 128)
            g, gc, h = g_all[there, :].astype(F32), sum_ref[at, :], h_ref[at, :]
            n2 = (h - jnp.mean(h, axis=-1, keepdims=True)) * s2_ref[at, :]
            gh = g + normalise_back(gc, n2, s2_ref[at, :], row(gain2))
            small_ref[2:3, :] += rows_sum(gh)
            small_ref[3:4, :] += rows_sum(gc * n2)
            small_ref[4:5, :] += rows_sum(gc)
            small_ref[5:6, :] += rows_sum(g)
            h_ref[at, :] = gh
            ga_ref[at, :] = gh.astype(BF16)

        tiles(rows, PATCHES, second_back)
        project_back(ga_ref, w_out, go_ref, 256)
        writing += write(here, 7)

        def backward(b, carry):
            at = pl.ds(pl.multiple_of(b * PATCHES, PATCHES), PATCHES)
            for g in range(features // 128):
                attention_backward(
                    qkv_ref, go_ref, o_ref, e_ref, rl_ref, gqkv_ref, at, PATCHES, features,
                    head_size, g,
                )
            return carry

        lax.fori_loop(0, samples, backward, 0, unroll=2)
        writing += write(here, 8)
        project_back(gqkv_ref, w_qkv, sum_ref, 256)

        def first_back(at):
            there = pl.ds(pl.multiple_of(step * rows + at.start, 128), 128)
            gn, z = sum_ref[at, :], z_ref[at, :]
            n1 = (z - jnp.mean(z, axis=-1, keepdims=True)) * s1_ref[at, :]
            gz = h_ref[at, :] + normalise_back(gn, n1, s1_ref[at, :], row(gain1))
            empty = jnp.concatenate([empty_ref[there, :]] * (features // 128), axis=1)
            small_ref[0:1, :] += rows_sum(gn * n1)
            small_ref[1:2, :] += rows_sum(gn)
            small_ref[6:7, :] += rows_sum(gz * empty)
            c_ref[at, :] = gz.astype(BF16)

        tiles(rows, PATCHES, first_back)
        ge_ref[...] += mm(place_ref[:, here], c_ref[...])
        for copy in writing:
            copy.wait()
        return carry

    lax.fori_loop(0, total // rows, one_step, 0)
    ge = ge_ref[...]
    small_ref[7:8, :] = rows_sum(ge)
    geb_ref[...] = ge.astype(BF16)
    gy_ref[...] = mm_nt(geb_ref[...], w_embed[...]).astype(BF16)


def in_vmem(count):
    return [pl.BlockSpec(memory_space=pltpu.VMEM)] * count


def in_hbm():
    return pl.BlockSpec(memory_space=pl.ANY)


def shape(rows, columns, dtype=BF16):
    return jax.ShapeDtypeStruct((rows, columns), dtype)


KERNEL_VMEM = 60 * 2**20


def encoder_forward(x, segments, params):
    rows, d = x.shape[0] // 2, x.shape[1]
    ff = params[7].shape[1]
    outs = [
        (rows, d, BF16),
        (d, rows, BF16),
        (rows, 3 * d, BF16),
        (rows, H_ENC * rows, BF16),
        (rows, d, F32),
        (rows, d, BF16),
        (d, rows, BF16),
        (rows, d, F32),
        (rows, 1, F32),
        (d, rows, BF16),
        (ff, rows, BF16),
        (rows, ff, BF16),
    ]
    more = [(rows, d, F32), (rows, d, BF16), (rows, ff, BF16), (rows, rows, F32)]
    args = [x, segments, *params]
    matrices = [w for w in params if w.dtype == BF16]
    return pl.pallas_call(
        encoder_forward_kernel,
        out_shape=[shape(*o) for o in outs],
        in_specs=in_vmem(2) + [in_hbm() if w.dtype == BF16 else in_vmem(1)[0] for w in params],
        out_specs=[in_hbm()] * len(outs),
        scratch_shapes=[pltpu.VMEM((r, w), t) for r, w, t in outs + more]
        + [pltpu.VMEM(w.shape, BF16) for w in matrices]
        + [pltpu.SemaphoreType.DMA((len(matrices),)), pltpu.SemaphoreType.DMA((len(outs),))],
        compiler_params=pltpu.CompilerParams(vmem_limit_bytes=KERNEL_VMEM),
        name="encoder_forward",
    )(*args)


def encoder_backward(x, gy, saved, params):
    gain1, _, w_qkv, w_out, _, gain2, _, w_up, _, w_down, _ = params
    rows, d = gy.shape
    ff = w_up.shape[1]
    outs = [
        shape(rows, d),
        shape(rows, ff),
        shape(rows, d),
        shape(rows, 3 * d),
        shape(8, d, F32),
        shape(1, ff, F32),
    ]
    args = [x, gy, *saved, gain1, w_qkv, w_out, gain2, w_up, w_down]
    return pl.pallas_call(
        encoder_backward_kernel,
        out_shape=outs,
        in_specs=in_vmem(len(args)),
        out_specs=in_vmem(len(outs)),
        scratch_shapes=[pltpu.VMEM((rows, d), F32), pltpu.VMEM((rows, d), BF16)],
        compiler_params=pltpu.CompilerParams(vmem_limit_bytes=KERNEL_VMEM),
        name="encoder_backward",
    )(*args)


def decoder_both(y, segments, orders, g, embed_params, params):
    packed, d_enc = y.shape
    total, d = g.shape[0] // 2, g.shape[1]
    rows = 6 * PATCHES
    ff = params[7].shape[1]
    args = [y, segments, orders, positions(PATCHES, d), g, *embed_params, *params]
    in_specs = in_vmem(4) + [in_hbm()]
    in_specs += [in_hbm() if x.dtype == BF16 else in_vmem(1)[0] for x in args[5:]]
    wide = [ff, ff, d, 3 * d]
    outs = [shape(total, d)] + [shape(d, total)] * 4 + [shape(total, w) for w in wide]
    buffers = [(rows, d, BF16)] + [(d, rows, BF16)] * 4 + [(rows, w, BF16) for w in wide]
    last = [shape(packed, d), shape(packed, d_enc), shape(8, d, F32), shape(1, ff, F32)]
    scratch = [
        (2 * packed, d, BF16),
        (rows, d, F32),
        (rows, 1, F32),
        (rows, H_DEC * PATCHES, BF16),
        (rows, d, F32),
        (rows, d, F32),
        (rows, 1, F32),
        (rows, d, BF16),
        (packed, d, F32),
        (rows, d, BF16),
        (rows, d, BF16),
        (rows, 3 * d, BF16),
        (rows, ff, BF16),
        (rows, d, F32),
        (total, d, BF16),
        (total, packed, BF16),
        (packed, total, BF16),
        (total, 128, F32),
    ]
    matrices = [x for x in args[5:] if x.dtype == BF16]
    return pl.pallas_call(
        decoder_kernel,
        out_shape=outs + last,
        in_specs=in_specs,
        out_specs=[in_hbm()] * len(outs) + in_vmem(len(last)),
        scratch_shapes=[pltpu.VMEM((r, w), t) for r, w, t in buffers + scratch]
        + [pltpu.VMEM(x.shape, BF16) for x in matrices]
        + [pltpu.SemaphoreType.DMA((k,)) for k in (len(matrices) + 1, len(outs))],
        compiler_params=pltpu.CompilerParams(vmem_limit_bytes=KERNEL_VMEM),
        name="decoder_both",
    )(*args)


MESH = pl.DeviceIdType.MESH
ENC_QKV, ENC_OUT, ENC_UP, ENC_DOWN, EMBED, DEC_QKV, DEC_OUT, DEC_UP, DEC_DOWN = range(9)
GIVE, PAIR, FFN, LN2, GO, ATT, GN, LAST = range(10, 18)
SMALL = -1
ROW_BUP, ROW_DEC_BUP, ROW_DEC, SMALL_ROWS = 6, 10, 16, 24
Z, Y, X, CORE = range(4)
ORDERS = ((X, Y, Z), (Y, X, Z), (X, Z, Y), (Y, Z, X), (Z, X, Y), (Z, Y, X))


class Chunk:
    def __init__(self, name, half, offset, rows, width, first_row=None):
        self.name, self.half, self.offset, self.rows, self.width = name, half, offset, rows, width
        self.first_row, self.turned, self.order = first_row, name == DEC_DOWN, None
        self.decoder = name in (DEC_QKV, DEC_UP, DEC_OUT)

    def columns(self, side):
        return pl.ds(pl.multiple_of(side * self.half + self.offset, 128), self.width)

    def place(self, side):
        if self.turned:
            return (pl.ds(pl.multiple_of(side * self.half + self.offset, 128), self.rows), slice(None))
        if self.first_row is None:
            return (slice(None), self.columns(side))
        return (pl.ds(self.first_row, self.rows), self.columns(side))

    @property
    def bytes(self):
        return 32 * self.rows * self.width

    def loads(self, order):
        if order[0] == Z:
            return (2 * self.bytes, self.bytes / 4, self.bytes / 8)
        if order[1] == Z:
            return (self.bytes, self.bytes, self.bytes / 8)
        return (self.bytes, self.bytes / 2, self.bytes / 2)


LINK_ORDERS = (0, 1, 2, 4, 3, 0, 3, 0, 3, 3, 0, 0, 0, 0, 1)


def make_chunks():
    chunks = [Chunk(ENC_DOWN, 384, 0, 48, 384, 48 * q) for q in range(4)]
    chunks += [Chunk(ENC_UP, 1536, 768 * q, 48, 768) for q in range(2)]
    chunks += [Chunk(ENC_OUT, 384, 0, 48, 384)]
    chunks += [Chunk(ENC_QKV, 1152, 0, 48, 768), Chunk(ENC_QKV, 1152, 768, 48, 384)]
    chunks += [Chunk(EMBED, 256, 0, 48, 256)]
    chunks += [Chunk(DEC_QKV, 768, 0, 32, 768), Chunk(DEC_DOWN, 256, 0, 256, 128)]
    chunks += [Chunk(DEC_UP, 1024, o, 32, 512) for o in (0, 512)]
    chunks += [Chunk(DEC_OUT, 256, 0, 32, 256)]
    for chunk, order in zip(chunks, LINK_ORDERS):
        chunk.order = ORDERS[order]
    return chunks


def make_groups(chunks):
    return [[c] for c in range(len(chunks))]


def product_cost(k, count):
    if k.turned:
        return 5.0
    return k.rows * k.width * (0.9 / 8192 if k.decoder else 0.6 / 18432)


def tasks_in_order(chunks, groups):
    def gives(name):
        found = [(g, chunks[m[0]], len(m)) for g, m in enumerate(groups)]
        kind = PAIR if name == DEC_DOWN else GIVE
        return [(kind, g, product_cost(k, size)) for g, k, size in found if k.name == name]

    tasks = gives(ENC_DOWN)
    tasks += [(FFN, t, 1.7) for t in range(4)] + gives(ENC_UP)
    tasks += [(LN2, 0, 1.0), (GO, 0, 0.9)]
    tasks += [(ATT, part, 4.5) for part in range(2)]
    tasks += gives(ENC_OUT) + gives(ENC_QKV) + gives(EMBED)
    tasks += gives(DEC_QKV) + gives(DEC_DOWN)
    tasks += [(GN, j, 0.9) for j in range(3)] + [(LAST, 0, 1.5)]
    return tasks + gives(DEC_UP) + gives(DEC_OUT)


def decoder_arrays(chunks):
    names = []
    for k in chunks:
        if (k.decoder or k.turned) and k.name not in names:
            names.append(k.name)
    return names


def make_plan(chunks, groups):
    tasks = tasks_in_order(chunks, groups)
    lhs = decoder_arrays(chunks)
    free = [0.0] * 4
    rate = [80e3, 80e3, 80e3, 500e3]
    pending, plan, now, owned = [], [], 2.0, set()

    def send(link, size, latency):
        begin = max(now, free[link])
        free[link] = begin + size / rate[link]
        return free[link] + latency

    def blocked(task):
        if task[0] not in (GIVE, PAIR):
            return False
        name = chunks[groups[task[1]][0]].name
        if name not in lhs[2:]:
            return False
        name = lhs[lhs.index(name) - 2]
        return any(chunks[m[0]].name == name and g not in owned for g, m in enumerate(groups))

    while tasks or pending:
        pending.sort()
        if pending and (pending[0][0] <= now or not tasks or blocked(tasks[0])):
            arrive, stage, c = pending.pop(0)
            now = max(now, arrive)
            plan.append((stage, c))
            if c == SMALL:
                now += 0.1
                if stage < 4:
                    pending.append((now + 2.0, stage + 1, c))
                continue
            members = groups[c] if stage == 1 else [c]
            k = chunks[members[0]]
            if stage == 1:
                owned.add(c)
                now += 0.6 if k.turned else product_cost(k, len(members)) + 0.2 * len(members)
            else:
                now += 0.25
            for c in members:
                k = chunks[c]
                if stage < 4:
                    axis = k.order[stage - 1]
                    latency = 2.0 if axis == Z else 1.5
                    arrive = send(axis, k.loads(k.order)[stage - 1], latency)
                    pending.append((arrive, stage + 1, c))
                elif stage == 4:
                    pending.append((send(CORE, k.bytes / 16, 1.0), 5, c))
            continue
        name, arg, cost = tasks.pop(0)
        plan.append((name, arg))
        now += cost
        if name in (GIVE, PAIR):
            arrive = [send(CORE, chunks[c].bytes, 1.0) for c in groups[arg]]
            pending.append((max(arrive), 1, arg))
        elif name == LAST:
            pending.append((now + 2.0, 1, SMALL))
    return plan


class Ring:
    def __init__(self, sources, slots, semaphores, depth):
        self.copies = [
            pltpu.make_async_copy(source, slot, semaphores())
            for source, slot in zip(sources, slots)
        ]
        self.slots, self.depth, self.at = slots, depth, 0

    def begin(self):
        for copy in self.copies[: self.depth]:
            copy.start()

    def take(self):
        self.copies[self.at].wait()
        return self.slots[self.at]

    def done(self):
        ahead = self.at + self.depth
        if ahead < len(self.copies):
            self.copies[ahead].start()
        self.at += 1


class Names:
    def __init__(self, names, refs):
        self.__dict__.update(zip(names, refs))


LOADS = 96


def finish_kernel(chunks, groups, plan, r):
    n = len(chunks)
    s = lax.axis_index("section")
    d = lax.axis_index("dp")
    here = (d // 4, (d // 2) % 2, d % 2)
    z, y, x = here
    sibling = {"section": 1 - s}
    z_at = [lax.rem(z + k, 4) for k in (1, 2, 3)]
    peers = {
        X: [(1 - x, {"dp": d + 1 - 2 * x})],
        Y: [(1 - y, {"dp": d + 2 - 4 * y})],
        Z: [(p, {"dp": d + 4 * (p - z)}) for p in z_at],
    }
    every = [sibling] + [peer for axis in (X, Y, Z) for _, peer in peers[axis]]

    barrier = pltpu.get_barrier_semaphore()
    for peer in every:
        pl.semaphore_signal(barrier, inc=1, device_id=peer, device_id_type=MESH)

    counter = iter(range(LOADS))

    def semaphore():
        return r.load_sem.at[next(counter)]

    def remote(src, dst, send, recv, peer):
        return pltpu.make_async_remote_copy(
            src_ref=src, dst_ref=dst, send_sem=send, recv_sem=recv, device_id=peer, device_id_type=MESH
        )

    rhs_of = {DEC_QKV: r.gqkv2, DEC_UP: r.gf2, DEC_OUT: r.ga2}
    lhs_of = {DEC_QKV: r.at2, DEC_UP: r.ct2, DEC_OUT: r.ot2, DEC_DOWN: r.gt2}
    sources, last_use = [], {}

    def wide_columns(g, side):
        k, width = chunks[groups[g][0]], sum(chunks[c].width for c in groups[g])
        return pl.ds(pl.multiple_of(side * k.half + k.offset, 128), width)

    for i, (name, arg) in enumerate(plan):
        if name == PAIR:
            sources += [r.u2.at[:, t * 512 : (t + 1) * 512] for t in range(4)]
            last_use[DEC_DOWN] = i
        elif name in (GIVE, 1) and arg != SMALL and chunks[groups[arg][0]].decoder:
            k = chunks[groups[arg][0]]
            sources.append(rhs_of[k.name].at[:, wide_columns(arg, 1 - s if name == GIVE else s)])
            last_use[k.name] = i
    lhs_names = decoder_arrays(chunks)
    assert sorted(lhs_names, key=last_use.get) == lhs_names
    rhs_slots = [r.rhs.at[i % 2, :, : tile.shape[1]] for i, tile in enumerate(sources)]
    rhs = Ring(sources, rhs_slots, semaphore, 2)
    lhs = Ring([lhs_of[k] for k in lhs_names], [r.lhs.at[i % 2] for i in range(4)], semaphore, 2)
    tokens, d_enc = r.gy.shape
    blocks = []
    for t in range(4):
        at = pl.ds(t * d_enc, d_enc)
        blocks += [r.w_down.at[at, :], r.w_up.at[:, at]]
    blocks.append(r.w_out)
    blocks += [r.w_qkv.at[:, pl.ds(j * d_enc, d_enc)] for j in range(3)]
    weights = Ring(blocks, [r.w.at[i % 4] for i in range(12)], semaphore, 4)
    def load(source, target):
        return pltpu.make_async_copy(source, target, semaphore())

    mine = pl.ds(pl.multiple_of(s * tokens, tokens), tokens)
    load_gy, load_slope, load_ut = load(r.gy, r.gy_v), load(r.slope, r.slope_v), load(r.ut, r.ut_v)
    load_ct, load_at, load_ot = load(r.ct, r.ct_v), load(r.at, r.at_v), load(r.ot, r.ot_v)
    load_n2, load_s2, load_qkv = load(r.n2, r.n2_v), load(r.s2, r.s2_v), load(r.qkv, r.qkv_v)
    load_o, load_rl, load_x = load(r.o, r.o_v), load(r.rl, r.rl_v), load(r.x.at[mine, :], r.x_v)
    load_y, load_geb, load_e = load(r.y, r.y_v), load(r.geb, r.geb_v), load(r.e, r.e_v)
    load_gy.start()
    load_ut.start()
    load_slope.start()
    weights.begin()
    begun = [
        (load_ct, load_n2, load_s2),
        (load_qkv, load_o, load_rl, load_e),
        (load_ot, load_at, load_y, load_geb),
        (load_x, lhs, rhs),
    ]

    def begin_some():
        for copy in begun.pop(0) if begun else ():
            copy.begin() if isinstance(copy, Ring) else copy.start()

    half = r.decoded.shape[1] // 2
    give_half = r.decoded.at[:, pl.ds(pl.multiple_of((1 - s) * half, half), half), :]
    decoded_away = remote(give_half, r.decoded_got, r.swap_sem.at[0], r.swap_sem.at[1], sibling)
    gx_columns = d_enc // 2
    gx_half = r.gx.at[:, pl.ds(pl.multiple_of((1 - s) * gx_columns, 128), gx_columns)]
    gx_away = remote(gx_half, r.gx_got, r.swap_sem.at[2], r.swap_sem.at[3], sibling)

    small = r.small
    small[...] = jnp.zeros_like(small)
    small[ROW_DEC : ROW_DEC + 8, : r.small2.shape[1]] = r.small2[...]
    quarter = r.gbup2.shape[1] // 4
    for i in range(4):
        piece = r.gbup2[:, i * quarter : (i + 1) * quarter]
        small[ROW_DEC_BUP + i : ROW_DEC_BUP + i + 1, :quarter] = piece

    pl.semaphore_wait(barrier, len(every))

    copies = {}
    first_slot = (0, 1, 4, 7, 10)

    def chunk_copy(c, slot, src, dst, peer):
        copy = remote(src, dst, r.send_sem.at[c, slot], r.recv_sem.at[c, slot], peer)
        copy.start()
        copies[c, slot] = copy

    sent = set()

    def sent_by(c, slot):
        if (c, slot) not in sent:
            sent.add((c, slot))
            copies[c, slot].wait_send()

    staged = {}

    def staging(c):
        k = chunks[c]
        buffers = r.stage[k.rows, k.width]
        turn = staged.setdefault((k.rows, k.width), [])
        if len(turn) >= len(buffers):
            sent_by(turn[-len(buffers)], 0)
        turn.append(c)
        return buffers[(len(turn) - 1) % len(buffers)]

    def shard(i):
        return (i // 4, (i // 2) % 2, i % 2)

    waited = set()

    def arrived(copy):
        if id(copy) not in waited:
            waited.add(id(copy))
            copy.wait()

    def product(g, side, store):
        k, columns = chunks[groups[g][0]], wide_columns(g, side)
        quarter = 4 * k.rows
        if k.decoder:
            left, right = lhs.slots[lhs_names.index(k.name)], rhs.take()
        elif k.name == EMBED:
            arrived(load_y)
            arrived(load_geb)
            left, right = r.yt_v, r.geb_v.at[:, columns]
            r.yt_v[...] = jnp.transpose(r.y_v[...])
        elif k.name == ENC_DOWN:
            arrived(load_ut)
            arrived(load_gy)
            left, right = r.ut_v, r.gy_v.at[:, columns]
        elif k.name == ENC_UP:
            arrived(load_ct)
            left, right = r.ct_v, r.slope_v.at[:, columns]
        elif k.name == ENC_OUT:
            arrived(load_ot)
            left, right = r.ot_v, r.ga_v.at[:, columns]
        else:
            arrived(load_at)
            left, right = r.at_v, r.qkv_v.at[:, columns]

        def body(q, carry):
            if k.name == ENC_DOWN:
                starts = [q * 768 + j * 192 + k.first_row for j in range(4)]
                parts = [left[pl.ds(pl.multiple_of(at, 16), k.rows), :] for at in starts]
                rows = jnp.concatenate(parts, axis=0)
            else:
                rows = left[pl.ds(pl.multiple_of(q * quarter, quarter), quarter), :]
            store(q, mm(rows, right[...]))
            return carry

        lax.fori_loop(0, 4, body, 0)

    def after_product(i, g):
        k = chunks[groups[g][0]]
        if k.decoder:
            rhs.done()
            if last_use[k.name] == i:
                lhs.done()

    def wait_lhs(k):
        if k.name in lhs_names:
            arrived(lhs.copies[lhs_names.index(k.name)])

    def give(i, g):
        (c,) = groups[g]
        k = chunks[c]
        wait_lhs(k)
        buffer = staging(c)

        def store(q, value):
            value = value.astype(BF16)
            for j in range(4):
                buffer[q, j // 2, j % 2] = value[j * k.rows : (j + 1) * k.rows]

        product(g, 1 - s, store)
        after_product(i, g)
        chunk_copy(c, 0, buffer, r.acc[c], sibling)
        begin_some()

    def pair(i, g):
        (c,) = groups[g]
        k = chunks[c]
        wait_lhs(k)
        left = lhs.slots[lhs_names.index(DEC_DOWN)]
        buffer, acc = staging(c), r.acc[c]
        for t in range(4):
            tile = rhs.take()

            def body(h, carry):
                row_at = pl.ds(pl.multiple_of(h * 128, 128), 128)
                for side, target in ((1 - s, buffer), (s, acc)):
                    at = pl.ds(pl.multiple_of(side * k.half + h * 128, 128), 128)
                    value = mm(left[at, :], tile[...]).astype(BF16)
                    for j in range(4):
                        target[t, j // 2, j % 2, row_at, :] = value[:, j * 128 : (j + 1) * 128]
                return carry

            lax.fori_loop(0, k.half // 128, body, 0)
            rhs.done()
        lhs.done()
        chunk_copy(c, 0, buffer, r.got[c], sibling)

    def spots(k, stage):
        fixed = {axis: here[axis] for axis in k.order[: stage - 1]}
        return [fixed.get(axis, slice(None)) for axis in (Z, Y, X)]

    def send_stage(c, stage):
        k = chunks[c]
        axis = k.order[stage - 1]
        for j, (coordinate, peer) in enumerate(peers[axis]):
            at = spots(k, stage)
            at[axis] = coordinate
            src = r.acc[c].at[tuple(at)]
            chunk_copy(c, first_slot[stage] + j, src, r.recv[stage - 1][c].at[j], peer)

    def got_stage(c, stage):
        k = chunks[c]
        count = len(peers[k.order[stage - 1]])
        for j in range(count):
            copies[c, first_slot[stage] + j].wait_recv()
        return count

    def add_stage(c, stage):
        k, acc, got = chunks[c], r.acc[c], r.recv[stage - 1][c]
        count = got_stage(c, stage)
        left = [axis for axis in (Z, Y, X) if axis not in k.order[:stage]]
        sizes = [(4, 2, 2)[axis] for axis in left]

        def body(j, carry):
            place, rest = {}, j
            for axis, size in reversed(list(zip(left, sizes))):
                place[axis] = rest % size
                rest = rest // size
            at = tuple(place.get(axis, here[axis]) for axis in (Z, Y, X))
            index = tuple(place[axis] for axis in left)
            if count == 1:
                acc[at] = acc[at] + got[(0,) + index]
            else:
                total = acc[at].astype(F32)
                for m in range(count):
                    total = total + got[(m,) + index].astype(F32)
                acc[at] = total.astype(BF16)
            return carry

        lax.fori_loop(0, math.prod(sizes), body, 0)

    def stage1(i, g):
        (c,) = groups[g]
        k, acc = chunks[c], r.acc[c]
        copies[c, 0].wait_recv()
        if k.turned:

            def add(j, carry):
                at = (j // 4, (j // 2) % 2, j % 2)
                acc[at] = acc[at] + r.got[c][at]
                return carry

            lax.fori_loop(0, 16, add, 0)
        else:

            def store(q, value):
                for j in range(4):
                    at = (q, j // 2, j % 2)
                    part = value[j * k.rows : (j + 1) * k.rows]
                    acc[at] = (part + acc[at].astype(F32)).astype(BF16)

            product(g, s, store)
            after_product(i, g)
        send_stage(c, 1)

    def stage2(i, c):
        add_stage(c, 1)
        send_stage(c, 2)

    def stage3(i, c):
        add_stage(c, 2)
        send_stage(c, 3)

    def stage4(i, c):
        k = chunks[c]
        total = r.acc[c][here].astype(F32)
        for j in range(got_stage(c, 3)):
            total = total + r.recv[2][c][j].astype(F32)
        out = r.out[k.name]
        out[k.place(s)] = total.astype(BF16)
        final = out.at[k.place(s)]
        chunk_copy(c, 10, final, final, sibling)

    def stage5(i, c):
        copies[c, 10].wait_recv()

    small_copies = []

    def small_copy(source, peer):
        slot = len(small_copies)
        copy = remote(
            source, r.small_got.at[slot], r.small_sem.at[0, slot], r.small_sem.at[1, slot], peer
        )
        copy.start()
        small_copies.append(copy)

    def small_stage(stage):
        if stage < 4:
            small_copies[stage - 1].wait()
            total = small[...] + r.small_got[stage - 1]
            if stage < 3:
                small[...] = total
                small_copy(small, peers[X if stage == 1 else Y][0][1])
            else:
                r.small_sum[...] = total
                for _, peer in peers[Z]:
                    small_copy(r.small_sum, peer)
        else:
            total = r.small_sum[...]
            for j in range(3):
                small_copies[3 + j].wait()
                total = total + r.small_got[3 + j]
            r.out_small[...] = total

    def ffn(i, t):
        if t == 0:
            arrived(load_gy)
            load_slope.wait()
        tile = weights.take()

        def up(at):
            there = pl.ds(pl.multiple_of(t * d_enc + at.start, 256), 256)
            gu = mm_nt(r.gy_v[...], tile[at, :])
            gf = (gu * r.slope_v[:, there].astype(F32)).astype(BF16)
            r.slope_v[:, there] = gf
            small[ROW_BUP + t : ROW_BUP + t + 1, at] = rows_sum(gf.astype(F32))

        tiles(d_enc, 256, up)
        weights.done()
        back_add(r.slope_v.at[:, t * d_enc : (t + 1) * d_enc], weights.take(), t == 0)
        weights.done()

    def back_add(left, right, first):
        def body(at):
            part = mm_nt(left[...], right[at, :])
            r.sum_v[:, at] = part if first else r.sum_v[:, at] + part

        tiles(d_enc, 256, body)

    def ln2(i, _):
        load_n2.wait()
        load_s2.wait()
        small[2:6, :] = jnp.zeros((4, d_enc), F32)

        def body(at):
            g, gc, n2 = r.gy_v[at, :].astype(F32), r.sum_v[at, :], r.n2_v[at, :]
            gh = g + normalise_back(gc, n2, r.s2_v[at, :], row(r.gain2))
            small[2:3, :] += rows_sum(gh)
            small[3:4, :] += rows_sum(gc * n2)
            small[4:5, :] += rows_sum(gc)
            small[5:6, :] += rows_sum(g)
            r.n2_v[at, :] = gh
            r.ga_v[at, :] = gh.astype(BF16)

        tiles(tokens, 128, body)

    def go(i, _):
        project_back(r.ga_v, weights.take(), r.go_v, 256)
        weights.done()

    def att(i, part):
        if part == 0:
            for copy in (load_qkv, load_o, load_rl, load_e):
                copy.wait()

        def body(g, carry):
            attention_backward(
                r.qkv_v, r.go_v, r.o_v, r.e_v, r.rl_v, r.qkv_v, slice(None), tokens, d_enc,
                d_enc // H_ENC, g,
            )
            return carry

        lax.fori_loop(3 * part, 3 * part + 3, body, 0)

    def gn(i, j):
        back_add(r.qkv_v.at[:, j * d_enc : (j + 1) * d_enc], weights.take(), j == 0)
        weights.done()

    def last(i, _):
        load_x.wait()
        small[0:2, :] = jnp.zeros((2, d_enc), F32)

        def body(at):
            n1, s1 = normalise(r.x_v[at, :].astype(F32))
            total = r.sum_v[at, :]
            small[0:1, :] += rows_sum(total * n1)
            small[1:2, :] += rows_sum(total)
            gx = r.n2_v[at, :] + normalise_back(total, n1, s1, row(r.gain1))
            r.gx[at, :] = gx.astype(BF16)

        tiles(tokens, 128, body)
        small_copy(small, sibling)
        gx_away.start()
        decoded_away.start()

    run = {
        GIVE: give, PAIR: pair, FFN: ffn, LN2: ln2, GO: go, ATT: att, GN: gn, LAST: last,
        1: stage1, 2: stage2, 3: stage3, 4: stage4, 5: stage5,
    }
    for i, (name, arg) in enumerate(plan):
        if arg == SMALL:
            small_stage(name)
        else:
            run[name](i, arg)

    for c, slot in copies:
        sent_by(c, slot)
    gx_away.wait()
    decoded_away.wait()


def finish_buffers(chunks, rows, d, ff, dec_total, dec):
    def of(dtype, *dims):
        return (dims, dtype)

    return dict(
        y_v=of(BF16, rows, d),
        geb_v=of(BF16, rows, dec),
        gy_v=of(BF16, rows, d),
        slope_v=of(BF16, rows, ff),
        n2_v=of(F32, rows, d),
        s2_v=of(F32, rows, 1),
        qkv_v=of(BF16, rows, 3 * d),
        o_v=of(BF16, rows, d),
        rl_v=of(F32, rows, d),
        x_v=of(BF16, rows, d),
        ga_v=of(BF16, rows, d),
        go_v=of(BF16, rows, d),
        sum_v=of(F32, rows, d),
        ut_v=of(BF16, ff, rows),
        ct_v=of(BF16, d, rows),
        at_v=of(BF16, d, rows),
        ot_v=of(BF16, d, rows),
        e_v=of(BF16, rows, H_ENC * rows),
        yt_v=of(BF16, d, rows),
        w=of(BF16, 4, d, d),
        lhs=of(BF16, 2, dec, dec_total),
        rhs=of(BF16, 2, dec_total, 768),
        small=of(F32, SMALL_ROWS, d),
        small_sum=of(F32, SMALL_ROWS, d),
        small_got=of(F32, 6, SMALL_ROWS, d),
    )


def finish(acts):
    enc, dec = acts["enc"], acts["dec"]
    gain1, _, w_qkv, w_out, _, gain2, _, w_up, _, w_down, _ = enc["params"]
    qkv, e, rl, o, n2, s2, slope = acts["saved"]
    given = dict(
        x=acts["x"], y=acts["y"], gy=acts["gy"], geb=acts["geb"], qkv=qkv, e=e, rl=rl, o=o, n2=n2,
        s2=s2, slope=slope, at=enc["at"], ot=enc["ot"], ct=enc["ct"], ut=enc["ut"], at2=dec["at"], ot2=dec["ot"],
        ct2=dec["ct"], gt2=dec["gt"], u2=dec["u"], gf2=dec["gf"], ga2=dec["ga"],
        gqkv2=dec["gqkv"], w_qkv=w_qkv, w_out=w_out, w_up=w_up, w_down=w_down,
        decoded=acts["decoded"].reshape(SAMP_MB, PATCHES, -1),
    )
    n_hbm = len(given)
    given.update(small2=acts["small2"], gbup2=acts["gbup2"], gain1=gain1, gain2=gain2)
    rows, d = acts["gy"].shape
    ff = w_up.shape[1]
    dec_d, dec_total = dec["at"].shape
    dec_ff = dec["u"].shape[1]
    chunks = make_chunks()
    n = len(chunks)
    groups = make_groups(chunks)
    plan = make_plan(chunks, groups)

    dims = {
        ENC_QKV: (d, 3 * d), ENC_OUT: (d, d), ENC_UP: (d, ff), ENC_DOWN: (ff, d),
        EMBED: (d, dec_d), DEC_QKV: (dec_d, 3 * dec_d), DEC_OUT: (dec_d, dec_d),
        DEC_UP: (dec_d, dec_ff), DEC_DOWN: (dec_ff, dec_d),
    }
    big = [
        shape(dims[k][1], dims[k][0] // 16) if k == DEC_DOWN else shape(dims[k][0] // 16, dims[k][1])
        for k in range(9)
    ]
    outs = dict(
        out_small=shape(SMALL_ROWS, d, F32),
        decoded_got=jax.ShapeDtypeStruct((SAMP_MB, PATCHES // 2, dec_d), BF16),
        gx=shape(rows, d),
        gx_got=shape(rows, d // 2),
    )
    single = finish_buffers(chunks, rows, d, ff, dec_total, dec_d)
    left = (4, 2, 2)
    lists = [[], [], [], [], []]
    for k in chunks:
        block = (k.rows, k.width)
        lists[0].append((left + block, BF16))
        if k.turned:
            lists[1].append((left + block, BF16))
        for stage in range(3):
            rest = [left[axis] for axis in (Z, Y, X) if axis not in k.order[: stage + 1]]
            count = 3 if k.order[stage] == Z else 1
            lists[2 + stage].append(((count, *rest, *block), BF16))
    blocks = sorted({(k.rows, k.width) for k in chunks})
    slots = [2 if block == (48, 384) else 1 for block in blocks]
    lists.append([(left + block, BF16) for block, m in zip(blocks, slots) for _ in range(m)])
    semaphores = dict(
        load_sem=(LOADS,), send_sem=(n, 11), recv_sem=(n, 11), small_sem=(2, 6), swap_sem=(4,)
    )

    def kernel(*refs):
        refs = list(refs)

        def take(count):
            taken = refs[:count]
            del refs[:count]
            return taken

        names = list(given) + list(outs)
        r = Names(names, take(len(names)))
        r.out = take(9)
        r.__dict__.update(zip(single, take(len(single))))
        r.acc = take(n)
        r.got = dict(zip([c for c, k in enumerate(chunks) if k.turned], take(len(lists[1]))))
        r.recv = [take(n) for _ in range(3)]
        r.stage = {block: take(m) for block, m in zip(blocks, slots)}
        r.__dict__.update(zip(semaphores, take(len(semaphores))))
        finish_kernel(chunks, groups, plan, r)

    flat = list(single.values()) + [b for group in lists for b in group]
    results = pl.pallas_call(
        kernel,
        out_shape=list(outs.values()) + big,
        in_specs=[in_hbm()] * n_hbm + in_vmem(len(given) - n_hbm),
        out_specs=in_vmem(len(outs) + 9),
        scratch_shapes=[pltpu.VMEM(*b) for b in flat]
        + [pltpu.SemaphoreType.DMA(v) for v in semaphores.values()],
        compiler_params=pltpu.CompilerParams(
            collective_id=1, has_side_effects=True, vmem_limit_bytes=FINISH_VMEM
        ),
        name="finish",
    )(*given.values())
    return write_outputs(results, given["decoded"], dims)


FINISH_VMEM = 62 * 2**20


def write_kernel(small, decoded_got, gx_own, gx_got, *refs):
    big, decoded_own = refs[:9], refs[9]
    decoded, gx, *totals = refs[10:]
    s = lax.axis_index("section")
    half = decoded.shape[1]
    samples, rows, columns = decoded_own.shape[0], gx_own.shape[0], gx.shape[1]
    own = decoded_own[:, pl.ds(pl.multiple_of(s * half, half), half), :]
    for side, part in ((s, own), (1 - s, decoded_got[...])):
        decoded[pl.ds(side * samples, samples)] = part
    own = gx_own[:, pl.ds(pl.multiple_of(s * columns, 128), columns)]
    for side, part in ((s, own), (1 - s, gx_got[...])):
        gx[pl.ds(pl.multiple_of(side * rows, rows), rows), :] = part
    d = lax.axis_index("dp")
    wide, narrow = small.shape[1], big[DEC_OUT].shape[1]

    def piece(out, line, lanes, position):
        size = out.shape[0]
        value = small[pl.ds(line, 1), :lanes]
        value = pltpu.roll(value, lax.rem(lanes - position * size, lanes), 1)
        out[...] = value[:, :size].reshape(size)

    def matrix(out, name):
        value = big[name][...].astype(F32)
        out[...] = jnp.transpose(value) if name == DEC_DOWN else value

    def block(outs, first_row, bup_row, lanes, names):
        for i, out in zip((0, 1, None, None, 2, 3, 4, None, None, None, 5), outs):
            if i is not None:
                piece(out, first_row + i, lanes, d)
        piece(outs[8], bup_row + d // 4, lanes, d % 4)
        for at, name in zip((2, 3, 7, 9), names):
            matrix(outs[at], name)

    block(totals[:11], 0, ROW_BUP, wide, (ENC_QKV, ENC_OUT, ENC_UP, ENC_DOWN))
    matrix(totals[11], EMBED)
    piece(totals[12], ROW_DEC + 7, narrow, d)
    piece(totals[13], ROW_DEC + 6, narrow, d)
    block(totals[14:], ROW_DEC, ROW_DEC_BUP, narrow, (DEC_QKV, DEC_OUT, DEC_UP, DEC_DOWN))


def write_outputs(results, decoded_own, dims):
    def vector(size):
        return jax.ShapeDtypeStruct((size // 16,), F32)

    def matrix(name):
        return shape(dims[name][0] // 16, dims[name][1], F32)

    def block(qkv, out, up, down):
        d, ff = dims[up]
        return [
            vector(d), vector(d), matrix(qkv), matrix(out), vector(d), vector(d), vector(d),
            matrix(up), vector(ff), matrix(down), vector(d),
        ]

    samples, half, width = results[1].shape
    rows, columns = results[3].shape
    out_shape = [
        jax.ShapeDtypeStruct((2 * samples, half, width), BF16),
        shape(2 * rows, columns),
        *block(ENC_QKV, ENC_OUT, ENC_UP, ENC_DOWN),
        matrix(EMBED),
        vector(width),
        vector(width),
        *block(DEC_QKV, DEC_OUT, DEC_UP, DEC_DOWN),
    ]
    return tuple(
        pl.pallas_call(
            write_kernel,
            out_shape=out_shape,
            in_specs=in_vmem(len(results) + 1),
            out_specs=in_vmem(len(out_shape)),
            compiler_params=pltpu.CompilerParams(vmem_limit_bytes=KERNEL_VMEM),
            name="write_outputs",
        )(*results, decoded_own)
    )


def reduce_plain(arrays, section_index):
    first = section_index == 0
    results = []
    for a in arrays:
        half = a.shape[1] // 2
        keep = lax.dynamic_slice_in_dim(a, section_index * half, half, 1)
        give = lax.dynamic_slice_in_dim(a, (1 - section_index) * half, half, 1)
        got = swapped(give, "section", 0)
        chip = (keep.astype(jnp.float32) + got.astype(jnp.float32)).astype(jnp.bfloat16)
        mine = lax.psum_scatter(chip, "dp", scatter_dimension=0, tiled=True)
        other = swapped(mine, "section", 0)
        whole = jnp.concatenate(
            [jnp.where(first, mine, other), jnp.where(first, other, mine)], axis=1
        )
        results.append(whole.astype(jnp.float32))
    return results


def finish_plain(acts, section_index):
    x, gy, seg_saved, enc, dec = acts["x"], acts["gy"], acts["saved"], acts["enc"], acts["dec"]
    gx, gf1, ga1, gqkv1, small1, gbup1 = encoder_backward(x, gy, seg_saved, enc["params"])
    small2, gbup2 = acts["small2"], acts["gbup2"]
    grads = (
        small1[0], small1[1], mm(enc["at"], gqkv1).astype(BF16), mm(enc["ot"], ga1).astype(BF16), small1[2],
        small1[3], small1[4], mm(enc["ct"], gf1).astype(BF16), gbup1[0], mm(enc["ut"], gy).astype(BF16),
        small1[5],
        weight_grad(acts["y"], acts["geb"]), small2[7], small2[6],
        small2[0], small2[1], mm(dec["at"], dec["gqkv"]).astype(BF16),
        mm(dec["ot"], dec["ga"]).astype(BF16), small2[2], small2[3], small2[4],
        mm(dec["ct"], dec["gf"]).astype(BF16), gbup2[0],
        jnp.transpose(mm(dec["gt"], dec["u"])).astype(BF16), small2[5],
    )
    groups = lax.axis_size("dp")
    big = reduce_plain([g for g in grads if g.ndim == 2], section_index)
    flat = jnp.concatenate([g.reshape(groups, -1) for g in grads if g.ndim == 1], axis=1)
    line = lax.psum_scatter(flat, ("dp"), scatter_dimension=0, tiled=True)
    line = lax.psum(line, "section")[0]
    totals, at = [], 0
    for g in grads:
        if g.ndim == 2:
            totals.append(big.pop(0))
        else:
            size = g.shape[0] // groups
            totals.append(line[at : at + size])
            at += size
    decoded = acts["decoded"].reshape(SAMP_MB, PATCHES, -1)
    first = section_index == 0

    def halves(whole):
        half = whole.shape[1] // 2
        keep = lax.dynamic_slice_in_dim(whole, section_index * half, half, 1)
        give = lax.dynamic_slice_in_dim(whole, (1 - section_index) * half, half, 1)
        got = swapped(give, "section", 0)
        return jnp.concatenate([jnp.where(first, keep, got), jnp.where(first, got, keep)])

    return (halves(decoded), halves(gx), *totals)


def shards(
    patches,
    segment_ids,
    patch_order,
    encoder_gain1,
    encoder_bias1,
    encoder_qkv,
    encoder_out,
    encoder_out_bias,
    encoder_gain2,
    encoder_bias2,
    encoder_up,
    encoder_up_bias,
    encoder_down,
    encoder_down_bias,
    embed_weight,
    embed_bias,
    mask_token,
    decoder_gain1,
    decoder_bias1,
    decoder_qkv,
    decoder_out,
    decoder_out_bias,
    decoder_gain2,
    decoder_bias2,
    decoder_up,
    decoder_up_bias,
    decoder_down,
    decoder_down_bias,
    cotangent,
):
    enc_params = (
        encoder_gain1,
        encoder_bias1,
        encoder_qkv,
        encoder_out,
        encoder_out_bias,
        encoder_gain2,
        encoder_bias2,
        encoder_up,
        encoder_up_bias,
        encoder_down,
        encoder_down_bias,
    )
    embed_params = (embed_weight, embed_bias, mask_token)
    dec_params = (
        decoder_gain1,
        decoder_bias1,
        decoder_qkv,
        decoder_out,
        decoder_out_bias,
        decoder_gain2,
        decoder_bias2,
        decoder_up,
        decoder_up_bias,
        decoder_down,
        decoder_down_bias,
    )
    section_index = lax.axis_index("section")
    y, at1, qkv, e, rl, o1, ot1, n2, s2, ct1, ut1, slope = encoder_forward(
        patches, segment_ids, enc_params
    )
    g = cotangent.reshape(-1, DECODER_WIDTH)
    decoded, at2, ot2, ct2, gt2, u2, gf2, ga2, gqkv2, geb, gy, small2, gbup2 = decoder_both(
        y, segment_ids, patch_order, g, embed_params, dec_params
    )
    acts = dict(
        x=patches,
        y=y,
        gy=gy,
        geb=geb,
        decoded=decoded,
        small2=small2,
        gbup2=gbup2,
        saved=(qkv, e, rl, o1, n2, s2, slope),
        enc=dict(at=at1, ot=ot1, ct=ct1, ut=ut1, params=enc_params),
        dec=dict(at=at2, ot=ot2, ct=ct2, gt=gt2, u=u2, gf=gf2, ga=ga2, gqkv=gqkv2),
    )
    if lax.axis_size("dp") == 16:
        return finish(acts)
    return finish_plain(acts, section_index)


def solution(mesh):
    in_specs = (
        P("dp", None),
        P("dp", None),
        P("dp", None),
        P(),
        P(),
        P(),
        P(),
        P(),
        P(),
        P(),
        P(),
        P(),
        P(),
        P(),
        P(),
        P(),
        P(),
        P(),
        P(),
        P(),
        P(),
        P(),
        P(),
        P(),
        P(),
        P(),
        P(),
        P(),
        P("dp", None, None),
    )
    out_specs = (
        P("dp", "section", None),
        P("dp", "section"),
        P("dp"),
        P("dp"),
        P("dp", None),
        P("dp", None),
        P("dp"),
        P("dp"),
        P("dp"),
        P("dp", None),
        P("dp"),
        P("dp", None),
        P("dp"),
        P("dp", None),
        P("dp"),
        P("dp"),
        P("dp"),
        P("dp"),
        P("dp", None),
        P("dp", None),
        P("dp"),
        P("dp"),
        P("dp"),
        P("dp", None),
        P("dp"),
        P("dp", None),
        P("dp"),
    )
    return jax.shard_map(shards, mesh=mesh, in_specs=in_specs, out_specs=out_specs, check_vma=False)
```

```python
import functools
import math

import jax
import jax.numpy as jnp
import numpy as np
from jax import lax
from jax.experimental import pallas as pl
from jax.experimental.pallas import tpu as pltpu
from jax.sharding import PartitionSpec as P

H_ENC = 12
DECODER_WIDTH = 512
H_DEC = 16
PATCHES = 128
SAMP_MB = 12


EPSILON = 1e-06
MASKED = -1e30


def swapped(block, axis, apart):
    count = lax.axis_size(axis)
    route = []
    for low in range(count):
        high = low | 1 << apart
        if high != low and high < count:
            route += [(low, high), (high, low)]
    return lax.ppermute(block, axis, route)


def positions(count, features):
    column = np.arange(features)
    rate = np.exp(-math.log(10000.0) * (2 * (column // 2)) / features)
    angles = np.arange(count)[:, None] * rate[None, :]
    return np.where(column % 2 == 0, np.sin(angles), np.cos(angles)).astype(np.float32)


def weight_grad(left_side, grads):
    return lax.dot_general(
        left_side, grads, (((0,), (0,)), ((), ())), preferred_element_type=jnp.float32
    ).astype(jnp.bfloat16)


BF16 = jnp.bfloat16
F32 = jnp.float32


def mm(left, right):
    return lax.dot_general(left, right, (((1,), (0,)), ((), ())), preferred_element_type=F32)


def mm_nt(left, right):
    return lax.dot_general(left, right, (((1,), (1,)), ((), ())), preferred_element_type=F32)


def mm_tn(left, right):
    return lax.dot_general(left, right, (((0,), (0,)), ((), ())), preferred_element_type=F32)


def normalise(x):
    center = x - jnp.mean(x, axis=-1, keepdims=True)
    scale = lax.rsqrt(jnp.mean(center * center, axis=-1, keepdims=True) + EPSILON)
    return center * scale, scale


def normalise_back(grad, n, scale, gain):
    gn = grad * gain
    mean_gn = jnp.mean(gn, axis=-1, keepdims=True)
    mean_gnn = jnp.mean(gn * n, axis=-1, keepdims=True)
    return (gn - mean_gn - n * mean_gnn) * scale


def rows_sum(x):
    return jnp.sum(x, axis=0, keepdims=True)


def gelu_both(f):
    c0, c1 = math.sqrt(2.0 / math.pi), 0.044715
    square = f * f
    half = 0.5 + 0.5 * jnp.tanh(f * (c0 + (c0 * c1) * square))
    u = f * half
    return u, half + u * (1.0 - half) * (2.0 * c0 + (6.0 * c0 * c1) * square)


def lanes(start, size):
    return slice(start, start + size) if isinstance(start, int) else pl.ds(pl.multiple_of(start, 128), size)


def lane_masks(head_size):
    lane = lax.broadcasted_iota(jnp.int32, (1, 128), 1)
    return [
        jnp.where((lane >= h * head_size) & (lane < (h + 1) * head_size), 1.0, 0.0).astype(BF16)
        for h in range(128 // head_size)
    ]


def stacked(x, masks):
    return jnp.concatenate([x * m for m in masks], axis=0)


def stacked_ones(x, masks, value):
    return jnp.concatenate(
        [jnp.broadcast_to(m * jnp.asarray(value, BF16), x.shape) for m in masks], axis=0
    )


def attention_forward(
    qkv_ref, o_ref, e_ref, rl_ref, rows, tokens, features, head_size, mask_ref, g
):
    masks = lane_masks(head_size)
    per_group = len(masks)
    factor = head_size ** (-0.5) * math.log2(math.e)
    q, k, v = (qkv_ref[rows, lanes(j * features + g * 128, 128)] for j in range(3))
    scores = mm_nt(q, stacked(k, masks))
    parts = []
    for h in range(per_group):
        part = scores[:, h * tokens : (h + 1) * tokens]
        if mask_ref is not None:
            part = jnp.where(mask_ref[...] > 0.0, part, MASKED)
        top = jnp.max(part, axis=-1, keepdims=True)
        parts.append(jnp.exp2((part - top) * factor).astype(BF16))
    e = jnp.concatenate(parts, axis=1)
    width = per_group * tokens
    e_ref[rows, lanes(g * width, width)] = e
    both = mm(e, jnp.concatenate([stacked(v, masks), stacked_ones(v, masks, 1.0)], axis=1))
    rl = 1.0 / both[:, 128:]
    rl_ref[rows, lanes(g * 128, 128)] = rl
    o_ref[rows, lanes(g * 128, 128)] = (both[:, :128] * rl).astype(BF16)


def attention_backward_group(q, k, v, e, go, o, rl, head_size):
    masks = lane_masks(head_size)
    per_group, tokens = len(masks), q.shape[0]
    scaling = head_size ** (-0.5)
    go = go.astype(F32) * rl
    go_low = go.astype(BF16)
    inner = (go * o.astype(F32)).astype(BF16)
    left = jnp.concatenate([go_low, inner], axis=1)
    right = jnp.concatenate([stacked(v, masks), stacked_ones(v, masks, -1.0)], axis=1)
    gs = (e.astype(F32) * mm_nt(left, right)).astype(BF16)

    def diagonal(wide):
        return jnp.concatenate(
            [
                wide[h * head_size : (h + 1) * head_size, h * tokens : (h + 1) * tokens]
                for h in range(per_group)
            ],
            axis=0,
        )

    gq = mm(gs, stacked(k, masks)) * scaling
    gk = jnp.transpose(diagonal(mm_tn(q, gs)) * scaling)
    gv = jnp.transpose(diagonal(mm_tn(go_low, e)))
    return gq.astype(BF16), gk.astype(BF16), gv.astype(BF16)


def attention_backward(
    qkv_ref, go_ref, o_ref, e_ref, rl_ref, gqkv_ref, rows, tokens, features, head_size, g
):
    width = 128 // head_size * tokens
    at = lanes(g * 128, 128)
    spots = [lanes(j * features + g * 128, 128) for j in range(3)]
    q, k, v = (qkv_ref[rows, spot] for spot in spots)
    e = e_ref[rows, lanes(g * width, width)]
    grads = attention_backward_group(
        q, k, v, e, go_ref[rows, at], o_ref[rows, at], rl_ref[rows, at], head_size
    )
    for spot, grad in zip(spots, grads):
        gqkv_ref[rows, spot] = grad


def tiles(extent, size, body):
    def step(t, carry):
        body(pl.ds(pl.multiple_of(t * size, size), size))
        return carry

    lax.fori_loop(0, extent // size, step, 0)


def feed_forward(c_ref, up_ref, bup_ref, u_ref, slope_ref, tile, ut_ref=None):
    def body(at):
        f = mm(c_ref[...], up_ref[:, at]) + bup_ref[at].reshape(1, tile)
        u, slope = gelu_both(f)
        u = u.astype(BF16)
        u_ref[:, at] = u
        slope_ref[:, at] = slope.astype(BF16)
        if ut_ref is not None:
            ut_ref[at, :] = jnp.transpose(u)

    tiles(up_ref.shape[1], tile, body)


def feed_forward_back(gm_ref, down_ref, slope_ref, gf_ref, gbup_ref, tile):
    def body(at):
        gu = mm_nt(gm_ref[...], down_ref[at, :])
        gf = (gu * slope_ref[:, at].astype(F32)).astype(BF16)
        gf_ref[:, at] = gf
        gbup_ref[:, at] += rows_sum(gf.astype(F32))

    tiles(down_ref.shape[0], tile, body)


def project(left_ref, right_ref, out_ref, tile, bias_ref=None, more_ref=None):
    def body(at):
        value = mm(left_ref[...], right_ref[:, at])
        if bias_ref is not None:
            value = value + bias_ref[at].reshape(1, tile)
        if more_ref is not None:
            value = more_ref[:, at].astype(F32) + value
        out_ref[:, at] = value.astype(out_ref.dtype)

    tiles(right_ref.shape[1], tile, body)


def project_back(left_ref, right_ref, out_ref, tile):
    def body(at):
        out_ref[:, at] = mm_nt(left_ref[...], right_ref[at, :]).astype(out_ref.dtype)

    tiles(right_ref.shape[0], tile, body)


def row(ref):
    return ref[...].reshape(1, -1)


def segment_mask(seg_ref, section):
    seg = seg_ref[pl.ds(section, 1), :].astype(F32)
    rows = seg.shape[1]
    column = jnp.transpose(jnp.broadcast_to(seg, (128, rows)))
    return jnp.concatenate([column] * (rows // 128), axis=1) == seg


class Writer:
    def __init__(self, semaphores):
        self.semaphores, self.copies = semaphores, []

    def start(self, source, target):
        copy = pltpu.make_async_copy(source, target, self.semaphores.at[len(self.copies)])
        copy.start()
        self.copies.append(copy)

    def wait(self):
        for copy in self.copies:
            copy.wait()


def encoder_forward_kernel(
    x_ref, seg_ref,
    gain1, bias1, w_qkv, w_out, b_out, gain2, bias2, w_up, b_up, w_down, b_down,
    *refs,
):
    outs, scratch = refs[:12], refs[12:24]
    y_ref, at_ref, qkv_ref, e_ref, rl_ref, o_ref, ot_ref, n2_ref, s2_ref, ct_ref, ut_ref, slope_ref = scratch
    h_ref, c_ref, u_ref, mask_ref, qkv_v, out_v, up_v, down_v, sem, out_sem = refs[24:]
    target = {id(v): o for v, o in zip(scratch, outs)}
    writer = Writer(out_sem)

    def write(*done):
        for v in done:
            writer.start(v, target[id(v)])

    tokens, features = y_ref.shape
    pairs = ((w_qkv, qkv_v), (w_out, out_v), (w_up, up_v), (w_down, down_v))
    loads = [pltpu.make_async_copy(w, v, sem.at[i]) for i, (w, v) in enumerate(pairs)]
    for load in loads:
        load.start()
    section = lax.axis_index("section")

    def first_norm(at):
        x = x_ref[pl.ds(pl.multiple_of(section * tokens + at.start, 128), at.size), :].astype(F32)
        h_ref[at, :] = x
        n1, _ = normalise(x)
        a = (n1 * row(gain1) + row(bias1)).astype(BF16)
        c_ref[at, :] = a
        at_ref[:, at] = jnp.transpose(a)

    tiles(tokens, 384, first_norm)
    mask_ref[...] = jnp.where(segment_mask(seg_ref, section), 1.0, 0.0)
    loads[0].wait()
    project(c_ref, qkv_v, qkv_ref, 768)
    write(at_ref, qkv_ref)

    def group(g, carry):
        attention_forward(
            qkv_ref, o_ref, e_ref, rl_ref, slice(None), tokens, features, features // H_ENC,
            mask_ref, g,
        )
        ot_ref[lanes(g * 128, 128), :] = jnp.transpose(o_ref[:, lanes(g * 128, 128)])
        return carry

    lax.fori_loop(0, features // 128, group, 0, unroll=E_UNROLL)
    write(e_ref, rl_ref, o_ref, ot_ref)
    loads[1].wait()
    project(o_ref, out_v, h_ref, 768, b_out, h_ref)

    def second_norm(at):
        n2, s2 = normalise(h_ref[at, :])
        n2_ref[at, :] = n2
        s2_ref[at, :] = s2
        c = (n2 * row(gain2) + row(bias2)).astype(BF16)
        c_ref[at, :] = c
        ct_ref[:, at] = jnp.transpose(c)

    tiles(tokens, 384, second_norm)
    write(n2_ref, s2_ref, ct_ref)
    loads[2].wait()
    feed_forward(c_ref, up_v, b_up, u_ref, slope_ref, 768, ut_ref)
    write(ut_ref, slope_ref)
    loads[3].wait()
    project(u_ref, down_v, y_ref, 256, b_down, h_ref)
    write(y_ref)
    writer.wait()


def encoder_backward_kernel(
    x_ref, gy_ref, qkv_ref, e_ref, rl_ref, o_ref, n2_ref, s2_ref, slope_ref,
    gain1, w_qkv, w_out, gain2, w_up, w_down,
    gx_ref, gf_ref, ga_ref, gqkv_ref, small_ref, gbup_ref,
    gh_ref, go_ref,
):
    tokens, features = gy_ref.shape
    section = lax.axis_index("section")
    x = x_ref[pl.ds(pl.multiple_of(section * tokens, tokens), tokens), :].astype(F32)
    gbup_ref[...] = jnp.zeros_like(gbup_ref)
    feed_forward_back(gy_ref, w_down, slope_ref, gf_ref, gbup_ref, 512)
    gc = mm_nt(gf_ref[...], w_up[...])
    g = gy_ref[...].astype(F32)
    n2 = n2_ref[...]
    gh = g + normalise_back(gc, n2, s2_ref[...], row(gain2))
    gh_ref[...] = gh
    ga_ref[...] = gh.astype(BF16)
    small_ref[2:3, :] = rows_sum(gh)
    small_ref[3:4, :] = rows_sum(gc * n2)
    small_ref[4:5, :] = rows_sum(gc)
    small_ref[5:6, :] = rows_sum(g)
    go_ref[...] = mm_nt(ga_ref[...], w_out[...]).astype(BF16)
    for g in range(features // 128):
        attention_backward(
            qkv_ref, go_ref, o_ref, e_ref, rl_ref, gqkv_ref, slice(None), tokens, features,
            features // H_ENC, g,
        )
    gn = mm_nt(gqkv_ref[...], w_qkv[...])
    n1, s1 = normalise(x)
    small_ref[0:1, :] = rows_sum(gn * n1)
    small_ref[1:2, :] = rows_sum(gn)
    gx_ref[...] = (gh_ref[...] + normalise_back(gn, n1, s1, row(gain1))).astype(BF16)


def split_low(x):
    high = x.astype(BF16)
    return high, (x - high.astype(F32)).astype(BF16)


def place_slots(order_ref, seg, section, hot_ref, place_ref, empty_ref):
    packed = seg.shape[1]
    line = lax.broadcasted_iota(jnp.int32, (PATCHES, PATCHES), 0).astype(F32)
    line_low = line.astype(BF16)
    lane_low = lax.broadcasted_iota(jnp.int32, (8, PATCHES), 1).astype(F32).astype(BF16)
    column = lax.broadcasted_iota(jnp.int32, (PATCHES, packed), 1).astype(F32)
    packed_line = lax.broadcasted_iota(jnp.int32, (packed, PATCHES), 0).astype(F32)

    def one_sample(j, carry):
        at = pl.ds(pl.multiple_of(j * PATCHES, PATCHES), PATCHES)
        order = order_ref[pl.ds(section * SAMP_MB + j, 1), :].astype(F32)
        hit = jnp.where(order == line, 1.0, 0.0).astype(BF16)
        mine = lax.convert_element_type(j, F32)
        start = jnp.sum(jnp.where(seg < mine, 1.0, 0.0), axis=1, keepdims=True)
        count = jnp.sum(jnp.where(seg == mine, 1.0, 0.0), axis=1, keepdims=True)
        down, across = mm(hit, line_low), mm_nt(lane_low, hit)[:1, :]
        down = jnp.where(down < count, start + down, -1.0)
        across = jnp.where(across < count, start + across, -1.0)
        wide = jnp.concatenate([down] * (packed // PATCHES), axis=1)
        hot_ref[at, :] = jnp.where(column == wide, 1.0, 0.0).astype(BF16)
        place_ref[:, at] = jnp.where(packed_line == across, 1.0, 0.0).astype(BF16)
        empty_ref[at, :] = jnp.where(down < 0.0, 1.0, 0.0)
        return carry

    lax.fori_loop(0, SAMP_MB, one_sample, 0, unroll=2)


def decoder_kernel(
    y_ref, seg_ref, order_ref, pos_ref, g_hbm,
    w_embed_hbm, b_embed, mask_token,
    gain1, bias1, w_qkv_hbm, w_out_hbm, b_out, gain2, bias2, w_up_hbm, b_up, w_down_hbm, b_down,
    *refs,
):
    hbm, (geb_ref, gy_ref, small_ref, gbup_ref) = refs[:9], refs[9:13]
    buffers = refs[13:22]
    out_ref, at_ref, ot_ref, ct_ref, gt_ref, u_ref, gf_ref, ga_ref, gqkv_ref = buffers
    (
        e2_ref, z_ref, s1_ref, e_ref, rl_ref, h_ref, s2_ref, go_ref, ge_ref, o_ref, c_ref, qkv_ref,
        slope_ref, sum_ref, g_all, hot_ref, place_ref, empty_ref, w_embed, w_qkv, w_out, w_up, w_down,
        w_sem, out_sem,
    ) = refs[22:]
    packed = y_ref.shape[0]
    rows, features = z_ref.shape
    samples = rows // PATCHES
    head_size = features // H_DEC
    total = g_all.shape[0]
    section = lax.axis_index("section")
    mine = pl.ds(pl.multiple_of(section * total, total), total)
    pairs = (
        (w_embed_hbm, w_embed), (w_qkv_hbm, w_qkv), (w_out_hbm, w_out), (w_up_hbm, w_up),
        (w_down_hbm, w_down), (g_hbm.at[mine, :], g_all),
    )
    loads = [pltpu.make_async_copy(a, b, w_sem.at[i]) for i, (a, b) in enumerate(pairs)]
    for load in loads:
        load.start()

    def write(at, *which):
        copies = []
        for i in which:
            target = hbm[i].at[:, at] if 1 <= i <= 4 else hbm[i].at[at, :]
            copies.append(pltpu.make_async_copy(buffers[i], target, out_sem.at[i]))
            copies[-1].start()
        return copies

    small_ref[...] = jnp.zeros_like(small_ref)
    gbup_ref[...] = jnp.zeros_like(gbup_ref)
    ge_ref[...] = jnp.zeros_like(ge_ref)
    seg = seg_ref[pl.ds(section, 1), :].astype(F32)
    place_slots(order_ref, seg, section, hot_ref, place_ref, empty_ref)
    loads[0].wait()
    high, low = split_low(mm(y_ref[...], w_embed[...]) + row(b_embed))
    e2_ref[:packed, :] = high
    e2_ref[packed:, :] = low
    for load in loads[1:]:
        load.wait()

    def one_step(step, carry):
        here = pl.ds(pl.multiple_of(step * rows, rows), rows)

        def first_norm(at):
            there = pl.ds(pl.multiple_of(step * rows + at.start, 128), at.size)
            one_hot = hot_ref[there, :]
            empty = jnp.concatenate([empty_ref[there, :]] * (features // 128), axis=1)
            twice = jnp.concatenate([one_hot, one_hot], axis=1)
            z = mm(twice, e2_ref[...]) + empty * row(mask_token)
            z = z + jnp.concatenate([pos_ref[...]] * (at.size // PATCHES), axis=0)
            n1, s1 = normalise(z)
            z_ref[at, :] = z
            s1_ref[at, :] = s1
            a = (n1 * row(gain1) + row(bias1)).astype(BF16)
            c_ref[at, :] = a
            at_ref[:, at] = jnp.transpose(a)

        tiles(rows, NORM_ROWS, first_norm)
        writing = write(here, 1)
        project(c_ref, w_qkv, qkv_ref, 512)

        def forward(b, carry):
            at = pl.ds(pl.multiple_of(b * PATCHES, PATCHES), PATCHES)
            for g in range(features // 128):
                attention_forward(
                    qkv_ref, o_ref, e_ref, rl_ref, at, PATCHES, features, head_size, None, g
                )
            ot_ref[:, at] = jnp.transpose(o_ref[at, :])
            return carry

        lax.fori_loop(0, samples, forward, 0, unroll=2)
        project(o_ref, w_out, h_ref, 512, b_out, z_ref)

        def second_norm(at):
            n2, s2 = normalise(h_ref[at, :])
            s2_ref[at, :] = s2
            c = (n2 * row(gain2) + row(bias2)).astype(BF16)
            c_ref[at, :] = c
            ct_ref[:, at] = jnp.transpose(c)

        tiles(rows, NORM_ROWS, second_norm)
        feed_forward(c_ref, w_up, b_up, u_ref, slope_ref, 512)
        writing += write(here, 2, 3, 5)
        project(u_ref, w_down, out_ref, 256, b_down, h_ref)

        def turn(at):
            gt_ref[:, at] = jnp.transpose(
                g_all[pl.ds(pl.multiple_of(step * rows + at.start, 128), at.size), :]
            )

        tiles(rows, NORM_ROWS, turn)
        g_ref = g_all.at[here, :]
        feed_forward_back(g_ref, w_down, slope_ref, gf_ref, gbup_ref, 512)
        writing += write(here, 0, 4, 6)
        project_back(gf_ref, w_up, sum_ref, 256)

        def second_back(at):
            there = pl.ds(pl.multiple_of(step * rows + at.start, 128), at.size)
            g, gc, h = g_all[there, :].astype(F32), sum_ref[at, :], h_ref[at, :]
            n2 = (h - jnp.mean(h, axis=-1, keepdims=True)) * s2_ref[at, :]
            gh = g + normalise_back(gc, n2, s2_ref[at, :], row(gain2))
            small_ref[2:3, :] += rows_sum(gh)
            small_ref[3:4, :] += rows_sum(gc * n2)
            small_ref[4:5, :] += rows_sum(gc)
            small_ref[5:6, :] += rows_sum(g)
            h_ref[at, :] = gh
            ga_ref[at, :] = gh.astype(BF16)

        tiles(rows, NORM_ROWS, second_back)
        project_back(ga_ref, w_out, go_ref, 512)
        writing += write(here, 7)

        def backward(b, carry):
            at = pl.ds(pl.multiple_of(b * PATCHES, PATCHES), PATCHES)
            for g in range(features // 128):
                attention_backward(
                    qkv_ref, go_ref, o_ref, e_ref, rl_ref, gqkv_ref, at, PATCHES, features,
                    head_size, g,
                )
            return carry

        lax.fori_loop(0, samples, backward, 0, unroll=2)
        writing += write(here, 8)
        project_back(gqkv_ref, w_qkv, sum_ref, 256)

        def first_back(at):
            there = pl.ds(pl.multiple_of(step * rows + at.start, 128), at.size)
            gn, z = sum_ref[at, :], z_ref[at, :]
            n1 = (z - jnp.mean(z, axis=-1, keepdims=True)) * s1_ref[at, :]
            gz = h_ref[at, :] + normalise_back(gn, n1, s1_ref[at, :], row(gain1))
            empty = jnp.concatenate([empty_ref[there, :]] * (features // 128), axis=1)
            small_ref[0:1, :] += rows_sum(gn * n1)
            small_ref[1:2, :] += rows_sum(gn)
            small_ref[6:7, :] += rows_sum(gz * empty)
            c_ref[at, :] = gz.astype(BF16)

        tiles(rows, NORM_ROWS, first_back)
        ge_ref[...] += mm(place_ref[:, here], c_ref[...])
        for copy in writing:
            copy.wait()
        return carry

    lax.fori_loop(0, total // rows, one_step, 0)
    ge = ge_ref[...]
    small_ref[7:8, :] = rows_sum(ge)
    geb_ref[...] = ge.astype(BF16)
    gy_ref[...] = mm_nt(geb_ref[...], w_embed[...]).astype(BF16)


NORM_ROWS, E_UNROLL = 384, 2


def in_vmem(count):
    return [pl.BlockSpec(memory_space=pltpu.VMEM)] * count


def in_hbm():
    return pl.BlockSpec(memory_space=pl.ANY)


def shape(rows, columns, dtype=BF16):
    return jax.ShapeDtypeStruct((rows, columns), dtype)


KERNEL_VMEM = 60 * 2**20


def encoder_forward(x, segments, params):
    rows, d = x.shape[0] // 2, x.shape[1]
    ff = params[7].shape[1]
    outs = [
        (rows, d, BF16),
        (d, rows, BF16),
        (rows, 3 * d, BF16),
        (rows, H_ENC * rows, BF16),
        (rows, d, F32),
        (rows, d, BF16),
        (d, rows, BF16),
        (rows, d, F32),
        (rows, 1, F32),
        (d, rows, BF16),
        (ff, rows, BF16),
        (rows, ff, BF16),
    ]
    more = [(rows, d, F32), (rows, d, BF16), (rows, ff, BF16), (rows, rows, F32)]
    args = [x, segments, *params]
    matrices = [w for w in params if w.dtype == BF16]
    return pl.pallas_call(
        encoder_forward_kernel,
        out_shape=[shape(*o) for o in outs],
        in_specs=in_vmem(2) + [in_hbm() if w.dtype == BF16 else in_vmem(1)[0] for w in params],
        out_specs=[in_hbm()] * len(outs),
        scratch_shapes=[pltpu.VMEM((r, w), t) for r, w, t in outs + more]
        + [pltpu.VMEM(w.shape, BF16) for w in matrices]
        + [pltpu.SemaphoreType.DMA((len(matrices),)), pltpu.SemaphoreType.DMA((len(outs),))],
        compiler_params=pltpu.CompilerParams(vmem_limit_bytes=KERNEL_VMEM),
        name="encoder_forward",
    )(*args)


def encoder_backward(x, gy, saved, params):
    gain1, _, w_qkv, w_out, _, gain2, _, w_up, _, w_down, _ = params
    rows, d = gy.shape
    ff = w_up.shape[1]
    outs = [
        shape(rows, d),
        shape(rows, ff),
        shape(rows, d),
        shape(rows, 3 * d),
        shape(8, d, F32),
        shape(1, ff, F32),
    ]
    args = [x, gy, *saved, gain1, w_qkv, w_out, gain2, w_up, w_down]
    return pl.pallas_call(
        encoder_backward_kernel,
        out_shape=outs,
        in_specs=in_vmem(len(args)),
        out_specs=in_vmem(len(outs)),
        scratch_shapes=[pltpu.VMEM((rows, d), F32), pltpu.VMEM((rows, d), BF16)],
        compiler_params=pltpu.CompilerParams(vmem_limit_bytes=KERNEL_VMEM),
        name="encoder_backward",
    )(*args)


def decoder_both(y, segments, orders, g, embed_params, params):
    packed, d_enc = y.shape
    total, d = g.shape[0] // 2, g.shape[1]
    rows = 6 * PATCHES
    ff = params[7].shape[1]
    args = [y, segments, orders, positions(PATCHES, d), g, *embed_params, *params]
    in_specs = in_vmem(4) + [in_hbm()]
    in_specs += [in_hbm() if x.dtype == BF16 else in_vmem(1)[0] for x in args[5:]]
    wide = [ff, ff, d, 3 * d]
    outs = [shape(total, d)] + [shape(d, total)] * 4 + [shape(total, w) for w in wide]
    buffers = [(rows, d, BF16)] + [(d, rows, BF16)] * 4 + [(rows, w, BF16) for w in wide]
    last = [shape(packed, d), shape(packed, d_enc), shape(8, d, F32), shape(1, ff, F32)]
    scratch = [
        (2 * packed, d, BF16),
        (rows, d, F32),
        (rows, 1, F32),
        (rows, H_DEC * PATCHES, BF16),
        (rows, d, F32),
        (rows, d, F32),
        (rows, 1, F32),
        (rows, d, BF16),
        (packed, d, F32),
        (rows, d, BF16),
        (rows, d, BF16),
        (rows, 3 * d, BF16),
        (rows, ff, BF16),
        (rows, d, F32),
        (total, d, BF16),
        (total, packed, BF16),
        (packed, total, BF16),
        (total, 128, F32),
    ]
    matrices = [x for x in args[5:] if x.dtype == BF16]
    return pl.pallas_call(
        decoder_kernel,
        out_shape=outs + last,
        in_specs=in_specs,
        out_specs=[in_hbm()] * len(outs) + in_vmem(len(last)),
        scratch_shapes=[pltpu.VMEM((r, w), t) for r, w, t in buffers + scratch]
        + [pltpu.VMEM(x.shape, BF16) for x in matrices]
        + [pltpu.SemaphoreType.DMA((k,)) for k in (len(matrices) + 1, len(outs))],
        compiler_params=pltpu.CompilerParams(vmem_limit_bytes=KERNEL_VMEM),
        name="decoder_both",
    )(*args)


MESH = pl.DeviceIdType.MESH
ENC_QKV, ENC_OUT, ENC_UP, ENC_DOWN, EMBED, DEC_QKV, DEC_OUT, DEC_UP, DEC_DOWN = range(9)
GIVE, PAIR, FFN, LN2, GO, ATT, GN, LAST = range(10, 18)
SMALL = -1
ROW_BUP, ROW_DEC_BUP, ROW_DEC, SMALL_ROWS = 6, 10, 16, 24
Z, Y, X, CORE = range(4)
ORDERS = ((X, Y, Z), (Y, X, Z), (X, Z, Y), (Y, Z, X), (Z, X, Y), (Z, Y, X))


class Chunk:
    def __init__(self, name, half, offset, rows, width, first_row=None):
        self.name, self.half, self.offset, self.rows, self.width = name, half, offset, rows, width
        self.first_row, self.turned, self.order = first_row, name == DEC_DOWN, None
        self.decoder = name in (DEC_QKV, DEC_UP, DEC_OUT)

    def columns(self, side):
        return pl.ds(pl.multiple_of(side * self.half + self.offset, 128), self.width)

    def place(self, side):
        if self.turned:
            return (pl.ds(pl.multiple_of(side * self.half + self.offset, 128), self.rows), slice(None))
        if self.first_row is None:
            return (slice(None), self.columns(side))
        return (pl.ds(self.first_row, self.rows), self.columns(side))

    @property
    def bytes(self):
        return 32 * self.rows * self.width

    def loads(self, order):
        if order[0] == Z:
            return (2 * self.bytes, self.bytes / 4, self.bytes / 8)
        if order[1] == Z:
            return (self.bytes, self.bytes, self.bytes / 8)
        return (self.bytes, self.bytes / 2, self.bytes / 2)


LINK_ORDERS = (0, 1, 2, 4, 3, 0, 3, 0, 3, 3, 0, 0, 0, 0, 1)


def make_chunks():
    chunks = [Chunk(ENC_DOWN, 384, 0, 48, 384, 48 * q) for q in range(4)]
    chunks += [Chunk(ENC_UP, 1536, 768 * q, 48, 768) for q in range(2)]
    chunks += [Chunk(ENC_OUT, 384, 0, 48, 384)]
    chunks += [Chunk(ENC_QKV, 1152, 0, 48, 768), Chunk(ENC_QKV, 1152, 768, 48, 384)]
    chunks += [Chunk(EMBED, 256, 0, 48, 256)]
    chunks += [Chunk(DEC_QKV, 768, 0, 32, 768), Chunk(DEC_DOWN, 256, 0, 256, 128)]
    chunks += [Chunk(DEC_UP, 1024, o, 32, 512) for o in (0, 512)]
    chunks += [Chunk(DEC_OUT, 256, 0, 32, 256)]
    for chunk, order in zip(chunks, LINK_ORDERS):
        chunk.order = ORDERS[order]
    return chunks


def make_groups(chunks):
    return [[c] for c in range(len(chunks))]


def product_cost(k, count):
    if k.turned:
        return 5.0
    return k.rows * k.width * (0.9 / 8192 if k.decoder else 0.6 / 18432)


def tasks_in_order(chunks, groups):
    def gives(name):
        found = [(g, chunks[m[0]], len(m)) for g, m in enumerate(groups)]
        kind = PAIR if name == DEC_DOWN else GIVE
        return [(kind, g, product_cost(k, size)) for g, k, size in found if k.name == name]

    tasks = gives(ENC_DOWN)
    tasks += [(FFN, t, 1.7) for t in range(4)] + gives(ENC_UP)
    tasks += [(LN2, 0, 1.0), (GO, 0, 0.9)]
    tasks += [(ATT, g, 1.5) for g in range(6)]
    tasks += gives(ENC_OUT) + gives(ENC_QKV) + gives(EMBED)
    tasks += gives(DEC_QKV) + gives(DEC_DOWN)
    tasks += [(GN, j, 0.9) for j in range(3)] + [(LAST, 0, 1.5)]
    return tasks + gives(DEC_UP) + gives(DEC_OUT)


def decoder_arrays(chunks):
    names = []
    for k in chunks:
        if (k.decoder or k.turned) and k.name not in names:
            names.append(k.name)
    return names


def make_plan(chunks, groups):
    tasks = tasks_in_order(chunks, groups)
    lhs = decoder_arrays(chunks)
    free = [0.0] * 4
    rate = [80e3, 80e3, 80e3, 500e3]
    pending, plan, now, owned = [], [], 2.0, set()

    def send(link, size, latency):
        begin = max(now, free[link])
        free[link] = begin + size / rate[link]
        return free[link] + latency

    def blocked(task):
        if task[0] not in (GIVE, PAIR):
            return False
        name = chunks[groups[task[1]][0]].name
        if name not in lhs[2:]:
            return False
        name = lhs[lhs.index(name) - 2]
        return any(chunks[m[0]].name == name and g not in owned for g, m in enumerate(groups))

    while tasks or pending:
        pending.sort()
        if pending and (pending[0][0] <= now or not tasks or blocked(tasks[0])):
            arrive, stage, c = pending.pop(0)
            now = max(now, arrive)
            plan.append((stage, c))
            if c == SMALL:
                now += 0.1
                if stage < 4:
                    pending.append((now + 2.0, stage + 1, c))
                continue
            members = groups[c] if stage == 1 else [c]
            k = chunks[members[0]]
            if stage == 1:
                owned.add(c)
                now += 0.6 if k.turned else product_cost(k, len(members)) + 0.2 * len(members)
            else:
                now += 0.25
            for c in members:
                k = chunks[c]
                if stage < 4:
                    axis = k.order[stage - 1]
                    latency = 2.0 if axis == Z else 1.5
                    arrive = send(axis, k.loads(k.order)[stage - 1], latency)
                    pending.append((arrive, stage + 1, c))
                elif stage == 4:
                    pending.append((send(CORE, k.bytes / 16, 1.0), 5, c))
            continue
        name, arg, cost = tasks.pop(0)
        plan.append((name, arg))
        now += cost
        if name in (GIVE, PAIR):
            arrive = [send(CORE, chunks[c].bytes, 1.0) for c in groups[arg]]
            pending.append((max(arrive), 1, arg))
        elif name == LAST:
            pending.append((now + 2.0, 1, SMALL))
    return plan


class Ring:
    def __init__(self, sources, slots, semaphores, depth):
        self.copies = [
            pltpu.make_async_copy(source, slot, semaphores())
            for source, slot in zip(sources, slots)
        ]
        self.slots, self.depth, self.at = slots, depth, 0

    def begin(self):
        for copy in self.copies[: self.depth]:
            copy.start(priority=1)

    def take(self):
        self.copies[self.at].wait()
        return self.slots[self.at]

    def done(self):
        ahead = self.at + self.depth
        if ahead < len(self.copies):
            self.copies[ahead].start(priority=1)
        self.at += 1


class Names:
    def __init__(self, names, refs):
        self.__dict__.update(zip(names, refs))


LOADS = 96


def finish_kernel(chunks, groups, plan, r):
    n = len(chunks)
    s = lax.axis_index("section")
    d = lax.axis_index("dp")
    here = (d // 4, (d // 2) % 2, d % 2)
    z, y, x = here
    sibling = {"section": 1 - s}
    z_at = [lax.rem(z + k, 4) for k in (1, 2, 3)]
    peers = {
        X: [(1 - x, {"dp": d + 1 - 2 * x})],
        Y: [(1 - y, {"dp": d + 2 - 4 * y})],
        Z: [(p, {"dp": d + 4 * (p - z)}) for p in z_at],
    }
    every = [sibling] + [peer for axis in (X, Y, Z) for _, peer in peers[axis]]

    barrier = pltpu.get_barrier_semaphore()
    for peer in every:
        pl.semaphore_signal(barrier, inc=1, device_id=peer, device_id_type=MESH)

    counter = iter(range(LOADS))

    def semaphore():
        return r.load_sem.at[next(counter)]

    def remote(src, dst, send, recv, peer):
        return pltpu.make_async_remote_copy(
            src_ref=src, dst_ref=dst, send_sem=send, recv_sem=recv, device_id=peer, device_id_type=MESH
        )

    rhs_of = {DEC_QKV: r.gqkv2, DEC_UP: r.gf2, DEC_OUT: r.ga2}
    lhs_of = {DEC_QKV: r.at2, DEC_UP: r.ct2, DEC_OUT: r.ot2, DEC_DOWN: r.gt2}
    tiles, widths, last_use = [], [], {}

    def wide_columns(g, side):
        k, width = chunks[groups[g][0]], sum(chunks[c].width for c in groups[g])
        return pl.ds(pl.multiple_of(side * k.half + k.offset, 128), width)

    for i, (name, arg) in enumerate(plan):
        if name == PAIR:
            tiles += [r.u2.at[:, t * 512 : (t + 1) * 512] for t in range(4)]
            last_use[DEC_DOWN] = i
        elif name in (GIVE, 1) and arg != SMALL and chunks[groups[arg][0]].decoder:
            k = chunks[groups[arg][0]]
            tiles.append(rhs_of[k.name].at[:, wide_columns(arg, 1 - s if name == GIVE else s)])
            last_use[k.name] = i
    lhs_names = decoder_arrays(chunks)
    assert sorted(lhs_names, key=last_use.get) == lhs_names
    rhs_slots = [r.rhs.at[i % 2, :, : tile.shape[1]] for i, tile in enumerate(tiles)]
    rhs = Ring(tiles, rhs_slots, semaphore, 2)
    lhs = Ring([lhs_of[k] for k in lhs_names], [r.lhs.at[i % 2] for i in range(4)], semaphore, 2)
    tokens, d_enc = r.gy.shape
    blocks = []
    for t in range(4):
        at = pl.ds(t * d_enc, d_enc)
        blocks += [r.w_down.at[at, :], r.w_up.at[:, at]]
    blocks.append(r.w_out)
    blocks += [r.w_qkv.at[:, pl.ds(j * d_enc, d_enc)] for j in range(3)]
    weights = Ring(blocks, [r.w.at[i % 4] for i in range(12)], semaphore, 4)
    e_width = 2 * tokens
    e_ring = Ring(
        [r.e.at[:, pl.ds(g * e_width, e_width)] for g in range(6)],
        [r.e_v.at[g % 2] for g in range(6)],
        semaphore,
        2,
    )

    def load(source, target):
        return pltpu.make_async_copy(source, target, semaphore())

    mine = pl.ds(pl.multiple_of(s * tokens, tokens), tokens)
    load_gy, load_slope, load_ut = load(r.gy, r.gy_v), load(r.slope, r.slope_v), load(r.ut, r.ut_v)
    load_ct, load_at, load_ot = load(r.ct, r.ct_v), load(r.at, r.at_v), load(r.ot, r.ot_v)
    load_n2, load_s2, load_qkv = load(r.n2, r.n2_v), load(r.s2, r.s2_v), load(r.qkv, r.qkv_v)
    load_o, load_rl, load_x = load(r.o, r.o_v), load(r.rl, r.rl_v), load(r.x.at[mine, :], r.x_v)
    load_y, load_geb = load(r.y, r.y_v), load(r.geb, r.geb_v)
    load_gy.start(priority=1)
    load_ut.start(priority=1)
    load_slope.start(priority=1)
    weights.begin()
    begun = [
        (load_ct, load_n2, load_s2),
        (load_qkv, load_o, load_rl, e_ring),
        (load_ot, load_at, load_y, load_geb),
        (load_x, lhs, rhs),
    ]

    def begin_some():
        for copy in begun.pop(0) if begun else ():
            copy.begin() if isinstance(copy, Ring) else copy.start(priority=1)

    half = r.decoded.shape[1] // 2
    give_half = r.decoded.at[:, pl.ds(pl.multiple_of((1 - s) * half, half), half), :]
    decoded_away = remote(give_half, r.decoded_got, r.swap_sem.at[0], r.swap_sem.at[1], sibling)
    gx_columns = d_enc // 2
    gx_half = r.gx.at[:, pl.ds(pl.multiple_of((1 - s) * gx_columns, 128), gx_columns)]
    gx_away = remote(gx_half, r.gx_got, r.swap_sem.at[2], r.swap_sem.at[3], sibling)

    small = r.small
    small[...] = jnp.zeros_like(small)
    small[ROW_DEC : ROW_DEC + 8, : r.small2.shape[1]] = r.small2[...]
    quarter = r.gbup2.shape[1] // 4
    for i in range(4):
        piece = r.gbup2[:, i * quarter : (i + 1) * quarter]
        small[ROW_DEC_BUP + i : ROW_DEC_BUP + i + 1, :quarter] = piece

    pl.semaphore_wait(barrier, len(every))

    copies = {}
    first_slot = (0, 1, 4, 7, 10)

    def chunk_copy(c, slot, src, dst, peer):
        copy = remote(src, dst, r.send_sem.at[c, slot], r.recv_sem.at[c, slot], peer)
        copy.start()
        copies[c, slot] = copy

    sent = set()

    def sent_by(c, slot):
        if (c, slot) not in sent:
            sent.add((c, slot))
            copies[c, slot].wait_send()

    staged = {}

    def staging(c):
        k = chunks[c]
        buffers = r.stage[k.rows, k.width]
        turn = staged.setdefault((k.rows, k.width), [])
        if len(turn) >= len(buffers):
            sent_by(turn[-len(buffers)], 0)
        turn.append(c)
        return buffers[(len(turn) - 1) % len(buffers)]

    def shard(i):
        return (i // 4, (i // 2) % 2, i % 2)

    waited = set()

    def arrived(copy):
        if id(copy) not in waited:
            waited.add(id(copy))
            copy.wait()

    def product(g, side):
        k, columns = chunks[groups[g][0]], wide_columns(g, side)
        if k.decoder:
            return mm(lhs.slots[lhs_names.index(k.name)][...], rhs.take()[...])
        if k.name == EMBED:
            arrived(load_y)
            arrived(load_geb)
            return mm_tn(r.y_v[...], r.geb_v[:, columns])
        if k.name == ENC_DOWN:
            arrived(load_ut)
            arrived(load_gy)
            at = [i * 192 + k.first_row for i in range(16)]
            left = jnp.concatenate([r.ut_v[i : i + k.rows, :] for i in at], axis=0)
            return mm(left, r.gy_v[:, columns])
        if k.name == ENC_UP:
            arrived(load_ct)
            return mm(r.ct_v[...], r.slope_v[:, columns])
        if k.name == ENC_OUT:
            arrived(load_ot)
            return mm(r.ot_v[...], r.ga_v[:, columns])
        arrived(load_at)
        return mm(r.at_v[...], r.qkv_v[:, columns])

    def after_product(i, g):
        k = chunks[groups[g][0]]
        if k.decoder:
            rhs.done()
            if last_use[k.name] == i:
                lhs.done()

    def wait_lhs(k):
        if k.name in lhs_names:
            arrived(lhs.copies[lhs_names.index(k.name)])

    def give(i, g):
        members = groups[g]
        wait_lhs(chunks[members[0]])
        buffers = [staging(c) for c in members]
        value = product(g, 1 - s).astype(BF16)
        for m, (c, buffer) in enumerate(zip(members, buffers)):
            k = chunks[c]
            part = value[:, m * k.width : (m + 1) * k.width]
            for j in range(16):
                buffer[shard(j)] = part[j * k.rows : (j + 1) * k.rows]
            chunk_copy(c, 0, buffer, r.acc[c], sibling)
        after_product(i, g)
        begin_some()

    def pair(i, g):
        both = groups[g]
        wait_lhs(chunks[both[0]])
        left = lhs.slots[lhs_names.index(DEC_DOWN)]
        side_rows = chunks[both[0]].half
        buffers = [staging(c) for c in both]
        for t in range(4):
            tile = rhs.take()
            for side, targets in ((1 - s, buffers), (s, [r.acc[c] for c in both])):
                at = pl.ds(pl.multiple_of(side * side_rows, side_rows), side_rows)
                value = mm(left[at, :], tile[...]).astype(BF16)
                for c, target in zip(both, targets):
                    k = chunks[c]
                    rows = slice(k.offset, k.offset + k.rows)
                    for j in range(4):
                        target[shard(4 * t + j)] = value[rows, j * k.width : (j + 1) * k.width]
            rhs.done()
        lhs.done()
        for c, buffer in zip(both, buffers):
            chunk_copy(c, 0, buffer, r.got[c], sibling)

    def spots(k, stage):
        fixed = {axis: here[axis] for axis in k.order[: stage - 1]}
        return [fixed.get(axis, slice(None)) for axis in (Z, Y, X)]

    def send_stage(c, stage):
        k = chunks[c]
        axis = k.order[stage - 1]
        for j, (coordinate, peer) in enumerate(peers[axis]):
            at = spots(k, stage)
            at[axis] = coordinate
            src = r.acc[c].at[tuple(at)]
            chunk_copy(c, first_slot[stage] + j, src, r.recv[stage - 1][c].at[j], peer)

    def got_stage(c, stage):
        k = chunks[c]
        count = len(peers[k.order[stage - 1]])
        for j in range(count):
            copies[c, first_slot[stage] + j].wait_recv()
        return count

    def add_stage(c, stage):
        k, acc, got = chunks[c], r.acc[c], r.recv[stage - 1][c]
        count = got_stage(c, stage)
        left = [axis for axis in (Z, Y, X) if axis not in k.order[:stage]]
        sizes = [(4, 2, 2)[axis] for axis in left]
        for j in range(math.prod(sizes)):
            place, rest = {}, j
            for axis, size in reversed(list(zip(left, sizes))):
                place[axis] = rest % size
                rest //= size
            at = tuple(place.get(axis, here[axis]) for axis in (Z, Y, X))
            index = tuple(place[axis] for axis in left)
            if count == 1:
                acc[at] = acc[at] + got[(0,) + index]
            else:
                total = acc[at].astype(F32)
                for m in range(count):
                    total = total + got[(m,) + index].astype(F32)
                acc[at] = total.astype(BF16)

    def stage1(i, g):
        members = groups[g]
        for c in members:
            copies[c, 0].wait_recv()
        if chunks[members[0]].turned:
            for c in members:
                acc = r.acc[c]
                for j in range(16):
                    acc[shard(j)] = acc[shard(j)] + r.got[c][shard(j)]
                send_stage(c, 1)
            return
        value = product(g, s)
        for m, c in enumerate(members):
            k, acc = chunks[c], r.acc[c]
            wide = value[:, m * k.width : (m + 1) * k.width]
            for j in range(16):
                part = wide[j * k.rows : (j + 1) * k.rows]
                acc[shard(j)] = (part + acc[shard(j)].astype(F32)).astype(BF16)
            send_stage(c, 1)
        after_product(i, g)

    def stage2(i, c):
        add_stage(c, 1)
        send_stage(c, 2)

    def stage3(i, c):
        add_stage(c, 2)
        send_stage(c, 3)

    def stage4(i, c):
        k = chunks[c]
        total = r.acc[c][here].astype(F32)
        for j in range(got_stage(c, 3)):
            total = total + r.recv[2][c][j].astype(F32)
        out = r.out[k.name]
        out[k.place(s)] = total.astype(BF16)
        final = out.at[k.place(s)]
        chunk_copy(c, 10, final, final, sibling)

    def stage5(i, c):
        copies[c, 10].wait_recv()

    small_copies = []

    def small_copy(source, peer):
        slot = len(small_copies)
        copy = remote(
            source, r.small_got.at[slot], r.small_sem.at[0, slot], r.small_sem.at[1, slot], peer
        )
        copy.start()
        small_copies.append(copy)

    def small_stage(stage):
        if stage < 4:
            small_copies[stage - 1].wait()
            total = small[...] + r.small_got[stage - 1]
            if stage < 3:
                small[...] = total
                small_copy(small, peers[X if stage == 1 else Y][0][1])
            else:
                r.small_sum[...] = total
                for _, peer in peers[Z]:
                    small_copy(r.small_sum, peer)
        else:
            total = r.small_sum[...]
            for j in range(3):
                small_copies[3 + j].wait()
                total = total + r.small_got[3 + j]
            r.out_small[...] = total

    def ffn(i, t):
        if t == 0:
            arrived(load_gy)
            load_slope.wait()
        at = slice(t * d_enc, (t + 1) * d_enc)
        gu = mm_nt(r.gy_v[...], weights.take()[...])
        weights.done()
        gf = (gu * r.slope_v[:, at].astype(F32)).astype(BF16)
        r.slope_v[:, at] = gf
        small[ROW_BUP + t : ROW_BUP + t + 1, :] = rows_sum(gf.astype(F32))
        gc = mm_nt(gf, weights.take()[...])
        weights.done()
        r.sum_v[...] = gc if t == 0 else r.sum_v[...] + gc

    def ln2(i, _):
        load_n2.wait()
        load_s2.wait()
        g, gc, n2 = r.gy_v[...].astype(F32), r.sum_v[...], r.n2_v[...]
        gh = g + normalise_back(gc, n2, r.s2_v[...], row(r.gain2))
        small[2:3, :] = rows_sum(gh)
        small[3:4, :] = rows_sum(gc * n2)
        small[4:5, :] = rows_sum(gc)
        small[5:6, :] = rows_sum(g)
        r.n2_v[...] = gh
        r.ga_v[...] = gh.astype(BF16)

    def go(i, _):
        r.go_v[...] = mm_nt(r.ga_v[...], weights.take()[...]).astype(BF16)
        weights.done()

    def att(i, g):
        if g == 0:
            for copy in (load_qkv, load_o, load_rl):
                copy.wait()
        at = slice(g * 128, (g + 1) * 128)
        parts = [slice(j * d_enc + g * 128, j * d_enc + (g + 1) * 128) for j in range(3)]
        q, k, v = (r.qkv_v[:, part] for part in parts)
        grads = attention_backward_group(
            q, k, v, e_ring.take()[...], r.go_v[:, at], r.o_v[:, at], r.rl_v[:, at],
            d_enc // H_ENC,
        )
        e_ring.done()
        for part, grad in zip(parts, grads):
            r.qkv_v[:, part] = grad

    def gn(i, j):
        part = mm_nt(r.qkv_v[:, j * d_enc : (j + 1) * d_enc], weights.take()[...])
        weights.done()
        r.sum_v[...] = part if j == 0 else r.sum_v[...] + part

    def last(i, _):
        load_x.wait()
        n1, s1 = normalise(r.x_v[...].astype(F32))
        total = r.sum_v[...]
        small[0:1, :] = rows_sum(total * n1)
        small[1:2, :] = rows_sum(total)
        small_copy(small, sibling)
        gx = r.n2_v[...] + normalise_back(total, n1, s1, row(r.gain1))
        r.gx[...] = gx.astype(BF16)
        gx_away.start()
        decoded_away.start()

    run = {
        GIVE: give, PAIR: pair, FFN: ffn, LN2: ln2, GO: go, ATT: att, GN: gn, LAST: last,
        1: stage1, 2: stage2, 3: stage3, 4: stage4, 5: stage5,
    }
    for i, (name, arg) in enumerate(plan):
        if arg == SMALL:
            small_stage(name)
        else:
            run[name](i, arg)

    for c, slot in copies:
        sent_by(c, slot)
    gx_away.wait()
    decoded_away.wait()


def finish_buffers(chunks, rows, d, ff, dec_total, dec):
    def of(dtype, *dims):
        return (dims, dtype)

    return dict(
        y_v=of(BF16, rows, d),
        geb_v=of(BF16, rows, dec),
        gy_v=of(BF16, rows, d),
        slope_v=of(BF16, rows, ff),
        n2_v=of(F32, rows, d),
        s2_v=of(F32, rows, 1),
        qkv_v=of(BF16, rows, 3 * d),
        o_v=of(BF16, rows, d),
        rl_v=of(F32, rows, d),
        x_v=of(BF16, rows, d),
        ga_v=of(BF16, rows, d),
        go_v=of(BF16, rows, d),
        sum_v=of(F32, rows, d),
        ut_v=of(BF16, ff, rows),
        ct_v=of(BF16, d, rows),
        at_v=of(BF16, d, rows),
        ot_v=of(BF16, d, rows),
        e_v=of(BF16, 2, rows, 2 * rows),
        w=of(BF16, 4, d, d),
        lhs=of(BF16, 2, dec, dec_total),
        rhs=of(BF16, 2, dec_total, 768),
        small=of(F32, SMALL_ROWS, d),
        small_sum=of(F32, SMALL_ROWS, d),
        small_got=of(F32, 6, SMALL_ROWS, d),
    )


def finish(acts):
    enc, dec = acts["enc"], acts["dec"]
    gain1, _, w_qkv, w_out, _, gain2, _, w_up, _, w_down, _ = enc["params"]
    qkv, e, rl, o, n2, s2, slope = acts["saved"]
    given = dict(
        x=acts["x"], y=acts["y"], gy=acts["gy"], geb=acts["geb"], qkv=qkv, e=e, rl=rl, o=o, n2=n2,
        s2=s2, slope=slope, at=enc["at"], ot=enc["ot"], ct=enc["ct"], ut=enc["ut"], at2=dec["at"], ot2=dec["ot"],
        ct2=dec["ct"], gt2=dec["gt"], u2=dec["u"], gf2=dec["gf"], ga2=dec["ga"],
        gqkv2=dec["gqkv"], w_qkv=w_qkv, w_out=w_out, w_up=w_up, w_down=w_down,
        decoded=acts["decoded"].reshape(SAMP_MB, PATCHES, -1),
    )
    n_hbm = len(given)
    given.update(small2=acts["small2"], gbup2=acts["gbup2"], gain1=gain1, gain2=gain2)
    rows, d = acts["gy"].shape
    ff = w_up.shape[1]
    dec_d, dec_total = dec["at"].shape
    dec_ff = dec["u"].shape[1]
    chunks = make_chunks()
    n = len(chunks)
    groups = make_groups(chunks)
    plan = make_plan(chunks, groups)

    dims = {
        ENC_QKV: (d, 3 * d), ENC_OUT: (d, d), ENC_UP: (d, ff), ENC_DOWN: (ff, d),
        EMBED: (d, dec_d), DEC_QKV: (dec_d, 3 * dec_d), DEC_OUT: (dec_d, dec_d),
        DEC_UP: (dec_d, dec_ff), DEC_DOWN: (dec_ff, dec_d),
    }
    big = [
        shape(dims[k][1], dims[k][0] // 16) if k == DEC_DOWN else shape(dims[k][0] // 16, dims[k][1])
        for k in range(9)
    ]
    outs = dict(
        out_small=shape(SMALL_ROWS, d, F32),
        decoded_got=jax.ShapeDtypeStruct((SAMP_MB, PATCHES // 2, dec_d), BF16),
        gx=shape(rows, d),
        gx_got=shape(rows, d // 2),
    )
    single = finish_buffers(chunks, rows, d, ff, dec_total, dec_d)
    left = (4, 2, 2)
    lists = [[], [], [], [], []]
    for k in chunks:
        block = (k.rows, k.width)
        lists[0].append((left + block, BF16))
        if k.turned:
            lists[1].append((left + block, BF16))
        for stage in range(3):
            rest = [left[axis] for axis in (Z, Y, X) if axis not in k.order[: stage + 1]]
            count = 3 if k.order[stage] == Z else 1
            lists[2 + stage].append(((count, *rest, *block), BF16))
    blocks = sorted({(k.rows, k.width) for k in chunks})
    slots = [2 if block == (48, 384) else 1 for block in blocks]
    lists.append([(left + block, BF16) for block, m in zip(blocks, slots) for _ in range(m)])
    semaphores = dict(
        load_sem=(LOADS,), send_sem=(n, 11), recv_sem=(n, 11), small_sem=(2, 6), swap_sem=(4,)
    )

    def kernel(*refs):
        refs = list(refs)

        def take(count):
            taken = refs[:count]
            del refs[:count]
            return taken

        names = list(given) + list(outs)
        r = Names(names, take(len(names)))
        r.out = take(9)
        r.__dict__.update(zip(single, take(len(single))))
        r.acc = take(n)
        r.got = dict(zip([c for c, k in enumerate(chunks) if k.turned], take(len(lists[1]))))
        r.recv = [take(n) for _ in range(3)]
        r.stage = {block: take(m) for block, m in zip(blocks, slots)}
        r.__dict__.update(zip(semaphores, take(len(semaphores))))
        finish_kernel(chunks, groups, plan, r)

    flat = list(single.values()) + [b for group in lists for b in group]
    results = pl.pallas_call(
        kernel,
        out_shape=list(outs.values()) + big,
        in_specs=[in_hbm()] * n_hbm + in_vmem(len(given) - n_hbm),
        out_specs=in_vmem(len(outs) + 9),
        scratch_shapes=[pltpu.VMEM(*b) for b in flat]
        + [pltpu.SemaphoreType.DMA(v) for v in semaphores.values()],
        compiler_params=pltpu.CompilerParams(
            collective_id=1, has_side_effects=True, vmem_limit_bytes=FINISH_VMEM
        ),
        name="finish",
    )(*given.values())
    return write_outputs(results, given["decoded"], dims)


FINISH_VMEM = 62 * 2**20


def write_kernel(small, decoded_got, gx_own, gx_got, *refs):
    big, decoded_own = refs[:9], refs[9]
    decoded, gx, *totals = refs[10:]
    s = lax.axis_index("section")
    half = decoded.shape[1]
    samples, rows, columns = decoded_own.shape[0], gx_own.shape[0], gx.shape[1]
    own = decoded_own[:, pl.ds(pl.multiple_of(s * half, half), half), :]
    for side, part in ((s, own), (1 - s, decoded_got[...])):
        decoded[pl.ds(side * samples, samples)] = part
    own = gx_own[:, pl.ds(pl.multiple_of(s * columns, 128), columns)]
    for side, part in ((s, own), (1 - s, gx_got[...])):
        gx[pl.ds(pl.multiple_of(side * rows, rows), rows), :] = part
    d = lax.axis_index("dp")
    wide, narrow = small.shape[1], big[DEC_OUT].shape[1]

    def piece(out, line, lanes, position):
        size = out.shape[0]
        value = small[pl.ds(line, 1), :lanes]
        value = pltpu.roll(value, lax.rem(lanes - position * size, lanes), 1)
        out[...] = value[:, :size].reshape(size)

    def matrix(out, name):
        value = big[name][...].astype(F32)
        out[...] = jnp.transpose(value) if name == DEC_DOWN else value

    def block(outs, first_row, bup_row, lanes, names):
        for i, out in zip((0, 1, None, None, 2, 3, 4, None, None, None, 5), outs):
            if i is not None:
                piece(out, first_row + i, lanes, d)
        piece(outs[8], bup_row + d // 4, lanes, d % 4)
        for at, name in zip((2, 3, 7, 9), names):
            matrix(outs[at], name)

    block(totals[:11], 0, ROW_BUP, wide, (ENC_QKV, ENC_OUT, ENC_UP, ENC_DOWN))
    matrix(totals[11], EMBED)
    piece(totals[12], ROW_DEC + 7, narrow, d)
    piece(totals[13], ROW_DEC + 6, narrow, d)
    block(totals[14:], ROW_DEC, ROW_DEC_BUP, narrow, (DEC_QKV, DEC_OUT, DEC_UP, DEC_DOWN))


def write_outputs(results, decoded_own, dims):
    def vector(size):
        return jax.ShapeDtypeStruct((size // 16,), F32)

    def matrix(name):
        return shape(dims[name][0] // 16, dims[name][1], F32)

    def block(qkv, out, up, down):
        d, ff = dims[up]
        return [
            vector(d), vector(d), matrix(qkv), matrix(out), vector(d), vector(d), vector(d),
            matrix(up), vector(ff), matrix(down), vector(d),
        ]

    samples, half, width = results[1].shape
    rows, columns = results[3].shape
    out_shape = [
        jax.ShapeDtypeStruct((2 * samples, half, width), BF16),
        shape(2 * rows, columns),
        *block(ENC_QKV, ENC_OUT, ENC_UP, ENC_DOWN),
        matrix(EMBED),
        vector(width),
        vector(width),
        *block(DEC_QKV, DEC_OUT, DEC_UP, DEC_DOWN),
    ]
    return tuple(
        pl.pallas_call(
            write_kernel,
            out_shape=out_shape,
            in_specs=in_vmem(len(results) + 1),
            out_specs=in_vmem(len(out_shape)),
            compiler_params=pltpu.CompilerParams(vmem_limit_bytes=KERNEL_VMEM),
            name="write_outputs",
        )(*results, decoded_own)
    )


def reduce_plain(arrays, section_index):
    first = section_index == 0
    results = []
    for a in arrays:
        half = a.shape[1] // 2
        keep = lax.dynamic_slice_in_dim(a, section_index * half, half, 1)
        give = lax.dynamic_slice_in_dim(a, (1 - section_index) * half, half, 1)
        got = swapped(give, "section", 0)
        chip = (keep.astype(jnp.float32) + got.astype(jnp.float32)).astype(jnp.bfloat16)
        mine = lax.psum_scatter(chip, "dp", scatter_dimension=0, tiled=True)
        other = swapped(mine, "section", 0)
        whole = jnp.concatenate(
            [jnp.where(first, mine, other), jnp.where(first, other, mine)], axis=1
        )
        results.append(whole.astype(jnp.float32))
    return results


def finish_plain(acts, section_index):
    x, gy, seg_saved, enc, dec = acts["x"], acts["gy"], acts["saved"], acts["enc"], acts["dec"]
    gx, gf1, ga1, gqkv1, small1, gbup1 = encoder_backward(x, gy, seg_saved, enc["params"])
    small2, gbup2 = acts["small2"], acts["gbup2"]
    grads = (
        small1[0], small1[1], mm(enc["at"], gqkv1).astype(BF16), mm(enc["ot"], ga1).astype(BF16), small1[2],
        small1[3], small1[4], mm(enc["ct"], gf1).astype(BF16), gbup1[0], mm(enc["ut"], gy).astype(BF16),
        small1[5],
        weight_grad(acts["y"], acts["geb"]), small2[7], small2[6],
        small2[0], small2[1], mm(dec["at"], dec["gqkv"]).astype(BF16),
        mm(dec["ot"], dec["ga"]).astype(BF16), small2[2], small2[3], small2[4],
        mm(dec["ct"], dec["gf"]).astype(BF16), gbup2[0],
        jnp.transpose(mm(dec["gt"], dec["u"])).astype(BF16), small2[5],
    )
    groups = lax.axis_size("dp")
    big = reduce_plain([g for g in grads if g.ndim == 2], section_index)
    flat = jnp.concatenate([g.reshape(groups, -1) for g in grads if g.ndim == 1], axis=1)
    line = lax.psum_scatter(flat, ("dp"), scatter_dimension=0, tiled=True)
    line = lax.psum(line, "section")[0]
    totals, at = [], 0
    for g in grads:
        if g.ndim == 2:
            totals.append(big.pop(0))
        else:
            size = g.shape[0] // groups
            totals.append(line[at : at + size])
            at += size
    decoded = acts["decoded"].reshape(SAMP_MB, PATCHES, -1)
    first = section_index == 0

    def halves(whole):
        half = whole.shape[1] // 2
        keep = lax.dynamic_slice_in_dim(whole, section_index * half, half, 1)
        give = lax.dynamic_slice_in_dim(whole, (1 - section_index) * half, half, 1)
        got = swapped(give, "section", 0)
        return jnp.concatenate([jnp.where(first, keep, got), jnp.where(first, got, keep)])

    return (halves(decoded), halves(gx), *totals)


def shards(
    patches,
    segment_ids,
    patch_order,
    encoder_gain1,
    encoder_bias1,
    encoder_qkv,
    encoder_out,
    encoder_out_bias,
    encoder_gain2,
    encoder_bias2,
    encoder_up,
    encoder_up_bias,
    encoder_down,
    encoder_down_bias,
    embed_weight,
    embed_bias,
    mask_token,
    decoder_gain1,
    decoder_bias1,
    decoder_qkv,
    decoder_out,
    decoder_out_bias,
    decoder_gain2,
    decoder_bias2,
    decoder_up,
    decoder_up_bias,
    decoder_down,
    decoder_down_bias,
    cotangent,
):
    enc_params = (
        encoder_gain1,
        encoder_bias1,
        encoder_qkv,
        encoder_out,
        encoder_out_bias,
        encoder_gain2,
        encoder_bias2,
        encoder_up,
        encoder_up_bias,
        encoder_down,
        encoder_down_bias,
    )
    embed_params = (embed_weight, embed_bias, mask_token)
    dec_params = (
        decoder_gain1,
        decoder_bias1,
        decoder_qkv,
        decoder_out,
        decoder_out_bias,
        decoder_gain2,
        decoder_bias2,
        decoder_up,
        decoder_up_bias,
        decoder_down,
        decoder_down_bias,
    )
    section_index = lax.axis_index("section")
    y, at1, qkv, e, rl, o1, ot1, n2, s2, ct1, ut1, slope = encoder_forward(
        patches, segment_ids, enc_params
    )
    g = cotangent.reshape(-1, DECODER_WIDTH)
    decoded, at2, ot2, ct2, gt2, u2, gf2, ga2, gqkv2, geb, gy, small2, gbup2 = decoder_both(
        y, segment_ids, patch_order, g, embed_params, dec_params
    )
    acts = dict(
        x=patches,
        y=y,
        gy=gy,
        geb=geb,
        decoded=decoded,
        small2=small2,
        gbup2=gbup2,
        saved=(qkv, e, rl, o1, n2, s2, slope),
        enc=dict(at=at1, ot=ot1, ct=ct1, ut=ut1, params=enc_params),
        dec=dict(at=at2, ot=ot2, ct=ct2, gt=gt2, u=u2, gf=gf2, ga=ga2, gqkv=gqkv2),
    )
    if lax.axis_size("dp") == 16:
        return finish(acts)
    return finish_plain(acts, section_index)


def solution(mesh):
    in_specs = (
        P("dp", None),
        P("dp", None),
        P("dp", None),
        P(),
        P(),
        P(),
        P(),
        P(),
        P(),
        P(),
        P(),
        P(),
        P(),
        P(),
        P(),
        P(),
        P(),
        P(),
        P(),
        P(),
        P(),
        P(),
        P(),
        P(),
        P(),
        P(),
        P(),
        P(),
        P("dp", None, None),
    )
    out_specs = (
        P("dp", "section", None),
        P("dp", "section"),
        P("dp"),
        P("dp"),
        P("dp", None),
        P("dp", None),
        P("dp"),
        P("dp"),
        P("dp"),
        P("dp", None),
        P("dp"),
        P("dp", None),
        P("dp"),
        P("dp", None),
        P("dp"),
        P("dp"),
        P("dp"),
        P("dp"),
        P("dp", None),
        P("dp", None),
        P("dp"),
        P("dp"),
        P("dp"),
        P("dp", None),
        P("dp"),
        P("dp", None),
        P("dp"),
    )
    return jax.shard_map(shards, mesh=mesh, in_specs=in_specs, out_specs=out_specs, check_vma=False)
```

```python
import functools
import math

import jax
import jax.numpy as jnp
import numpy as np
from jax import lax
from jax.experimental import pallas as pl
from jax.experimental.pallas import tpu as pltpu
from jax.sharding import PartitionSpec as P

H_ENC = 12
DECODER_WIDTH = 512
H_DEC = 16
PATCHES = 128
SAMP_MB = 12


EPSILON = 1e-06
MASKED = -1e30


def swapped(block, axis, apart):
    count = lax.axis_size(axis)
    route = []
    for low in range(count):
        high = low | 1 << apart
        if high != low and high < count:
            route += [(low, high), (high, low)]
    return lax.ppermute(block, axis, route)


def positions(count, features):
    column = np.arange(features)
    rate = np.exp(-math.log(10000.0) * (2 * (column // 2)) / features)
    angles = np.arange(count)[:, None] * rate[None, :]
    return np.where(column % 2 == 0, np.sin(angles), np.cos(angles)).astype(np.float32)


def weight_grad(left_side, grads):
    return lax.dot_general(
        left_side, grads, (((0,), (0,)), ((), ())), preferred_element_type=jnp.float32
    ).astype(jnp.bfloat16)


BF16 = jnp.bfloat16
F32 = jnp.float32


def mm(left, right):
    return lax.dot_general(left, right, (((1,), (0,)), ((), ())), preferred_element_type=F32)


def mm_nt(left, right):
    return lax.dot_general(left, right, (((1,), (1,)), ((), ())), preferred_element_type=F32)


def mm_tn(left, right):
    return lax.dot_general(left, right, (((0,), (0,)), ((), ())), preferred_element_type=F32)


def normalise(x):
    center = x - jnp.mean(x, axis=-1, keepdims=True)
    scale = lax.rsqrt(jnp.mean(center * center, axis=-1, keepdims=True) + EPSILON)
    return center * scale, scale


def normalise_back(grad, n, scale, gain):
    gn = grad * gain
    mean_gn = jnp.mean(gn, axis=-1, keepdims=True)
    mean_gnn = jnp.mean(gn * n, axis=-1, keepdims=True)
    return (gn - mean_gn - n * mean_gnn) * scale


def rows_sum(x):
    return jnp.sum(x, axis=0, keepdims=True)


def gelu_both(f):
    c0, c1 = math.sqrt(2.0 / math.pi), 0.044715
    square = f * f
    half = 0.5 + 0.5 * jnp.tanh(f * (c0 + (c0 * c1) * square))
    u = f * half
    return u, half + u * (1.0 - half) * (2.0 * c0 + (6.0 * c0 * c1) * square)


def lane_masks(head_size):
    lane = lax.broadcasted_iota(jnp.int32, (1, 128), 1)
    return [
        jnp.where((lane >= h * head_size) & (lane < (h + 1) * head_size), 1.0, 0.0).astype(BF16)
        for h in range(128 // head_size)
    ]


def stacked(x, masks):
    return jnp.concatenate([x * m for m in masks], axis=0)


def stacked_ones(x, masks, value):
    return jnp.concatenate(
        [jnp.broadcast_to(m * jnp.asarray(value, BF16), x.shape) for m in masks], axis=0
    )


def attention_forward(qkv_ref, o_ref, e_ref, rl_ref, rows, tokens, features, head_size, allowed):
    masks = lane_masks(head_size)
    per_group = len(masks)
    factor = head_size ** (-0.5) * math.log2(math.e)
    for g in range(features // 128):
        q, k, v = (qkv_ref[rows, j * features + g * 128 : j * features + (g + 1) * 128] for j in range(3))
        scores = mm_nt(q, stacked(k, masks))
        parts = []
        for h in range(per_group):
            part = scores[:, h * tokens : (h + 1) * tokens]
            if allowed is not None:
                part = jnp.where(allowed, part, MASKED)
            top = jnp.max(part, axis=-1, keepdims=True)
            parts.append(jnp.exp2((part - top) * factor).astype(BF16))
        e = jnp.concatenate(parts, axis=1)
        width = per_group * tokens
        e_ref[rows, g * width : (g + 1) * width] = e
        both = mm(e, jnp.concatenate([stacked(v, masks), stacked_ones(v, masks, 1.0)], axis=1))
        rl = 1.0 / both[:, 128:]
        rl_ref[rows, g * 128 : (g + 1) * 128] = rl
        o_ref[rows, g * 128 : (g + 1) * 128] = (both[:, :128] * rl).astype(BF16)


def attention_backward_group(q, k, v, e, go, o, rl, head_size):
    masks = lane_masks(head_size)
    per_group, tokens = len(masks), q.shape[0]
    scaling = head_size ** (-0.5)
    go = go.astype(F32) * rl
    go_low = go.astype(BF16)
    inner = (go * o.astype(F32)).astype(BF16)
    left = jnp.concatenate([go_low, inner], axis=1)
    right = jnp.concatenate([stacked(v, masks), stacked_ones(v, masks, -1.0)], axis=1)
    gs = (e.astype(F32) * mm_nt(left, right)).astype(BF16)

    def diagonal(wide):
        return jnp.concatenate(
            [
                wide[h * head_size : (h + 1) * head_size, h * tokens : (h + 1) * tokens]
                for h in range(per_group)
            ],
            axis=0,
        )

    gq = mm(gs, stacked(k, masks)) * scaling
    gk = jnp.transpose(diagonal(mm_tn(q, gs)) * scaling)
    gv = jnp.transpose(diagonal(mm_tn(go_low, e)))
    return gq.astype(BF16), gk.astype(BF16), gv.astype(BF16)


def attention_backward(
    qkv_ref, go_ref, o_ref, e_ref, rl_ref, gqkv_ref, rows, tokens, features, head_size
):
    width = 128 // head_size * tokens
    for g in range(features // 128):
        at = slice(g * 128, (g + 1) * 128)
        spots = [slice(j * features + g * 128, j * features + (g + 1) * 128) for j in range(3)]
        q, k, v = (qkv_ref[rows, spot] for spot in spots)
        e = e_ref[rows, g * width : (g + 1) * width]
        grads = attention_backward_group(
            q, k, v, e, go_ref[rows, at], o_ref[rows, at], rl_ref[rows, at], head_size
        )
        for spot, grad in zip(spots, grads):
            gqkv_ref[rows, spot] = grad


def feed_forward(c_ref, up_ref, bup_ref, u_ref, slope_ref, tile, ut_ref=None):
    for t in range(up_ref.shape[1] // tile):
        at = slice(t * tile, (t + 1) * tile)
        f = mm(c_ref[...], up_ref[:, at]) + bup_ref[at].reshape(1, tile)
        u, slope = gelu_both(f)
        u = u.astype(BF16)
        u_ref[:, at] = u
        slope_ref[:, at] = slope.astype(BF16)
        if ut_ref is not None:
            ut_ref[at, :] = jnp.transpose(u)


def feed_forward_back(gm_ref, down_ref, slope_ref, gf_ref, gbup_ref, tile):
    for t in range(down_ref.shape[0] // tile):
        at = slice(t * tile, (t + 1) * tile)
        gu = mm_nt(gm_ref[...], down_ref[at, :])
        gf = (gu * slope_ref[:, at].astype(F32)).astype(BF16)
        gf_ref[:, at] = gf
        gbup_ref[:, at] += rows_sum(gf.astype(F32))


def row(ref):
    return ref[...].reshape(1, -1)


def segment_mask(seg_ref, section):
    seg = seg_ref[pl.ds(section, 1), :].astype(F32)
    rows = seg.shape[1]
    column = jnp.transpose(jnp.broadcast_to(seg, (128, rows)))
    return jnp.concatenate([column] * (rows // 128), axis=1) == seg


class Writer:
    def __init__(self, semaphores):
        self.semaphores, self.copies = semaphores, []

    def start(self, source, target):
        copy = pltpu.make_async_copy(source, target, self.semaphores.at[len(self.copies)])
        copy.start()
        self.copies.append(copy)

    def wait(self):
        for copy in self.copies:
            copy.wait()


def encoder_forward_kernel(
    x_ref, seg_ref,
    gain1, bias1, w_qkv, w_out, b_out, gain2, bias2, w_up, b_up, w_down, b_down,
    *refs,
):
    outs, scratch = refs[:12], refs[12:24]
    y_ref, at_ref, qkv_ref, e_ref, rl_ref, o_ref, ot_ref, n2_ref, s2_ref, ct_ref, ut_ref, slope_ref = scratch
    h_ref, c_ref, u_ref, qkv_v, out_v, up_v, down_v, sem, out_sem = refs[24:]
    target = {id(v): o for v, o in zip(scratch, outs)}
    writer = Writer(out_sem)

    def write(*done):
        for v in done:
            writer.start(v, target[id(v)])

    tokens, features = y_ref.shape
    pairs = ((w_qkv, qkv_v), (w_out, out_v), (w_up, up_v), (w_down, down_v))
    loads = [pltpu.make_async_copy(w, v, sem.at[i]) for i, (w, v) in enumerate(pairs)]
    for load in loads:
        load.start()
    section = lax.axis_index("section")
    x = x_ref[pl.ds(pl.multiple_of(section * tokens, tokens), tokens), :].astype(F32)
    n1, _ = normalise(x)
    a = (n1 * row(gain1) + row(bias1)).astype(BF16)
    at_ref[...] = jnp.transpose(a)
    allowed = segment_mask(seg_ref, section)
    loads[0].wait()
    qkv_ref[...] = mm(a, qkv_v[...]).astype(BF16)
    write(at_ref, qkv_ref)
    attention_forward(
        qkv_ref, o_ref, e_ref, rl_ref, slice(None), tokens, features, features // H_ENC, allowed
    )
    ot_ref[...] = jnp.transpose(o_ref[...])
    write(e_ref, rl_ref, o_ref, ot_ref)
    loads[1].wait()
    h_ref[...] = x + (mm(o_ref[...], out_v[...]) + row(b_out))
    n2, s2 = normalise(h_ref[...])
    n2_ref[...] = n2
    s2_ref[...] = s2
    c_ref[...] = (n2 * row(gain2) + row(bias2)).astype(BF16)
    ct_ref[...] = jnp.transpose(c_ref[...])
    write(n2_ref, s2_ref, ct_ref)
    loads[2].wait()
    feed_forward(c_ref, up_v, b_up, u_ref, slope_ref, 512, ut_ref)
    write(ut_ref, slope_ref)
    loads[3].wait()
    y_ref[...] = (h_ref[...] + (mm(u_ref[...], down_v[...]) + row(b_down))).astype(BF16)
    write(y_ref)
    writer.wait()


def encoder_backward_kernel(
    x_ref, gy_ref, qkv_ref, e_ref, rl_ref, o_ref, n2_ref, s2_ref, slope_ref,
    gain1, w_qkv, w_out, gain2, w_up, w_down,
    gx_ref, gf_ref, ga_ref, gqkv_ref, small_ref, gbup_ref,
    gh_ref, go_ref,
):
    tokens, features = gy_ref.shape
    section = lax.axis_index("section")
    x = x_ref[pl.ds(pl.multiple_of(section * tokens, tokens), tokens), :].astype(F32)
    gbup_ref[...] = jnp.zeros_like(gbup_ref)
    feed_forward_back(gy_ref, w_down, slope_ref, gf_ref, gbup_ref, 512)
    gc = mm_nt(gf_ref[...], w_up[...])
    g = gy_ref[...].astype(F32)
    n2 = n2_ref[...]
    gh = g + normalise_back(gc, n2, s2_ref[...], row(gain2))
    gh_ref[...] = gh
    ga_ref[...] = gh.astype(BF16)
    small_ref[2:3, :] = rows_sum(gh)
    small_ref[3:4, :] = rows_sum(gc * n2)
    small_ref[4:5, :] = rows_sum(gc)
    small_ref[5:6, :] = rows_sum(g)
    go_ref[...] = mm_nt(ga_ref[...], w_out[...]).astype(BF16)
    attention_backward(
        qkv_ref, go_ref, o_ref, e_ref, rl_ref, gqkv_ref, slice(None), tokens, features,
        features // H_ENC,
    )
    gn = mm_nt(gqkv_ref[...], w_qkv[...])
    n1, s1 = normalise(x)
    small_ref[0:1, :] = rows_sum(gn * n1)
    small_ref[1:2, :] = rows_sum(gn)
    gx_ref[...] = (gh_ref[...] + normalise_back(gn, n1, s1, row(gain1))).astype(BF16)


def split_low(x):
    high = x.astype(BF16)
    return high, (x - high.astype(F32)).astype(BF16)


def place_slots(order_ref, seg, section, hot_ref, place_ref, empty_ref):
    packed = seg.shape[1]
    sample = lax.broadcasted_iota(jnp.int32, (16, packed), 0).astype(F32)
    starts = jnp.sum(jnp.where(seg < sample, 1.0, 0.0), axis=1, keepdims=True)
    counts = jnp.sum(jnp.where(seg == sample, 1.0, 0.0), axis=1, keepdims=True)
    line = lax.broadcasted_iota(jnp.int32, (PATCHES, PATCHES), 0).astype(F32)
    line_low = line.astype(BF16)
    lane_low = lax.broadcasted_iota(jnp.int32, (8, PATCHES), 1).astype(F32).astype(BF16)
    column = lax.broadcasted_iota(jnp.int32, (PATCHES, packed), 1).astype(F32)
    packed_line = lax.broadcasted_iota(jnp.int32, (packed, PATCHES), 0).astype(F32)
    for j in range(SAMP_MB):
        at = slice(j * PATCHES, (j + 1) * PATCHES)
        order = order_ref[pl.ds(section * SAMP_MB + j, 1), :].astype(F32)
        hit = jnp.where(order == line, 1.0, 0.0).astype(BF16)
        start, count = starts[j : j + 1, :], counts[j : j + 1, :]
        down, across = mm(hit, line_low), mm_nt(lane_low, hit)[:1, :]
        down = jnp.where(down < count, start + down, -1.0)
        across = jnp.where(across < count, start + across, -1.0)
        wide = jnp.concatenate([down] * (packed // PATCHES), axis=1)
        hot_ref[at, :] = jnp.where(column == wide, 1.0, 0.0).astype(BF16)
        place_ref[:, at] = jnp.where(packed_line == across, 1.0, 0.0).astype(BF16)
        empty_ref[at, :] = jnp.where(down < 0.0, 1.0, 0.0)


def decoder_kernel(
    y_ref, seg_ref, order_ref, pos_ref, g_hbm,
    w_embed_hbm, b_embed, mask_token,
    gain1, bias1, w_qkv_hbm, w_out_hbm, b_out, gain2, bias2, w_up_hbm, b_up, w_down_hbm, b_down,
    *refs,
):
    hbm, (geb_ref, gy_ref, small_ref, gbup_ref) = refs[:9], refs[9:13]
    buffers = refs[13:22]
    out_ref, at_ref, ot_ref, ct_ref, gt_ref, u_ref, gf_ref, ga_ref, gqkv_ref = buffers
    (
        e2_ref, z_ref, s1_ref, e_ref, rl_ref, h_ref, s2_ref, go_ref, ge_ref, o_ref, c_ref, qkv_ref,
        slope_ref, g_all, hot_ref, place_ref, empty_ref, w_embed, w_qkv, w_out, w_up, w_down,
        w_sem, out_sem,
    ) = refs[22:]
    packed = y_ref.shape[0]
    rows, features = z_ref.shape
    samples = rows // PATCHES
    head_size = features // H_DEC
    total = g_all.shape[0]
    section = lax.axis_index("section")
    mine = pl.ds(pl.multiple_of(section * total, total), total)
    pairs = (
        (w_embed_hbm, w_embed), (w_qkv_hbm, w_qkv), (w_out_hbm, w_out), (w_up_hbm, w_up),
        (w_down_hbm, w_down), (g_hbm.at[mine, :], g_all),
    )
    loads = [pltpu.make_async_copy(a, b, w_sem.at[i]) for i, (a, b) in enumerate(pairs)]
    for load in loads:
        load.start()

    def write(at, *which):
        copies = []
        for i in which:
            target = hbm[i].at[:, at] if 1 <= i <= 4 else hbm[i].at[at, :]
            copies.append(pltpu.make_async_copy(buffers[i], target, out_sem.at[i]))
            copies[-1].start()
        return copies

    small_ref[...] = jnp.zeros_like(small_ref)
    gbup_ref[...] = jnp.zeros_like(gbup_ref)
    ge_ref[...] = jnp.zeros_like(ge_ref)
    seg = seg_ref[pl.ds(section, 1), :].astype(F32)
    place_slots(order_ref, seg, section, hot_ref, place_ref, empty_ref)
    loads[0].wait()
    high, low = split_low(mm(y_ref[...], w_embed[...]) + row(b_embed))
    e2_ref[:packed, :] = high
    e2_ref[packed:, :] = low
    for load in loads[1:]:
        load.wait()

    def one_step(step, carry):
        here = pl.ds(pl.multiple_of(step * rows, rows), rows)
        one_hot = hot_ref[here, :]
        empty = jnp.concatenate([empty_ref[here, :]] * (features // 128), axis=1)
        twice = jnp.concatenate([one_hot, one_hot], axis=1)
        z = mm(twice, e2_ref[...]) + empty * row(mask_token)
        z = z + jnp.concatenate([pos_ref[...]] * samples, axis=0)
        n1, s1 = normalise(z)
        z_ref[...] = z
        s1_ref[...] = s1
        a = (n1 * row(gain1) + row(bias1)).astype(BF16)
        at_ref[...] = jnp.transpose(a)
        writing = write(here, 1)
        qkv_ref[...] = mm(a, w_qkv[...]).astype(BF16)

        def forward(b, carry):
            at = pl.ds(pl.multiple_of(b * PATCHES, PATCHES), PATCHES)
            attention_forward(qkv_ref, o_ref, e_ref, rl_ref, at, PATCHES, features, head_size, None)
            return carry

        lax.fori_loop(0, samples, forward, 0, unroll=2)
        ot_ref[...] = jnp.transpose(o_ref[...])
        h_ref[...] = z_ref[...] + (mm(o_ref[...], w_out[...]) + row(b_out))
        n2, s2 = normalise(h_ref[...])
        s2_ref[...] = s2
        c_ref[...] = (n2 * row(gain2) + row(bias2)).astype(BF16)
        ct_ref[...] = jnp.transpose(c_ref[...])
        feed_forward(c_ref, w_up, b_up, u_ref, slope_ref, 512)
        writing += write(here, 2, 3, 5)
        out_ref[...] = (h_ref[...] + (mm(u_ref[...], w_down[...]) + row(b_down))).astype(BF16)

        g_ref = g_all.at[here, :]
        gt_ref[...] = jnp.transpose(g_ref[...])
        feed_forward_back(g_ref, w_down, slope_ref, gf_ref, gbup_ref, 512)
        writing += write(here, 0, 4, 6)
        gc = mm_nt(gf_ref[...], w_up[...])
        g = g_ref[...].astype(F32)
        h = h_ref[...]
        n2 = (h - jnp.mean(h, axis=-1, keepdims=True)) * s2_ref[...]
        gh = g + normalise_back(gc, n2, s2_ref[...], row(gain2))
        small_ref[2:3, :] += rows_sum(gh)
        small_ref[3:4, :] += rows_sum(gc * n2)
        small_ref[4:5, :] += rows_sum(gc)
        small_ref[5:6, :] += rows_sum(g)
        h_ref[...] = gh
        ga_ref[...] = gh.astype(BF16)
        go_ref[...] = mm_nt(ga_ref[...], w_out[...]).astype(BF16)
        writing += write(here, 7)

        def backward(b, carry):
            at = pl.ds(pl.multiple_of(b * PATCHES, PATCHES), PATCHES)
            attention_backward(
                qkv_ref, go_ref, o_ref, e_ref, rl_ref, gqkv_ref, at, PATCHES, features, head_size
            )
            return carry

        lax.fori_loop(0, samples, backward, 0, unroll=2)
        writing += write(here, 8)
        gn = mm_nt(gqkv_ref[...], w_qkv[...])
        z = z_ref[...]
        n1 = (z - jnp.mean(z, axis=-1, keepdims=True)) * s1_ref[...]
        gz = h_ref[...] + normalise_back(gn, n1, s1_ref[...], row(gain1))
        small_ref[0:1, :] += rows_sum(gn * n1)
        small_ref[1:2, :] += rows_sum(gn)
        small_ref[6:7, :] += rows_sum(gz * empty)
        ge_ref[...] += mm(place_ref[:, here], gz.astype(BF16))
        for copy in writing:
            copy.wait()
        return carry

    lax.fori_loop(0, total // rows, one_step, 0)
    ge = ge_ref[...]
    small_ref[7:8, :] = rows_sum(ge)
    geb_ref[...] = ge.astype(BF16)
    gy_ref[...] = mm_nt(geb_ref[...], w_embed[...]).astype(BF16)


def in_vmem(count):
    return [pl.BlockSpec(memory_space=pltpu.VMEM)] * count


def in_hbm():
    return pl.BlockSpec(memory_space=pl.ANY)


def shape(rows, columns, dtype=BF16):
    return jax.ShapeDtypeStruct((rows, columns), dtype)


KERNEL_VMEM = 60 * 2**20


def encoder_forward(x, segments, params):
    rows, d = x.shape[0] // 2, x.shape[1]
    ff = params[7].shape[1]
    outs = [
        (rows, d, BF16),
        (d, rows, BF16),
        (rows, 3 * d, BF16),
        (rows, H_ENC * rows, BF16),
        (rows, d, F32),
        (rows, d, BF16),
        (d, rows, BF16),
        (rows, d, F32),
        (rows, 1, F32),
        (d, rows, BF16),
        (ff, rows, BF16),
        (rows, ff, BF16),
    ]
    more = [(rows, d, F32), (rows, d, BF16), (rows, ff, BF16)]
    args = [x, segments, *params]
    matrices = [w for w in params if w.dtype == BF16]
    return pl.pallas_call(
        encoder_forward_kernel,
        out_shape=[shape(*o) for o in outs],
        in_specs=in_vmem(2) + [in_hbm() if w.dtype == BF16 else in_vmem(1)[0] for w in params],
        out_specs=[in_hbm()] * len(outs),
        scratch_shapes=[pltpu.VMEM((r, w), t) for r, w, t in outs + more]
        + [pltpu.VMEM(w.shape, BF16) for w in matrices]
        + [pltpu.SemaphoreType.DMA((len(matrices),)), pltpu.SemaphoreType.DMA((len(outs),))],
        compiler_params=pltpu.CompilerParams(vmem_limit_bytes=KERNEL_VMEM),
        name="encoder_forward",
    )(*args)


def encoder_backward(x, gy, saved, params):
    gain1, _, w_qkv, w_out, _, gain2, _, w_up, _, w_down, _ = params
    rows, d = gy.shape
    ff = w_up.shape[1]
    outs = [
        shape(rows, d),
        shape(rows, ff),
        shape(rows, d),
        shape(rows, 3 * d),
        shape(8, d, F32),
        shape(1, ff, F32),
    ]
    args = [x, gy, *saved, gain1, w_qkv, w_out, gain2, w_up, w_down]
    return pl.pallas_call(
        encoder_backward_kernel,
        out_shape=outs,
        in_specs=in_vmem(len(args)),
        out_specs=in_vmem(len(outs)),
        scratch_shapes=[pltpu.VMEM((rows, d), F32), pltpu.VMEM((rows, d), BF16)],
        compiler_params=pltpu.CompilerParams(vmem_limit_bytes=KERNEL_VMEM),
        name="encoder_backward",
    )(*args)


def decoder_both(y, segments, orders, g, embed_params, params):
    packed, d_enc = y.shape
    total, d = g.shape[0] // 2, g.shape[1]
    rows = 6 * PATCHES
    ff = params[7].shape[1]
    args = [y, segments, orders, positions(PATCHES, d), g, *embed_params, *params]
    in_specs = in_vmem(4) + [in_hbm()]
    in_specs += [in_hbm() if x.dtype == BF16 else in_vmem(1)[0] for x in args[5:]]
    wide = [ff, ff, d, 3 * d]
    outs = [shape(total, d)] + [shape(d, total)] * 4 + [shape(total, w) for w in wide]
    buffers = [(rows, d, BF16)] + [(d, rows, BF16)] * 4 + [(rows, w, BF16) for w in wide]
    last = [shape(packed, d), shape(packed, d_enc), shape(8, d, F32), shape(1, ff, F32)]
    scratch = [
        (2 * packed, d, BF16),
        (rows, d, F32),
        (rows, 1, F32),
        (rows, H_DEC * PATCHES, BF16),
        (rows, d, F32),
        (rows, d, F32),
        (rows, 1, F32),
        (rows, d, BF16),
        (packed, d, F32),
        (rows, d, BF16),
        (rows, d, BF16),
        (rows, 3 * d, BF16),
        (rows, ff, BF16),
        (total, d, BF16),
        (total, packed, BF16),
        (packed, total, BF16),
        (total, 128, F32),
    ]
    matrices = [x for x in args[5:] if x.dtype == BF16]
    return pl.pallas_call(
        decoder_kernel,
        out_shape=outs + last,
        in_specs=in_specs,
        out_specs=[in_hbm()] * len(outs) + in_vmem(len(last)),
        scratch_shapes=[pltpu.VMEM((r, w), t) for r, w, t in buffers + scratch]
        + [pltpu.VMEM(x.shape, BF16) for x in matrices]
        + [pltpu.SemaphoreType.DMA((k,)) for k in (len(matrices) + 1, len(outs))],
        compiler_params=pltpu.CompilerParams(vmem_limit_bytes=KERNEL_VMEM),
        name="decoder_both",
    )(*args)


MESH = pl.DeviceIdType.MESH
ENC_QKV, ENC_OUT, ENC_UP, ENC_DOWN, EMBED, DEC_QKV, DEC_OUT, DEC_UP, DEC_DOWN = range(9)
GIVE, PAIR, FFN, LN2, GO, ATT, GN, LAST = range(10, 18)
SMALL = -1
ROW_BUP, ROW_DEC_BUP, ROW_DEC, SMALL_ROWS = 6, 10, 16, 24
Z, Y, X, CORE = range(4)
ORDERS = ((X, Y, Z), (Y, X, Z), (X, Z, Y), (Y, Z, X), (Z, X, Y), (Z, Y, X))


class Chunk:
    def __init__(self, name, half, offset, rows, width, first_row=None):
        self.name, self.half, self.offset, self.rows, self.width = name, half, offset, rows, width
        self.first_row, self.turned, self.order = first_row, name == DEC_DOWN, None
        self.decoder = name in (DEC_QKV, DEC_UP, DEC_OUT)

    def columns(self, side):
        return pl.ds(pl.multiple_of(side * self.half + self.offset, 128), self.width)

    def place(self, side):
        if self.turned:
            return (pl.ds(pl.multiple_of(side * self.half + self.offset, 128), self.rows), slice(None))
        if self.first_row is None:
            return (slice(None), self.columns(side))
        return (pl.ds(self.first_row, self.rows), self.columns(side))

    @property
    def bytes(self):
        return 32 * self.rows * self.width

    def loads(self, order):
        if order[0] == Z:
            return (2 * self.bytes, self.bytes / 4, self.bytes / 8)
        if order[1] == Z:
            return (self.bytes, self.bytes, self.bytes / 8)
        return (self.bytes, self.bytes / 2, self.bytes / 2)


LINK_ORDERS = (0, 1, 2, 4, 3, 0, 3, 0, 3, 3, 0, 0, 0, 0, 1)


def make_chunks():
    chunks = [Chunk(ENC_DOWN, 384, 0, 48, 384, 48 * q) for q in range(4)]
    chunks += [Chunk(ENC_UP, 1536, 768 * q, 48, 768) for q in range(2)]
    chunks += [Chunk(ENC_OUT, 384, 0, 48, 384)]
    chunks += [Chunk(ENC_QKV, 1152, 0, 48, 768), Chunk(ENC_QKV, 1152, 768, 48, 384)]
    chunks += [Chunk(EMBED, 256, 0, 48, 256)]
    chunks += [Chunk(DEC_QKV, 768, 0, 32, 768), Chunk(DEC_DOWN, 256, 0, 256, 128)]
    chunks += [Chunk(DEC_UP, 1024, o, 32, 512) for o in (0, 512)]
    chunks += [Chunk(DEC_OUT, 256, 0, 32, 256)]
    for chunk, order in zip(chunks, LINK_ORDERS):
        chunk.order = ORDERS[order]
    return chunks


def make_groups(chunks):
    return [[c] for c in range(len(chunks))]


def product_cost(k, count):
    if k.turned:
        return 5.0
    return k.rows * k.width * (0.9 / 8192 if k.decoder else 0.6 / 18432)


def tasks_in_order(chunks, groups):
    def gives(name):
        found = [(g, chunks[m[0]], len(m)) for g, m in enumerate(groups)]
        kind = PAIR if name == DEC_DOWN else GIVE
        return [(kind, g, product_cost(k, size)) for g, k, size in found if k.name == name]

    tasks = gives(ENC_DOWN)
    tasks += [(FFN, t, 1.7) for t in range(4)] + gives(ENC_UP)
    tasks += [(LN2, 0, 1.0), (GO, 0, 0.9)]
    tasks += [(ATT, g, 1.5) for g in range(6)]
    tasks += gives(ENC_OUT) + gives(ENC_QKV) + gives(EMBED)
    tasks += gives(DEC_QKV) + gives(DEC_DOWN)
    tasks += [(GN, j, 0.9) for j in range(3)] + [(LAST, 0, 1.5)]
    return tasks + gives(DEC_UP) + gives(DEC_OUT)


def decoder_arrays(chunks):
    names = []
    for k in chunks:
        if (k.decoder or k.turned) and k.name not in names:
            names.append(k.name)
    return names


def make_plan(chunks, groups):
    tasks = tasks_in_order(chunks, groups)
    lhs = decoder_arrays(chunks)
    free = [0.0] * 4
    rate = [80e3, 80e3, 80e3, 500e3]
    pending, plan, now, owned = [], [], 2.0, set()

    def send(link, size, latency):
        begin = max(now, free[link])
        free[link] = begin + size / rate[link]
        return free[link] + latency

    def blocked(task):
        if task[0] not in (GIVE, PAIR):
            return False
        name = chunks[groups[task[1]][0]].name
        if name not in lhs[2:]:
            return False
        name = lhs[lhs.index(name) - 2]
        return any(chunks[m[0]].name == name and g not in owned for g, m in enumerate(groups))

    while tasks or pending:
        pending.sort()
        if pending and (pending[0][0] <= now or not tasks or blocked(tasks[0])):
            arrive, stage, c = pending.pop(0)
            now = max(now, arrive)
            plan.append((stage, c))
            if c == SMALL:
                now += 0.1
                if stage < 4:
                    pending.append((now + 2.0, stage + 1, c))
                continue
            members = groups[c] if stage == 1 else [c]
            k = chunks[members[0]]
            if stage == 1:
                owned.add(c)
                now += 0.6 if k.turned else product_cost(k, len(members)) + 0.2 * len(members)
            else:
                now += 0.25
            for c in members:
                k = chunks[c]
                if stage < 4:
                    axis = k.order[stage - 1]
                    latency = 2.0 if axis == Z else 1.5
                    arrive = send(axis, k.loads(k.order)[stage - 1], latency)
                    pending.append((arrive, stage + 1, c))
                elif stage == 4:
                    pending.append((send(CORE, k.bytes / 16, 1.0), 5, c))
            continue
        name, arg, cost = tasks.pop(0)
        plan.append((name, arg))
        now += cost
        if name in (GIVE, PAIR):
            arrive = [send(CORE, chunks[c].bytes, 1.0) for c in groups[arg]]
            pending.append((max(arrive), 1, arg))
        elif name == LAST:
            pending.append((now + 2.0, 1, SMALL))
    return plan


class Ring:
    def __init__(self, sources, slots, semaphores, depth):
        self.copies = [
            pltpu.make_async_copy(source, slot, semaphores())
            for source, slot in zip(sources, slots)
        ]
        self.slots, self.depth, self.at = slots, depth, 0

    def begin(self):
        for copy in self.copies[: self.depth]:
            copy.start()

    def take(self):
        self.copies[self.at].wait()
        return self.slots[self.at]

    def done(self):
        ahead = self.at + self.depth
        if ahead < len(self.copies):
            self.copies[ahead].start()
        self.at += 1


class Names:
    def __init__(self, names, refs):
        self.__dict__.update(zip(names, refs))


LOADS = 96


def finish_kernel(chunks, groups, plan, r):
    n = len(chunks)
    s = lax.axis_index("section")
    d = lax.axis_index("dp")
    here = (d // 4, (d // 2) % 2, d % 2)
    z, y, x = here
    sibling = {"section": 1 - s}
    z_at = [lax.rem(z + k, 4) for k in (1, 2, 3)]
    peers = {
        X: [(1 - x, {"dp": d + 1 - 2 * x})],
        Y: [(1 - y, {"dp": d + 2 - 4 * y})],
        Z: [(p, {"dp": d + 4 * (p - z)}) for p in z_at],
    }
    every = [sibling] + [peer for axis in (X, Y, Z) for _, peer in peers[axis]]

    barrier = pltpu.get_barrier_semaphore()
    for peer in every:
        pl.semaphore_signal(barrier, inc=1, device_id=peer, device_id_type=MESH)

    counter = iter(range(LOADS))

    def semaphore():
        return r.load_sem.at[next(counter)]

    def remote(src, dst, send, recv, peer):
        return pltpu.make_async_remote_copy(
            src_ref=src, dst_ref=dst, send_sem=send, recv_sem=recv, device_id=peer, device_id_type=MESH
        )

    rhs_of = {DEC_QKV: r.gqkv2, DEC_UP: r.gf2, DEC_OUT: r.ga2}
    lhs_of = {DEC_QKV: r.at2, DEC_UP: r.ct2, DEC_OUT: r.ot2, DEC_DOWN: r.gt2}
    tiles, widths, last_use = [], [], {}

    def wide_columns(g, side):
        k, width = chunks[groups[g][0]], sum(chunks[c].width for c in groups[g])
        return pl.ds(pl.multiple_of(side * k.half + k.offset, 128), width)

    for i, (name, arg) in enumerate(plan):
        if name == PAIR:
            tiles += [r.u2.at[:, t * 512 : (t + 1) * 512] for t in range(4)]
            last_use[DEC_DOWN] = i
        elif name in (GIVE, 1) and arg != SMALL and chunks[groups[arg][0]].decoder:
            k = chunks[groups[arg][0]]
            tiles.append(rhs_of[k.name].at[:, wide_columns(arg, 1 - s if name == GIVE else s)])
            last_use[k.name] = i
    lhs_names = decoder_arrays(chunks)
    assert sorted(lhs_names, key=last_use.get) == lhs_names
    rhs_slots = [r.rhs.at[i % 2, :, : tile.shape[1]] for i, tile in enumerate(tiles)]
    rhs = Ring(tiles, rhs_slots, semaphore, 2)
    lhs = Ring([lhs_of[k] for k in lhs_names], [r.lhs.at[i % 2] for i in range(4)], semaphore, 2)
    tokens, d_enc = r.gy.shape
    blocks = []
    for t in range(4):
        at = pl.ds(t * d_enc, d_enc)
        blocks += [r.w_down.at[at, :], r.w_up.at[:, at]]
    blocks.append(r.w_out)
    blocks += [r.w_qkv.at[:, pl.ds(j * d_enc, d_enc)] for j in range(3)]
    weights = Ring(blocks, [r.w.at[i % 4] for i in range(12)], semaphore, 4)
    e_width = 2 * tokens
    e_ring = Ring(
        [r.e.at[:, pl.ds(g * e_width, e_width)] for g in range(6)],
        [r.e_v.at[g % 2] for g in range(6)],
        semaphore,
        2,
    )

    def load(source, target):
        return pltpu.make_async_copy(source, target, semaphore())

    mine = pl.ds(pl.multiple_of(s * tokens, tokens), tokens)
    load_gy, load_slope, load_ut = load(r.gy, r.gy_v), load(r.slope, r.slope_v), load(r.ut, r.ut_v)
    load_ct, load_at, load_ot = load(r.ct, r.ct_v), load(r.at, r.at_v), load(r.ot, r.ot_v)
    load_n2, load_s2, load_qkv = load(r.n2, r.n2_v), load(r.s2, r.s2_v), load(r.qkv, r.qkv_v)
    load_o, load_rl, load_x = load(r.o, r.o_v), load(r.rl, r.rl_v), load(r.x.at[mine, :], r.x_v)
    load_y, load_geb = load(r.y, r.y_v), load(r.geb, r.geb_v)
    load_gy.start()
    load_ut.start()
    load_slope.start()
    weights.begin()
    begun = [
        (load_ct, load_n2, load_s2),
        (load_qkv, load_o, load_rl, e_ring),
        (load_ot, load_at, load_y, load_geb),
        (load_x, lhs, rhs),
    ]

    def begin_some():
        for copy in begun.pop(0) if begun else ():
            copy.begin() if isinstance(copy, Ring) else copy.start()

    half = r.decoded.shape[1] // 2
    give_half = r.decoded.at[:, pl.ds(pl.multiple_of((1 - s) * half, half), half), :]
    decoded_away = [
        remote(
            give_half.at[4 * i : 4 * i + 4], r.decoded_got.at[4 * i : 4 * i + 4],
            r.swap_sem.at[2 + i], r.swap_sem.at[5 + i], sibling,
        )
        for i in range(3)
    ]
    gx_columns = d_enc // 2
    gx_half = r.gx.at[:, pl.ds(pl.multiple_of((1 - s) * gx_columns, 128), gx_columns)]
    gx_away = remote(gx_half, r.gx_got, r.swap_sem.at[0], r.swap_sem.at[1], sibling)

    small = r.small
    small[...] = jnp.zeros_like(small)
    small[ROW_DEC : ROW_DEC + 8, : r.small2.shape[1]] = r.small2[...]
    quarter = r.gbup2.shape[1] // 4
    for i in range(4):
        piece = r.gbup2[:, i * quarter : (i + 1) * quarter]
        small[ROW_DEC_BUP + i : ROW_DEC_BUP + i + 1, :quarter] = piece

    pl.semaphore_wait(barrier, len(every))

    copies = {}
    first_slot = (0, 1, 4, 7, 10)

    def chunk_copy(c, slot, src, dst, peer):
        copy = remote(src, dst, r.send_sem.at[c, slot], r.recv_sem.at[c, slot], peer)
        copy.start()
        copies[c, slot] = copy

    exchange = (0, 11, 12, 13)

    def swap_copy(c, src, dst):
        for i, slot in enumerate(exchange):
            chunk_copy(c, slot, src.at[i], dst.at[i], sibling)

    sent = set()

    def sent_by(c, slot):
        if (c, slot) not in sent:
            sent.add((c, slot))
            copies[c, slot].wait_send()

    staged = {}

    def staging(c):
        k = chunks[c]
        buffers = r.stage[k.rows, k.width]
        turn = staged.setdefault((k.rows, k.width), [])
        if len(turn) >= len(buffers):
            for slot in exchange:
                sent_by(turn[-len(buffers)], slot)
        turn.append(c)
        return buffers[(len(turn) - 1) % len(buffers)]

    def shard(i):
        return (i // 4, (i // 2) % 2, i % 2)

    waited = set()

    def arrived(copy):
        if id(copy) not in waited:
            waited.add(id(copy))
            copy.wait()

    def product(g, side):
        k, columns = chunks[groups[g][0]], wide_columns(g, side)
        if k.decoder:
            return mm(lhs.slots[lhs_names.index(k.name)][...], rhs.take()[...])
        if k.name == EMBED:
            arrived(load_y)
            arrived(load_geb)
            return mm_tn(r.y_v[...], r.geb_v[:, columns])
        if k.name == ENC_DOWN:
            arrived(load_ut)
            arrived(load_gy)
            at = [i * 192 + k.first_row for i in range(16)]
            left = jnp.concatenate([r.ut_v[i : i + k.rows, :] for i in at], axis=0)
            return mm(left, r.gy_v[:, columns])
        if k.name == ENC_UP:
            arrived(load_ct)
            return mm(r.ct_v[...], r.slope_v[:, columns])
        if k.name == ENC_OUT:
            arrived(load_ot)
            return mm(r.ot_v[...], r.ga_v[:, columns])
        arrived(load_at)
        return mm(r.at_v[...], r.qkv_v[:, columns])

    def after_product(i, g):
        k = chunks[groups[g][0]]
        if k.decoder:
            rhs.done()
            if last_use[k.name] == i:
                lhs.done()

    def wait_lhs(k):
        if k.name in lhs_names:
            arrived(lhs.copies[lhs_names.index(k.name)])

    def give(i, g):
        members = groups[g]
        wait_lhs(chunks[members[0]])
        buffers = [staging(c) for c in members]
        value = product(g, 1 - s).astype(BF16)
        for m, (c, buffer) in enumerate(zip(members, buffers)):
            k = chunks[c]
            part = value[:, m * k.width : (m + 1) * k.width]
            for j in range(16):
                buffer[shard(j)] = part[j * k.rows : (j + 1) * k.rows]
            swap_copy(c, buffer, r.acc[c])
        after_product(i, g)
        begin_some()

    def pair(i, g):
        both = groups[g]
        wait_lhs(chunks[both[0]])
        left = lhs.slots[lhs_names.index(DEC_DOWN)]
        side_rows = chunks[both[0]].half
        buffers = [staging(c) for c in both]
        for t in range(4):
            tile = rhs.take()
            for side, targets in ((1 - s, buffers), (s, [r.acc[c] for c in both])):
                at = pl.ds(pl.multiple_of(side * side_rows, side_rows), side_rows)
                value = mm(left[at, :], tile[...]).astype(BF16)
                for c, target in zip(both, targets):
                    k = chunks[c]
                    rows = slice(k.offset, k.offset + k.rows)
                    for j in range(4):
                        target[shard(4 * t + j)] = value[rows, j * k.width : (j + 1) * k.width]
            rhs.done()
        lhs.done()
        for c, buffer in zip(both, buffers):
            swap_copy(c, buffer, r.got[c])

    def spots(k, stage):
        fixed = {axis: here[axis] for axis in k.order[: stage - 1]}
        return [fixed.get(axis, slice(None)) for axis in (Z, Y, X)]

    def send_stage(c, stage):
        k = chunks[c]
        axis = k.order[stage - 1]
        for j, (coordinate, peer) in enumerate(peers[axis]):
            at = spots(k, stage)
            at[axis] = coordinate
            src = r.acc[c].at[tuple(at)]
            chunk_copy(c, first_slot[stage] + j, src, r.recv[stage - 1][c].at[j], peer)

    def got_stage(c, stage):
        k = chunks[c]
        count = len(peers[k.order[stage - 1]])
        for j in range(count):
            copies[c, first_slot[stage] + j].wait_recv()
        return count

    def add_stage(c, stage):
        k, acc, got = chunks[c], r.acc[c], r.recv[stage - 1][c]
        count = got_stage(c, stage)
        left = [axis for axis in (Z, Y, X) if axis not in k.order[:stage]]
        sizes = [(4, 2, 2)[axis] for axis in left]
        for j in range(math.prod(sizes)):
            place, rest = {}, j
            for axis, size in reversed(list(zip(left, sizes))):
                place[axis] = rest % size
                rest //= size
            at = tuple(place.get(axis, here[axis]) for axis in (Z, Y, X))
            index = tuple(place[axis] for axis in left)
            if count == 1:
                acc[at] = acc[at] + got[(0,) + index]
            else:
                total = acc[at].astype(F32)
                for m in range(count):
                    total = total + got[(m,) + index].astype(F32)
                acc[at] = total.astype(BF16)

    def stage1(i, g):
        members = groups[g]
        for c in members:
            for slot in exchange:
                copies[c, slot].wait_recv()
        if chunks[members[0]].turned:
            for c in members:
                acc = r.acc[c]
                for j in range(16):
                    acc[shard(j)] = acc[shard(j)] + r.got[c][shard(j)]
                send_stage(c, 1)
            return
        value = product(g, s)
        for m, c in enumerate(members):
            k, acc = chunks[c], r.acc[c]
            wide = value[:, m * k.width : (m + 1) * k.width]
            for j in range(16):
                part = wide[j * k.rows : (j + 1) * k.rows]
                acc[shard(j)] = (part + acc[shard(j)].astype(F32)).astype(BF16)
            send_stage(c, 1)
        after_product(i, g)

    def stage2(i, c):
        add_stage(c, 1)
        send_stage(c, 2)

    def stage3(i, c):
        add_stage(c, 2)
        send_stage(c, 3)

    def stage4(i, c):
        k = chunks[c]
        total = r.acc[c][here].astype(F32)
        for j in range(got_stage(c, 3)):
            total = total + r.recv[2][c][j].astype(F32)
        out = r.out[k.name]
        out[k.place(s)] = total.astype(BF16)
        final = out.at[k.place(s)]
        chunk_copy(c, 10, final, final, sibling)

    def stage5(i, c):
        copies[c, 10].wait_recv()

    small_copies = []

    def small_copy(source, peer):
        slot = len(small_copies)
        copy = remote(
            source, r.small_got.at[slot], r.small_sem.at[0, slot], r.small_sem.at[1, slot], peer
        )
        copy.start()
        small_copies.append(copy)

    def small_stage(stage):
        if stage < 4:
            small_copies[stage - 1].wait()
            total = small[...] + r.small_got[stage - 1]
            if stage < 3:
                small[...] = total
                small_copy(small, peers[X if stage == 1 else Y][0][1])
            else:
                r.small_sum[...] = total
                for _, peer in peers[Z]:
                    small_copy(r.small_sum, peer)
        else:
            total = r.small_sum[...]
            for j in range(3):
                small_copies[3 + j].wait()
                total = total + r.small_got[3 + j]
            r.out_small[...] = total

    def ffn(i, t):
        if t == 0:
            arrived(load_gy)
            load_slope.wait()
        at = slice(t * d_enc, (t + 1) * d_enc)
        gu = mm_nt(r.gy_v[...], weights.take()[...])
        weights.done()
        gf = (gu * r.slope_v[:, at].astype(F32)).astype(BF16)
        r.slope_v[:, at] = gf
        small[ROW_BUP + t : ROW_BUP + t + 1, :] = rows_sum(gf.astype(F32))
        gc = mm_nt(gf, weights.take()[...])
        weights.done()
        r.sum_v[...] = gc if t == 0 else r.sum_v[...] + gc

    def ln2(i, _):
        load_n2.wait()
        load_s2.wait()
        g, gc, n2 = r.gy_v[...].astype(F32), r.sum_v[...], r.n2_v[...]
        gh = g + normalise_back(gc, n2, r.s2_v[...], row(r.gain2))
        small[2:3, :] = rows_sum(gh)
        small[3:4, :] = rows_sum(gc * n2)
        small[4:5, :] = rows_sum(gc)
        small[5:6, :] = rows_sum(g)
        r.n2_v[...] = gh
        r.ga_v[...] = gh.astype(BF16)

    def go(i, _):
        r.go_v[...] = mm_nt(r.ga_v[...], weights.take()[...]).astype(BF16)
        weights.done()

    def att(i, g):
        if g == 0:
            for copy in (load_qkv, load_o, load_rl):
                copy.wait()
        at = slice(g * 128, (g + 1) * 128)
        parts = [slice(j * d_enc + g * 128, j * d_enc + (g + 1) * 128) for j in range(3)]
        q, k, v = (r.qkv_v[:, part] for part in parts)
        grads = attention_backward_group(
            q, k, v, e_ring.take()[...], r.go_v[:, at], r.o_v[:, at], r.rl_v[:, at],
            d_enc // H_ENC,
        )
        e_ring.done()
        for part, grad in zip(parts, grads):
            r.qkv_v[:, part] = grad

    def gn(i, j):
        part = mm_nt(r.qkv_v[:, j * d_enc : (j + 1) * d_enc], weights.take()[...])
        weights.done()
        r.sum_v[...] = part if j == 0 else r.sum_v[...] + part

    def last(i, _):
        load_x.wait()
        n1, s1 = normalise(r.x_v[...].astype(F32))
        total = r.sum_v[...]
        small[0:1, :] = rows_sum(total * n1)
        small[1:2, :] = rows_sum(total)
        small_copy(small, sibling)
        gx = r.n2_v[...] + normalise_back(total, n1, s1, row(r.gain1))
        r.gx[...] = gx.astype(BF16)
        gx_away.start()
        for copy in decoded_away:
            copy.start()

    run = {
        GIVE: give, PAIR: pair, FFN: ffn, LN2: ln2, GO: go, ATT: att, GN: gn, LAST: last,
        1: stage1, 2: stage2, 3: stage3, 4: stage4, 5: stage5,
    }
    for i, (name, arg) in enumerate(plan):
        if arg == SMALL:
            small_stage(name)
        else:
            run[name](i, arg)

    for c, slot in copies:
        sent_by(c, slot)
    gx_away.wait()
    for copy in decoded_away:
        copy.wait()


def finish_buffers(chunks, rows, d, ff, dec_total, dec):
    def of(dtype, *dims):
        return (dims, dtype)

    return dict(
        y_v=of(BF16, rows, d),
        geb_v=of(BF16, rows, dec),
        gy_v=of(BF16, rows, d),
        slope_v=of(BF16, rows, ff),
        n2_v=of(F32, rows, d),
        s2_v=of(F32, rows, 1),
        qkv_v=of(BF16, rows, 3 * d),
        o_v=of(BF16, rows, d),
        rl_v=of(F32, rows, d),
        x_v=of(BF16, rows, d),
        ga_v=of(BF16, rows, d),
        go_v=of(BF16, rows, d),
        sum_v=of(F32, rows, d),
        ut_v=of(BF16, ff, rows),
        ct_v=of(BF16, d, rows),
        at_v=of(BF16, d, rows),
        ot_v=of(BF16, d, rows),
        e_v=of(BF16, 2, rows, 2 * rows),
        w=of(BF16, 4, d, d),
        lhs=of(BF16, 2, dec, dec_total),
        rhs=of(BF16, 2, dec_total, 768),
        small=of(F32, SMALL_ROWS, d),
        small_sum=of(F32, SMALL_ROWS, d),
        small_got=of(F32, 6, SMALL_ROWS, d),
    )


def finish(acts):
    enc, dec = acts["enc"], acts["dec"]
    gain1, _, w_qkv, w_out, _, gain2, _, w_up, _, w_down, _ = enc["params"]
    qkv, e, rl, o, n2, s2, slope = acts["saved"]
    given = dict(
        x=acts["x"], y=acts["y"], gy=acts["gy"], geb=acts["geb"], qkv=qkv, e=e, rl=rl, o=o, n2=n2,
        s2=s2, slope=slope, at=enc["at"], ot=enc["ot"], ct=enc["ct"], ut=enc["ut"], at2=dec["at"], ot2=dec["ot"],
        ct2=dec["ct"], gt2=dec["gt"], u2=dec["u"], gf2=dec["gf"], ga2=dec["ga"],
        gqkv2=dec["gqkv"], w_qkv=w_qkv, w_out=w_out, w_up=w_up, w_down=w_down,
        decoded=acts["decoded"].reshape(SAMP_MB, PATCHES, -1),
    )
    n_hbm = len(given)
    given.update(small2=acts["small2"], gbup2=acts["gbup2"], gain1=gain1, gain2=gain2)
    rows, d = acts["gy"].shape
    ff = w_up.shape[1]
    dec_d, dec_total = dec["at"].shape
    dec_ff = dec["u"].shape[1]
    chunks = make_chunks()
    n = len(chunks)
    groups = make_groups(chunks)
    plan = make_plan(chunks, groups)

    dims = {
        ENC_QKV: (d, 3 * d), ENC_OUT: (d, d), ENC_UP: (d, ff), ENC_DOWN: (ff, d),
        EMBED: (d, dec_d), DEC_QKV: (dec_d, 3 * dec_d), DEC_OUT: (dec_d, dec_d),
        DEC_UP: (dec_d, dec_ff), DEC_DOWN: (dec_ff, dec_d),
    }
    big = [
        shape(dims[k][1], dims[k][0] // 16) if k == DEC_DOWN else shape(dims[k][0] // 16, dims[k][1])
        for k in range(9)
    ]
    outs = dict(
        out_small=shape(SMALL_ROWS, d, F32),
        decoded_got=jax.ShapeDtypeStruct((SAMP_MB, PATCHES // 2, dec_d), BF16),
        gx=shape(rows, d),
        gx_got=shape(rows, d // 2),
    )
    single = finish_buffers(chunks, rows, d, ff, dec_total, dec_d)
    left = (4, 2, 2)
    lists = [[], [], [], [], []]
    for k in chunks:
        block = (k.rows, k.width)
        lists[0].append((left + block, BF16))
        if k.turned:
            lists[1].append((left + block, BF16))
        for stage in range(3):
            rest = [left[axis] for axis in (Z, Y, X) if axis not in k.order[: stage + 1]]
            count = 3 if k.order[stage] == Z else 1
            lists[2 + stage].append(((count, *rest, *block), BF16))
    blocks = sorted({(k.rows, k.width) for k in chunks})
    slots = [2 if block == (48, 384) else 1 for block in blocks]
    lists.append([(left + block, BF16) for block, m in zip(blocks, slots) for _ in range(m)])
    semaphores = dict(
        load_sem=(LOADS,), send_sem=(n, 14), recv_sem=(n, 14), small_sem=(2, 6), swap_sem=(8,)
    )

    def kernel(*refs):
        refs = list(refs)

        def take(count):
            taken = refs[:count]
            del refs[:count]
            return taken

        names = list(given) + list(outs)
        r = Names(names, take(len(names)))
        r.out = take(9)
        r.__dict__.update(zip(single, take(len(single))))
        r.acc = take(n)
        r.got = dict(zip([c for c, k in enumerate(chunks) if k.turned], take(len(lists[1]))))
        r.recv = [take(n) for _ in range(3)]
        r.stage = {block: take(m) for block, m in zip(blocks, slots)}
        r.__dict__.update(zip(semaphores, take(len(semaphores))))
        finish_kernel(chunks, groups, plan, r)

    flat = list(single.values()) + [b for group in lists for b in group]
    results = pl.pallas_call(
        kernel,
        out_shape=list(outs.values()) + big,
        in_specs=[in_hbm()] * n_hbm + in_vmem(len(given) - n_hbm),
        out_specs=in_vmem(len(outs) + 9),
        scratch_shapes=[pltpu.VMEM(*b) for b in flat]
        + [pltpu.SemaphoreType.DMA(v) for v in semaphores.values()],
        compiler_params=pltpu.CompilerParams(
            collective_id=1, has_side_effects=True, vmem_limit_bytes=FINISH_VMEM
        ),
        name="finish",
    )(*given.values())
    return write_outputs(results, given["decoded"], dims)


FINISH_VMEM = 62 * 2**20


def write_kernel(small, decoded_got, gx_own, gx_got, *refs):
    big, decoded_own = refs[:9], refs[9]
    decoded, gx, *totals = refs[10:]
    s = lax.axis_index("section")
    half = decoded.shape[1]
    samples, rows, columns = decoded_own.shape[0], gx_own.shape[0], gx.shape[1]
    own = decoded_own[:, pl.ds(pl.multiple_of(s * half, half), half), :]
    for side, part in ((s, own), (1 - s, decoded_got[...])):
        decoded[pl.ds(side * samples, samples)] = part
    own = gx_own[:, pl.ds(pl.multiple_of(s * columns, 128), columns)]
    for side, part in ((s, own), (1 - s, gx_got[...])):
        gx[pl.ds(pl.multiple_of(side * rows, rows), rows), :] = part
    d = lax.axis_index("dp")
    wide, narrow = small.shape[1], big[DEC_OUT].shape[1]

    def piece(out, line, lanes, position):
        size = out.shape[0]
        value = small[pl.ds(line, 1), :lanes]
        value = pltpu.roll(value, lax.rem(lanes - position * size, lanes), 1)
        out[...] = value[:, :size].reshape(size)

    def matrix(out, name):
        value = big[name][...].astype(F32)
        out[...] = jnp.transpose(value) if name == DEC_DOWN else value

    def block(outs, first_row, bup_row, lanes, names):
        for i, out in zip((0, 1, None, None, 2, 3, 4, None, None, None, 5), outs):
            if i is not None:
                piece(out, first_row + i, lanes, d)
        piece(outs[8], bup_row + d // 4, lanes, d % 4)
        for at, name in zip((2, 3, 7, 9), names):
            matrix(outs[at], name)

    block(totals[:11], 0, ROW_BUP, wide, (ENC_QKV, ENC_OUT, ENC_UP, ENC_DOWN))
    matrix(totals[11], EMBED)
    piece(totals[12], ROW_DEC + 7, narrow, d)
    piece(totals[13], ROW_DEC + 6, narrow, d)
    block(totals[14:], ROW_DEC, ROW_DEC_BUP, narrow, (DEC_QKV, DEC_OUT, DEC_UP, DEC_DOWN))


def write_outputs(results, decoded_own, dims):
    def vector(size):
        return jax.ShapeDtypeStruct((size // 16,), F32)

    def matrix(name):
        return shape(dims[name][0] // 16, dims[name][1], F32)

    def block(qkv, out, up, down):
        d, ff = dims[up]
        return [
            vector(d), vector(d), matrix(qkv), matrix(out), vector(d), vector(d), vector(d),
            matrix(up), vector(ff), matrix(down), vector(d),
        ]

    samples, half, width = results[1].shape
    rows, columns = results[3].shape
    out_shape = [
        jax.ShapeDtypeStruct((2 * samples, half, width), BF16),
        shape(2 * rows, columns),
        *block(ENC_QKV, ENC_OUT, ENC_UP, ENC_DOWN),
        matrix(EMBED),
        vector(width),
        vector(width),
        *block(DEC_QKV, DEC_OUT, DEC_UP, DEC_DOWN),
    ]
    return tuple(
        pl.pallas_call(
            write_kernel,
            out_shape=out_shape,
            in_specs=in_vmem(len(results) + 1),
            out_specs=in_vmem(len(out_shape)),
            compiler_params=pltpu.CompilerParams(vmem_limit_bytes=KERNEL_VMEM),
            name="write_outputs",
        )(*results, decoded_own)
    )


def reduce_plain(arrays, section_index):
    first = section_index == 0
    results = []
    for a in arrays:
        half = a.shape[1] // 2
        keep = lax.dynamic_slice_in_dim(a, section_index * half, half, 1)
        give = lax.dynamic_slice_in_dim(a, (1 - section_index) * half, half, 1)
        got = swapped(give, "section", 0)
        chip = (keep.astype(jnp.float32) + got.astype(jnp.float32)).astype(jnp.bfloat16)
        mine = lax.psum_scatter(chip, "dp", scatter_dimension=0, tiled=True)
        other = swapped(mine, "section", 0)
        whole = jnp.concatenate(
            [jnp.where(first, mine, other), jnp.where(first, other, mine)], axis=1
        )
        results.append(whole.astype(jnp.float32))
    return results


def finish_plain(acts, section_index):
    x, gy, seg_saved, enc, dec = acts["x"], acts["gy"], acts["saved"], acts["enc"], acts["dec"]
    gx, gf1, ga1, gqkv1, small1, gbup1 = encoder_backward(x, gy, seg_saved, enc["params"])
    small2, gbup2 = acts["small2"], acts["gbup2"]
    grads = (
        small1[0], small1[1], mm(enc["at"], gqkv1).astype(BF16), mm(enc["ot"], ga1).astype(BF16), small1[2],
        small1[3], small1[4], mm(enc["ct"], gf1).astype(BF16), gbup1[0], mm(enc["ut"], gy).astype(BF16),
        small1[5],
        weight_grad(acts["y"], acts["geb"]), small2[7], small2[6],
        small2[0], small2[1], mm(dec["at"], dec["gqkv"]).astype(BF16),
        mm(dec["ot"], dec["ga"]).astype(BF16), small2[2], small2[3], small2[4],
        mm(dec["ct"], dec["gf"]).astype(BF16), gbup2[0],
        jnp.transpose(mm(dec["gt"], dec["u"])).astype(BF16), small2[5],
    )
    groups = lax.axis_size("dp")
    big = reduce_plain([g for g in grads if g.ndim == 2], section_index)
    flat = jnp.concatenate([g.reshape(groups, -1) for g in grads if g.ndim == 1], axis=1)
    line = lax.psum_scatter(flat, ("dp"), scatter_dimension=0, tiled=True)
    line = lax.psum(line, "section")[0]
    totals, at = [], 0
    for g in grads:
        if g.ndim == 2:
            totals.append(big.pop(0))
        else:
            size = g.shape[0] // groups
            totals.append(line[at : at + size])
            at += size
    decoded = acts["decoded"].reshape(SAMP_MB, PATCHES, -1)
    first = section_index == 0

    def halves(whole):
        half = whole.shape[1] // 2
        keep = lax.dynamic_slice_in_dim(whole, section_index * half, half, 1)
        give = lax.dynamic_slice_in_dim(whole, (1 - section_index) * half, half, 1)
        got = swapped(give, "section", 0)
        return jnp.concatenate([jnp.where(first, keep, got), jnp.where(first, got, keep)])

    return (halves(decoded), halves(gx), *totals)


def shards(
    patches,
    segment_ids,
    patch_order,
    encoder_gain1,
    encoder_bias1,
    encoder_qkv,
    encoder_out,
    encoder_out_bias,
    encoder_gain2,
    encoder_bias2,
    encoder_up,
    encoder_up_bias,
    encoder_down,
    encoder_down_bias,
    embed_weight,
    embed_bias,
    mask_token,
    decoder_gain1,
    decoder_bias1,
    decoder_qkv,
    decoder_out,
    decoder_out_bias,
    decoder_gain2,
    decoder_bias2,
    decoder_up,
    decoder_up_bias,
    decoder_down,
    decoder_down_bias,
    cotangent,
):
    enc_params = (
        encoder_gain1,
        encoder_bias1,
        encoder_qkv,
        encoder_out,
        encoder_out_bias,
        encoder_gain2,
        encoder_bias2,
        encoder_up,
        encoder_up_bias,
        encoder_down,
        encoder_down_bias,
    )
    embed_params = (embed_weight, embed_bias, mask_token)
    dec_params = (
        decoder_gain1,
        decoder_bias1,
        decoder_qkv,
        decoder_out,
        decoder_out_bias,
        decoder_gain2,
        decoder_bias2,
        decoder_up,
        decoder_up_bias,
        decoder_down,
        decoder_down_bias,
    )
    section_index = lax.axis_index("section")
    y, at1, qkv, e, rl, o1, ot1, n2, s2, ct1, ut1, slope = encoder_forward(
        patches, segment_ids, enc_params
    )
    g = cotangent.reshape(-1, DECODER_WIDTH)
    decoded, at2, ot2, ct2, gt2, u2, gf2, ga2, gqkv2, geb, gy, small2, gbup2 = decoder_both(
        y, segment_ids, patch_order, g, embed_params, dec_params
    )
    acts = dict(
        x=patches,
        y=y,
        gy=gy,
        geb=geb,
        decoded=decoded,
        small2=small2,
        gbup2=gbup2,
        saved=(qkv, e, rl, o1, n2, s2, slope),
        enc=dict(at=at1, ot=ot1, ct=ct1, ut=ut1, params=enc_params),
        dec=dict(at=at2, ot=ot2, ct=ct2, gt=gt2, u=u2, gf=gf2, ga=ga2, gqkv=gqkv2),
    )
    if lax.axis_size("dp") == 16:
        return finish(acts)
    return finish_plain(acts, section_index)


def solution(mesh):
    in_specs = (
        P("dp", None),
        P("dp", None),
        P("dp", None),
        P(),
        P(),
        P(),
        P(),
        P(),
        P(),
        P(),
        P(),
        P(),
        P(),
        P(),
        P(),
        P(),
        P(),
        P(),
        P(),
        P(),
        P(),
        P(),
        P(),
        P(),
        P(),
        P(),
        P(),
        P(),
        P("dp", None, None),
    )
    out_specs = (
        P("dp", "section", None),
        P("dp", "section"),
        P("dp"),
        P("dp"),
        P("dp", None),
        P("dp", None),
        P("dp"),
        P("dp"),
        P("dp"),
        P("dp", None),
        P("dp"),
        P("dp", None),
        P("dp"),
        P("dp", None),
        P("dp"),
        P("dp"),
        P("dp"),
        P("dp"),
        P("dp", None),
        P("dp", None),
        P("dp"),
        P("dp"),
        P("dp"),
        P("dp", None),
        P("dp"),
        P("dp", None),
        P("dp"),
    )
    return jax.shard_map(shards, mesh=mesh, in_specs=in_specs, out_specs=out_specs, check_vma=False)
```

```python
import functools
import math

import jax
import jax.numpy as jnp
import numpy as np
from jax import lax
from jax.experimental import pallas as pl
from jax.experimental.pallas import tpu as pltpu
from jax.sharding import PartitionSpec as P

H_ENC = 12
DECODER_WIDTH = 512
H_DEC = 16
PATCHES = 128
SAMP_MB = 12


EPSILON = 1e-06
MASKED = -1e30


def swapped(block, axis, apart):
    count = lax.axis_size(axis)
    route = []
    for low in range(count):
        high = low | 1 << apart
        if high != low and high < count:
            route += [(low, high), (high, low)]
    return lax.ppermute(block, axis, route)


def positions(count, features):
    column = np.arange(features)
    rate = np.exp(-math.log(10000.0) * (2 * (column // 2)) / features)
    angles = np.arange(count)[:, None] * rate[None, :]
    return np.where(column % 2 == 0, np.sin(angles), np.cos(angles)).astype(np.float32)


def weight_grad(left_side, grads):
    return lax.dot_general(
        left_side, grads, (((0,), (0,)), ((), ())), preferred_element_type=jnp.float32
    ).astype(jnp.bfloat16)


BF16 = jnp.bfloat16
F32 = jnp.float32


def mm(left, right):
    return lax.dot_general(left, right, (((1,), (0,)), ((), ())), preferred_element_type=F32)


def mm_nt(left, right):
    return lax.dot_general(left, right, (((1,), (1,)), ((), ())), preferred_element_type=F32)


def mm_tn(left, right):
    return lax.dot_general(left, right, (((0,), (0,)), ((), ())), preferred_element_type=F32)


def normalise(x):
    center = x - jnp.mean(x, axis=-1, keepdims=True)
    scale = lax.rsqrt(jnp.mean(center * center, axis=-1, keepdims=True) + EPSILON)
    return center * scale, scale


def normalise_back(grad, n, scale, gain):
    gn = grad * gain
    mean_gn = jnp.mean(gn, axis=-1, keepdims=True)
    mean_gnn = jnp.mean(gn * n, axis=-1, keepdims=True)
    return (gn - mean_gn - n * mean_gnn) * scale


def rows_sum(x):
    return jnp.sum(x, axis=0, keepdims=True)


def gelu_both(f):
    c0, c1 = math.sqrt(2.0 / math.pi), 0.044715
    square = f * f
    half = 0.5 + 0.5 * jnp.tanh(f * (c0 + (c0 * c1) * square))
    u = f * half
    return u, half + u * (1.0 - half) * (2.0 * c0 + (6.0 * c0 * c1) * square)


def lane_masks(head_size):
    lane = lax.broadcasted_iota(jnp.int32, (1, 128), 1)
    return [
        jnp.where((lane >= h * head_size) & (lane < (h + 1) * head_size), 1.0, 0.0).astype(BF16)
        for h in range(128 // head_size)
    ]


def stacked(x, masks):
    return jnp.concatenate([x * m for m in masks], axis=0)


def stacked_ones(x, masks, value):
    return jnp.concatenate(
        [jnp.broadcast_to(m * jnp.asarray(value, BF16), x.shape) for m in masks], axis=0
    )


def attention_forward(qkv_ref, o_ref, e_ref, rl_ref, rows, tokens, features, head_size, allowed):
    masks = lane_masks(head_size)
    per_group = len(masks)
    factor = head_size ** (-0.5) * math.log2(math.e)
    for g in range(features // 128):
        q, k, v = (qkv_ref[rows, j * features + g * 128 : j * features + (g + 1) * 128] for j in range(3))
        scores = mm_nt(q, stacked(k, masks))
        parts = []
        for h in range(per_group):
            part = scores[:, h * tokens : (h + 1) * tokens]
            if allowed is not None:
                part = jnp.where(allowed, part, MASKED)
            top = jnp.max(part, axis=-1, keepdims=True)
            parts.append(jnp.exp2((part - top) * factor).astype(BF16))
        e = jnp.concatenate(parts, axis=1)
        width = per_group * tokens
        e_ref[rows, g * width : (g + 1) * width] = e
        both = mm(e, jnp.concatenate([stacked(v, masks), stacked_ones(v, masks, 1.0)], axis=1))
        rl = 1.0 / both[:, 128:]
        rl_ref[rows, g * 128 : (g + 1) * 128] = rl
        o_ref[rows, g * 128 : (g + 1) * 128] = (both[:, :128] * rl).astype(BF16)


def attention_backward_group(q, k, v, e, go, o, rl, head_size):
    masks = lane_masks(head_size)
    per_group, tokens = len(masks), q.shape[0]
    scaling = head_size ** (-0.5)
    go = go.astype(F32) * rl
    go_low = go.astype(BF16)
    inner = (go * o.astype(F32)).astype(BF16)
    left = jnp.concatenate([go_low, inner], axis=1)
    right = jnp.concatenate([stacked(v, masks), stacked_ones(v, masks, -1.0)], axis=1)
    gs = (e.astype(F32) * mm_nt(left, right)).astype(BF16)

    def diagonal(wide):
        return jnp.concatenate(
            [
                wide[h * head_size : (h + 1) * head_size, h * tokens : (h + 1) * tokens]
                for h in range(per_group)
            ],
            axis=0,
        )

    gq = mm(gs, stacked(k, masks)) * scaling
    gk = jnp.transpose(diagonal(mm_tn(q, gs)) * scaling)
    gv = jnp.transpose(diagonal(mm_tn(go_low, e)))
    return gq.astype(BF16), gk.astype(BF16), gv.astype(BF16)


def attention_backward(
    qkv_ref, go_ref, o_ref, e_ref, rl_ref, gqkv_ref, rows, tokens, features, head_size
):
    width = 128 // head_size * tokens
    for g in range(features // 128):
        at = slice(g * 128, (g + 1) * 128)
        spots = [slice(j * features + g * 128, j * features + (g + 1) * 128) for j in range(3)]
        q, k, v = (qkv_ref[rows, spot] for spot in spots)
        e = e_ref[rows, g * width : (g + 1) * width]
        grads = attention_backward_group(
            q, k, v, e, go_ref[rows, at], o_ref[rows, at], rl_ref[rows, at], head_size
        )
        for spot, grad in zip(spots, grads):
            gqkv_ref[rows, spot] = grad


def feed_forward(c_ref, up_ref, bup_ref, u_ref, slope_ref, tile, ut_ref=None):
    for t in range(up_ref.shape[1] // tile):
        at = slice(t * tile, (t + 1) * tile)
        f = mm(c_ref[...], up_ref[:, at]) + bup_ref[at].reshape(1, tile)
        u, slope = gelu_both(f)
        u = u.astype(BF16)
        u_ref[:, at] = u
        slope_ref[:, at] = slope.astype(BF16)
        if ut_ref is not None:
            ut_ref[at, :] = jnp.transpose(u)


def feed_forward_back(gm_ref, down_ref, slope_ref, gf_ref, gbup_ref, tile):
    for t in range(down_ref.shape[0] // tile):
        at = slice(t * tile, (t + 1) * tile)
        gu = mm_nt(gm_ref[...], down_ref[at, :])
        gf = (gu * slope_ref[:, at].astype(F32)).astype(BF16)
        gf_ref[:, at] = gf
        gbup_ref[:, at] += rows_sum(gf.astype(F32))


def row(ref):
    return ref[...].reshape(1, -1)


def segment_mask(seg_ref, section):
    seg = seg_ref[pl.ds(section, 1), :].astype(F32)
    rows = seg.shape[1]
    column = jnp.transpose(jnp.broadcast_to(seg, (128, rows)))
    return jnp.concatenate([column] * (rows // 128), axis=1) == seg


class Writer:
    def __init__(self, semaphores):
        self.semaphores, self.copies = semaphores, []

    def start(self, source, target):
        copy = pltpu.make_async_copy(source, target, self.semaphores.at[len(self.copies)])
        copy.start()
        self.copies.append(copy)

    def wait(self):
        for copy in self.copies:
            copy.wait()


def encoder_forward_kernel(
    x_ref, seg_ref,
    gain1, bias1, w_qkv, w_out, b_out, gain2, bias2, w_up, b_up, w_down, b_down,
    *refs,
):
    outs, scratch = refs[:12], refs[12:24]
    y_ref, at_ref, qkv_ref, e_ref, rl_ref, o_ref, ot_ref, n2_ref, s2_ref, ct_ref, ut_ref, slope_ref = scratch
    h_ref, c_ref, u_ref, qkv_v, out_v, up_v, down_v, sem, out_sem = refs[24:]
    target = {id(v): o for v, o in zip(scratch, outs)}
    writer = Writer(out_sem)

    def write(*done):
        for v in done:
            writer.start(v, target[id(v)])

    tokens, features = y_ref.shape
    pairs = ((w_qkv, qkv_v), (w_out, out_v), (w_up, up_v), (w_down, down_v))
    loads = [pltpu.make_async_copy(w, v, sem.at[i]) for i, (w, v) in enumerate(pairs)]
    for load in loads:
        load.start()
    section = lax.axis_index("section")
    x = x_ref[pl.ds(pl.multiple_of(section * tokens, tokens), tokens), :].astype(F32)
    n1, _ = normalise(x)
    a = (n1 * row(gain1) + row(bias1)).astype(BF16)
    at_ref[...] = jnp.transpose(a)
    allowed = segment_mask(seg_ref, section)
    loads[0].wait()
    qkv_ref[...] = mm(a, qkv_v[...]).astype(BF16)
    write(at_ref, qkv_ref)
    attention_forward(
        qkv_ref, o_ref, e_ref, rl_ref, slice(None), tokens, features, features // H_ENC, allowed
    )
    ot_ref[...] = jnp.transpose(o_ref[...])
    write(e_ref, rl_ref, o_ref, ot_ref)
    loads[1].wait()
    h_ref[...] = x + (mm(o_ref[...], out_v[...]) + row(b_out))
    n2, s2 = normalise(h_ref[...])
    n2_ref[...] = n2
    s2_ref[...] = s2
    c_ref[...] = (n2 * row(gain2) + row(bias2)).astype(BF16)
    ct_ref[...] = jnp.transpose(c_ref[...])
    write(n2_ref, s2_ref, ct_ref)
    loads[2].wait()
    feed_forward(c_ref, up_v, b_up, u_ref, slope_ref, 512, ut_ref)
    write(ut_ref, slope_ref)
    loads[3].wait()
    y_ref[...] = (h_ref[...] + (mm(u_ref[...], down_v[...]) + row(b_down))).astype(BF16)
    write(y_ref)
    writer.wait()


def encoder_backward_kernel(
    x_ref, gy_ref, qkv_ref, e_ref, rl_ref, o_ref, n2_ref, s2_ref, slope_ref,
    gain1, w_qkv, w_out, gain2, w_up, w_down,
    gx_ref, gf_ref, ga_ref, gqkv_ref, small_ref, gbup_ref,
    gh_ref, go_ref,
):
    tokens, features = gy_ref.shape
    section = lax.axis_index("section")
    x = x_ref[pl.ds(pl.multiple_of(section * tokens, tokens), tokens), :].astype(F32)
    gbup_ref[...] = jnp.zeros_like(gbup_ref)
    feed_forward_back(gy_ref, w_down, slope_ref, gf_ref, gbup_ref, 512)
    gc = mm_nt(gf_ref[...], w_up[...])
    g = gy_ref[...].astype(F32)
    n2 = n2_ref[...]
    gh = g + normalise_back(gc, n2, s2_ref[...], row(gain2))
    gh_ref[...] = gh
    ga_ref[...] = gh.astype(BF16)
    small_ref[2:3, :] = rows_sum(gh)
    small_ref[3:4, :] = rows_sum(gc * n2)
    small_ref[4:5, :] = rows_sum(gc)
    small_ref[5:6, :] = rows_sum(g)
    go_ref[...] = mm_nt(ga_ref[...], w_out[...]).astype(BF16)
    attention_backward(
        qkv_ref, go_ref, o_ref, e_ref, rl_ref, gqkv_ref, slice(None), tokens, features,
        features // H_ENC,
    )
    gn = mm_nt(gqkv_ref[...], w_qkv[...])
    n1, s1 = normalise(x)
    small_ref[0:1, :] = rows_sum(gn * n1)
    small_ref[1:2, :] = rows_sum(gn)
    gx_ref[...] = (gh_ref[...] + normalise_back(gn, n1, s1, row(gain1))).astype(BF16)


def split_low(x):
    high = x.astype(BF16)
    return high, (x - high.astype(F32)).astype(BF16)


def place_slots(order_ref, seg, section, hot_ref, place_ref, empty_ref):
    packed = seg.shape[1]
    sample = lax.broadcasted_iota(jnp.int32, (16, packed), 0).astype(F32)
    starts = jnp.sum(jnp.where(seg < sample, 1.0, 0.0), axis=1, keepdims=True)
    counts = jnp.sum(jnp.where(seg == sample, 1.0, 0.0), axis=1, keepdims=True)
    line = lax.broadcasted_iota(jnp.int32, (PATCHES, PATCHES), 0).astype(F32)
    line_low = line.astype(BF16)
    lane_low = lax.broadcasted_iota(jnp.int32, (8, PATCHES), 1).astype(F32).astype(BF16)
    column = lax.broadcasted_iota(jnp.int32, (PATCHES, packed), 1).astype(F32)
    packed_line = lax.broadcasted_iota(jnp.int32, (packed, PATCHES), 0).astype(F32)
    for j in range(SAMP_MB):
        at = slice(j * PATCHES, (j + 1) * PATCHES)
        order = order_ref[pl.ds(section * SAMP_MB + j, 1), :].astype(F32)
        hit = jnp.where(order == line, 1.0, 0.0).astype(BF16)
        start, count = starts[j : j + 1, :], counts[j : j + 1, :]
        down, across = mm(hit, line_low), mm_nt(lane_low, hit)[:1, :]
        down = jnp.where(down < count, start + down, -1.0)
        across = jnp.where(across < count, start + across, -1.0)
        wide = jnp.concatenate([down] * (packed // PATCHES), axis=1)
        hot_ref[at, :] = jnp.where(column == wide, 1.0, 0.0).astype(BF16)
        place_ref[:, at] = jnp.where(packed_line == across, 1.0, 0.0).astype(BF16)
        empty_ref[at, :] = jnp.where(down < 0.0, 1.0, 0.0)


def decoder_kernel(
    y_ref, seg_ref, order_ref, pos_ref, g_hbm,
    w_embed_hbm, b_embed, mask_token,
    gain1, bias1, w_qkv_hbm, w_out_hbm, b_out, gain2, bias2, w_up_hbm, b_up, w_down_hbm, b_down,
    *refs,
):
    hbm, (geb_ref, gy_ref, small_ref, gbup_ref) = refs[:9], refs[9:13]
    buffers = refs[13:22]
    out_ref, at_ref, ot_ref, ct_ref, gt_ref, u_ref, gf_ref, ga_ref, gqkv_ref = buffers
    (
        e2_ref, z_ref, s1_ref, e_ref, rl_ref, h_ref, s2_ref, go_ref, ge_ref, o_ref, c_ref, qkv_ref,
        slope_ref, g_all, hot_ref, place_ref, empty_ref, w_embed, w_qkv, w_out, w_up, w_down,
        w_sem, out_sem,
    ) = refs[22:]
    packed = y_ref.shape[0]
    rows, features = z_ref.shape
    samples = rows // PATCHES
    head_size = features // H_DEC
    total = g_all.shape[0]
    section = lax.axis_index("section")
    mine = pl.ds(pl.multiple_of(section * total, total), total)
    pairs = (
        (w_embed_hbm, w_embed), (w_qkv_hbm, w_qkv), (w_out_hbm, w_out), (w_up_hbm, w_up),
        (w_down_hbm, w_down), (g_hbm.at[mine, :], g_all),
    )
    loads = [pltpu.make_async_copy(a, b, w_sem.at[i]) for i, (a, b) in enumerate(pairs)]
    for load in loads:
        load.start()

    def write(at, *which):
        copies = []
        for i in which:
            target = hbm[i].at[:, at] if 1 <= i <= 4 else hbm[i].at[at, :]
            copies.append(pltpu.make_async_copy(buffers[i], target, out_sem.at[i]))
            copies[-1].start()
        return copies

    small_ref[...] = jnp.zeros_like(small_ref)
    gbup_ref[...] = jnp.zeros_like(gbup_ref)
    ge_ref[...] = jnp.zeros_like(ge_ref)
    seg = seg_ref[pl.ds(section, 1), :].astype(F32)
    place_slots(order_ref, seg, section, hot_ref, place_ref, empty_ref)
    loads[0].wait()
    high, low = split_low(mm(y_ref[...], w_embed[...]) + row(b_embed))
    e2_ref[:packed, :] = high
    e2_ref[packed:, :] = low
    for load in loads[1:]:
        load.wait()

    def one_step(step, carry):
        here = pl.ds(pl.multiple_of(step * rows, rows), rows)
        one_hot = hot_ref[here, :]
        empty = jnp.concatenate([empty_ref[here, :]] * (features // 128), axis=1)
        twice = jnp.concatenate([one_hot, one_hot], axis=1)
        z = mm(twice, e2_ref[...]) + empty * row(mask_token)
        z = z + jnp.concatenate([pos_ref[...]] * samples, axis=0)
        n1, s1 = normalise(z)
        z_ref[...] = z
        s1_ref[...] = s1
        a = (n1 * row(gain1) + row(bias1)).astype(BF16)
        at_ref[...] = jnp.transpose(a)
        writing = write(here, 1)
        qkv_ref[...] = mm(a, w_qkv[...]).astype(BF16)

        def forward(b, carry):
            at = pl.ds(pl.multiple_of(b * PATCHES, PATCHES), PATCHES)
            attention_forward(qkv_ref, o_ref, e_ref, rl_ref, at, PATCHES, features, head_size, None)
            return carry

        lax.fori_loop(0, samples, forward, 0)
        ot_ref[...] = jnp.transpose(o_ref[...])
        h_ref[...] = z_ref[...] + (mm(o_ref[...], w_out[...]) + row(b_out))
        n2, s2 = normalise(h_ref[...])
        s2_ref[...] = s2
        c_ref[...] = (n2 * row(gain2) + row(bias2)).astype(BF16)
        ct_ref[...] = jnp.transpose(c_ref[...])
        feed_forward(c_ref, w_up, b_up, u_ref, slope_ref, 512)
        writing += write(here, 2, 3, 5)
        out_ref[...] = (h_ref[...] + (mm(u_ref[...], w_down[...]) + row(b_down))).astype(BF16)

        g_ref = g_all.at[here, :]
        gt_ref[...] = jnp.transpose(g_ref[...])
        feed_forward_back(g_ref, w_down, slope_ref, gf_ref, gbup_ref, 512)
        writing += write(here, 0, 4, 6)
        gc = mm_nt(gf_ref[...], w_up[...])
        g = g_ref[...].astype(F32)
        h = h_ref[...]
        n2 = (h - jnp.mean(h, axis=-1, keepdims=True)) * s2_ref[...]
        gh = g + normalise_back(gc, n2, s2_ref[...], row(gain2))
        small_ref[2:3, :] += rows_sum(gh)
        small_ref[3:4, :] += rows_sum(gc * n2)
        small_ref[4:5, :] += rows_sum(gc)
        small_ref[5:6, :] += rows_sum(g)
        h_ref[...] = gh
        ga_ref[...] = gh.astype(BF16)
        go_ref[...] = mm_nt(ga_ref[...], w_out[...]).astype(BF16)
        writing += write(here, 7)

        def backward(b, carry):
            at = pl.ds(pl.multiple_of(b * PATCHES, PATCHES), PATCHES)
            attention_backward(
                qkv_ref, go_ref, o_ref, e_ref, rl_ref, gqkv_ref, at, PATCHES, features, head_size
            )
            return carry

        lax.fori_loop(0, samples, backward, 0)
        writing += write(here, 8)
        gn = mm_nt(gqkv_ref[...], w_qkv[...])
        z = z_ref[...]
        n1 = (z - jnp.mean(z, axis=-1, keepdims=True)) * s1_ref[...]
        gz = h_ref[...] + normalise_back(gn, n1, s1_ref[...], row(gain1))
        small_ref[0:1, :] += rows_sum(gn * n1)
        small_ref[1:2, :] += rows_sum(gn)
        small_ref[6:7, :] += rows_sum(gz * empty)
        ge_ref[...] += mm(place_ref[:, here], gz.astype(BF16))
        for copy in writing:
            copy.wait()
        return carry

    lax.fori_loop(0, total // rows, one_step, 0)
    ge = ge_ref[...]
    small_ref[7:8, :] = rows_sum(ge)
    geb_ref[...] = ge.astype(BF16)
    gy_ref[...] = mm_nt(geb_ref[...], w_embed[...]).astype(BF16)


def in_vmem(count):
    return [pl.BlockSpec(memory_space=pltpu.VMEM)] * count


def in_hbm():
    return pl.BlockSpec(memory_space=pl.ANY)


def shape(rows, columns, dtype=BF16):
    return jax.ShapeDtypeStruct((rows, columns), dtype)


KERNEL_VMEM = 60 * 2**20


def encoder_forward(x, segments, params):
    rows, d = x.shape[0] // 2, x.shape[1]
    ff = params[7].shape[1]
    outs = [
        (rows, d, BF16),
        (d, rows, BF16),
        (rows, 3 * d, BF16),
        (rows, H_ENC * rows, BF16),
        (rows, d, F32),
        (rows, d, BF16),
        (d, rows, BF16),
        (rows, d, F32),
        (rows, 1, F32),
        (d, rows, BF16),
        (ff, rows, BF16),
        (rows, ff, BF16),
    ]
    more = [(rows, d, F32), (rows, d, BF16), (rows, ff, BF16)]
    args = [x, segments, *params]
    matrices = [w for w in params if w.dtype == BF16]
    return pl.pallas_call(
        encoder_forward_kernel,
        out_shape=[shape(*o) for o in outs],
        in_specs=in_vmem(2) + [in_hbm() if w.dtype == BF16 else in_vmem(1)[0] for w in params],
        out_specs=[in_hbm()] * len(outs),
        scratch_shapes=[pltpu.VMEM((r, w), t) for r, w, t in outs + more]
        + [pltpu.VMEM(w.shape, BF16) for w in matrices]
        + [pltpu.SemaphoreType.DMA((len(matrices),)), pltpu.SemaphoreType.DMA((len(outs),))],
        compiler_params=pltpu.CompilerParams(vmem_limit_bytes=KERNEL_VMEM),
        name="encoder_forward",
    )(*args)


def encoder_backward(x, gy, saved, params):
    gain1, _, w_qkv, w_out, _, gain2, _, w_up, _, w_down, _ = params
    rows, d = gy.shape
    ff = w_up.shape[1]
    outs = [
        shape(rows, d),
        shape(rows, ff),
        shape(rows, d),
        shape(rows, 3 * d),
        shape(8, d, F32),
        shape(1, ff, F32),
    ]
    args = [x, gy, *saved, gain1, w_qkv, w_out, gain2, w_up, w_down]
    return pl.pallas_call(
        encoder_backward_kernel,
        out_shape=outs,
        in_specs=in_vmem(len(args)),
        out_specs=in_vmem(len(outs)),
        scratch_shapes=[pltpu.VMEM((rows, d), F32), pltpu.VMEM((rows, d), BF16)],
        compiler_params=pltpu.CompilerParams(vmem_limit_bytes=KERNEL_VMEM),
        name="encoder_backward",
    )(*args)


def decoder_both(y, segments, orders, g, embed_params, params):
    packed, d_enc = y.shape
    total, d = g.shape[0] // 2, g.shape[1]
    rows = 6 * PATCHES
    ff = params[7].shape[1]
    args = [y, segments, orders, positions(PATCHES, d), g, *embed_params, *params]
    in_specs = in_vmem(4) + [in_hbm()]
    in_specs += [in_hbm() if x.dtype == BF16 else in_vmem(1)[0] for x in args[5:]]
    wide = [ff, ff, d, 3 * d]
    outs = [shape(total, d)] + [shape(d, total)] * 4 + [shape(total, w) for w in wide]
    buffers = [(rows, d, BF16)] + [(d, rows, BF16)] * 4 + [(rows, w, BF16) for w in wide]
    last = [shape(packed, d), shape(packed, d_enc), shape(8, d, F32), shape(1, ff, F32)]
    scratch = [
        (2 * packed, d, BF16),
        (rows, d, F32),
        (rows, 1, F32),
        (rows, H_DEC * PATCHES, BF16),
        (rows, d, F32),
        (rows, d, F32),
        (rows, 1, F32),
        (rows, d, BF16),
        (packed, d, F32),
        (rows, d, BF16),
        (rows, d, BF16),
        (rows, 3 * d, BF16),
        (rows, ff, BF16),
        (total, d, BF16),
        (total, packed, BF16),
        (packed, total, BF16),
        (total, 128, F32),
    ]
    matrices = [x for x in args[5:] if x.dtype == BF16]
    return pl.pallas_call(
        decoder_kernel,
        out_shape=outs + last,
        in_specs=in_specs,
        out_specs=[in_hbm()] * len(outs) + in_vmem(len(last)),
        scratch_shapes=[pltpu.VMEM((r, w), t) for r, w, t in buffers + scratch]
        + [pltpu.VMEM(x.shape, BF16) for x in matrices]
        + [pltpu.SemaphoreType.DMA((k,)) for k in (len(matrices) + 1, len(outs))],
        compiler_params=pltpu.CompilerParams(vmem_limit_bytes=KERNEL_VMEM),
        name="decoder_both",
    )(*args)


MESH = pl.DeviceIdType.MESH
ENC_QKV, ENC_OUT, ENC_UP, ENC_DOWN, EMBED, DEC_QKV, DEC_OUT, DEC_UP, DEC_DOWN = range(9)
GIVE, PAIR, FFN, LN2, GO, ATT, GN, LAST = range(10, 18)
SMALL = -1
ROW_BUP, ROW_DEC_BUP, ROW_DEC, SMALL_ROWS = 6, 10, 16, 24
Z, Y, X, CORE = range(4)
ORDERS = ((X, Y, Z), (Y, X, Z), (X, Z, Y), (Y, Z, X), (Z, X, Y), (Z, Y, X))


class Chunk:
    def __init__(self, name, half, offset, rows, width, first_row=None):
        self.name, self.half, self.offset, self.rows, self.width = name, half, offset, rows, width
        self.first_row, self.turned, self.order = first_row, name == DEC_DOWN, None
        self.decoder = name in (DEC_QKV, DEC_UP, DEC_OUT)

    def columns(self, side):
        return pl.ds(pl.multiple_of(side * self.half + self.offset, 128), self.width)

    def place(self, side):
        if self.turned:
            return (pl.ds(pl.multiple_of(side * self.half + self.offset, 128), self.rows), slice(None))
        if self.first_row is None:
            return (slice(None), self.columns(side))
        return (pl.ds(self.first_row, self.rows), self.columns(side))

    @property
    def bytes(self):
        return 32 * self.rows * self.width

    def loads(self, order):
        if order[0] == Z:
            return (2 * self.bytes, self.bytes / 4, self.bytes / 8)
        if order[1] == Z:
            return (self.bytes, self.bytes, self.bytes / 8)
        return (self.bytes, self.bytes / 2, self.bytes / 2)


LINK_ORDERS = (2, 1, 2, 5, 3, 0, 3, 0, 3, 3, 0, 0, 0, 0, 1)


def make_chunks():
    chunks = [Chunk(ENC_DOWN, 384, 0, 48, 384, 48 * q) for q in range(4)]
    chunks += [Chunk(ENC_UP, 1536, 768 * q, 48, 768) for q in range(2)]
    chunks += [Chunk(ENC_OUT, 384, 0, 48, 384)]
    chunks += [Chunk(ENC_QKV, 1152, 0, 48, 768), Chunk(ENC_QKV, 1152, 768, 48, 384)]
    chunks += [Chunk(EMBED, 256, 0, 48, 256)]
    chunks += [Chunk(DEC_QKV, 768, 0, 32, 768), Chunk(DEC_DOWN, 256, 0, 256, 128)]
    chunks += [Chunk(DEC_UP, 1024, o, 32, 512) for o in (0, 512)]
    chunks += [Chunk(DEC_OUT, 256, 0, 32, 256)]
    for chunk, order in zip(chunks, LINK_ORDERS):
        chunk.order = ORDERS[order]
    return chunks


def make_groups(chunks):
    return [[c] for c in range(len(chunks))]


def product_cost(k, count):
    if k.turned:
        return 5.0
    return k.rows * k.width * (0.9 / 8192 if k.decoder else 0.6 / 18432)


def tasks_in_order(chunks, groups):
    def gives(name):
        found = [(g, chunks[m[0]], len(m)) for g, m in enumerate(groups)]
        kind = PAIR if name == DEC_DOWN else GIVE
        return [(kind, g, product_cost(k, size)) for g, k, size in found if k.name == name]

    tasks = gives(ENC_DOWN)
    tasks += [(FFN, t, 1.7) for t in range(4)] + gives(ENC_UP)
    tasks += [(LN2, 0, 1.0), (GO, 0, 0.9)]
    tasks += [(ATT, g, 1.5) for g in range(6)]
    tasks += gives(ENC_OUT) + gives(ENC_QKV) + gives(EMBED)
    tasks += gives(DEC_QKV) + gives(DEC_DOWN)
    tasks += [(GN, j, 0.9) for j in range(3)] + [(LAST, 0, 1.5)]
    return tasks + gives(DEC_UP) + gives(DEC_OUT)


def decoder_arrays(chunks):
    names = []
    for k in chunks:
        if (k.decoder or k.turned) and k.name not in names:
            names.append(k.name)
    return names


def make_plan(chunks, groups):
    tasks = tasks_in_order(chunks, groups)
    lhs = decoder_arrays(chunks)
    free = [0.0] * 4
    rate = [80e3, 80e3, 80e3, 500e3]
    pending, plan, now, owned = [], [], 2.0, set()

    def send(link, size, latency):
        begin = max(now, free[link])
        free[link] = begin + size / rate[link]
        return free[link] + latency

    def blocked(task):
        if task[0] not in (GIVE, PAIR):
            return False
        name = chunks[groups[task[1]][0]].name
        if name not in lhs[2:]:
            return False
        name = lhs[lhs.index(name) - 2]
        return any(chunks[m[0]].name == name and g not in owned for g, m in enumerate(groups))

    while tasks or pending:
        pending.sort()
        if pending and (pending[0][0] <= now or not tasks or blocked(tasks[0])):
            arrive, stage, c = pending.pop(0)
            now = max(now, arrive)
            plan.append((stage, c))
            if c == SMALL:
                now += 0.1
                if stage < 4:
                    pending.append((now + 2.0, stage + 1, c))
                continue
            members = groups[c] if stage == 1 else [c]
            k = chunks[members[0]]
            if stage == 1:
                owned.add(c)
                now += 0.6 if k.turned else product_cost(k, len(members)) + 0.2 * len(members)
            else:
                now += 0.25
            for c in members:
                k = chunks[c]
                if stage < 4:
                    axis = k.order[stage - 1]
                    latency = 3.5 if axis == Z else 3.0
                    arrive = send(axis, k.loads(k.order)[stage - 1], latency)
                    pending.append((arrive, stage + 1, c))
                elif stage == 4:
                    pending.append((send(CORE, k.bytes / 16, 1.8), 5, c))
            continue
        name, arg, cost = tasks.pop(0)
        plan.append((name, arg))
        now += cost
        if name in (GIVE, PAIR):
            arrive = [send(CORE, chunks[c].bytes, 1.8) for c in groups[arg]]
            pending.append((max(arrive), 1, arg))
        elif name == LAST:
            pending.append((now + 2.0, 1, SMALL))
    return plan


class Ring:
    def __init__(self, sources, slots, semaphores, depth):
        self.copies = [
            pltpu.make_async_copy(source, slot, semaphores())
            for source, slot in zip(sources, slots)
        ]
        self.slots, self.depth, self.at = slots, depth, 0

    def begin(self):
        for copy in self.copies[: self.depth]:
            copy.start()

    def take(self):
        self.copies[self.at].wait()
        return self.slots[self.at]

    def done(self):
        ahead = self.at + self.depth
        if ahead < len(self.copies):
            self.copies[ahead].start()
        self.at += 1


class Names:
    def __init__(self, names, refs):
        self.__dict__.update(zip(names, refs))


LOADS = 96


def finish_kernel(chunks, groups, plan, r):
    n = len(chunks)
    s = lax.axis_index("section")
    d = lax.axis_index("dp")
    here = (d // 4, (d // 2) % 2, d % 2)
    z, y, x = here
    sibling = {"section": 1 - s}
    z_at = [lax.rem(z + k, 4) for k in (1, 2, 3)]
    peers = {
        X: [(1 - x, {"dp": d + 1 - 2 * x})],
        Y: [(1 - y, {"dp": d + 2 - 4 * y})],
        Z: [(p, {"dp": d + 4 * (p - z)}) for p in z_at],
    }
    every = [sibling] + [peer for axis in (X, Y, Z) for _, peer in peers[axis]]

    barrier = pltpu.get_barrier_semaphore()
    for peer in every:
        pl.semaphore_signal(barrier, inc=1, device_id=peer, device_id_type=MESH)

    counter = iter(range(LOADS))

    def semaphore():
        return r.load_sem.at[next(counter)]

    def remote(src, dst, send, recv, peer):
        return pltpu.make_async_remote_copy(
            src_ref=src, dst_ref=dst, send_sem=send, recv_sem=recv, device_id=peer, device_id_type=MESH
        )

    rhs_of = {DEC_QKV: r.gqkv2, DEC_UP: r.gf2, DEC_OUT: r.ga2}
    lhs_of = {DEC_QKV: r.at2, DEC_UP: r.ct2, DEC_OUT: r.ot2, DEC_DOWN: r.gt2}
    tiles, widths, last_use = [], [], {}

    def wide_columns(g, side):
        k, width = chunks[groups[g][0]], sum(chunks[c].width for c in groups[g])
        return pl.ds(pl.multiple_of(side * k.half + k.offset, 128), width)

    for i, (name, arg) in enumerate(plan):
        if name == PAIR:
            tiles += [r.u2.at[:, t * 512 : (t + 1) * 512] for t in range(4)]
            last_use[DEC_DOWN] = i
        elif name in (GIVE, 1) and arg != SMALL and chunks[groups[arg][0]].decoder:
            k = chunks[groups[arg][0]]
            tiles.append(rhs_of[k.name].at[:, wide_columns(arg, 1 - s if name == GIVE else s)])
            last_use[k.name] = i
    lhs_names = decoder_arrays(chunks)
    assert sorted(lhs_names, key=last_use.get) == lhs_names
    rhs_slots = [r.rhs.at[i % 2, :, : tile.shape[1]] for i, tile in enumerate(tiles)]
    rhs = Ring(tiles, rhs_slots, semaphore, 2)
    lhs = Ring([lhs_of[k] for k in lhs_names], [r.lhs.at[i % 2] for i in range(4)], semaphore, 2)
    tokens, d_enc = r.gy.shape
    blocks = []
    for t in range(4):
        at = pl.ds(t * d_enc, d_enc)
        blocks += [r.w_down.at[at, :], r.w_up.at[:, at]]
    blocks.append(r.w_out)
    blocks += [r.w_qkv.at[:, pl.ds(j * d_enc, d_enc)] for j in range(3)]
    weights = Ring(blocks, [r.w.at[i % 4] for i in range(12)], semaphore, 4)
    e_width = 2 * tokens
    e_ring = Ring(
        [r.e.at[:, pl.ds(g * e_width, e_width)] for g in range(6)],
        [r.e_v.at[g % 2] for g in range(6)],
        semaphore,
        2,
    )

    def load(source, target):
        return pltpu.make_async_copy(source, target, semaphore())

    mine = pl.ds(pl.multiple_of(s * tokens, tokens), tokens)
    load_gy, load_slope, load_ut = load(r.gy, r.gy_v), load(r.slope, r.slope_v), load(r.ut, r.ut_v)
    load_ct, load_at, load_ot = load(r.ct, r.ct_v), load(r.at, r.at_v), load(r.ot, r.ot_v)
    load_n2, load_s2, load_qkv = load(r.n2, r.n2_v), load(r.s2, r.s2_v), load(r.qkv, r.qkv_v)
    load_o, load_rl, load_x = load(r.o, r.o_v), load(r.rl, r.rl_v), load(r.x.at[mine, :], r.x_v)
    load_y, load_geb = load(r.y, r.y_v), load(r.geb, r.geb_v)
    load_gy.start()
    load_ut.start()
    load_slope.start()
    weights.begin()
    begun = [
        (load_ct, load_n2, load_s2),
        (load_qkv, load_o, load_rl, e_ring),
        (load_ot, load_at, load_y, load_geb),
        (load_x, lhs, rhs),
    ]

    def begin_some():
        for copy in begun.pop(0) if begun else ():
            copy.begin() if isinstance(copy, Ring) else copy.start()

    half = r.decoded.shape[1] // 2
    give_half = r.decoded.at[:, pl.ds(pl.multiple_of((1 - s) * half, half), half), :]
    decoded_away = remote(give_half, r.decoded_got, r.swap_sem.at[0], r.swap_sem.at[1], sibling)
    gx_columns = d_enc // 2
    gx_half = r.gx.at[:, pl.ds(pl.multiple_of((1 - s) * gx_columns, 128), gx_columns)]
    gx_away = remote(gx_half, r.gx_got, r.swap_sem.at[2], r.swap_sem.at[3], sibling)

    small = r.small
    small[...] = jnp.zeros_like(small)
    small[ROW_DEC : ROW_DEC + 8, : r.small2.shape[1]] = r.small2[...]
    quarter = r.gbup2.shape[1] // 4
    for i in range(4):
        piece = r.gbup2[:, i * quarter : (i + 1) * quarter]
        small[ROW_DEC_BUP + i : ROW_DEC_BUP + i + 1, :quarter] = piece

    pl.semaphore_wait(barrier, len(every))

    copies = {}
    first_slot = (0, 1, 4, 7, 10)

    def chunk_copy(c, slot, src, dst, peer):
        copy = remote(src, dst, r.send_sem.at[c, slot], r.recv_sem.at[c, slot], peer)
        copy.start()
        copies[c, slot] = copy

    sent = set()

    def sent_by(c, slot):
        if (c, slot) not in sent:
            sent.add((c, slot))
            copies[c, slot].wait_send()

    staged = {}

    def staging(c):
        k = chunks[c]
        buffers = r.stage[k.rows, k.width]
        turn = staged.setdefault((k.rows, k.width), [])
        if len(turn) >= len(buffers):
            sent_by(turn[-len(buffers)], 0)
        turn.append(c)
        return buffers[(len(turn) - 1) % len(buffers)]

    def shard(i):
        return (i // 4, (i // 2) % 2, i % 2)

    waited = set()

    def arrived(copy):
        if id(copy) not in waited:
            waited.add(id(copy))
            copy.wait()

    def product(g, side):
        k, columns = chunks[groups[g][0]], wide_columns(g, side)
        if k.decoder:
            return mm(lhs.slots[lhs_names.index(k.name)][...], rhs.take()[...])
        if k.name == EMBED:
            arrived(load_y)
            arrived(load_geb)
            return mm_tn(r.y_v[...], r.geb_v[:, columns])
        if k.name == ENC_DOWN:
            arrived(load_ut)
            arrived(load_gy)
            at = [i * 192 + k.first_row for i in range(16)]
            left = jnp.concatenate([r.ut_v[i : i + k.rows, :] for i in at], axis=0)
            return mm(left, r.gy_v[:, columns])
        if k.name == ENC_UP:
            arrived(load_ct)
            return mm(r.ct_v[...], r.slope_v[:, columns])
        if k.name == ENC_OUT:
            arrived(load_ot)
            return mm(r.ot_v[...], r.ga_v[:, columns])
        arrived(load_at)
        return mm(r.at_v[...], r.qkv_v[:, columns])

    def after_product(i, g):
        k = chunks[groups[g][0]]
        if k.decoder:
            rhs.done()
            if last_use[k.name] == i:
                lhs.done()

    def wait_lhs(k):
        if k.name in lhs_names:
            arrived(lhs.copies[lhs_names.index(k.name)])

    def give(i, g):
        members = groups[g]
        wait_lhs(chunks[members[0]])
        buffers = [staging(c) for c in members]
        value = product(g, 1 - s).astype(BF16)
        for m, (c, buffer) in enumerate(zip(members, buffers)):
            k = chunks[c]
            part = value[:, m * k.width : (m + 1) * k.width]
            for j in range(16):
                buffer[shard(j)] = part[j * k.rows : (j + 1) * k.rows]
            chunk_copy(c, 0, buffer, r.acc[c], sibling)
        after_product(i, g)
        begin_some()

    def pair(i, g):
        both = groups[g]
        wait_lhs(chunks[both[0]])
        left = lhs.slots[lhs_names.index(DEC_DOWN)]
        side_rows = chunks[both[0]].half
        buffers = [staging(c) for c in both]
        for t in range(4):
            tile = rhs.take()
            for side, targets in ((1 - s, buffers), (s, [r.acc[c] for c in both])):
                at = pl.ds(pl.multiple_of(side * side_rows, side_rows), side_rows)
                value = mm(left[at, :], tile[...]).astype(BF16)
                for c, target in zip(both, targets):
                    k = chunks[c]
                    rows = slice(k.offset, k.offset + k.rows)
                    for j in range(4):
                        target[shard(4 * t + j)] = value[rows, j * k.width : (j + 1) * k.width]
            rhs.done()
        lhs.done()
        for c, buffer in zip(both, buffers):
            chunk_copy(c, 0, buffer, r.got[c], sibling)

    def spots(k, stage):
        fixed = {axis: here[axis] for axis in k.order[: stage - 1]}
        return [fixed.get(axis, slice(None)) for axis in (Z, Y, X)]

    def send_stage(c, stage):
        k = chunks[c]
        axis = k.order[stage - 1]
        for j, (coordinate, peer) in enumerate(peers[axis]):
            at = spots(k, stage)
            at[axis] = coordinate
            src = r.acc[c].at[tuple(at)]
            chunk_copy(c, first_slot[stage] + j, src, r.recv[stage - 1][c].at[j], peer)

    def got_stage(c, stage):
        k = chunks[c]
        count = len(peers[k.order[stage - 1]])
        for j in range(count):
            copies[c, first_slot[stage] + j].wait_recv()
        return count

    def add_stage(c, stage):
        k, acc, got = chunks[c], r.acc[c], r.recv[stage - 1][c]
        count = got_stage(c, stage)
        left = [axis for axis in (Z, Y, X) if axis not in k.order[:stage]]
        sizes = [(4, 2, 2)[axis] for axis in left]
        for j in range(math.prod(sizes)):
            place, rest = {}, j
            for axis, size in reversed(list(zip(left, sizes))):
                place[axis] = rest % size
                rest //= size
            at = tuple(place.get(axis, here[axis]) for axis in (Z, Y, X))
            index = tuple(place[axis] for axis in left)
            if count == 1:
                acc[at] = acc[at] + got[(0,) + index]
            else:
                total = acc[at].astype(F32)
                for m in range(count):
                    total = total + got[(m,) + index].astype(F32)
                acc[at] = total.astype(BF16)

    def stage1(i, g):
        members = groups[g]
        for c in members:
            copies[c, 0].wait_recv()
        if chunks[members[0]].turned:
            for c in members:
                acc = r.acc[c]
                for j in range(16):
                    acc[shard(j)] = acc[shard(j)] + r.got[c][shard(j)]
                send_stage(c, 1)
            return
        value = product(g, s)
        for m, c in enumerate(members):
            k, acc = chunks[c], r.acc[c]
            wide = value[:, m * k.width : (m + 1) * k.width]
            for j in range(16):
                part = wide[j * k.rows : (j + 1) * k.rows]
                acc[shard(j)] = (part + acc[shard(j)].astype(F32)).astype(BF16)
            send_stage(c, 1)
        after_product(i, g)

    def stage2(i, c):
        add_stage(c, 1)
        send_stage(c, 2)

    def stage3(i, c):
        add_stage(c, 2)
        send_stage(c, 3)

    def stage4(i, c):
        k = chunks[c]
        total = r.acc[c][here].astype(F32)
        for j in range(got_stage(c, 3)):
            total = total + r.recv[2][c][j].astype(F32)
        out = r.out[k.name]
        out[k.place(s)] = total.astype(BF16)
        final = out.at[k.place(s)]
        chunk_copy(c, 10, final, final, sibling)

    def stage5(i, c):
        copies[c, 10].wait_recv()

    small_copies = []

    def small_copy(source, peer):
        slot = len(small_copies)
        copy = remote(
            source, r.small_got.at[slot], r.small_sem.at[0, slot], r.small_sem.at[1, slot], peer
        )
        copy.start()
        small_copies.append(copy)

    def small_stage(stage):
        if stage < 4:
            small_copies[stage - 1].wait()
            total = small[...] + r.small_got[stage - 1]
            if stage < 3:
                small[...] = total
                small_copy(small, peers[X if stage == 1 else Y][0][1])
            else:
                r.small_sum[...] = total
                for _, peer in peers[Z]:
                    small_copy(r.small_sum, peer)
        else:
            total = r.small_sum[...]
            for j in range(3):
                small_copies[3 + j].wait()
                total = total + r.small_got[3 + j]
            r.out_small[...] = total

    def ffn(i, t):
        if t == 0:
            arrived(load_gy)
            load_slope.wait()
        at = slice(t * d_enc, (t + 1) * d_enc)
        gu = mm_nt(r.gy_v[...], weights.take()[...])
        weights.done()
        gf = (gu * r.slope_v[:, at].astype(F32)).astype(BF16)
        r.slope_v[:, at] = gf
        small[ROW_BUP + t : ROW_BUP + t + 1, :] = rows_sum(gf.astype(F32))
        gc = mm_nt(gf, weights.take()[...])
        weights.done()
        r.sum_v[...] = gc if t == 0 else r.sum_v[...] + gc

    def ln2(i, _):
        load_n2.wait()
        load_s2.wait()
        g, gc, n2 = r.gy_v[...].astype(F32), r.sum_v[...], r.n2_v[...]
        gh = g + normalise_back(gc, n2, r.s2_v[...], row(r.gain2))
        small[2:3, :] = rows_sum(gh)
        small[3:4, :] = rows_sum(gc * n2)
        small[4:5, :] = rows_sum(gc)
        small[5:6, :] = rows_sum(g)
        r.n2_v[...] = gh
        r.ga_v[...] = gh.astype(BF16)

    def go(i, _):
        r.go_v[...] = mm_nt(r.ga_v[...], weights.take()[...]).astype(BF16)
        weights.done()

    def att(i, g):
        if g == 0:
            for copy in (load_qkv, load_o, load_rl):
                copy.wait()
        at = slice(g * 128, (g + 1) * 128)
        parts = [slice(j * d_enc + g * 128, j * d_enc + (g + 1) * 128) for j in range(3)]
        q, k, v = (r.qkv_v[:, part] for part in parts)
        grads = attention_backward_group(
            q, k, v, e_ring.take()[...], r.go_v[:, at], r.o_v[:, at], r.rl_v[:, at],
            d_enc // H_ENC,
        )
        e_ring.done()
        for part, grad in zip(parts, grads):
            r.qkv_v[:, part] = grad

    def gn(i, j):
        part = mm_nt(r.qkv_v[:, j * d_enc : (j + 1) * d_enc], weights.take()[...])
        weights.done()
        r.sum_v[...] = part if j == 0 else r.sum_v[...] + part

    def last(i, _):
        load_x.wait()
        n1, s1 = normalise(r.x_v[...].astype(F32))
        total = r.sum_v[...]
        small[0:1, :] = rows_sum(total * n1)
        small[1:2, :] = rows_sum(total)
        small_copy(small, sibling)
        gx = r.n2_v[...] + normalise_back(total, n1, s1, row(r.gain1))
        r.gx[...] = gx.astype(BF16)
        gx_away.start()
        decoded_away.start()

    run = {
        GIVE: give, PAIR: pair, FFN: ffn, LN2: ln2, GO: go, ATT: att, GN: gn, LAST: last,
        1: stage1, 2: stage2, 3: stage3, 4: stage4, 5: stage5,
    }
    for i, (name, arg) in enumerate(plan):
        if arg == SMALL:
            small_stage(name)
        else:
            run[name](i, arg)

    for c, slot in copies:
        sent_by(c, slot)
    gx_away.wait()
    decoded_away.wait()


def finish_buffers(chunks, rows, d, ff, dec_total, dec):
    def of(dtype, *dims):
        return (dims, dtype)

    return dict(
        y_v=of(BF16, rows, d),
        geb_v=of(BF16, rows, dec),
        gy_v=of(BF16, rows, d),
        slope_v=of(BF16, rows, ff),
        n2_v=of(F32, rows, d),
        s2_v=of(F32, rows, 1),
        qkv_v=of(BF16, rows, 3 * d),
        o_v=of(BF16, rows, d),
        rl_v=of(F32, rows, d),
        x_v=of(BF16, rows, d),
        ga_v=of(BF16, rows, d),
        go_v=of(BF16, rows, d),
        sum_v=of(F32, rows, d),
        ut_v=of(BF16, ff, rows),
        ct_v=of(BF16, d, rows),
        at_v=of(BF16, d, rows),
        ot_v=of(BF16, d, rows),
        e_v=of(BF16, 2, rows, 2 * rows),
        w=of(BF16, 4, d, d),
        lhs=of(BF16, 2, dec, dec_total),
        rhs=of(BF16, 2, dec_total, 768),
        small=of(F32, SMALL_ROWS, d),
        small_sum=of(F32, SMALL_ROWS, d),
        small_got=of(F32, 6, SMALL_ROWS, d),
    )


def finish(acts):
    enc, dec = acts["enc"], acts["dec"]
    gain1, _, w_qkv, w_out, _, gain2, _, w_up, _, w_down, _ = enc["params"]
    qkv, e, rl, o, n2, s2, slope = acts["saved"]
    given = dict(
        x=acts["x"], y=acts["y"], gy=acts["gy"], geb=acts["geb"], qkv=qkv, e=e, rl=rl, o=o, n2=n2,
        s2=s2, slope=slope, at=enc["at"], ot=enc["ot"], ct=enc["ct"], ut=enc["ut"], at2=dec["at"], ot2=dec["ot"],
        ct2=dec["ct"], gt2=dec["gt"], u2=dec["u"], gf2=dec["gf"], ga2=dec["ga"],
        gqkv2=dec["gqkv"], w_qkv=w_qkv, w_out=w_out, w_up=w_up, w_down=w_down,
        decoded=acts["decoded"].reshape(SAMP_MB, PATCHES, -1),
    )
    n_hbm = len(given)
    given.update(small2=acts["small2"], gbup2=acts["gbup2"], gain1=gain1, gain2=gain2)
    rows, d = acts["gy"].shape
    ff = w_up.shape[1]
    dec_d, dec_total = dec["at"].shape
    dec_ff = dec["u"].shape[1]
    chunks = make_chunks()
    n = len(chunks)
    groups = make_groups(chunks)
    plan = make_plan(chunks, groups)

    dims = {
        ENC_QKV: (d, 3 * d), ENC_OUT: (d, d), ENC_UP: (d, ff), ENC_DOWN: (ff, d),
        EMBED: (d, dec_d), DEC_QKV: (dec_d, 3 * dec_d), DEC_OUT: (dec_d, dec_d),
        DEC_UP: (dec_d, dec_ff), DEC_DOWN: (dec_ff, dec_d),
    }
    big = [
        shape(dims[k][1], dims[k][0] // 16) if k == DEC_DOWN else shape(dims[k][0] // 16, dims[k][1])
        for k in range(9)
    ]
    outs = dict(
        out_small=shape(SMALL_ROWS, d, F32),
        decoded_got=jax.ShapeDtypeStruct((SAMP_MB, PATCHES // 2, dec_d), BF16),
        gx=shape(rows, d),
        gx_got=shape(rows, d // 2),
    )
    single = finish_buffers(chunks, rows, d, ff, dec_total, dec_d)
    left = (4, 2, 2)
    lists = [[], [], [], [], []]
    for k in chunks:
        block = (k.rows, k.width)
        lists[0].append((left + block, BF16))
        if k.turned:
            lists[1].append((left + block, BF16))
        for stage in range(3):
            rest = [left[axis] for axis in (Z, Y, X) if axis not in k.order[: stage + 1]]
            count = 3 if k.order[stage] == Z else 1
            lists[2 + stage].append(((count, *rest, *block), BF16))
    blocks = sorted({(k.rows, k.width) for k in chunks})
    slots = [2 if block == (48, 384) else 1 for block in blocks]
    lists.append([(left + block, BF16) for block, m in zip(blocks, slots) for _ in range(m)])
    semaphores = dict(
        load_sem=(LOADS,), send_sem=(n, 11), recv_sem=(n, 11), small_sem=(2, 6), swap_sem=(4,)
    )

    def kernel(*refs):
        refs = list(refs)

        def take(count):
            taken = refs[:count]
            del refs[:count]
            return taken

        names = list(given) + list(outs)
        r = Names(names, take(len(names)))
        r.out = take(9)
        r.__dict__.update(zip(single, take(len(single))))
        r.acc = take(n)
        r.got = dict(zip([c for c, k in enumerate(chunks) if k.turned], take(len(lists[1]))))
        r.recv = [take(n) for _ in range(3)]
        r.stage = {block: take(m) for block, m in zip(blocks, slots)}
        r.__dict__.update(zip(semaphores, take(len(semaphores))))
        finish_kernel(chunks, groups, plan, r)

    flat = list(single.values()) + [b for group in lists for b in group]
    results = pl.pallas_call(
        kernel,
        out_shape=list(outs.values()) + big,
        in_specs=[in_hbm()] * n_hbm + in_vmem(len(given) - n_hbm),
        out_specs=in_vmem(len(outs) + 9),
        scratch_shapes=[pltpu.VMEM(*b) for b in flat]
        + [pltpu.SemaphoreType.DMA(v) for v in semaphores.values()],
        compiler_params=pltpu.CompilerParams(
            collective_id=1, has_side_effects=True, vmem_limit_bytes=FINISH_VMEM
        ),
        name="finish",
    )(*given.values())
    return write_outputs(results, given["decoded"], dims)


FINISH_VMEM = 62 * 2**20


def write_kernel(small, decoded_got, gx_own, gx_got, *refs):
    big, decoded_own = refs[:9], refs[9]
    decoded, gx, *totals = refs[10:]
    s = lax.axis_index("section")
    half = decoded.shape[1]
    samples, rows, columns = decoded_own.shape[0], gx_own.shape[0], gx.shape[1]
    own = decoded_own[:, pl.ds(pl.multiple_of(s * half, half), half), :]
    for side, part in ((s, own), (1 - s, decoded_got[...])):
        decoded[pl.ds(side * samples, samples)] = part
    own = gx_own[:, pl.ds(pl.multiple_of(s * columns, 128), columns)]
    for side, part in ((s, own), (1 - s, gx_got[...])):
        gx[pl.ds(pl.multiple_of(side * rows, rows), rows), :] = part
    d = lax.axis_index("dp")
    wide, narrow = small.shape[1], big[DEC_OUT].shape[1]

    def piece(out, line, lanes, position):
        size = out.shape[0]
        value = small[pl.ds(line, 1), :lanes]
        value = pltpu.roll(value, lax.rem(lanes - position * size, lanes), 1)
        out[...] = value[:, :size].reshape(size)

    def matrix(out, name):
        value = big[name][...].astype(F32)
        out[...] = jnp.transpose(value) if name == DEC_DOWN else value

    def block(outs, first_row, bup_row, lanes, names):
        for i, out in zip((0, 1, None, None, 2, 3, 4, None, None, None, 5), outs):
            if i is not None:
                piece(out, first_row + i, lanes, d)
        piece(outs[8], bup_row + d // 4, lanes, d % 4)
        for at, name in zip((2, 3, 7, 9), names):
            matrix(outs[at], name)

    block(totals[:11], 0, ROW_BUP, wide, (ENC_QKV, ENC_OUT, ENC_UP, ENC_DOWN))
    matrix(totals[11], EMBED)
    piece(totals[12], ROW_DEC + 7, narrow, d)
    piece(totals[13], ROW_DEC + 6, narrow, d)
    block(totals[14:], ROW_DEC, ROW_DEC_BUP, narrow, (DEC_QKV, DEC_OUT, DEC_UP, DEC_DOWN))


def write_outputs(results, decoded_own, dims):
    def vector(size):
        return jax.ShapeDtypeStruct((size // 16,), F32)

    def matrix(name):
        return shape(dims[name][0] // 16, dims[name][1], F32)

    def block(qkv, out, up, down):
        d, ff = dims[up]
        return [
            vector(d), vector(d), matrix(qkv), matrix(out), vector(d), vector(d), vector(d),
            matrix(up), vector(ff), matrix(down), vector(d),
        ]

    samples, half, width = results[1].shape
    rows, columns = results[3].shape
    out_shape = [
        jax.ShapeDtypeStruct((2 * samples, half, width), BF16),
        shape(2 * rows, columns),
        *block(ENC_QKV, ENC_OUT, ENC_UP, ENC_DOWN),
        matrix(EMBED),
        vector(width),
        vector(width),
        *block(DEC_QKV, DEC_OUT, DEC_UP, DEC_DOWN),
    ]
    return tuple(
        pl.pallas_call(
            write_kernel,
            out_shape=out_shape,
            in_specs=in_vmem(len(results) + 1),
            out_specs=in_vmem(len(out_shape)),
            compiler_params=pltpu.CompilerParams(vmem_limit_bytes=KERNEL_VMEM),
            name="write_outputs",
        )(*results, decoded_own)
    )


def reduce_plain(arrays, section_index):
    first = section_index == 0
    results = []
    for a in arrays:
        half = a.shape[1] // 2
        keep = lax.dynamic_slice_in_dim(a, section_index * half, half, 1)
        give = lax.dynamic_slice_in_dim(a, (1 - section_index) * half, half, 1)
        got = swapped(give, "section", 0)
        chip = (keep.astype(jnp.float32) + got.astype(jnp.float32)).astype(jnp.bfloat16)
        mine = lax.psum_scatter(chip, "dp", scatter_dimension=0, tiled=True)
        other = swapped(mine, "section", 0)
        whole = jnp.concatenate(
            [jnp.where(first, mine, other), jnp.where(first, other, mine)], axis=1
        )
        results.append(whole.astype(jnp.float32))
    return results


def finish_plain(acts, section_index):
    x, gy, seg_saved, enc, dec = acts["x"], acts["gy"], acts["saved"], acts["enc"], acts["dec"]
    gx, gf1, ga1, gqkv1, small1, gbup1 = encoder_backward(x, gy, seg_saved, enc["params"])
    small2, gbup2 = acts["small2"], acts["gbup2"]
    grads = (
        small1[0], small1[1], mm(enc["at"], gqkv1).astype(BF16), mm(enc["ot"], ga1).astype(BF16), small1[2],
        small1[3], small1[4], mm(enc["ct"], gf1).astype(BF16), gbup1[0], mm(enc["ut"], gy).astype(BF16),
        small1[5],
        weight_grad(acts["y"], acts["geb"]), small2[7], small2[6],
        small2[0], small2[1], mm(dec["at"], dec["gqkv"]).astype(BF16),
        mm(dec["ot"], dec["ga"]).astype(BF16), small2[2], small2[3], small2[4],
        mm(dec["ct"], dec["gf"]).astype(BF16), gbup2[0],
        jnp.transpose(mm(dec["gt"], dec["u"])).astype(BF16), small2[5],
    )
    groups = lax.axis_size("dp")
    big = reduce_plain([g for g in grads if g.ndim == 2], section_index)
    flat = jnp.concatenate([g.reshape(groups, -1) for g in grads if g.ndim == 1], axis=1)
    line = lax.psum_scatter(flat, ("dp"), scatter_dimension=0, tiled=True)
    line = lax.psum(line, "section")[0]
    totals, at = [], 0
    for g in grads:
        if g.ndim == 2:
            totals.append(big.pop(0))
        else:
            size = g.shape[0] // groups
            totals.append(line[at : at + size])
            at += size
    decoded = acts["decoded"].reshape(SAMP_MB, PATCHES, -1)
    first = section_index == 0

    def halves(whole):
        half = whole.shape[1] // 2
        keep = lax.dynamic_slice_in_dim(whole, section_index * half, half, 1)
        give = lax.dynamic_slice_in_dim(whole, (1 - section_index) * half, half, 1)
        got = swapped(give, "section", 0)
        return jnp.concatenate([jnp.where(first, keep, got), jnp.where(first, got, keep)])

    return (halves(decoded), halves(gx), *totals)


def shards(
    patches,
    segment_ids,
    patch_order,
    encoder_gain1,
    encoder_bias1,
    encoder_qkv,
    encoder_out,
    encoder_out_bias,
    encoder_gain2,
    encoder_bias2,
    encoder_up,
    encoder_up_bias,
    encoder_down,
    encoder_down_bias,
    embed_weight,
    embed_bias,
    mask_token,
    decoder_gain1,
    decoder_bias1,
    decoder_qkv,
    decoder_out,
    decoder_out_bias,
    decoder_gain2,
    decoder_bias2,
    decoder_up,
    decoder_up_bias,
    decoder_down,
    decoder_down_bias,
    cotangent,
):
    enc_params = (
        encoder_gain1,
        encoder_bias1,
        encoder_qkv,
        encoder_out,
        encoder_out_bias,
        encoder_gain2,
        encoder_bias2,
        encoder_up,
        encoder_up_bias,
        encoder_down,
        encoder_down_bias,
    )
    embed_params = (embed_weight, embed_bias, mask_token)
    dec_params = (
        decoder_gain1,
        decoder_bias1,
        decoder_qkv,
        decoder_out,
        decoder_out_bias,
        decoder_gain2,
        decoder_bias2,
        decoder_up,
        decoder_up_bias,
        decoder_down,
        decoder_down_bias,
    )
    section_index = lax.axis_index("section")
    y, at1, qkv, e, rl, o1, ot1, n2, s2, ct1, ut1, slope = encoder_forward(
        patches, segment_ids, enc_params
    )
    g = cotangent.reshape(-1, DECODER_WIDTH)
    decoded, at2, ot2, ct2, gt2, u2, gf2, ga2, gqkv2, geb, gy, small2, gbup2 = decoder_both(
        y, segment_ids, patch_order, g, embed_params, dec_params
    )
    acts = dict(
        x=patches,
        y=y,
        gy=gy,
        geb=geb,
        decoded=decoded,
        small2=small2,
        gbup2=gbup2,
        saved=(qkv, e, rl, o1, n2, s2, slope),
        enc=dict(at=at1, ot=ot1, ct=ct1, ut=ut1, params=enc_params),
        dec=dict(at=at2, ot=ot2, ct=ct2, gt=gt2, u=u2, gf=gf2, ga=ga2, gqkv=gqkv2),
    )
    if lax.axis_size("dp") == 16:
        return finish(acts)
    return finish_plain(acts, section_index)


def solution(mesh):
    in_specs = (
        P("dp", None),
        P("dp", None),
        P("dp", None),
        P(),
        P(),
        P(),
        P(),
        P(),
        P(),
        P(),
        P(),
        P(),
        P(),
        P(),
        P(),
        P(),
        P(),
        P(),
        P(),
        P(),
        P(),
        P(),
        P(),
        P(),
        P(),
        P(),
        P(),
        P(),
        P("dp", None, None),
    )
    out_specs = (
        P("dp", "section", None),
        P("dp", "section"),
        P("dp"),
        P("dp"),
        P("dp", None),
        P("dp", None),
        P("dp"),
        P("dp"),
        P("dp"),
        P("dp", None),
        P("dp"),
        P("dp", None),
        P("dp"),
        P("dp", None),
        P("dp"),
        P("dp"),
        P("dp"),
        P("dp"),
        P("dp", None),
        P("dp", None),
        P("dp"),
        P("dp"),
        P("dp"),
        P("dp", None),
        P("dp"),
        P("dp", None),
        P("dp"),
    )
    return jax.shard_map(shards, mesh=mesh, in_specs=in_specs, out_specs=out_specs, check_vma=False)
```

```python
import functools
import math

import jax
import jax.numpy as jnp
import numpy as np
from jax import lax
from jax.experimental import pallas as pl
from jax.experimental.pallas import tpu as pltpu
from jax.sharding import PartitionSpec as P

H_ENC = 12
DECODER_WIDTH = 512
H_DEC = 16
PATCHES = 128
SAMP_MB = 12


EPSILON = 1e-06
MASKED = -1e30


def swapped(block, axis, apart):
    count = lax.axis_size(axis)
    route = []
    for low in range(count):
        high = low | 1 << apart
        if high != low and high < count:
            route += [(low, high), (high, low)]
    return lax.ppermute(block, axis, route)


def positions(count, features):
    column = np.arange(features)
    rate = np.exp(-math.log(10000.0) * (2 * (column // 2)) / features)
    angles = np.arange(count)[:, None] * rate[None, :]
    return np.where(column % 2 == 0, np.sin(angles), np.cos(angles)).astype(np.float32)


def weight_grad(left_side, grads):
    return lax.dot_general(
        left_side, grads, (((0,), (0,)), ((), ())), preferred_element_type=jnp.float32
    ).astype(jnp.bfloat16)


BF16 = jnp.bfloat16
F32 = jnp.float32


def mm(left, right):
    return lax.dot_general(left, right, (((1,), (0,)), ((), ())), preferred_element_type=F32)


def mm_nt(left, right):
    return lax.dot_general(left, right, (((1,), (1,)), ((), ())), preferred_element_type=F32)


def mm_tn(left, right):
    return lax.dot_general(left, right, (((0,), (0,)), ((), ())), preferred_element_type=F32)


def normalise(x):
    center = x - jnp.mean(x, axis=-1, keepdims=True)
    scale = lax.rsqrt(jnp.mean(center * center, axis=-1, keepdims=True) + EPSILON)
    return center * scale, scale


def normalise_back(grad, n, scale, gain):
    gn = grad * gain
    mean_gn = jnp.mean(gn, axis=-1, keepdims=True)
    mean_gnn = jnp.mean(gn * n, axis=-1, keepdims=True)
    return (gn - mean_gn - n * mean_gnn) * scale


def rows_sum(x):
    return jnp.sum(x, axis=0, keepdims=True)


def gelu_both(f):
    c0, c1 = math.sqrt(2.0 / math.pi), 0.044715
    square = f * f
    half = 0.5 + 0.5 * jnp.tanh(f * (c0 + (c0 * c1) * square))
    u = f * half
    return u, half + u * (1.0 - half) * (2.0 * c0 + (6.0 * c0 * c1) * square)


def lane_masks(head_size):
    lane = lax.broadcasted_iota(jnp.int32, (1, 128), 1)
    return [
        jnp.where((lane >= h * head_size) & (lane < (h + 1) * head_size), 1.0, 0.0).astype(BF16)
        for h in range(128 // head_size)
    ]


def stacked(x, masks):
    return jnp.concatenate([x * m for m in masks], axis=0)


def stacked_ones(x, masks, value):
    return jnp.concatenate(
        [jnp.broadcast_to(m * jnp.asarray(value, BF16), x.shape) for m in masks], axis=0
    )


def attention_forward(qkv_ref, o_ref, e_ref, rl_ref, rows, tokens, features, head_size, allowed):
    masks = lane_masks(head_size)
    per_group = len(masks)
    factor = head_size ** (-0.5) * math.log2(math.e)
    for g in range(features // 128):
        q, k, v = (qkv_ref[rows, j * features + g * 128 : j * features + (g + 1) * 128] for j in range(3))
        scores = mm_nt(q, stacked(k, masks))
        parts = []
        for h in range(per_group):
            part = scores[:, h * tokens : (h + 1) * tokens]
            if allowed is not None:
                part = jnp.where(allowed, part, MASKED)
            top = jnp.max(part, axis=-1, keepdims=True)
            parts.append(jnp.exp2((part - top) * factor).astype(BF16))
        e = jnp.concatenate(parts, axis=1)
        width = per_group * tokens
        e_ref[rows, g * width : (g + 1) * width] = e
        both = mm(e, jnp.concatenate([stacked(v, masks), stacked_ones(v, masks, 1.0)], axis=1))
        rl = 1.0 / both[:, 128:]
        rl_ref[rows, g * 128 : (g + 1) * 128] = rl
        o_ref[rows, g * 128 : (g + 1) * 128] = (both[:, :128] * rl).astype(BF16)


def attention_backward_group(q, k, v, e, go, o, rl, head_size):
    masks = lane_masks(head_size)
    per_group, tokens = len(masks), q.shape[0]
    scaling = head_size ** (-0.5)
    go = go.astype(F32) * rl
    go_low = go.astype(BF16)
    inner = (go * o.astype(F32)).astype(BF16)
    left = jnp.concatenate([go_low, inner], axis=1)
    right = jnp.concatenate([stacked(v, masks), stacked_ones(v, masks, -1.0)], axis=1)
    gs = (e.astype(F32) * mm_nt(left, right)).astype(BF16)

    def diagonal(wide):
        return jnp.concatenate(
            [
                wide[h * head_size : (h + 1) * head_size, h * tokens : (h + 1) * tokens]
                for h in range(per_group)
            ],
            axis=0,
        )

    gq = mm(gs, stacked(k, masks)) * scaling
    gk = jnp.transpose(diagonal(mm_tn(q, gs)) * scaling)
    gv = jnp.transpose(diagonal(mm_tn(go_low, e)))
    return gq.astype(BF16), gk.astype(BF16), gv.astype(BF16)


def attention_backward(
    qkv_ref, go_ref, o_ref, e_ref, rl_ref, gqkv_ref, rows, tokens, features, head_size
):
    width = 128 // head_size * tokens
    for g in range(features // 128):
        at = slice(g * 128, (g + 1) * 128)
        spots = [slice(j * features + g * 128, j * features + (g + 1) * 128) for j in range(3)]
        q, k, v = (qkv_ref[rows, spot] for spot in spots)
        e = e_ref[rows, g * width : (g + 1) * width]
        grads = attention_backward_group(
            q, k, v, e, go_ref[rows, at], o_ref[rows, at], rl_ref[rows, at], head_size
        )
        for spot, grad in zip(spots, grads):
            if len(gqkv_ref.shape) == 3:
                block, start = divmod(spot.start, gqkv_ref.shape[2])
                gqkv_ref[block, rows, start : start + 128] = grad
            else:
                gqkv_ref[rows, spot] = grad


def feed_forward(c_ref, up_ref, bup_ref, u_ref, slope_ref, tile, ut_ref=None):
    for t in range(up_ref.shape[1] // tile):
        at = slice(t * tile, (t + 1) * tile)
        f = mm(c_ref[...], up_ref[:, at]) + bup_ref[at].reshape(1, tile)
        u, slope = gelu_both(f)
        u = u.astype(BF16)
        here = t if len(u_ref.shape) == 3 else (slice(None), at)
        u_ref[here] = u
        slope_ref[:, at] = slope.astype(BF16)
        if ut_ref is not None:
            ut_ref[at, :] = jnp.transpose(u)


def feed_forward_back(gm_ref, down_ref, slope_ref, gf_ref, gbup_ref, tile):
    for t in range(down_ref.shape[0] // tile):
        at = slice(t * tile, (t + 1) * tile)
        gu = mm_nt(gm_ref[...], down_ref[at, :])
        gf = (gu * slope_ref[:, at].astype(F32)).astype(BF16)
        gf_ref[t if len(gf_ref.shape) == 3 else (slice(None), at)] = gf
        gbup_ref[:, at] += rows_sum(gf.astype(F32))


def joined(ref):
    return jnp.concatenate([ref[b] for b in range(ref.shape[0])], axis=1)


def row(ref):
    return ref[...].reshape(1, -1)


def segment_mask(seg_ref, section):
    seg = seg_ref[pl.ds(section, 1), :].astype(F32)
    rows = seg.shape[1]
    column = jnp.transpose(jnp.broadcast_to(seg, (128, rows)))
    return jnp.concatenate([column] * (rows // 128), axis=1) == seg


class Writer:
    def __init__(self, semaphores):
        self.semaphores, self.copies = semaphores, []

    def start(self, source, target):
        copy = pltpu.make_async_copy(source, target, self.semaphores.at[len(self.copies)])
        copy.start()
        self.copies.append(copy)

    def wait(self):
        for copy in self.copies:
            copy.wait()


def encoder_forward_kernel(
    x_ref, seg_ref,
    gain1, bias1, w_qkv, w_out, b_out, gain2, bias2, w_up, b_up, w_down, b_down,
    *refs,
):
    outs, scratch = refs[:12], refs[12:24]
    y_ref, at_ref, qkv_ref, e_ref, rl_ref, o_ref, ot_ref, n2_ref, s2_ref, ct_ref, ut_ref, slope_ref = scratch
    h_ref, c_ref, u_ref, qkv_v, out_v, up_v, down_v, sem, out_sem = refs[24:]
    target = {id(v): o for v, o in zip(scratch, outs)}
    writer = Writer(out_sem)

    def write(*done):
        for v in done:
            writer.start(v, target[id(v)])

    tokens, features = y_ref.shape
    pairs = ((w_qkv, qkv_v), (w_out, out_v), (w_up, up_v), (w_down, down_v))
    loads = [pltpu.make_async_copy(w, v, sem.at[i]) for i, (w, v) in enumerate(pairs)]
    for load in loads:
        load.start()
    section = lax.axis_index("section")
    x = x_ref[pl.ds(pl.multiple_of(section * tokens, tokens), tokens), :].astype(F32)
    n1, _ = normalise(x)
    a = (n1 * row(gain1) + row(bias1)).astype(BF16)
    at_ref[...] = jnp.transpose(a)
    allowed = segment_mask(seg_ref, section)
    loads[0].wait()
    qkv_ref[...] = mm(a, qkv_v[...]).astype(BF16)
    write(at_ref, qkv_ref)
    attention_forward(
        qkv_ref, o_ref, e_ref, rl_ref, slice(None), tokens, features, features // H_ENC, allowed
    )
    ot_ref[...] = jnp.transpose(o_ref[...])
    write(e_ref, rl_ref, o_ref, ot_ref)
    loads[1].wait()
    h_ref[...] = x + (mm(o_ref[...], out_v[...]) + row(b_out))
    n2, s2 = normalise(h_ref[...])
    n2_ref[...] = n2
    s2_ref[...] = s2
    c_ref[...] = (n2 * row(gain2) + row(bias2)).astype(BF16)
    ct_ref[...] = jnp.transpose(c_ref[...])
    write(n2_ref, s2_ref, ct_ref)
    loads[2].wait()
    feed_forward(c_ref, up_v, b_up, u_ref, slope_ref, 512, ut_ref)
    write(ut_ref, slope_ref)
    loads[3].wait()
    y_ref[...] = (h_ref[...] + (mm(u_ref[...], down_v[...]) + row(b_down))).astype(BF16)
    write(y_ref)
    writer.wait()


def encoder_backward_kernel(
    x_ref, gy_ref, qkv_ref, e_ref, rl_ref, o_ref, n2_ref, s2_ref, slope_ref,
    gain1, w_qkv, w_out, gain2, w_up, w_down,
    gx_ref, gf_ref, ga_ref, gqkv_ref, small_ref, gbup_ref,
    gh_ref, go_ref,
):
    tokens, features = gy_ref.shape
    section = lax.axis_index("section")
    x = x_ref[pl.ds(pl.multiple_of(section * tokens, tokens), tokens), :].astype(F32)
    gbup_ref[...] = jnp.zeros_like(gbup_ref)
    feed_forward_back(gy_ref, w_down, slope_ref, gf_ref, gbup_ref, 512)
    gc = mm_nt(gf_ref[...], w_up[...])
    g = gy_ref[...].astype(F32)
    n2 = n2_ref[...]
    gh = g + normalise_back(gc, n2, s2_ref[...], row(gain2))
    gh_ref[...] = gh
    ga_ref[...] = gh.astype(BF16)
    small_ref[2:3, :] = rows_sum(gh)
    small_ref[3:4, :] = rows_sum(gc * n2)
    small_ref[4:5, :] = rows_sum(gc)
    small_ref[5:6, :] = rows_sum(g)
    go_ref[...] = mm_nt(ga_ref[...], w_out[...]).astype(BF16)
    attention_backward(
        qkv_ref, go_ref, o_ref, e_ref, rl_ref, gqkv_ref, slice(None), tokens, features,
        features // H_ENC,
    )
    gn = mm_nt(gqkv_ref[...], w_qkv[...])
    n1, s1 = normalise(x)
    small_ref[0:1, :] = rows_sum(gn * n1)
    small_ref[1:2, :] = rows_sum(gn)
    gx_ref[...] = (gh_ref[...] + normalise_back(gn, n1, s1, row(gain1))).astype(BF16)


def split_low(x):
    high = x.astype(BF16)
    return high, (x - high.astype(F32)).astype(BF16)


def place_slots(order_ref, seg, section, hot_ref, place_ref, empty_ref):
    packed = seg.shape[1]
    sample = lax.broadcasted_iota(jnp.int32, (16, packed), 0).astype(F32)
    starts = jnp.sum(jnp.where(seg < sample, 1.0, 0.0), axis=1, keepdims=True)
    counts = jnp.sum(jnp.where(seg == sample, 1.0, 0.0), axis=1, keepdims=True)
    line = lax.broadcasted_iota(jnp.int32, (PATCHES, PATCHES), 0).astype(F32)
    line_low = line.astype(BF16)
    lane_low = lax.broadcasted_iota(jnp.int32, (8, PATCHES), 1).astype(F32).astype(BF16)
    column = lax.broadcasted_iota(jnp.int32, (PATCHES, packed), 1).astype(F32)
    packed_line = lax.broadcasted_iota(jnp.int32, (packed, PATCHES), 0).astype(F32)
    for j in range(SAMP_MB):
        at = slice(j * PATCHES, (j + 1) * PATCHES)
        order = order_ref[pl.ds(section * SAMP_MB + j, 1), :].astype(F32)
        hit = jnp.where(order == line, 1.0, 0.0).astype(BF16)
        start, count = starts[j : j + 1, :], counts[j : j + 1, :]
        down, across = mm(hit, line_low), mm_nt(lane_low, hit)[:1, :]
        down = jnp.where(down < count, start + down, -1.0)
        across = jnp.where(across < count, start + across, -1.0)
        wide = jnp.concatenate([down] * (packed // PATCHES), axis=1)
        hot_ref[at, :] = jnp.where(column == wide, 1.0, 0.0).astype(BF16)
        place_ref[:, at] = jnp.where(packed_line == across, 1.0, 0.0).astype(BF16)
        empty_ref[at, :] = jnp.where(down < 0.0, 1.0, 0.0)


def decoder_kernel(
    y_ref, seg_ref, order_ref, pos_ref, g_hbm,
    w_embed_hbm, b_embed, mask_token,
    gain1, bias1, w_qkv_hbm, w_out_hbm, b_out, gain2, bias2, w_up_hbm, b_up, w_down_hbm, b_down,
    *refs,
):
    hbm, (geb_ref, gy_ref, small_ref, gbup_ref) = refs[:9], refs[9:13]
    buffers = refs[13:22]
    out_ref, at_ref, ot_ref, ct_ref, gt_ref, u_ref, gf_ref, ga_ref, gqkv_ref = buffers
    (
        e2_ref, z_ref, s1_ref, e_ref, rl_ref, h_ref, s2_ref, go_ref, ge_ref, o_ref, c_ref, qkv_ref,
        slope_ref, g_all, hot_ref, place_ref, empty_ref, w_embed, w_qkv, w_out, w_up, w_down,
        w_sem, out_sem,
    ) = refs[22:]
    packed = y_ref.shape[0]
    rows, features = z_ref.shape
    samples = rows // PATCHES
    head_size = features // H_DEC
    total = g_all.shape[0]
    section = lax.axis_index("section")
    mine = pl.ds(pl.multiple_of(section * total, total), total)
    pairs = (
        (w_embed_hbm, w_embed), (w_qkv_hbm, w_qkv), (w_out_hbm, w_out), (w_up_hbm, w_up),
        (w_down_hbm, w_down), (g_hbm.at[mine, :], g_all),
    )
    loads = [pltpu.make_async_copy(a, b, w_sem.at[i]) for i, (a, b) in enumerate(pairs)]
    for load in loads:
        load.start()

    def write(at, *which):
        copies = []
        for i in which:
            if i > 4:
                for b in range(buffers[i].shape[0]):
                    source, target = buffers[i].at[b], hbm[i].at[b, at, :]
                    copies.append(pltpu.make_async_copy(source, target, out_sem.at[i, b]))
                    copies[-1].start()
                continue
            target = hbm[i].at[:, at] if i else hbm[i].at[at, :]
            copies.append(pltpu.make_async_copy(buffers[i], target, out_sem.at[i, 0]))
            copies[-1].start()
        return copies

    small_ref[...] = jnp.zeros_like(small_ref)
    gbup_ref[...] = jnp.zeros_like(gbup_ref)
    ge_ref[...] = jnp.zeros_like(ge_ref)
    seg = seg_ref[pl.ds(section, 1), :].astype(F32)
    place_slots(order_ref, seg, section, hot_ref, place_ref, empty_ref)
    loads[0].wait()
    high, low = split_low(mm(y_ref[...], w_embed[...]) + row(b_embed))
    e2_ref[:packed, :] = high
    e2_ref[packed:, :] = low
    for load in loads[1:]:
        load.wait()

    def one_step(step, carry):
        here = pl.ds(pl.multiple_of(step * rows, rows), rows)
        one_hot = hot_ref[here, :]
        empty = jnp.concatenate([empty_ref[here, :]] * (features // 128), axis=1)
        twice = jnp.concatenate([one_hot, one_hot], axis=1)
        z = mm(twice, e2_ref[...]) + empty * row(mask_token)
        z = z + jnp.concatenate([pos_ref[...]] * samples, axis=0)
        n1, s1 = normalise(z)
        z_ref[...] = z
        s1_ref[...] = s1
        a = (n1 * row(gain1) + row(bias1)).astype(BF16)
        at_ref[...] = jnp.transpose(a)
        writing = write(here, 1)
        qkv_ref[...] = mm(a, w_qkv[...]).astype(BF16)

        def forward(b, carry):
            at = pl.ds(pl.multiple_of(b * PATCHES, PATCHES), PATCHES)
            attention_forward(qkv_ref, o_ref, e_ref, rl_ref, at, PATCHES, features, head_size, None)
            return carry

        lax.fori_loop(0, samples, forward, 0, unroll=2)
        ot_ref[...] = jnp.transpose(o_ref[...])
        h_ref[...] = z_ref[...] + (mm(o_ref[...], w_out[...]) + row(b_out))
        n2, s2 = normalise(h_ref[...])
        s2_ref[...] = s2
        c_ref[...] = (n2 * row(gain2) + row(bias2)).astype(BF16)
        ct_ref[...] = jnp.transpose(c_ref[...])
        feed_forward(c_ref, w_up, b_up, u_ref, slope_ref, 512)
        writing += write(here, 2, 3, 5)
        out_ref[...] = (h_ref[...] + (mm(joined(u_ref), w_down[...]) + row(b_down))).astype(BF16)

        g_ref = g_all.at[here, :]
        gt_ref[...] = jnp.transpose(g_ref[...])
        feed_forward_back(g_ref, w_down, slope_ref, gf_ref, gbup_ref, 512)
        writing += write(here, 0, 4, 6)
        gc = mm_nt(joined(gf_ref), w_up[...])
        g = g_ref[...].astype(F32)
        h = h_ref[...]
        n2 = (h - jnp.mean(h, axis=-1, keepdims=True)) * s2_ref[...]
        gh = g + normalise_back(gc, n2, s2_ref[...], row(gain2))
        small_ref[2:3, :] += rows_sum(gh)
        small_ref[3:4, :] += rows_sum(gc * n2)
        small_ref[4:5, :] += rows_sum(gc)
        small_ref[5:6, :] += rows_sum(g)
        h_ref[...] = gh
        ga = gh.astype(BF16)
        for b in range(2):
            ga_ref[b] = ga[:, b * features // 2 : (b + 1) * features // 2]
        go_ref[...] = mm_nt(ga, w_out[...]).astype(BF16)
        writing += write(here, 7)

        def backward(b, carry):
            at = pl.ds(pl.multiple_of(b * PATCHES, PATCHES), PATCHES)
            attention_backward(
                qkv_ref, go_ref, o_ref, e_ref, rl_ref, gqkv_ref, at, PATCHES, features, head_size
            )
            return carry

        lax.fori_loop(0, samples, backward, 0, unroll=2)
        writing += write(here, 8)
        gn = mm_nt(joined(gqkv_ref), w_qkv[...])
        z = z_ref[...]
        n1 = (z - jnp.mean(z, axis=-1, keepdims=True)) * s1_ref[...]
        gz = h_ref[...] + normalise_back(gn, n1, s1_ref[...], row(gain1))
        small_ref[0:1, :] += rows_sum(gn * n1)
        small_ref[1:2, :] += rows_sum(gn)
        small_ref[6:7, :] += rows_sum(gz * empty)
        ge_ref[...] += mm(place_ref[:, here], gz.astype(BF16))
        for copy in writing:
            copy.wait()
        return carry

    lax.fori_loop(0, total // rows, one_step, 0)
    ge = ge_ref[...]
    small_ref[7:8, :] = rows_sum(ge)
    geb_ref[...] = ge.astype(BF16)
    gy_ref[...] = mm_nt(geb_ref[...], w_embed[...]).astype(BF16)


def in_vmem(count):
    return [pl.BlockSpec(memory_space=pltpu.VMEM)] * count


def in_hbm():
    return pl.BlockSpec(memory_space=pl.ANY)


def shape(rows, columns, dtype=BF16):
    return jax.ShapeDtypeStruct((rows, columns), dtype)


KERNEL_VMEM = 60 * 2**20


def encoder_forward(x, segments, params):
    rows, d = x.shape[0] // 2, x.shape[1]
    ff = params[7].shape[1]
    outs = [
        (rows, d, BF16),
        (d, rows, BF16),
        (rows, 3 * d, BF16),
        (rows, H_ENC * rows, BF16),
        (rows, d, F32),
        (rows, d, BF16),
        (d, rows, BF16),
        (rows, d, F32),
        (rows, 1, F32),
        (d, rows, BF16),
        (ff, rows, BF16),
        (rows, ff, BF16),
    ]
    more = [(rows, d, F32), (rows, d, BF16), (rows, ff, BF16)]
    args = [x, segments, *params]
    matrices = [w for w in params if w.dtype == BF16]
    return pl.pallas_call(
        encoder_forward_kernel,
        out_shape=[shape(*o) for o in outs],
        in_specs=in_vmem(2) + [in_hbm() if w.dtype == BF16 else in_vmem(1)[0] for w in params],
        out_specs=[in_hbm()] * len(outs),
        scratch_shapes=[pltpu.VMEM((r, w), t) for r, w, t in outs + more]
        + [pltpu.VMEM(w.shape, BF16) for w in matrices]
        + [pltpu.SemaphoreType.DMA((len(matrices),)), pltpu.SemaphoreType.DMA((len(outs),))],
        compiler_params=pltpu.CompilerParams(vmem_limit_bytes=KERNEL_VMEM),
        name="encoder_forward",
    )(*args)


def encoder_backward(x, gy, saved, params):
    gain1, _, w_qkv, w_out, _, gain2, _, w_up, _, w_down, _ = params
    rows, d = gy.shape
    ff = w_up.shape[1]
    outs = [
        shape(rows, d),
        shape(rows, ff),
        shape(rows, d),
        shape(rows, 3 * d),
        shape(8, d, F32),
        shape(1, ff, F32),
    ]
    args = [x, gy, *saved, gain1, w_qkv, w_out, gain2, w_up, w_down]
    return pl.pallas_call(
        encoder_backward_kernel,
        out_shape=outs,
        in_specs=in_vmem(len(args)),
        out_specs=in_vmem(len(outs)),
        scratch_shapes=[pltpu.VMEM((rows, d), F32), pltpu.VMEM((rows, d), BF16)],
        compiler_params=pltpu.CompilerParams(vmem_limit_bytes=KERNEL_VMEM),
        name="encoder_backward",
    )(*args)


def decoder_both(y, segments, orders, g, embed_params, params):
    packed, d_enc = y.shape
    total, d = g.shape[0] // 2, g.shape[1]
    rows = 6 * PATCHES
    ff = params[7].shape[1]
    args = [y, segments, orders, positions(PATCHES, d), g, *embed_params, *params]
    in_specs = in_vmem(4) + [in_hbm()]
    in_specs += [in_hbm() if x.dtype == BF16 else in_vmem(1)[0] for x in args[5:]]
    blocks = [(4, ff // 4), (4, ff // 4), (2, d // 2), (6, d // 2)]
    outs = [shape(total, d)] + [shape(d, total)] * 4
    outs += [jax.ShapeDtypeStruct((n, total, w), BF16) for n, w in blocks]
    buffers = [(rows, d)] + [(d, rows)] * 4 + [(n, rows, w) for n, w in blocks]
    last = [shape(packed, d), shape(packed, d_enc), shape(8, d, F32), shape(1, ff, F32)]
    scratch = [
        (2 * packed, d, BF16),
        (rows, d, F32),
        (rows, 1, F32),
        (rows, H_DEC * PATCHES, BF16),
        (rows, d, F32),
        (rows, d, F32),
        (rows, 1, F32),
        (rows, d, BF16),
        (packed, d, F32),
        (rows, d, BF16),
        (rows, d, BF16),
        (rows, 3 * d, BF16),
        (rows, ff, BF16),
        (total, d, BF16),
        (total, packed, BF16),
        (packed, total, BF16),
        (total, 128, F32),
    ]
    matrices = [x for x in args[5:] if x.dtype == BF16]
    return pl.pallas_call(
        decoder_kernel,
        out_shape=outs + last,
        in_specs=in_specs,
        out_specs=[in_hbm()] * len(outs) + in_vmem(len(last)),
        scratch_shapes=[pltpu.VMEM(b, BF16) for b in buffers]
        + [pltpu.VMEM((r, w), t) for r, w, t in scratch]
        + [pltpu.VMEM(x.shape, BF16) for x in matrices]
        + [pltpu.SemaphoreType.DMA((len(matrices) + 1,)), pltpu.SemaphoreType.DMA((len(outs), 6))],
        compiler_params=pltpu.CompilerParams(vmem_limit_bytes=KERNEL_VMEM),
        name="decoder_both",
    )(*args)


MESH = pl.DeviceIdType.MESH
ENC_QKV, ENC_OUT, ENC_UP, ENC_DOWN, EMBED, DEC_QKV, DEC_OUT, DEC_UP, DEC_DOWN = range(9)
GIVE, PAIR, FFN, GC, LN2, GO, ATT, GN, LAST = range(10, 19)
SMALL = -1
ROW_BUP, ROW_DEC_BUP, ROW_DEC, SMALL_ROWS = 6, 10, 16, 24
Z, Y, X, CORE = range(4)
ORDERS = ((X, Y, Z), (Y, X, Z), (X, Z, Y), (Y, Z, X), (Z, X, Y), (Z, Y, X))


class Chunk:
    def __init__(self, name, half, offset, rows, width, first_row=None):
        self.name, self.half, self.offset, self.rows, self.width = name, half, offset, rows, width
        self.first_row, self.turned, self.order = first_row, name == DEC_DOWN, None
        self.decoder = name in (DEC_QKV, DEC_UP, DEC_OUT)

    def columns(self, side):
        return pl.ds(pl.multiple_of(side * self.half + self.offset, 128), self.width)

    def place(self, side):
        if self.turned:
            return (pl.ds(pl.multiple_of(side * self.half + self.offset, 128), self.rows), slice(None))
        if self.first_row is None:
            return (slice(None), self.columns(side))
        return (pl.ds(self.first_row, self.rows), self.columns(side))

    @property
    def bytes(self):
        return 32 * self.rows * self.width

    def loads(self, order):
        if order[0] == Z:
            return (2 * self.bytes, self.bytes / 4, self.bytes / 8)
        if order[1] == Z:
            return (self.bytes, self.bytes, self.bytes / 8)
        return (self.bytes, self.bytes / 2, self.bytes / 2)


LINK_ORDERS = (2, 1, 2, 5, 3, 0, 3, 0, 3, 3, 0, 0, 0, 0, 1)


def make_chunks():
    chunks = [Chunk(ENC_DOWN, 384, 0, 48, 384, 48 * q) for q in range(4)]
    chunks += [Chunk(ENC_UP, 1536, 768 * q, 48, 768) for q in range(2)]
    chunks += [Chunk(ENC_OUT, 384, 0, 48, 384)]
    chunks += [Chunk(ENC_QKV, 1152, 0, 48, 768), Chunk(ENC_QKV, 1152, 768, 48, 384)]
    chunks += [Chunk(EMBED, 256, 0, 48, 256)]
    chunks += [Chunk(DEC_QKV, 768, 0, 32, 768), Chunk(DEC_DOWN, 256, 0, 256, 128)]
    chunks += [Chunk(DEC_UP, 1024, o, 32, 512) for o in (0, 512)]
    chunks += [Chunk(DEC_OUT, 256, 0, 32, 256)]
    for chunk, order in zip(chunks, LINK_ORDERS):
        chunk.order = ORDERS[order]
    return chunks


def make_groups(chunks):
    return [[c] for c in range(len(chunks))]


def product_cost(k, count):
    if k.turned:
        return 5.0
    return k.rows * k.width * (0.9 / 8192 if k.decoder else 0.6 / 18432)


def tasks_in_order(chunks, groups):
    def gives(name):
        found = [(g, chunks[m[0]], len(m)) for g, m in enumerate(groups)]
        kind = PAIR if name == DEC_DOWN else GIVE
        return [(kind, g, product_cost(k, size)) for g, k, size in found if k.name == name]

    tasks = gives(ENC_DOWN)
    tasks += [(FFN, t, 0.9) for t in range(4)] + gives(ENC_UP)
    tasks += [(GC, t, 1.1) for t in range(3)]
    tasks += [(LN2, 0, 1.0), (GO, 0, 0.9)]
    tasks += [(ATT, g, 1.5) for g in range(6)]
    tasks += gives(ENC_OUT) + gives(ENC_QKV) + gives(EMBED)
    tasks += gives(DEC_QKV) + gives(DEC_DOWN)
    tasks += [(GN, j, 0.9) for j in range(3)] + [(LAST, 0, 1.5)]
    return tasks + gives(DEC_UP) + gives(DEC_OUT)


def decoder_arrays(chunks):
    names = []
    for k in chunks:
        if (k.decoder or k.turned) and k.name not in names:
            names.append(k.name)
    return names


def make_plan(chunks, groups):
    tasks = tasks_in_order(chunks, groups)
    lhs = decoder_arrays(chunks)
    free = [0.0] * 4
    rate = [80e3, 80e3, 80e3, 500e3]
    pending, plan, now, owned = [], [], 2.0, set()

    def send(link, size, latency):
        begin = max(now, free[link])
        free[link] = begin + size / rate[link]
        return free[link] + latency

    def blocked(task):
        if task[0] not in (GIVE, PAIR):
            return False
        name = chunks[groups[task[1]][0]].name
        if name not in lhs[2:]:
            return False
        name = lhs[lhs.index(name) - 2]
        return any(chunks[m[0]].name == name and g not in owned for g, m in enumerate(groups))

    while tasks or pending:
        pending.sort()
        if pending and (pending[0][0] <= now or not tasks or blocked(tasks[0])):
            arrive, stage, c = pending.pop(0)
            now = max(now, arrive)
            plan.append((stage, c))
            if c == SMALL:
                now += 0.1
                if stage < 4:
                    pending.append((now + 2.0, stage + 1, c))
                continue
            members = groups[c] if stage == 1 else [c]
            k = chunks[members[0]]
            if stage == 1:
                owned.add(c)
                now += 0.6 if k.turned else product_cost(k, len(members)) + 0.2 * len(members)
            else:
                now += 0.25
            for c in members:
                k = chunks[c]
                if stage < 4:
                    axis = k.order[stage - 1]
                    latency = 3.5 if axis == Z else 3.0
                    arrive = send(axis, k.loads(k.order)[stage - 1], latency)
                    pending.append((arrive, stage + 1, c))
                elif stage == 4:
                    pending.append((send(CORE, k.bytes / 16, 1.8), 5, c))
            continue
        name, arg, cost = tasks.pop(0)
        plan.append((name, arg))
        now += cost
        if name in (GIVE, PAIR):
            arrive = [send(CORE, chunks[c].bytes, 1.8) for c in groups[arg]]
            pending.append((max(arrive), 1, arg))
        elif name == LAST:
            pending.append((now + 2.0, 1, SMALL))
    return plan


class Ring:
    def __init__(self, sources, slots, semaphores, depth):
        self.copies = [
            pltpu.make_async_copy(source, slot, semaphores())
            for source, slot in zip(sources, slots)
        ]
        self.slots, self.depth, self.at = slots, depth, 0

    def begin(self):
        for copy in self.copies[: self.depth]:
            copy.start()

    def take(self):
        self.copies[self.at].wait()
        return self.slots[self.at]

    def done(self):
        ahead = self.at + self.depth
        if ahead < len(self.copies):
            self.copies[ahead].start()
        self.at += 1


class Names:
    def __init__(self, names, refs):
        self.__dict__.update(zip(names, refs))


LOADS = 96


def finish_kernel(chunks, groups, plan, r):
    n = len(chunks)
    s = lax.axis_index("section")
    d = lax.axis_index("dp")
    here = (d // 4, (d // 2) % 2, d % 2)
    z, y, x = here
    sibling = {"section": 1 - s}
    z_at = [lax.rem(z + k, 4) for k in (1, 2, 3)]
    peers = {
        X: [(1 - x, {"dp": d + 1 - 2 * x})],
        Y: [(1 - y, {"dp": d + 2 - 4 * y})],
        Z: [(p, {"dp": d + 4 * (p - z)}) for p in z_at],
    }
    every = [sibling] + [peer for axis in (X, Y, Z) for _, peer in peers[axis]]

    barrier = pltpu.get_barrier_semaphore()
    for peer in every:
        pl.semaphore_signal(barrier, inc=1, device_id=peer, device_id_type=MESH)

    counter = iter(range(LOADS))

    def semaphore():
        return r.load_sem.at[next(counter)]

    def remote(src, dst, send, recv, peer):
        return pltpu.make_async_remote_copy(
            src_ref=src, dst_ref=dst, send_sem=send, recv_sem=recv, device_id=peer, device_id_type=MESH
        )

    rhs_of = {DEC_QKV: r.gqkv2, DEC_UP: r.gf2, DEC_OUT: r.ga2}
    lhs_of = {DEC_QKV: r.at2, DEC_UP: r.ct2, DEC_OUT: r.ot2, DEC_DOWN: r.gt2}
    tiles, last_use = [], {}

    def wide_columns(g, side):
        k, width = chunks[groups[g][0]], sum(chunks[c].width for c in groups[g])
        return pl.ds(pl.multiple_of(side * k.half + k.offset, 128), width)

    for i, (name, arg) in enumerate(plan):
        if name == PAIR:
            tiles += [(DEC_UP, r.u2.at[t]) for t in range(4)]
            last_use[DEC_DOWN] = i
        elif name in (GIVE, 1) and arg != SMALL and chunks[groups[arg][0]].decoder:
            k = chunks[groups[arg][0]]
            side = 1 - s if name == GIVE else s
            size = rhs_of[k.name].shape[2]
            block = side * (k.half // size) + k.offset // size
            for b in range(k.width // size):
                tiles.append((k.name, rhs_of[k.name].at[block + b]))
            last_use[k.name] = i
    lhs_names = decoder_arrays(chunks)
    assert sorted(lhs_names, key=last_use.get) == lhs_names
    rhs = {}
    for names, slots in (((DEC_QKV, DEC_OUT), r.rhs_narrow), ((DEC_UP,), r.rhs_up)):
        sources = [source for k, source in tiles if k in names]
        places = [slots.at[i % 2] for i in range(len(sources))]
        ring = Ring(sources, places, semaphore, 2)
        rhs.update({name: ring for name in names})
    rhs[DEC_DOWN] = rhs[DEC_UP]
    lhs = Ring([lhs_of[k] for k in lhs_names], [r.lhs.at[i % 2] for i in range(4)], semaphore, 2)
    tokens, d_enc = r.gy.shape
    def by_rows(source, size, slots):
        count, depth = source.shape[0] // size, slots.shape[0]
        return [source.at[pl.ds(t * size, size), :] for t in range(count)], [
            slots.at[t % depth] for t in range(count)
        ]

    down_blocks, down_slots = by_rows(r.w_down, d_enc, r.w)
    down_blocks.append(r.w_out)
    down_slots.append(r.w.at[len(down_slots) % 2])
    w_down = Ring(down_blocks, down_slots, semaphore, 2)
    up_blocks, up_slots = by_rows(r.w_up, 256, r.w_up_v)
    qkv_blocks = by_rows(r.w_qkv, 256, r.w_up_v)[0]
    qkv_slots = [r.w_up_v.at[(3 + t) % 2, :, : 3 * d_enc] for t in range(3)]
    w_rows = Ring(up_blocks + qkv_blocks, up_slots + qkv_slots, semaphore, 2)
    e_width = 2 * tokens
    e_ring = Ring(
        [r.e.at[:, pl.ds(g * e_width, e_width)] for g in range(6)],
        [r.e_v.at[g % 2] for g in range(6)],
        semaphore,
        2,
    )

    def load(source, target):
        return pltpu.make_async_copy(source, target, semaphore())

    mine = pl.ds(pl.multiple_of(s * tokens, tokens), tokens)
    load_gy, load_slope, load_ut = load(r.gy, r.gy_v), load(r.slope, r.slope_v), load(r.ut, r.ut_v)
    load_ct, load_at, load_ot = load(r.ct, r.ct_v), load(r.at, r.at_v), load(r.ot, r.ot_v)
    load_n2, load_s2, load_qkv = load(r.n2, r.n2_v), load(r.s2, r.s2_v), load(r.qkv, r.qkv_v)
    load_o, load_rl, load_x = load(r.o, r.o_v), load(r.rl, r.rl_v), load(r.x.at[mine, :], r.go_v)
    load_y, load_geb = load(r.y, r.y_v), load(r.geb, r.geb_v)
    load_gy.start()
    load_ut.start()
    load_slope.start()
    w_down.begin()
    w_rows.begin()
    begun = [
        (load_ct, load_n2, load_s2),
        (load_qkv, load_o, load_rl, e_ring),
        (load_ot, load_at, load_y, load_geb),
        (lhs, rhs[DEC_QKV], rhs[DEC_UP]),
    ]

    def begin_some():
        for copy in begun.pop(0) if begun else ():
            copy.begin() if isinstance(copy, Ring) else copy.start()

    half = r.decoded.shape[1] // 2
    give_half = r.decoded.at[:, pl.ds(pl.multiple_of((1 - s) * half, half), half), :]
    decoded_away = remote(give_half, r.decoded_got, r.swap_sem.at[0], r.swap_sem.at[1], sibling)
    gx_columns = d_enc // 2
    gx_half = r.gx.at[:, pl.ds(pl.multiple_of((1 - s) * gx_columns, 128), gx_columns)]
    gx_away = remote(gx_half, r.gx_got, r.swap_sem.at[2], r.swap_sem.at[3], sibling)

    small = r.small
    small[...] = jnp.zeros_like(small)
    small[ROW_DEC : ROW_DEC + 8, : r.small2.shape[1]] = r.small2[...]
    quarter = r.gbup2.shape[1] // 4
    for i in range(4):
        piece = r.gbup2[:, i * quarter : (i + 1) * quarter]
        small[ROW_DEC_BUP + i : ROW_DEC_BUP + i + 1, :quarter] = piece

    pl.semaphore_wait(barrier, len(every))

    copies = {}
    first_slot = (0, 1, 4, 7, 10)

    def chunk_copy(c, slot, src, dst, peer):
        copy = remote(src, dst, r.send_sem.at[c, slot], r.recv_sem.at[c, slot], peer)
        copy.start()
        copies[c, slot] = copy

    sent = set()

    def sent_by(c, slot):
        if (c, slot) not in sent:
            sent.add((c, slot))
            copies[c, slot].wait_send()

    staged = {}

    def staging(c):
        k = chunks[c]
        buffers = r.stage[k.rows, k.width]
        turn = staged.setdefault((k.rows, k.width), [])
        if len(turn) >= len(buffers):
            sent_by(turn[-len(buffers)], 0)
        turn.append(c)
        return buffers[(len(turn) - 1) % len(buffers)]

    def shard(i):
        return (i // 4, (i // 2) % 2, i % 2)

    waited = set()

    def arrived(copy):
        if id(copy) not in waited:
            waited.add(id(copy))
            copy.wait()

    def product(g, side):
        k, columns = chunks[groups[g][0]], wide_columns(g, side)
        if k.decoder:
            left, ring, parts = lhs.slots[lhs_names.index(k.name)], rhs[k.name], []
            for _ in range(k.width // rhs_of[k.name].shape[2]):
                parts.append(mm(left[...], ring.take()[...]))
                ring.done()
            return jnp.concatenate(parts, axis=1)
        if k.name == EMBED:
            arrived(load_y)
            arrived(load_geb)
            return mm_tn(r.y_v[...], r.geb_v[:, columns])
        if k.name == ENC_DOWN:
            arrived(load_ut)
            arrived(load_gy)
            at = [i * 192 + k.first_row for i in range(16)]
            left = jnp.concatenate([r.ut_v[i : i + k.rows, :] for i in at], axis=0)
            return mm(left, r.gy_v[:, columns])
        if k.name == ENC_UP:
            arrived(load_ct)
            return mm(r.ct_v[...], r.slope_v[:, columns])
        if k.name == ENC_OUT:
            arrived(load_ot)
            return mm(r.ot_v[...], r.ga_v[:, columns])
        arrived(load_at)
        return mm(r.at_v[...], r.qkv_v[:, columns])

    def after_product(i, g):
        k = chunks[groups[g][0]]
        if k.decoder:
            if last_use[k.name] == i:
                lhs.done()

    def wait_lhs(k):
        if k.name in lhs_names:
            arrived(lhs.copies[lhs_names.index(k.name)])

    def give(i, g):
        members = groups[g]
        wait_lhs(chunks[members[0]])
        buffers = [staging(c) for c in members]
        value = product(g, 1 - s).astype(BF16)
        for m, (c, buffer) in enumerate(zip(members, buffers)):
            k = chunks[c]
            part = value[:, m * k.width : (m + 1) * k.width]
            for j in range(16):
                buffer[shard(j)] = part[j * k.rows : (j + 1) * k.rows]
            chunk_copy(c, 0, buffer, r.acc[c], sibling)
        after_product(i, g)
        begin_some()

    def pair(i, g):
        both = groups[g]
        wait_lhs(chunks[both[0]])
        left = lhs.slots[lhs_names.index(DEC_DOWN)]
        side_rows = chunks[both[0]].half
        buffers = [staging(c) for c in both]
        for t in range(4):
            tile = rhs[DEC_DOWN].take()
            for side, targets in ((1 - s, buffers), (s, [r.acc[c] for c in both])):
                at = pl.ds(pl.multiple_of(side * side_rows, side_rows), side_rows)
                value = mm(left[at, :], tile[...]).astype(BF16)
                for c, target in zip(both, targets):
                    k = chunks[c]
                    rows = slice(k.offset, k.offset + k.rows)
                    for j in range(4):
                        target[shard(4 * t + j)] = value[rows, j * k.width : (j + 1) * k.width]
            rhs[DEC_DOWN].done()
        lhs.done()
        for c, buffer in zip(both, buffers):
            chunk_copy(c, 0, buffer, r.got[c], sibling)

    def spots(k, stage):
        fixed = {axis: here[axis] for axis in k.order[: stage - 1]}
        return [fixed.get(axis, slice(None)) for axis in (Z, Y, X)]

    def send_stage(c, stage):
        k = chunks[c]
        axis = k.order[stage - 1]
        for j, (coordinate, peer) in enumerate(peers[axis]):
            at = spots(k, stage)
            at[axis] = coordinate
            src = r.acc[c].at[tuple(at)]
            chunk_copy(c, first_slot[stage] + j, src, r.recv[stage - 1][c].at[j], peer)

    def got_stage(c, stage):
        k = chunks[c]
        count = len(peers[k.order[stage - 1]])
        for j in range(count):
            copies[c, first_slot[stage] + j].wait_recv()
        return count

    def add_stage(c, stage):
        k, acc, got = chunks[c], r.acc[c], r.recv[stage - 1][c]
        count = got_stage(c, stage)
        left = [axis for axis in (Z, Y, X) if axis not in k.order[:stage]]
        sizes = [(4, 2, 2)[axis] for axis in left]
        for j in range(math.prod(sizes)):
            place, rest = {}, j
            for axis, size in reversed(list(zip(left, sizes))):
                place[axis] = rest % size
                rest //= size
            at = tuple(place.get(axis, here[axis]) for axis in (Z, Y, X))
            index = tuple(place[axis] for axis in left)
            if count == 1:
                acc[at] = acc[at] + got[(0,) + index]
            else:
                total = acc[at].astype(F32)
                for m in range(count):
                    total = total + got[(m,) + index].astype(F32)
                acc[at] = total.astype(BF16)

    def stage1(i, g):
        members = groups[g]
        for c in members:
            copies[c, 0].wait_recv()
        if chunks[members[0]].turned:
            for c in members:
                acc = r.acc[c]
                for j in range(16):
                    acc[shard(j)] = acc[shard(j)] + r.got[c][shard(j)]
                send_stage(c, 1)
            return
        value = product(g, s)
        for m, c in enumerate(members):
            k, acc = chunks[c], r.acc[c]
            wide = value[:, m * k.width : (m + 1) * k.width]
            for j in range(16):
                part = wide[j * k.rows : (j + 1) * k.rows]
                acc[shard(j)] = (part + acc[shard(j)].astype(F32)).astype(BF16)
            send_stage(c, 1)
        after_product(i, g)

    def stage2(i, c):
        add_stage(c, 1)
        send_stage(c, 2)

    def stage3(i, c):
        add_stage(c, 2)
        send_stage(c, 3)

    def stage4(i, c):
        k = chunks[c]
        total = r.acc[c][here].astype(F32)
        for j in range(got_stage(c, 3)):
            total = total + r.recv[2][c][j].astype(F32)
        out = r.out[k.name]
        out[k.place(s)] = total.astype(BF16)
        final = out.at[k.place(s)]
        chunk_copy(c, 10, final, final, sibling)

    def stage5(i, c):
        copies[c, 10].wait_recv()

    small_copies = []

    def small_copy(source, peer):
        slot = len(small_copies)
        copy = remote(
            source, r.small_got.at[slot], r.small_sem.at[0, slot], r.small_sem.at[1, slot], peer
        )
        copy.start()
        small_copies.append(copy)

    def small_stage(stage):
        if stage < 4:
            small_copies[stage - 1].wait()
            total = small[...] + r.small_got[stage - 1]
            if stage < 3:
                small[...] = total
                small_copy(small, peers[X if stage == 1 else Y][0][1])
            else:
                r.small_sum[...] = total
                for _, peer in peers[Z]:
                    small_copy(r.small_sum, peer)
        else:
            total = r.small_sum[...]
            for j in range(3):
                small_copies[3 + j].wait()
                total = total + r.small_got[3 + j]
            r.out_small[...] = total

    def ffn(i, t):
        if t == 0:
            arrived(load_gy)
            load_slope.wait()
        at = slice(t * d_enc, (t + 1) * d_enc)
        gu = mm_nt(r.gy_v[...], w_down.take()[...])
        w_down.done()
        gf = (gu * r.slope_v[:, at].astype(F32)).astype(BF16)
        r.slope_v[:, at] = gf
        small[ROW_BUP + t : ROW_BUP + t + 1, :] = rows_sum(gf.astype(F32))

    def gc_task(i, t):
        r.sum_v[:, t * 256 : (t + 1) * 256] = mm_nt(r.slope_v[...], w_rows.take()[...])
        w_rows.done()

    def ln2(i, _):
        load_n2.wait()
        load_s2.wait()
        g, gc, n2 = r.gy_v[...].astype(F32), r.sum_v[...], r.n2_v[...]
        gh = g + normalise_back(gc, n2, r.s2_v[...], row(r.gain2))
        small[2:3, :] = rows_sum(gh)
        small[3:4, :] = rows_sum(gc * n2)
        small[4:5, :] = rows_sum(gc)
        small[5:6, :] = rows_sum(g)
        r.n2_v[...] = gh
        r.ga_v[...] = gh.astype(BF16)

    def go(i, _):
        r.go_v[...] = mm_nt(r.ga_v[...], w_down.take()[...]).astype(BF16)
        w_down.done()

    def att(i, g):
        if g == 0:
            for copy in (load_qkv, load_o, load_rl):
                copy.wait()
        at = slice(g * 128, (g + 1) * 128)
        parts = [slice(j * d_enc + g * 128, j * d_enc + (g + 1) * 128) for j in range(3)]
        q, k, v = (r.qkv_v[:, part] for part in parts)
        grads = attention_backward_group(
            q, k, v, e_ring.take()[...], r.go_v[:, at], r.o_v[:, at], r.rl_v[:, at],
            d_enc // H_ENC,
        )
        e_ring.done()
        for part, grad in zip(parts, grads):
            r.qkv_v[:, part] = grad

    def gn(i, j):
        if j == 0:
            load_x.start()
        r.sum_v[:, j * 256 : (j + 1) * 256] = mm_nt(r.qkv_v[...], w_rows.take()[...])
        w_rows.done()

    def last(i, _):
        load_x.wait()
        n1, s1 = normalise(r.go_v[...].astype(F32))
        total = r.sum_v[...]
        small[0:1, :] = rows_sum(total * n1)
        small[1:2, :] = rows_sum(total)
        small_copy(small, sibling)
        gx = r.n2_v[...] + normalise_back(total, n1, s1, row(r.gain1))
        r.gx[...] = gx.astype(BF16)
        gx_away.start()
        decoded_away.start()

    run = {
        GIVE: give, PAIR: pair, FFN: ffn, GC: gc_task, LN2: ln2, GO: go, ATT: att, GN: gn, LAST: last,
        1: stage1, 2: stage2, 3: stage3, 4: stage4, 5: stage5,
    }
    for i, (name, arg) in enumerate(plan):
        if arg == SMALL:
            small_stage(name)
        else:
            run[name](i, arg)

    for c, slot in copies:
        sent_by(c, slot)
    gx_away.wait()
    decoded_away.wait()


def finish_buffers(chunks, rows, d, ff, dec_total, dec):
    def of(dtype, *dims):
        return (dims, dtype)

    return dict(
        y_v=of(BF16, rows, d),
        geb_v=of(BF16, rows, dec),
        gy_v=of(BF16, rows, d),
        slope_v=of(BF16, rows, ff),
        n2_v=of(F32, rows, d),
        s2_v=of(F32, rows, 1),
        qkv_v=of(BF16, rows, 3 * d),
        o_v=of(BF16, rows, d),
        rl_v=of(F32, rows, d),
        ga_v=of(BF16, rows, d),
        go_v=of(BF16, rows, d),
        sum_v=of(F32, rows, d),
        ut_v=of(BF16, ff, rows),
        ct_v=of(BF16, d, rows),
        at_v=of(BF16, d, rows),
        ot_v=of(BF16, d, rows),
        e_v=of(BF16, 2, rows, 2 * rows),
        w=of(BF16, 2, d, d),
        w_up_v=of(BF16, 2, 256, ff),
        lhs=of(BF16, 2, dec, dec_total),
        rhs_up=of(BF16, 2, dec_total, dec),
        rhs_narrow=of(BF16, 2, dec_total, dec // 2),
        small=of(F32, SMALL_ROWS, d),
        small_sum=of(F32, SMALL_ROWS, d),
        small_got=of(F32, 6, SMALL_ROWS, d),
    )


def finish(acts):
    enc, dec = acts["enc"], acts["dec"]
    gain1, _, w_qkv, w_out, _, gain2, _, w_up, _, w_down, _ = enc["params"]
    qkv, e, rl, o, n2, s2, slope = acts["saved"]
    given = dict(
        x=acts["x"], y=acts["y"], gy=acts["gy"], geb=acts["geb"], qkv=qkv, e=e, rl=rl, o=o, n2=n2,
        s2=s2, slope=slope, at=enc["at"], ot=enc["ot"], ct=enc["ct"], ut=enc["ut"], at2=dec["at"], ot2=dec["ot"],
        ct2=dec["ct"], gt2=dec["gt"], u2=dec["u"], gf2=dec["gf"], ga2=dec["ga"],
        gqkv2=dec["gqkv"], w_qkv=w_qkv, w_out=w_out, w_up=w_up, w_down=w_down,
        decoded=acts["decoded"].reshape(SAMP_MB, PATCHES, -1),
    )
    n_hbm = len(given)
    given.update(small2=acts["small2"], gbup2=acts["gbup2"], gain1=gain1, gain2=gain2)
    rows, d = acts["gy"].shape
    ff = w_up.shape[1]
    dec_d, dec_total = dec["at"].shape
    dec_ff = dec["u"].shape[0] * dec["u"].shape[2]
    chunks = make_chunks()
    n = len(chunks)
    groups = make_groups(chunks)
    plan = make_plan(chunks, groups)

    dims = {
        ENC_QKV: (d, 3 * d), ENC_OUT: (d, d), ENC_UP: (d, ff), ENC_DOWN: (ff, d),
        EMBED: (d, dec_d), DEC_QKV: (dec_d, 3 * dec_d), DEC_OUT: (dec_d, dec_d),
        DEC_UP: (dec_d, dec_ff), DEC_DOWN: (dec_ff, dec_d),
    }
    big = [
        shape(dims[k][1], dims[k][0] // 16) if k == DEC_DOWN else shape(dims[k][0] // 16, dims[k][1])
        for k in range(9)
    ]
    outs = dict(
        out_small=shape(SMALL_ROWS, d, F32),
        decoded_got=jax.ShapeDtypeStruct((SAMP_MB, PATCHES // 2, dec_d), BF16),
        gx=shape(rows, d),
        gx_got=shape(rows, d // 2),
    )
    single = finish_buffers(chunks, rows, d, ff, dec_total, dec_d)
    left = (4, 2, 2)
    lists = [[], [], [], [], []]
    for k in chunks:
        block = (k.rows, k.width)
        lists[0].append((left + block, BF16))
        if k.turned:
            lists[1].append((left + block, BF16))
        for stage in range(3):
            rest = [left[axis] for axis in (Z, Y, X) if axis not in k.order[: stage + 1]]
            count = 3 if k.order[stage] == Z else 1
            lists[2 + stage].append(((count, *rest, *block), BF16))
    blocks = sorted({(k.rows, k.width) for k in chunks})
    slots = [1] * len(blocks)
    lists.append([(left + block, BF16) for block, m in zip(blocks, slots) for _ in range(m)])
    semaphores = dict(
        load_sem=(LOADS,), send_sem=(n, 11), recv_sem=(n, 11), small_sem=(2, 6), swap_sem=(4,)
    )

    def kernel(*refs):
        refs = list(refs)

        def take(count):
            taken = refs[:count]
            del refs[:count]
            return taken

        names = list(given) + list(outs)
        r = Names(names, take(len(names)))
        r.out = take(9)
        r.__dict__.update(zip(single, take(len(single))))
        r.acc = take(n)
        r.got = dict(zip([c for c, k in enumerate(chunks) if k.turned], take(len(lists[1]))))
        r.recv = [take(n) for _ in range(3)]
        r.stage = {block: take(m) for block, m in zip(blocks, slots)}
        r.__dict__.update(zip(semaphores, take(len(semaphores))))
        finish_kernel(chunks, groups, plan, r)

    flat = list(single.values()) + [b for group in lists for b in group]
    results = pl.pallas_call(
        kernel,
        out_shape=list(outs.values()) + big,
        in_specs=[in_hbm()] * n_hbm + in_vmem(len(given) - n_hbm),
        out_specs=in_vmem(len(outs) + 9),
        scratch_shapes=[pltpu.VMEM(*b) for b in flat]
        + [pltpu.SemaphoreType.DMA(v) for v in semaphores.values()],
        compiler_params=pltpu.CompilerParams(
            collective_id=1, has_side_effects=True, vmem_limit_bytes=FINISH_VMEM
        ),
        name="finish",
    )(*given.values())
    return write_outputs(results, given["decoded"], dims)


FINISH_VMEM = 62 * 2**20


def write_kernel(small, decoded_got, gx_own, gx_got, *refs):
    big, decoded_own = refs[:9], refs[9]
    decoded, gx, *totals = refs[10:]
    s = lax.axis_index("section")
    half = decoded.shape[1]
    samples, rows, columns = decoded_own.shape[0], gx_own.shape[0], gx.shape[1]
    own = decoded_own[:, pl.ds(pl.multiple_of(s * half, half), half), :]
    for side, part in ((s, own), (1 - s, decoded_got[...])):
        decoded[pl.ds(side * samples, samples)] = part
    own = gx_own[:, pl.ds(pl.multiple_of(s * columns, 128), columns)]
    for side, part in ((s, own), (1 - s, gx_got[...])):
        gx[pl.ds(pl.multiple_of(side * rows, rows), rows), :] = part
    d = lax.axis_index("dp")
    wide, narrow = small.shape[1], big[DEC_OUT].shape[1]

    def piece(out, line, lanes, position):
        size = out.shape[0]
        value = small[pl.ds(line, 1), :lanes]
        value = pltpu.roll(value, lax.rem(lanes - position * size, lanes), 1)
        out[...] = value[:, :size].reshape(size)

    def matrix(out, name):
        value = big[name][...].astype(F32)
        out[...] = jnp.transpose(value) if name == DEC_DOWN else value

    def block(outs, first_row, bup_row, lanes, names):
        for i, out in zip((0, 1, None, None, 2, 3, 4, None, None, None, 5), outs):
            if i is not None:
                piece(out, first_row + i, lanes, d)
        piece(outs[8], bup_row + d // 4, lanes, d % 4)
        for at, name in zip((2, 3, 7, 9), names):
            matrix(outs[at], name)

    block(totals[:11], 0, ROW_BUP, wide, (ENC_QKV, ENC_OUT, ENC_UP, ENC_DOWN))
    matrix(totals[11], EMBED)
    piece(totals[12], ROW_DEC + 7, narrow, d)
    piece(totals[13], ROW_DEC + 6, narrow, d)
    block(totals[14:], ROW_DEC, ROW_DEC_BUP, narrow, (DEC_QKV, DEC_OUT, DEC_UP, DEC_DOWN))


def write_outputs(results, decoded_own, dims):
    def vector(size):
        return jax.ShapeDtypeStruct((size // 16,), F32)

    def matrix(name):
        return shape(dims[name][0] // 16, dims[name][1], F32)

    def block(qkv, out, up, down):
        d, ff = dims[up]
        return [
            vector(d), vector(d), matrix(qkv), matrix(out), vector(d), vector(d), vector(d),
            matrix(up), vector(ff), matrix(down), vector(d),
        ]

    samples, half, width = results[1].shape
    rows, columns = results[3].shape
    out_shape = [
        jax.ShapeDtypeStruct((2 * samples, half, width), BF16),
        shape(2 * rows, columns),
        *block(ENC_QKV, ENC_OUT, ENC_UP, ENC_DOWN),
        matrix(EMBED),
        vector(width),
        vector(width),
        *block(DEC_QKV, DEC_OUT, DEC_UP, DEC_DOWN),
    ]
    return tuple(
        pl.pallas_call(
            write_kernel,
            out_shape=out_shape,
            in_specs=in_vmem(len(results) + 1),
            out_specs=in_vmem(len(out_shape)),
            compiler_params=pltpu.CompilerParams(vmem_limit_bytes=KERNEL_VMEM),
            name="write_outputs",
        )(*results, decoded_own)
    )


def reduce_plain(arrays, section_index):
    first = section_index == 0
    results = []
    for a in arrays:
        half = a.shape[1] // 2
        keep = lax.dynamic_slice_in_dim(a, section_index * half, half, 1)
        give = lax.dynamic_slice_in_dim(a, (1 - section_index) * half, half, 1)
        got = swapped(give, "section", 0)
        chip = (keep.astype(jnp.float32) + got.astype(jnp.float32)).astype(jnp.bfloat16)
        mine = lax.psum_scatter(chip, "dp", scatter_dimension=0, tiled=True)
        other = swapped(mine, "section", 0)
        whole = jnp.concatenate(
            [jnp.where(first, mine, other), jnp.where(first, other, mine)], axis=1
        )
        results.append(whole.astype(jnp.float32))
    return results


def finish_plain(acts, section_index):
    x, gy, seg_saved, enc, dec = acts["x"], acts["gy"], acts["saved"], acts["enc"], acts["dec"]
    gx, gf1, ga1, gqkv1, small1, gbup1 = encoder_backward(x, gy, seg_saved, enc["params"])
    small2, gbup2 = acts["small2"], acts["gbup2"]
    grads = (
        small1[0], small1[1], mm(enc["at"], gqkv1).astype(BF16), mm(enc["ot"], ga1).astype(BF16), small1[2],
        small1[3], small1[4], mm(enc["ct"], gf1).astype(BF16), gbup1[0], mm(enc["ut"], gy).astype(BF16),
        small1[5],
        weight_grad(acts["y"], acts["geb"]), small2[7], small2[6],
        small2[0], small2[1], mm(dec["at"], joined(dec["gqkv"])).astype(BF16),
        mm(dec["ot"], joined(dec["ga"])).astype(BF16), small2[2], small2[3], small2[4],
        mm(dec["ct"], joined(dec["gf"])).astype(BF16), gbup2[0],
        jnp.transpose(mm(dec["gt"], joined(dec["u"]))).astype(BF16), small2[5],
    )
    groups = lax.axis_size("dp")
    big = reduce_plain([g for g in grads if g.ndim == 2], section_index)
    flat = jnp.concatenate([g.reshape(groups, -1) for g in grads if g.ndim == 1], axis=1)
    line = lax.psum_scatter(flat, ("dp"), scatter_dimension=0, tiled=True)
    line = lax.psum(line, "section")[0]
    totals, at = [], 0
    for g in grads:
        if g.ndim == 2:
            totals.append(big.pop(0))
        else:
            size = g.shape[0] // groups
            totals.append(line[at : at + size])
            at += size
    decoded = acts["decoded"].reshape(SAMP_MB, PATCHES, -1)
    first = section_index == 0

    def halves(whole):
        half = whole.shape[1] // 2
        keep = lax.dynamic_slice_in_dim(whole, section_index * half, half, 1)
        give = lax.dynamic_slice_in_dim(whole, (1 - section_index) * half, half, 1)
        got = swapped(give, "section", 0)
        return jnp.concatenate([jnp.where(first, keep, got), jnp.where(first, got, keep)])

    return (halves(decoded), halves(gx), *totals)


def shards(
    patches,
    segment_ids,
    patch_order,
    encoder_gain1,
    encoder_bias1,
    encoder_qkv,
    encoder_out,
    encoder_out_bias,
    encoder_gain2,
    encoder_bias2,
    encoder_up,
    encoder_up_bias,
    encoder_down,
    encoder_down_bias,
    embed_weight,
    embed_bias,
    mask_token,
    decoder_gain1,
    decoder_bias1,
    decoder_qkv,
    decoder_out,
    decoder_out_bias,
    decoder_gain2,
    decoder_bias2,
    decoder_up,
    decoder_up_bias,
    decoder_down,
    decoder_down_bias,
    cotangent,
):
    enc_params = (
        encoder_gain1,
        encoder_bias1,
        encoder_qkv,
        encoder_out,
        encoder_out_bias,
        encoder_gain2,
        encoder_bias2,
        encoder_up,
        encoder_up_bias,
        encoder_down,
        encoder_down_bias,
    )
    embed_params = (embed_weight, embed_bias, mask_token)
    dec_params = (
        decoder_gain1,
        decoder_bias1,
        decoder_qkv,
        decoder_out,
        decoder_out_bias,
        decoder_gain2,
        decoder_bias2,
        decoder_up,
        decoder_up_bias,
        decoder_down,
        decoder_down_bias,
    )
    section_index = lax.axis_index("section")
    y, at1, qkv, e, rl, o1, ot1, n2, s2, ct1, ut1, slope = encoder_forward(
        patches, segment_ids, enc_params
    )
    g = cotangent.reshape(-1, DECODER_WIDTH)
    decoded, at2, ot2, ct2, gt2, u2, gf2, ga2, gqkv2, geb, gy, small2, gbup2 = decoder_both(
        y, segment_ids, patch_order, g, embed_params, dec_params
    )
    acts = dict(
        x=patches,
        y=y,
        gy=gy,
        geb=geb,
        decoded=decoded,
        small2=small2,
        gbup2=gbup2,
        saved=(qkv, e, rl, o1, n2, s2, slope),
        enc=dict(at=at1, ot=ot1, ct=ct1, ut=ut1, params=enc_params),
        dec=dict(at=at2, ot=ot2, ct=ct2, gt=gt2, u=u2, gf=gf2, ga=ga2, gqkv=gqkv2),
    )
    if lax.axis_size("dp") == 16:
        return finish(acts)
    return finish_plain(acts, section_index)


def solution(mesh):
    in_specs = (
        P("dp", None),
        P("dp", None),
        P("dp", None),
        P(),
        P(),
        P(),
        P(),
        P(),
        P(),
        P(),
        P(),
        P(),
        P(),
        P(),
        P(),
        P(),
        P(),
        P(),
        P(),
        P(),
        P(),
        P(),
        P(),
        P(),
        P(),
        P(),
        P(),
        P(),
        P("dp", None, None),
    )
    out_specs = (
        P("dp", "section", None),
        P("dp", "section"),
        P("dp"),
        P("dp"),
        P("dp", None),
        P("dp", None),
        P("dp"),
        P("dp"),
        P("dp"),
        P("dp", None),
        P("dp"),
        P("dp", None),
        P("dp"),
        P("dp", None),
        P("dp"),
        P("dp"),
        P("dp"),
        P("dp"),
        P("dp", None),
        P("dp", None),
        P("dp"),
        P("dp"),
        P("dp"),
        P("dp", None),
        P("dp"),
        P("dp", None),
        P("dp"),
    )
    return jax.shard_map(shards, mesh=mesh, in_specs=in_specs, out_specs=out_specs, check_vma=False)
```

```python
import functools
import math

import jax
import jax.numpy as jnp
import numpy as np
from jax import lax
from jax.experimental import pallas as pl
from jax.experimental.pallas import tpu as pltpu
from jax.sharding import PartitionSpec as P

H_ENC = 12
DECODER_WIDTH = 512
H_DEC = 16
PATCHES = 128
SAMP_MB = 12


EPSILON = 1e-06
MASKED = -1e30


def swapped(block, axis, apart):
    count = lax.axis_size(axis)
    route = []
    for low in range(count):
        high = low | 1 << apart
        if high != low and high < count:
            route += [(low, high), (high, low)]
    return lax.ppermute(block, axis, route)


def positions(count, features):
    column = np.arange(features)
    rate = np.exp(-math.log(10000.0) * (2 * (column // 2)) / features)
    angles = np.arange(count)[:, None] * rate[None, :]
    return np.where(column % 2 == 0, np.sin(angles), np.cos(angles)).astype(np.float32)


def weight_grad(left_side, grads):
    return lax.dot_general(
        left_side, grads, (((0,), (0,)), ((), ())), preferred_element_type=jnp.float32
    ).astype(jnp.bfloat16)


BF16 = jnp.bfloat16
F32 = jnp.float32


def mm(left, right):
    return lax.dot_general(left, right, (((1,), (0,)), ((), ())), preferred_element_type=F32)


def mm_nt(left, right):
    return lax.dot_general(left, right, (((1,), (1,)), ((), ())), preferred_element_type=F32)


def mm_tn(left, right):
    return lax.dot_general(left, right, (((0,), (0,)), ((), ())), preferred_element_type=F32)


def normalise(x):
    center = x - jnp.mean(x, axis=-1, keepdims=True)
    scale = lax.rsqrt(jnp.mean(center * center, axis=-1, keepdims=True) + EPSILON)
    return center * scale, scale


def normalise_back(grad, n, scale, gain):
    gn = grad * gain
    mean_gn = jnp.mean(gn, axis=-1, keepdims=True)
    mean_gnn = jnp.mean(gn * n, axis=-1, keepdims=True)
    return (gn - mean_gn - n * mean_gnn) * scale


def rows_sum(x):
    return jnp.sum(x, axis=0, keepdims=True)


def gelu_both(f):
    c0, c1 = math.sqrt(2.0 / math.pi), 0.044715
    square = f * f
    half = 0.5 + 0.5 * jnp.tanh(f * (c0 + (c0 * c1) * square))
    u = f * half
    return u, half + u * (1.0 - half) * (2.0 * c0 + (6.0 * c0 * c1) * square)


def lane_masks(head_size):
    lane = lax.broadcasted_iota(jnp.int32, (1, 128), 1)
    return [
        jnp.where((lane >= h * head_size) & (lane < (h + 1) * head_size), 1.0, 0.0).astype(BF16)
        for h in range(128 // head_size)
    ]


def stacked(x, masks):
    return jnp.concatenate([x * m for m in masks], axis=0)


def stacked_ones(x, masks, value):
    return jnp.concatenate(
        [jnp.broadcast_to(m * jnp.asarray(value, BF16), x.shape) for m in masks], axis=0
    )


def attention_forward(qkv_ref, o_ref, e_ref, rl_ref, rows, tokens, features, head_size, allowed):
    masks = lane_masks(head_size)
    per_group = len(masks)
    factor = head_size ** (-0.5) * math.log2(math.e)
    for g in range(features // 128):
        q, k, v = (qkv_ref[rows, j * features + g * 128 : j * features + (g + 1) * 128] for j in range(3))
        scores = mm_nt(q, stacked(k, masks))
        parts = []
        for h in range(per_group):
            part = scores[:, h * tokens : (h + 1) * tokens]
            if allowed is not None:
                part = jnp.where(allowed, part, MASKED)
            top = jnp.max(part, axis=-1, keepdims=True)
            parts.append(jnp.exp2((part - top) * factor).astype(BF16))
        e = jnp.concatenate(parts, axis=1)
        width = per_group * tokens
        e_ref[rows, g * width : (g + 1) * width] = e
        both = mm(e, jnp.concatenate([stacked(v, masks), stacked_ones(v, masks, 1.0)], axis=1))
        rl = 1.0 / both[:, 128:]
        rl_ref[rows, g * 128 : (g + 1) * 128] = rl
        o_ref[rows, g * 128 : (g + 1) * 128] = (both[:, :128] * rl).astype(BF16)


def attention_backward_group(q, k, v, e, go, o, rl, head_size):
    masks = lane_masks(head_size)
    per_group, tokens = len(masks), q.shape[0]
    scaling = head_size ** (-0.5)
    go = go.astype(F32) * rl
    go_low = go.astype(BF16)
    inner = (go * o.astype(F32)).astype(BF16)
    left = jnp.concatenate([go_low, inner], axis=1)
    right = jnp.concatenate([stacked(v, masks), stacked_ones(v, masks, -1.0)], axis=1)
    gs = (e.astype(F32) * mm_nt(left, right)).astype(BF16)

    def diagonal(wide):
        return jnp.concatenate(
            [
                wide[h * head_size : (h + 1) * head_size, h * tokens : (h + 1) * tokens]
                for h in range(per_group)
            ],
            axis=0,
        )

    gq = mm(gs, stacked(k, masks)) * scaling
    gk = jnp.transpose(diagonal(mm_tn(q, gs)) * scaling)
    gv = jnp.transpose(diagonal(mm_tn(go_low, e)))
    return gq.astype(BF16), gk.astype(BF16), gv.astype(BF16)


def attention_backward(
    qkv_ref, go_ref, o_ref, e_ref, rl_ref, gqkv_ref, rows, tokens, features, head_size
):
    width = 128 // head_size * tokens
    for g in range(features // 128):
        at = slice(g * 128, (g + 1) * 128)
        spots = [slice(j * features + g * 128, j * features + (g + 1) * 128) for j in range(3)]
        q, k, v = (qkv_ref[rows, spot] for spot in spots)
        e = e_ref[rows, g * width : (g + 1) * width]
        grads = attention_backward_group(
            q, k, v, e, go_ref[rows, at], o_ref[rows, at], rl_ref[rows, at], head_size
        )
        for spot, grad in zip(spots, grads):
            gqkv_ref[rows, spot] = grad


def feed_forward(c_ref, up_ref, bup_ref, u_ref, slope_ref, tile, ut_ref=None):
    for t in range(up_ref.shape[1] // tile):
        at = slice(t * tile, (t + 1) * tile)
        f = mm(c_ref[...], up_ref[:, at]) + bup_ref[at].reshape(1, tile)
        u, slope = gelu_both(f)
        u = u.astype(BF16)
        u_ref[:, at] = u
        slope_ref[:, at] = slope.astype(BF16)
        if ut_ref is not None:
            ut_ref[at, :] = jnp.transpose(u)


def feed_forward_back(gm_ref, down_ref, slope_ref, gf_ref, gbup_ref, tile):
    for t in range(down_ref.shape[0] // tile):
        at = slice(t * tile, (t + 1) * tile)
        gu = mm_nt(gm_ref[...], down_ref[at, :])
        gf = (gu * slope_ref[:, at].astype(F32)).astype(BF16)
        gf_ref[:, at] = gf
        gbup_ref[:, at] += rows_sum(gf.astype(F32))


def row(ref):
    return ref[...].reshape(1, -1)


def segment_mask(seg_ref, section):
    seg = seg_ref[pl.ds(section, 1), :].astype(F32)
    rows = seg.shape[1]
    column = jnp.transpose(jnp.broadcast_to(seg, (128, rows)))
    return jnp.concatenate([column] * (rows // 128), axis=1) == seg


class Writer:
    def __init__(self, semaphores):
        self.semaphores, self.copies = semaphores, []

    def start(self, source, target):
        copy = pltpu.make_async_copy(source, target, self.semaphores.at[len(self.copies)])
        copy.start()
        self.copies.append(copy)

    def wait(self):
        for copy in self.copies:
            copy.wait()


def encoder_forward_kernel(
    x_ref, seg_ref,
    gain1, bias1, w_qkv, w_out, b_out, gain2, bias2, w_up, b_up, w_down, b_down,
    *refs,
):
    outs, scratch = refs[:12], refs[12:24]
    y_ref, at_ref, qkv_ref, e_ref, rl_ref, o_ref, ot_ref, n2_ref, s2_ref, ct_ref, ut_ref, slope_ref = scratch
    h_ref, c_ref, u_ref, qkv_v, out_v, up_v, down_v, sem, out_sem = refs[24:]
    target = {id(v): o for v, o in zip(scratch, outs)}
    writer = Writer(out_sem)

    def write(*done):
        for v in done:
            writer.start(v, target[id(v)])

    tokens, features = y_ref.shape
    pairs = ((w_qkv, qkv_v), (w_out, out_v), (w_up, up_v), (w_down, down_v))
    loads = [pltpu.make_async_copy(w, v, sem.at[i]) for i, (w, v) in enumerate(pairs)]
    for load in loads:
        load.start()
    section = lax.axis_index("section")
    x = x_ref[pl.ds(pl.multiple_of(section * tokens, tokens), tokens), :].astype(F32)
    n1, _ = normalise(x)
    a = (n1 * row(gain1) + row(bias1)).astype(BF16)
    at_ref[...] = jnp.transpose(a)
    allowed = segment_mask(seg_ref, section)
    loads[0].wait()
    qkv_ref[...] = mm(a, qkv_v[...]).astype(BF16)
    write(at_ref, qkv_ref)
    attention_forward(
        qkv_ref, o_ref, e_ref, rl_ref, slice(None), tokens, features, features // H_ENC, allowed
    )
    ot_ref[...] = jnp.transpose(o_ref[...])
    write(e_ref, rl_ref, o_ref, ot_ref)
    loads[1].wait()
    h_ref[...] = x + (mm(o_ref[...], out_v[...]) + row(b_out))
    n2, s2 = normalise(h_ref[...])
    n2_ref[...] = n2
    s2_ref[...] = s2
    c_ref[...] = (n2 * row(gain2) + row(bias2)).astype(BF16)
    ct_ref[...] = jnp.transpose(c_ref[...])
    write(n2_ref, s2_ref, ct_ref)
    loads[2].wait()
    feed_forward(c_ref, up_v, b_up, u_ref, slope_ref, 512, ut_ref)
    write(ut_ref, slope_ref)
    loads[3].wait()
    y_ref[...] = (h_ref[...] + (mm(u_ref[...], down_v[...]) + row(b_down))).astype(BF16)
    write(y_ref)
    writer.wait()


def encoder_backward_kernel(
    x_ref, gy_ref, qkv_ref, e_ref, rl_ref, o_ref, n2_ref, s2_ref, slope_ref,
    gain1, w_qkv, w_out, gain2, w_up, w_down,
    gx_ref, gf_ref, ga_ref, gqkv_ref, small_ref, gbup_ref,
    gh_ref, go_ref,
):
    tokens, features = gy_ref.shape
    section = lax.axis_index("section")
    x = x_ref[pl.ds(pl.multiple_of(section * tokens, tokens), tokens), :].astype(F32)
    gbup_ref[...] = jnp.zeros_like(gbup_ref)
    feed_forward_back(gy_ref, w_down, slope_ref, gf_ref, gbup_ref, 512)
    gc = mm_nt(gf_ref[...], w_up[...])
    g = gy_ref[...].astype(F32)
    n2 = n2_ref[...]
    gh = g + normalise_back(gc, n2, s2_ref[...], row(gain2))
    gh_ref[...] = gh
    ga_ref[...] = gh.astype(BF16)
    small_ref[2:3, :] = rows_sum(gh)
    small_ref[3:4, :] = rows_sum(gc * n2)
    small_ref[4:5, :] = rows_sum(gc)
    small_ref[5:6, :] = rows_sum(g)
    go_ref[...] = mm_nt(ga_ref[...], w_out[...]).astype(BF16)
    attention_backward(
        qkv_ref, go_ref, o_ref, e_ref, rl_ref, gqkv_ref, slice(None), tokens, features,
        features // H_ENC,
    )
    gn = mm_nt(gqkv_ref[...], w_qkv[...])
    n1, s1 = normalise(x)
    small_ref[0:1, :] = rows_sum(gn * n1)
    small_ref[1:2, :] = rows_sum(gn)
    gx_ref[...] = (gh_ref[...] + normalise_back(gn, n1, s1, row(gain1))).astype(BF16)


def split_low(x):
    high = x.astype(BF16)
    return high, (x - high.astype(F32)).astype(BF16)


def place_slots(order_ref, seg, section, hot_ref, place_ref, empty_ref):
    packed = seg.shape[1]
    sample = lax.broadcasted_iota(jnp.int32, (16, packed), 0).astype(F32)
    starts = jnp.sum(jnp.where(seg < sample, 1.0, 0.0), axis=1, keepdims=True)
    counts = jnp.sum(jnp.where(seg == sample, 1.0, 0.0), axis=1, keepdims=True)
    line = lax.broadcasted_iota(jnp.int32, (PATCHES, PATCHES), 0).astype(F32)
    line_low = line.astype(BF16)
    lane_low = lax.broadcasted_iota(jnp.int32, (8, PATCHES), 1).astype(F32).astype(BF16)
    column = lax.broadcasted_iota(jnp.int32, (PATCHES, packed), 1).astype(F32)
    packed_line = lax.broadcasted_iota(jnp.int32, (packed, PATCHES), 0).astype(F32)
    for j in range(SAMP_MB):
        at = slice(j * PATCHES, (j + 1) * PATCHES)
        order = order_ref[pl.ds(section * SAMP_MB + j, 1), :].astype(F32)
        hit = jnp.where(order == line, 1.0, 0.0).astype(BF16)
        start, count = starts[j : j + 1, :], counts[j : j + 1, :]
        down, across = mm(hit, line_low), mm_nt(lane_low, hit)[:1, :]
        down = jnp.where(down < count, start + down, -1.0)
        across = jnp.where(across < count, start + across, -1.0)
        wide = jnp.concatenate([down] * (packed // PATCHES), axis=1)
        hot_ref[at, :] = jnp.where(column == wide, 1.0, 0.0).astype(BF16)
        place_ref[:, at] = jnp.where(packed_line == across, 1.0, 0.0).astype(BF16)
        empty_ref[at, :] = jnp.where(down < 0.0, 1.0, 0.0)


def decoder_kernel(
    y_ref, seg_ref, order_ref, pos_ref, g_hbm,
    w_embed_hbm, b_embed, mask_token,
    gain1, bias1, w_qkv_hbm, w_out_hbm, b_out, gain2, bias2, w_up_hbm, b_up, w_down_hbm, b_down,
    *refs,
):
    hbm, (geb_ref, gy_ref, small_ref, gbup_ref) = refs[:9], refs[9:13]
    buffers = refs[13:22]
    out_ref, at_ref, ot_ref, ct_ref, gt_ref, u_ref, gf_ref, ga_ref, gqkv_ref = buffers
    (
        e2_ref, z_ref, s1_ref, e_ref, rl_ref, h_ref, s2_ref, go_ref, ge_ref, o_ref, c_ref, qkv_ref,
        slope_ref, g_all, hot_ref, place_ref, empty_ref, w_embed, w_qkv, w_out, w_up, w_down,
        w_sem, out_sem,
    ) = refs[22:]
    packed = y_ref.shape[0]
    rows, features = z_ref.shape
    samples = rows // PATCHES
    head_size = features // H_DEC
    total = g_all.shape[0]
    section = lax.axis_index("section")
    mine = pl.ds(pl.multiple_of(section * total, total), total)
    pairs = (
        (w_embed_hbm, w_embed), (w_qkv_hbm, w_qkv), (w_out_hbm, w_out), (w_up_hbm, w_up),
        (w_down_hbm, w_down), (g_hbm.at[mine, :], g_all),
    )
    loads = [pltpu.make_async_copy(a, b, w_sem.at[i]) for i, (a, b) in enumerate(pairs)]
    for load in loads:
        load.start()

    def write(at, *which):
        copies = []
        for i in which:
            target = hbm[i].at[:, at] if 1 <= i <= 4 else hbm[i].at[at, :]
            copies.append(pltpu.make_async_copy(buffers[i], target, out_sem.at[i]))
            copies[-1].start()
        return copies

    small_ref[...] = jnp.zeros_like(small_ref)
    gbup_ref[...] = jnp.zeros_like(gbup_ref)
    ge_ref[...] = jnp.zeros_like(ge_ref)
    seg = seg_ref[pl.ds(section, 1), :].astype(F32)
    place_slots(order_ref, seg, section, hot_ref, place_ref, empty_ref)
    loads[0].wait()
    high, low = split_low(mm(y_ref[...], w_embed[...]) + row(b_embed))
    e2_ref[:packed, :] = high
    e2_ref[packed:, :] = low
    for load in loads[1:]:
        load.wait()

    def one_step(step, carry):
        here = pl.ds(pl.multiple_of(step * rows, rows), rows)
        one_hot = hot_ref[here, :]
        empty = jnp.concatenate([empty_ref[here, :]] * (features // 128), axis=1)
        twice = jnp.concatenate([one_hot, one_hot], axis=1)
        z = mm(twice, e2_ref[...]) + empty * row(mask_token)
        z = z + jnp.concatenate([pos_ref[...]] * samples, axis=0)
        n1, s1 = normalise(z)
        z_ref[...] = z
        s1_ref[...] = s1
        a = (n1 * row(gain1) + row(bias1)).astype(BF16)
        at_ref[...] = jnp.transpose(a)
        writing = write(here, 1)
        qkv_ref[...] = mm(a, w_qkv[...]).astype(BF16)

        def forward(b, carry):
            at = pl.ds(pl.multiple_of(b * PATCHES, PATCHES), PATCHES)
            attention_forward(qkv_ref, o_ref, e_ref, rl_ref, at, PATCHES, features, head_size, None)
            return carry

        lax.fori_loop(0, samples, forward, 0, unroll=2)
        ot_ref[...] = jnp.transpose(o_ref[...])
        h_ref[...] = z_ref[...] + (mm(o_ref[...], w_out[...]) + row(b_out))
        n2, s2 = normalise(h_ref[...])
        s2_ref[...] = s2
        c_ref[...] = (n2 * row(gain2) + row(bias2)).astype(BF16)
        ct_ref[...] = jnp.transpose(c_ref[...])
        feed_forward(c_ref, w_up, b_up, u_ref, slope_ref, 512)
        writing += write(here, 2, 3, 5)
        out_ref[...] = (h_ref[...] + (mm(u_ref[...], w_down[...]) + row(b_down))).astype(BF16)

        g_ref = g_all.at[here, :]
        gt_ref[...] = jnp.transpose(g_ref[...])
        feed_forward_back(g_ref, w_down, slope_ref, gf_ref, gbup_ref, 512)
        writing += write(here, 0, 4, 6)
        gc = mm_nt(gf_ref[...], w_up[...])
        g = g_ref[...].astype(F32)
        h = h_ref[...]
        n2 = (h - jnp.mean(h, axis=-1, keepdims=True)) * s2_ref[...]
        gh = g + normalise_back(gc, n2, s2_ref[...], row(gain2))
        small_ref[2:3, :] += rows_sum(gh)
        small_ref[3:4, :] += rows_sum(gc * n2)
        small_ref[4:5, :] += rows_sum(gc)
        small_ref[5:6, :] += rows_sum(g)
        h_ref[...] = gh
        ga_ref[...] = gh.astype(BF16)
        go_ref[...] = mm_nt(ga_ref[...], w_out[...]).astype(BF16)
        writing += write(here, 7)

        def backward(b, carry):
            at = pl.ds(pl.multiple_of(b * PATCHES, PATCHES), PATCHES)
            attention_backward(
                qkv_ref, go_ref, o_ref, e_ref, rl_ref, gqkv_ref, at, PATCHES, features, head_size
            )
            return carry

        lax.fori_loop(0, samples, backward, 0, unroll=2)
        writing += write(here, 8)
        gn = mm_nt(gqkv_ref[...], w_qkv[...])
        z = z_ref[...]
        n1 = (z - jnp.mean(z, axis=-1, keepdims=True)) * s1_ref[...]
        gz = h_ref[...] + normalise_back(gn, n1, s1_ref[...], row(gain1))
        small_ref[0:1, :] += rows_sum(gn * n1)
        small_ref[1:2, :] += rows_sum(gn)
        small_ref[6:7, :] += rows_sum(gz * empty)
        ge_ref[...] += mm(place_ref[:, here], gz.astype(BF16))
        for copy in writing:
            copy.wait()
        return carry

    lax.fori_loop(0, total // rows, one_step, 0)
    ge = ge_ref[...]
    small_ref[7:8, :] = rows_sum(ge)
    geb_ref[...] = ge.astype(BF16)
    gy_ref[...] = mm_nt(geb_ref[...], w_embed[...]).astype(BF16)


def in_vmem(count):
    return [pl.BlockSpec(memory_space=pltpu.VMEM)] * count


def in_hbm():
    return pl.BlockSpec(memory_space=pl.ANY)


def shape(rows, columns, dtype=BF16):
    return jax.ShapeDtypeStruct((rows, columns), dtype)


KERNEL_VMEM = 60 * 2**20


def encoder_forward(x, segments, params):
    rows, d = x.shape[0] // 2, x.shape[1]
    ff = params[7].shape[1]
    outs = [
        (rows, d, BF16),
        (d, rows, BF16),
        (rows, 3 * d, BF16),
        (rows, H_ENC * rows, BF16),
        (rows, d, F32),
        (rows, d, BF16),
        (d, rows, BF16),
        (rows, d, F32),
        (rows, 1, F32),
        (d, rows, BF16),
        (ff, rows, BF16),
        (rows, ff, BF16),
    ]
    more = [(rows, d, F32), (rows, d, BF16), (rows, ff, BF16)]
    args = [x, segments, *params]
    matrices = [w for w in params if w.dtype == BF16]
    return pl.pallas_call(
        encoder_forward_kernel,
        out_shape=[shape(*o) for o in outs],
        in_specs=in_vmem(2) + [in_hbm() if w.dtype == BF16 else in_vmem(1)[0] for w in params],
        out_specs=[in_hbm()] * len(outs),
        scratch_shapes=[pltpu.VMEM((r, w), t) for r, w, t in outs + more]
        + [pltpu.VMEM(w.shape, BF16) for w in matrices]
        + [pltpu.SemaphoreType.DMA((len(matrices),)), pltpu.SemaphoreType.DMA((len(outs),))],
        compiler_params=pltpu.CompilerParams(vmem_limit_bytes=KERNEL_VMEM),
        name="encoder_forward",
    )(*args)


def encoder_backward(x, gy, saved, params):
    gain1, _, w_qkv, w_out, _, gain2, _, w_up, _, w_down, _ = params
    rows, d = gy.shape
    ff = w_up.shape[1]
    outs = [
        shape(rows, d),
        shape(rows, ff),
        shape(rows, d),
        shape(rows, 3 * d),
        shape(8, d, F32),
        shape(1, ff, F32),
    ]
    args = [x, gy, *saved, gain1, w_qkv, w_out, gain2, w_up, w_down]
    return pl.pallas_call(
        encoder_backward_kernel,
        out_shape=outs,
        in_specs=in_vmem(len(args)),
        out_specs=in_vmem(len(outs)),
        scratch_shapes=[pltpu.VMEM((rows, d), F32), pltpu.VMEM((rows, d), BF16)],
        compiler_params=pltpu.CompilerParams(vmem_limit_bytes=KERNEL_VMEM),
        name="encoder_backward",
    )(*args)


def decoder_both(y, segments, orders, g, embed_params, params):
    packed, d_enc = y.shape
    total, d = g.shape[0] // 2, g.shape[1]
    rows = 6 * PATCHES
    ff = params[7].shape[1]
    args = [y, segments, orders, positions(PATCHES, d), g, *embed_params, *params]
    in_specs = in_vmem(4) + [in_hbm()]
    in_specs += [in_hbm() if x.dtype == BF16 else in_vmem(1)[0] for x in args[5:]]
    wide = [ff, ff, d, 3 * d]
    outs = [shape(total, d)] + [shape(d, total)] * 4 + [shape(total, w) for w in wide]
    buffers = [(rows, d, BF16)] + [(d, rows, BF16)] * 4 + [(rows, w, BF16) for w in wide]
    last = [shape(packed, d), shape(packed, d_enc), shape(8, d, F32), shape(1, ff, F32)]
    scratch = [
        (2 * packed, d, BF16),
        (rows, d, F32),
        (rows, 1, F32),
        (rows, H_DEC * PATCHES, BF16),
        (rows, d, F32),
        (rows, d, F32),
        (rows, 1, F32),
        (rows, d, BF16),
        (packed, d, F32),
        (rows, d, BF16),
        (rows, d, BF16),
        (rows, 3 * d, BF16),
        (rows, ff, BF16),
        (total, d, BF16),
        (total, packed, BF16),
        (packed, total, BF16),
        (total, 128, F32),
    ]
    matrices = [x for x in args[5:] if x.dtype == BF16]
    return pl.pallas_call(
        decoder_kernel,
        out_shape=outs + last,
        in_specs=in_specs,
        out_specs=[in_hbm()] * len(outs) + in_vmem(len(last)),
        scratch_shapes=[pltpu.VMEM((r, w), t) for r, w, t in buffers + scratch]
        + [pltpu.VMEM(x.shape, BF16) for x in matrices]
        + [pltpu.SemaphoreType.DMA((k,)) for k in (len(matrices) + 1, len(outs))],
        compiler_params=pltpu.CompilerParams(vmem_limit_bytes=KERNEL_VMEM),
        name="decoder_both",
    )(*args)


MESH = pl.DeviceIdType.MESH
ENC_QKV, ENC_OUT, ENC_UP, ENC_DOWN, EMBED, DEC_QKV, DEC_OUT, DEC_UP, DEC_DOWN = range(9)
GIVE, PAIR, FFN, LN2, GO, ATT, GN, LAST = range(10, 18)
SMALL = -1
ROW_BUP, ROW_DEC_BUP, ROW_DEC, SMALL_ROWS = 6, 10, 16, 24
Z, Y, X, CORE = range(4)
ORDERS = ((X, Y, Z), (Y, X, Z), (X, Z, Y), (Y, Z, X))


class Chunk:
    def __init__(self, name, half, offset, rows, width, first_row=None):
        self.name, self.half, self.offset, self.rows, self.width = name, half, offset, rows, width
        self.first_row, self.turned, self.order = first_row, name == DEC_DOWN, None
        self.decoder = name in (DEC_QKV, DEC_UP, DEC_OUT)

    def columns(self, side):
        return pl.ds(pl.multiple_of(side * self.half + self.offset, 128), self.width)

    def place(self, side):
        if self.turned:
            return (pl.ds(pl.multiple_of(side * self.half + self.offset, 128), self.rows), slice(None))
        if self.first_row is None:
            return (slice(None), self.columns(side))
        return (pl.ds(self.first_row, self.rows), self.columns(side))

    @property
    def bytes(self):
        return 32 * self.rows * self.width

    def loads(self, order):
        first, second, third = order
        if second == Z:
            return (self.bytes, self.bytes, self.bytes / 8)
        return (self.bytes, self.bytes / 2, self.bytes / 2)


def make_chunks():
    chunks = [Chunk(DEC_OUT, 256, 0, 32, 256), Chunk(DEC_QKV, 768, 0, 32, 768)]
    for q in range(2):
        chunks.append(Chunk(ENC_DOWN, 384, 0, 96, 384, 96 * q))
        chunks.append(Chunk(ENC_UP, 1536, 768 * q, 48, 768))
    chunks += [Chunk(ENC_OUT, 384, 0, 48, 384)]
    chunks += [Chunk(ENC_QKV, 1152, 0, 48, 768), Chunk(ENC_QKV, 1152, 768, 48, 384)]
    chunks += [Chunk(EMBED, 256, 0, 48, 256), Chunk(DEC_DOWN, 256, 0, 256, 128)]
    chunks += [Chunk(DEC_UP, 1024, o, 32, 512) for o in (0, 512)]
    for c, chunk in enumerate(chunks):
        chunk.order = ORDERS[c % 2]

    def busiest():
        load = [0.0, 0.0, 0.0]
        for chunk in chunks:
            for axis, size in zip(chunk.order, chunk.loads(chunk.order)):
                load[axis] += size
        return sorted(load, reverse=True)

    best, better = busiest(), True
    while better:
        better = False
        for chunk in chunks:
            for order in ORDERS:
                before, chunk.order = chunk.order, order
                if busiest() < best:
                    best, better = busiest(), True
                else:
                    chunk.order = before
    return chunks


def make_groups(chunks):
    return [[c] for c in range(len(chunks))]


def product_cost(k, count):
    if k.turned:
        return 6.0
    return k.rows * k.width * (1.1 / 8192 if k.decoder else 0.7 / 18432)


def tasks_in_order(chunks, groups):
    def gives(name):
        found = [(g, chunks[m[0]], len(m)) for g, m in enumerate(groups)]
        kind = PAIR if name == DEC_DOWN else GIVE
        return [(kind, g, product_cost(k, size)) for g, k, size in found if k.name == name]

    tasks = gives(DEC_OUT) + gives(DEC_QKV)
    tasks += [(FFN, t, 2.5) for t in range(4)]
    for pair in zip(gives(ENC_DOWN), gives(ENC_UP)):
        tasks += pair
    tasks += [(LN2, 0, 1.5), (GO, 0, 1.2)]
    tasks += [(ATT, g, 2.2) for g in range(6)]
    tasks += gives(ENC_OUT) + gives(ENC_QKV)
    tasks += [(GN, j, 1.2) for j in range(3)] + [(LAST, 0, 2.0)]
    return tasks + gives(EMBED) + gives(DEC_DOWN) + gives(DEC_UP)


def decoder_arrays(chunks):
    names = []
    for k in chunks:
        if (k.decoder or k.turned) and k.name not in names:
            names.append(k.name)
    return names


def make_plan(chunks, groups):
    tasks = tasks_in_order(chunks, groups)
    lhs = decoder_arrays(chunks)
    free = [0.0] * 4
    rate = [82e3, 82e3, 82e3, 500e3]
    pending, plan, now, owned = [], [], 2.0, set()

    def send(link, size, latency):
        begin = max(now, free[link])
        free[link] = begin + size / rate[link]
        return free[link] + latency

    def blocked(task):
        if task[0] not in (GIVE, PAIR):
            return False
        name = chunks[groups[task[1]][0]].name
        if name not in lhs[2:]:
            return False
        name = lhs[lhs.index(name) - 2]
        return any(chunks[m[0]].name == name and g not in owned for g, m in enumerate(groups))

    while tasks or pending:
        pending.sort()
        if pending and (pending[0][0] <= now or not tasks or blocked(tasks[0])):
            arrive, stage, c = pending.pop(0)
            now = max(now, arrive)
            plan.append((stage, c))
            if c == SMALL:
                now += 0.1
                if stage < 4:
                    pending.append((now + 2.0, stage + 1, c))
                continue
            members = groups[c] if stage == 1 else [c]
            k = chunks[members[0]]
            if stage == 1:
                owned.add(c)
                now += 0.6 if k.turned else product_cost(k, len(members)) + 0.2 * len(members)
            else:
                now += 0.25
            for c in members:
                k = chunks[c]
                if stage < 4:
                    axis = k.order[stage - 1]
                    latency = 3.5 if axis == Z else 3.0
                    arrive = send(axis, k.loads(k.order)[stage - 1], latency)
                    pending.append((arrive, stage + 1, c))
                elif stage == 4:
                    pending.append((send(CORE, k.bytes / 16, 1.8), 5, c))
            continue
        name, arg, cost = tasks.pop(0)
        plan.append((name, arg))
        now += cost
        if name in (GIVE, PAIR):
            arrive = [send(CORE, chunks[c].bytes, 1.8) for c in groups[arg]]
            pending.append((max(arrive), 1, arg))
        elif name == LAST:
            pending.append((now + 2.0, 1, SMALL))
    return plan


class Ring:
    def __init__(self, sources, slots, semaphores, depth):
        self.copies = [
            pltpu.make_async_copy(source, slot, semaphores())
            for source, slot in zip(sources, slots)
        ]
        self.slots, self.depth, self.at = slots, depth, 0

    def begin(self):
        for copy in self.copies[: self.depth]:
            copy.start()

    def take(self):
        self.copies[self.at].wait()
        return self.slots[self.at]

    def done(self):
        ahead = self.at + self.depth
        if ahead < len(self.copies):
            self.copies[ahead].start()
        self.at += 1


class Names:
    def __init__(self, names, refs):
        self.__dict__.update(zip(names, refs))


LOADS = 96


def finish_kernel(chunks, groups, plan, r):
    n = len(chunks)
    s = lax.axis_index("section")
    d = lax.axis_index("dp")
    here = (d // 4, (d // 2) % 2, d % 2)
    z, y, x = here
    sibling = {"section": 1 - s}
    z_at = [lax.rem(z + k, 4) for k in (1, 2, 3)]
    peers = {
        X: [(1 - x, {"dp": d + 1 - 2 * x})],
        Y: [(1 - y, {"dp": d + 2 - 4 * y})],
        Z: [(p, {"dp": d + 4 * (p - z)}) for p in z_at],
    }
    every = [sibling] + [peer for axis in (X, Y, Z) for _, peer in peers[axis]]

    barrier = pltpu.get_barrier_semaphore()
    for peer in every:
        pl.semaphore_signal(barrier, inc=1, device_id=peer, device_id_type=MESH)

    counter = iter(range(LOADS))

    def semaphore():
        return r.load_sem.at[next(counter)]

    def remote(src, dst, send, recv, peer):
        return pltpu.make_async_remote_copy(
            src_ref=src, dst_ref=dst, send_sem=send, recv_sem=recv, device_id=peer, device_id_type=MESH
        )

    rhs_of = {DEC_QKV: r.gqkv2, DEC_UP: r.gf2, DEC_OUT: r.ga2}
    lhs_of = {DEC_QKV: r.at2, DEC_UP: r.ct2, DEC_OUT: r.ot2, DEC_DOWN: r.gt2}
    tiles, widths, last_use = [], [], {}

    def wide_columns(g, side):
        k, width = chunks[groups[g][0]], sum(chunks[c].width for c in groups[g])
        return pl.ds(pl.multiple_of(side * k.half + k.offset, 128), width)

    for i, (name, arg) in enumerate(plan):
        if name == PAIR:
            tiles += [r.u2.at[:, t * 512 : (t + 1) * 512] for t in range(4)]
            last_use[DEC_DOWN] = i
        elif name in (GIVE, 1) and arg != SMALL and chunks[groups[arg][0]].decoder:
            k = chunks[groups[arg][0]]
            tiles.append(rhs_of[k.name].at[:, wide_columns(arg, 1 - s if name == GIVE else s)])
            last_use[k.name] = i
    lhs_names = decoder_arrays(chunks)
    assert sorted(lhs_names, key=last_use.get) == lhs_names
    rhs_slots = [r.rhs.at[i % 2, :, : tile.shape[1]] for i, tile in enumerate(tiles)]
    rhs = Ring(tiles, rhs_slots, semaphore, 2)
    lhs = Ring([lhs_of[k] for k in lhs_names], [r.lhs.at[i % 2] for i in range(4)], semaphore, 2)
    lhs.copies[0].start()
    rhs.begin()
    lhs.copies[1].start()
    tokens, d_enc = r.gy.shape
    blocks = []
    for t in range(4):
        at = pl.ds(t * d_enc, d_enc)
        blocks += [r.w_down.at[at, :], r.w_up.at[:, at]]
    blocks.append(r.w_out)
    blocks += [r.w_qkv.at[:, pl.ds(j * d_enc, d_enc)] for j in range(3)]
    weights = Ring(blocks, [r.w.at[i % 4] for i in range(12)], semaphore, 4)
    e_width = 2 * tokens
    e_ring = Ring(
        [r.e.at[:, pl.ds(g * e_width, e_width)] for g in range(6)],
        [r.e_v.at[g % 2] for g in range(6)],
        semaphore,
        2,
    )

    def load(source, target):
        return pltpu.make_async_copy(source, target, semaphore())

    mine = pl.ds(pl.multiple_of(s * tokens, tokens), tokens)
    load_gy, load_slope, load_ut = load(r.gy, r.gy_v), load(r.slope, r.slope_v), load(r.ut, r.ut_v)
    load_ct, load_at, load_ot = load(r.ct, r.ct_v), load(r.at, r.at_v), load(r.ot, r.ot_v)
    load_n2, load_s2, load_qkv = load(r.n2, r.n2_v), load(r.s2, r.s2_v), load(r.qkv, r.qkv_v)
    load_o, load_rl, load_x = load(r.o, r.o_v), load(r.rl, r.rl_v), load(r.x.at[mine, :], r.x_v)
    load_y, load_geb = load(r.y, r.y_v), load(r.geb, r.geb_v)
    begun = [
        (load_gy, load_slope, weights),
        (load_ut, load_ct, load_n2, load_s2),
        (load_qkv, load_o, load_rl, e_ring),
        (load_ot, load_at, load_x, load_y, load_geb),
    ]

    def begin_some():
        for copy in begun.pop(0) if begun else ():
            copy.begin() if isinstance(copy, Ring) else copy.start()

    half = r.decoded.shape[1] // 2
    give_half = r.decoded.at[:, pl.ds(pl.multiple_of((1 - s) * half, half), half), :]
    decoded_away = remote(give_half, r.decoded_got, r.swap_sem.at[0], r.swap_sem.at[1], sibling)
    gx_columns = d_enc // 2
    gx_half = r.gx.at[:, pl.ds(pl.multiple_of((1 - s) * gx_columns, 128), gx_columns)]
    gx_away = remote(gx_half, r.gx_got, r.swap_sem.at[2], r.swap_sem.at[3], sibling)

    small = r.small
    small[...] = jnp.zeros_like(small)
    small[ROW_DEC : ROW_DEC + 8, : r.small2.shape[1]] = r.small2[...]
    quarter = r.gbup2.shape[1] // 4
    for i in range(4):
        piece = r.gbup2[:, i * quarter : (i + 1) * quarter]
        small[ROW_DEC_BUP + i : ROW_DEC_BUP + i + 1, :quarter] = piece

    pl.semaphore_wait(barrier, len(every))

    copies = {}
    first_slot = (0, 1, 2, 5, 8)

    def chunk_copy(c, slot, src, dst, peer):
        copy = remote(src, dst, r.send_sem.at[c, slot], r.recv_sem.at[c, slot], peer)
        copy.start()
        copies[c, slot] = copy

    sent = set()

    def sent_by(c, slot):
        if (c, slot) not in sent:
            sent.add((c, slot))
            copies[c, slot].wait_send()

    staged = {}

    def staging(c):
        k = chunks[c]
        buffers = r.stage[k.rows, k.width]
        turn = staged.setdefault((k.rows, k.width), [])
        if len(turn) >= len(buffers):
            sent_by(turn[-len(buffers)], 0)
        turn.append(c)
        return buffers[(len(turn) - 1) % len(buffers)]

    def shard(i):
        return (i // 4, (i // 2) % 2, i % 2)

    waited = set()

    def arrived(copy):
        if id(copy) not in waited:
            waited.add(id(copy))
            copy.wait()

    def product(g, side):
        k, columns = chunks[groups[g][0]], wide_columns(g, side)
        if k.decoder:
            return mm(lhs.slots[lhs_names.index(k.name)][...], rhs.take()[...])
        if k.name == EMBED:
            arrived(load_y)
            arrived(load_geb)
            return mm_tn(r.y_v[...], r.geb_v[:, columns])
        if k.name == ENC_DOWN:
            arrived(load_ut)
            at = [i * 192 + k.first_row for i in range(16)]
            left = jnp.concatenate([r.ut_v[i : i + k.rows, :] for i in at], axis=0)
            return mm(left, r.gy_v[:, columns])
        if k.name == ENC_UP:
            arrived(load_ct)
            return mm(r.ct_v[...], r.slope_v[:, columns])
        if k.name == ENC_OUT:
            arrived(load_ot)
            return mm(r.ot_v[...], r.ga_v[:, columns])
        arrived(load_at)
        return mm(r.at_v[...], r.qkv_v[:, columns])

    def after_product(i, g):
        k = chunks[groups[g][0]]
        if k.decoder:
            rhs.done()
            if last_use[k.name] == i:
                lhs.done()

    def wait_lhs(k):
        if k.name in lhs_names:
            arrived(lhs.copies[lhs_names.index(k.name)])

    def give(i, g):
        members = groups[g]
        wait_lhs(chunks[members[0]])
        buffers = [staging(c) for c in members]
        value = product(g, 1 - s).astype(BF16)
        for m, (c, buffer) in enumerate(zip(members, buffers)):
            k = chunks[c]
            part = value[:, m * k.width : (m + 1) * k.width]
            for j in range(16):
                buffer[shard(j)] = part[j * k.rows : (j + 1) * k.rows]
            chunk_copy(c, 0, buffer, r.acc[c], sibling)
        after_product(i, g)
        begin_some()

    def pair(i, g):
        both = groups[g]
        wait_lhs(chunks[both[0]])
        left = lhs.slots[lhs_names.index(DEC_DOWN)]
        side_rows = chunks[both[0]].half
        buffers = [staging(c) for c in both]
        for t in range(4):
            tile = rhs.take()
            for side, targets in ((1 - s, buffers), (s, [r.acc[c] for c in both])):
                at = pl.ds(pl.multiple_of(side * side_rows, side_rows), side_rows)
                value = mm(left[at, :], tile[...]).astype(BF16)
                for c, target in zip(both, targets):
                    k = chunks[c]
                    rows = slice(k.offset, k.offset + k.rows)
                    for j in range(4):
                        target[shard(4 * t + j)] = value[rows, j * k.width : (j + 1) * k.width]
            rhs.done()
        lhs.done()
        for c, buffer in zip(both, buffers):
            chunk_copy(c, 0, buffer, r.got[c], sibling)

    def spots(k, stage):
        fixed = {axis: here[axis] for axis in k.order[: stage - 1]}
        return [fixed.get(axis, slice(None)) for axis in (Z, Y, X)]

    def send_stage(c, stage):
        k = chunks[c]
        axis = k.order[stage - 1]
        for j, (coordinate, peer) in enumerate(peers[axis]):
            at = spots(k, stage)
            at[axis] = coordinate
            src = r.acc[c].at[tuple(at)]
            chunk_copy(c, first_slot[stage] + j, src, r.recv[stage - 1][c].at[j], peer)

    def got_stage(c, stage):
        k = chunks[c]
        count = len(peers[k.order[stage - 1]])
        for j in range(count):
            copies[c, first_slot[stage] + j].wait_recv()
        return count

    def add_stage(c, stage):
        k, acc, got = chunks[c], r.acc[c], r.recv[stage - 1][c]
        count = got_stage(c, stage)
        left = [axis for axis in (Z, Y, X) if axis not in k.order[:stage]]
        sizes = [(4, 2, 2)[axis] for axis in left]
        for j in range(math.prod(sizes)):
            place, rest = {}, j
            for axis, size in reversed(list(zip(left, sizes))):
                place[axis] = rest % size
                rest //= size
            at = tuple(place.get(axis, here[axis]) for axis in (Z, Y, X))
            index = tuple(place[axis] for axis in left)
            if count == 1:
                acc[at] = acc[at] + got[(0,) + index]
            else:
                total = acc[at].astype(F32)
                for m in range(count):
                    total = total + got[(m,) + index].astype(F32)
                acc[at] = total.astype(BF16)

    def stage1(i, g):
        members = groups[g]
        for c in members:
            copies[c, 0].wait_recv()
        if chunks[members[0]].turned:
            for c in members:
                acc = r.acc[c]
                for j in range(16):
                    acc[shard(j)] = acc[shard(j)] + r.got[c][shard(j)]
                send_stage(c, 1)
            return
        value = product(g, s)
        for m, c in enumerate(members):
            k, acc = chunks[c], r.acc[c]
            wide = value[:, m * k.width : (m + 1) * k.width]
            for j in range(16):
                part = wide[j * k.rows : (j + 1) * k.rows]
                acc[shard(j)] = (part + acc[shard(j)].astype(F32)).astype(BF16)
            send_stage(c, 1)
        after_product(i, g)

    def stage2(i, c):
        add_stage(c, 1)
        send_stage(c, 2)

    def stage3(i, c):
        add_stage(c, 2)
        send_stage(c, 3)

    def stage4(i, c):
        k = chunks[c]
        total = r.acc[c][here].astype(F32)
        for j in range(got_stage(c, 3)):
            total = total + r.recv[2][c][j].astype(F32)
        out = r.out[k.name]
        out[k.place(s)] = total.astype(BF16)
        final = out.at[k.place(s)]
        chunk_copy(c, 8, final, final, sibling)

    def stage5(i, c):
        copies[c, 8].wait_recv()

    small_copies = []

    def small_copy(source, peer):
        slot = len(small_copies)
        copy = remote(
            source, r.small_got.at[slot], r.small_sem.at[0, slot], r.small_sem.at[1, slot], peer
        )
        copy.start()
        small_copies.append(copy)

    def small_stage(stage):
        if stage < 4:
            small_copies[stage - 1].wait()
            total = small[...] + r.small_got[stage - 1]
            if stage < 3:
                small[...] = total
                small_copy(small, peers[X if stage == 1 else Y][0][1])
            else:
                r.small_sum[...] = total
                for _, peer in peers[Z]:
                    small_copy(r.small_sum, peer)
        else:
            total = r.small_sum[...]
            for j in range(3):
                small_copies[3 + j].wait()
                total = total + r.small_got[3 + j]
            r.out_small[...] = total

    def ffn(i, t):
        if t == 0:
            load_gy.wait()
            load_slope.wait()
            begin_some()
        at = slice(t * d_enc, (t + 1) * d_enc)
        gu = mm_nt(r.gy_v[...], weights.take()[...])
        weights.done()
        gf = (gu * r.slope_v[:, at].astype(F32)).astype(BF16)
        r.slope_v[:, at] = gf
        small[ROW_BUP + t : ROW_BUP + t + 1, :] = rows_sum(gf.astype(F32))
        gc = mm_nt(gf, weights.take()[...])
        weights.done()
        r.sum_v[...] = gc if t == 0 else r.sum_v[...] + gc

    def ln2(i, _):
        load_n2.wait()
        load_s2.wait()
        g, gc, n2 = r.gy_v[...].astype(F32), r.sum_v[...], r.n2_v[...]
        gh = g + normalise_back(gc, n2, r.s2_v[...], row(r.gain2))
        begin_some()
        small[2:3, :] = rows_sum(gh)
        small[3:4, :] = rows_sum(gc * n2)
        small[4:5, :] = rows_sum(gc)
        small[5:6, :] = rows_sum(g)
        r.n2_v[...] = gh
        r.ga_v[...] = gh.astype(BF16)

    def go(i, _):
        r.go_v[...] = mm_nt(r.ga_v[...], weights.take()[...]).astype(BF16)
        weights.done()

    def att(i, g):
        if g == 0:
            for copy in (load_qkv, load_o, load_rl):
                copy.wait()
        at = slice(g * 128, (g + 1) * 128)
        parts = [slice(j * d_enc + g * 128, j * d_enc + (g + 1) * 128) for j in range(3)]
        q, k, v = (r.qkv_v[:, part] for part in parts)
        grads = attention_backward_group(
            q, k, v, e_ring.take()[...], r.go_v[:, at], r.o_v[:, at], r.rl_v[:, at],
            d_enc // H_ENC,
        )
        e_ring.done()
        for part, grad in zip(parts, grads):
            r.qkv_v[:, part] = grad

    def gn(i, j):
        part = mm_nt(r.qkv_v[:, j * d_enc : (j + 1) * d_enc], weights.take()[...])
        weights.done()
        r.sum_v[...] = part if j == 0 else r.sum_v[...] + part

    def last(i, _):
        load_x.wait()
        n1, s1 = normalise(r.x_v[...].astype(F32))
        total = r.sum_v[...]
        small[0:1, :] = rows_sum(total * n1)
        small[1:2, :] = rows_sum(total)
        small_copy(small, sibling)
        gx = r.n2_v[...] + normalise_back(total, n1, s1, row(r.gain1))
        r.gx[...] = gx.astype(BF16)
        gx_away.start()
        decoded_away.start()

    run = {
        GIVE: give, PAIR: pair, FFN: ffn, LN2: ln2, GO: go, ATT: att, GN: gn, LAST: last,
        1: stage1, 2: stage2, 3: stage3, 4: stage4, 5: stage5,
    }
    for i, (name, arg) in enumerate(plan):
        if arg == SMALL:
            small_stage(name)
        else:
            run[name](i, arg)

    for c, slot in copies:
        sent_by(c, slot)
    gx_away.wait()
    decoded_away.wait()


def finish_buffers(chunks, rows, d, ff, dec_total, dec):
    def of(dtype, *dims):
        return (dims, dtype)

    return dict(
        y_v=of(BF16, rows, d),
        geb_v=of(BF16, rows, dec),
        gy_v=of(BF16, rows, d),
        slope_v=of(BF16, rows, ff),
        n2_v=of(F32, rows, d),
        s2_v=of(F32, rows, 1),
        qkv_v=of(BF16, rows, 3 * d),
        o_v=of(BF16, rows, d),
        rl_v=of(F32, rows, d),
        x_v=of(BF16, rows, d),
        ga_v=of(BF16, rows, d),
        go_v=of(BF16, rows, d),
        sum_v=of(F32, rows, d),
        ut_v=of(BF16, ff, rows),
        ct_v=of(BF16, d, rows),
        at_v=of(BF16, d, rows),
        ot_v=of(BF16, d, rows),
        e_v=of(BF16, 2, rows, 2 * rows),
        w=of(BF16, 4, d, d),
        lhs=of(BF16, 2, dec, dec_total),
        rhs=of(BF16, 2, dec_total, 768),
        small=of(F32, SMALL_ROWS, d),
        small_sum=of(F32, SMALL_ROWS, d),
        small_got=of(F32, 6, SMALL_ROWS, d),
    )


def finish(acts):
    enc, dec = acts["enc"], acts["dec"]
    gain1, _, w_qkv, w_out, _, gain2, _, w_up, _, w_down, _ = enc["params"]
    qkv, e, rl, o, n2, s2, slope = acts["saved"]
    given = dict(
        x=acts["x"], y=acts["y"], gy=acts["gy"], geb=acts["geb"], qkv=qkv, e=e, rl=rl, o=o, n2=n2,
        s2=s2, slope=slope, at=enc["at"], ot=enc["ot"], ct=enc["ct"], ut=enc["ut"], at2=dec["at"], ot2=dec["ot"],
        ct2=dec["ct"], gt2=dec["gt"], u2=dec["u"], gf2=dec["gf"], ga2=dec["ga"],
        gqkv2=dec["gqkv"], w_qkv=w_qkv, w_out=w_out, w_up=w_up, w_down=w_down,
        decoded=acts["decoded"].reshape(SAMP_MB, PATCHES, -1),
    )
    n_hbm = len(given)
    given.update(small2=acts["small2"], gbup2=acts["gbup2"], gain1=gain1, gain2=gain2)
    rows, d = acts["gy"].shape
    ff = w_up.shape[1]
    dec_d, dec_total = dec["at"].shape
    dec_ff = dec["u"].shape[1]
    chunks = make_chunks()
    n = len(chunks)
    groups = make_groups(chunks)
    plan = make_plan(chunks, groups)

    dims = {
        ENC_QKV: (d, 3 * d), ENC_OUT: (d, d), ENC_UP: (d, ff), ENC_DOWN: (ff, d),
        EMBED: (d, dec_d), DEC_QKV: (dec_d, 3 * dec_d), DEC_OUT: (dec_d, dec_d),
        DEC_UP: (dec_d, dec_ff), DEC_DOWN: (dec_ff, dec_d),
    }
    big = [
        shape(dims[k][1], dims[k][0] // 16) if k == DEC_DOWN else shape(dims[k][0] // 16, dims[k][1])
        for k in range(9)
    ]
    outs = dict(
        out_small=shape(SMALL_ROWS, d, F32),
        decoded_got=jax.ShapeDtypeStruct((SAMP_MB, PATCHES // 2, dec_d), BF16),
        gx=shape(rows, d),
        gx_got=shape(rows, d // 2),
    )
    single = finish_buffers(chunks, rows, d, ff, dec_total, dec_d)
    left = (4, 2, 2)
    lists = [[], [], [], [], []]
    for k in chunks:
        block = (k.rows, k.width)
        lists[0].append((left + block, BF16))
        if k.turned:
            lists[1].append((left + block, BF16))
        for stage in range(3):
            rest = [left[axis] for axis in (Z, Y, X) if axis not in k.order[: stage + 1]]
            count = 3 if k.order[stage] == Z else 1
            lists[2 + stage].append(((count, *rest, *block), BF16))
    blocks = sorted({(k.rows, k.width) for k in chunks})
    slots = [1] * len(blocks)
    lists.append([(left + block, BF16) for block, m in zip(blocks, slots) for _ in range(m)])
    semaphores = dict(
        load_sem=(LOADS,), send_sem=(n, 9), recv_sem=(n, 9), small_sem=(2, 6), swap_sem=(4,)
    )

    def kernel(*refs):
        refs = list(refs)

        def take(count):
            taken = refs[:count]
            del refs[:count]
            return taken

        names = list(given) + list(outs)
        r = Names(names, take(len(names)))
        r.out = take(9)
        r.__dict__.update(zip(single, take(len(single))))
        r.acc = take(n)
        r.got = dict(zip([c for c, k in enumerate(chunks) if k.turned], take(len(lists[1]))))
        r.recv = [take(n) for _ in range(3)]
        r.stage = {block: take(m) for block, m in zip(blocks, slots)}
        r.__dict__.update(zip(semaphores, take(len(semaphores))))
        finish_kernel(chunks, groups, plan, r)

    flat = list(single.values()) + [b for group in lists for b in group]
    results = pl.pallas_call(
        kernel,
        out_shape=list(outs.values()) + big,
        in_specs=[in_hbm()] * n_hbm + in_vmem(len(given) - n_hbm),
        out_specs=in_vmem(len(outs) + 9),
        scratch_shapes=[pltpu.VMEM(*b) for b in flat]
        + [pltpu.SemaphoreType.DMA(v) for v in semaphores.values()],
        compiler_params=pltpu.CompilerParams(
            collective_id=1, has_side_effects=True, vmem_limit_bytes=FINISH_VMEM
        ),
        name="finish",
    )(*given.values())
    return write_outputs(results, given["decoded"], dims)


FINISH_VMEM = 62 * 2**20


def write_kernel(small, decoded_got, gx_own, gx_got, *refs):
    big, decoded_own = refs[:9], refs[9]
    decoded, gx, *totals = refs[10:-1]
    sem = refs[-1]
    s = lax.axis_index("section")
    half = decoded.shape[1]
    samples, rows, columns = decoded_own.shape[0], gx_own.shape[0], gx.shape[1]
    own = decoded_own.at[:, pl.ds(pl.multiple_of(s * half, half), half), :]
    own_gx = gx_own.at[:, pl.ds(pl.multiple_of(s * columns, 128), columns)]
    copies = []
    for side, part, part_gx in ((s, own, own_gx), (1 - s, decoded_got, gx_got)):
        target = decoded.at[pl.ds(side * samples, samples)]
        copies.append(pltpu.make_async_copy(part, target, sem.at[len(copies)]))
        target = gx.at[pl.ds(pl.multiple_of(side * rows, rows), rows), :]
        copies.append(pltpu.make_async_copy(part_gx, target, sem.at[len(copies)]))
    for copy in copies:
        copy.start()
    d = lax.axis_index("dp")
    wide, narrow = small.shape[1], big[DEC_OUT].shape[1]

    def piece(out, line, lanes, position):
        size = out.shape[0]
        value = small[pl.ds(line, 1), :lanes]
        value = pltpu.roll(value, lax.rem(lanes - position * size, lanes), 1)
        out[...] = value[:, :size].reshape(size)

    def matrix(out, name):
        value = big[name][...].astype(F32)
        out[...] = jnp.transpose(value) if name == DEC_DOWN else value

    def block(outs, first_row, bup_row, lanes, names):
        for i, out in zip((0, 1, None, None, 2, 3, 4, None, None, None, 5), outs):
            if i is not None:
                piece(out, first_row + i, lanes, d)
        piece(outs[8], bup_row + d // 4, lanes, d % 4)
        for at, name in zip((2, 3, 7, 9), names):
            matrix(outs[at], name)

    block(totals[:11], 0, ROW_BUP, wide, (ENC_QKV, ENC_OUT, ENC_UP, ENC_DOWN))
    matrix(totals[11], EMBED)
    piece(totals[12], ROW_DEC + 7, narrow, d)
    piece(totals[13], ROW_DEC + 6, narrow, d)
    block(totals[14:], ROW_DEC, ROW_DEC_BUP, narrow, (DEC_QKV, DEC_OUT, DEC_UP, DEC_DOWN))
    for copy in copies:
        copy.wait()


def write_outputs(results, decoded_own, dims):
    def vector(size):
        return jax.ShapeDtypeStruct((size // 16,), F32)

    def matrix(name):
        return shape(dims[name][0] // 16, dims[name][1], F32)

    def block(qkv, out, up, down):
        d, ff = dims[up]
        return [
            vector(d), vector(d), matrix(qkv), matrix(out), vector(d), vector(d), vector(d),
            matrix(up), vector(ff), matrix(down), vector(d),
        ]

    samples, half, width = results[1].shape
    rows, columns = results[3].shape
    out_shape = [
        jax.ShapeDtypeStruct((2 * samples, half, width), BF16),
        shape(2 * rows, columns),
        *block(ENC_QKV, ENC_OUT, ENC_UP, ENC_DOWN),
        matrix(EMBED),
        vector(width),
        vector(width),
        *block(DEC_QKV, DEC_OUT, DEC_UP, DEC_DOWN),
    ]
    return tuple(
        pl.pallas_call(
            write_kernel,
            out_shape=out_shape,
            in_specs=in_vmem(len(results) + 1),
            out_specs=[in_hbm()] * 2 + in_vmem(len(out_shape) - 2),
            scratch_shapes=[pltpu.SemaphoreType.DMA((4,))],
            compiler_params=pltpu.CompilerParams(vmem_limit_bytes=KERNEL_VMEM),
            name="write_outputs",
        )(*results, decoded_own)
    )


def reduce_plain(arrays, section_index):
    first = section_index == 0
    results = []
    for a in arrays:
        half = a.shape[1] // 2
        keep = lax.dynamic_slice_in_dim(a, section_index * half, half, 1)
        give = lax.dynamic_slice_in_dim(a, (1 - section_index) * half, half, 1)
        got = swapped(give, "section", 0)
        chip = (keep.astype(jnp.float32) + got.astype(jnp.float32)).astype(jnp.bfloat16)
        mine = lax.psum_scatter(chip, "dp", scatter_dimension=0, tiled=True)
        other = swapped(mine, "section", 0)
        whole = jnp.concatenate(
            [jnp.where(first, mine, other), jnp.where(first, other, mine)], axis=1
        )
        results.append(whole.astype(jnp.float32))
    return results


def finish_plain(acts, section_index):
    x, gy, seg_saved, enc, dec = acts["x"], acts["gy"], acts["saved"], acts["enc"], acts["dec"]
    gx, gf1, ga1, gqkv1, small1, gbup1 = encoder_backward(x, gy, seg_saved, enc["params"])
    small2, gbup2 = acts["small2"], acts["gbup2"]
    grads = (
        small1[0], small1[1], mm(enc["at"], gqkv1).astype(BF16), mm(enc["ot"], ga1).astype(BF16), small1[2],
        small1[3], small1[4], mm(enc["ct"], gf1).astype(BF16), gbup1[0], mm(enc["ut"], gy).astype(BF16),
        small1[5],
        weight_grad(acts["y"], acts["geb"]), small2[7], small2[6],
        small2[0], small2[1], mm(dec["at"], dec["gqkv"]).astype(BF16),
        mm(dec["ot"], dec["ga"]).astype(BF16), small2[2], small2[3], small2[4],
        mm(dec["ct"], dec["gf"]).astype(BF16), gbup2[0],
        jnp.transpose(mm(dec["gt"], dec["u"])).astype(BF16), small2[5],
    )
    groups = lax.axis_size("dp")
    big = reduce_plain([g for g in grads if g.ndim == 2], section_index)
    flat = jnp.concatenate([g.reshape(groups, -1) for g in grads if g.ndim == 1], axis=1)
    line = lax.psum_scatter(flat, ("dp"), scatter_dimension=0, tiled=True)
    line = lax.psum(line, "section")[0]
    totals, at = [], 0
    for g in grads:
        if g.ndim == 2:
            totals.append(big.pop(0))
        else:
            size = g.shape[0] // groups
            totals.append(line[at : at + size])
            at += size
    decoded = acts["decoded"].reshape(SAMP_MB, PATCHES, -1)
    first = section_index == 0

    def halves(whole):
        half = whole.shape[1] // 2
        keep = lax.dynamic_slice_in_dim(whole, section_index * half, half, 1)
        give = lax.dynamic_slice_in_dim(whole, (1 - section_index) * half, half, 1)
        got = swapped(give, "section", 0)
        return jnp.concatenate([jnp.where(first, keep, got), jnp.where(first, got, keep)])

    return (halves(decoded), halves(gx), *totals)


def shards(
    patches,
    segment_ids,
    patch_order,
    encoder_gain1,
    encoder_bias1,
    encoder_qkv,
    encoder_out,
    encoder_out_bias,
    encoder_gain2,
    encoder_bias2,
    encoder_up,
    encoder_up_bias,
    encoder_down,
    encoder_down_bias,
    embed_weight,
    embed_bias,
    mask_token,
    decoder_gain1,
    decoder_bias1,
    decoder_qkv,
    decoder_out,
    decoder_out_bias,
    decoder_gain2,
    decoder_bias2,
    decoder_up,
    decoder_up_bias,
    decoder_down,
    decoder_down_bias,
    cotangent,
):
    enc_params = (
        encoder_gain1,
        encoder_bias1,
        encoder_qkv,
        encoder_out,
        encoder_out_bias,
        encoder_gain2,
        encoder_bias2,
        encoder_up,
        encoder_up_bias,
        encoder_down,
        encoder_down_bias,
    )
    embed_params = (embed_weight, embed_bias, mask_token)
    dec_params = (
        decoder_gain1,
        decoder_bias1,
        decoder_qkv,
        decoder_out,
        decoder_out_bias,
        decoder_gain2,
        decoder_bias2,
        decoder_up,
        decoder_up_bias,
        decoder_down,
        decoder_down_bias,
    )
    section_index = lax.axis_index("section")
    y, at1, qkv, e, rl, o1, ot1, n2, s2, ct1, ut1, slope = encoder_forward(
        patches, segment_ids, enc_params
    )
    g = cotangent.reshape(-1, DECODER_WIDTH)
    decoded, at2, ot2, ct2, gt2, u2, gf2, ga2, gqkv2, geb, gy, small2, gbup2 = decoder_both(
        y, segment_ids, patch_order, g, embed_params, dec_params
    )
    acts = dict(
        x=patches,
        y=y,
        gy=gy,
        geb=geb,
        decoded=decoded,
        small2=small2,
        gbup2=gbup2,
        saved=(qkv, e, rl, o1, n2, s2, slope),
        enc=dict(at=at1, ot=ot1, ct=ct1, ut=ut1, params=enc_params),
        dec=dict(at=at2, ot=ot2, ct=ct2, gt=gt2, u=u2, gf=gf2, ga=ga2, gqkv=gqkv2),
    )
    if lax.axis_size("dp") == 16:
        return finish(acts)
    return finish_plain(acts, section_index)


def solution(mesh):
    in_specs = (
        P("dp", None),
        P("dp", None),
        P("dp", None),
        P(),
        P(),
        P(),
        P(),
        P(),
        P(),
        P(),
        P(),
        P(),
        P(),
        P(),
        P(),
        P(),
        P(),
        P(),
        P(),
        P(),
        P(),
        P(),
        P(),
        P(),
        P(),
        P(),
        P(),
        P(),
        P("dp", None, None),
    )
    out_specs = (
        P("dp", "section", None),
        P("dp", "section"),
        P("dp"),
        P("dp"),
        P("dp", None),
        P("dp", None),
        P("dp"),
        P("dp"),
        P("dp"),
        P("dp", None),
        P("dp"),
        P("dp", None),
        P("dp"),
        P("dp", None),
        P("dp"),
        P("dp"),
        P("dp"),
        P("dp"),
        P("dp", None),
        P("dp", None),
        P("dp"),
        P("dp"),
        P("dp"),
        P("dp", None),
        P("dp"),
        P("dp", None),
        P("dp"),
    )
    return jax.shard_map(shards, mesh=mesh, in_specs=in_specs, out_specs=out_specs, check_vma=False)
```

```python
import functools
import math

import jax
import jax.numpy as jnp
import numpy as np
from jax import lax
from jax.experimental import pallas as pl
from jax.experimental.pallas import tpu as pltpu
from jax.sharding import PartitionSpec as P

H_ENC = 12
DECODER_WIDTH = 512
H_DEC = 16
PATCHES = 128
SAMP_MB = 12


EPSILON = 1e-06
MASKED = -1e30


def swapped(block, axis, apart):
    count = lax.axis_size(axis)
    route = []
    for low in range(count):
        high = low | 1 << apart
        if high != low and high < count:
            route += [(low, high), (high, low)]
    return lax.ppermute(block, axis, route)


def positions(count, features):
    column = np.arange(features)
    rate = np.exp(-math.log(10000.0) * (2 * (column // 2)) / features)
    angles = np.arange(count)[:, None] * rate[None, :]
    return np.where(column % 2 == 0, np.sin(angles), np.cos(angles)).astype(np.float32)


def weight_grad(left_side, grads):
    return lax.dot_general(
        left_side, grads, (((0,), (0,)), ((), ())), preferred_element_type=jnp.float32
    ).astype(jnp.bfloat16)


BF16 = jnp.bfloat16
F32 = jnp.float32


def mm(left, right):
    return lax.dot_general(left, right, (((1,), (0,)), ((), ())), preferred_element_type=F32)


def mm_nt(left, right):
    return lax.dot_general(left, right, (((1,), (1,)), ((), ())), preferred_element_type=F32)


def mm_tn(left, right):
    return lax.dot_general(left, right, (((0,), (0,)), ((), ())), preferred_element_type=F32)


def normalise(x):
    center = x - jnp.mean(x, axis=-1, keepdims=True)
    scale = lax.rsqrt(jnp.mean(center * center, axis=-1, keepdims=True) + EPSILON)
    return center * scale, scale


def normalise_back(grad, n, scale, gain):
    gn = grad * gain
    mean_gn = jnp.mean(gn, axis=-1, keepdims=True)
    mean_gnn = jnp.mean(gn * n, axis=-1, keepdims=True)
    return (gn - mean_gn - n * mean_gnn) * scale


def rows_sum(x):
    return jnp.sum(x, axis=0, keepdims=True)


def gelu_both(f):
    c0, c1 = math.sqrt(2.0 / math.pi), 0.044715
    square = f * f
    half = 0.5 + 0.5 * jnp.tanh(f * (c0 + (c0 * c1) * square))
    u = f * half
    return u, half + u * (1.0 - half) * (2.0 * c0 + (6.0 * c0 * c1) * square)


def lane_masks(head_size):
    lane = lax.broadcasted_iota(jnp.int32, (1, 128), 1)
    return [
        jnp.where((lane >= h * head_size) & (lane < (h + 1) * head_size), 1.0, 0.0).astype(BF16)
        for h in range(128 // head_size)
    ]


def stacked(x, masks):
    return jnp.concatenate([x * m for m in masks], axis=0)


def stacked_ones(x, masks, value):
    return jnp.concatenate(
        [jnp.broadcast_to(m * jnp.asarray(value, BF16), x.shape) for m in masks], axis=0
    )


def attention_forward(qkv_ref, o_ref, e_ref, rl_ref, rows, tokens, features, head_size, allowed):
    masks = lane_masks(head_size)
    per_group = len(masks)
    factor = head_size ** (-0.5) * math.log2(math.e)
    for g in range(features // 128):
        q, k, v = (qkv_ref[rows, j * features + g * 128 : j * features + (g + 1) * 128] for j in range(3))
        scores = mm_nt(q, stacked(k, masks))
        parts = []
        for h in range(per_group):
            part = scores[:, h * tokens : (h + 1) * tokens]
            if allowed is not None:
                part = jnp.where(allowed, part, MASKED)
            top = jnp.max(part, axis=-1, keepdims=True)
            parts.append(jnp.exp2((part - top) * factor).astype(BF16))
        e = jnp.concatenate(parts, axis=1)
        width = per_group * tokens
        e_ref[rows, g * width : (g + 1) * width] = e
        both = mm(e, jnp.concatenate([stacked(v, masks), stacked_ones(v, masks, 1.0)], axis=1))
        rl = 1.0 / both[:, 128:]
        rl_ref[rows, g * 128 : (g + 1) * 128] = rl
        o_ref[rows, g * 128 : (g + 1) * 128] = (both[:, :128] * rl).astype(BF16)


def attention_backward_group(q, k, v, e, go, o, rl, head_size):
    masks = lane_masks(head_size)
    per_group, tokens = len(masks), q.shape[0]
    scaling = head_size ** (-0.5)
    go = go.astype(F32) * rl
    go_low = go.astype(BF16)
    inner = (go * o.astype(F32)).astype(BF16)
    left = jnp.concatenate([go_low, inner], axis=1)
    right = jnp.concatenate([stacked(v, masks), stacked_ones(v, masks, -1.0)], axis=1)
    gs = (e.astype(F32) * mm_nt(left, right)).astype(BF16)

    def diagonal(wide):
        return jnp.concatenate(
            [
                wide[h * head_size : (h + 1) * head_size, h * tokens : (h + 1) * tokens]
                for h in range(per_group)
            ],
            axis=0,
        )

    gq = mm(gs, stacked(k, masks)) * scaling
    gk = jnp.transpose(diagonal(mm_tn(q, gs)) * scaling)
    gv = jnp.transpose(diagonal(mm_tn(go_low, e)))
    return gq.astype(BF16), gk.astype(BF16), gv.astype(BF16)


def attention_backward(
    qkv_ref, go_ref, o_ref, e_ref, rl_ref, gqkv_ref, rows, tokens, features, head_size
):
    width = 128 // head_size * tokens
    for g in range(features // 128):
        at = slice(g * 128, (g + 1) * 128)
        spots = [slice(j * features + g * 128, j * features + (g + 1) * 128) for j in range(3)]
        q, k, v = (qkv_ref[rows, spot] for spot in spots)
        e = e_ref[rows, g * width : (g + 1) * width]
        grads = attention_backward_group(
            q, k, v, e, go_ref[rows, at], o_ref[rows, at], rl_ref[rows, at], head_size
        )
        for spot, grad in zip(spots, grads):
            gqkv_ref[rows, spot] = grad


def feed_forward(c_ref, up_ref, bup_ref, u_ref, slope_ref, tile, ut_ref=None):
    for t in range(up_ref.shape[1] // tile):
        at = slice(t * tile, (t + 1) * tile)
        f = mm(c_ref[...], up_ref[:, at]) + bup_ref[at].reshape(1, tile)
        u, slope = gelu_both(f)
        u = u.astype(BF16)
        u_ref[:, at] = u
        slope_ref[:, at] = slope.astype(BF16)
        if ut_ref is not None:
            ut_ref[at, :] = jnp.transpose(u)


def feed_forward_back(gm_ref, down_ref, slope_ref, gf_ref, gbup_ref, tile):
    for t in range(down_ref.shape[0] // tile):
        at = slice(t * tile, (t + 1) * tile)
        gu = mm_nt(gm_ref[...], down_ref[at, :])
        gf = (gu * slope_ref[:, at].astype(F32)).astype(BF16)
        gf_ref[:, at] = gf
        gbup_ref[:, at] += rows_sum(gf.astype(F32))


def row(ref):
    return ref[...].reshape(1, -1)


def segment_mask(seg_ref, section):
    seg = seg_ref[pl.ds(section, 1), :].astype(F32)
    rows = seg.shape[1]
    column = jnp.transpose(jnp.broadcast_to(seg, (128, rows)))
    return jnp.concatenate([column] * (rows // 128), axis=1) == seg


class Writer:
    def __init__(self, semaphores):
        self.semaphores, self.copies = semaphores, []

    def start(self, source, target):
        copy = pltpu.make_async_copy(source, target, self.semaphores.at[len(self.copies)])
        copy.start()
        self.copies.append(copy)

    def wait(self):
        for copy in self.copies:
            copy.wait()


def encoder_forward_kernel(
    x_ref, seg_ref,
    gain1, bias1, w_qkv, w_out, b_out, gain2, bias2, w_up, b_up, w_down, b_down,
    *refs,
):
    outs, scratch = refs[:12], refs[12:24]
    y_ref, at_ref, qkv_ref, e_ref, rl_ref, o_ref, ot_ref, n2_ref, s2_ref, ct_ref, ut_ref, slope_ref = scratch
    h_ref, c_ref, u_ref, qkv_v, out_v, up_v, down_v, sem, out_sem = refs[24:]
    target = {id(v): o for v, o in zip(scratch, outs)}
    writer = Writer(out_sem)

    def write(*done):
        for v in done:
            writer.start(v, target[id(v)])

    tokens, features = y_ref.shape
    pairs = ((w_qkv, qkv_v), (w_out, out_v), (w_up, up_v), (w_down, down_v))
    loads = [pltpu.make_async_copy(w, v, sem.at[i]) for i, (w, v) in enumerate(pairs)]
    for load in loads:
        load.start()
    section = lax.axis_index("section")
    x = x_ref[pl.ds(pl.multiple_of(section * tokens, tokens), tokens), :].astype(F32)
    n1, _ = normalise(x)
    a = (n1 * row(gain1) + row(bias1)).astype(BF16)
    at_ref[...] = jnp.transpose(a)
    allowed = segment_mask(seg_ref, section)
    loads[0].wait()
    qkv_ref[...] = mm(a, qkv_v[...]).astype(BF16)
    write(at_ref, qkv_ref)
    attention_forward(
        qkv_ref, o_ref, e_ref, rl_ref, slice(None), tokens, features, features // H_ENC, allowed
    )
    ot_ref[...] = jnp.transpose(o_ref[...])
    write(e_ref, rl_ref, o_ref, ot_ref)
    loads[1].wait()
    h_ref[...] = x + (mm(o_ref[...], out_v[...]) + row(b_out))
    n2, s2 = normalise(h_ref[...])
    n2_ref[...] = n2
    s2_ref[...] = s2
    c_ref[...] = (n2 * row(gain2) + row(bias2)).astype(BF16)
    ct_ref[...] = jnp.transpose(c_ref[...])
    write(n2_ref, s2_ref, ct_ref)
    loads[2].wait()
    feed_forward(c_ref, up_v, b_up, u_ref, slope_ref, 512, ut_ref)
    write(ut_ref, slope_ref)
    loads[3].wait()
    y_ref[...] = (h_ref[...] + (mm(u_ref[...], down_v[...]) + row(b_down))).astype(BF16)
    write(y_ref)
    writer.wait()


def encoder_backward_kernel(
    x_ref, gy_ref, qkv_ref, e_ref, rl_ref, o_ref, n2_ref, s2_ref, slope_ref,
    gain1, w_qkv, w_out, gain2, w_up, w_down,
    gx_ref, gf_ref, ga_ref, gqkv_ref, small_ref, gbup_ref,
    gh_ref, go_ref,
):
    tokens, features = gy_ref.shape
    section = lax.axis_index("section")
    x = x_ref[pl.ds(pl.multiple_of(section * tokens, tokens), tokens), :].astype(F32)
    gbup_ref[...] = jnp.zeros_like(gbup_ref)
    feed_forward_back(gy_ref, w_down, slope_ref, gf_ref, gbup_ref, 512)
    gc = mm_nt(gf_ref[...], w_up[...])
    g = gy_ref[...].astype(F32)
    n2 = n2_ref[...]
    gh = g + normalise_back(gc, n2, s2_ref[...], row(gain2))
    gh_ref[...] = gh
    ga_ref[...] = gh.astype(BF16)
    small_ref[2:3, :] = rows_sum(gh)
    small_ref[3:4, :] = rows_sum(gc * n2)
    small_ref[4:5, :] = rows_sum(gc)
    small_ref[5:6, :] = rows_sum(g)
    go_ref[...] = mm_nt(ga_ref[...], w_out[...]).astype(BF16)
    attention_backward(
        qkv_ref, go_ref, o_ref, e_ref, rl_ref, gqkv_ref, slice(None), tokens, features,
        features // H_ENC,
    )
    gn = mm_nt(gqkv_ref[...], w_qkv[...])
    n1, s1 = normalise(x)
    small_ref[0:1, :] = rows_sum(gn * n1)
    small_ref[1:2, :] = rows_sum(gn)
    gx_ref[...] = (gh_ref[...] + normalise_back(gn, n1, s1, row(gain1))).astype(BF16)


def split_low(x):
    high = x.astype(BF16)
    return high, (x - high.astype(F32)).astype(BF16)


def place_slots(order_ref, seg, section, hot_ref, place_ref, empty_ref):
    packed = seg.shape[1]
    sample = lax.broadcasted_iota(jnp.int32, (16, packed), 0).astype(F32)
    starts = jnp.sum(jnp.where(seg < sample, 1.0, 0.0), axis=1, keepdims=True)
    counts = jnp.sum(jnp.where(seg == sample, 1.0, 0.0), axis=1, keepdims=True)
    line = lax.broadcasted_iota(jnp.int32, (PATCHES, PATCHES), 0).astype(F32)
    line_low = line.astype(BF16)
    lane_low = lax.broadcasted_iota(jnp.int32, (8, PATCHES), 1).astype(F32).astype(BF16)
    column = lax.broadcasted_iota(jnp.int32, (PATCHES, packed), 1).astype(F32)
    packed_line = lax.broadcasted_iota(jnp.int32, (packed, PATCHES), 0).astype(F32)
    for j in range(SAMP_MB):
        at = slice(j * PATCHES, (j + 1) * PATCHES)
        order = order_ref[pl.ds(section * SAMP_MB + j, 1), :].astype(F32)
        hit = jnp.where(order == line, 1.0, 0.0).astype(BF16)
        start, count = starts[j : j + 1, :], counts[j : j + 1, :]
        down, across = mm(hit, line_low), mm_nt(lane_low, hit)[:1, :]
        down = jnp.where(down < count, start + down, -1.0)
        across = jnp.where(across < count, start + across, -1.0)
        wide = jnp.concatenate([down] * (packed // PATCHES), axis=1)
        hot_ref[at, :] = jnp.where(column == wide, 1.0, 0.0).astype(BF16)
        place_ref[:, at] = jnp.where(packed_line == across, 1.0, 0.0).astype(BF16)
        empty_ref[at, :] = jnp.where(down < 0.0, 1.0, 0.0)


def decoder_kernel(
    y_ref, seg_ref, order_ref, pos_ref, g_hbm,
    w_embed_hbm, b_embed, mask_token,
    gain1, bias1, w_qkv_hbm, w_out_hbm, b_out, gain2, bias2, w_up_hbm, b_up, w_down_hbm, b_down,
    *refs,
):
    hbm, (geb_ref, gy_ref, small_ref, gbup_ref) = refs[:9], refs[9:13]
    buffers = refs[13:22]
    out_ref, at_ref, ot_ref, ct_ref, gt_ref, u_ref, gf_ref, ga_ref, gqkv_ref = buffers
    (
        e2_ref, z_ref, s1_ref, e_ref, rl_ref, h_ref, s2_ref, go_ref, ge_ref, o_ref, c_ref, qkv_ref,
        slope_ref, g_all, hot_ref, place_ref, empty_ref, w_embed, w_qkv, w_out, w_up, w_down,
        w_sem, out_sem,
    ) = refs[22:]
    packed = y_ref.shape[0]
    rows, features = z_ref.shape
    samples = rows // PATCHES
    head_size = features // H_DEC
    total = g_all.shape[0]
    section = lax.axis_index("section")
    mine = pl.ds(pl.multiple_of(section * total, total), total)
    pairs = (
        (w_embed_hbm, w_embed), (w_qkv_hbm, w_qkv), (w_out_hbm, w_out), (w_up_hbm, w_up),
        (w_down_hbm, w_down), (g_hbm.at[mine, :], g_all),
    )
    loads = [pltpu.make_async_copy(a, b, w_sem.at[i]) for i, (a, b) in enumerate(pairs)]
    for load in loads:
        load.start()

    def write(at, *which):
        copies = []
        for i in which:
            target = hbm[i].at[:, at] if 1 <= i <= 4 else hbm[i].at[at, :]
            copies.append(pltpu.make_async_copy(buffers[i], target, out_sem.at[i]))
            copies[-1].start()
        return copies

    small_ref[...] = jnp.zeros_like(small_ref)
    gbup_ref[...] = jnp.zeros_like(gbup_ref)
    ge_ref[...] = jnp.zeros_like(ge_ref)
    seg = seg_ref[pl.ds(section, 1), :].astype(F32)
    place_slots(order_ref, seg, section, hot_ref, place_ref, empty_ref)
    loads[0].wait()
    high, low = split_low(mm(y_ref[...], w_embed[...]) + row(b_embed))
    e2_ref[:packed, :] = high
    e2_ref[packed:, :] = low
    for load in loads[1:]:
        load.wait()

    def one_step(step, carry):
        here = pl.ds(pl.multiple_of(step * rows, rows), rows)
        one_hot = hot_ref[here, :]
        empty = jnp.concatenate([empty_ref[here, :]] * (features // 128), axis=1)
        twice = jnp.concatenate([one_hot, one_hot], axis=1)
        z = mm(twice, e2_ref[...]) + empty * row(mask_token)
        z = z + jnp.concatenate([pos_ref[...]] * samples, axis=0)
        n1, s1 = normalise(z)
        z_ref[...] = z
        s1_ref[...] = s1
        a = (n1 * row(gain1) + row(bias1)).astype(BF16)
        at_ref[...] = jnp.transpose(a)
        writing = write(here, 1)
        qkv_ref[...] = mm(a, w_qkv[...]).astype(BF16)

        def forward(b, carry):
            at = pl.ds(pl.multiple_of(b * PATCHES, PATCHES), PATCHES)
            attention_forward(qkv_ref, o_ref, e_ref, rl_ref, at, PATCHES, features, head_size, None)
            return carry

        lax.fori_loop(0, samples, forward, 0, unroll=2)
        ot_ref[...] = jnp.transpose(o_ref[...])
        h_ref[...] = z_ref[...] + (mm(o_ref[...], w_out[...]) + row(b_out))
        n2, s2 = normalise(h_ref[...])
        s2_ref[...] = s2
        c_ref[...] = (n2 * row(gain2) + row(bias2)).astype(BF16)
        ct_ref[...] = jnp.transpose(c_ref[...])
        feed_forward(c_ref, w_up, b_up, u_ref, slope_ref, 512)
        writing += write(here, 2, 3, 5)
        out_ref[...] = (h_ref[...] + (mm(u_ref[...], w_down[...]) + row(b_down))).astype(BF16)

        g_ref = g_all.at[here, :]
        gt_ref[...] = jnp.transpose(g_ref[...])
        feed_forward_back(g_ref, w_down, slope_ref, gf_ref, gbup_ref, 512)
        writing += write(here, 0, 4, 6)
        gc = mm_nt(gf_ref[...], w_up[...])
        g = g_ref[...].astype(F32)
        h = h_ref[...]
        n2 = (h - jnp.mean(h, axis=-1, keepdims=True)) * s2_ref[...]
        gh = g + normalise_back(gc, n2, s2_ref[...], row(gain2))
        small_ref[2:3, :] += rows_sum(gh)
        small_ref[3:4, :] += rows_sum(gc * n2)
        small_ref[4:5, :] += rows_sum(gc)
        small_ref[5:6, :] += rows_sum(g)
        h_ref[...] = gh
        ga_ref[...] = gh.astype(BF16)
        go_ref[...] = mm_nt(ga_ref[...], w_out[...]).astype(BF16)
        writing += write(here, 7)

        def backward(b, carry):
            at = pl.ds(pl.multiple_of(b * PATCHES, PATCHES), PATCHES)
            attention_backward(
                qkv_ref, go_ref, o_ref, e_ref, rl_ref, gqkv_ref, at, PATCHES, features, head_size
            )
            return carry

        lax.fori_loop(0, samples, backward, 0, unroll=2)
        writing += write(here, 8)
        gn = mm_nt(gqkv_ref[...], w_qkv[...])
        z = z_ref[...]
        n1 = (z - jnp.mean(z, axis=-1, keepdims=True)) * s1_ref[...]
        gz = h_ref[...] + normalise_back(gn, n1, s1_ref[...], row(gain1))
        small_ref[0:1, :] += rows_sum(gn * n1)
        small_ref[1:2, :] += rows_sum(gn)
        small_ref[6:7, :] += rows_sum(gz * empty)
        ge_ref[...] += mm(place_ref[:, here], gz.astype(BF16))
        for copy in writing:
            copy.wait()
        return carry

    lax.fori_loop(0, total // rows, one_step, 0)
    ge = ge_ref[...]
    small_ref[7:8, :] = rows_sum(ge)
    geb_ref[...] = ge.astype(BF16)
    gy_ref[...] = mm_nt(geb_ref[...], w_embed[...]).astype(BF16)


def in_vmem(count):
    return [pl.BlockSpec(memory_space=pltpu.VMEM)] * count


def in_hbm():
    return pl.BlockSpec(memory_space=pl.ANY)


def shape(rows, columns, dtype=BF16):
    return jax.ShapeDtypeStruct((rows, columns), dtype)


KERNEL_VMEM = 60 * 2**20


def encoder_forward(x, segments, params):
    rows, d = x.shape[0] // 2, x.shape[1]
    ff = params[7].shape[1]
    outs = [
        (rows, d, BF16),
        (d, rows, BF16),
        (rows, 3 * d, BF16),
        (rows, H_ENC * rows, BF16),
        (rows, d, F32),
        (rows, d, BF16),
        (d, rows, BF16),
        (rows, d, F32),
        (rows, 1, F32),
        (d, rows, BF16),
        (ff, rows, BF16),
        (rows, ff, BF16),
    ]
    more = [(rows, d, F32), (rows, d, BF16), (rows, ff, BF16)]
    args = [x, segments, *params]
    matrices = [w for w in params if w.dtype == BF16]
    return pl.pallas_call(
        encoder_forward_kernel,
        out_shape=[shape(*o) for o in outs],
        in_specs=in_vmem(2) + [in_hbm() if w.dtype == BF16 else in_vmem(1)[0] for w in params],
        out_specs=[in_hbm()] * len(outs),
        scratch_shapes=[pltpu.VMEM((r, w), t) for r, w, t in outs + more]
        + [pltpu.VMEM(w.shape, BF16) for w in matrices]
        + [pltpu.SemaphoreType.DMA((len(matrices),)), pltpu.SemaphoreType.DMA((len(outs),))],
        compiler_params=pltpu.CompilerParams(vmem_limit_bytes=KERNEL_VMEM),
        name="encoder_forward",
    )(*args)


def encoder_backward(x, gy, saved, params):
    gain1, _, w_qkv, w_out, _, gain2, _, w_up, _, w_down, _ = params
    rows, d = gy.shape
    ff = w_up.shape[1]
    outs = [
        shape(rows, d),
        shape(rows, ff),
        shape(rows, d),
        shape(rows, 3 * d),
        shape(8, d, F32),
        shape(1, ff, F32),
    ]
    args = [x, gy, *saved, gain1, w_qkv, w_out, gain2, w_up, w_down]
    return pl.pallas_call(
        encoder_backward_kernel,
        out_shape=outs,
        in_specs=in_vmem(len(args)),
        out_specs=in_vmem(len(outs)),
        scratch_shapes=[pltpu.VMEM((rows, d), F32), pltpu.VMEM((rows, d), BF16)],
        compiler_params=pltpu.CompilerParams(vmem_limit_bytes=KERNEL_VMEM),
        name="encoder_backward",
    )(*args)


def decoder_both(y, segments, orders, g, embed_params, params):
    packed, d_enc = y.shape
    total, d = g.shape[0] // 2, g.shape[1]
    rows = 6 * PATCHES
    ff = params[7].shape[1]
    args = [y, segments, orders, positions(PATCHES, d), g, *embed_params, *params]
    in_specs = in_vmem(4) + [in_hbm()]
    in_specs += [in_hbm() if x.dtype == BF16 else in_vmem(1)[0] for x in args[5:]]
    wide = [ff, ff, d, 3 * d]
    outs = [shape(total, d)] + [shape(d, total)] * 4 + [shape(total, w) for w in wide]
    buffers = [(rows, d, BF16)] + [(d, rows, BF16)] * 4 + [(rows, w, BF16) for w in wide]
    last = [shape(packed, d), shape(packed, d_enc), shape(8, d, F32), shape(1, ff, F32)]
    scratch = [
        (2 * packed, d, BF16),
        (rows, d, F32),
        (rows, 1, F32),
        (rows, H_DEC * PATCHES, BF16),
        (rows, d, F32),
        (rows, d, F32),
        (rows, 1, F32),
        (rows, d, BF16),
        (packed, d, F32),
        (rows, d, BF16),
        (rows, d, BF16),
        (rows, 3 * d, BF16),
        (rows, ff, BF16),
        (total, d, BF16),
        (total, packed, BF16),
        (packed, total, BF16),
        (total, 128, F32),
    ]
    matrices = [x for x in args[5:] if x.dtype == BF16]
    return pl.pallas_call(
        decoder_kernel,
        out_shape=outs + last,
        in_specs=in_specs,
        out_specs=[in_hbm()] * len(outs) + in_vmem(len(last)),
        scratch_shapes=[pltpu.VMEM((r, w), t) for r, w, t in buffers + scratch]
        + [pltpu.VMEM(x.shape, BF16) for x in matrices]
        + [pltpu.SemaphoreType.DMA((k,)) for k in (len(matrices) + 1, len(outs))],
        compiler_params=pltpu.CompilerParams(vmem_limit_bytes=KERNEL_VMEM),
        name="decoder_both",
    )(*args)


MESH = pl.DeviceIdType.MESH
ENC_QKV, ENC_OUT, ENC_UP, ENC_DOWN, EMBED, DEC_QKV, DEC_OUT, DEC_UP, DEC_DOWN = range(9)
GIVE, PAIR, FFN, LN2, GO, ATT, GN, LAST = range(10, 18)
SMALL = -1
ROW_BUP, ROW_DEC_BUP, ROW_DEC, SMALL_ROWS = 6, 10, 16, 24
Z, Y, X, CORE = range(4)
ORDERS = ((X, Y, Z), (Y, X, Z), (X, Z, Y), (Y, Z, X))


class Chunk:
    def __init__(self, name, half, offset, rows, width, first_row=None):
        self.name, self.half, self.offset, self.rows, self.width = name, half, offset, rows, width
        self.first_row, self.turned, self.order = first_row, name == DEC_DOWN, None
        self.decoder = name in (DEC_QKV, DEC_UP, DEC_OUT)

    def columns(self, side):
        return pl.ds(pl.multiple_of(side * self.half + self.offset, 128), self.width)

    def place(self, side):
        if self.turned:
            return (pl.ds(pl.multiple_of(side * self.half + self.offset, 128), self.rows), slice(None))
        if self.first_row is None:
            return (slice(None), self.columns(side))
        return (pl.ds(self.first_row, self.rows), self.columns(side))

    @property
    def bytes(self):
        return 32 * self.rows * self.width

    def loads(self, order):
        first, second, third = order
        if second == Z:
            return (self.bytes, self.bytes, self.bytes / 8)
        return (self.bytes, self.bytes / 2, self.bytes / 2)


def make_chunks():
    chunks = [Chunk(DEC_OUT, 256, 0, 32, 256), Chunk(DEC_QKV, 768, 0, 32, 768)]
    for q in range(2):
        chunks.append(Chunk(ENC_DOWN, 384, 0, 96, 384, 96 * q))
        chunks.append(Chunk(ENC_UP, 1536, 768 * q, 48, 768))
    chunks += [Chunk(ENC_OUT, 384, 0, 48, 384)]
    chunks += [Chunk(ENC_QKV, 1152, 0, 48, 768), Chunk(ENC_QKV, 1152, 768, 48, 384)]
    chunks += [Chunk(EMBED, 256, 0, 48, 256), Chunk(DEC_DOWN, 256, 0, 256, 128)]
    chunks += [Chunk(DEC_UP, 1024, o, 32, 512) for o in (0, 512)]
    for c, chunk in enumerate(chunks):
        chunk.order = ORDERS[c % 2]

    def busiest():
        load = [0.0, 0.0, 0.0]
        for chunk in chunks:
            for axis, size in zip(chunk.order, chunk.loads(chunk.order)):
                load[axis] += size
        return sorted(load, reverse=True)

    best, better = busiest(), True
    while better:
        better = False
        for chunk in chunks:
            for order in ORDERS:
                before, chunk.order = chunk.order, order
                if busiest() < best:
                    best, better = busiest(), True
                else:
                    chunk.order = before
    return chunks


def make_groups(chunks):
    return [[c] for c in range(len(chunks))]


def product_cost(k, count):
    if k.turned:
        return 6.0
    return k.rows * k.width * (1.1 / 8192 if k.decoder else 0.7 / 18432)


def tasks_in_order(chunks, groups):
    def gives(name):
        found = [(g, chunks[m[0]], len(m)) for g, m in enumerate(groups)]
        kind = PAIR if name == DEC_DOWN else GIVE
        return [(kind, g, product_cost(k, size)) for g, k, size in found if k.name == name]

    tasks = gives(DEC_OUT) + gives(DEC_QKV)
    tasks += [(FFN, t, 2.5) for t in range(4)]
    for pair in zip(gives(ENC_DOWN), gives(ENC_UP)):
        tasks += pair
    tasks += [(LN2, 0, 1.5), (GO, 0, 1.2)]
    tasks += [(ATT, g, 2.2) for g in range(6)]
    tasks += gives(ENC_OUT) + gives(ENC_QKV)
    tasks += [(GN, j, 1.2) for j in range(3)] + [(LAST, 0, 2.0)]
    return tasks + gives(EMBED) + gives(DEC_DOWN) + gives(DEC_UP)


def decoder_arrays(chunks):
    names = []
    for k in chunks:
        if (k.decoder or k.turned) and k.name not in names:
            names.append(k.name)
    return names


def make_plan(chunks, groups):
    tasks = tasks_in_order(chunks, groups)
    lhs = decoder_arrays(chunks)
    free = [0.0] * 4
    rate = [82e3, 82e3, 82e3, 500e3]
    pending, plan, now, owned = [], [], 2.0, set()

    def send(link, size, latency):
        begin = max(now, free[link])
        free[link] = begin + size / rate[link]
        return free[link] + latency

    def blocked(task):
        if task[0] not in (GIVE, PAIR):
            return False
        name = chunks[groups[task[1]][0]].name
        if name not in lhs[2:]:
            return False
        name = lhs[lhs.index(name) - 2]
        return any(chunks[m[0]].name == name and g not in owned for g, m in enumerate(groups))

    while tasks or pending:
        pending.sort()
        if pending and (pending[0][0] <= now or not tasks or blocked(tasks[0])):
            arrive, stage, c = pending.pop(0)
            now = max(now, arrive)
            plan.append((stage, c))
            if c == SMALL:
                now += 0.1
                if stage < 4:
                    pending.append((now + 2.0, stage + 1, c))
                continue
            members = groups[c] if stage == 1 else [c]
            k = chunks[members[0]]
            if stage == 1:
                owned.add(c)
                now += 0.6 if k.turned else product_cost(k, len(members)) + 0.2 * len(members)
            else:
                now += 0.25
            for c in members:
                k = chunks[c]
                if stage < 4:
                    axis = k.order[stage - 1]
                    latency = 2.0 if axis == Z else 1.5
                    arrive = send(axis, k.loads(k.order)[stage - 1], latency)
                    pending.append((arrive, stage + 1, c))
                elif stage == 4:
                    pending.append((send(CORE, k.bytes / 16, 1.0), 5, c))
            continue
        name, arg, cost = tasks.pop(0)
        plan.append((name, arg))
        now += cost
        if name in (GIVE, PAIR):
            arrive = [send(CORE, chunks[c].bytes, 1.0) for c in groups[arg]]
            pending.append((max(arrive), 1, arg))
        elif name == LAST:
            pending.append((now + 2.0, 1, SMALL))
    return plan


class Ring:
    def __init__(self, sources, slots, semaphores, depth):
        self.copies = [
            pltpu.make_async_copy(source, slot, semaphores())
            for source, slot in zip(sources, slots)
        ]
        self.slots, self.depth, self.at = slots, depth, 0

    def begin(self):
        for copy in self.copies[: self.depth]:
            copy.start()

    def take(self):
        self.copies[self.at].wait()
        return self.slots[self.at]

    def done(self):
        ahead = self.at + self.depth
        if ahead < len(self.copies):
            self.copies[ahead].start()
        self.at += 1


class Names:
    def __init__(self, names, refs):
        self.__dict__.update(zip(names, refs))


LOADS = 96


def finish_kernel(chunks, groups, plan, r):
    n = len(chunks)
    s = lax.axis_index("section")
    d = lax.axis_index("dp")
    here = (d // 4, (d // 2) % 2, d % 2)
    z, y, x = here
    sibling = {"section": 1 - s}
    z_at = [lax.rem(z + k, 4) for k in (1, 2, 3)]
    peers = {
        X: [(1 - x, {"dp": d + 1 - 2 * x})],
        Y: [(1 - y, {"dp": d + 2 - 4 * y})],
        Z: [(p, {"dp": d + 4 * (p - z)}) for p in z_at],
    }
    every = [sibling] + [peer for axis in (X, Y, Z) for _, peer in peers[axis]]

    barrier = pltpu.get_barrier_semaphore()
    for peer in every:
        pl.semaphore_signal(barrier, inc=1, device_id=peer, device_id_type=MESH)

    counter = iter(range(LOADS))

    def semaphore():
        return r.load_sem.at[next(counter)]

    def remote(src, dst, send, recv, peer):
        return pltpu.make_async_remote_copy(
            src_ref=src, dst_ref=dst, send_sem=send, recv_sem=recv, device_id=peer, device_id_type=MESH
        )

    rhs_of = {DEC_QKV: r.gqkv2, DEC_UP: r.gf2, DEC_OUT: r.ga2}
    lhs_of = {DEC_QKV: r.at2, DEC_UP: r.ct2, DEC_OUT: r.ot2, DEC_DOWN: r.gt2}
    tiles, widths, last_use = [], [], {}

    def wide_columns(g, side):
        k, width = chunks[groups[g][0]], sum(chunks[c].width for c in groups[g])
        return pl.ds(pl.multiple_of(side * k.half + k.offset, 128), width)

    for i, (name, arg) in enumerate(plan):
        if name == PAIR:
            tiles += [r.u2.at[:, t * 512 : (t + 1) * 512] for t in range(4)]
            last_use[DEC_DOWN] = i
        elif name in (GIVE, 1) and arg != SMALL and chunks[groups[arg][0]].decoder:
            k = chunks[groups[arg][0]]
            tiles.append(rhs_of[k.name].at[:, wide_columns(arg, 1 - s if name == GIVE else s)])
            last_use[k.name] = i
    lhs_names = decoder_arrays(chunks)
    assert sorted(lhs_names, key=last_use.get) == lhs_names
    rhs_slots = [r.rhs.at[i % 2, :, : tile.shape[1]] for i, tile in enumerate(tiles)]
    rhs = Ring(tiles, rhs_slots, semaphore, 2)
    lhs = Ring([lhs_of[k] for k in lhs_names], [r.lhs.at[i % 2] for i in range(4)], semaphore, 2)
    lhs.copies[0].start()
    rhs.begin()
    lhs.copies[1].start()
    tokens, d_enc = r.gy.shape
    blocks = []
    for t in range(4):
        at = pl.ds(t * d_enc, d_enc)
        blocks += [r.w_down.at[at, :], r.w_up.at[:, at]]
    blocks.append(r.w_out)
    blocks += [r.w_qkv.at[:, pl.ds(j * d_enc, d_enc)] for j in range(3)]
    weights = Ring(blocks, [r.w.at[i % 4] for i in range(12)], semaphore, 4)
    e_width = 2 * tokens
    e_ring = Ring(
        [r.e.at[:, pl.ds(g * e_width, e_width)] for g in range(6)],
        [r.e_v.at[g % 2] for g in range(6)],
        semaphore,
        2,
    )

    def load(source, target):
        return pltpu.make_async_copy(source, target, semaphore())

    mine = pl.ds(pl.multiple_of(s * tokens, tokens), tokens)
    load_gy, load_slope, load_ut = load(r.gy, r.gy_v), load(r.slope, r.slope_v), load(r.ut, r.ut_v)
    load_ct, load_at, load_ot = load(r.ct, r.ct_v), load(r.at, r.at_v), load(r.ot, r.ot_v)
    load_n2, load_s2, load_qkv = load(r.n2, r.n2_v), load(r.s2, r.s2_v), load(r.qkv, r.qkv_v)
    load_o, load_rl, load_x = load(r.o, r.o_v), load(r.rl, r.rl_v), load(r.x.at[mine, :], r.x_v)
    load_y, load_geb = load(r.y, r.y_v), load(r.geb, r.geb_v)
    begun = [
        (load_gy, load_slope, weights),
        (load_ut, load_ct, load_n2, load_s2),
        (load_qkv, load_o, load_rl, e_ring),
        (load_ot, load_at, load_x, load_y, load_geb),
    ]

    def begin_some():
        for copy in begun.pop(0) if begun else ():
            copy.begin() if isinstance(copy, Ring) else copy.start()

    half = r.decoded.shape[1] // 2
    give_half = r.decoded.at[:, pl.ds(pl.multiple_of((1 - s) * half, half), half), :]
    decoded_away = remote(give_half, r.decoded_got, r.swap_sem.at[0], r.swap_sem.at[1], sibling)
    gx_columns = d_enc // 2
    gx_half = r.gx.at[:, pl.ds(pl.multiple_of((1 - s) * gx_columns, 128), gx_columns)]
    gx_away = remote(gx_half, r.gx_got, r.swap_sem.at[2], r.swap_sem.at[3], sibling)

    small = r.small
    small[...] = jnp.zeros_like(small)
    small[ROW_DEC : ROW_DEC + 8, : r.small2.shape[1]] = r.small2[...]
    quarter = r.gbup2.shape[1] // 4
    for i in range(4):
        piece = r.gbup2[:, i * quarter : (i + 1) * quarter]
        small[ROW_DEC_BUP + i : ROW_DEC_BUP + i + 1, :quarter] = piece

    pl.semaphore_wait(barrier, len(every))
    decoded_away.start()

    copies = {}
    first_slot = (0, 1, 2, 5, 8)

    def chunk_copy(c, slot, src, dst, peer):
        copy = remote(src, dst, r.send_sem.at[c, slot], r.recv_sem.at[c, slot], peer)
        copy.start()
        copies[c, slot] = copy

    sent = set()

    def sent_by(c, slot):
        if (c, slot) not in sent:
            sent.add((c, slot))
            copies[c, slot].wait_send()

    staged = {}

    def staging(c):
        k = chunks[c]
        buffers = r.stage[k.rows, k.width]
        turn = staged.setdefault((k.rows, k.width), [])
        if len(turn) >= len(buffers):
            sent_by(turn[-len(buffers)], 0)
        turn.append(c)
        return buffers[(len(turn) - 1) % len(buffers)]

    def shard(i):
        return (i // 4, (i // 2) % 2, i % 2)

    waited = set()

    def arrived(copy):
        if id(copy) not in waited:
            waited.add(id(copy))
            copy.wait()

    def product(g, side):
        k, columns = chunks[groups[g][0]], wide_columns(g, side)
        if k.decoder:
            return mm(lhs.slots[lhs_names.index(k.name)][...], rhs.take()[...])
        if k.name == EMBED:
            arrived(load_y)
            arrived(load_geb)
            return mm_tn(r.y_v[...], r.geb_v[:, columns])
        if k.name == ENC_DOWN:
            arrived(load_ut)
            at = [i * 192 + k.first_row for i in range(16)]
            left = jnp.concatenate([r.ut_v[i : i + k.rows, :] for i in at], axis=0)
            return mm(left, r.gy_v[:, columns])
        if k.name == ENC_UP:
            arrived(load_ct)
            return mm(r.ct_v[...], r.slope_v[:, columns])
        if k.name == ENC_OUT:
            arrived(load_ot)
            return mm(r.ot_v[...], r.ga_v[:, columns])
        arrived(load_at)
        return mm(r.at_v[...], r.qkv_v[:, columns])

    def after_product(i, g):
        k = chunks[groups[g][0]]
        if k.decoder:
            rhs.done()
            if last_use[k.name] == i:
                lhs.done()

    def wait_lhs(k):
        if k.name in lhs_names:
            arrived(lhs.copies[lhs_names.index(k.name)])

    def give(i, g):
        members = groups[g]
        wait_lhs(chunks[members[0]])
        buffers = [staging(c) for c in members]
        value = product(g, 1 - s).astype(BF16)
        for m, (c, buffer) in enumerate(zip(members, buffers)):
            k = chunks[c]
            part = value[:, m * k.width : (m + 1) * k.width]
            for j in range(16):
                buffer[shard(j)] = part[j * k.rows : (j + 1) * k.rows]
            chunk_copy(c, 0, buffer, r.acc[c], sibling)
        after_product(i, g)
        begin_some()

    def pair(i, g):
        both = groups[g]
        wait_lhs(chunks[both[0]])
        left = lhs.slots[lhs_names.index(DEC_DOWN)]
        side_rows = chunks[both[0]].half
        buffers = [staging(c) for c in both]
        for t in range(4):
            tile = rhs.take()
            for side, targets in ((1 - s, buffers), (s, [r.acc[c] for c in both])):
                at = pl.ds(pl.multiple_of(side * side_rows, side_rows), side_rows)
                value = mm(left[at, :], tile[...]).astype(BF16)
                for c, target in zip(both, targets):
                    k = chunks[c]
                    rows = slice(k.offset, k.offset + k.rows)
                    for j in range(4):
                        target[shard(4 * t + j)] = value[rows, j * k.width : (j + 1) * k.width]
            rhs.done()
        lhs.done()
        for c, buffer in zip(both, buffers):
            chunk_copy(c, 0, buffer, r.got[c], sibling)

    def spots(k, stage):
        fixed = {axis: here[axis] for axis in k.order[: stage - 1]}
        return [fixed.get(axis, slice(None)) for axis in (Z, Y, X)]

    def send_stage(c, stage):
        k = chunks[c]
        axis = k.order[stage - 1]
        for j, (coordinate, peer) in enumerate(peers[axis]):
            at = spots(k, stage)
            at[axis] = coordinate
            src = r.acc[c].at[tuple(at)]
            chunk_copy(c, first_slot[stage] + j, src, r.recv[stage - 1][c].at[j], peer)

    def got_stage(c, stage):
        k = chunks[c]
        count = len(peers[k.order[stage - 1]])
        for j in range(count):
            copies[c, first_slot[stage] + j].wait_recv()
        return count

    def add_stage(c, stage):
        k, acc, got = chunks[c], r.acc[c], r.recv[stage - 1][c]
        count = got_stage(c, stage)
        left = [axis for axis in (Z, Y, X) if axis not in k.order[:stage]]
        sizes = [(4, 2, 2)[axis] for axis in left]
        for j in range(math.prod(sizes)):
            place, rest = {}, j
            for axis, size in reversed(list(zip(left, sizes))):
                place[axis] = rest % size
                rest //= size
            at = tuple(place.get(axis, here[axis]) for axis in (Z, Y, X))
            index = tuple(place[axis] for axis in left)
            if count == 1:
                acc[at] = acc[at] + got[(0,) + index]
            else:
                total = acc[at].astype(F32)
                for m in range(count):
                    total = total + got[(m,) + index].astype(F32)
                acc[at] = total.astype(BF16)

    def stage1(i, g):
        members = groups[g]
        for c in members:
            copies[c, 0].wait_recv()
        if chunks[members[0]].turned:
            for c in members:
                acc = r.acc[c]
                for j in range(16):
                    acc[shard(j)] = acc[shard(j)] + r.got[c][shard(j)]
                send_stage(c, 1)
            return
        value = product(g, s)
        for m, c in enumerate(members):
            k, acc = chunks[c], r.acc[c]
            wide = value[:, m * k.width : (m + 1) * k.width]
            for j in range(16):
                part = wide[j * k.rows : (j + 1) * k.rows]
                acc[shard(j)] = (part + acc[shard(j)].astype(F32)).astype(BF16)
            send_stage(c, 1)
        after_product(i, g)

    def stage2(i, c):
        add_stage(c, 1)
        send_stage(c, 2)

    def stage3(i, c):
        add_stage(c, 2)
        send_stage(c, 3)

    def stage4(i, c):
        k = chunks[c]
        total = r.acc[c][here].astype(F32)
        for j in range(got_stage(c, 3)):
            total = total + r.recv[2][c][j].astype(F32)
        out = r.out[k.name]
        out[k.place(s)] = total.astype(BF16)
        final = out.at[k.place(s)]
        chunk_copy(c, 8, final, final, sibling)

    def stage5(i, c):
        copies[c, 8].wait_recv()

    small_copies = []

    def small_copy(source, peer):
        slot = len(small_copies)
        copy = remote(
            source, r.small_got.at[slot], r.small_sem.at[0, slot], r.small_sem.at[1, slot], peer
        )
        copy.start()
        small_copies.append(copy)

    def small_stage(stage):
        if stage < 4:
            small_copies[stage - 1].wait()
            total = small[...] + r.small_got[stage - 1]
            if stage < 3:
                small[...] = total
                small_copy(small, peers[X if stage == 1 else Y][0][1])
            else:
                r.small_sum[...] = total
                for _, peer in peers[Z]:
                    small_copy(r.small_sum, peer)
        else:
            total = r.small_sum[...]
            for j in range(3):
                small_copies[3 + j].wait()
                total = total + r.small_got[3 + j]
            r.out_small[...] = total

    def ffn(i, t):
        if t == 0:
            load_gy.wait()
            load_slope.wait()
            begin_some()
        at = slice(t * d_enc, (t + 1) * d_enc)
        gu = mm_nt(r.gy_v[...], weights.take()[...])
        weights.done()
        gf = (gu * r.slope_v[:, at].astype(F32)).astype(BF16)
        r.slope_v[:, at] = gf
        small[ROW_BUP + t : ROW_BUP + t + 1, :] = rows_sum(gf.astype(F32))
        gc = mm_nt(gf, weights.take()[...])
        weights.done()
        r.sum_v[...] = gc if t == 0 else r.sum_v[...] + gc

    def ln2(i, _):
        load_n2.wait()
        load_s2.wait()
        g, gc, n2 = r.gy_v[...].astype(F32), r.sum_v[...], r.n2_v[...]
        gh = g + normalise_back(gc, n2, r.s2_v[...], row(r.gain2))
        begin_some()
        small[2:3, :] = rows_sum(gh)
        small[3:4, :] = rows_sum(gc * n2)
        small[4:5, :] = rows_sum(gc)
        small[5:6, :] = rows_sum(g)
        r.n2_v[...] = gh
        r.ga_v[...] = gh.astype(BF16)

    def go(i, _):
        r.go_v[...] = mm_nt(r.ga_v[...], weights.take()[...]).astype(BF16)
        weights.done()

    def att(i, g):
        if g == 0:
            for copy in (load_qkv, load_o, load_rl):
                copy.wait()
        at = slice(g * 128, (g + 1) * 128)
        parts = [slice(j * d_enc + g * 128, j * d_enc + (g + 1) * 128) for j in range(3)]
        q, k, v = (r.qkv_v[:, part] for part in parts)
        grads = attention_backward_group(
            q, k, v, e_ring.take()[...], r.go_v[:, at], r.o_v[:, at], r.rl_v[:, at],
            d_enc // H_ENC,
        )
        e_ring.done()
        for part, grad in zip(parts, grads):
            r.qkv_v[:, part] = grad

    def gn(i, j):
        part = mm_nt(r.qkv_v[:, j * d_enc : (j + 1) * d_enc], weights.take()[...])
        weights.done()
        r.sum_v[...] = part if j == 0 else r.sum_v[...] + part

    def last(i, _):
        load_x.wait()
        n1, s1 = normalise(r.x_v[...].astype(F32))
        total = r.sum_v[...]
        small[0:1, :] = rows_sum(total * n1)
        small[1:2, :] = rows_sum(total)
        small_copy(small, sibling)
        gx = r.n2_v[...] + normalise_back(total, n1, s1, row(r.gain1))
        r.gx[...] = gx.astype(BF16)
        gx_away.start()

    run = {
        GIVE: give, PAIR: pair, FFN: ffn, LN2: ln2, GO: go, ATT: att, GN: gn, LAST: last,
        1: stage1, 2: stage2, 3: stage3, 4: stage4, 5: stage5,
    }
    for i, (name, arg) in enumerate(plan):
        if arg == SMALL:
            small_stage(name)
        else:
            run[name](i, arg)

    for c, slot in copies:
        sent_by(c, slot)
    gx_away.wait()
    decoded_away.wait()


def finish_buffers(chunks, rows, d, ff, dec_total, dec):
    def of(dtype, *dims):
        return (dims, dtype)

    return dict(
        y_v=of(BF16, rows, d),
        geb_v=of(BF16, rows, dec),
        gy_v=of(BF16, rows, d),
        slope_v=of(BF16, rows, ff),
        n2_v=of(F32, rows, d),
        s2_v=of(F32, rows, 1),
        qkv_v=of(BF16, rows, 3 * d),
        o_v=of(BF16, rows, d),
        rl_v=of(F32, rows, d),
        x_v=of(BF16, rows, d),
        ga_v=of(BF16, rows, d),
        go_v=of(BF16, rows, d),
        sum_v=of(F32, rows, d),
        ut_v=of(BF16, ff, rows),
        ct_v=of(BF16, d, rows),
        at_v=of(BF16, d, rows),
        ot_v=of(BF16, d, rows),
        e_v=of(BF16, 2, rows, 2 * rows),
        w=of(BF16, 4, d, d),
        lhs=of(BF16, 2, dec, dec_total),
        rhs=of(BF16, 2, dec_total, 768),
        small=of(F32, SMALL_ROWS, d),
        small_sum=of(F32, SMALL_ROWS, d),
        small_got=of(F32, 6, SMALL_ROWS, d),
    )


def finish(acts):
    enc, dec = acts["enc"], acts["dec"]
    gain1, _, w_qkv, w_out, _, gain2, _, w_up, _, w_down, _ = enc["params"]
    qkv, e, rl, o, n2, s2, slope = acts["saved"]
    given = dict(
        x=acts["x"], y=acts["y"], gy=acts["gy"], geb=acts["geb"], qkv=qkv, e=e, rl=rl, o=o, n2=n2,
        s2=s2, slope=slope, at=enc["at"], ot=enc["ot"], ct=enc["ct"], ut=enc["ut"], at2=dec["at"], ot2=dec["ot"],
        ct2=dec["ct"], gt2=dec["gt"], u2=dec["u"], gf2=dec["gf"], ga2=dec["ga"],
        gqkv2=dec["gqkv"], w_qkv=w_qkv, w_out=w_out, w_up=w_up, w_down=w_down,
        decoded=acts["decoded"].reshape(SAMP_MB, PATCHES, -1),
    )
    n_hbm = len(given)
    given.update(small2=acts["small2"], gbup2=acts["gbup2"], gain1=gain1, gain2=gain2)
    rows, d = acts["gy"].shape
    ff = w_up.shape[1]
    dec_d, dec_total = dec["at"].shape
    dec_ff = dec["u"].shape[1]
    chunks = make_chunks()
    n = len(chunks)
    groups = make_groups(chunks)
    plan = make_plan(chunks, groups)

    dims = {
        ENC_QKV: (d, 3 * d), ENC_OUT: (d, d), ENC_UP: (d, ff), ENC_DOWN: (ff, d),
        EMBED: (d, dec_d), DEC_QKV: (dec_d, 3 * dec_d), DEC_OUT: (dec_d, dec_d),
        DEC_UP: (dec_d, dec_ff), DEC_DOWN: (dec_ff, dec_d),
    }
    big = [
        shape(dims[k][1], dims[k][0] // 16) if k == DEC_DOWN else shape(dims[k][0] // 16, dims[k][1])
        for k in range(9)
    ]
    outs = dict(
        out_small=shape(SMALL_ROWS, d, F32),
        decoded_got=jax.ShapeDtypeStruct((SAMP_MB, PATCHES // 2, dec_d), BF16),
        gx=shape(rows, d),
        gx_got=shape(rows, d // 2),
    )
    single = finish_buffers(chunks, rows, d, ff, dec_total, dec_d)
    left = (4, 2, 2)
    lists = [[], [], [], [], []]
    for k in chunks:
        block = (k.rows, k.width)
        lists[0].append((left + block, BF16))
        if k.turned:
            lists[1].append((left + block, BF16))
        for stage in range(3):
            rest = [left[axis] for axis in (Z, Y, X) if axis not in k.order[: stage + 1]]
            count = 3 if k.order[stage] == Z else 1
            lists[2 + stage].append(((count, *rest, *block), BF16))
    blocks = sorted({(k.rows, k.width) for k in chunks})
    slots = [1] * len(blocks)
    lists.append([(left + block, BF16) for block, m in zip(blocks, slots) for _ in range(m)])
    semaphores = dict(
        load_sem=(LOADS,), send_sem=(n, 9), recv_sem=(n, 9), small_sem=(2, 6), swap_sem=(4,)
    )

    def kernel(*refs):
        refs = list(refs)

        def take(count):
            taken = refs[:count]
            del refs[:count]
            return taken

        names = list(given) + list(outs)
        r = Names(names, take(len(names)))
        r.out = take(9)
        r.__dict__.update(zip(single, take(len(single))))
        r.acc = take(n)
        r.got = dict(zip([c for c, k in enumerate(chunks) if k.turned], take(len(lists[1]))))
        r.recv = [take(n) for _ in range(3)]
        r.stage = {block: take(m) for block, m in zip(blocks, slots)}
        r.__dict__.update(zip(semaphores, take(len(semaphores))))
        finish_kernel(chunks, groups, plan, r)

    flat = list(single.values()) + [b for group in lists for b in group]
    results = pl.pallas_call(
        kernel,
        out_shape=list(outs.values()) + big,
        in_specs=[in_hbm()] * n_hbm + in_vmem(len(given) - n_hbm),
        out_specs=in_vmem(len(outs) + 9),
        scratch_shapes=[pltpu.VMEM(*b) for b in flat]
        + [pltpu.SemaphoreType.DMA(v) for v in semaphores.values()],
        compiler_params=pltpu.CompilerParams(
            collective_id=1, has_side_effects=True, vmem_limit_bytes=FINISH_VMEM
        ),
        name="finish",
    )(*given.values())
    return write_outputs(results, given["decoded"], dims)


FINISH_VMEM = 62 * 2**20


def write_kernel(small, decoded_got, gx_own, gx_got, *refs):
    big, decoded_own = refs[:9], refs[9]
    decoded, gx, *totals = refs[10:]
    s = lax.axis_index("section")
    half = decoded.shape[1]
    samples, rows, columns = decoded_own.shape[0], gx_own.shape[0], gx.shape[1]
    own = decoded_own[:, pl.ds(pl.multiple_of(s * half, half), half), :]
    for side, part in ((s, own), (1 - s, decoded_got[...])):
        decoded[pl.ds(side * samples, samples)] = part
    own = gx_own[:, pl.ds(pl.multiple_of(s * columns, 128), columns)]
    for side, part in ((s, own), (1 - s, gx_got[...])):
        gx[pl.ds(pl.multiple_of(side * rows, rows), rows), :] = part
    d = lax.axis_index("dp")
    wide, narrow = small.shape[1], big[DEC_OUT].shape[1]

    def piece(out, line, lanes, position):
        size = out.shape[0]
        value = small[pl.ds(line, 1), :lanes]
        value = pltpu.roll(value, lax.rem(lanes - position * size, lanes), 1)
        out[...] = value[:, :size].reshape(size)

    def matrix(out, name):
        value = big[name][...].astype(F32)
        out[...] = jnp.transpose(value) if name == DEC_DOWN else value

    def block(outs, first_row, bup_row, lanes, names):
        for i, out in zip((0, 1, None, None, 2, 3, 4, None, None, None, 5), outs):
            if i is not None:
                piece(out, first_row + i, lanes, d)
        piece(outs[8], bup_row + d // 4, lanes, d % 4)
        for at, name in zip((2, 3, 7, 9), names):
            matrix(outs[at], name)

    block(totals[:11], 0, ROW_BUP, wide, (ENC_QKV, ENC_OUT, ENC_UP, ENC_DOWN))
    matrix(totals[11], EMBED)
    piece(totals[12], ROW_DEC + 7, narrow, d)
    piece(totals[13], ROW_DEC + 6, narrow, d)
    block(totals[14:], ROW_DEC, ROW_DEC_BUP, narrow, (DEC_QKV, DEC_OUT, DEC_UP, DEC_DOWN))


def write_outputs(results, decoded_own, dims):
    def vector(size):
        return jax.ShapeDtypeStruct((size // 16,), F32)

    def matrix(name):
        return shape(dims[name][0] // 16, dims[name][1], F32)

    def block(qkv, out, up, down):
        d, ff = dims[up]
        return [
            vector(d), vector(d), matrix(qkv), matrix(out), vector(d), vector(d), vector(d),
            matrix(up), vector(ff), matrix(down), vector(d),
        ]

    samples, half, width = results[1].shape
    rows, columns = results[3].shape
    out_shape = [
        jax.ShapeDtypeStruct((2 * samples, half, width), BF16),
        shape(2 * rows, columns),
        *block(ENC_QKV, ENC_OUT, ENC_UP, ENC_DOWN),
        matrix(EMBED),
        vector(width),
        vector(width),
        *block(DEC_QKV, DEC_OUT, DEC_UP, DEC_DOWN),
    ]
    return tuple(
        pl.pallas_call(
            write_kernel,
            out_shape=out_shape,
            in_specs=in_vmem(len(results) + 1),
            out_specs=in_vmem(len(out_shape)),
            compiler_params=pltpu.CompilerParams(vmem_limit_bytes=KERNEL_VMEM),
            name="write_outputs",
        )(*results, decoded_own)
    )


def reduce_plain(arrays, section_index):
    first = section_index == 0
    results = []
    for a in arrays:
        half = a.shape[1] // 2
        keep = lax.dynamic_slice_in_dim(a, section_index * half, half, 1)
        give = lax.dynamic_slice_in_dim(a, (1 - section_index) * half, half, 1)
        got = swapped(give, "section", 0)
        chip = (keep.astype(jnp.float32) + got.astype(jnp.float32)).astype(jnp.bfloat16)
        mine = lax.psum_scatter(chip, "dp", scatter_dimension=0, tiled=True)
        other = swapped(mine, "section", 0)
        whole = jnp.concatenate(
            [jnp.where(first, mine, other), jnp.where(first, other, mine)], axis=1
        )
        results.append(whole.astype(jnp.float32))
    return results


def finish_plain(acts, section_index):
    x, gy, seg_saved, enc, dec = acts["x"], acts["gy"], acts["saved"], acts["enc"], acts["dec"]
    gx, gf1, ga1, gqkv1, small1, gbup1 = encoder_backward(x, gy, seg_saved, enc["params"])
    small2, gbup2 = acts["small2"], acts["gbup2"]
    grads = (
        small1[0], small1[1], mm(enc["at"], gqkv1).astype(BF16), mm(enc["ot"], ga1).astype(BF16), small1[2],
        small1[3], small1[4], mm(enc["ct"], gf1).astype(BF16), gbup1[0], mm(enc["ut"], gy).astype(BF16),
        small1[5],
        weight_grad(acts["y"], acts["geb"]), small2[7], small2[6],
        small2[0], small2[1], mm(dec["at"], dec["gqkv"]).astype(BF16),
        mm(dec["ot"], dec["ga"]).astype(BF16), small2[2], small2[3], small2[4],
        mm(dec["ct"], dec["gf"]).astype(BF16), gbup2[0],
        jnp.transpose(mm(dec["gt"], dec["u"])).astype(BF16), small2[5],
    )
    groups = lax.axis_size("dp")
    big = reduce_plain([g for g in grads if g.ndim == 2], section_index)
    flat = jnp.concatenate([g.reshape(groups, -1) for g in grads if g.ndim == 1], axis=1)
    line = lax.psum_scatter(flat, ("dp"), scatter_dimension=0, tiled=True)
    line = lax.psum(line, "section")[0]
    totals, at = [], 0
    for g in grads:
        if g.ndim == 2:
            totals.append(big.pop(0))
        else:
            size = g.shape[0] // groups
            totals.append(line[at : at + size])
            at += size
    decoded = acts["decoded"].reshape(SAMP_MB, PATCHES, -1)
    first = section_index == 0

    def halves(whole):
        half = whole.shape[1] // 2
        keep = lax.dynamic_slice_in_dim(whole, section_index * half, half, 1)
        give = lax.dynamic_slice_in_dim(whole, (1 - section_index) * half, half, 1)
        got = swapped(give, "section", 0)
        return jnp.concatenate([jnp.where(first, keep, got), jnp.where(first, got, keep)])

    return (halves(decoded), halves(gx), *totals)


def shards(
    patches,
    segment_ids,
    patch_order,
    encoder_gain1,
    encoder_bias1,
    encoder_qkv,
    encoder_out,
    encoder_out_bias,
    encoder_gain2,
    encoder_bias2,
    encoder_up,
    encoder_up_bias,
    encoder_down,
    encoder_down_bias,
    embed_weight,
    embed_bias,
    mask_token,
    decoder_gain1,
    decoder_bias1,
    decoder_qkv,
    decoder_out,
    decoder_out_bias,
    decoder_gain2,
    decoder_bias2,
    decoder_up,
    decoder_up_bias,
    decoder_down,
    decoder_down_bias,
    cotangent,
):
    enc_params = (
        encoder_gain1,
        encoder_bias1,
        encoder_qkv,
        encoder_out,
        encoder_out_bias,
        encoder_gain2,
        encoder_bias2,
        encoder_up,
        encoder_up_bias,
        encoder_down,
        encoder_down_bias,
    )
    embed_params = (embed_weight, embed_bias, mask_token)
    dec_params = (
        decoder_gain1,
        decoder_bias1,
        decoder_qkv,
        decoder_out,
        decoder_out_bias,
        decoder_gain2,
        decoder_bias2,
        decoder_up,
        decoder_up_bias,
        decoder_down,
        decoder_down_bias,
    )
    section_index = lax.axis_index("section")
    y, at1, qkv, e, rl, o1, ot1, n2, s2, ct1, ut1, slope = encoder_forward(
        patches, segment_ids, enc_params
    )
    g = cotangent.reshape(-1, DECODER_WIDTH)
    decoded, at2, ot2, ct2, gt2, u2, gf2, ga2, gqkv2, geb, gy, small2, gbup2 = decoder_both(
        y, segment_ids, patch_order, g, embed_params, dec_params
    )
    acts = dict(
        x=patches,
        y=y,
        gy=gy,
        geb=geb,
        decoded=decoded,
        small2=small2,
        gbup2=gbup2,
        saved=(qkv, e, rl, o1, n2, s2, slope),
        enc=dict(at=at1, ot=ot1, ct=ct1, ut=ut1, params=enc_params),
        dec=dict(at=at2, ot=ot2, ct=ct2, gt=gt2, u=u2, gf=gf2, ga=ga2, gqkv=gqkv2),
    )
    if lax.axis_size("dp") == 16:
        return finish(acts)
    return finish_plain(acts, section_index)


def solution(mesh):
    in_specs = (
        P("dp", None),
        P("dp", None),
        P("dp", None),
        P(),
        P(),
        P(),
        P(),
        P(),
        P(),
        P(),
        P(),
        P(),
        P(),
        P(),
        P(),
        P(),
        P(),
        P(),
        P(),
        P(),
        P(),
        P(),
        P(),
        P(),
        P(),
        P(),
        P(),
        P(),
        P("dp", None, None),
    )
    out_specs = (
        P("dp", "section", None),
        P("dp", "section"),
        P("dp"),
        P("dp"),
        P("dp", None),
        P("dp", None),
        P("dp"),
        P("dp"),
        P("dp"),
        P("dp", None),
        P("dp"),
        P("dp", None),
        P("dp"),
        P("dp", None),
        P("dp"),
        P("dp"),
        P("dp"),
        P("dp"),
        P("dp", None),
        P("dp", None),
        P("dp"),
        P("dp"),
        P("dp"),
        P("dp", None),
        P("dp"),
        P("dp", None),
        P("dp"),
    )
    return jax.shard_map(shards, mesh=mesh, in_specs=in_specs, out_specs=out_specs, check_vma=False)
```
